32 devices in a mesh: dp: 4 (over x, core), space: 8 (over z, y).
Axes of the slice: x: 2, y: 2, z: 4, core: 2. Of those that a mesh axis runs over, the one named last changes fastest.
Arguments:
- net: bfloat16 [8, 40, 128, 128], P('dp', 'space'), may hold values from -1 to 1
- context: bfloat16 [8, 40, 128, 128], P('dp', 'space'), may hold values from -6 to 6
- corr: bfloat16 [8, 40, 128, 324], P('dp', 'space'), may hold values from -6 to 6
- flow: bfloat16 [8, 2, 40, 128], P('dp', None, 'space'), may hold values from -12 to 12
- target: float32 [8, 2, 40, 128], P('dp', None, None, 'space'), may hold values from -12 to 12
- valid: int32 [8, 40, 128], P('dp', None, 'space'), may hold values from 0 to 1
- grad_net: bfloat16 [8, 40, 128, 128], P('dp', None, 'space'), may hold values from -6 to 6
- grad_mask: bfloat16 [8, 40, 128, 576], P('dp', None, 'space'), may hold values from -6 to 6
- params: bfloat16 [3120960], P('dp'), may hold values from -2 to 2
Outputs:
- new_net: bfloat16 [8, 40, 128, 128], P('dp', None, 'space')
- new_flow: float32 [8, 2, 40, 128], P('dp', None, None, 'space')
- mask: bfloat16 [8, 40, 128, 576], P('dp', None, 'space')
- loss: float32 [8], P('dp')
- grad_params: float32 [3120960], P('dp')
- grad_net_in: float32 [8, 40, 128, 128], P('dp', 'space')
- grad_context: float32 [8, 40, 128, 128], P('dp', 'space')
- grad_corr: float32 [8, 40, 128, 324], P('dp', 'space')
- grad_flow: float32 [8, 2, 40, 128], P('dp', None, 'space')
The draws below stay inside these ranges and needn't reach their ends.
All inputs are finite; a program needn't handle non-finite values.
Results may differ from the reference program's by a relative error of at most 0.014.
Values may be sent and summed in bfloat16 or wider, within the bound.
A program may use at most 192 MiB of HBM per device.

```python
import jax
import jax.numpy as jnp
from jax import lax

HID = 128
CTX = 128
MOT = 128
CORR = 324
C1 = 256
C2 = 192
F1 = 128
F2 = 64
HEAD = 256
MASK = 576
WIDTH = 128
HEIGHT = 40
IMAGES = 8


def shapes_drawn():
    inputs_width = HID + CTX + MOT
    return [('corr_in', CORR, C1), ('corr_mix', 9 * C1, C2), ('flow_in', 98, F1), ('flow_mix', 9 * F1, F2), ('motion_mix', 9 * (C2 + F2), MOT - 2), ('rows_gates', 5 * inputs_width, 2 * HID), ('rows_candidate', 5 * inputs_width, HID), ('columns_gates', 5 * inputs_width, 2 * HID), ('columns_candidate', 5 * inputs_width, HID), ('flow_hidden', 9 * HID, HEAD), ('flow_out', 9 * HEAD, 2), ('mask_hidden', 9 * HID, HEAD), ('mask_out', HEAD, MASK)]


def draw_params(key, part):
    key = jax.random.fold_in(key, 7)
    table = shapes_drawn()
    entries = []
    for number, entry in enumerate(table):
        entries.append((jax.random.fold_in(key, number), entry[1] * entry[2], entry[1] ** (-0.5) * (2.0 if entry[0] == 'mask_out' else 1.0)))
    for number, entry in enumerate(table):
        entries.append((jax.random.fold_in(key, 100 + number), entry[2], 0.3))
    pieces = []
    for sub_key, count, scale in entries:
        values = jnp.clip(jax.random.normal(sub_key, (count,), jnp.float32), -4.0, 4.0)
        pieces.append(values * scale)
    return jnp.concatenate(pieces).astype(jnp.bfloat16)


def draw_valid(key, part):
    key = jax.random.fold_in(key, 3)
    extent = (IMAGES, HEIGHT, WIDTH)
    image_index = lax.broadcasted_iota(jnp.int32, extent, 0)
    row_index = lax.broadcasted_iota(jnp.int32, extent, 1)
    column_index = lax.broadcasted_iota(jnp.int32, extent, 2)
    level = (200 + 600 * column_index // WIDTH) * (500 + 500 * row_index // HEIGHT) // 1000
    ticket = jax.random.randint(jax.random.fold_in(key, 1), extent, 0, 1000)
    empty = jax.random.randint(jax.random.fold_in(key, 2), (), 0, IMAGES)
    return jnp.where((ticket < level) & (image_index != empty), 1, 0).astype(jnp.int32)


def levels(stream_key, dims, shards, low, largest):
    def one(position, shards_of):
        draws = jax.random.uniform(jax.random.fold_in(jax.random.fold_in(stream_key, 6), position), (shards_of,), jnp.float32, low / len(shards), largest / len(shards))
        return jnp.repeat(jnp.exp(draws), dims[position] // shards_of).reshape((-1,) + (1,) * (len(dims) - position - 1))

    gain = one(*shards[0])
    for cut in shards[1:]:
        gain = gain * one(*cut)
    return gain


def normal_values(key, shape, deviation, reach, cuts=(), kind=jnp.bfloat16):
    level = levels(key, shape, cuts, -0.22, 0.18) if cuts else 1.0
    values = jax.random.normal(key, shape, jnp.float32) * deviation * level
    return jnp.minimum(jnp.maximum(values, -reach), reach).astype(kind)


def setup_inputs(seed: int = 0) -> dict:
    arg_keys = jax.random.split(jax.random.key(seed), 10)
    net = jnp.clip(jax.random.uniform(arg_keys[0], (IMAGES, HEIGHT, WIDTH, HID), jnp.float32, -1.0, 1.0) * levels(arg_keys[0], (IMAGES, HEIGHT, WIDTH, HID), ((0, 4), (1, 8)), -0.4, 0.0), -1.0, 1.0).astype(jnp.bfloat16)
    context = normal_values(arg_keys[1], (IMAGES, HEIGHT, WIDTH, CTX), 1.0, 6.0, ((0, 4), (1, 8)))
    corr = normal_values(arg_keys[2], (IMAGES, HEIGHT, WIDTH, CORR), 1.0, 6.0, ((0, 4), (1, 8)))
    flow = normal_values(arg_keys[3], (IMAGES, 2, HEIGHT, WIDTH), 2.0, 12.0, ((0, 4), (2, 8)))
    target = normal_values(arg_keys[4], (IMAGES, 2, HEIGHT, WIDTH), 2.0, 12.0, ((0, 4), (3, 8)), jnp.float32)
    valid = draw_valid(jax.random.fold_in(arg_keys[9], 71), 0)
    grad_net = normal_values(arg_keys[6], (IMAGES, HEIGHT, WIDTH, HID), 1.0, 6.0, ((0, 4), (2, 8)))
    grad_mask = normal_values(arg_keys[7], (IMAGES, HEIGHT, WIDTH, MASK), 1.0, 6.0, ((0, 4), (2, 8)))
    params = draw_params(jax.random.fold_in(arg_keys[9], 71), 0)
    return dict(net=net, context=context, corr=corr, flow=flow, target=target, valid=valid, grad_net=grad_net, grad_mask=grad_mask, params=params)


@jax.custom_vjp
def low(v):
    return lax.optimization_barrier(v.astype(jnp.bfloat16)).astype(jnp.float32)

@jax.custom_vjp
def low_back(v):
    return v

def low_keep(v):
    return (low(v), None)

def low_pass(kept, grad):
    return (grad,)

def back_keep(v):
    return (v, None)

def back_low(kept, grad):
    return (low(grad),)
low.defvjp(low_keep, low_pass)
low_back.defvjp(back_keep, back_low)

def shapes():
    inputs_width = HID + CTX + MOT
    return [('corr_in', CORR, C1), ('corr_mix', 9 * C1, C2), ('flow_in', 98, F1), ('flow_mix', 9 * F1, F2), ('motion_mix', 9 * (C2 + F2), MOT - 2), ('rows_gates', 5 * inputs_width, 2 * HID), ('rows_candidate', 5 * inputs_width, HID), ('columns_gates', 5 * inputs_width, 2 * HID), ('columns_candidate', 5 * inputs_width, HID), ('flow_hidden', 9 * HID, HEAD), ('flow_out', 9 * HEAD, 2), ('mask_hidden', 9 * HID, HEAD), ('mask_out', HEAD, MASK)]

def unpack(flat):
    weights = {}
    biases = {}
    offset = 0
    table = shapes()
    for name, height, width in table:
        weights[name] = flat[offset:offset + height * width].reshape(height, width)
        offset = offset + height * width
    for name, height, width in table:
        biases[name] = flat[offset:offset + width]
        offset = offset + width
    return (weights, biases)

def patches(padded, tall, wide):
    out_rows = padded.shape[0] - tall + 1
    out_columns = padded.shape[1] - wide + 1
    return jnp.concatenate([padded[down:down + out_rows, across:across + out_columns] for down in range(tall) for across in range(wide)], axis=-1)

def convolve(field, weight, bias, tall, wide):
    padded = jnp.pad(field, ((tall // 2, tall // 2), (wide // 2, wide // 2), (0, 0)))
    stacked = patches(padded, tall, wide)
    return jnp.einsum('hwk,ko->hwo', stacked, weight, precision=lax.Precision.HIGHEST) + bias

def forward(flat, net, context, corr, flow):
    weights, biases = unpack(flat)

    def layer(field, name, tall, wide):
        return low_back(convolve(field, weights[name], biases[name], tall, wide))

    def gru_half(state, inputs, gate_name, candidate_name, tall, wide):
        gates = jax.nn.sigmoid(layer(jnp.concatenate([state, inputs], -1), gate_name, tall, wide))
        update = gates[..., :HID]
        reset = gates[..., HID:]
        mixed = jnp.concatenate([low(reset * state), inputs], -1)
        candidate = jnp.tanh(layer(mixed, candidate_name, tall, wide))
        return state + update * (candidate - state)
    corr_one = low(jax.nn.silu(layer(corr, 'corr_in', 1, 1)))
    corr_two = low(jax.nn.silu(layer(corr_one, 'corr_mix', 3, 3)))
    flow_one = low(jax.nn.silu(layer(flow, 'flow_in', 7, 7)))
    flow_two = low(jax.nn.silu(layer(flow_one, 'flow_mix', 3, 3)))
    motion = low(jax.nn.silu(layer(jnp.concatenate([corr_two, flow_two], -1), 'motion_mix', 3, 3)))
    inputs = jnp.concatenate([context, motion, flow], -1)
    state = gru_half(net, inputs, 'rows_gates', 'rows_candidate', 1, 5)
    state_low = low(low_back(state))
    inputs_sent = low_back(inputs)
    final = gru_half(state_low, inputs_sent, 'columns_gates', 'columns_candidate', 5, 1)
    final_low = low(final)
    flow_features = low(jax.nn.silu(layer(final_low, 'flow_hidden', 3, 3)))
    delta = layer(flow_features, 'flow_out', 3, 3)
    mask_features = low(jax.nn.silu(layer(final_low, 'mask_hidden', 3, 3)))
    mask_full = 0.25 * layer(mask_features, 'mask_out', 1, 1)
    new_flow = inputs_sent[..., CTX + MOT - 2:] + delta
    return (final, mask_full, new_flow)

def reference(net, context, corr, flow, target, valid, grad_net, grad_mask, params):
    flat = params.astype(jnp.float32)
    counts = lax.optimization_barrier(jnp.sum(valid, axis=(1, 2))).astype(jnp.float32)
    plane = jnp.float32(HEIGHT * WIDTH)

    def one_image(total, items):
        net_one, context_one, corr_one, flow_one, target_one, valid_one, count_one, net_cotangent, mask_cotangent = items
        target_last = jnp.transpose(target_one, (1, 2, 0))
        valid_float = valid_one.astype(jnp.float32)

        def objective(flat_in, net_in, context_in, corr_in, flow_in):
            final, mask_full, new_flow = forward(flat_in, net_in, context_in, corr_in, flow_in)
            error = new_flow - target_last
            penalty = lax.optimization_barrier(jnp.sum(jnp.sqrt(error * error + 1.0), axis=-1))
            loss = jnp.sum(valid_float * penalty) / jnp.maximum(count_one, 1.0)
            return ((final, mask_full, plane * loss), (new_flow, loss))
        primal, pullback, extras = jax.vjp(objective, flat, net_one.astype(jnp.float32), context_one.astype(jnp.float32), corr_one.astype(jnp.float32), jnp.transpose(flow_one, (1, 2, 0)).astype(jnp.float32), has_aux=True)
        grads = pullback((net_cotangent.astype(jnp.float32), mask_cotangent.astype(jnp.float32), jnp.float32(1.0)))
        outputs = (primal[0].astype(jnp.bfloat16), jnp.transpose(extras[0], (2, 0, 1)), primal[1].astype(jnp.bfloat16), extras[1], grads[1], grads[2], grads[3], jnp.transpose(grads[4], (2, 0, 1)))
        return (total + grads[0], outputs)
    total, stacked = lax.scan(one_image, jnp.zeros_like(flat), (net, context, corr, flow, target, valid, counts, grad_net, grad_mask))
    return (stacked[0], stacked[1], stacked[2], stacked[3], total, stacked[4], stacked[5], stacked[6], stacked[7])
```

```python
import functools

import jax
import jax.numpy as jnp
from jax import lax
from jax.experimental import pallas as pl
from jax.experimental.pallas import tpu as pltpu
from jax.sharding import PartitionSpec as P

HID = 128
CTX = 128
MOT = 128
CORR = 324
SPACE = "space"
DP = "dp"
(
    CORR_IN,
    CORR_MIX,
    FLOW_IN,
    FLOW_MIX,
    MOTION_MIX,
    ROWS_GATES,
    ROWS_CANDIDATE,
    COLUMNS_GATES,
    COLUMNS_CANDIDATE,
    FLOW_HIDDEN,
    FLOW_OUT,
    MASK_HIDDEN,
    MASK_OUT,
) = range(13)
C1 = 256
C2 = 192
F1 = 128
F2 = 64
HEAD = 256
MASK = 576


def with_halo(block, sides, width):
    for axis, dim in sides:
        count = lax.axis_size(axis)
        forward = [(i, i + 1) for i in range(count - 1)]
        backward = [(target, source) for source, target in forward]
        low = lax.ppermute(
            lax.slice_in_dim(block, block.shape[dim] - width, None, axis=dim), axis, forward
        )
        high = lax.ppermute(lax.slice_in_dim(block, 0, width, axis=dim), axis, backward)
        block = jnp.concatenate([low, block, high], axis=dim)
    return block


def shapes():
    inputs_width = HID + CTX + MOT
    return [
        (CORR_IN, CORR, C1),
        (CORR_MIX, 9 * C1, C2),
        (FLOW_IN, 98, F1),
        (FLOW_MIX, 9 * F1, F2),
        (MOTION_MIX, 9 * (C2 + F2), MOT - 2),
        (ROWS_GATES, 5 * inputs_width, 2 * HID),
        (ROWS_CANDIDATE, 5 * inputs_width, HID),
        (COLUMNS_GATES, 5 * inputs_width, 2 * HID),
        (COLUMNS_CANDIDATE, 5 * inputs_width, HID),
        (FLOW_HIDDEN, 9 * HID, HEAD),
        (FLOW_OUT, 9 * HEAD, 2),
        (MASK_HIDDEN, 9 * HID, HEAD),
        (MASK_OUT, HEAD, MASK),
    ]


def unpack(flat):
    weights = {}
    biases = {}
    offset = 0
    table = shapes()
    for name, height, width in table:
        weights[name] = flat[offset // LANES : (offset + height * width) // LANES].reshape(height, width)
        offset = offset + height * width
    rest = flat[offset // LANES :].reshape(-1)
    offset = 0
    for name, height, width in table:
        biases[name] = rest[offset : offset + width].astype(jnp.float32)
        offset = offset + width
    return (weights, biases)


def pack(grads, total):
    table = shapes()
    rows = [grads[entry[0]][0].astype(jnp.bfloat16).reshape(-1, LANES) for entry in table]
    biases = jnp.concatenate([grads[entry[0]][1] for entry in table]).astype(jnp.bfloat16)
    left = total * LANES - sum(entry[1] * entry[2] for entry in table) - biases.shape[0]
    return jnp.concatenate(rows + [jnp.pad(biases, (0, left)).reshape(-1, LANES)])


def patches(padded, tall, wide):
    out_rows = padded.shape[1] - tall + 1
    out_columns = padded.shape[2] - wide + 1
    return jnp.concatenate(
        [
            padded[:, down : down + out_rows, across : across + out_columns]
            for down in range(tall)
            for across in range(wide)
        ],
        axis=-1,
    )


def apply(stacked, weight):
    return jnp.einsum("bhwk,ko->bhwo", stacked, weight, preferred_element_type=jnp.float32)


def apply_back(grad, weight):
    return jnp.einsum("bhwo,ko->bhwk", grad, weight, preferred_element_type=jnp.float32)


def weight_grad(stacked, pre_grad):
    return jnp.einsum("bhwk,bhwo->ko", stacked, pre_grad, preferred_element_type=jnp.float32)


def record(grads, name, stacked, pre_grad):
    grads[name] = (
        weight_grad(stacked, pre_grad),
        jnp.sum(pre_grad, axis=(0, 1, 2), dtype=jnp.float32),
    )


def flipped(weight, tall, wide):
    inner = weight.shape[0] // (tall * wide)
    shaped = weight.reshape(tall, wide, inner, weight.shape[1])[::-1, ::-1]
    return jnp.transpose(shaped, (0, 1, 3, 2)).reshape(-1, inner)


def slope(pre):
    sigma = jax.nn.sigmoid(pre)
    return sigma * (1.0 + pre * (1.0 - sigma))


def local_pad(field, tall, wide):
    return jnp.pad(field, ((0, 0), (tall // 2, tall // 2), (wide // 2, wide // 2), (0, 0)))


def row_pad(field, tall):
    field = with_halo(field, ((SPACE, 1),), tall // 2)
    return jnp.pad(field, ((0, 0), (0, 0), (tall // 2, tall // 2), (0, 0)))


def column_pad(field, tall, wide):
    field = with_halo(field, ((SPACE, 2),), wide // 2)
    return jnp.pad(field, ((0, 0), (tall // 2, tall // 2), (0, 0), (0, 0)))


MESH = pl.DeviceIdType.MESH
LANES = 128
BLOCK = 6144


def quarter_start(rank, count):
    return lax.div(rank * count, LANES)


def quarter_base(rank, count):
    return lax.div(rank * count, LANES * 16) * 16


def mate_of(rank):
    return rank + 1 - 2 * lax.rem(rank, 2)


def remote(src, dst, send, recv, device):
    return pltpu.make_async_remote_copy(
        src_ref=src, dst_ref=dst, send_sem=send, recv_sem=recv, device_id=device, device_id_type=MESH
    )


def greet(devices):
    barrier = pltpu.get_barrier_semaphore()
    for device in devices:
        pl.semaphore_signal(barrier, inc=1, device_id=device, device_id_type=MESH)
    pl.semaphore_wait(barrier, len(devices))


def lane_matrix(shift, forward):
    source = lax.broadcasted_iota(jnp.int32, (LANES, 2 * LANES), 0)
    target = lax.broadcasted_iota(jnp.int32, (LANES, 2 * LANES), 1)
    if forward:
        return jnp.where(target == source + shift, 1.0, 0.0).astype(jnp.bfloat16)
    return jnp.where(lax.rem(target + LANES, 2 * LANES) == source - shift + LANES, 1.0, 0.0).astype(jnp.bfloat16)


def gather_kernel(count, local_ref, out_ref, own_ref, send, recv):
    rank, spot = lax.axis_index(DP), lax.axis_index(SPACE)
    mate, across, twin = mate_of(rank), lax.rem(rank + 2, 4), mate_of(spot)
    pieces = 4
    rows = BLOCK // 2 // pieces
    peers = ({DP: mate}, {DP: across}, {SPACE: twin})
    greet(peers)
    matrix = lane_matrix(lax.rem(rank * count, LANES), True)
    first = lax.broadcasted_iota(jnp.int32, (256, LANES), 0) == 0

    def rotate(step, carry):
        at = pl.ds(pl.multiple_of(step * 256, 256), 256)
        both = jnp.dot(local_ref[at, :], matrix, preferred_element_type=jnp.float32)
        spill = pltpu.roll(both[:, LANES:], 1, 0)
        own_ref[at, :] = (both[:, :LANES] + jnp.where(first, carry, spill)).astype(jnp.bfloat16)
        return spill[0:1]

    lax.fori_loop(0, BLOCK // 256, rotate, jnp.zeros((1, LANES), jnp.float32))

    half, other_half = lax.rem(spot, 2), lax.rem(spot + 1, 2)

    def piece(which, index):
        return pl.ds(pl.multiple_of(which * (BLOCK // 2) + index * rows, 16), rows)

    own_x = [
        remote(own_ref.at[piece(half, k)], out_ref.at[rank, piece(half, k)], send.at[0, k], recv.at[0, k], peers[1])
        for k in range(pieces)
    ]
    own_c = remote(own_ref, out_ref.at[rank], send.at[4, 0], recv.at[4, 0], peers[0])
    for copy in own_x:
        copy.start()
    own_c.start()
    later = []
    for k in range(pieces):
        own_x[k].wait_recv()
        block = out_ref.at[across, piece(half, k)]
        to_twin = remote(block, block, send.at[1, k], recv.at[1, k], peers[2])
        to_mate = remote(block, block, send.at[2, k], recv.at[2, k], peers[0])
        to_twin.start()
        to_mate.start()
        later.append((to_twin, to_mate))
    for at in range(BLOCK // 256):
        out_ref[rank, at * 256 : (at + 1) * 256, :] = own_ref[at * 256 : (at + 1) * 256, :]
    for k in range(pieces):
        later[k][0].wait_recv()
        block = out_ref.at[across, piece(other_half, k)]
        to_mate = remote(block, block, send.at[3, k], recv.at[3, k], peers[0])
        to_mate.start()
        later.append((to_mate,))
    for k in range(pieces):
        own_x[k].wait_send()
        later[k][0].wait_send()
        later[k][1].wait()
        later[pieces + k][0].wait()
    own_c.wait()


def gather_blocks(params):
    count = params.shape[0]
    local = jnp.pad(params, (0, BLOCK * LANES - count)).reshape(BLOCK, LANES)
    return pl.pallas_call(
        functools.partial(gather_kernel, count),
        out_shape=jax.ShapeDtypeStruct((4, BLOCK, LANES), jnp.bfloat16),
        in_specs=[pl.BlockSpec(memory_space=pltpu.VMEM)],
        out_specs=pl.BlockSpec(memory_space=pltpu.VMEM),
        scratch_shapes=[
            pltpu.VMEM((BLOCK, LANES), jnp.bfloat16),
            pltpu.SemaphoreType.DMA((5, 4)),
            pltpu.SemaphoreType.DMA((5, 4)),
        ],
        compiler_params=pltpu.CompilerParams(
            collective_id=0, has_side_effects=True, vmem_limit_bytes=32 * 2**20
        ),
    )(local)


def gather_params(params):
    count = params.shape[0]
    blocks = gather_blocks(params)
    pieces = []
    reach = 0
    for rank in range(4):
        start = rank * count // LANES
        stop = -(-(rank + 1) * count // LANES)
        head = blocks[rank, :1] if rank == 0 else blocks[rank, :1] + pieces.pop()
        pieces += [head, blocks[rank, 1 : stop - start - 1], blocks[rank, stop - start - 1 : stop - start]]
    return jnp.concatenate(pieces)


def reduce_kernel(count, space, pieces, grads_ref, out_ref, rc, tx, rx, acc, ty, ry, tz, rz, gath, send, recv, zsend, zrecv):
    rank, spot = lax.axis_index(DP), lax.axis_index(SPACE)
    mate, across, twin = mate_of(rank), lax.rem(rank + 2, 4), mate_of(spot)
    group = space // 2
    side, depth = lax.rem(spot, 2), lax.div(spot, 2)
    rows = BLOCK // pieces
    half = rows // 2
    part = half // group

    def partner(step):
        return lax.rem(depth + step, group)

    peers = [{DP: mate}, {DP: across}, {SPACE: twin}]
    barrier = pltpu.get_barrier_semaphore()
    for device in peers:
        pl.semaphore_signal(barrier, inc=1, device_id=device, device_id_type=MESH)

    def hello(step, carry):
        pl.semaphore_signal(barrier, inc=1, device_id={SPACE: partner(step) * 2 + side}, device_id_type=MESH)
        return carry

    lax.fori_loop(1, group, hello, 0)
    pl.semaphore_wait(barrier, 3 + group - 1)

    gath[BLOCK:, :] = jnp.zeros((32, LANES), jnp.bfloat16)
    lower = lax.rem(rank, 2)
    upper = lax.div(rank, 2)

    def base(who):
        return pl.multiple_of(quarter_base(who, count), 16)

    def rows_of(start, index, length):
        return pl.ds(pl.multiple_of(start + index, 16), length)

    core = []
    for p in range(pieces):
        for high in range(2):
            copy = remote(
                grads_ref.at[rows_of(base(2 * high + 1 - lower), p * rows, rows)],
                rc.at[p, high],
                send.at[high, p],
                recv.at[high, p],
                peers[0],
            )
            copy.start()
            core.append(copy)
    step_rows = 192 if half % 192 == 0 else 16
    xs, ys, gs = [], [], []

    def z_copy(p, step):
        to = partner(step)
        return remote(
            tz.at[p, pl.ds(pl.multiple_of(to * part, 16), part)],
            rz.at[p, pl.ds(pl.multiple_of(depth * part, 16), part)],
            zsend.at[0, p, step],
            zrecv.at[0, p, step],
            {SPACE: to * 2 + side},
        )

    def home(p, which, slot):
        return pl.ds(pl.multiple_of(p * rows + which * half + slot * part, 16), part)

    def g_copy(p, step):
        block = gath.at[home(p, side, depth)]
        return remote(block, block, zsend.at[1, p, step], zrecv.at[1, p, step], {SPACE: partner(step) * 2 + side})

    def each(body):
        def run(step, carry):
            body(step)
            return carry

        lax.fori_loop(1, group, run, 0)

    def stage_core(p):
        core[2 * p].wait_recv()
        core[2 * p + 1].wait_recv()
        far = 1 - upper

        def add(step, carry):
            at = pl.multiple_of(step * step_rows, 16)
            mine = grads_ref[rows_of(base(2 * far + lower), p * rows + at, step_rows), :].astype(jnp.float32)
            tx[p, pl.ds(at, step_rows), :] = (
                mine + rc[p, far, pl.ds(at, step_rows), :].astype(jnp.float32)
            ).astype(jnp.bfloat16)
            return carry

        lax.fori_loop(0, rows // step_rows, add, 0)
        copy = remote(tx.at[p], rx.at[p], send.at[2, p], recv.at[2, p], peers[1])
        copy.start()
        xs.append(copy)

    def stage_x(p):
        xs[p].wait_recv()

        def total(at):
            return (
                grads_ref[rows_of(base(rank), p * rows + at, step_rows), :].astype(jnp.float32)
                + rc[p, upper, pl.ds(at, step_rows), :].astype(jnp.float32)
                + rx[p, pl.ds(at, step_rows), :].astype(jnp.float32)
            )

        def add(step, carry):
            at = pl.multiple_of(step * step_rows, 16)
            far = pl.multiple_of((1 - side) * half + at, 16)
            near = pl.multiple_of(side * half + at, 16)
            ty[p, pl.ds(at, step_rows), :] = total(far).astype(jnp.bfloat16)
            acc[p, pl.ds(at, step_rows), :] = total(near)
            return carry

        lax.fori_loop(0, half // step_rows, add, 0)
        copy = remote(ty.at[p], ry.at[p], send.at[3, p], recv.at[3, p], peers[2])
        copy.start()
        ys.append(copy)

    def stage_y(p):
        ys[p].wait_recv()

        def add(step, carry):
            at = pl.ds(pl.multiple_of(step * step_rows, 16), step_rows)
            value = acc[p, at, :] + ry[p, at, :].astype(jnp.float32)
            acc[p, at, :] = value
            tz[p, at, :] = value.astype(jnp.bfloat16)
            return carry

        lax.fori_loop(0, half // step_rows, add, 0)
        each(lambda step: z_copy(p, step).start())

    def stage_z(p):
        each(lambda step: z_copy(p, step).wait_recv())
        value = acc[p, pl.ds(pl.multiple_of(depth * part, 16), part), :]

        def add(step, value):
            other = lax.rem(depth + group - step, group)
            return value + rz[p, pl.ds(pl.multiple_of(other * part, 16), part), :].astype(jnp.float32)

        value = lax.fori_loop(1, group, add, value)
        gath[home(p, side, depth), :] = value.astype(jnp.bfloat16)
        each(lambda step: g_copy(p, step).start())

    def stage_zg(p):
        each(lambda step: g_copy(p, step).wait_recv())
        block = gath.at[pl.ds(pl.multiple_of(p * rows + side * half, 16), half)]
        copy = remote(block, block, send.at[4, p], recv.at[4, p], peers[2])
        copy.start()
        gs.append(copy)

    def stage_yg(p):
        gs[p].wait_recv()

    stages = [stage_core, stage_x, stage_y, stage_z, stage_zg, stage_yg]
    for tick in range(pieces + len(stages) - 1):
        for number in reversed(range(len(stages))):
            if 0 <= tick - number < pieces:
                stages[number](tick - number)

    for copy in core + xs + ys + gs:
        copy.wait_send()
    for p in range(pieces):

        def done(step):
            z_copy(p, step).wait_send()
            g_copy(p, step).wait_send()

        each(done)

    offset = rank * count - quarter_base(rank, count) * LANES
    skip = lax.div(offset, LANES)
    matrix = lane_matrix(lax.rem(offset, LANES), False)
    wide = jnp.where(
        lax.broadcasted_iota(jnp.int32, (256, 288), 1)
        == lax.broadcasted_iota(jnp.int32, (256, 288), 0) + skip,
        1.0,
        0.0,
    ).astype(jnp.bfloat16)
    wide_next = jnp.where(
        lax.broadcasted_iota(jnp.int32, (256, 288), 1)
        == lax.broadcasted_iota(jnp.int32, (256, 288), 0) + skip + 1,
        1.0,
        0.0,
    ).astype(jnp.bfloat16)

    def place(step, carry):
        at = pl.multiple_of(step * 256, 256)
        block = gath[pl.ds(at, 288), :]
        both = jnp.dot(block, matrix, preferred_element_type=jnp.float32).astype(jnp.bfloat16)
        out_ref[pl.ds(at, 256), :] = jnp.dot(wide, both[:, :LANES], preferred_element_type=jnp.float32) + jnp.dot(
            wide_next, both[:, LANES:], preferred_element_type=jnp.float32
        )
        return carry

    lax.fori_loop(0, BLOCK // 256, place, 0)


def reduce_grads(flat, space, count):
    pieces = next(k for k in (4, 2, 1) if BLOCK // (k * space) % 16 == 0)
    rows = BLOCK // pieces
    half = rows // 2
    out = pl.pallas_call(
        functools.partial(reduce_kernel, count, space, pieces),
        out_shape=jax.ShapeDtypeStruct((BLOCK, LANES), jnp.float32),
        in_specs=[pl.BlockSpec(memory_space=pltpu.VMEM)],
        out_specs=pl.BlockSpec(memory_space=pltpu.VMEM),
        scratch_shapes=[
            pltpu.VMEM((pieces, 2, rows, LANES), jnp.bfloat16),
            pltpu.VMEM((pieces, rows, LANES), jnp.bfloat16),
            pltpu.VMEM((pieces, rows, LANES), jnp.bfloat16),
            pltpu.VMEM((pieces, half, LANES), jnp.float32),
            pltpu.VMEM((pieces, half, LANES), jnp.bfloat16),
            pltpu.VMEM((pieces, half, LANES), jnp.bfloat16),
            pltpu.VMEM((pieces, half, LANES), jnp.bfloat16),
            pltpu.VMEM((pieces, half, LANES), jnp.bfloat16),
            pltpu.VMEM((BLOCK + 32, LANES), jnp.bfloat16),
            pltpu.SemaphoreType.DMA((5, pieces)),
            pltpu.SemaphoreType.DMA((5, pieces)),
            pltpu.SemaphoreType.DMA((2, pieces, space // 2)),
            pltpu.SemaphoreType.DMA((2, pieces, space // 2)),
        ],
        compiler_params=pltpu.CompilerParams(
            collective_id=1, has_side_effects=True, vmem_limit_bytes=48 * 2**20
        ),
    )(flat)
    return out.reshape(-1)[:count]


def gru_forward(state, inputs, weights, biases, gate_name, candidate_name, tall, wide, padder):
    joined_stack = patches(padder(jnp.concatenate([state, inputs], -1), tall, wide), tall, wide)
    gates = jax.nn.sigmoid(apply(joined_stack, weights[gate_name]) + biases[gate_name])
    hidden = state.shape[-1]
    update = gates[..., :hidden]
    reset = gates[..., hidden:]
    state_wide = state.astype(jnp.float32)
    mixed = jnp.concatenate([(reset * state_wide).astype(jnp.bfloat16), inputs], -1)
    mixed_stack = patches(padder(mixed, tall, wide), tall, wide)
    candidate = jnp.tanh(apply(mixed_stack, weights[candidate_name]) + biases[candidate_name])
    result = state_wide + update * (candidate - state_wide)
    return (result, (joined_stack, mixed_stack, update, reset, candidate, state_wide))


def gru_backward(result_grad, kept, weights, grads, gate_name, candidate_name, tall, wide, padder):
    joined_stack, mixed_stack, update, reset, candidate, state_wide = kept
    hidden = update.shape[-1]
    candidate_grad = (result_grad * update * (1.0 - candidate * candidate)).astype(jnp.bfloat16)
    record(grads, candidate_name, mixed_stack, candidate_grad)
    mixed_grad = apply(
        patches(padder(candidate_grad, tall, wide), tall, wide),
        flipped(weights[candidate_name], tall, wide),
    )
    reset_grad = mixed_grad[..., :hidden]
    gate_grad = jnp.concatenate(
        [
            result_grad * (candidate - state_wide) * update * (1.0 - update),
            reset_grad * state_wide * reset * (1.0 - reset),
        ],
        -1,
    ).astype(jnp.bfloat16)
    record(grads, gate_name, joined_stack, gate_grad)
    joined_grad = apply(
        patches(padder(gate_grad, tall, wide), tall, wide), flipped(weights[gate_name], tall, wide)
    )
    state_grad = result_grad * (1.0 - update) + reset_grad * reset + joined_grad[..., :hidden]
    inputs_grad = joined_grad[..., hidden:] + mixed_grad[..., hidden:]
    return (state_grad, inputs_grad)


def shards(net, context, corr, flow, target, valid, grad_net, grad_mask, params):
    flow_start = CTX + MOT - 2
    plane = jnp.float32(target.shape[2] * net.shape[2])
    counts = lax.psum(jnp.sum(valid, axis=(1, 2)).astype(jnp.float32), SPACE)
    divisor = jnp.maximum(counts, 1.0)
    weights, biases = unpack(gather_params(params))
    grads = {}
    flow_rows = jnp.transpose(flow, (0, 2, 3, 1))
    corr_pre = apply(corr, weights[CORR_IN]) + biases[CORR_IN]
    corr_one = jax.nn.silu(corr_pre).astype(jnp.bfloat16)
    corr_stack = patches(row_pad(corr_one, 3), 3, 3)
    corr_mix_pre = apply(corr_stack, weights[CORR_MIX]) + biases[CORR_MIX]
    corr_two = jax.nn.silu(corr_mix_pre).astype(jnp.bfloat16)
    flow_stack = patches(row_pad(flow_rows, 7), 7, 7)
    flow_pre = apply(flow_stack, weights[FLOW_IN]) + biases[FLOW_IN]
    flow_one = jax.nn.silu(flow_pre).astype(jnp.bfloat16)
    flow_mix_stack = patches(row_pad(flow_one, 3), 3, 3)
    flow_mix_pre = apply(flow_mix_stack, weights[FLOW_MIX]) + biases[FLOW_MIX]
    flow_two = jax.nn.silu(flow_mix_pre).astype(jnp.bfloat16)
    joint_stack = patches(row_pad(jnp.concatenate([corr_two, flow_two], -1), 3), 3, 3)
    motion_pre = apply(joint_stack, weights[MOTION_MIX]) + biases[MOTION_MIX]
    motion = jax.nn.silu(motion_pre).astype(jnp.bfloat16)
    inputs = jnp.concatenate([context, motion, flow_rows], -1)
    state, rows_kept = gru_forward(
        net, inputs, weights, biases, ROWS_GATES, ROWS_CANDIDATE, 1, 5, local_pad
    )
    state_columns, inputs_columns = (
        lax.all_to_all(
            state.astype(jnp.bfloat16), SPACE, split_axis=2, concat_axis=1, tiled=True
        ),
        lax.all_to_all(inputs, SPACE, split_axis=2, concat_axis=1, tiled=True),
    )
    target_here = jnp.transpose(target, (0, 2, 3, 1))
    valid_here = valid.astype(jnp.float32)
    net_cotangent = grad_net
    mask_cotangent = grad_mask
    final, columns_kept = gru_forward(
        state_columns,
        inputs_columns,
        weights,
        biases,
        COLUMNS_GATES,
        COLUMNS_CANDIDATE,
        5,
        1,
        local_pad,
    )
    final_low = final.astype(jnp.bfloat16)
    heads_weight = jnp.concatenate([weights[FLOW_HIDDEN], weights[MASK_HIDDEN]], 1)
    heads_bias = jnp.concatenate([biases[FLOW_HIDDEN], biases[MASK_HIDDEN]])
    net_stack = patches(column_pad(final_low, 3, 3), 3, 3)
    heads_pre = apply(net_stack, heads_weight) + heads_bias
    heads_act = jax.nn.silu(heads_pre).astype(jnp.bfloat16)
    flow_features = heads_act[..., :HEAD]
    mask_features = heads_act[..., HEAD:]
    hidden_stack = patches(column_pad(flow_features, 3, 3), 3, 3)
    delta = apply(hidden_stack, weights[FLOW_OUT]) + biases[FLOW_OUT]
    mask_full = 0.25 * (apply(mask_features, weights[MASK_OUT]) + biases[MASK_OUT])
    new_flow = inputs_columns[..., flow_start:].astype(jnp.float32) + delta
    error = new_flow - target_here
    root = jnp.sqrt(error * error + 1.0)
    partials = jnp.sum(valid_here * jnp.sum(root, axis=-1), axis=(1, 2))
    flow_grad = plane / divisor[:, None, None, None] * valid_here[..., None] * error / root
    mask_low = mask_full.astype(jnp.bfloat16)
    nets_out = final_low
    flows_out = jnp.transpose(new_flow, (0, 3, 1, 2))
    masks_out = mask_low
    delta_grad = flow_grad.astype(jnp.bfloat16)
    mask_grad = (0.25 * mask_cotangent.astype(jnp.float32)).astype(jnp.bfloat16)
    record(grads, MASK_OUT, mask_features, mask_grad)
    record(grads, FLOW_OUT, hidden_stack, delta_grad)
    from_flow = apply(
        patches(column_pad(delta_grad, 3, 3), 3, 3), flipped(weights[FLOW_OUT], 3, 3)
    )
    from_mask = apply_back(mask_grad, weights[MASK_OUT])
    heads_grad = (jnp.concatenate([from_flow, from_mask], -1) * slope(heads_pre)).astype(
        jnp.bfloat16
    )
    heads_wgrad = weight_grad(net_stack, heads_grad)
    heads_bgrad = jnp.sum(heads_grad, axis=(0, 1, 2), dtype=jnp.float32)
    grads[FLOW_HIDDEN] = (heads_wgrad[:, :HEAD], heads_bgrad[:HEAD])
    grads[MASK_HIDDEN] = (heads_wgrad[:, HEAD:], heads_bgrad[HEAD:])
    final_grad = net_cotangent.astype(jnp.float32) + apply(
        patches(column_pad(heads_grad, 3, 3), 3, 3), flipped(heads_weight, 3, 3)
    )
    state_grad_columns, inputs_grad_columns = gru_backward(
        final_grad,
        columns_kept,
        weights,
        grads,
        COLUMNS_GATES,
        COLUMNS_CANDIDATE,
        5,
        1,
        local_pad,
    )
    inputs_grad_columns = jnp.concatenate(
        [
            inputs_grad_columns[..., :flow_start],
            inputs_grad_columns[..., flow_start:] + flow_grad,
        ],
        -1,
    )
    state_back, inputs_back = (
        lax.all_to_all(
            state_grad_columns.astype(jnp.bfloat16),
            SPACE,
            split_axis=1,
            concat_axis=2,
            tiled=True,
        ),
        lax.all_to_all(
            inputs_grad_columns.astype(jnp.bfloat16),
            SPACE,
            split_axis=1,
            concat_axis=2,
            tiled=True,
        ),
    )
    net_grad, inputs_grad = gru_backward(
        state_back.astype(jnp.float32),
        rows_kept,
        weights,
        grads,
        ROWS_GATES,
        ROWS_CANDIDATE,
        1,
        5,
        local_pad,
    )
    inputs_total = inputs_grad + inputs_back.astype(jnp.float32)
    motion_grad = (inputs_total[..., CTX:flow_start] * slope(motion_pre)).astype(jnp.bfloat16)
    record(grads, MOTION_MIX, joint_stack, motion_grad)
    joint_grad = apply(
        patches(row_pad(motion_grad, 3), 3, 3), flipped(weights[MOTION_MIX], 3, 3)
    )
    branch_grad = jnp.concatenate(
        [
            joint_grad[..., :C2] * slope(corr_mix_pre),
            joint_grad[..., C2:] * slope(flow_mix_pre),
        ],
        -1,
    ).astype(jnp.bfloat16)
    record(grads, CORR_MIX, corr_stack, branch_grad[..., :C2])
    record(grads, FLOW_MIX, flow_mix_stack, branch_grad[..., C2:])
    branch_pad = row_pad(branch_grad, 3)
    corr_one_grad = apply(
        patches(branch_pad[..., :C2], 3, 3), flipped(weights[CORR_MIX], 3, 3)
    )
    flow_one_grad = apply(
        patches(branch_pad[..., C2:], 3, 3), flipped(weights[FLOW_MIX], 3, 3)
    )
    corr_pre_grad = (corr_one_grad * slope(corr_pre)).astype(jnp.bfloat16)
    flow_pre_grad = (flow_one_grad * slope(flow_pre)).astype(jnp.bfloat16)
    record(grads, CORR_IN, corr, corr_pre_grad)
    record(grads, FLOW_IN, flow_stack, flow_pre_grad)
    corr_grads = apply_back(corr_pre_grad, weights[CORR_IN])
    flow_total = inputs_total[..., flow_start:] + apply(
        patches(row_pad(flow_pre_grad, 7), 7, 7), flipped(weights[FLOW_IN], 7, 7)
    )
    flow_grads = jnp.transpose(flow_total, (0, 3, 1, 2))
    net_grads = net_grad
    context_grads = inputs_total[..., :CTX]
    count = params.shape[0]
    local = pack(grads, 3 * count // (LANES * 16) * 16 + BLOCK)
    collected = reduce_grads(local, lax.axis_size(SPACE), count)
    losses = lax.psum(partials, SPACE) / divisor
    return (
        nets_out,
        flows_out,
        masks_out,
        losses,
        collected,
        net_grads,
        context_grads,
        corr_grads,
        flow_grads,
    )


BATCH = 2
ROWS = 5
WIDE = 128
TALL = 40
COLS = 16
AREA = 640
PITCH = 20
SPREAD = TALL * PITCH
SPAN = 896
EDGE = 64


def mm(a, b):
    return jnp.dot(a, b, preferred_element_type=jnp.float32)


def nt(a, b):
    return lax.dot_general(a, b, (((1,), (1,)), ((), ())), preferred_element_type=jnp.float32)


def tn(a, b):
    return lax.dot_general(a, b, (((0,), (0,)), ((), ())), preferred_element_type=jnp.float32)


def half_of(value):
    return value.astype(jnp.bfloat16)


def full_of(value):
    return value.astype(jnp.float32)


def quarter_of(value):
    return half_of(0.25 * full_of(value))


def lane_index(shape):
    return lax.broadcasted_iota(jnp.int32, shape, 1)


def row_index(shape):
    return lax.broadcasted_iota(jnp.int32, shape, 0)


def act_slope(pre):
    sigma = jax.nn.sigmoid(pre)
    act = pre * sigma
    return act, sigma + act * (1.0 - sigma)


def flat_rows():
    table = shapes()
    offset = 0
    starts = {}
    for name, height, width in table:
        starts[name] = offset // LANES
        offset += height * width
    bias_row = offset // LANES
    spots = {}
    inner = 0
    for name, height, width in table:
        spots[name] = inner
        inner += width
    return starts, bias_row, spots, inner


def cast_rows(dst, to, src, start, count, kind):
    big = 256
    whole = count // big

    if whole > 1:

        def body(step, carry):
            at = pl.multiple_of(step * big, big)
            dst[pl.ds(to + at, big), :] = src[pl.ds(start + at, big), :].astype(kind)
            return carry

        lax.fori_loop(0, whole, body, 0)
    elif whole == 1:
        dst[to : to + big, :] = src[start : start + big, :].astype(kind)
    rest = count - whole * big
    if rest:
        low = whole * big
        dst[to + low : to + count, :] = src[start + low : start + count, :].astype(kind)


MARGIN = 16


def stage_plan(count, start, rows):
    stop = start + rows
    pieces, fill = [], 0
    for rank in range(4):
        first = rank * count // LANES
        last = -(-(rank + 1) * count // LANES)
        low, high = max(start, first), min(stop, last)
        if low >= high:
            continue
        place = low - first + rank * BLOCK
        base = place // 16 * 16
        length = -(-(place - base + high - low) // 16) * 16
        to = MARGIN + low - start - (place - base)
        seam = MARGIN + low - start if start < first else None
        pieces.append((base, length, fill, to, seam))
        fill += length
    return pieces


class Stages:
    def __init__(self, v, count, segments):
        self.v, self.at = v, 0
        self.plans = [stage_plan(count, start, rows) for start, rows in segments]
        self.fetch(0)

    def copies(self, index):
        v, slot = self.v, index % 2
        return [
            pltpu.make_async_copy(
                v.gathered.at[base : base + length], v.stage.at[slot, fill : fill + length], v.ssem.at[slot, number]
            )
            for number, (base, length, fill, to, seam) in enumerate(self.plans[index])
        ]

    def fetch(self, index):
        if index < len(self.plans):
            for copy in self.copies(index):
                copy.start()

    def take(self):
        v, index = self.v, self.at
        self.at += 1
        for copy in self.copies(index):
            copy.wait()
        self.fetch(index + 1)
        for base, length, fill, to, seam in self.plans[index]:
            saved = None if seam is None else v.flat[seam : seam + 1, :]
            cast_rows(v.flat, to, v.stage.at[index % 2], fill, length, jnp.float32)
            if seam is not None:
                v.flat[seam : seam + 1, :] = v.flat[seam : seam + 1, :] + saved


def strided(ref, start, count, stride):
    if stride == 1:
        return ref[pl.ds(start, count), :]
    return ref[pl.ds(start, count, stride=stride), :]


def unpack_pairs(flat, row, count, dst, to, lane):
    dst[to : to + count, lane : lane + LANES] = half_of(strided(flat, MARGIN + 2 * row, count, 2))
    dst[to : to + count, lane + LANES : lane + 2 * LANES] = half_of(strided(flat, MARGIN + 2 * row + 1, count, 2))


def pack_pairs(flat, row, count, low, high):
    flat[pl.ds(MARGIN + 2 * row, count, stride=2), :] = low
    flat[pl.ds(MARGIN + 2 * row + 1, count, stride=2), :] = high


def split_pick(which, quarter):
    source = lax.broadcasted_iota(jnp.int32, (LANES, HEAD), 0)
    target = lax.broadcasted_iota(jnp.int32, (LANES, HEAD), 1)
    return jnp.where(source == 2 * (target - 64 * quarter) + which, 1.0, 0.0).astype(jnp.bfloat16)


def unpack_all(v, count):
    starts, bias_row, spots, inner = flat_rows()
    flat = v.flat
    order = (
        (CORR_IN, 648), (CORR_MIX, 3456), (FLOW_IN, 98), (FLOW_MIX, 576), (MOTION_MIX, 2268),
        (ROWS_GATES, 3840), (ROWS_CANDIDATE, 1920), (COLUMNS_GATES, 3840), (COLUMNS_CANDIDATE, 1920),
        (FLOW_HIDDEN, 2304), (MASK_HIDDEN, 2304), (FLOW_OUT, 36), (MASK_OUT, 1152),
    )
    stages = Stages(v, count, [(starts[name], rows) for name, rows in order] + [(bias_row, 21)])

    def stage(name, rows):
        assert order[stages.at] == (name, rows)
        stages.take()

    stage(CORR_IN, 648)
    unpack_pairs(flat, 0, 324, v.w_ci, 0, 0)

    stage(CORR_MIX, 3456)
    lane = lane_index((128, LANES))
    low_half = lane < 64

    def mix_step(step, carry):
        at = MARGIN + 384 * step
        r0, r1, r2 = (strided(flat, at + i, 128, 3) for i in range(3))
        r1s, r2s = pltpu.roll(r1, 64, 1), pltpu.roll(r2, 64, 1)
        v.pair_a[pl.ds(0, 128, stride=2), :] = r0
        v.pair_a[pl.ds(1, 128, stride=2), :] = jnp.where(low_half, r1s, r2s)
        v.pair_b[pl.ds(0, 128, stride=2), :] = jnp.where(low_half, r1, 0.0)
        v.pair_b[pl.ds(1, 128, stride=2), :] = jnp.where(low_half, r2s, 0.0)
        to = pl.ds(pl.multiple_of(step * 256, 256), 256)
        v.w_cm[to, 0:128] = half_of(v.pair_a[...])
        v.w_cm[to, 128:256] = half_of(v.pair_b[...])
        return carry

    lax.fori_loop(0, 9, mix_step, 0)

    stage(FLOW_IN, 98)
    v.flow_tmp[...] = jnp.zeros_like(v.flow_tmp)
    for across in range(7):
        for comp in range(2):
            v.flow_tmp[pl.ds(across * 16 + comp, 7, stride=2), :] = strided(
                flat, MARGIN + across * 2 + comp, 7, 14
            )
    v.w_fi[...] = half_of(v.flow_tmp[...])

    stage(FLOW_MIX, 576)
    for step in range(9):
        r0 = strided(flat, MARGIN + 64 * step, 64, 1)
        high_half = lane_index((64, LANES)) >= 64
        v.pair_a[pl.ds(0, 64, stride=2), :] = jnp.where(high_half, pltpu.roll(r0, 64, 1), 0.0)
        v.pair_a[pl.ds(1, 64, stride=2), :] = jnp.where(high_half, r0, 0.0)
        v.w_fm[step * 128 : (step + 1) * 128, :] = half_of(v.pair_a[0:128, :])

    stage(MOTION_MIX, 2268)
    lane36 = lane_index((36, LANES))
    for i in range(64):
        if i == 0:
            value = strided(flat, MARGIN, 36, 63)
        elif i == 63:
            value = pltpu.roll(strided(flat, MARGIN + 62, 36, 63), 126, 1)
        else:
            low = pltpu.roll(strided(flat, MARGIN + i - 1, 36, 63), 2 * i, 1)
            high = pltpu.roll(strided(flat, MARGIN + i, 36, 63), 2 * i, 1)
            value = jnp.where(lane36 < 2 * i, low, high)
        v.mm_tmp[pl.ds(i, 36, stride=64), :] = jnp.where(lane36 < 126, value, 0.0)
    for step in range(9):
        v.w_mm[step * 256 : (step + 1) * 256, :] = half_of(v.mm_tmp[step * 256 : (step + 1) * 256, :])

    for gates_name, cand_name, w_i, w_s in ((ROWS_GATES, ROWS_CANDIDATE, v.w_ri, v.w_rs), (COLUMNS_GATES, COLUMNS_CANDIDATE, v.w_li, v.w_ls)):
        stage(gates_name, 3840)
        for tap in range(5):
            unpack_pairs(flat, tap * 384, 128, w_s, tap * 128, 0)
            unpack_pairs(flat, tap * 384 + 128, 256, w_i, tap * 256, 0)
        stage(cand_name, 1920)
        for tap in range(5):
            w_s[tap * 128 : (tap + 1) * 128, 256:384] = half_of(strided(flat, MARGIN + tap * 384, 128, 1))
            w_i[tap * 256 : (tap + 1) * 256, 256:384] = half_of(strided(flat, MARGIN + tap * 384 + 128, 256, 1))

    for name, lane0 in ((FLOW_HIDDEN, 0), (MASK_HIDDEN, 256)):
        stage(name, 2304)
        for tap in range(9):
            unpack_pairs(flat, tap * 128, 128, v.w_h, tap * 128, lane0)

    stage(FLOW_OUT, 36)
    v.fo_tmp[...] = jnp.zeros_like(v.fo_tmp)
    for which in range(2):
        total = jnp.zeros((9, HEAD), jnp.float32)
        for quarter in range(4):
            total = total + mm(half_of(strided(flat, MARGIN + quarter, 9, 4)), split_pick(which, quarter))
        v.fo_tmp[pl.ds(which, 9, stride=2), 0:128] = total[:, :128]
        v.fo_tmp2[pl.ds(which, 9, stride=2), 0:128] = total[:, 128:]
    v.fo_tmp2[18:32, :] = jnp.zeros((14, LANES), jnp.float32)
    v.w_fo[:, 0:128] = half_of(v.fo_tmp[...])
    v.w_fo[:, 128:256] = half_of(v.fo_tmp2[...])

    stage(MASK_OUT, 1152)
    r = [strided(flat, MARGIN + i, 128, 9) for i in range(9)]
    rs = [pltpu.roll(r[i], 64, 1) for i in range(4, 9)]
    for block in range(5):
        even = r[block] if block < 4 else jnp.where(low_half, r[4], 0.0)
        odd = jnp.where(low_half, rs[block], rs[block + 1]) if block < 4 else jnp.where(low_half, rs[4], 0.0)
        v.pair_a[pl.ds(0, 128, stride=2), :] = even
        v.pair_a[pl.ds(1, 128, stride=2), :] = odd
        v.w_mo[:, block * 128 : (block + 1) * 128] = half_of(v.pair_a[...])

    stages.take()
    place = 0
    lane1 = lane_index((1, LANES))
    for name, height, width in shapes():
        spot = spots[name]
        for block in range(-(-width // LANES)):
            at = spot + block * LANES
            row, shift = at // LANES, at % LANES
            value = flat[MARGIN + row : MARGIN + row + 1, :]
            if shift:
                after = flat[MARGIN + row + 1 : MARGIN + row + 2, :]
                value = jnp.where(
                    lane1 < LANES - shift, pltpu.roll(value, LANES - shift, 1), pltpu.roll(after, LANES - shift, 1)
                )
            left = width - block * LANES
            if left < LANES:
                value = jnp.where(lane1 < left, value, 0.0)
            if name == FLOW_MIX:
                value = pltpu.roll(value, 64, 1)
            v.bias[place : place + 1, :] = value
            place += 1


BIAS_AT = {}
_place = 0
for _name, _height, _width in shapes():
    BIAS_AT[_name] = _place
    _place += -(-_width // 128)
BIAS_ROWS = 32


def bias_of(v, name, blocks):
    at = BIAS_AT[name]
    return jnp.concatenate([v.bias[at + i : at + i + 1, :] for i in range(blocks)], axis=1)


class Halo:
    def __init__(self, v, sem, up_src, down_src, from_down, from_up):
        up = {SPACE: jnp.maximum(v.spot - 1, 0)}
        down = {SPACE: jnp.minimum(v.spot + 1, v.space - 1)}
        self.v = v
        self.up = remote(up_src, from_down, v.hsend.at[sem, 0], v.hrecv.at[sem, 0], up)
        self.down = remote(down_src, from_up, v.hsend.at[sem, 1], v.hrecv.at[sem, 1], down)

    def start(self):
        pl.when(self.v.spot > 0)(self.up.start)
        pl.when(self.v.spot < self.v.space - 1)(self.down.start)

    def receive(self):
        pl.when(self.v.spot < self.v.space - 1)(self.up.wait_recv)
        pl.when(self.v.spot > 0)(self.down.wait_recv)

    def sent(self):
        pl.when(self.v.spot > 0)(self.up.wait_send)
        pl.when(self.v.spot < self.v.space - 1)(self.down.wait_send)


class Swap:
    def __init__(self, v, sem, src, dst, broadcast=False):
        self.v, self.sem, self.src, self.dst, self.broadcast = v, sem, src, dst, broadcast

    def copy(self, step):
        v = self.v
        to = lax.rem(v.spot + step, v.space)
        src = self.src if self.broadcast else self.src.at[to]
        return remote(src, self.dst.at[v.spot], v.asend.at[self.sem, step], v.arecv.at[self.sem, step], {SPACE: to})

    def each(self, what):
        def body(step, carry):
            what(self.copy(step))
            return carry

        lax.fori_loop(1, self.v.space, body, 0)

    def start(self):
        self.each(lambda copy: copy.start())

    def receive(self):
        self.each(lambda copy: copy.wait_recv())

    def sent(self):
        self.each(lambda copy: copy.wait_send())


def spread_rows(v, b, acts, rows, dst, row0, width, backward=False):
    x = lax.rem(row_index((rows, LANES)), WIDE)
    for block, act in enumerate(acts):
        v.tmp[8 : 8 + rows, :] = act
        for tap in range(3):
            d = (1 - tap) if backward else (tap - 1)
            value = act if d == 0 else v.tmp[8 + d : 8 + d + rows, :]
            if d == -1:
                value = jnp.where(x > 0, value, 0.0)
            if d == 1:
                value = jnp.where(x < WIDE - 1, value, 0.0)
            lane = tap * width + block * LANES
            if backward:
                dst[row0 : row0 + rows, b + lane : b + lane + LANES] = half_of(value)
            else:
                dst[b, row0 : row0 + rows, lane : lane + LANES] = half_of(value)


def spread_five(v, value, dst, lane_of, backward=False):
    x = lax.rem(row_index((AREA, LANES)), WIDE)
    v.tmp[8 : 8 + AREA, :] = value
    for tap in range(5):
        d = (2 - tap) if backward else (tap - 2)
        moved = value if d == 0 else v.tmp[8 + d : 8 + d + AREA, :]
        if d:
            moved = jnp.where((x + d >= 0) & (x + d < WIDE), moved, 0.0)
        if backward:
            taps_part(v, tap, lane_of, lane_of + LANES)[...] = half_of(moved)
        else:
            lane = lane_of(tap)
            dst[:, lane : lane + LANES] = half_of(moved)


def forward_rows(v):
    spot, last = v.spot, v.space - 1
    rows9 = lax.div(row_index((9 * WIDE, LANES)), WIDE)
    rows7 = lax.div(row_index((7 * WIDE, LANES)), WIDE)
    seen9 = (rows9 + spot * ROWS >= 2) & (rows9 + spot * ROWS < TALL + 2)
    seen7 = (rows7 + spot * ROWS >= 1) & (rows7 + spot * ROWS < TALL + 1)

    def image(b, carry):
        pieces = (
            (v.corr_up, 0, 256, 0, spot > 0),
            (v.corr, 256, 640, 2, None),
            (v.corr_down, 896, 256, 7, spot < last),
        )
        bias = bias_of(v, CORR_IN, 2)
        for ref, row0, rows, ext, seen in pieces:
            act, slope = act_slope(mm(ref[b], v.w_ci[...]) + bias)
            if seen is None:
                v.slope_ci[b] = half_of(slope)
            else:
                act = jnp.where(seen, act, 0.0)
            spread_rows(v, b, (act[:, :128], act[:, 128:]), rows, v.hx_c, row0, 256)

        up = jnp.where(spot > 0, v.flow_up[b], 0.0)
        down = jnp.where(spot < last, v.flow_down[b], 0.0)
        lane = lane_index((16, LANES))
        v.fs[...] = jnp.zeros_like(v.fs)
        for across in range(7):
            d = across - 3
            for part, value in enumerate((up, v.flow[b], down)):
                moved = value
                if d:
                    moved = pltpu.roll(value, (-d) % LANES, 1)
                    moved = jnp.where((lane + d >= 0) & (lane + d < WIDE), moved, 0.0)
                v.fs[across, part * 10 : part * 10 + 10, :] = moved[0:10, :]
        for y in range(9):
            for across in range(7):
                v.flow_tmp[across * 16 : across * 16 + 16, :] = v.fs[across, 2 * y : 2 * y + 16, :]
            v.xt[b, :, y * 128 : (y + 1) * 128] = half_of(v.flow_tmp[...])
        act, slope = act_slope(tn(v.xt[b], v.w_fi[...]) + bias_of(v, FLOW_IN, 1))
        v.slope_fi[b] = half_of(slope[256:896])
        spread_rows(v, b, (jnp.where(seen9, act, 0.0),), 9 * WIDE, v.hx_f, 0, 128)

        pre = bias_of(v, CORR_MIX, 2)
        flow_pre = bias_of(v, FLOW_MIX, 1)
        for a in range(3):
            pre = pre + mm(v.hx_c[b, a * 128 : a * 128 + 896, :], v.w_cm[a * 768 : (a + 1) * 768, :])
            flow_pre = flow_pre + mm(v.hx_f[b, a * 128 : a * 128 + 896, :], v.w_fm[a * 384 : (a + 1) * 384, :])
        low, low_slope = act_slope(pre[:, :128])
        high, high_slope = act_slope(pre[:, 128:] + flow_pre)
        v.slope_j[b, :, 0:128] = half_of(low_slope)
        v.slope_j[b, :, 128:256] = half_of(high_slope)
        spread_rows(v, b, (jnp.where(seen7, low, 0.0), jnp.where(seen7, high, 0.0)), 896, v.hx_j, 0, 256)

        pre = bias_of(v, MOTION_MIX, 1)
        for a in range(3):
            pre = pre + mm(v.hx_j[b, a * 128 : a * 128 + 640, :], v.w_mm[a * 768 : (a + 1) * 768, :])
        act, slope = act_slope(pre)
        v.slope_m[b] = half_of(jnp.where(lane_index((AREA, LANES)) < 126, slope, 0.0))
        pick = jnp.where(lane_index((16, LANES)) == row_index((16, LANES)) + 126, 1.0, 0.0)
        own_flow = v.flow[b]
        for y in range(ROWS):
            v.tmp2[0:2, :] = own_flow[2 * y : 2 * y + 2, :]
            v.tmp2[2:16, :] = jnp.zeros((14, LANES), jnp.float32)
            v.motion[b, y * 128 : (y + 1) * 128, :] = act[y * 128 : (y + 1) * 128, :] + tn(
                half_of(v.tmp2[0:16, :]), half_of(pick)
            )
        v.motion[b] = full_of(half_of(v.motion[b]))
        pack_rows(v, v.motion, b, v.a_motion)
        return carry

    lax.fori_loop(0, BATCH, image, 0)
    v.swap_motion.start()

    def gru(b, carry):
        at = pl.ds(pl.multiple_of(b * AREA, AREA), AREA)
        s = full_of(v.net[b])
        spread_five(v, full_of(v.context[b]), v.xi.at[at], lambda t: t * 256)
        spread_five(v, v.motion[b], v.xi.at[at], lambda t: t * 256 + 128)
        spread_five(v, s, v.xs.at[at], lambda t: t * 128)
        both = mm(v.xi[at, :], v.w_ri[...])
        gates = jax.nn.sigmoid(both[:, :256] + mm(v.xs[at, :], v.w_rs[:, :256]) + bias_of(v, ROWS_GATES, 2))
        update, reset = gates[:, :128], gates[:, 128:]
        v.ru[b] = update
        v.rr[b] = reset
        spread_five(v, full_of(half_of(reset * s)), v.xr.at[at], lambda t: t * 128)
        cand = jnp.tanh(both[:, 256:] + mm(v.xr[at, :], v.w_rs[:, 256:]) + bias_of(v, ROWS_CANDIDATE, 1))
        v.rc[b] = cand
        v.state[b] = s + update * (cand - s)
        pack_rows(v, v.state, b, v.a_state)
        return carry

    lax.fori_loop(0, BATCH, gru, 0)
    v.swap_state.start()


def pack_rows(v, src, b, dst):
    def peer(t, carry):
        for y in range(ROWS):
            at = pl.multiple_of(y * WIDE + t * COLS, COLS)
            dst[t, b, y * COLS : (y + 1) * COLS, :] = half_of(src[b, pl.ds(at, COLS), :])
        return carry

    lax.fori_loop(0, v.space, peer, 0)


def take_own(v, src, dst):
    dst[v.spot] = src[v.spot]


def columns_in(v):
    def zero(b, carry):
        for ref, wide in ((v.xc, 384), (v.xcr, 128), (v.gc, 384)):
            for low in (0, 32 + AREA):
                ref[b, low : low + 32, :] = jnp.zeros((32, wide), jnp.bfloat16)
        return carry

    lax.fori_loop(0, BATCH, zero, 0)

    def peer(t, carry):
        at = pl.ds(pl.multiple_of(32 + t * ROWS * COLS, 16), ROWS * COLS)
        for b in range(BATCH):
            v.xc[b, at, 0:128] = v.b_state[t, b]
            v.xc[b, at, 128:256] = v.b_context[t, b]
            v.xc[b, at, 256:384] = v.b_motion[t, b]
        return carry

    lax.fori_loop(0, v.space, peer, 0)


FX_ROWS = 16 + (TALL + 2) * PITCH


def fx_base(b):
    return pl.multiple_of(b * FX_ROWS, 8)


def columns_forward(v):
    def gru(b, carry):
        s = full_of(v.xc[b, 32 : 32 + AREA, 0:128])
        both = bias_of(v, COLUMNS_GATES, 2)
        both = jnp.concatenate([both, bias_of(v, COLUMNS_CANDIDATE, 1)], axis=1)
        gates = 0.0
        for t in range(5):
            rows = slice(t * COLS, t * COLS + AREA)
            both = both + mm(v.xc[b, rows, 128:384], v.w_li[t * 256 : (t + 1) * 256, :])
            gates = gates + mm(v.xc[b, rows, 0:128], v.w_ls[t * 128 : (t + 1) * 128, 0:256])
        gates = jax.nn.sigmoid(gates + both[:, :256])
        update, reset = gates[:, :128], gates[:, 128:]
        v.lu[b] = update
        v.lr[b] = reset
        v.xcr[b, 32 : 32 + AREA, :] = half_of(reset * s)
        cand = both[:, 256:]
        for t in range(5):
            rows = slice(t * COLS, t * COLS + AREA)
            cand = cand + mm(v.xcr[b, rows, :], v.w_ls[t * 128 : (t + 1) * 128, 256:384])
        cand = jnp.tanh(cand)
        v.lc[b] = cand
        final = s + update * (cand - s)
        v.out_net[b] = half_of(final)
        v.final[...] = full_of(half_of(final))
        fx = fx_base(b)
        v.mm_tmp[pl.ds(fx, FX_ROWS), :] = jnp.zeros((FX_ROWS, LANES), jnp.float32)
        for x in range(COLS):
            v.mm_tmp[pl.ds(fx + 8 + PITCH + 2 + x, TALL, stride=PITCH), :] = v.final[pl.ds(x, TALL, stride=COLS), :]
        for j in range(2):
            v.e_left[b, j, 0:TALL, :] = half_of(v.final[pl.ds(j, TALL, stride=COLS), :])
            v.e_right[b, j, 0:TALL, :] = half_of(v.final[pl.ds(COLS - 2 + j, TALL, stride=COLS), :])
        return carry

    lax.fori_loop(0, BATCH, gru, 0)
    v.halo_final.start()


def ring_masks(v, shape):
    x = lax.rem(row_index(shape), PITCH)
    place = v.spot * COLS + x - 2
    seen = (place >= 0) & (place < WIDE) & (x >= 1) & (x < PITCH - 1)
    own = (x >= 2) & (x < PITCH - 2)
    return seen, own


def mask_gradient(v):
    def image(b, carry):
        value = nt(quarter_of(v.grad_mask[b]), v.w_mo[:, 0:MASK])
        for block in range(2):
            v.final[...] = value[:, block * 128 : (block + 1) * 128]
            v.tmp[0:SPREAD, :] = jnp.zeros((SPREAD, LANES), jnp.float32)
            for x in range(COLS):
                v.tmp[pl.ds(2 + x, TALL, stride=PITCH), :] = v.final[pl.ds(x, TALL, stride=COLS), :]
            v.fm[b, block] = half_of(v.tmp[0:SPREAD, :])
            v.m_left[b, block, 0:TALL, :] = half_of(v.final[pl.ds(0, TALL, stride=COLS), :])
            v.m_right[b, block, 0:TALL, :] = half_of(v.final[pl.ds(COLS - 1, TALL, stride=COLS), :])
        return carry

    lax.fori_loop(0, BATCH, image, 0)
    v.halo_mask.start()


def heads_part(v, b, tap):
    ref = v.hx_c if tap < 6 else v.hx_f
    lane = tap % 6 * 128
    return ref.at[b, 0:SPREAD, lane : lane + 128]


def taps_part(v, t, low, high):
    ref = v.hx_f if t % 3 == 2 else v.hx_c
    lane = (t % 3) % 2 * 384
    return ref.at[t // 3, 0:AREA, lane + low : lane + high]


def heads(v):
    spot, last = v.spot, v.space - 1
    v.halo_final.receive()
    v.halo_mask.receive()
    v.swap_count.receive()
    v.counts[v.spot] = v.count_out[...]
    counts = jnp.sum(v.counts[...], axis=0)
    seen, own = ring_masks(v, (SPREAD, LANES))
    steps = [(a - 1) * PITCH + (c - 1) for a in range(3) for c in range(3)]
    plane = jnp.float32(TALL * WIDE)

    def image(b, carry):
        fx = fx_base(b)
        for j in range(2):
            left = jnp.where(spot > 0, full_of(v.f_left[b, j, 0:TALL, :]), 0.0)
            right = jnp.where(spot < last, full_of(v.f_right[b, j, 0:TALL, :]), 0.0)
            v.mm_tmp[pl.ds(fx + 8 + PITCH + j, TALL, stride=PITCH), :] = left
            v.mm_tmp[pl.ds(fx + 8 + PITCH + PITCH - 2 + j, TALL, stride=PITCH), :] = right
        for block in range(2):
            left = jnp.where(spot > 0, full_of(v.n_left[b, block, 0:TALL, :]), 0.0)
            right = jnp.where(spot < last, full_of(v.n_right[b, block, 0:TALL, :]), 0.0)
            v.tmp[0:SPREAD, :] = full_of(v.fm[b, block])
            v.tmp[pl.ds(1, TALL, stride=PITCH), :] = left
            v.tmp[pl.ds(PITCH - 2, TALL, stride=PITCH), :] = right
            v.fm[b, block] = half_of(v.tmp[0:SPREAD, :])
        for tap in range(9):
            at = 8 + PITCH + steps[tap]
            heads_part(v, b, tap)[...] = half_of(v.mm_tmp[pl.ds(fx + at, SPREAD), :])
        for part in range(2):
            name = (FLOW_HIDDEN, MASK_HIDDEN)[part]
            lanes = slice(part * 256, (part + 1) * 256)
            act, slope = act_slope(mm(v.hx_c[b, 0:SPREAD, :], v.w_h[0:768, lanes]) + mm(v.hx_f[b, 0:SPREAD, :], v.w_h[768:1152, lanes]) + bias_of(v, name, 2))
            v.slope_h[b, :, lanes] = half_of(slope)
            if part == 0:
                for block in range(2):
                    value = jnp.where(seen, act[:, block * 128 : (block + 1) * 128], 0.0)
                    v.feat[b, 0:SPREAD, block * 128 : (block + 1) * 128] = half_of(value)
                v.feat[b, SPREAD:SPAN, :] = jnp.zeros((SPAN - SPREAD, HEAD), jnp.bfloat16)
            else:
                for block in range(2):
                    v.tmp[0:SPREAD, :] = act[:, block * 128 : (block + 1) * 128]
                    for x in range(COLS):
                        v.final[pl.ds(x, TALL, stride=COLS), :] = v.tmp[pl.ds(2 + x, TALL, stride=PITCH), :]
                    v.mf[b, :, block * 128 : (block + 1) * 128] = half_of(v.final[...])
        moved = nt(v.w_fo[...], v.feat[b])
        v.zt[...] = moved
        delta = jnp.zeros((8, SPAN), jnp.float32)
        for tap in range(9):
            pair = jnp.concatenate([v.zt[2 * tap : 2 * tap + 2, :], jnp.zeros((6, SPAN), jnp.float32)], axis=0)
            delta = delta + pltpu.roll(pair, (-steps[tap]) % SPAN, 1)
        v.tmp[0:SPAN, :] = jnp.zeros((SPAN, LANES), jnp.float32)
        v.final[...] = full_of(v.xc[b, 32 : 32 + AREA, 256:384])
        for x in range(COLS):
            v.tmp[pl.ds(2 + x, TALL, stride=PITCH), :] = v.final[pl.ds(x, TALL, stride=COLS), :]
        pick = jnp.where(lane_index((16, LANES)) == row_index((16, LANES)) + 126, 1.0, 0.0)
        base = nt(half_of(pick), half_of(v.tmp[0:SPAN, :]))[0:8, :]
        bias = v.bias[BIAS_AT[FLOW_OUT] : BIAS_AT[FLOW_OUT] + 1, :]
        first = row_index((8, SPAN)) == 0
        second = row_index((8, SPAN)) == 1
        shift = jnp.where(first, bias[0:1, 0:1], jnp.where(second, bias[0:1, 1:2], 0.0))
        new = base + delta + shift
        v.out_flow[b] = new
        error = new - v.target[b]
        root = jnp.sqrt(error * error + 1.0)
        valid = jnp.where(first | second, v.valid[b], 0.0)
        piece = jnp.sum(valid * root)
        divisor = jnp.maximum(v.pick_count(counts, b), 1.0)
        gradient = plane / divisor * valid * error / root
        v.dg[b] = gradient
        v.losses[...] = jnp.where(row_index((8, LANES)) == b, piece, v.losses[...])
        return carry

    v.losses[...] = jnp.zeros((8, LANES), jnp.float32)
    lax.fori_loop(0, BATCH, image, 0)
    v.halo_dg.start()
    v.swap_loss.start()


def mask_output(v):
    def image(b, carry):
        for block in range(5):
            wide = min(128, MASK - block * 128)
            lanes = slice(block * 128, block * 128 + wide)
            at = BIAS_AT[MASK_OUT] + block
            value = mm(v.mf[b], v.w_mo[:, lanes]) + v.bias[at : at + 1, 0:wide]
            v.out_mask[b, :, lanes] = half_of(0.25 * value)
        return carry

    lax.fori_loop(0, BATCH, image, 0)


def heads_back(v):
    spot, last = v.spot, v.space - 1
    seen, own = ring_masks(v, (SPREAD, LANES))
    steps = [(a - 1) * PITCH + (c - 1) for a in range(3) for c in range(3)]
    v.halo_dg.receive()

    def zb(c, low, rows):
        at = c * (2 * EDGE + SPREAD) + low
        return v.mm_tmp.at[at : at + rows]

    def image(b, carry):
        x = lax.rem(lane_index((8, SPAN)), PITCH)
        own_dg = v.dg[b]
        left = jnp.where((x < 2) & (spot > 0), pltpu.roll(v.dg_left[b], SPAN - COLS, 1), 0.0)
        right = jnp.where((x >= PITCH - 2) & (spot < last), pltpu.roll(v.dg_right[b], COLS, 1), 0.0)
        inside = lane_index((8, SPAN)) < SPREAD
        wide_dg = full_of(half_of(jnp.where(inside, own_dg + left + right, 0.0)))
        own_low = full_of(half_of(own_dg))
        v.dt[...] = jnp.zeros_like(v.dt)
        v.dto[...] = jnp.zeros_like(v.dto)
        for tap in range(9):
            v.dt[2 * tap : 2 * tap + 2, :] = pltpu.roll(wide_dg, steps[tap] % SPAN, 1)[0:2, :]
            v.dto[2 * tap : 2 * tap + 2, :] = pltpu.roll(own_low, steps[tap] % SPAN, 1)[0:2, :]
        v.dtb[b] = half_of(v.dto[...])
        from_flow = tn(half_of(v.dt[...]), v.w_fo[...])
        for block in range(4):
            lanes = slice(block * 128, (block + 1) * 128)
            value = from_flow[0:SPREAD, lanes] if block < 2 else full_of(v.fm[b, block - 2])
            value = value * full_of(v.slope_h[b, :, lanes])
            v.hgo[b, :, lanes] = half_of(jnp.where(seen, value, 0.0))
        total = jnp.zeros((SPREAD, LANES), jnp.float32)
        for a in range(3):
            value = nt(v.hgo[b], v.w_h[a * 384 : (a + 1) * 384, :])
            for c in range(3):
                zb(c, EDGE, SPREAD)[...] = value[:, c * 128 : (c + 1) * 128]
            for c in range(3):
                at = EDGE - steps[a * 3 + c]
                total = total + zb(c, at, SPREAD)[...]
        for block in range(4):
            lanes = slice(block * 128, (block + 1) * 128)
            v.hgo[b, :, lanes] = half_of(jnp.where(own, full_of(v.hgo[b, :, lanes]), 0.0))
        v.tmp[0:SPREAD, :] = total
        for x in range(COLS):
            v.final[pl.ds(x, TALL, stride=COLS), :] = v.tmp[pl.ds(2 + x, TALL, stride=PITCH), :]
        r = v.final[...] + full_of(v.grad_net[b])

        s = full_of(v.xc[b, 32 : 32 + AREA, 0:128])
        update, reset, cand = v.lu[b], v.lr[b], v.lc[b]
        cg = half_of(r * update * (1.0 - cand * cand))
        v.gc[b, 32 : 32 + AREA, 256:384] = cg
        reset_grad = 0.0
        for t in range(5):
            rows = slice((4 - t) * COLS, (4 - t) * COLS + AREA)
            reset_grad = reset_grad + nt(v.gc[b, rows, 256:384], v.w_ls[t * 128 : (t + 1) * 128, 256:384])
        v.gc[b, 32 : 32 + AREA, 0:128] = half_of(r * (cand - s) * update * (1.0 - update))
        v.gc[b, 32 : 32 + AREA, 128:256] = half_of(reset_grad * s * reset * (1.0 - reset))
        state_grad = r * (1.0 - update) + reset_grad * reset
        inputs_grad = 0.0
        for t in range(5):
            rows = slice((4 - t) * COLS, (4 - t) * COLS + AREA)
            state_grad = state_grad + nt(v.gc[b, rows, 0:256], v.w_ls[t * 128 : (t + 1) * 128, 0:256])
            inputs_grad = inputs_grad + nt(v.gc[b, rows, :], v.w_li[t * 256 : (t + 1) * 256, :])
        high = half_of(own_dg)
        low = half_of(own_dg - full_of(high))
        pick = half_of(jnp.where(lane_index((8, LANES)) == row_index((8, LANES)) + 126, 1.0, 0.0))
        v.tmp[0:SPAN, :] = tn(high, pick) + tn(low, pick)
        for x in range(COLS):
            v.final[pl.ds(x, TALL, stride=COLS), :] = v.tmp[pl.ds(2 + x, TALL, stride=PITCH), :]
        v.lu[b] = state_grad
        v.lr[b] = inputs_grad[:, 0:128]
        v.lc[b] = inputs_grad[:, 128:256] + v.final[...]

        def peer(t, carry):
            at = pl.ds(pl.multiple_of(t * ROWS * COLS, 16), ROWS * COLS)
            v.a_state[t, b] = half_of(v.lu[b, at, :])
            v.a_context[t, b] = half_of(v.lr[b, at, :])
            v.a_motion[t, b] = half_of(v.lc[b, at, :])
            return carry

        lax.fori_loop(0, v.space, peer, 0)
        return carry

    for c in range(3):
        zb(c, 0, EDGE)[...] = jnp.zeros((EDGE, LANES), jnp.float32)
        zb(c, EDGE + SPREAD, EDGE)[...] = jnp.zeros((EDGE, LANES), jnp.float32)
    lax.fori_loop(0, BATCH, image, 0)
    v.back_state.start()
    v.back_context.start()
    v.back_motion.start()


def unpack_back(v, src, dst):
    def peer(t, carry):
        for b in range(BATCH):
            value = full_of(src[t, b])
            for y in range(ROWS):
                at = pl.multiple_of(y * WIDE + t * COLS, COLS)
                dst[b, pl.ds(at, COLS), :] = value[y * COLS : (y + 1) * COLS, :]
        return carry

    lax.fori_loop(0, v.space, peer, 0)


def seams():
    starts, bias_row, _, _ = flat_rows()
    tiles = sorted({row // 16 for row in list(starts.values()) + [bias_row, bias_row + 21] if row % 16})
    return {tile: index for index, tile in enumerate(tiles)}


class Flush:
    def __init__(self, v):
        self.v, self.at, self.busy = v, 0, {}
        v.seam[...] = jnp.zeros_like(v.seam)

    def send(self, low, length, base):
        v, slot = self.v, self.at % 2
        self.at += 1
        if slot in self.busy:
            self.busy[slot].wait()
        cast_rows(v.stage.at[slot], 0, v.flat, low, length, jnp.bfloat16)
        copy = pltpu.make_async_copy(
            v.stage.at[slot, 0:length], v.out_flat.at[base : base + length], v.ssem.at[slot, 0]
        )
        copy.start()
        self.busy[slot] = copy

    def layer(self, start, rows):
        v, stop = self.v, start + rows
        low, high = -(-start // 16) * 16, stop // 16 * 16
        tiles = seams()
        if start % 16:
            index, lead = tiles[start // 16], start % 16
            take = min(16 - lead, rows)
            v.seam[index, lead : lead + take, :] = v.flat[MARGIN : MARGIN + take, :]
        if stop % 16 and stop // 16 * 16 >= start:
            index, rest = tiles[stop // 16], stop % 16
            v.seam[index, 0:rest, :] = v.flat[MARGIN + rows - rest : MARGIN + rows, :]
        if high > low:
            self.send(MARGIN + low - start, high - low, low)

    def end(self):
        v = self.v
        for copy in self.busy.values():
            copy.wait()
        tiles = seams()
        count = len(tiles)
        for tile, index in tiles.items():
            v.stage[0, index * 16 : (index + 1) * 16, :] = half_of(v.seam[index])
        top = (max(tiles) + 1) * 16
        left = v.out_flat.shape[0] - top
        v.stage[0, count * 16 : count * 16 + left, :] = jnp.zeros((left, LANES), jnp.bfloat16)
        copies = [
            pltpu.make_async_copy(
                v.stage.at[0, index * 16 : (index + 1) * 16],
                v.out_flat.at[tile * 16 : tile * 16 + 16],
                v.fsem.at[index],
            )
            for tile, index in tiles.items()
        ]
        copies.append(
            pltpu.make_async_copy(
                v.stage.at[0, count * 16 : count * 16 + left], v.out_flat.at[top : top + left], v.fsem.at[count]
            )
        )
        for copy in copies:
            copy.start()
        for copy in copies:
            copy.wait()


def ones_sum(g):
    return mm(jnp.ones((8, g.shape[0]), jnp.bfloat16), g)[0:1, :]


def keep_bias(v, name, value):
    for block in range(-(-value.shape[1] // 128)):
        at = BIAS_AT[name] + block
        v.gbias[at : at + 1, :] = value[:, block * 128 : (block + 1) * 128]


def gradients_gru(v, gates_name, cand_name, parts, g_of):
    starts, _, _, _ = flat_rows()
    total = 0.0
    for b in range(BATCH):
        total = total + ones_sum(g_of(b))
    keep_bias(v, gates_name, total[:, 0:256])
    keep_bias(v, cand_name, total[:, 256:384])

    for t in range(5):
        s_part, i_part, r_part = parts(t)
        state = tn_all(s_part, g_of, 0, 256)
        v.mm_tmp[pl.ds(MARGIN + t * 384, 128), :] = tn_all(r_part, g_of, 256, 384)
        inputs = tn_all(i_part, g_of, 0, 384)
        pack_pairs(v.flat, t * 384, 128, state[:, 0:128], state[:, 128:256])
        pack_pairs(v.flat, t * 384 + 128, 256, inputs[:, 0:128], inputs[:, 128:256])
        v.mm_tmp[pl.ds(MARGIN + t * 384 + 128, 256), :] = inputs[:, 256:384]
    v.flush.layer(starts[gates_name], 3840)
    cast_rows(v.flat, MARGIN, v.mm_tmp, MARGIN, 1920, jnp.float32)
    v.flush.layer(starts[cand_name], 1920)


def tn_all(part, g_of, low, high):
    total = 0.0
    for b in range(BATCH):
        total = total + tn(part(b), g_of(b, low, high))
    return total


def gradients_heads(v):
    starts, _, _, _ = flat_rows()
    total = 0.0
    for b in range(BATCH):
        total = total + ones_sum(v.hgo[b])
    keep_bias(v, FLOW_HIDDEN, total[:, 0:256])
    keep_bias(v, MASK_HIDDEN, total[:, 256:512])
    for name, lane in ((FLOW_HIDDEN, 0), (MASK_HIDDEN, 256)):
        for tap in range(9):
            value = 0.0
            for b in range(BATCH):
                value = value + tn(heads_part(v, b, tap)[...], v.hgo[b, :, lane : lane + 256])
            pack_pairs(v.flat, tap * 128, 128, value[:, 0:128], value[:, 128:256])
        v.flush.layer(starts[name], 2304)

    total = 0.0
    sums = 0.0
    for b in range(BATCH):
        total = total + mm(v.dtb[b], v.feat[b])
        sums = sums + jnp.sum(full_of(half_of(v.dg[b])), axis=1, keepdims=True)
    lane1 = lane_index((1, LANES))
    at = BIAS_AT[FLOW_OUT]
    v.gbias[at : at + 1, :] = jnp.where(lane1 == 0, sums[0:1, :], jnp.where(lane1 == 1, sums[1:2, :], 0.0))
    v.fo_tmp[...] = total[:, 0:128]
    v.fo_tmp2[...] = total[:, 128:256]
    for quarter in range(4):
        value = 0.0
        for which in range(2):
            rows = jnp.concatenate(
                [v.fo_tmp[pl.ds(which, 9, stride=2), :], v.fo_tmp2[pl.ds(which, 9, stride=2), :]], axis=1
            )
            value = value + nt(half_of(rows), split_pick(which, quarter))
        v.flat[pl.ds(MARGIN + quarter, 9, stride=4), :] = value
    v.flush.layer(starts[FLOW_OUT], 36)

    lane = lane_index((128, LANES))
    low_half = lane < 64
    even, odd = [], []
    total = 0.0
    for b in range(BATCH):
        total = total + ones_sum(quarter_of(v.grad_mask[b]))
    for block in range(5):
        wide = min(128, MASK - block * 128)
        at = BIAS_AT[MASK_OUT] + block
        v.gbias[at : at + 1, 0:wide] = total[:, block * 128 : block * 128 + wide]
        value = 0.0
        for b in range(BATCH):
            value = value + tn(v.mf[b], quarter_of(v.grad_mask[b, :, block * 128 : block * 128 + wide]))
        v.pair_a[:, 0:wide] = value
        even.append(v.pair_a[pl.ds(0, 128, stride=2), :])
        odd.append(pltpu.roll(v.pair_a[pl.ds(1, 128, stride=2), :], 64, 1))
    for i in range(4):
        v.flat[pl.ds(MARGIN + i, 128, stride=9), :] = even[i]
    v.flat[pl.ds(MARGIN + 4, 128, stride=9), :] = jnp.where(low_half, even[4], odd[0])
    for i in range(4):
        v.flat[pl.ds(MARGIN + 5 + i, 128, stride=9), :] = jnp.where(low_half, odd[i], odd[i + 1])
    v.flush.layer(starts[MASK_OUT], 1152)


def rows_back(v):
    v.back_state.receive()
    take_own(v, v.a_state, v.b_state)
    unpack_back(v, v.b_state, v.state)
    v.back_context.receive()
    v.back_motion.receive()
    take_own(v, v.a_context, v.b_context)
    take_own(v, v.a_motion, v.b_motion)
    unpack_back(v, v.b_context, v.lr)
    unpack_back(v, v.b_motion, v.lc)

    def image(b, carry):
        at = pl.ds(pl.multiple_of(b * AREA, AREA), AREA)
        r = v.state[b]
        s = full_of(v.net[b])
        update, reset, cand = v.ru[b], v.rr[b], v.rc[b]
        cg = full_of(half_of(r * update * (1.0 - cand * cand)))
        spread_five(v, cg, None, 256, True)
        reset_grad = 0.0
        for t in range(5):
            reset_grad = reset_grad + nt(
                taps_part(v, t, 256, 384)[...], v.w_rs[t * 128 : (t + 1) * 128, 256:384]
            )
        low = full_of(half_of(r * (cand - s) * update * (1.0 - update)))
        high = full_of(half_of(reset_grad * s * reset * (1.0 - reset)))
        spread_five(v, low, None, 0, True)
        spread_five(v, high, None, 128, True)
        v.gr[b] = taps_part(v, 2, 0, 384)[...]
        state_grad = r * (1.0 - update) + reset_grad * reset
        inputs_grad = jnp.concatenate([v.lr[b], v.lc[b]], axis=1)
        for t in range(5):
            state_grad = state_grad + nt(taps_part(v, t, 0, 256)[...], v.w_rs[t * 128 : (t + 1) * 128, 0:256])
            inputs_grad = inputs_grad + nt(taps_part(v, t, 0, 384)[...], v.w_ri[t * 256 : (t + 1) * 256, :])
        v.ru[b] = state_grad
        v.rr[b] = inputs_grad[:, 0:128]
        motion = inputs_grad[:, 128:256]
        grad = half_of(motion * full_of(v.slope_m[b]))
        v.mge[b, 256:896, :] = grad
        high = half_of(motion)
        low = half_of(motion - full_of(high))
        pick = half_of(jnp.where(lane_index((16, LANES)) == row_index((16, LANES)) + 126, 1.0, 0.0))
        v.gf_base[b] = (nt(pick, high) + nt(pick, low))[0:8, :]
        return carry

    lax.fori_loop(0, BATCH, image, 0)
    v.halo_mg.start()
    v.store_gnet.start()
    v.store_gctx.start()


def encoder_back(v):
    spot, last = v.spot, v.space - 1
    v.halo_mg.receive()
    rows7 = lax.div(row_index((7 * WIDE, LANES)), WIDE)
    seen7 = (rows7 + spot * ROWS >= 1) & (rows7 + spot * ROWS < TALL + 1)

    def image(b, carry):
        up = jnp.where(spot > 0, full_of(v.mge[b, 0:256, :]), 0.0)
        own = full_of(v.mge[b, 256:896, :])
        down = jnp.where(spot < last, full_of(v.mge[b, 896:1152, :]), 0.0)
        spread_rows(v, 0, (jnp.concatenate([up, own, down], axis=0),), 1152, v.xi, 0, 128, True)
        joint = 0.0
        for a in range(3):
            for c in range(3):
                k = (a * 3 + c) * 256
                joint = joint + nt(
                    v.xi[(2 - a) * 128 : (2 - a) * 128 + 896, c * 128 : (c + 1) * 128], v.w_mm[k : k + 256, :]
                )
        branch = joint * full_of(v.slope_j[b])
        low = full_of(half_of(jnp.where(seen7, branch[:, 0:128], 0.0)))
        high = full_of(half_of(jnp.where(seen7, branch[:, 128:256], 0.0)))
        v.bg[b, :, 0:128] = half_of(low[128:768])
        v.bg[b, :, 128:256] = half_of(high[128:768])
        spread_rows(v, 384, (low, high), 896, v.xi, 0, 256, True)
        corr_grad = 0.0
        flow_grad = 0.0
        for a in range(3):
            rows = slice((2 - a) * 128, (2 - a) * 128 + 640)
            for c in range(3):
                k = a * 3 + c
                corr_grad = corr_grad + nt(v.xi[rows, 384 + c * 256 : 384 + (c + 1) * 256], v.w_cm[k * 256 : (k + 1) * 256, :])
                flow_grad = flow_grad + nt(
                    v.xi[rows, 384 + c * 256 + 128 : 384 + (c + 1) * 256], v.w_fm[k * 128 : (k + 1) * 128, :]
                )
        v.cpg[b] = half_of(corr_grad * full_of(v.slope_ci[b]))
        v.fpg[b] = half_of(flow_grad * full_of(v.slope_fi[b]))
        store = pltpu.make_async_copy(v.gcorr, v.out_gcorr.at[b], v.osem.at[2])
        pl.when(b > 0)(store.wait)
        v.gcorr[...] = nt(v.cpg[b], v.w_ci[...])
        store.start()
        z = nt(v.w_fi[...], v.fpg[b])
        total = jnp.zeros((32, LANES), jnp.float32)
        lane = lane_index((32, LANES))
        for across in range(7):
            v.fs[across] = jnp.zeros((32, LANES), jnp.float32)
            for y in range(ROWS):
                v.fs[across, 2 * y : 2 * y + 16, :] += z[across * 16 : across * 16 + 16, y * 128 : (y + 1) * 128]
            d = across - 3
            value = v.fs[across]
            if d:
                value = pltpu.roll(value, d % LANES, 1)
                value = jnp.where((lane - d >= 0) & (lane - d < WIDE), value, 0.0)
            total = total + value
        v.gf[b] = total
        return carry

    lax.fori_loop(0, BATCH, image, 0)
    v.halo_gf.start()


def gradients_encoder(v):
    starts, bias_row, spots, inner = flat_rows()

    def summed(ref, name):
        total = 0.0
        for b in range(BATCH):
            total = total + ones_sum(ref(b))
        keep_bias(v, name, total)

    summed(lambda b: v.mge[b, 256:896, :], MOTION_MIX)
    summed(lambda b: v.bg[b], CORR_MIX)
    summed(lambda b: v.bg[b, :, 128:256], FLOW_MIX)
    summed(lambda b: v.cpg[b], CORR_IN)
    summed(lambda b: v.fpg[b], FLOW_IN)

    for k in range(9):
        a, c = k // 3, k % 3
        value = 0.0
        for b in range(BATCH):
            value = value + tn(
                v.hx_j[b, a * 128 : a * 128 + 640, c * 256 : (c + 1) * 256], v.mge[b, 256:896, :]
            )
        v.mm_tmp[k * 256 : (k + 1) * 256, :] = value
    lane36 = lane_index((36, LANES))
    for r in range(63):
        first = v.mm_tmp[pl.ds(r, 36, stride=64), :]
        second = v.mm_tmp[pl.ds(r + 1, 36, stride=64), :]
        if r:
            first = pltpu.roll(first, LANES - 2 * r, 1)
        second = pltpu.roll(second, 126 - 2 * r, 1)
        v.flat[pl.ds(MARGIN + r, 36, stride=63), :] = jnp.where(lane36 < 126 - 2 * r, first, second)
    v.flush.layer(starts[MOTION_MIX], 2268)

    lane = lane_index((128, LANES))
    low_half = lane < 64
    for k in range(9):
        a, c = k // 3, k % 3
        value = 0.0
        for b in range(BATCH):
            value = value + tn(
                v.hx_c[b, (a + 1) * 128 : (a + 1) * 128 + 640, c * 256 : (c + 1) * 256], v.bg[b]
            )
        v.pair_a[...] = value[:, 0:128]
        v.pair_b[...] = value[:, 128:256]
        even, odd = (v.pair_a[pl.ds(i, 128, stride=2), :] for i in range(2))
        even_high, odd_high = (v.pair_b[pl.ds(i, 128, stride=2), :] for i in range(2))
        odd, odd_high = pltpu.roll(odd, 64, 1), pltpu.roll(odd_high, 64, 1)
        at = MARGIN + 384 * k
        v.flat[pl.ds(at, 128, stride=3), :] = even
        v.flat[pl.ds(at + 1, 128, stride=3), :] = jnp.where(low_half, even_high, odd)
        v.flat[pl.ds(at + 2, 128, stride=3), :] = jnp.where(low_half, odd, odd_high)
    v.flush.layer(starts[CORR_MIX], 3456)

    for k in range(9):
        a, c = k // 3, k % 3
        value = 0.0
        for b in range(BATCH):
            value = value + tn(
                v.hx_f[b, (a + 1) * 128 : (a + 1) * 128 + 640, c * 128 : (c + 1) * 128], v.bg[b, :, 128:256]
            )
        v.pair_a[0:128, :] = value
        even, odd = (v.pair_a[pl.ds(i, 64, stride=2), :] for i in range(2))
        v.flat[MARGIN + 64 * k : MARGIN + 64 * (k + 1), :] = jnp.where(
            lane_index((64, LANES)) < 64, pltpu.roll(even, 64, 1), odd
        )
    v.flush.layer(starts[FLOW_MIX], 576)

    value = 0.0
    for b in range(BATCH):
        value = value + tn(v.corr[b], v.cpg[b])
    pack_pairs(v.flat, 0, 324, value[:, 0:128], value[:, 128:256])
    v.flush.layer(starts[CORR_IN], 648)

    value = 0.0
    for b in range(BATCH):
        value = value + mm(v.xt[b, :, 256:896], v.fpg[b])
    v.flow_tmp[...] = value
    for across in range(7):
        for comp in range(2):
            v.flat[pl.ds(MARGIN + across * 2 + comp, 7, stride=14), :] = v.flow_tmp[
                pl.ds(across * 16 + comp, 7, stride=2), :
            ]
    v.flush.layer(starts[FLOW_IN], 98)

    lane1 = lane_index((1, LANES))
    v.flat[MARGIN : MARGIN + 24, :] = jnp.zeros((24, LANES), jnp.float32)
    for name, height, width in shapes():
        for block in range(-(-width // LANES)):
            value = v.gbias[BIAS_AT[name] + block : BIAS_AT[name] + block + 1, :]
            if name == FLOW_MIX:
                value = pltpu.roll(value, 64, 1)
            left = width - block * LANES
            if left < LANES:
                value = jnp.where(lane1 < left, value, 0.0)
            at = spots[name] + block * LANES
            row, shift = at // LANES, at % LANES
            moved = pltpu.roll(value, shift, 1) if shift else value
            low = jnp.where(lane1 >= shift, moved, 0.0)
            v.flat[MARGIN + row : MARGIN + row + 1, :] += low
            if shift:
                v.flat[MARGIN + row + 1 : MARGIN + row + 2, :] += jnp.where(lane1 < shift, moved, 0.0)
    v.flush.layer(bias_row, 21)


def finish(v):
    spot, last = v.spot, v.space - 1
    v.halo_gf.receive()
    for b in range(BATCH):
        v.tmp2[...] = v.gf[b]
        up = jnp.where(spot > 0, v.gf_up[b], 0.0)
        down = jnp.where(spot < last, v.gf_down[b], 0.0)
        v.tmp2[6:12, :] += up[16:22, :]
        v.tmp2[10:16, :] += down[0:6, :]
        for y in range(ROWS):
            v.out_gflow[b, 2 * y : 2 * y + 2, :] = (
                v.tmp2[6 + 2 * y : 8 + 2 * y, :] + v.gf_base[b, 0:2, y * 128 : (y + 1) * 128]
            )
    v.swap_loss.receive()
    v.loss_in[v.spot] = v.losses[...]
    total = jnp.sum(v.loss_in[...], axis=0)
    counts = jnp.sum(v.counts[...], axis=0)
    v.out_loss[...] = total / jnp.maximum(counts, 1.0)


class View:
    pass


def main_kernel(names, space, count, *refs):
    v = View()
    for name, ref in zip(names, refs):
        setattr(v, name, ref)
    v.space = space
    v.spot = lax.axis_index(SPACE)
    spot = v.spot
    barrier = pltpu.get_barrier_semaphore()

    def hello(step, carry):
        pl.semaphore_signal(barrier, inc=1, device_id={SPACE: lax.rem(spot + step, space)}, device_id_type=MESH)
        return carry

    lax.fori_loop(1, space, hello, 0)
    pl.semaphore_wait(barrier, space - 1)

    v.store_gnet = pltpu.make_async_copy(v.ru, v.out_gnet, v.osem.at[0])
    v.store_gctx = pltpu.make_async_copy(v.rr, v.out_gctx, v.osem.at[1])
    rows = row_index((8, LANES))
    counted = jnp.zeros((8, LANES), jnp.float32)
    for b in range(BATCH):
        counted = jnp.where(rows == b, jnp.sum(v.valid[b, 0:1, :]), counted)
    v.count_out[...] = counted
    v.pick_count = lambda counts, b: jnp.sum(jnp.where((rows == b) & (lane_index((8, LANES)) == 0), counts, 0.0))
    v.swap_count = Swap(v, 0, v.count_out, v.counts, True)
    v.swap_context = Swap(v, 1, v.a_context, v.b_context)
    v.swap_motion = Swap(v, 2, v.a_motion, v.b_motion)
    v.swap_state = Swap(v, 3, v.a_state, v.b_state)
    v.back_context = Swap(v, 4, v.a_context, v.c_context)
    v.back_motion = Swap(v, 5, v.a_motion, v.c_motion)
    v.back_state = Swap(v, 6, v.a_state, v.c_state)
    v.swap_loss = Swap(v, 7, v.losses, v.loss_in, True)
    v.halo_corr = Halo(v, 0, v.corr.at[:, 0:256], v.corr.at[:, 384:640], v.corr_down, v.corr_up)
    v.halo_flow = Halo(v, 1, v.flow, v.flow, v.flow_down, v.flow_up)
    v.halo_final = Halo(v, 2, v.e_left, v.e_right, v.f_right, v.f_left)
    v.halo_mask = Halo(v, 3, v.m_left, v.m_right, v.n_right, v.n_left)
    v.halo_dg = Halo(v, 4, v.dg, v.dg, v.dg_right, v.dg_left)
    v.halo_mg = Halo(v, 5, v.mge.at[:, 256:512], v.mge.at[:, 640:896], v.mge.at[:, 896:1152], v.mge.at[:, 0:256])
    v.halo_gf = Halo(v, 6, v.gf, v.gf, v.gf_down, v.gf_up)

    v.halo_corr.start()
    v.halo_flow.start()
    v.swap_count.start()

    def first(b, carry):
        v.state[b] = full_of(v.context[b])
        pack_rows(v, v.state, b, v.a_context)
        return carry

    lax.fori_loop(0, BATCH, first, 0)
    v.swap_context.start()
    unpack_all(v, count)
    v.halo_flow.receive()
    v.halo_corr.receive()
    forward_rows(v)
    keep = [pltpu.make_async_copy(v.hx_c, v.out_keep_c, v.ksem.at[0]), pltpu.make_async_copy(v.hx_f, v.out_keep_f, v.ksem.at[1])]
    for copy in keep:
        copy.start()
    mask_gradient(v)
    v.swap_context.receive()
    v.swap_motion.receive()
    v.swap_state.receive()
    take_own(v, v.a_context, v.b_context)
    take_own(v, v.a_motion, v.b_motion)
    take_own(v, v.a_state, v.b_state)
    columns_in(v)
    columns_forward(v)
    for copy in keep:
        copy.wait()
    heads(v)
    mask_output(v)
    v.swap_context.sent()
    v.swap_motion.sent()
    v.swap_state.sent()
    heads_back(v)
    v.flush = Flush(v)
    gradients_heads(v)
    gradients_gru(
        v,
        COLUMNS_GATES,
        COLUMNS_CANDIDATE,
        lambda t: (
            lambda b: v.xc[b, t * COLS : t * COLS + AREA, 0:128],
            lambda b: v.xc[b, t * COLS : t * COLS + AREA, 128:384],
            lambda b: v.xcr[b, t * COLS : t * COLS + AREA, :],
        ),
        lambda b, low=0, high=384: v.gc[b, 32 : 32 + AREA, low:high],
    )
    v.b_state, v.b_context, v.b_motion = v.c_state, v.c_context, v.c_motion
    rows_back(v)
    keep = [pltpu.make_async_copy(v.out_keep_c, v.hx_c, v.ksem.at[0]), pltpu.make_async_copy(v.out_keep_f, v.hx_f, v.ksem.at[1])]
    for copy in keep:
        copy.start()
    gradients_gru(
        v,
        ROWS_GATES,
        ROWS_CANDIDATE,
        lambda t: (
            lambda b: v.xs[b * AREA : (b + 1) * AREA, t * 128 : (t + 1) * 128],
            lambda b: v.xi[b * AREA : (b + 1) * AREA, t * 256 : (t + 1) * 256],
            lambda b: v.xr[b * AREA : (b + 1) * AREA, t * 128 : (t + 1) * 128],
        ),
        lambda b, low=0, high=384: v.gr[b, :, low:high],
    )
    encoder_back(v)
    for copy in keep:
        copy.wait()
    gradients_encoder(v)
    finish(v)
    v.flush.end()
    for swap in (v.swap_count, v.back_context, v.back_motion, v.back_state, v.swap_loss):
        swap.sent()
    for halo in (v.halo_corr, v.halo_flow, v.halo_final, v.halo_mask, v.halo_dg, v.halo_mg, v.halo_gf):
        halo.sent()
    v.store_gnet.wait()
    v.store_gctx.wait()
    pltpu.make_async_copy(v.gcorr, v.out_gcorr.at[0], v.osem.at[2]).wait()


def main_call(space, count, gathered, net, context, corr, flow, target, valid, grad_net, grad_mask):
    total = 3 * count // (LANES * 16) * 16 + BLOCK
    low, wide = jnp.bfloat16, jnp.float32
    peers = (space, BATCH, ROWS * COLS, LANES)
    ins = dict(
        gathered=gathered, net=net, context=context, corr=corr, flow=flow, target=target, valid=valid,
        grad_net=grad_net, grad_mask=grad_mask,
    )
    outs = dict(
        out_net=((BATCH, AREA, 128), low),
        out_flow=((BATCH, 8, SPAN), wide),
        out_mask=((BATCH, AREA, MASK), low),
        out_loss=((8, 128), wide),
        out_flat=((total, 128), low),
        out_gnet=((BATCH, AREA, 128), wide),
        out_gctx=((BATCH, AREA, 128), wide),
        out_gcorr=((BATCH, AREA, CORR), wide),
        out_gflow=((BATCH, 16, 128), wide),
        out_keep_c=((BATCH, 1152, 768), low),
        out_keep_f=((BATCH, 1152, 384), low),
    )
    scratch = dict(
        stage=((2, 3904, 128), low),
        seam=((16, 16, 128), wide),
        flat=((3904, 128), wide),
        pair_a=((256, 128), wide),
        pair_b=((256, 128), wide),
        flow_tmp=((112, 128), wide),
        mm_tmp=((3 * (2 * EDGE + SPREAD), 128), wide),
        fo_tmp=((32, 128), wide),
        fo_tmp2=((32, 128), wide),
        w_ci=((CORR, 256), low),
        w_cm=((2304, 256), low),
        w_fi=((112, 128), low),
        w_fm=((1152, 128), low),
        w_mm=((2304, 128), low),
        w_ri=((1280, 384), low),
        w_rs=((640, 384), low),
        w_li=((1280, 384), low),
        w_ls=((640, 384), low),
        w_h=((1152, 512), low),
        w_fo=((32, 256), low),
        w_mo=((256, 640), low),
        bias=((BIAS_ROWS, 128), wide),
        gbias=((BIAS_ROWS, 128), wide),
        corr_up=((BATCH, 256, CORR), low),
        corr_down=((BATCH, 256, CORR), low),
        flow_up=((BATCH, 16, 128), wide),
        flow_down=((BATCH, 16, 128), wide),
        fs=((7, 32, 128), wide),
        xt=((BATCH, 112, 1152), low),
        tmp=((1168, 128), wide),
        tmp2=((32, 128), wide),
        hx_c=((BATCH, 1152, 768), low),
        hx_f=((BATCH, 1152, 384), low),
        hx_j=((BATCH, 896, 768), low),
        slope_ci=((BATCH, AREA, 256), low),
        slope_fi=((BATCH, AREA, 128), low),
        slope_j=((BATCH, 896, 256), low),
        slope_m=((BATCH, AREA, 128), low),
        motion=((BATCH, AREA, 128), wide),
        state=((BATCH, AREA, 128), wide),
        xi=((BATCH * AREA, 1280), low),
        xs=((BATCH * AREA, 640), low),
        xr=((BATCH * AREA, 640), low),
        ru=((BATCH, AREA, 128), wide),
        rr=((BATCH, AREA, 128), wide),
        rc=((BATCH, AREA, 128), wide),
        lu=((BATCH, AREA, 128), wide),
        lr=((BATCH, AREA, 128), wide),
        lc=((BATCH, AREA, 128), wide),
        a_state=(peers, low), a_context=(peers, low), a_motion=(peers, low),
        b_state=(peers, low), b_context=(peers, low), b_motion=(peers, low),
        c_state=(peers, low), c_context=(peers, low), c_motion=(peers, low),
        xc=((BATCH, AREA + 64, 384), low),
        xcr=((BATCH, AREA + 64, 128), low),
        gc=((BATCH, AREA + 64, 384), low),
        final=((AREA, 128), wide),
        e_left=((BATCH, 2, 48, 128), low), e_right=((BATCH, 2, 48, 128), low),
        f_left=((BATCH, 2, 48, 128), low), f_right=((BATCH, 2, 48, 128), low),
        m_left=((BATCH, 2, 48, 128), low), m_right=((BATCH, 2, 48, 128), low),
        n_left=((BATCH, 2, 48, 128), low), n_right=((BATCH, 2, 48, 128), low),
        fm=((BATCH, 2, SPREAD, 128), low),
        slope_h=((BATCH, SPREAD, 512), low),
        feat=((BATCH, SPAN, 256), low),
        mf=((BATCH, AREA, 256), low),
        zt=((32, SPAN), wide),
        dg=((BATCH, 8, SPAN), wide),
        dg_left=((BATCH, 8, SPAN), wide), dg_right=((BATCH, 8, SPAN), wide),
        dt=((32, SPAN), wide),
        dto=((32, SPAN), wide),
        dtb=((BATCH, 32, SPAN), low),
        hgo=((BATCH, SPREAD, 512), low),
        gr=((BATCH, AREA, 384), low),
        mge=((BATCH, 1152, 128), low),
        bg=((BATCH, AREA, 256), low),
        gcorr=((AREA, CORR), wide),
        cpg=((BATCH, AREA, 256), low),
        fpg=((BATCH, AREA, 128), low),
        gf_base=((BATCH, 8, AREA), wide),
        gf=((BATCH, 32, 128), wide), gf_up=((BATCH, 32, 128), wide), gf_down=((BATCH, 32, 128), wide),
        count_out=((8, 128), wide), counts=((space, 8, 128), wide),
        losses=((8, 128), wide), loss_in=((space, 8, 128), wide),
    )
    sems = dict(
        hsend=pltpu.SemaphoreType.DMA((7, 2)), hrecv=pltpu.SemaphoreType.DMA((7, 2)),
        asend=pltpu.SemaphoreType.DMA((8, space)), arecv=pltpu.SemaphoreType.DMA((8, space)),
        ssem=pltpu.SemaphoreType.DMA((2, 2)),
        fsem=pltpu.SemaphoreType.DMA((16,)),
        ksem=pltpu.SemaphoreType.DMA((2,)),
        osem=pltpu.SemaphoreType.DMA((3,)),
    )
    vmem = pl.BlockSpec(memory_space=pltpu.VMEM)
    hbm = pl.BlockSpec(memory_space=pl.ANY)
    names = list(ins) + list(outs) + list(scratch) + list(sems)
    return pl.pallas_call(
        functools.partial(main_kernel, names, space, count),
        out_shape=[jax.ShapeDtypeStruct(*entry) for entry in outs.values()],
        in_specs=[hbm if name == "gathered" else vmem for name in ins],
        out_specs=[hbm if name in ("out_flat", "out_gnet", "out_gctx", "out_gcorr", "out_keep_c", "out_keep_f") else vmem for name in outs],
        scratch_shapes=[pltpu.VMEM(*entry) for entry in scratch.values()] + list(sems.values()),
        compiler_params=pltpu.CompilerParams(
            collective_id=2, has_side_effects=True, vmem_limit_bytes=VMEM_LIMIT
        ),
    )(*ins.values())


VMEM_LIMIT = 64 * 2**20 - 2**17


def shards_wide(net, context, corr, flow, target, valid, grad_net, grad_mask, params):
    space = lax.axis_size(SPACE)
    count = params.shape[0]
    gathered = gather_blocks(params).reshape(4 * BLOCK, LANES)
    flow_rows = jnp.transpose(flow.astype(jnp.float32), (0, 2, 1, 3)).reshape(BATCH, 2 * ROWS, WIDE)
    flow_rows = jnp.pad(flow_rows, ((0, 0), (0, 16 - 2 * ROWS), (0, 0)))
    pad = ((0, 0), (0, 0), (0, 0), (2, 2))
    target_ext = jnp.pad(target, pad).reshape(BATCH, 2, SPREAD)
    target_ext = jnp.pad(target_ext, ((0, 0), (0, 6), (0, SPAN - SPREAD)))
    valid_ext = jnp.pad(valid.astype(jnp.float32)[:, None], pad).reshape(BATCH, 1, SPREAD)
    valid_ext = jnp.broadcast_to(jnp.pad(valid_ext, ((0, 0), (0, 0), (0, SPAN - SPREAD))), (BATCH, 8, SPAN))
    outs = main_call(
        space, count, gathered, net.reshape(BATCH, AREA, HID), context.reshape(BATCH, AREA, CTX),
        corr.reshape(BATCH, AREA, CORR), flow_rows, target_ext, valid_ext,
        grad_net.reshape(BATCH, AREA, HID), grad_mask.reshape(BATCH, AREA, MASK),
    )
    new_net, new_flow, mask, loss, flat, gnet, gctx, gcorr, gflow = outs[:9]
    new_flow = new_flow[:, 0:2, 0:SPREAD].reshape(BATCH, 2, TALL, PITCH)[..., 2 : 2 + COLS]
    grads = reduce_grads(flat, space, count)
    return (
        new_net.reshape(BATCH, TALL, COLS, HID),
        new_flow,
        mask.reshape(BATCH, TALL, COLS, MASK),
        loss[0:BATCH, 0],
        grads,
        gnet.reshape(BATCH, ROWS, WIDE, HID),
        gctx.reshape(BATCH, ROWS, WIDE, CTX),
        gcorr.reshape(BATCH, ROWS, WIDE, CORR),
        jnp.transpose(gflow[:, 0 : 2 * ROWS].reshape(BATCH, ROWS, 2, WIDE), (0, 2, 1, 3)),
    )


def solution(mesh):
    def plan(*arrays):
        net, valid = arrays[0], arrays[5]
        if (net.shape[1:3], valid.shape[1:]) == ((ROWS, WIDE), (TALL, COLS)):
            return shards_wide(*arrays)
        return shards(*arrays)

    return jax.shard_map(
        plan,
        mesh=mesh,
        in_specs=(
            P(DP, SPACE, None, None),
            P(DP, SPACE, None, None),
            P(DP, SPACE, None, None),
            P(DP, None, SPACE, None),
            P(DP, None, None, SPACE),
            P(DP, None, SPACE),
            P(DP, None, SPACE, None),
            P(DP, None, SPACE, None),
            P(DP),
        ),
        out_specs=(
            P(DP, None, SPACE, None),
            P(DP, None, None, SPACE),
            P(DP, None, SPACE, None),
            P(DP),
            P(DP),
            P(DP, SPACE, None, None),
            P(DP, SPACE, None, None),
            P(DP, SPACE, None, None),
            P(DP, None, SPACE, None),
        ),
        check_vma=False,
    )
```

```python
import functools

import jax
import jax.numpy as jnp
from jax import lax
from jax.experimental import pallas as pl
from jax.experimental.pallas import tpu as pltpu
from jax.sharding import PartitionSpec as P

HID = 128
CTX = 128
MOT = 128
CORR = 324
SPACE = "space"
DP = "dp"
(
    CORR_IN,
    CORR_MIX,
    FLOW_IN,
    FLOW_MIX,
    MOTION_MIX,
    ROWS_GATES,
    ROWS_CANDIDATE,
    COLUMNS_GATES,
    COLUMNS_CANDIDATE,
    FLOW_HIDDEN,
    FLOW_OUT,
    MASK_HIDDEN,
    MASK_OUT,
) = range(13)
C1 = 256
C2 = 192
F1 = 128
F2 = 64
HEAD = 256
MASK = 576


def with_halo(block, sides, width):
    for axis, dim in sides:
        count = lax.axis_size(axis)
        forward = [(i, i + 1) for i in range(count - 1)]
        backward = [(target, source) for source, target in forward]
        low = lax.ppermute(
            lax.slice_in_dim(block, block.shape[dim] - width, None, axis=dim), axis, forward
        )
        high = lax.ppermute(lax.slice_in_dim(block, 0, width, axis=dim), axis, backward)
        block = jnp.concatenate([low, block, high], axis=dim)
    return block


def shapes():
    inputs_width = HID + CTX + MOT
    return [
        (CORR_IN, CORR, C1),
        (CORR_MIX, 9 * C1, C2),
        (FLOW_IN, 98, F1),
        (FLOW_MIX, 9 * F1, F2),
        (MOTION_MIX, 9 * (C2 + F2), MOT - 2),
        (ROWS_GATES, 5 * inputs_width, 2 * HID),
        (ROWS_CANDIDATE, 5 * inputs_width, HID),
        (COLUMNS_GATES, 5 * inputs_width, 2 * HID),
        (COLUMNS_CANDIDATE, 5 * inputs_width, HID),
        (FLOW_HIDDEN, 9 * HID, HEAD),
        (FLOW_OUT, 9 * HEAD, 2),
        (MASK_HIDDEN, 9 * HID, HEAD),
        (MASK_OUT, HEAD, MASK),
    ]


def unpack(flat):
    weights = {}
    biases = {}
    offset = 0
    table = shapes()
    for name, height, width in table:
        weights[name] = flat[offset // LANES : (offset + height * width) // LANES].reshape(height, width)
        offset = offset + height * width
    rest = flat[offset // LANES :].reshape(-1)
    offset = 0
    for name, height, width in table:
        biases[name] = rest[offset : offset + width].astype(jnp.float32)
        offset = offset + width
    return (weights, biases)


def pack(grads, total):
    table = shapes()
    rows = [grads[entry[0]][0].astype(jnp.bfloat16).reshape(-1, LANES) for entry in table]
    biases = jnp.concatenate([grads[entry[0]][1] for entry in table]).astype(jnp.bfloat16)
    left = total * LANES - sum(entry[1] * entry[2] for entry in table) - biases.shape[0]
    return jnp.concatenate(rows + [jnp.pad(biases, (0, left)).reshape(-1, LANES)])


def patches(padded, tall, wide):
    out_rows = padded.shape[1] - tall + 1
    out_columns = padded.shape[2] - wide + 1
    return jnp.concatenate(
        [
            padded[:, down : down + out_rows, across : across + out_columns]
            for down in range(tall)
            for across in range(wide)
        ],
        axis=-1,
    )


def apply(stacked, weight):
    return jnp.einsum("bhwk,ko->bhwo", stacked, weight, preferred_element_type=jnp.float32)


def apply_back(grad, weight):
    return jnp.einsum("bhwo,ko->bhwk", grad, weight, preferred_element_type=jnp.float32)


def weight_grad(stacked, pre_grad):
    return jnp.einsum("bhwk,bhwo->ko", stacked, pre_grad, preferred_element_type=jnp.float32)


def record(grads, name, stacked, pre_grad):
    grads[name] = (
        weight_grad(stacked, pre_grad),
        jnp.sum(pre_grad, axis=(0, 1, 2), dtype=jnp.float32),
    )


def flipped(weight, tall, wide):
    inner = weight.shape[0] // (tall * wide)
    shaped = weight.reshape(tall, wide, inner, weight.shape[1])[::-1, ::-1]
    return jnp.transpose(shaped, (0, 1, 3, 2)).reshape(-1, inner)


def slope(pre):
    sigma = jax.nn.sigmoid(pre)
    return sigma * (1.0 + pre * (1.0 - sigma))


def local_pad(field, tall, wide):
    return jnp.pad(field, ((0, 0), (tall // 2, tall // 2), (wide // 2, wide // 2), (0, 0)))


def row_pad(field, tall):
    field = with_halo(field, ((SPACE, 1),), tall // 2)
    return jnp.pad(field, ((0, 0), (0, 0), (tall // 2, tall // 2), (0, 0)))


def column_pad(field, tall, wide):
    field = with_halo(field, ((SPACE, 2),), wide // 2)
    return jnp.pad(field, ((0, 0), (tall // 2, tall // 2), (0, 0), (0, 0)))


MESH = pl.DeviceIdType.MESH
LANES = 128
BLOCK = 6144


def quarter_start(rank, count):
    return lax.div(rank * count, LANES)


def quarter_base(rank, count):
    return lax.div(rank * count, LANES * 16) * 16


def mate_of(rank):
    return rank + 1 - 2 * lax.rem(rank, 2)


def remote(src, dst, send, recv, device):
    return pltpu.make_async_remote_copy(
        src_ref=src, dst_ref=dst, send_sem=send, recv_sem=recv, device_id=device, device_id_type=MESH
    )


def greet(devices):
    barrier = pltpu.get_barrier_semaphore()
    for device in devices:
        pl.semaphore_signal(barrier, inc=1, device_id=device, device_id_type=MESH)
    pl.semaphore_wait(barrier, len(devices))


def lane_matrix(shift, forward):
    source = lax.broadcasted_iota(jnp.int32, (LANES, 2 * LANES), 0)
    target = lax.broadcasted_iota(jnp.int32, (LANES, 2 * LANES), 1)
    if forward:
        return jnp.where(target == source + shift, 1.0, 0.0).astype(jnp.bfloat16)
    return jnp.where(lax.rem(target + LANES, 2 * LANES) == source - shift + LANES, 1.0, 0.0).astype(jnp.bfloat16)


def gather_kernel(count, local_ref, out_ref, own_ref, send, recv):
    rank, spot = lax.axis_index(DP), lax.axis_index(SPACE)
    mate, across, twin = mate_of(rank), lax.rem(rank + 2, 4), mate_of(spot)
    pieces = 4
    rows = BLOCK // 2 // pieces
    peers = ({DP: mate}, {DP: across}, {SPACE: twin})
    greet(peers)
    matrix = lane_matrix(lax.rem(rank * count, LANES), True)
    first = lax.broadcasted_iota(jnp.int32, (256, LANES), 0) == 0

    def rotate(step, carry):
        at = pl.ds(pl.multiple_of(step * 256, 256), 256)
        both = jnp.dot(local_ref[at, :], matrix, preferred_element_type=jnp.float32)
        spill = pltpu.roll(both[:, LANES:], 1, 0)
        own_ref[at, :] = (both[:, :LANES] + jnp.where(first, carry, spill)).astype(jnp.bfloat16)
        return spill[0:1]

    lax.fori_loop(0, BLOCK // 256, rotate, jnp.zeros((1, LANES), jnp.float32))

    half, other_half = lax.rem(spot, 2), lax.rem(spot + 1, 2)

    def piece(which, index):
        return pl.ds(pl.multiple_of(which * (BLOCK // 2) + index * rows, 16), rows)

    own_x = [
        remote(own_ref.at[piece(half, k)], out_ref.at[rank, piece(half, k)], send.at[0, k], recv.at[0, k], peers[1])
        for k in range(pieces)
    ]
    own_c = remote(own_ref, out_ref.at[rank], send.at[4, 0], recv.at[4, 0], peers[0])
    for copy in own_x:
        copy.start()
    own_c.start()
    later = []
    for k in range(pieces):
        own_x[k].wait_recv()
        block = out_ref.at[across, piece(half, k)]
        to_twin = remote(block, block, send.at[1, k], recv.at[1, k], peers[2])
        to_mate = remote(block, block, send.at[2, k], recv.at[2, k], peers[0])
        to_twin.start()
        to_mate.start()
        later.append((to_twin, to_mate))
    for at in range(BLOCK // 256):
        out_ref[rank, at * 256 : (at + 1) * 256, :] = own_ref[at * 256 : (at + 1) * 256, :]
    for k in range(pieces):
        later[k][0].wait_recv()
        block = out_ref.at[across, piece(other_half, k)]
        to_mate = remote(block, block, send.at[3, k], recv.at[3, k], peers[0])
        to_mate.start()
        later.append((to_mate,))
    for k in range(pieces):
        own_x[k].wait_send()
        later[k][0].wait_send()
        later[k][1].wait()
        later[pieces + k][0].wait()
    own_c.wait()


def gather_blocks(params):
    count = params.shape[0]
    local = jnp.pad(params, (0, BLOCK * LANES - count)).reshape(BLOCK, LANES)
    return pl.pallas_call(
        functools.partial(gather_kernel, count),
        out_shape=jax.ShapeDtypeStruct((4, BLOCK, LANES), jnp.bfloat16),
        in_specs=[pl.BlockSpec(memory_space=pltpu.VMEM)],
        out_specs=pl.BlockSpec(memory_space=pltpu.VMEM),
        scratch_shapes=[
            pltpu.VMEM((BLOCK, LANES), jnp.bfloat16),
            pltpu.SemaphoreType.DMA((5, 4)),
            pltpu.SemaphoreType.DMA((5, 4)),
        ],
        compiler_params=pltpu.CompilerParams(
            collective_id=0, has_side_effects=True, vmem_limit_bytes=32 * 2**20
        ),
    )(local)


def gather_params(params):
    count = params.shape[0]
    blocks = gather_blocks(params)
    pieces = []
    reach = 0
    for rank in range(4):
        start = rank * count // LANES
        stop = -(-(rank + 1) * count // LANES)
        head = blocks[rank, :1] if rank == 0 else blocks[rank, :1] + pieces.pop()
        pieces += [head, blocks[rank, 1 : stop - start - 1], blocks[rank, stop - start - 1 : stop - start]]
    return jnp.concatenate(pieces)


def reduce_kernel(count, space, pieces, grads_ref, out_ref, rc, tx, rx, acc, ty, ry, tz, rz, gath, send, recv, zsend, zrecv):
    rank, spot = lax.axis_index(DP), lax.axis_index(SPACE)
    mate, across, twin = mate_of(rank), lax.rem(rank + 2, 4), mate_of(spot)
    group = space // 2
    side, depth = lax.rem(spot, 2), lax.div(spot, 2)
    rows = BLOCK // pieces
    half = rows // 2
    part = half // group

    def partner(step):
        return lax.rem(depth + step, group)

    peers = [{DP: mate}, {DP: across}, {SPACE: twin}]
    barrier = pltpu.get_barrier_semaphore()
    for device in peers:
        pl.semaphore_signal(barrier, inc=1, device_id=device, device_id_type=MESH)

    def hello(step, carry):
        pl.semaphore_signal(barrier, inc=1, device_id={SPACE: partner(step) * 2 + side}, device_id_type=MESH)
        return carry

    lax.fori_loop(1, group, hello, 0)
    pl.semaphore_wait(barrier, 3 + group - 1)

    gath[BLOCK:, :] = jnp.zeros((32, LANES), jnp.bfloat16)
    lower = lax.rem(rank, 2)
    upper = lax.div(rank, 2)

    def base(who):
        return pl.multiple_of(quarter_base(who, count), 16)

    def rows_of(start, index, length):
        return pl.ds(pl.multiple_of(start + index, 16), length)

    core = []
    for p in range(pieces):
        for high in range(2):
            copy = remote(
                grads_ref.at[rows_of(base(2 * high + 1 - lower), p * rows, rows)],
                rc.at[p, high],
                send.at[high, p],
                recv.at[high, p],
                peers[0],
            )
            copy.start()
            core.append(copy)
    step_rows = 192 if half % 192 == 0 else 16
    xs, ys, gs = [], [], []

    def z_copy(p, step):
        to = partner(step)
        return remote(
            tz.at[p, pl.ds(pl.multiple_of(to * part, 16), part)],
            rz.at[p, pl.ds(pl.multiple_of(depth * part, 16), part)],
            zsend.at[0, p, step],
            zrecv.at[0, p, step],
            {SPACE: to * 2 + side},
        )

    def home(p, which, slot):
        return pl.ds(pl.multiple_of(p * rows + which * half + slot * part, 16), part)

    def g_copy(p, step):
        block = gath.at[home(p, side, depth)]
        return remote(block, block, zsend.at[1, p, step], zrecv.at[1, p, step], {SPACE: partner(step) * 2 + side})

    def each(body):
        def run(step, carry):
            body(step)
            return carry

        lax.fori_loop(1, group, run, 0)

    def stage_core(p):
        core[2 * p].wait_recv()
        core[2 * p + 1].wait_recv()
        far = 1 - upper

        def add(step, carry):
            at = pl.multiple_of(step * step_rows, 16)
            mine = grads_ref[rows_of(base(2 * far + lower), p * rows + at, step_rows), :].astype(jnp.float32)
            tx[p, pl.ds(at, step_rows), :] = (
                mine + rc[p, far, pl.ds(at, step_rows), :].astype(jnp.float32)
            ).astype(jnp.bfloat16)
            return carry

        lax.fori_loop(0, rows // step_rows, add, 0)
        copy = remote(tx.at[p], rx.at[p], send.at[2, p], recv.at[2, p], peers[1])
        copy.start()
        xs.append(copy)

    def stage_x(p):
        xs[p].wait_recv()

        def total(at):
            return (
                grads_ref[rows_of(base(rank), p * rows + at, step_rows), :].astype(jnp.float32)
                + rc[p, upper, pl.ds(at, step_rows), :].astype(jnp.float32)
                + rx[p, pl.ds(at, step_rows), :].astype(jnp.float32)
            )

        def add(step, carry):
            at = pl.multiple_of(step * step_rows, 16)
            far = pl.multiple_of((1 - side) * half + at, 16)
            near = pl.multiple_of(side * half + at, 16)
            ty[p, pl.ds(at, step_rows), :] = total(far).astype(jnp.bfloat16)
            acc[p, pl.ds(at, step_rows), :] = total(near)
            return carry

        lax.fori_loop(0, half // step_rows, add, 0)
        copy = remote(ty.at[p], ry.at[p], send.at[3, p], recv.at[3, p], peers[2])
        copy.start()
        ys.append(copy)

    def stage_y(p):
        ys[p].wait_recv()

        def add(step, carry):
            at = pl.ds(pl.multiple_of(step * step_rows, 16), step_rows)
            value = acc[p, at, :] + ry[p, at, :].astype(jnp.float32)
            acc[p, at, :] = value
            tz[p, at, :] = value.astype(jnp.bfloat16)
            return carry

        lax.fori_loop(0, half // step_rows, add, 0)
        each(lambda step: z_copy(p, step).start())

    def stage_z(p):
        each(lambda step: z_copy(p, step).wait_recv())
        value = acc[p, pl.ds(pl.multiple_of(depth * part, 16), part), :]

        def add(step, value):
            other = lax.rem(depth + group - step, group)
            return value + rz[p, pl.ds(pl.multiple_of(other * part, 16), part), :].astype(jnp.float32)

        value = lax.fori_loop(1, group, add, value)
        gath[home(p, side, depth), :] = value.astype(jnp.bfloat16)
        each(lambda step: g_copy(p, step).start())

    def stage_zg(p):
        each(lambda step: g_copy(p, step).wait_recv())
        block = gath.at[pl.ds(pl.multiple_of(p * rows + side * half, 16), half)]
        copy = remote(block, block, send.at[4, p], recv.at[4, p], peers[2])
        copy.start()
        gs.append(copy)

    def stage_yg(p):
        gs[p].wait_recv()

    stages = [stage_core, stage_x, stage_y, stage_z, stage_zg, stage_yg]
    for tick in range(pieces + len(stages) - 1):
        for number in reversed(range(len(stages))):
            if 0 <= tick - number < pieces:
                stages[number](tick - number)

    for copy in core + xs + ys + gs:
        copy.wait_send()
    for p in range(pieces):

        def done(step):
            z_copy(p, step).wait_send()
            g_copy(p, step).wait_send()

        each(done)

    offset = rank * count - quarter_base(rank, count) * LANES
    skip = lax.div(offset, LANES)
    matrix = lane_matrix(lax.rem(offset, LANES), False)
    wide = jnp.where(
        lax.broadcasted_iota(jnp.int32, (256, 288), 1)
        == lax.broadcasted_iota(jnp.int32, (256, 288), 0) + skip,
        1.0,
        0.0,
    ).astype(jnp.bfloat16)
    wide_next = jnp.where(
        lax.broadcasted_iota(jnp.int32, (256, 288), 1)
        == lax.broadcasted_iota(jnp.int32, (256, 288), 0) + skip + 1,
        1.0,
        0.0,
    ).astype(jnp.bfloat16)

    def place(step, carry):
        at = pl.multiple_of(step * 256, 256)
        block = gath[pl.ds(at, 288), :]
        both = jnp.dot(block, matrix, preferred_element_type=jnp.float32).astype(jnp.bfloat16)
        out_ref[pl.ds(at, 256), :] = jnp.dot(wide, both[:, :LANES], preferred_element_type=jnp.float32) + jnp.dot(
            wide_next, both[:, LANES:], preferred_element_type=jnp.float32
        )
        return carry

    lax.fori_loop(0, BLOCK // 256, place, 0)


def reduce_grads(flat, space, count):
    pieces = next(k for k in (4, 2, 1) if BLOCK // (k * space) % 16 == 0)
    rows = BLOCK // pieces
    half = rows // 2
    out = pl.pallas_call(
        functools.partial(reduce_kernel, count, space, pieces),
        out_shape=jax.ShapeDtypeStruct((BLOCK, LANES), jnp.float32),
        in_specs=[pl.BlockSpec(memory_space=pltpu.VMEM)],
        out_specs=pl.BlockSpec(memory_space=pltpu.VMEM),
        scratch_shapes=[
            pltpu.VMEM((pieces, 2, rows, LANES), jnp.bfloat16),
            pltpu.VMEM((pieces, rows, LANES), jnp.bfloat16),
            pltpu.VMEM((pieces, rows, LANES), jnp.bfloat16),
            pltpu.VMEM((pieces, half, LANES), jnp.float32),
            pltpu.VMEM((pieces, half, LANES), jnp.bfloat16),
            pltpu.VMEM((pieces, half, LANES), jnp.bfloat16),
            pltpu.VMEM((pieces, half, LANES), jnp.bfloat16),
            pltpu.VMEM((pieces, half, LANES), jnp.bfloat16),
            pltpu.VMEM((BLOCK + 32, LANES), jnp.bfloat16),
            pltpu.SemaphoreType.DMA((5, pieces)),
            pltpu.SemaphoreType.DMA((5, pieces)),
            pltpu.SemaphoreType.DMA((2, pieces, space // 2)),
            pltpu.SemaphoreType.DMA((2, pieces, space // 2)),
        ],
        compiler_params=pltpu.CompilerParams(
            collective_id=1, has_side_effects=True, vmem_limit_bytes=48 * 2**20
        ),
    )(flat)
    return out.reshape(-1)[:count]


def gru_forward(state, inputs, weights, biases, gate_name, candidate_name, tall, wide, padder):
    joined_stack = patches(padder(jnp.concatenate([state, inputs], -1), tall, wide), tall, wide)
    gates = jax.nn.sigmoid(apply(joined_stack, weights[gate_name]) + biases[gate_name])
    hidden = state.shape[-1]
    update = gates[..., :hidden]
    reset = gates[..., hidden:]
    state_wide = state.astype(jnp.float32)
    mixed = jnp.concatenate([(reset * state_wide).astype(jnp.bfloat16), inputs], -1)
    mixed_stack = patches(padder(mixed, tall, wide), tall, wide)
    candidate = jnp.tanh(apply(mixed_stack, weights[candidate_name]) + biases[candidate_name])
    result = state_wide + update * (candidate - state_wide)
    return (result, (joined_stack, mixed_stack, update, reset, candidate, state_wide))


def gru_backward(result_grad, kept, weights, grads, gate_name, candidate_name, tall, wide, padder):
    joined_stack, mixed_stack, update, reset, candidate, state_wide = kept
    hidden = update.shape[-1]
    candidate_grad = (result_grad * update * (1.0 - candidate * candidate)).astype(jnp.bfloat16)
    record(grads, candidate_name, mixed_stack, candidate_grad)
    mixed_grad = apply(
        patches(padder(candidate_grad, tall, wide), tall, wide),
        flipped(weights[candidate_name], tall, wide),
    )
    reset_grad = mixed_grad[..., :hidden]
    gate_grad = jnp.concatenate(
        [
            result_grad * (candidate - state_wide) * update * (1.0 - update),
            reset_grad * state_wide * reset * (1.0 - reset),
        ],
        -1,
    ).astype(jnp.bfloat16)
    record(grads, gate_name, joined_stack, gate_grad)
    joined_grad = apply(
        patches(padder(gate_grad, tall, wide), tall, wide), flipped(weights[gate_name], tall, wide)
    )
    state_grad = result_grad * (1.0 - update) + reset_grad * reset + joined_grad[..., :hidden]
    inputs_grad = joined_grad[..., hidden:] + mixed_grad[..., hidden:]
    return (state_grad, inputs_grad)


def shards(net, context, corr, flow, target, valid, grad_net, grad_mask, params):
    flow_start = CTX + MOT - 2
    plane = jnp.float32(target.shape[2] * net.shape[2])
    counts = lax.psum(jnp.sum(valid, axis=(1, 2)).astype(jnp.float32), SPACE)
    divisor = jnp.maximum(counts, 1.0)
    weights, biases = unpack(gather_params(params))
    grads = {}
    flow_rows = jnp.transpose(flow, (0, 2, 3, 1))
    corr_pre = apply(corr, weights[CORR_IN]) + biases[CORR_IN]
    corr_one = jax.nn.silu(corr_pre).astype(jnp.bfloat16)
    corr_stack = patches(row_pad(corr_one, 3), 3, 3)
    corr_mix_pre = apply(corr_stack, weights[CORR_MIX]) + biases[CORR_MIX]
    corr_two = jax.nn.silu(corr_mix_pre).astype(jnp.bfloat16)
    flow_stack = patches(row_pad(flow_rows, 7), 7, 7)
    flow_pre = apply(flow_stack, weights[FLOW_IN]) + biases[FLOW_IN]
    flow_one = jax.nn.silu(flow_pre).astype(jnp.bfloat16)
    flow_mix_stack = patches(row_pad(flow_one, 3), 3, 3)
    flow_mix_pre = apply(flow_mix_stack, weights[FLOW_MIX]) + biases[FLOW_MIX]
    flow_two = jax.nn.silu(flow_mix_pre).astype(jnp.bfloat16)
    joint_stack = patches(row_pad(jnp.concatenate([corr_two, flow_two], -1), 3), 3, 3)
    motion_pre = apply(joint_stack, weights[MOTION_MIX]) + biases[MOTION_MIX]
    motion = jax.nn.silu(motion_pre).astype(jnp.bfloat16)
    inputs = jnp.concatenate([context, motion, flow_rows], -1)
    state, rows_kept = gru_forward(
        net, inputs, weights, biases, ROWS_GATES, ROWS_CANDIDATE, 1, 5, local_pad
    )
    state_columns, inputs_columns = (
        lax.all_to_all(
            state.astype(jnp.bfloat16), SPACE, split_axis=2, concat_axis=1, tiled=True
        ),
        lax.all_to_all(inputs, SPACE, split_axis=2, concat_axis=1, tiled=True),
    )
    target_here = jnp.transpose(target, (0, 2, 3, 1))
    valid_here = valid.astype(jnp.float32)
    net_cotangent = grad_net
    mask_cotangent = grad_mask
    final, columns_kept = gru_forward(
        state_columns,
        inputs_columns,
        weights,
        biases,
        COLUMNS_GATES,
        COLUMNS_CANDIDATE,
        5,
        1,
        local_pad,
    )
    final_low = final.astype(jnp.bfloat16)
    heads_weight = jnp.concatenate([weights[FLOW_HIDDEN], weights[MASK_HIDDEN]], 1)
    heads_bias = jnp.concatenate([biases[FLOW_HIDDEN], biases[MASK_HIDDEN]])
    net_stack = patches(column_pad(final_low, 3, 3), 3, 3)
    heads_pre = apply(net_stack, heads_weight) + heads_bias
    heads_act = jax.nn.silu(heads_pre).astype(jnp.bfloat16)
    flow_features = heads_act[..., :HEAD]
    mask_features = heads_act[..., HEAD:]
    hidden_stack = patches(column_pad(flow_features, 3, 3), 3, 3)
    delta = apply(hidden_stack, weights[FLOW_OUT]) + biases[FLOW_OUT]
    mask_full = 0.25 * (apply(mask_features, weights[MASK_OUT]) + biases[MASK_OUT])
    new_flow = inputs_columns[..., flow_start:].astype(jnp.float32) + delta
    error = new_flow - target_here
    root = jnp.sqrt(error * error + 1.0)
    partials = jnp.sum(valid_here * jnp.sum(root, axis=-1), axis=(1, 2))
    flow_grad = plane / divisor[:, None, None, None] * valid_here[..., None] * error / root
    mask_low = mask_full.astype(jnp.bfloat16)
    nets_out = final_low
    flows_out = jnp.transpose(new_flow, (0, 3, 1, 2))
    masks_out = mask_low
    delta_grad = flow_grad.astype(jnp.bfloat16)
    mask_grad = (0.25 * mask_cotangent.astype(jnp.float32)).astype(jnp.bfloat16)
    record(grads, MASK_OUT, mask_features, mask_grad)
    record(grads, FLOW_OUT, hidden_stack, delta_grad)
    from_flow = apply(
        patches(column_pad(delta_grad, 3, 3), 3, 3), flipped(weights[FLOW_OUT], 3, 3)
    )
    from_mask = apply_back(mask_grad, weights[MASK_OUT])
    heads_grad = (jnp.concatenate([from_flow, from_mask], -1) * slope(heads_pre)).astype(
        jnp.bfloat16
    )
    heads_wgrad = weight_grad(net_stack, heads_grad)
    heads_bgrad = jnp.sum(heads_grad, axis=(0, 1, 2), dtype=jnp.float32)
    grads[FLOW_HIDDEN] = (heads_wgrad[:, :HEAD], heads_bgrad[:HEAD])
    grads[MASK_HIDDEN] = (heads_wgrad[:, HEAD:], heads_bgrad[HEAD:])
    final_grad = net_cotangent.astype(jnp.float32) + apply(
        patches(column_pad(heads_grad, 3, 3), 3, 3), flipped(heads_weight, 3, 3)
    )
    state_grad_columns, inputs_grad_columns = gru_backward(
        final_grad,
        columns_kept,
        weights,
        grads,
        COLUMNS_GATES,
        COLUMNS_CANDIDATE,
        5,
        1,
        local_pad,
    )
    inputs_grad_columns = jnp.concatenate(
        [
            inputs_grad_columns[..., :flow_start],
            inputs_grad_columns[..., flow_start:] + flow_grad,
        ],
        -1,
    )
    state_back, inputs_back = (
        lax.all_to_all(
            state_grad_columns.astype(jnp.bfloat16),
            SPACE,
            split_axis=1,
            concat_axis=2,
            tiled=True,
        ),
        lax.all_to_all(
            inputs_grad_columns.astype(jnp.bfloat16),
            SPACE,
            split_axis=1,
            concat_axis=2,
            tiled=True,
        ),
    )
    net_grad, inputs_grad = gru_backward(
        state_back.astype(jnp.float32),
        rows_kept,
        weights,
        grads,
        ROWS_GATES,
        ROWS_CANDIDATE,
        1,
        5,
        local_pad,
    )
    inputs_total = inputs_grad + inputs_back.astype(jnp.float32)
    motion_grad = (inputs_total[..., CTX:flow_start] * slope(motion_pre)).astype(jnp.bfloat16)
    record(grads, MOTION_MIX, joint_stack, motion_grad)
    joint_grad = apply(
        patches(row_pad(motion_grad, 3), 3, 3), flipped(weights[MOTION_MIX], 3, 3)
    )
    branch_grad = jnp.concatenate(
        [
            joint_grad[..., :C2] * slope(corr_mix_pre),
            joint_grad[..., C2:] * slope(flow_mix_pre),
        ],
        -1,
    ).astype(jnp.bfloat16)
    record(grads, CORR_MIX, corr_stack, branch_grad[..., :C2])
    record(grads, FLOW_MIX, flow_mix_stack, branch_grad[..., C2:])
    branch_pad = row_pad(branch_grad, 3)
    corr_one_grad = apply(
        patches(branch_pad[..., :C2], 3, 3), flipped(weights[CORR_MIX], 3, 3)
    )
    flow_one_grad = apply(
        patches(branch_pad[..., C2:], 3, 3), flipped(weights[FLOW_MIX], 3, 3)
    )
    corr_pre_grad = (corr_one_grad * slope(corr_pre)).astype(jnp.bfloat16)
    flow_pre_grad = (flow_one_grad * slope(flow_pre)).astype(jnp.bfloat16)
    record(grads, CORR_IN, corr, corr_pre_grad)
    record(grads, FLOW_IN, flow_stack, flow_pre_grad)
    corr_grads = apply_back(corr_pre_grad, weights[CORR_IN])
    flow_total = inputs_total[..., flow_start:] + apply(
        patches(row_pad(flow_pre_grad, 7), 7, 7), flipped(weights[FLOW_IN], 7, 7)
    )
    flow_grads = jnp.transpose(flow_total, (0, 3, 1, 2))
    net_grads = net_grad
    context_grads = inputs_total[..., :CTX]
    count = params.shape[0]
    local = pack(grads, 3 * count // (LANES * 16) * 16 + BLOCK)
    collected = reduce_grads(local, lax.axis_size(SPACE), count)
    losses = lax.psum(partials, SPACE) / divisor
    return (
        nets_out,
        flows_out,
        masks_out,
        losses,
        collected,
        net_grads,
        context_grads,
        corr_grads,
        flow_grads,
    )


BATCH = 2
ROWS = 5
WIDE = 128
TALL = 40
COLS = 16
AREA = 640
PITCH = 20
SPREAD = TALL * PITCH
SPAN = 896
EDGE = 64


def mm(a, b):
    return jnp.dot(a, b, preferred_element_type=jnp.float32)


def nt(a, b):
    return lax.dot_general(a, b, (((1,), (1,)), ((), ())), preferred_element_type=jnp.float32)


def tn(a, b):
    return lax.dot_general(a, b, (((0,), (0,)), ((), ())), preferred_element_type=jnp.float32)


def half_of(value):
    return value.astype(jnp.bfloat16)


def full_of(value):
    return value.astype(jnp.float32)


def quarter_of(value):
    return half_of(0.25 * full_of(value))


def lane_index(shape):
    return lax.broadcasted_iota(jnp.int32, shape, 1)


def row_index(shape):
    return lax.broadcasted_iota(jnp.int32, shape, 0)


def act_slope(pre):
    sigma = jax.nn.sigmoid(pre)
    act = pre * sigma
    return act, sigma + act * (1.0 - sigma)


def flat_rows():
    table = shapes()
    offset = 0
    starts = {}
    for name, height, width in table:
        starts[name] = offset // LANES
        offset += height * width
    bias_row = offset // LANES
    spots = {}
    inner = 0
    for name, height, width in table:
        spots[name] = inner
        inner += width
    return starts, bias_row, spots, inner


def cast_rows(dst, to, src, start, count, kind):
    big = 256
    whole = count // big

    if whole > 1:

        def body(step, carry):
            at = pl.multiple_of(step * big, big)
            dst[pl.ds(to + at, big), :] = src[pl.ds(start + at, big), :].astype(kind)
            return carry

        lax.fori_loop(0, whole, body, 0)
    elif whole == 1:
        dst[to : to + big, :] = src[start : start + big, :].astype(kind)
    rest = count - whole * big
    if rest:
        low = whole * big
        dst[to + low : to + count, :] = src[start + low : start + count, :].astype(kind)


MARGIN = 16


def stage_plan(count, start, rows):
    stop = start + rows
    pieces, fill = [], 0
    for rank in range(4):
        first = rank * count // LANES
        last = -(-(rank + 1) * count // LANES)
        low, high = max(start, first), min(stop, last)
        if low >= high:
            continue
        place = low - first + rank * BLOCK
        base = place // 16 * 16
        length = -(-(place - base + high - low) // 16) * 16
        to = MARGIN + low - start - (place - base)
        seam = MARGIN + low - start if start < first else None
        pieces.append((base, length, fill, to, seam))
        fill += length
    return pieces


class Stages:
    def __init__(self, v, count, segments):
        self.v, self.at = v, 0
        self.plans = [stage_plan(count, start, rows) for start, rows in segments]
        self.fetch(0)

    def copies(self, index):
        v, slot = self.v, index % 2
        return [
            pltpu.make_async_copy(
                v.gathered.at[base : base + length], v.stage.at[slot, fill : fill + length], v.ssem.at[slot, number]
            )
            for number, (base, length, fill, to, seam) in enumerate(self.plans[index])
        ]

    def fetch(self, index):
        if index < len(self.plans):
            for copy in self.copies(index):
                copy.start()

    def take(self):
        v, index = self.v, self.at
        self.at += 1
        for copy in self.copies(index):
            copy.wait()
        self.fetch(index + 1)
        for base, length, fill, to, seam in self.plans[index]:
            saved = None if seam is None else v.flat[seam : seam + 1, :]
            cast_rows(v.flat, to, v.stage.at[index % 2], fill, length, jnp.float32)
            if seam is not None:
                v.flat[seam : seam + 1, :] = v.flat[seam : seam + 1, :] + saved


def strided(ref, start, count, stride):
    if stride == 1:
        return ref[pl.ds(start, count), :]
    return ref[pl.ds(start, count, stride=stride), :]


def unpack_pairs(flat, row, count, dst, to, lane):
    dst[to : to + count, lane : lane + LANES] = half_of(strided(flat, MARGIN + 2 * row, count, 2))
    dst[to : to + count, lane + LANES : lane + 2 * LANES] = half_of(strided(flat, MARGIN + 2 * row + 1, count, 2))


def pack_pairs(flat, row, count, low, high):
    flat[pl.ds(MARGIN + 2 * row, count, stride=2), :] = low
    flat[pl.ds(MARGIN + 2 * row + 1, count, stride=2), :] = high


def split_pick(which, quarter):
    source = lax.broadcasted_iota(jnp.int32, (LANES, HEAD), 0)
    target = lax.broadcasted_iota(jnp.int32, (LANES, HEAD), 1)
    return jnp.where(source == 2 * (target - 64 * quarter) + which, 1.0, 0.0).astype(jnp.bfloat16)


def unpack_all(v, count):
    starts, bias_row, spots, inner = flat_rows()
    flat = v.flat
    order = (
        (CORR_IN, 648), (CORR_MIX, 3456), (FLOW_IN, 98), (FLOW_MIX, 576), (MOTION_MIX, 2268),
        (ROWS_GATES, 3840), (ROWS_CANDIDATE, 1920), (COLUMNS_GATES, 3840), (COLUMNS_CANDIDATE, 1920),
        (FLOW_HIDDEN, 2304), (MASK_HIDDEN, 2304), (FLOW_OUT, 36), (MASK_OUT, 1152),
    )
    stages = Stages(v, count, [(starts[name], rows) for name, rows in order] + [(bias_row, 21)])

    def stage(name, rows):
        assert order[stages.at] == (name, rows)
        stages.take()

    stage(CORR_IN, 648)
    unpack_pairs(flat, 0, 324, v.w_ci, 0, 0)

    stage(CORR_MIX, 3456)
    lane = lane_index((128, LANES))
    low_half = lane < 64

    def mix_step(step, carry):
        at = MARGIN + 384 * step
        r0, r1, r2 = (strided(flat, at + i, 128, 3) for i in range(3))
        r1s, r2s = pltpu.roll(r1, 64, 1), pltpu.roll(r2, 64, 1)
        v.pair_a[pl.ds(0, 128, stride=2), :] = r0
        v.pair_a[pl.ds(1, 128, stride=2), :] = jnp.where(low_half, r1s, r2s)
        v.pair_b[pl.ds(0, 128, stride=2), :] = jnp.where(low_half, r1, 0.0)
        v.pair_b[pl.ds(1, 128, stride=2), :] = jnp.where(low_half, r2s, 0.0)
        to = pl.ds(pl.multiple_of(step * 256, 256), 256)
        v.w_cm[to, 0:128] = half_of(v.pair_a[...])
        v.w_cm[to, 128:256] = half_of(v.pair_b[...])
        return carry

    lax.fori_loop(0, 9, mix_step, 0)

    stage(FLOW_IN, 98)
    v.flow_tmp[...] = jnp.zeros_like(v.flow_tmp)
    for across in range(7):
        for comp in range(2):
            v.flow_tmp[pl.ds(across * 16 + comp, 7, stride=2), :] = strided(
                flat, MARGIN + across * 2 + comp, 7, 14
            )
    v.w_fi[...] = half_of(v.flow_tmp[...])

    stage(FLOW_MIX, 576)
    for step in range(9):
        r0 = strided(flat, MARGIN + 64 * step, 64, 1)
        high_half = lane_index((64, LANES)) >= 64
        v.pair_a[pl.ds(0, 64, stride=2), :] = jnp.where(high_half, pltpu.roll(r0, 64, 1), 0.0)
        v.pair_a[pl.ds(1, 64, stride=2), :] = jnp.where(high_half, r0, 0.0)
        v.w_fm[step * 128 : (step + 1) * 128, :] = half_of(v.pair_a[0:128, :])

    stage(MOTION_MIX, 2268)
    lane36 = lane_index((36, LANES))
    for i in range(64):
        if i == 0:
            value = strided(flat, MARGIN, 36, 63)
        elif i == 63:
            value = pltpu.roll(strided(flat, MARGIN + 62, 36, 63), 126, 1)
        else:
            low = pltpu.roll(strided(flat, MARGIN + i - 1, 36, 63), 2 * i, 1)
            high = pltpu.roll(strided(flat, MARGIN + i, 36, 63), 2 * i, 1)
            value = jnp.where(lane36 < 2 * i, low, high)
        v.mm_tmp[pl.ds(i, 36, stride=64), :] = jnp.where(lane36 < 126, value, 0.0)
    for step in range(9):
        v.w_mm[step * 256 : (step + 1) * 256, :] = half_of(v.mm_tmp[step * 256 : (step + 1) * 256, :])

    for gates_name, cand_name, w_i, w_s in ((ROWS_GATES, ROWS_CANDIDATE, v.w_ri, v.w_rs), (COLUMNS_GATES, COLUMNS_CANDIDATE, v.w_li, v.w_ls)):
        stage(gates_name, 3840)
        for tap in range(5):
            unpack_pairs(flat, tap * 384, 128, w_s, tap * 128, 0)
            unpack_pairs(flat, tap * 384 + 128, 256, w_i, tap * 256, 0)
        stage(cand_name, 1920)
        for tap in range(5):
            w_s[tap * 128 : (tap + 1) * 128, 256:384] = half_of(strided(flat, MARGIN + tap * 384, 128, 1))
            w_i[tap * 256 : (tap + 1) * 256, 256:384] = half_of(strided(flat, MARGIN + tap * 384 + 128, 256, 1))

    for name, lane0 in ((FLOW_HIDDEN, 0), (MASK_HIDDEN, 256)):
        stage(name, 2304)
        for tap in range(9):
            unpack_pairs(flat, tap * 128, 128, v.w_h, tap * 128, lane0)

    stage(FLOW_OUT, 36)
    v.fo_tmp[...] = jnp.zeros_like(v.fo_tmp)
    for which in range(2):
        total = jnp.zeros((9, HEAD), jnp.float32)
        for quarter in range(4):
            total = total + mm(half_of(strided(flat, MARGIN + quarter, 9, 4)), split_pick(which, quarter))
        v.fo_tmp[pl.ds(which, 9, stride=2), 0:128] = total[:, :128]
        v.fo_tmp2[pl.ds(which, 9, stride=2), 0:128] = total[:, 128:]
    v.fo_tmp2[18:32, :] = jnp.zeros((14, LANES), jnp.float32)
    v.w_fo[:, 0:128] = half_of(v.fo_tmp[...])
    v.w_fo[:, 128:256] = half_of(v.fo_tmp2[...])

    stage(MASK_OUT, 1152)
    r = [strided(flat, MARGIN + i, 128, 9) for i in range(9)]
    rs = [pltpu.roll(r[i], 64, 1) for i in range(4, 9)]
    for block in range(5):
        even = r[block] if block < 4 else jnp.where(low_half, r[4], 0.0)
        odd = jnp.where(low_half, rs[block], rs[block + 1]) if block < 4 else jnp.where(low_half, rs[4], 0.0)
        v.pair_a[pl.ds(0, 128, stride=2), :] = even
        v.pair_a[pl.ds(1, 128, stride=2), :] = odd
        v.w_mo[:, block * 128 : (block + 1) * 128] = half_of(v.pair_a[...])

    stages.take()
    place = 0
    lane1 = lane_index((1, LANES))
    for name, height, width in shapes():
        spot = spots[name]
        for block in range(-(-width // LANES)):
            at = spot + block * LANES
            row, shift = at // LANES, at % LANES
            value = flat[MARGIN + row : MARGIN + row + 1, :]
            if shift:
                after = flat[MARGIN + row + 1 : MARGIN + row + 2, :]
                value = jnp.where(
                    lane1 < LANES - shift, pltpu.roll(value, LANES - shift, 1), pltpu.roll(after, LANES - shift, 1)
                )
            left = width - block * LANES
            if left < LANES:
                value = jnp.where(lane1 < left, value, 0.0)
            if name == FLOW_MIX:
                value = pltpu.roll(value, 64, 1)
            v.bias[place : place + 1, :] = value
            place += 1


BIAS_AT = {}
_place = 0
for _name, _height, _width in shapes():
    BIAS_AT[_name] = _place
    _place += -(-_width // 128)
BIAS_ROWS = 32


def bias_of(v, name, blocks):
    at = BIAS_AT[name]
    return jnp.concatenate([v.bias[at + i : at + i + 1, :] for i in range(blocks)], axis=1)


class Halo:
    def __init__(self, v, sem, up_src, down_src, from_down, from_up):
        up = {SPACE: jnp.maximum(v.spot - 1, 0)}
        down = {SPACE: jnp.minimum(v.spot + 1, v.space - 1)}
        self.v = v
        self.up = remote(up_src, from_down, v.hsend.at[sem, 0], v.hrecv.at[sem, 0], up)
        self.down = remote(down_src, from_up, v.hsend.at[sem, 1], v.hrecv.at[sem, 1], down)

    def start(self):
        pl.when(self.v.spot > 0)(self.up.start)
        pl.when(self.v.spot < self.v.space - 1)(self.down.start)

    def receive(self):
        pl.when(self.v.spot < self.v.space - 1)(self.up.wait_recv)
        pl.when(self.v.spot > 0)(self.down.wait_recv)

    def sent(self):
        pl.when(self.v.spot > 0)(self.up.wait_send)
        pl.when(self.v.spot < self.v.space - 1)(self.down.wait_send)


class Swap:
    def __init__(self, v, sem, src, dst, broadcast=False):
        self.v, self.sem, self.src, self.dst, self.broadcast = v, sem, src, dst, broadcast

    def copy(self, step):
        v = self.v
        to = lax.rem(v.spot + step, v.space)
        src = self.src if self.broadcast else self.src.at[to]
        return remote(src, self.dst.at[v.spot], v.asend.at[self.sem, step], v.arecv.at[self.sem, step], {SPACE: to})

    def each(self, what):
        def body(step, carry):
            what(self.copy(step))
            return carry

        lax.fori_loop(1, self.v.space, body, 0)

    def start(self):
        self.each(lambda copy: copy.start())

    def receive(self):
        self.each(lambda copy: copy.wait_recv())

    def sent(self):
        self.each(lambda copy: copy.wait_send())


def spread_rows(v, b, acts, rows, dst, row0, width, backward=False):
    x = lax.rem(row_index((rows, LANES)), WIDE)
    for block, act in enumerate(acts):
        v.tmp[8 : 8 + rows, :] = act
        for tap in range(3):
            d = (1 - tap) if backward else (tap - 1)
            value = act if d == 0 else v.tmp[8 + d : 8 + d + rows, :]
            if d == -1:
                value = jnp.where(x > 0, value, 0.0)
            if d == 1:
                value = jnp.where(x < WIDE - 1, value, 0.0)
            lane = tap * width + block * LANES
            if backward:
                dst[row0 : row0 + rows, b + lane : b + lane + LANES] = half_of(value)
            else:
                dst[b, row0 : row0 + rows, lane : lane + LANES] = half_of(value)


def spread_five(v, value, dst, lane_of, backward=False):
    x = lax.rem(row_index((AREA, LANES)), WIDE)
    v.tmp[8 : 8 + AREA, :] = value
    for tap in range(5):
        d = (2 - tap) if backward else (tap - 2)
        moved = value if d == 0 else v.tmp[8 + d : 8 + d + AREA, :]
        if d:
            moved = jnp.where((x + d >= 0) & (x + d < WIDE), moved, 0.0)
        if backward:
            taps_part(v, tap, lane_of, lane_of + LANES)[...] = half_of(moved)
        else:
            lane = lane_of(tap)
            dst[:, lane : lane + LANES] = half_of(moved)


def lines_of(ref, b, lines):
    return jnp.concatenate([ref[b, y] for y in range(lines)], axis=1)


def edge_rows(v, value, rows):
    low = jnp.where(v.spot > 0, value[0:rows], 0.0)
    high = jnp.where(v.spot < v.space - 1, value[-rows:], 0.0)
    return jnp.concatenate([low, value[rows:-rows], high], axis=0)


def forward_rows(v):
    spot, last = v.spot, v.space - 1
    def image(b, carry):
        pieces = (
            (v.corr_up, 0, 256, 2, spot > 0),
            (v.corr, 256, 640, 5, None),
            (v.corr_down, 896, 256, 2, spot < last),
        )
        bias = bias_of(v, CORR_IN, 2)
        for ref, row0, rows, lines, seen in pieces:
            act, slope = act_slope(tn(lines_of(ref, b, lines), v.w_ci[...]) + bias)
            if seen is None:
                v.slope_ci[b] = half_of(slope)
            else:
                act = jnp.where(seen, act, 0.0)
            spread_rows(v, b, (act[:, :128], act[:, 128:]), rows, v.hx_c, row0, 256)

        up = jnp.where(spot > 0, v.flow_up[b], 0.0)
        down = jnp.where(spot < last, v.flow_down[b], 0.0)
        lane = lane_index((16, LANES))
        v.fs[...] = jnp.zeros_like(v.fs)
        for across in range(7):
            d = across - 3
            for part, value in enumerate((up, v.flow[b], down)):
                moved = value
                if d:
                    moved = pltpu.roll(value, (-d) % LANES, 1)
                    moved = jnp.where((lane + d >= 0) & (lane + d < WIDE), moved, 0.0)
                v.fs[across, part * 10 : part * 10 + 10, :] = moved[0:10, :]
        for y in range(9):
            for across in range(7):
                v.flow_tmp[across * 16 : across * 16 + 16, :] = v.fs[across, 2 * y : 2 * y + 16, :]
            v.xt[b, :, y * 128 : (y + 1) * 128] = half_of(v.flow_tmp[...])
        act, slope = act_slope(tn(v.xt[b], v.w_fi[...]) + bias_of(v, FLOW_IN, 1))
        v.slope_fi[b] = half_of(slope[256:896])
        spread_rows(v, b, (edge_rows(v, act, 2 * WIDE),), 9 * WIDE, v.hx_f, 0, 128)

        pre = bias_of(v, CORR_MIX, 2)
        flow_pre = bias_of(v, FLOW_MIX, 1)
        for a in range(3):
            pre = pre + mm(v.hx_c[b, a * 128 : a * 128 + 896, :], v.w_cm[a * 768 : (a + 1) * 768, :])
            flow_pre = flow_pre + mm(v.hx_f[b, a * 128 : a * 128 + 896, :], v.w_fm[a * 384 : (a + 1) * 384, :])
        low, low_slope = act_slope(pre[:, :128])
        high, high_slope = act_slope(pre[:, 128:] + flow_pre)
        v.slope_j[b, :, 0:128] = half_of(low_slope)
        v.slope_j[b, :, 128:256] = half_of(high_slope)
        spread_rows(v, b, (edge_rows(v, low, WIDE), edge_rows(v, high, WIDE)), 896, v.hx_j, 0, 256)

        pre = bias_of(v, MOTION_MIX, 1)
        for a in range(3):
            pre = pre + mm(v.hx_j[b, a * 128 : a * 128 + 640, :], v.w_mm[a * 768 : (a + 1) * 768, :])
        act, slope = act_slope(pre)
        v.slope_m[b] = half_of(jnp.where(lane_index((AREA, LANES)) < 126, slope, 0.0))
        pick = jnp.where(lane_index((16, LANES)) == row_index((16, LANES)) + 126, 1.0, 0.0)
        own_flow = v.flow[b]
        for y in range(ROWS):
            v.tmp2[0:2, :] = own_flow[2 * y : 2 * y + 2, :]
            v.tmp2[2:16, :] = jnp.zeros((14, LANES), jnp.float32)
            v.motion[b, y * 128 : (y + 1) * 128, :] = act[y * 128 : (y + 1) * 128, :] + tn(
                half_of(v.tmp2[0:16, :]), half_of(pick)
            )
        v.motion[b] = full_of(half_of(v.motion[b]))
        pack_rows(v, v.motion, b, v.a_motion)
        return carry

    lax.fori_loop(0, BATCH, image, 0)
    v.swap_motion.start()

    def gru(b, carry):
        at = pl.ds(pl.multiple_of(b * AREA, AREA), AREA)
        s = full_of(v.net[b])
        spread_five(v, full_of(v.context[b]), v.xi.at[at], lambda t: t * 256)
        spread_five(v, v.motion[b], v.xi.at[at], lambda t: t * 256 + 128)
        spread_five(v, s, v.xs.at[at], lambda t: t * 128)
        both = mm(v.xi[at, :], v.w_ri[...])
        gates = jax.nn.sigmoid(both[:, :256] + mm(v.xs[at, :], v.w_rs[:, :256]) + bias_of(v, ROWS_GATES, 2))
        update, reset = gates[:, :128], gates[:, 128:]
        v.ru[b] = update
        v.rr[b] = reset
        spread_five(v, full_of(half_of(reset * s)), v.xr.at[at], lambda t: t * 128)
        cand = jnp.tanh(both[:, 256:] + mm(v.xr[at, :], v.w_rs[:, 256:]) + bias_of(v, ROWS_CANDIDATE, 1))
        v.rc[b] = cand
        v.state[b] = s + update * (cand - s)
        pack_rows(v, v.state, b, v.a_state)
        return carry

    lax.fori_loop(0, BATCH, gru, 0)
    v.swap_state.start()


def pack_rows(v, src, b, dst):
    def peer(t, carry):
        for y in range(ROWS):
            at = pl.multiple_of(y * WIDE + t * COLS, COLS)
            dst[t, b, y * COLS : (y + 1) * COLS, :] = half_of(src[b, pl.ds(at, COLS), :])
        return carry

    lax.fori_loop(0, v.space, peer, 0)


def take_own(v, src, dst):
    dst[v.spot] = src[v.spot]


def columns_in(v):
    def zero(b, carry):
        for ref, wide in ((v.xc, 384), (v.xcr, 128), (v.gc, 384)):
            for low in (0, 32 + AREA):
                ref[b, low : low + 32, :] = jnp.zeros((32, wide), jnp.bfloat16)
        return carry

    lax.fori_loop(0, BATCH, zero, 0)

    def peer(t, carry):
        at = pl.ds(pl.multiple_of(32 + t * ROWS * COLS, 16), ROWS * COLS)
        for b in range(BATCH):
            v.xc[b, at, 0:128] = v.b_state[t, b]
            v.xc[b, at, 128:256] = v.b_context[t, b]
            v.xc[b, at, 256:384] = v.b_motion[t, b]
        return carry

    lax.fori_loop(0, v.space, peer, 0)


FX_ROWS = 16 + (TALL + 2) * PITCH


def fx_base(b):
    return pl.multiple_of(b * FX_ROWS, 8)


def columns_forward(v):
    def gru(b, carry):
        s = full_of(v.xc[b, 32 : 32 + AREA, 0:128])
        both = bias_of(v, COLUMNS_GATES, 2)
        both = jnp.concatenate([both, bias_of(v, COLUMNS_CANDIDATE, 1)], axis=1)
        gates = 0.0
        for t in range(5):
            rows = slice(t * COLS, t * COLS + AREA)
            both = both + mm(v.xc[b, rows, 128:384], v.w_li[t * 256 : (t + 1) * 256, :])
            gates = gates + mm(v.xc[b, rows, 0:128], v.w_ls[t * 128 : (t + 1) * 128, 0:256])
        gates = jax.nn.sigmoid(gates + both[:, :256])
        update, reset = gates[:, :128], gates[:, 128:]
        v.lu[b] = update
        v.lr[b] = reset
        v.xcr[b, 32 : 32 + AREA, :] = half_of(reset * s)
        cand = both[:, 256:]
        for t in range(5):
            rows = slice(t * COLS, t * COLS + AREA)
            cand = cand + mm(v.xcr[b, rows, :], v.w_ls[t * 128 : (t + 1) * 128, 256:384])
        cand = jnp.tanh(cand)
        v.lc[b] = cand
        final = s + update * (cand - s)
        v.out_net[b] = half_of(final)
        v.final[...] = full_of(half_of(final))
        fx = fx_base(b)
        v.mm_tmp[pl.ds(fx, FX_ROWS), :] = jnp.zeros((FX_ROWS, LANES), jnp.float32)
        for x in range(COLS):
            v.mm_tmp[pl.ds(fx + 8 + PITCH + 2 + x, TALL, stride=PITCH), :] = v.final[pl.ds(x, TALL, stride=COLS), :]
        for j in range(2):
            v.e_left[b, j, 0:TALL, :] = half_of(v.final[pl.ds(j, TALL, stride=COLS), :])
            v.e_right[b, j, 0:TALL, :] = half_of(v.final[pl.ds(COLS - 2 + j, TALL, stride=COLS), :])
        return carry

    lax.fori_loop(0, BATCH, gru, 0)
    v.halo_final.start()


def ring_masks(v, shape):
    x = lax.rem(row_index(shape), PITCH)
    place = v.spot * COLS + x - 2
    seen = (place >= 0) & (place < WIDE) & (x >= 1) & (x < PITCH - 1)
    own = (x >= 2) & (x < PITCH - 2)
    return seen, own


def mask_gradient(v):
    def image(b, carry):
        value = nt(quarter_of(v.grad_mask[b]), v.w_mo[:, 0:MASK])
        for block in range(2):
            v.final[...] = value[:, block * 128 : (block + 1) * 128]
            v.tmp[0:SPREAD, :] = jnp.zeros((SPREAD, LANES), jnp.float32)
            for x in range(COLS):
                v.tmp[pl.ds(2 + x, TALL, stride=PITCH), :] = v.final[pl.ds(x, TALL, stride=COLS), :]
            v.hgo[b, :, 256 + block * 128 : 384 + block * 128] = half_of(v.tmp[0:SPREAD, :])
            v.m_left[b, block, 0:TALL, :] = half_of(v.final[pl.ds(0, TALL, stride=COLS), :])
            v.m_right[b, block, 0:TALL, :] = half_of(v.final[pl.ds(COLS - 1, TALL, stride=COLS), :])
        return carry

    lax.fori_loop(0, BATCH, image, 0)
    v.halo_mask.start()


def heads_part(v, b, tap):
    ref = v.hx_c if tap < 6 else v.hx_f
    lane = tap % 6 * 128
    return ref.at[b, 0:SPREAD, lane : lane + 128]


def taps_part(v, t, low, high):
    ref = v.hx_f if t % 3 == 2 else v.hx_c
    lane = (t % 3) % 2 * 384
    return ref.at[t // 3, 0:AREA, lane + low : lane + high]


def heads(v):
    spot, last = v.spot, v.space - 1
    v.halo_final.receive()
    v.halo_mask.receive()
    v.swap_count.receive()
    v.counts[v.spot] = v.count_out[...]
    counts = jnp.sum(v.counts[...], axis=0)
    seen, own = ring_masks(v, (SPREAD, LANES))
    steps = [(a - 1) * PITCH + (c - 1) for a in range(3) for c in range(3)]
    plane = jnp.float32(TALL * WIDE)

    def image(b, carry):
        fx = fx_base(b)
        for j in range(2):
            left = jnp.where(spot > 0, full_of(v.f_left[b, j, 0:TALL, :]), 0.0)
            right = jnp.where(spot < last, full_of(v.f_right[b, j, 0:TALL, :]), 0.0)
            v.mm_tmp[pl.ds(fx + 8 + PITCH + j, TALL, stride=PITCH), :] = left
            v.mm_tmp[pl.ds(fx + 8 + PITCH + PITCH - 2 + j, TALL, stride=PITCH), :] = right
        for block in range(2):
            left = jnp.where(spot > 0, full_of(v.n_left[b, block, 0:TALL, :]), 0.0)
            right = jnp.where(spot < last, full_of(v.n_right[b, block, 0:TALL, :]), 0.0)
            v.tmp[0:SPREAD, :] = full_of(v.hgo[b, :, 256 + block * 128 : 384 + block * 128])
            v.tmp[pl.ds(1, TALL, stride=PITCH), :] = left
            v.tmp[pl.ds(PITCH - 2, TALL, stride=PITCH), :] = right
            v.hgo[b, :, 256 + block * 128 : 384 + block * 128] = half_of(v.tmp[0:SPREAD, :])
        for tap in range(9):
            at = 8 + PITCH + steps[tap]
            heads_part(v, b, tap)[...] = half_of(v.mm_tmp[pl.ds(fx + at, SPREAD), :])
        for part in range(2):
            name = (FLOW_HIDDEN, MASK_HIDDEN)[part]
            lanes = slice(part * 256, (part + 1) * 256)
            act, slope = act_slope(mm(v.hx_c[b, 0:SPREAD, :], v.w_h[0:768, lanes]) + mm(v.hx_f[b, 0:SPREAD, :], v.w_h[768:1152, lanes]) + bias_of(v, name, 2))
            v.slope_h[b, :, lanes] = half_of(slope)
            if part == 0:
                for block in range(2):
                    value = jnp.where(seen, act[:, block * 128 : (block + 1) * 128], 0.0)
                    v.feat[b, 0:SPREAD, block * 128 : (block + 1) * 128] = half_of(value)
                v.feat[b, SPREAD:SPAN, :] = jnp.zeros((SPAN - SPREAD, HEAD), jnp.bfloat16)
            else:
                for block in range(2):
                    v.tmp[0:SPREAD, :] = act[:, block * 128 : (block + 1) * 128]
                    for x in range(COLS):
                        v.final[pl.ds(x, TALL, stride=COLS), :] = v.tmp[pl.ds(2 + x, TALL, stride=PITCH), :]
                    v.mf[b, :, block * 128 : (block + 1) * 128] = half_of(v.final[...])
        moved = nt(v.w_fo[...], v.feat[b])
        v.zt[...] = moved
        delta = jnp.zeros((8, SPAN), jnp.float32)
        for tap in range(9):
            pair = jnp.concatenate([v.zt[2 * tap : 2 * tap + 2, :], jnp.zeros((6, SPAN), jnp.float32)], axis=0)
            delta = delta + pltpu.roll(pair, (-steps[tap]) % SPAN, 1)
        v.tmp[0:SPAN, :] = jnp.zeros((SPAN, LANES), jnp.float32)
        v.final[...] = full_of(v.xc[b, 32 : 32 + AREA, 256:384])
        for x in range(COLS):
            v.tmp[pl.ds(2 + x, TALL, stride=PITCH), :] = v.final[pl.ds(x, TALL, stride=COLS), :]
        pick = jnp.where(lane_index((16, LANES)) == row_index((16, LANES)) + 126, 1.0, 0.0)
        base = nt(half_of(pick), half_of(v.tmp[0:SPAN, :]))[0:8, :]
        bias = v.bias[BIAS_AT[FLOW_OUT] : BIAS_AT[FLOW_OUT] + 1, :]
        first = row_index((8, SPAN)) == 0
        second = row_index((8, SPAN)) == 1
        shift = jnp.where(first, bias[0:1, 0:1], jnp.where(second, bias[0:1, 1:2], 0.0))
        new = base + delta + shift
        v.out_flow[b] = new
        error = new - v.target[b]
        root = jnp.sqrt(error * error + 1.0)
        valid = jnp.where(first | second, v.valid[b], 0.0)
        piece = jnp.sum(valid * root)
        divisor = jnp.maximum(v.pick_count(counts, b), 1.0)
        gradient = plane / divisor * valid * error / root
        v.dg[b] = gradient
        v.losses[...] = jnp.where(row_index((8, LANES)) == b, piece, v.losses[...])
        return carry

    v.losses[...] = jnp.zeros((8, LANES), jnp.float32)
    lax.fori_loop(0, BATCH, image, 0)
    v.halo_dg.start()
    v.swap_loss.start()


def mask_output(v):
    def image(b, carry):
        store = pltpu.make_async_copy(v.mask_low, v.out_mask.at[b], v.osem.at[3])
        pl.when(b > 0)(store.wait)
        for block in range(5):
            wide = min(128, MASK - block * 128)
            lanes = slice(block * 128, block * 128 + wide)
            at = BIAS_AT[MASK_OUT] + block
            value = mm(v.mf[b], v.w_mo[:, lanes]) + v.bias[at : at + 1, 0:wide]
            v.mask_low[:, lanes] = half_of(0.25 * value)
        store.start()
        return carry

    lax.fori_loop(0, BATCH, image, 0)


def heads_back(v):
    spot, last = v.spot, v.space - 1
    seen, own = ring_masks(v, (SPREAD, LANES))
    steps = [(a - 1) * PITCH + (c - 1) for a in range(3) for c in range(3)]
    v.halo_dg.receive()

    def zb(c, low, rows):
        at = c * (2 * EDGE + SPREAD) + low
        return v.mm_tmp.at[at : at + rows]

    def image(b, carry):
        x = lax.rem(lane_index((8, SPAN)), PITCH)
        own_dg = v.dg[b]
        left = jnp.where((x < 2) & (spot > 0), pltpu.roll(v.dg_left[b], SPAN - COLS, 1), 0.0)
        right = jnp.where((x >= PITCH - 2) & (spot < last), pltpu.roll(v.dg_right[b], COLS, 1), 0.0)
        inside = lane_index((8, SPAN)) < SPREAD
        wide_dg = full_of(half_of(jnp.where(inside, own_dg + left + right, 0.0)))
        own_low = full_of(half_of(own_dg))
        v.dt[...] = jnp.zeros_like(v.dt)
        v.dto[...] = jnp.zeros_like(v.dto)
        for tap in range(9):
            v.dt[2 * tap : 2 * tap + 2, :] = pltpu.roll(wide_dg, steps[tap] % SPAN, 1)[0:2, :]
            v.dto[2 * tap : 2 * tap + 2, :] = pltpu.roll(own_low, steps[tap] % SPAN, 1)[0:2, :]
        v.dtb[b] = half_of(v.dto[...])
        from_flow = tn(half_of(v.dt[...]), v.w_fo[...])
        for block in range(4):
            lanes = slice(block * 128, (block + 1) * 128)
            value = from_flow[0:SPREAD, lanes] if block < 2 else full_of(v.hgo[b, :, lanes])
            value = value * full_of(v.slope_h[b, :, lanes])
            v.hgo[b, :, lanes] = half_of(jnp.where(seen, value, 0.0))
        total = jnp.zeros((SPREAD, LANES), jnp.float32)
        for a in range(3):
            value = nt(v.hgo[b], v.w_h[a * 384 : (a + 1) * 384, :])
            for c in range(3):
                zb(c, EDGE, SPREAD)[...] = value[:, c * 128 : (c + 1) * 128]
            for c in range(3):
                at = EDGE - steps[a * 3 + c]
                total = total + zb(c, at, SPREAD)[...]
        for block in range(4):
            lanes = slice(block * 128, (block + 1) * 128)
            v.hgo[b, :, lanes] = half_of(jnp.where(own, full_of(v.hgo[b, :, lanes]), 0.0))
        v.tmp[0:SPREAD, :] = total
        for x in range(COLS):
            v.final[pl.ds(x, TALL, stride=COLS), :] = v.tmp[pl.ds(2 + x, TALL, stride=PITCH), :]
        r = v.final[...] + full_of(v.grad_net[b])

        s = full_of(v.xc[b, 32 : 32 + AREA, 0:128])
        update, reset, cand = v.lu[b], v.lr[b], v.lc[b]
        cg = half_of(r * update * (1.0 - cand * cand))
        v.gc[b, 32 : 32 + AREA, 256:384] = cg
        reset_grad = 0.0
        for t in range(5):
            rows = slice((4 - t) * COLS, (4 - t) * COLS + AREA)
            reset_grad = reset_grad + nt(v.gc[b, rows, 256:384], v.w_ls[t * 128 : (t + 1) * 128, 256:384])
        v.gc[b, 32 : 32 + AREA, 0:128] = half_of(r * (cand - s) * update * (1.0 - update))
        v.gc[b, 32 : 32 + AREA, 128:256] = half_of(reset_grad * s * reset * (1.0 - reset))
        state_grad = r * (1.0 - update) + reset_grad * reset
        inputs_grad = 0.0
        for t in range(5):
            rows = slice((4 - t) * COLS, (4 - t) * COLS + AREA)
            state_grad = state_grad + nt(v.gc[b, rows, 0:256], v.w_ls[t * 128 : (t + 1) * 128, 0:256])
            inputs_grad = inputs_grad + nt(v.gc[b, rows, :], v.w_li[t * 256 : (t + 1) * 256, :])
        high = half_of(own_dg)
        low = half_of(own_dg - full_of(high))
        pick = half_of(jnp.where(lane_index((8, LANES)) == row_index((8, LANES)) + 126, 1.0, 0.0))
        v.tmp[0:SPAN, :] = tn(high, pick) + tn(low, pick)
        for x in range(COLS):
            v.final[pl.ds(x, TALL, stride=COLS), :] = v.tmp[pl.ds(2 + x, TALL, stride=PITCH), :]
        v.lu[b] = state_grad
        v.lr[b] = inputs_grad[:, 0:128]
        v.lc[b] = inputs_grad[:, 128:256] + v.final[...]

        def peer(t, carry):
            at = pl.ds(pl.multiple_of(t * ROWS * COLS, 16), ROWS * COLS)
            v.a_state[t, b] = half_of(v.lu[b, at, :])
            v.a_context[t, b] = half_of(v.lr[b, at, :])
            v.a_motion[t, b] = half_of(v.lc[b, at, :])
            return carry

        lax.fori_loop(0, v.space, peer, 0)
        return carry

    for c in range(3):
        zb(c, 0, EDGE)[...] = jnp.zeros((EDGE, LANES), jnp.float32)
        zb(c, EDGE + SPREAD, EDGE)[...] = jnp.zeros((EDGE, LANES), jnp.float32)
    lax.fori_loop(0, BATCH, image, 0)
    v.swap_loss.receive()
    v.back_state.start()
    v.back_context.start()
    v.back_motion.start()


def unpack_back(v, src, dst):
    def peer(t, carry):
        for b in range(BATCH):
            value = full_of(src[t, b])
            for y in range(ROWS):
                at = pl.multiple_of(y * WIDE + t * COLS, COLS)
                dst[b, pl.ds(at, COLS), :] = value[y * COLS : (y + 1) * COLS, :]
        return carry

    lax.fori_loop(0, v.space, peer, 0)


def seams():
    starts, bias_row, _, _ = flat_rows()
    edges = sorted(starts.values()) + [bias_row]
    tiles = sorted({row // 16 for row in edges if row % 16})
    parts = {}
    for low, high in zip(edges, edges[1:]):
        for tile in tiles:
            if low < (tile + 1) * 16 and high > tile * 16:
                parts[tile] = parts.get(tile, 0) + 1
    return {tile: (index, parts[tile]) for index, tile in enumerate(tiles)}


class Flush:
    def __init__(self, v):
        self.v, self.at, self.busy, self.small = v, 0, {}, []
        self.tiles = seams()
        self.left = {tile: parts for tile, (_, parts) in self.tiles.items()}
        v.seam[...] = jnp.zeros_like(v.seam)
        top = (max(self.tiles) + 1) * 16
        rest = v.out_flat.shape[0] - top
        v.seam_low[16 * 16 : 16 * 16 + rest, :] = jnp.zeros((rest, LANES), jnp.bfloat16)
        self.write(16, rest, top)

    def write(self, index, rows, base):
        v = self.v
        copy = pltpu.make_async_copy(
            v.seam_low.at[index * 16 : index * 16 + rows], v.out_flat.at[base : base + rows], v.fsem.at[index]
        )
        copy.start()
        self.small.append(copy)

    def send(self, low, length, base):
        v, slot = self.v, self.at % 2
        self.at += 1
        if slot in self.busy:
            self.busy[slot].wait()
        cast_rows(v.stage.at[slot], 0, v.flat, low, length, jnp.bfloat16)
        copy = pltpu.make_async_copy(
            v.stage.at[slot, 0:length], v.out_flat.at[base : base + length], v.ssem.at[slot, 0]
        )
        copy.start()
        self.busy[slot] = copy

    def layer(self, start, rows):
        v, stop = self.v, start + rows
        for tile in self.tiles:
            low, high = max(start, tile * 16), min(stop, tile * 16 + 16)
            if low >= high:
                continue
            index = self.tiles[tile][0]
            v.seam[index, low - tile * 16 : high - tile * 16, :] = v.flat[MARGIN + low - start : MARGIN + high - start, :]
            self.left[tile] -= 1
            if not self.left[tile]:
                v.seam_low[index * 16 : index * 16 + 16, :] = half_of(v.seam[index])
                self.write(index, 16, tile * 16)
        low, high = -(-start // 16) * 16, stop // 16 * 16
        if high > low:
            self.send(MARGIN + low - start, high - low, low)

    def settle(self):
        for copy in list(self.busy.values()) + self.small:
            copy.wait()
        self.busy, self.small = {}, []


SHARE = 3072


class Reduce:
    ORDER = ((3, 1), (3, 0), (2, 1), (2, 0), (1, 1), (1, 0), (0, 1), (0, 0))

    def __init__(self, v, count):
        self.v, self.count = v, count
        self.flying, self.queue, self.next = [], [], 0
        self.copies = {}
        rank = v.rank
        self.lower, self.upper = lax.rem(rank, 2), lax.div(rank, 2)
        self.side, self.depth = lax.rem(v.spot, 2), lax.div(v.spot, 2)
        self.group = v.space // 2
        self.part = SHARE // 4 // v.space

    def slice_at(self, spot):
        return lax.rem(spot, 2) * (SHARE // 8) + lax.div(spot, 2) * self.part

    def offer(self, number):
        self.queue += [number]

    def tick(self):
        stages = (self.core, self.across, self.stripes, self.home, self.along, self.beside)
        for entry in self.flying:
            stages[entry[1]](entry[0])
            entry[1] += 1
        self.flying = [entry for entry in self.flying if entry[1] < len(stages)]
        if self.queue:
            number = self.queue.pop(0)
            self.begin(number)
            self.flying.append([number, 0])

    def begin(self, k):
        v, slot = self.v, k % 2
        quarter, high = self.ORDER[k]
        start = quarter * self.count // (LANES * 16) * 16 + high * SHARE
        half = SHARE // 2

        def rows(which):
            return v.out_flat.at[pl.ds(pl.multiple_of(start + which * half, 16), half)]

        copy = remote(
            rows(1 - self.lower), v.rcore.at[slot], v.rsend.at[0, slot], v.rrecv.at[0, slot], {DP: v.mate}
        )
        own = pltpu.make_async_copy(rows(self.lower), v.own.at[slot], v.rlocal.at[slot])
        copy.start()
        own.start()
        self.copies[k] = (copy, own)

    def core(self, k):
        v, slot = self.v, k % 2
        copy, own = self.copies[k]
        copy.wait()
        own.wait()
        if k >= 2:
            self.x_copy(k - 2).wait_send()
        quarter = SHARE // 4

        def add(step, carry):
            at = pl.multiple_of(step * 128, 128)
            near = pl.ds(pl.multiple_of(self.upper * quarter + at, 128), 128)
            far = pl.ds(pl.multiple_of((1 - self.upper) * quarter + at, 128), 128)
            to = pl.ds(at, 128)
            v.tx[slot, to, :] = half_of(full_of(v.own[slot, far, :]) + full_of(v.rcore[slot, far, :]))
            v.ks[slot, to, :] = full_of(v.own[slot, near, :]) + full_of(v.rcore[slot, near, :])
            return carry

        lax.fori_loop(0, quarter // 128, add, 0)
        self.x_copy(k).start()

    def x_copy(self, k):
        v, slot = self.v, k % 2
        return remote(v.tx.at[slot], v.rx.at[slot], v.rsend.at[1, slot], v.rrecv.at[1, slot], {DP: v.other})

    def s_copy(self, k, step):
        v, slot = self.v, k % 2
        to = lax.rem(v.spot + step, v.space)
        src = v.ts.at[slot, pl.ds(pl.multiple_of(self.slice_at(to), 16), self.part)]
        return remote(src, v.rs.at[slot, v.spot], v.s2send.at[slot, step], v.s2recv.at[slot, step], {SPACE: to})

    def each(self, what, stop):
        def body(step, carry):
            what(step)
            return carry

        lax.fori_loop(1, stop, body, 0)

    def across(self, k):
        v, slot = self.v, k % 2
        self.x_copy(k).wait_recv()
        if k >= 2:
            self.each(lambda step: self.s_copy(k - 2, step).wait_send(), v.space)

        def add(step, carry):
            to = pl.ds(pl.multiple_of(step * 128, 128), 128)
            value = v.ks[slot, to, :] + full_of(v.rx[slot, to, :])
            v.ks[slot, to, :] = value
            v.ts[slot, to, :] = half_of(value)
            return carry

        lax.fori_loop(0, SHARE // 4 // 128, add, 0)
        v.acc[slot] = v.ks[slot, pl.ds(pl.multiple_of(self.slice_at(v.spot), 16), self.part), :]
        self.each(lambda step: self.s_copy(k, step).start(), v.space)

    def f_copy(self, k):
        v, slot = self.v, k % 2
        quarter, high = self.ORDER[k]
        return remote(
            v.fin.at[slot], v.gath.at[self.place(high, self.lower, self.upper)],
            v.fsend.at[slot], v.frecv.at[high, v.rank], {DP: quarter},
        )

    def place(self, high, lower, upper):
        at = high * SHARE + lower * (SHARE // 2) + upper * (SHARE // 4) + self.slice_at(self.v.spot)
        return pl.ds(pl.multiple_of(at, 16), self.part)

    def stripes(self, k):
        v, slot = self.v, k % 2
        quarter, high = self.ORDER[k]
        self.each(lambda step: self.s_copy(k, step).wait_recv(), v.space)

        def add(step, value):
            return value + full_of(v.rs[slot, lax.rem(v.spot + step, v.space)])

        value = half_of(lax.fori_loop(1, v.space, add, v.acc[slot]))
        if k >= 2:
            pl.when(v.rank != self.ORDER[k - 2][0])(self.f_copy(k - 2).wait_send)
        v.fin[slot] = value

        @pl.when(v.rank == quarter)
        def _():
            v.gath[self.place(high, self.lower, self.upper), :] = v.fin[slot]

        pl.when(v.rank != quarter)(self.f_copy(k).start)

    def z_copies(self, high, step):
        v = self.v
        to = lax.rem(self.depth + step, self.group) * 2 + self.side
        blocks = [v.gath.at[self.place(high, c, x)] for c in range(2) for x in range(2)]
        return [
            remote(block, block, v.zsend.at[high, step, i], v.zrecv.at[high, step, i], {SPACE: to})
            for i, block in enumerate(blocks)
        ]

    def y_copies(self, high):
        v = self.v
        out = []
        for i in range(4):
            at = pl.multiple_of(high * SHARE + i * (SHARE // 4) + self.side * (SHARE // 8), 16)
            block = v.gath.at[pl.ds(at, SHARE // 8)]
            out.append(remote(block, block, v.ysend.at[high, i], v.yrecv.at[high, i], {SPACE: v.twin}))
        return out

    def home(self, k):
        v = self.v
        quarter, high = self.ORDER[k]

        @pl.when(v.rank == quarter)
        def _():
            for source in range(4):
                if source != quarter:
                    remote(
                        v.fin.at[0], v.gath.at[self.place(high, source % 2, source // 2)],
                        v.fsend.at[0], v.frecv.at[high, source], {DP: source},
                    ).wait_recv()
            self.each(lambda step: [copy.start() for copy in self.z_copies(high, step)], self.group)

    def along(self, k):
        v = self.v
        quarter, high = self.ORDER[k]

        @pl.when(v.rank == quarter)
        def _():
            self.each(lambda step: [copy.wait() for copy in self.z_copies(high, step)], self.group)
            for copy in self.y_copies(high):
                copy.start()

    def beside(self, k):
        v = self.v
        quarter, high = self.ORDER[k]

        @pl.when(v.rank == quarter)
        def _():
            for copy in self.y_copies(high):
                copy.wait()

    def drain(self):
        v = self.v
        while self.flying or self.queue:
            self.tick()
        for k in range(len(self.ORDER) - 2, len(self.ORDER)):
            self.x_copy(k).wait_send()
            self.each(lambda step: self.s_copy(k, step).wait_send(), v.space)
            pl.when(v.rank != self.ORDER[k][0])(self.f_copy(k).wait_send)

    def finish(self):
        v, count = self.v, self.count
        v.gath[2 * SHARE :, :] = jnp.zeros((32, LANES), jnp.bfloat16)

        @pl.when(v.rank == 3)
        def _():
            at = self.bias_base() - 3 * count // (LANES * 16) * 16
            v.gath[at : at + 32, :] = half_of(full_of(v.gath[at : at + 32, :]) + v.bsum[...])

        offset = v.rank * count - quarter_base(v.rank, count) * LANES
        skip = lax.div(offset, LANES)
        matrix = lane_matrix(lax.rem(offset, LANES), False)

        def place(step, carry):
            at = pl.multiple_of(step * 256, 256)
            both = mm(v.gath[pl.ds(at, 288), :], matrix)
            v.tmp[0:288, :] = both[:, 0:LANES]
            v.tmp[288:576, :] = both[:, LANES:]
            slot = lax.rem(step, 2)
            store = pltpu.make_async_copy(v.gout.at[slot], v.out_grads.at[pl.ds(at, 256)], v.osem.at[4 + slot])
            pl.when(step > 1)(store.wait)
            v.gout[slot] = v.tmp[pl.ds(skip, 256), :] + v.tmp[pl.ds(skip + 289, 256), :]
            store.start()
            return carry

        lax.fori_loop(0, 2 * SHARE // 256, place, 0)
        for slot in range(2):
            pltpu.make_async_copy(v.gout.at[slot], v.out_grads.at[0:256], v.osem.at[4 + slot]).wait()

    def bias_base(self):
        return flat_rows()[1] // 16 * 16

    def bias_core(self):
        v = self.v
        self.b1 = remote(v.bown, v.bcore, v.bsend.at[0], v.brecv.at[0], {DP: v.mate})
        self.b1.start()

    def bias_across(self):
        v = self.v
        self.b1.wait()
        v.btwo[...] = v.bown[...] + v.bcore[...]
        self.b2 = remote(v.btwo, v.bacross, v.bsend.at[1], v.brecv.at[1], {DP: v.other})
        self.b2.start()

    def bias_stripes(self):
        v = self.v
        self.b2.wait()
        v.bfour[...] = v.btwo[...] + v.bacross[...]
        self.b3 = Swap(v, 8, v.bfour, v.ball, True)
        self.b3.start()

    def bias_end(self):
        v = self.v
        self.b3.receive()
        self.b3.sent()
        v.ball[v.spot] = v.bfour[...]
        v.bsum[...] = jnp.sum(v.ball[...], axis=0)


def ones_sum(g):
    return mm(jnp.ones((8, g.shape[0]), jnp.bfloat16), g)[0:1, :]


def keep_bias(v, name, value):
    for block in range(-(-value.shape[1] // 128)):
        at = BIAS_AT[name] + block
        v.gbias[at : at + 1, :] = value[:, block * 128 : (block + 1) * 128]


def gradients_gru(v, gates_name, cand_name, parts, g_of):
    starts, _, _, _ = flat_rows()
    total = 0.0
    for b in range(BATCH):
        total = total + ones_sum(g_of(b))
    keep_bias(v, gates_name, total[:, 0:256])
    keep_bias(v, cand_name, total[:, 256:384])

    for t in range(5):
        s_part, i_part, r_part = parts(t)
        state = tn_all(s_part, g_of, 0, 256)
        v.mm_tmp[pl.ds(MARGIN + t * 384, 128), :] = tn_all(r_part, g_of, 256, 384)
        inputs = tn_all(i_part, g_of, 0, 384)
        pack_pairs(v.flat, t * 384, 128, state[:, 0:128], state[:, 128:256])
        pack_pairs(v.flat, t * 384 + 128, 256, inputs[:, 0:128], inputs[:, 128:256])
        v.mm_tmp[pl.ds(MARGIN + t * 384 + 128, 256), :] = inputs[:, 256:384]
    v.flush.layer(starts[gates_name], 3840)
    cast_rows(v.flat, MARGIN, v.mm_tmp, MARGIN, 1920, jnp.float32)
    v.flush.layer(starts[cand_name], 1920)


def tn_all(part, g_of, low, high):
    total = 0.0
    for b in range(BATCH):
        total = total + tn(part(b), g_of(b, low, high))
    return total


def gradients_heads(v):
    starts, _, _, _ = flat_rows()
    total = 0.0
    for b in range(BATCH):
        total = total + ones_sum(v.hgo[b])
    keep_bias(v, FLOW_HIDDEN, total[:, 0:256])
    keep_bias(v, MASK_HIDDEN, total[:, 256:512])
    for name, lane in ((FLOW_HIDDEN, 0), (MASK_HIDDEN, 256)):
        for tap in range(9):
            value = 0.0
            for b in range(BATCH):
                value = value + tn(heads_part(v, b, tap)[...], v.hgo[b, :, lane : lane + 256])
            pack_pairs(v.flat, tap * 128, 128, value[:, 0:128], value[:, 128:256])
        v.flush.layer(starts[name], 2304)

    total = 0.0
    sums = 0.0
    for b in range(BATCH):
        total = total + mm(v.dtb[b], v.feat[b])
        sums = sums + jnp.sum(full_of(half_of(v.dg[b])), axis=1, keepdims=True)
    lane1 = lane_index((1, LANES))
    at = BIAS_AT[FLOW_OUT]
    v.gbias[at : at + 1, :] = jnp.where(lane1 == 0, sums[0:1, :], jnp.where(lane1 == 1, sums[1:2, :], 0.0))
    v.fo_tmp[...] = total[:, 0:128]
    v.fo_tmp2[...] = total[:, 128:256]
    for quarter in range(4):
        value = 0.0
        for which in range(2):
            rows = jnp.concatenate(
                [v.fo_tmp[pl.ds(which, 9, stride=2), :], v.fo_tmp2[pl.ds(which, 9, stride=2), :]], axis=1
            )
            value = value + nt(half_of(rows), split_pick(which, quarter))
        v.flat[pl.ds(MARGIN + quarter, 9, stride=4), :] = value
    v.flush.layer(starts[FLOW_OUT], 36)

    lane = lane_index((128, LANES))
    low_half = lane < 64
    even, odd = [], []
    total = 0.0
    for b in range(BATCH):
        total = total + ones_sum(quarter_of(v.grad_mask[b]))
    for block in range(5):
        wide = min(128, MASK - block * 128)
        at = BIAS_AT[MASK_OUT] + block
        v.gbias[at : at + 1, 0:wide] = total[:, block * 128 : block * 128 + wide]
        value = 0.0
        for b in range(BATCH):
            value = value + tn(v.mf[b], quarter_of(v.grad_mask[b, :, block * 128 : block * 128 + wide]))
        v.pair_a[:, 0:wide] = value
        even.append(v.pair_a[pl.ds(0, 128, stride=2), :])
        odd.append(pltpu.roll(v.pair_a[pl.ds(1, 128, stride=2), :], 64, 1))
    for i in range(4):
        v.flat[pl.ds(MARGIN + i, 128, stride=9), :] = even[i]
    v.flat[pl.ds(MARGIN + 4, 128, stride=9), :] = jnp.where(low_half, even[4], odd[0])
    for i in range(4):
        v.flat[pl.ds(MARGIN + 5 + i, 128, stride=9), :] = jnp.where(low_half, odd[i], odd[i + 1])
    v.flush.layer(starts[MASK_OUT], 1152)


def rows_back(v):
    v.back_state.receive()
    take_own(v, v.a_state, v.b_state)
    unpack_back(v, v.b_state, v.state)
    v.reduce.tick()
    v.back_context.receive()
    v.back_motion.receive()
    take_own(v, v.a_context, v.b_context)
    take_own(v, v.a_motion, v.b_motion)
    unpack_back(v, v.b_context, v.lr)
    unpack_back(v, v.b_motion, v.lu)

    def image(b, carry):
        at = pl.ds(pl.multiple_of(b * AREA, AREA), AREA)
        r = v.state[b]
        s = full_of(v.net[b])
        update, reset, cand = v.ru[b], v.rr[b], v.rc[b]
        cg = full_of(half_of(r * update * (1.0 - cand * cand)))
        spread_five(v, cg, None, 256, True)
        reset_grad = 0.0
        for t in range(5):
            reset_grad = reset_grad + nt(
                taps_part(v, t, 256, 384)[...], v.w_rs[t * 128 : (t + 1) * 128, 256:384]
            )
        low = full_of(half_of(r * (cand - s) * update * (1.0 - update)))
        high = full_of(half_of(reset_grad * s * reset * (1.0 - reset)))
        spread_five(v, low, None, 0, True)
        spread_five(v, high, None, 128, True)
        v.gr[b] = taps_part(v, 2, 0, 384)[...]
        state_grad = r * (1.0 - update) + reset_grad * reset
        inputs_grad = jnp.concatenate([v.lr[b], v.lu[b]], axis=1)
        for t in range(5):
            state_grad = state_grad + nt(taps_part(v, t, 0, 256)[...], v.w_rs[t * 128 : (t + 1) * 128, 0:256])
            inputs_grad = inputs_grad + nt(taps_part(v, t, 0, 384)[...], v.w_ri[t * 256 : (t + 1) * 256, :])
        v.ru[b] = state_grad
        v.rr[b] = inputs_grad[:, 0:128]
        motion = inputs_grad[:, 128:256]
        grad = half_of(motion * full_of(v.slope_m[b]))
        v.mge[b, 256:896, :] = grad
        high = half_of(motion)
        low = half_of(motion - full_of(high))
        pick = half_of(jnp.where(lane_index((16, LANES)) == row_index((16, LANES)) + 126, 1.0, 0.0))
        v.gf_base[b] = (nt(pick, high) + nt(pick, low))[0:8, :]
        return carry

    lax.fori_loop(0, BATCH, image, 0)
    v.halo_mg.start()
    v.store_gnet.start()
    v.store_gctx.start()


def gcorr_stores(v, b):
    return [
        pltpu.make_async_copy(v.mm_tmp.at[y * 328 : y * 328 + CORR], v.out_gcorr.at[b, y], v.gsem.at[y])
        for y in range(ROWS)
    ]


def encoder_back(v):
    spot, last = v.spot, v.space - 1
    v.halo_mg.receive()
    def image(b, carry):
        up = jnp.where(spot > 0, full_of(v.mge[b, 0:256, :]), 0.0)
        own = full_of(v.mge[b, 256:896, :])
        down = jnp.where(spot < last, full_of(v.mge[b, 896:1152, :]), 0.0)
        spread_rows(v, 0, (jnp.concatenate([up, own, down], axis=0),), 1152, v.xi, 0, 128, True)
        joint = 0.0
        for a in range(3):
            for c in range(3):
                k = (a * 3 + c) * 256
                joint = joint + nt(
                    v.xi[(2 - a) * 128 : (2 - a) * 128 + 896, c * 128 : (c + 1) * 128], v.w_mm[k : k + 256, :]
                )
        branch = joint * full_of(v.slope_j[b])
        low = full_of(half_of(edge_rows(v, branch[:, 0:128], WIDE)))
        high = full_of(half_of(edge_rows(v, branch[:, 128:256], WIDE)))
        v.bg[b, :, 0:128] = half_of(low[128:768])
        v.bg[b, :, 128:256] = half_of(high[128:768])
        spread_rows(v, 384, (low, high), 896, v.xi, 0, 256, True)
        corr_grad = 0.0
        flow_grad = 0.0
        for a in range(3):
            rows = slice((2 - a) * 128, (2 - a) * 128 + 640)
            for c in range(3):
                k = a * 3 + c
                corr_grad = corr_grad + nt(v.xi[rows, 384 + c * 256 : 384 + (c + 1) * 256], v.w_cm[k * 256 : (k + 1) * 256, :])
                flow_grad = flow_grad + nt(
                    v.xi[rows, 384 + c * 256 + 128 : 384 + (c + 1) * 256], v.w_fm[k * 128 : (k + 1) * 128, :]
                )
        v.cpg[b] = half_of(corr_grad * full_of(v.slope_ci[b]))
        v.fpg[b] = half_of(flow_grad * full_of(v.slope_fi[b]))
        stores = gcorr_stores(v, b)
        for store in stores:
            pl.when(b > 0)(store.wait)
        gcorr = nt(v.w_ci[...], v.cpg[b])
        for y in range(ROWS):
            v.mm_tmp[y * 328 : y * 328 + CORR, :] = gcorr[:, y * WIDE : (y + 1) * WIDE]
        for store in stores:
            store.start()
        z = nt(v.w_fi[...], v.fpg[b])
        total = jnp.zeros((32, LANES), jnp.float32)
        lane = lane_index((32, LANES))
        for across in range(7):
            v.fs[across] = jnp.zeros((32, LANES), jnp.float32)
            for y in range(ROWS):
                v.fs[across, 2 * y : 2 * y + 16, :] += z[across * 16 : across * 16 + 16, y * 128 : (y + 1) * 128]
            d = across - 3
            value = v.fs[across]
            if d:
                value = pltpu.roll(value, d % LANES, 1)
                value = jnp.where((lane - d >= 0) & (lane - d < WIDE), value, 0.0)
            total = total + value
        v.gf[b] = total
        return carry

    lax.fori_loop(0, BATCH, image, 0)
    v.halo_gf.start()


def gradients_encoder(v):
    starts, bias_row, spots, inner = flat_rows()
    for store in gcorr_stores(v, 0):
        store.wait()

    def summed(ref, name):
        total = 0.0
        for b in range(BATCH):
            total = total + ones_sum(ref(b))
        keep_bias(v, name, total)

    summed(lambda b: v.mge[b, 256:896, :], MOTION_MIX)
    summed(lambda b: v.bg[b], CORR_MIX)
    summed(lambda b: v.bg[b, :, 128:256], FLOW_MIX)
    summed(lambda b: v.cpg[b], CORR_IN)
    summed(lambda b: v.fpg[b], FLOW_IN)

    for k in range(9):
        a, c = k // 3, k % 3
        value = 0.0
        for b in range(BATCH):
            value = value + tn(
                v.hx_j[b, a * 128 : a * 128 + 640, c * 256 : (c + 1) * 256], v.mge[b, 256:896, :]
            )
        v.mm_tmp[k * 256 : (k + 1) * 256, :] = value
    lane36 = lane_index((36, LANES))
    for r in range(63):
        first = v.mm_tmp[pl.ds(r, 36, stride=64), :]
        second = v.mm_tmp[pl.ds(r + 1, 36, stride=64), :]
        if r:
            first = pltpu.roll(first, LANES - 2 * r, 1)
        second = pltpu.roll(second, 126 - 2 * r, 1)
        v.flat[pl.ds(MARGIN + r, 36, stride=63), :] = jnp.where(lane36 < 126 - 2 * r, first, second)
    v.flush.layer(starts[MOTION_MIX], 2268)
    v.flush.settle()
    v.reduce.offer(5)
    v.reduce.tick()

    bias_tile(v)
    v.reduce.bias_core()
    for k in range(9):
        a, c = k // 3, k % 3
        value = 0.0
        for b in range(BATCH):
            value = value + tn(
                v.hx_f[b, (a + 1) * 128 : (a + 1) * 128 + 640, c * 128 : (c + 1) * 128], v.bg[b, :, 128:256]
            )
        v.pair_a[0:128, :] = value
        even, odd = (v.pair_a[pl.ds(i, 64, stride=2), :] for i in range(2))
        v.flat[MARGIN + 64 * k : MARGIN + 64 * (k + 1), :] = jnp.where(
            lane_index((64, LANES)) < 64, pltpu.roll(even, 64, 1), odd
        )
    v.flush.layer(starts[FLOW_MIX], 576)

    value = 0.0
    for b in range(BATCH):
        value = value + mm(v.xt[b, :, 256:896], v.fpg[b])
    v.flow_tmp[...] = value
    for across in range(7):
        for comp in range(2):
            v.flat[pl.ds(MARGIN + across * 2 + comp, 7, stride=14), :] = v.flow_tmp[
                pl.ds(across * 16 + comp, 7, stride=2), :
            ]
    v.flush.layer(starts[FLOW_IN], 98)
    v.reduce.bias_across()
    v.reduce.tick()
    lane = lane_index((128, LANES))
    low_half = lane < 64
    for k in range(9):
        a, c = k // 3, k % 3
        value = 0.0
        for b in range(BATCH):
            value = value + tn(
                v.hx_c[b, (a + 1) * 128 : (a + 1) * 128 + 640, c * 256 : (c + 1) * 256], v.bg[b]
            )
        v.pair_a[...] = value[:, 0:128]
        v.pair_b[...] = value[:, 128:256]
        even, odd = (v.pair_a[pl.ds(i, 128, stride=2), :] for i in range(2))
        even_high, odd_high = (v.pair_b[pl.ds(i, 128, stride=2), :] for i in range(2))
        odd, odd_high = pltpu.roll(odd, 64, 1), pltpu.roll(odd_high, 64, 1)
        at = MARGIN + 384 * k
        v.flat[pl.ds(at, 128, stride=3), :] = even
        v.flat[pl.ds(at + 1, 128, stride=3), :] = jnp.where(low_half, even_high, odd)
        v.flat[pl.ds(at + 2, 128, stride=3), :] = jnp.where(low_half, odd, odd_high)
        if k == 4:
            v.reduce.tick()
    v.flush.layer(starts[CORR_MIX], 3456)

    v.flush.settle()
    v.reduce.offer(6)
    v.reduce.tick()
    v.reduce.bias_stripes()
    value = 0.0
    for b in range(BATCH):
        value = value + mm(lines_of(v.corr, b, ROWS), v.cpg[b])
    pack_pairs(v.flat, 0, 324, value[:, 0:128], value[:, 128:256])
    v.flush.layer(starts[CORR_IN], 648)

    v.flush.settle()
    v.reduce.offer(7)
    v.reduce.tick()


def bias_tile(v):
    starts, bias_row, spots, inner = flat_rows()
    lead = bias_row % 16
    lane1 = lane_index((1, LANES))
    v.bown[...] = jnp.zeros_like(v.bown)
    for name, height, width in shapes():
        for block in range(-(-width // LANES)):
            value = v.gbias[BIAS_AT[name] + block : BIAS_AT[name] + block + 1, :]
            if name == FLOW_MIX:
                value = pltpu.roll(value, 64, 1)
            left = width - block * LANES
            if left < LANES:
                value = jnp.where(lane1 < left, value, 0.0)
            at = spots[name] + block * LANES
            row, shift = lead + at // LANES, at % LANES
            moved = pltpu.roll(value, shift, 1) if shift else value
            v.bown[row : row + 1, :] = v.bown[row : row + 1, :] + jnp.where(lane1 >= shift, moved, 0.0)
            if shift:
                v.bown[row + 1 : row + 2, :] = v.bown[row + 1 : row + 2, :] + jnp.where(lane1 < shift, moved, 0.0)


def finish(v):
    spot, last = v.spot, v.space - 1
    v.halo_gf.receive()
    for b in range(BATCH):
        v.tmp2[...] = v.gf[b]
        up = jnp.where(spot > 0, v.gf_up[b], 0.0)
        down = jnp.where(spot < last, v.gf_down[b], 0.0)
        v.tmp2[6:12, :] += up[16:22, :]
        v.tmp2[10:16, :] += down[0:6, :]
        for y in range(ROWS):
            v.out_gflow[b, 2 * y : 2 * y + 2, :] = (
                v.tmp2[6 + 2 * y : 8 + 2 * y, :] + v.gf_base[b, 0:2, y * 128 : (y + 1) * 128]
            )
    v.loss_in[v.spot] = v.losses[...]
    total = jnp.sum(v.loss_in[...], axis=0)
    counts = jnp.sum(v.counts[...], axis=0)
    v.out_loss[...] = total / jnp.maximum(counts, 1.0)


class View:
    pass


def main_kernel(names, space, count, *refs):
    v = View()
    for name, ref in zip(names, refs):
        setattr(v, name, ref)
    v.space = space
    v.lu, v.lc = v.motion, v.state
    v.spot = lax.axis_index(SPACE)
    v.rank = lax.axis_index(DP)
    v.mate, v.other, v.twin = mate_of(v.rank), lax.rem(v.rank + 2, 4), mate_of(v.spot)
    spot = v.spot
    barrier = pltpu.get_barrier_semaphore()

    def hello(step, carry):
        pl.semaphore_signal(barrier, inc=1, device_id={SPACE: lax.rem(spot + step, space)}, device_id_type=MESH)
        return carry

    lax.fori_loop(1, space, hello, 0)
    for step in range(1, 4):
        pl.semaphore_signal(barrier, inc=1, device_id={DP: lax.rem(v.rank + step, 4)}, device_id_type=MESH)
    pl.semaphore_wait(barrier, space + 2)

    v.store_gnet = pltpu.make_async_copy(v.ru, v.out_gnet, v.osem.at[0])
    v.store_gctx = pltpu.make_async_copy(v.rr, v.out_gctx, v.osem.at[1])
    rows = row_index((8, LANES))
    counted = jnp.zeros((8, LANES), jnp.float32)
    for b in range(BATCH):
        counted = jnp.where(rows == b, jnp.sum(v.valid[b, 0:1, :]), counted)
    v.count_out[...] = counted
    v.pick_count = lambda counts, b: jnp.sum(jnp.where((rows == b) & (lane_index((8, LANES)) == 0), counts, 0.0))
    v.swap_count = Swap(v, 0, v.count_out, v.counts, True)
    v.swap_context = Swap(v, 1, v.a_context, v.b_context)
    v.swap_motion = Swap(v, 2, v.a_motion, v.b_motion)
    v.swap_state = Swap(v, 3, v.a_state, v.b_state)
    v.back_context = Swap(v, 4, v.a_context, v.b_context)
    v.back_motion = Swap(v, 5, v.a_motion, v.b_motion)
    v.back_state = Swap(v, 6, v.a_state, v.b_state)
    v.swap_loss = Swap(v, 7, v.losses, v.loss_in, True)
    v.halo_corr = Halo(v, 0, v.corr.at[:, 0:2], v.corr.at[:, 3:5], v.corr_down, v.corr_up)
    v.halo_flow = Halo(v, 1, v.flow, v.flow, v.flow_down, v.flow_up)
    v.halo_final = Halo(v, 2, v.e_left, v.e_right, v.f_right, v.f_left)
    v.halo_mask = Halo(v, 3, v.m_left, v.m_right, v.n_right, v.n_left)
    v.halo_dg = Halo(v, 4, v.dg, v.dg, v.dg_right, v.dg_left)
    v.halo_mg = Halo(v, 5, v.mge.at[:, 256:512], v.mge.at[:, 640:896], v.mge.at[:, 896:1152], v.mge.at[:, 0:256])
    v.halo_gf = Halo(v, 6, v.gf, v.gf, v.gf_down, v.gf_up)

    v.halo_corr.start()
    v.halo_flow.start()
    v.swap_count.start()

    def first(b, carry):
        v.state[b] = full_of(v.context[b])
        pack_rows(v, v.state, b, v.a_context)
        return carry

    lax.fori_loop(0, BATCH, first, 0)
    v.swap_context.start()
    unpack_all(v, count)
    v.halo_flow.receive()
    v.halo_corr.receive()
    forward_rows(v)
    keep = [pltpu.make_async_copy(v.hx_c, v.out_keep_c, v.ksem.at[0]), pltpu.make_async_copy(v.hx_f, v.out_keep_f, v.ksem.at[1])]
    for copy in keep:
        copy.start()
    mask_gradient(v)
    v.swap_context.receive()
    v.swap_motion.receive()
    v.swap_state.receive()
    take_own(v, v.a_context, v.b_context)
    take_own(v, v.a_motion, v.b_motion)
    take_own(v, v.a_state, v.b_state)
    columns_in(v)
    columns_forward(v)
    for copy in keep:
        copy.wait()
    heads(v)
    mask_output(v)
    v.swap_context.sent()
    v.swap_motion.sent()
    v.swap_state.sent()
    heads_back(v)
    v.flush = Flush(v)
    red = v.reduce = Reduce(v, count)
    gradients_heads(v)
    v.flush.settle()
    red.offer(0)
    red.tick()
    gradients_gru(
        v,
        COLUMNS_GATES,
        COLUMNS_CANDIDATE,
        lambda t: (
            lambda b: v.xc[b, t * COLS : t * COLS + AREA, 0:128],
            lambda b: v.xc[b, t * COLS : t * COLS + AREA, 128:384],
            lambda b: v.xcr[b, t * COLS : t * COLS + AREA, :],
        ),
        lambda b, low=0, high=384: v.gc[b, 32 : 32 + AREA, low:high],
    )
    v.flush.settle()
    red.offer(1)
    red.offer(2)
    red.tick()
    rows_back(v)
    red.tick()
    keep = [pltpu.make_async_copy(v.out_keep_c, v.hx_c, v.ksem.at[0]), pltpu.make_async_copy(v.out_keep_f, v.hx_f, v.ksem.at[1])]
    for copy in keep:
        copy.start()
    gradients_gru(
        v,
        ROWS_GATES,
        ROWS_CANDIDATE,
        lambda t: (
            lambda b: v.xs[b * AREA : (b + 1) * AREA, t * 128 : (t + 1) * 128],
            lambda b: v.xi[b * AREA : (b + 1) * AREA, t * 256 : (t + 1) * 256],
            lambda b: v.xr[b * AREA : (b + 1) * AREA, t * 128 : (t + 1) * 128],
        ),
        lambda b, low=0, high=384: v.gr[b, :, low:high],
    )
    v.flush.settle()
    red.offer(3)
    red.offer(4)
    red.tick()
    encoder_back(v)
    red.tick()
    for copy in keep:
        copy.wait()
    gradients_encoder(v)
    finish(v)
    red.tick()
    red.bias_end()
    red.drain()
    red.finish()
    for swap in (v.swap_count, v.back_context, v.back_motion, v.back_state, v.swap_loss):
        swap.sent()
    for halo in (v.halo_corr, v.halo_flow, v.halo_final, v.halo_mask, v.halo_dg, v.halo_mg, v.halo_gf):
        halo.sent()
    v.store_gnet.wait()
    v.store_gctx.wait()
    pltpu.make_async_copy(v.mask_low, v.out_mask.at[0], v.osem.at[3]).wait()


def main_call(space, count, gathered, net, context, corr, flow, target, valid, grad_net, grad_mask):
    total = 3 * count // (LANES * 16) * 16 + BLOCK
    low, wide = jnp.bfloat16, jnp.float32
    peers = (space, BATCH, ROWS * COLS, LANES)
    ins = dict(
        gathered=gathered, net=net, context=context, corr=corr, flow=flow, target=target, valid=valid,
        grad_net=grad_net, grad_mask=grad_mask,
    )
    outs = dict(
        out_net=((BATCH, AREA, 128), low),
        out_flow=((BATCH, 8, SPAN), wide),
        out_mask=((BATCH, AREA, MASK), low),
        out_loss=((8, 128), wide),
        out_flat=((total, 128), low),
        out_gnet=((BATCH, AREA, 128), wide),
        out_gctx=((BATCH, AREA, 128), wide),
        out_gcorr=((BATCH, ROWS, CORR, 128), wide),
        out_gflow=((BATCH, 16, 128), wide),
        out_keep_c=((BATCH, 1152, 768), low),
        out_keep_f=((BATCH, 1152, 384), low),
        out_grads=((BLOCK, 128), wide),
    )
    scratch = dict(
        stage=((2, 3904, 128), low),
        seam=((16, 16, 128), wide),
        mask_low=((AREA, MASK), low),
        gout=((2, 256, 128), wide),
        seam_low=((16 * 20, 128), low),
        own=((2, SHARE // 2, 128), low),
        rcore=((2, SHARE // 2, 128), low),
        tx=((2, SHARE // 4, 128), low),
        rx=((2, SHARE // 4, 128), low),
        ks=((2, SHARE // 4, 128), wide),
        ts=((2, SHARE // 4, 128), low),
        acc=((2, SHARE // 4 // space, 128), wide),
        rs=((2, space, SHARE // 4 // space, 128), low),
        fin=((2, SHARE // 4 // space, 128), low),
        gath=((2 * SHARE + 32, 128), low),
        bown=((32, 128), wide), bcore=((32, 128), wide), btwo=((32, 128), wide), bacross=((32, 128), wide),
        bfour=((32, 128), wide), ball=((space, 32, 128), wide), bsum=((32, 128), wide),
        flat=((3904, 128), wide),
        pair_a=((256, 128), wide),
        pair_b=((256, 128), wide),
        flow_tmp=((112, 128), wide),
        mm_tmp=((3 * (2 * EDGE + SPREAD), 128), wide),
        fo_tmp=((32, 128), wide),
        fo_tmp2=((32, 128), wide),
        w_ci=((CORR, 256), low),
        w_cm=((2304, 256), low),
        w_fi=((112, 128), low),
        w_fm=((1152, 128), low),
        w_mm=((2304, 128), low),
        w_ri=((1280, 384), low),
        w_rs=((640, 384), low),
        w_li=((1280, 384), low),
        w_ls=((640, 384), low),
        w_h=((1152, 512), low),
        w_fo=((32, 256), low),
        w_mo=((256, 640), low),
        bias=((BIAS_ROWS, 128), wide),
        gbias=((BIAS_ROWS, 128), wide),
        corr_up=((BATCH, 2, CORR, 128), low),
        corr_down=((BATCH, 2, CORR, 128), low),
        flow_up=((BATCH, 16, 128), wide),
        flow_down=((BATCH, 16, 128), wide),
        fs=((7, 32, 128), wide),
        xt=((BATCH, 112, 1152), low),
        tmp=((1168, 128), wide),
        tmp2=((32, 128), wide),
        hx_c=((BATCH, 1152, 768), low),
        hx_f=((BATCH, 1152, 384), low),
        hx_j=((BATCH, 896, 768), low),
        slope_ci=((BATCH, AREA, 256), low),
        slope_fi=((BATCH, AREA, 128), low),
        slope_j=((BATCH, 896, 256), low),
        slope_m=((BATCH, AREA, 128), low),
        motion=((BATCH, AREA, 128), wide),
        state=((BATCH, AREA, 128), wide),
        xi=((BATCH * AREA, 1280), low),
        xs=((BATCH * AREA, 640), low),
        xr=((BATCH * AREA, 640), low),
        ru=((BATCH, AREA, 128), wide),
        rr=((BATCH, AREA, 128), wide),
        rc=((BATCH, AREA, 128), wide),
        lr=((BATCH, AREA, 128), wide),
        a_state=(peers, low), a_context=(peers, low), a_motion=(peers, low),
        b_state=(peers, low), b_context=(peers, low), b_motion=(peers, low),
        xc=((BATCH, AREA + 64, 384), low),
        xcr=((BATCH, AREA + 64, 128), low),
        gc=((BATCH, AREA + 64, 384), low),
        final=((AREA, 128), wide),
        e_left=((BATCH, 2, 48, 128), low), e_right=((BATCH, 2, 48, 128), low),
        f_left=((BATCH, 2, 48, 128), low), f_right=((BATCH, 2, 48, 128), low),
        m_left=((BATCH, 2, 48, 128), low), m_right=((BATCH, 2, 48, 128), low),
        n_left=((BATCH, 2, 48, 128), low), n_right=((BATCH, 2, 48, 128), low),
        slope_h=((BATCH, SPREAD, 512), low),
        feat=((BATCH, SPAN, 256), low),
        mf=((BATCH, AREA, 256), low),
        zt=((32, SPAN), wide),
        dg=((BATCH, 8, SPAN), wide),
        dg_left=((BATCH, 8, SPAN), wide), dg_right=((BATCH, 8, SPAN), wide),
        dt=((32, SPAN), wide),
        dto=((32, SPAN), wide),
        dtb=((BATCH, 32, SPAN), low),
        hgo=((BATCH, SPREAD, 512), low),
        gr=((BATCH, AREA, 384), low),
        mge=((BATCH, 1152, 128), low),
        bg=((BATCH, AREA, 256), low),
        cpg=((BATCH, AREA, 256), low),
        fpg=((BATCH, AREA, 128), low),
        gf_base=((BATCH, 8, AREA), wide),
        gf=((BATCH, 32, 128), wide), gf_up=((BATCH, 32, 128), wide), gf_down=((BATCH, 32, 128), wide),
        count_out=((8, 128), wide), counts=((space, 8, 128), wide),
        losses=((8, 128), wide), loss_in=((space, 8, 128), wide),
    )
    sems = dict(
        hsend=pltpu.SemaphoreType.DMA((7, 2)), hrecv=pltpu.SemaphoreType.DMA((7, 2)),
        asend=pltpu.SemaphoreType.DMA((9, space)), arecv=pltpu.SemaphoreType.DMA((9, space)),
        ssem=pltpu.SemaphoreType.DMA((2, 2)),
        fsem=pltpu.SemaphoreType.DMA((17,)),
        rsend=pltpu.SemaphoreType.DMA((2, 2)), rrecv=pltpu.SemaphoreType.DMA((2, 2)),
        rlocal=pltpu.SemaphoreType.DMA((2,)),
        s2send=pltpu.SemaphoreType.DMA((2, space)), s2recv=pltpu.SemaphoreType.DMA((2, space)),
        fsend=pltpu.SemaphoreType.DMA((2,)), frecv=pltpu.SemaphoreType.DMA((2, 4)),
        zsend=pltpu.SemaphoreType.DMA((2, space // 2, 4)), zrecv=pltpu.SemaphoreType.DMA((2, space // 2, 4)),
        ysend=pltpu.SemaphoreType.DMA((2, 4)), yrecv=pltpu.SemaphoreType.DMA((2, 4)),
        bsend=pltpu.SemaphoreType.DMA((2,)), brecv=pltpu.SemaphoreType.DMA((2,)),
        ksem=pltpu.SemaphoreType.DMA((2,)),
        gsem=pltpu.SemaphoreType.DMA((ROWS,)),
        osem=pltpu.SemaphoreType.DMA((6,)),
    )
    vmem = pl.BlockSpec(memory_space=pltpu.VMEM)
    hbm = pl.BlockSpec(memory_space=pl.ANY)
    names = list(ins) + list(outs) + list(scratch) + list(sems)
    return pl.pallas_call(
        functools.partial(main_kernel, names, space, count),
        out_shape=[jax.ShapeDtypeStruct(*entry) for entry in outs.values()],
        in_specs=[hbm if name == "gathered" else vmem for name in ins],
        out_specs=[hbm if name in ("out_flat", "out_gnet", "out_gctx", "out_gcorr", "out_keep_c", "out_keep_f", "out_mask", "out_grads") else vmem for name in outs],
        scratch_shapes=[pltpu.VMEM(*entry) for entry in scratch.values()] + list(sems.values()),
        compiler_params=pltpu.CompilerParams(
            collective_id=2, has_side_effects=True, vmem_limit_bytes=VMEM_LIMIT
        ),
    )(*ins.values())


VMEM_LIMIT = 64 * 2**20 - 2**17


def shards_wide(net, context, corr, flow, target, valid, grad_net, grad_mask, params):
    space = lax.axis_size(SPACE)
    count = params.shape[0]
    gathered = gather_blocks(params).reshape(4 * BLOCK, LANES)
    flow_rows = jnp.transpose(flow.astype(jnp.float32), (0, 2, 1, 3)).reshape(BATCH, 2 * ROWS, WIDE)
    flow_rows = jnp.pad(flow_rows, ((0, 0), (0, 16 - 2 * ROWS), (0, 0)))
    pad = ((0, 0), (0, 0), (0, 0), (2, 2))
    target_ext = jnp.pad(target, pad).reshape(BATCH, 2, SPREAD)
    target_ext = jnp.pad(target_ext, ((0, 0), (0, 6), (0, SPAN - SPREAD)))
    valid_ext = jnp.pad(valid.astype(jnp.float32)[:, None], pad).reshape(BATCH, 1, SPREAD)
    valid_ext = jnp.broadcast_to(jnp.pad(valid_ext, ((0, 0), (0, 0), (0, SPAN - SPREAD))), (BATCH, 8, SPAN))
    outs = main_call(
        space, count, gathered, net.reshape(BATCH, AREA, HID), context.reshape(BATCH, AREA, CTX),
        jnp.transpose(corr, (0, 1, 3, 2)), flow_rows, target_ext, valid_ext,
        grad_net.reshape(BATCH, AREA, HID), grad_mask.reshape(BATCH, AREA, MASK),
    )
    new_net, new_flow, mask, loss, _, gnet, gctx, gcorr, gflow = outs[:9]
    new_flow = new_flow[:, 0:2, 0:SPREAD].reshape(BATCH, 2, TALL, PITCH)[..., 2 : 2 + COLS]
    grads = outs[-1].reshape(-1)[:count]
    return (
        new_net.reshape(BATCH, TALL, COLS, HID),
        new_flow,
        mask.reshape(BATCH, TALL, COLS, MASK),
        loss[0:BATCH, 0],
        grads,
        gnet.reshape(BATCH, ROWS, WIDE, HID),
        gctx.reshape(BATCH, ROWS, WIDE, CTX),
        jnp.transpose(gcorr, (0, 1, 3, 2)),
        jnp.transpose(gflow[:, 0 : 2 * ROWS].reshape(BATCH, ROWS, 2, WIDE), (0, 2, 1, 3)),
    )


def solution(mesh):
    def plan(*arrays):
        net, valid = arrays[0], arrays[5]
        if (net.shape[1:3], valid.shape[1:]) == ((ROWS, WIDE), (TALL, COLS)):
            return shards_wide(*arrays)
        return shards(*arrays)

    return jax.shard_map(
        plan,
        mesh=mesh,
        in_specs=(
            P(DP, SPACE, None, None),
            P(DP, SPACE, None, None),
            P(DP, SPACE, None, None),
            P(DP, None, SPACE, None),
            P(DP, None, None, SPACE),
            P(DP, None, SPACE),
            P(DP, None, SPACE, None),
            P(DP, None, SPACE, None),
            P(DP),
        ),
        out_specs=(
            P(DP, None, SPACE, None),
            P(DP, None, None, SPACE),
            P(DP, None, SPACE, None),
            P(DP),
            P(DP),
            P(DP, SPACE, None, None),
            P(DP, SPACE, None, None),
            P(DP, SPACE, None, None),
            P(DP, None, SPACE, None),
        ),
        check_vma=False,
    )
```

```python
import functools

import jax
import jax.numpy as jnp
from jax import lax
from jax.experimental import pallas as pl
from jax.experimental.pallas import tpu as pltpu
from jax.sharding import PartitionSpec as P

HID = 128
CTX = 128
MOT = 128
CORR = 324
SPACE = "space"
DP = "dp"
(
    CORR_IN,
    CORR_MIX,
    FLOW_IN,
    FLOW_MIX,
    MOTION_MIX,
    ROWS_GATES,
    ROWS_CANDIDATE,
    COLUMNS_GATES,
    COLUMNS_CANDIDATE,
    FLOW_HIDDEN,
    FLOW_OUT,
    MASK_HIDDEN,
    MASK_OUT,
) = range(13)
C1 = 256
C2 = 192
F1 = 128
F2 = 64
HEAD = 256
MASK = 576


def with_halo(block, sides, width):
    for axis, dim in sides:
        count = lax.axis_size(axis)
        forward = [(i, i + 1) for i in range(count - 1)]
        backward = [(target, source) for source, target in forward]
        low = lax.ppermute(
            lax.slice_in_dim(block, block.shape[dim] - width, None, axis=dim), axis, forward
        )
        high = lax.ppermute(lax.slice_in_dim(block, 0, width, axis=dim), axis, backward)
        block = jnp.concatenate([low, block, high], axis=dim)
    return block


def shapes():
    inputs_width = HID + CTX + MOT
    return [
        (CORR_IN, CORR, C1),
        (CORR_MIX, 9 * C1, C2),
        (FLOW_IN, 98, F1),
        (FLOW_MIX, 9 * F1, F2),
        (MOTION_MIX, 9 * (C2 + F2), MOT - 2),
        (ROWS_GATES, 5 * inputs_width, 2 * HID),
        (ROWS_CANDIDATE, 5 * inputs_width, HID),
        (COLUMNS_GATES, 5 * inputs_width, 2 * HID),
        (COLUMNS_CANDIDATE, 5 * inputs_width, HID),
        (FLOW_HIDDEN, 9 * HID, HEAD),
        (FLOW_OUT, 9 * HEAD, 2),
        (MASK_HIDDEN, 9 * HID, HEAD),
        (MASK_OUT, HEAD, MASK),
    ]


def unpack(flat):
    weights = {}
    biases = {}
    offset = 0
    table = shapes()
    for name, height, width in table:
        weights[name] = flat[offset // LANES : (offset + height * width) // LANES].reshape(height, width)
        offset = offset + height * width
    rest = flat[offset // LANES :].reshape(-1)
    offset = 0
    for name, height, width in table:
        biases[name] = rest[offset : offset + width].astype(jnp.float32)
        offset = offset + width
    return (weights, biases)


def pack(grads, total):
    table = shapes()
    rows = [grads[entry[0]][0].astype(jnp.bfloat16).reshape(-1, LANES) for entry in table]
    biases = jnp.concatenate([grads[entry[0]][1] for entry in table]).astype(jnp.bfloat16)
    left = total * LANES - sum(entry[1] * entry[2] for entry in table) - biases.shape[0]
    return jnp.concatenate(rows + [jnp.pad(biases, (0, left)).reshape(-1, LANES)])


def patches(padded, tall, wide):
    out_rows = padded.shape[1] - tall + 1
    out_columns = padded.shape[2] - wide + 1
    return jnp.concatenate(
        [
            padded[:, down : down + out_rows, across : across + out_columns]
            for down in range(tall)
            for across in range(wide)
        ],
        axis=-1,
    )


def apply(stacked, weight):
    return jnp.einsum("bhwk,ko->bhwo", stacked, weight, preferred_element_type=jnp.float32)


def apply_back(grad, weight):
    return jnp.einsum("bhwo,ko->bhwk", grad, weight, preferred_element_type=jnp.float32)


def weight_grad(stacked, pre_grad):
    return jnp.einsum("bhwk,bhwo->ko", stacked, pre_grad, preferred_element_type=jnp.float32)


def record(grads, name, stacked, pre_grad):
    grads[name] = (
        weight_grad(stacked, pre_grad),
        jnp.sum(pre_grad, axis=(0, 1, 2), dtype=jnp.float32),
    )


def flipped(weight, tall, wide):
    inner = weight.shape[0] // (tall * wide)
    shaped = weight.reshape(tall, wide, inner, weight.shape[1])[::-1, ::-1]
    return jnp.transpose(shaped, (0, 1, 3, 2)).reshape(-1, inner)


def slope(pre):
    sigma = jax.nn.sigmoid(pre)
    return sigma * (1.0 + pre * (1.0 - sigma))


def local_pad(field, tall, wide):
    return jnp.pad(field, ((0, 0), (tall // 2, tall // 2), (wide // 2, wide // 2), (0, 0)))


def row_pad(field, tall):
    field = with_halo(field, ((SPACE, 1),), tall // 2)
    return jnp.pad(field, ((0, 0), (0, 0), (tall // 2, tall // 2), (0, 0)))


def column_pad(field, tall, wide):
    field = with_halo(field, ((SPACE, 2),), wide // 2)
    return jnp.pad(field, ((0, 0), (tall // 2, tall // 2), (0, 0), (0, 0)))


MESH = pl.DeviceIdType.MESH
LANES = 128
BLOCK = 6144


def quarter_start(rank, count):
    return lax.div(rank * count, LANES)


def quarter_base(rank, count):
    return lax.div(rank * count, LANES * 16) * 16


def mate_of(rank):
    return rank + 1 - 2 * lax.rem(rank, 2)


def remote(src, dst, send, recv, device):
    return pltpu.make_async_remote_copy(
        src_ref=src, dst_ref=dst, send_sem=send, recv_sem=recv, device_id=device, device_id_type=MESH
    )


def greet(devices):
    barrier = pltpu.get_barrier_semaphore()
    for device in devices:
        pl.semaphore_signal(barrier, inc=1, device_id=device, device_id_type=MESH)
    pl.semaphore_wait(barrier, len(devices))


def lane_matrix(shift, forward):
    source = lax.broadcasted_iota(jnp.int32, (LANES, 2 * LANES), 0)
    target = lax.broadcasted_iota(jnp.int32, (LANES, 2 * LANES), 1)
    if forward:
        return jnp.where(target == source + shift, 1.0, 0.0).astype(jnp.bfloat16)
    return jnp.where(lax.rem(target + LANES, 2 * LANES) == source - shift + LANES, 1.0, 0.0).astype(jnp.bfloat16)


def gather_kernel(count, local_ref, out_ref, own_ref, send, recv):
    rank, spot = lax.axis_index(DP), lax.axis_index(SPACE)
    mate, across, twin = mate_of(rank), lax.rem(rank + 2, 4), mate_of(spot)
    pieces = 4
    rows = BLOCK // 2 // pieces
    peers = ({DP: mate}, {DP: across}, {SPACE: twin})
    greet(peers)
    matrix = lane_matrix(lax.rem(rank * count, LANES), True)
    first = lax.broadcasted_iota(jnp.int32, (256, LANES), 0) == 0

    def rotate(step, carry):
        at = pl.ds(pl.multiple_of(step * 256, 256), 256)
        both = jnp.dot(local_ref[at, :], matrix, preferred_element_type=jnp.float32)
        spill = pltpu.roll(both[:, LANES:], 1, 0)
        own_ref[at, :] = (both[:, :LANES] + jnp.where(first, carry, spill)).astype(jnp.bfloat16)
        return spill[0:1]

    lax.fori_loop(0, BLOCK // 256, rotate, jnp.zeros((1, LANES), jnp.float32))

    half, other_half = lax.rem(spot, 2), lax.rem(spot + 1, 2)

    def piece(which, index):
        return pl.ds(pl.multiple_of(which * (BLOCK // 2) + index * rows, 16), rows)

    own_x = [
        remote(own_ref.at[piece(half, k)], out_ref.at[rank, piece(half, k)], send.at[0, k], recv.at[0, k], peers[1])
        for k in range(pieces)
    ]
    own_c = remote(own_ref, out_ref.at[rank], send.at[4, 0], recv.at[4, 0], peers[0])
    for copy in own_x:
        copy.start()
    own_c.start()
    later = []
    for k in range(pieces):
        own_x[k].wait_recv()
        block = out_ref.at[across, piece(half, k)]
        to_twin = remote(block, block, send.at[1, k], recv.at[1, k], peers[2])
        to_mate = remote(block, block, send.at[2, k], recv.at[2, k], peers[0])
        to_twin.start()
        to_mate.start()
        later.append((to_twin, to_mate))
    for at in range(BLOCK // 256):
        out_ref[rank, at * 256 : (at + 1) * 256, :] = own_ref[at * 256 : (at + 1) * 256, :]
    for k in range(pieces):
        later[k][0].wait_recv()
        block = out_ref.at[across, piece(other_half, k)]
        to_mate = remote(block, block, send.at[3, k], recv.at[3, k], peers[0])
        to_mate.start()
        later.append((to_mate,))
    for k in range(pieces):
        own_x[k].wait_send()
        later[k][0].wait_send()
        later[k][1].wait()
        later[pieces + k][0].wait()
    own_c.wait()


def gather_blocks(params):
    count = params.shape[0]
    local = jnp.pad(params, (0, BLOCK * LANES - count)).reshape(BLOCK, LANES)
    return pl.pallas_call(
        functools.partial(gather_kernel, count),
        out_shape=jax.ShapeDtypeStruct((4, BLOCK, LANES), jnp.bfloat16),
        in_specs=[pl.BlockSpec(memory_space=pltpu.VMEM)],
        out_specs=pl.BlockSpec(memory_space=pltpu.VMEM),
        scratch_shapes=[
            pltpu.VMEM((BLOCK, LANES), jnp.bfloat16),
            pltpu.SemaphoreType.DMA((5, 4)),
            pltpu.SemaphoreType.DMA((5, 4)),
        ],
        compiler_params=pltpu.CompilerParams(
            collective_id=0, has_side_effects=True, vmem_limit_bytes=32 * 2**20
        ),
    )(local)


def gather_params(params):
    count = params.shape[0]
    blocks = gather_blocks(params)
    pieces = []
    reach = 0
    for rank in range(4):
        start = rank * count // LANES
        stop = -(-(rank + 1) * count // LANES)
        head = blocks[rank, :1] if rank == 0 else blocks[rank, :1] + pieces.pop()
        pieces += [head, blocks[rank, 1 : stop - start - 1], blocks[rank, stop - start - 1 : stop - start]]
    return jnp.concatenate(pieces)


def reduce_kernel(count, space, pieces, grads_ref, out_ref, rc, tx, rx, acc, ty, ry, tz, rz, gath, send, recv, zsend, zrecv):
    rank, spot = lax.axis_index(DP), lax.axis_index(SPACE)
    mate, across, twin = mate_of(rank), lax.rem(rank + 2, 4), mate_of(spot)
    group = space // 2
    side, depth = lax.rem(spot, 2), lax.div(spot, 2)
    rows = BLOCK // pieces
    half = rows // 2
    part = half // group

    def partner(step):
        return lax.rem(depth + step, group)

    peers = [{DP: mate}, {DP: across}, {SPACE: twin}]
    barrier = pltpu.get_barrier_semaphore()
    for device in peers:
        pl.semaphore_signal(barrier, inc=1, device_id=device, device_id_type=MESH)

    def hello(step, carry):
        pl.semaphore_signal(barrier, inc=1, device_id={SPACE: partner(step) * 2 + side}, device_id_type=MESH)
        return carry

    lax.fori_loop(1, group, hello, 0)
    pl.semaphore_wait(barrier, 3 + group - 1)

    gath[BLOCK:, :] = jnp.zeros((32, LANES), jnp.bfloat16)
    lower = lax.rem(rank, 2)
    upper = lax.div(rank, 2)

    def base(who):
        return pl.multiple_of(quarter_base(who, count), 16)

    def rows_of(start, index, length):
        return pl.ds(pl.multiple_of(start + index, 16), length)

    core = []
    for p in range(pieces):
        for high in range(2):
            copy = remote(
                grads_ref.at[rows_of(base(2 * high + 1 - lower), p * rows, rows)],
                rc.at[p, high],
                send.at[high, p],
                recv.at[high, p],
                peers[0],
            )
            copy.start()
            core.append(copy)
    step_rows = 192 if half % 192 == 0 else 16
    xs, ys, gs = [], [], []

    def z_copy(p, step):
        to = partner(step)
        return remote(
            tz.at[p, pl.ds(pl.multiple_of(to * part, 16), part)],
            rz.at[p, pl.ds(pl.multiple_of(depth * part, 16), part)],
            zsend.at[0, p, step],
            zrecv.at[0, p, step],
            {SPACE: to * 2 + side},
        )

    def home(p, which, slot):
        return pl.ds(pl.multiple_of(p * rows + which * half + slot * part, 16), part)

    def g_copy(p, step):
        block = gath.at[home(p, side, depth)]
        return remote(block, block, zsend.at[1, p, step], zrecv.at[1, p, step], {SPACE: partner(step) * 2 + side})

    def each(body):
        def run(step, carry):
            body(step)
            return carry

        lax.fori_loop(1, group, run, 0)

    def stage_core(p):
        core[2 * p].wait_recv()
        core[2 * p + 1].wait_recv()
        far = 1 - upper

        def add(step, carry):
            at = pl.multiple_of(step * step_rows, 16)
            mine = grads_ref[rows_of(base(2 * far + lower), p * rows + at, step_rows), :].astype(jnp.float32)
            tx[p, pl.ds(at, step_rows), :] = (
                mine + rc[p, far, pl.ds(at, step_rows), :].astype(jnp.float32)
            ).astype(jnp.bfloat16)
            return carry

        lax.fori_loop(0, rows // step_rows, add, 0)
        copy = remote(tx.at[p], rx.at[p], send.at[2, p], recv.at[2, p], peers[1])
        copy.start()
        xs.append(copy)

    def stage_x(p):
        xs[p].wait_recv()

        def total(at):
            return (
                grads_ref[rows_of(base(rank), p * rows + at, step_rows), :].astype(jnp.float32)
                + rc[p, upper, pl.ds(at, step_rows), :].astype(jnp.float32)
                + rx[p, pl.ds(at, step_rows), :].astype(jnp.float32)
            )

        def add(step, carry):
            at = pl.multiple_of(step * step_rows, 16)
            far = pl.multiple_of((1 - side) * half + at, 16)
            near = pl.multiple_of(side * half + at, 16)
            ty[p, pl.ds(at, step_rows), :] = total(far).astype(jnp.bfloat16)
            acc[p, pl.ds(at, step_rows), :] = total(near)
            return carry

        lax.fori_loop(0, half // step_rows, add, 0)
        copy = remote(ty.at[p], ry.at[p], send.at[3, p], recv.at[3, p], peers[2])
        copy.start()
        ys.append(copy)

    def stage_y(p):
        ys[p].wait_recv()

        def add(step, carry):
            at = pl.ds(pl.multiple_of(step * step_rows, 16), step_rows)
            value = acc[p, at, :] + ry[p, at, :].astype(jnp.float32)
            acc[p, at, :] = value
            tz[p, at, :] = value.astype(jnp.bfloat16)
            return carry

        lax.fori_loop(0, half // step_rows, add, 0)
        each(lambda step: z_copy(p, step).start())

    def stage_z(p):
        each(lambda step: z_copy(p, step).wait_recv())
        value = acc[p, pl.ds(pl.multiple_of(depth * part, 16), part), :]

        def add(step, value):
            other = lax.rem(depth + group - step, group)
            return value + rz[p, pl.ds(pl.multiple_of(other * part, 16), part), :].astype(jnp.float32)

        value = lax.fori_loop(1, group, add, value)
        gath[home(p, side, depth), :] = value.astype(jnp.bfloat16)
        each(lambda step: g_copy(p, step).start())

    def stage_zg(p):
        each(lambda step: g_copy(p, step).wait_recv())
        block = gath.at[pl.ds(pl.multiple_of(p * rows + side * half, 16), half)]
        copy = remote(block, block, send.at[4, p], recv.at[4, p], peers[2])
        copy.start()
        gs.append(copy)

    def stage_yg(p):
        gs[p].wait_recv()

    stages = [stage_core, stage_x, stage_y, stage_z, stage_zg, stage_yg]
    for tick in range(pieces + len(stages) - 1):
        for number in reversed(range(len(stages))):
            if 0 <= tick - number < pieces:
                stages[number](tick - number)

    for copy in core + xs + ys + gs:
        copy.wait_send()
    for p in range(pieces):

        def done(step):
            z_copy(p, step).wait_send()
            g_copy(p, step).wait_send()

        each(done)

    offset = rank * count - quarter_base(rank, count) * LANES
    skip = lax.div(offset, LANES)
    matrix = lane_matrix(lax.rem(offset, LANES), False)
    wide = jnp.where(
        lax.broadcasted_iota(jnp.int32, (256, 288), 1)
        == lax.broadcasted_iota(jnp.int32, (256, 288), 0) + skip,
        1.0,
        0.0,
    ).astype(jnp.bfloat16)
    wide_next = jnp.where(
        lax.broadcasted_iota(jnp.int32, (256, 288), 1)
        == lax.broadcasted_iota(jnp.int32, (256, 288), 0) + skip + 1,
        1.0,
        0.0,
    ).astype(jnp.bfloat16)

    def place(step, carry):
        at = pl.multiple_of(step * 256, 256)
        block = gath[pl.ds(at, 288), :]
        both = jnp.dot(block, matrix, preferred_element_type=jnp.float32).astype(jnp.bfloat16)
        out_ref[pl.ds(at, 256), :] = jnp.dot(wide, both[:, :LANES], preferred_element_type=jnp.float32) + jnp.dot(
            wide_next, both[:, LANES:], preferred_element_type=jnp.float32
        )
        return carry

    lax.fori_loop(0, BLOCK // 256, place, 0)


def reduce_grads(flat, space, count):
    pieces = next(k for k in (4, 2, 1) if BLOCK // (k * space) % 16 == 0)
    rows = BLOCK // pieces
    half = rows // 2
    out = pl.pallas_call(
        functools.partial(reduce_kernel, count, space, pieces),
        out_shape=jax.ShapeDtypeStruct((BLOCK, LANES), jnp.float32),
        in_specs=[pl.BlockSpec(memory_space=pltpu.VMEM)],
        out_specs=pl.BlockSpec(memory_space=pltpu.VMEM),
        scratch_shapes=[
            pltpu.VMEM((pieces, 2, rows, LANES), jnp.bfloat16),
            pltpu.VMEM((pieces, rows, LANES), jnp.bfloat16),
            pltpu.VMEM((pieces, rows, LANES), jnp.bfloat16),
            pltpu.VMEM((pieces, half, LANES), jnp.float32),
            pltpu.VMEM((pieces, half, LANES), jnp.bfloat16),
            pltpu.VMEM((pieces, half, LANES), jnp.bfloat16),
            pltpu.VMEM((pieces, half, LANES), jnp.bfloat16),
            pltpu.VMEM((pieces, half, LANES), jnp.bfloat16),
            pltpu.VMEM((BLOCK + 32, LANES), jnp.bfloat16),
            pltpu.SemaphoreType.DMA((5, pieces)),
            pltpu.SemaphoreType.DMA((5, pieces)),
            pltpu.SemaphoreType.DMA((2, pieces, space // 2)),
            pltpu.SemaphoreType.DMA((2, pieces, space // 2)),
        ],
        compiler_params=pltpu.CompilerParams(
            collective_id=1, has_side_effects=True, vmem_limit_bytes=48 * 2**20
        ),
    )(flat)
    return out.reshape(-1)[:count]


def gru_forward(state, inputs, weights, biases, gate_name, candidate_name, tall, wide, padder):
    joined_stack = patches(padder(jnp.concatenate([state, inputs], -1), tall, wide), tall, wide)
    gates = jax.nn.sigmoid(apply(joined_stack, weights[gate_name]) + biases[gate_name])
    hidden = state.shape[-1]
    update = gates[..., :hidden]
    reset = gates[..., hidden:]
    state_wide = state.astype(jnp.float32)
    mixed = jnp.concatenate([(reset * state_wide).astype(jnp.bfloat16), inputs], -1)
    mixed_stack = patches(padder(mixed, tall, wide), tall, wide)
    candidate = jnp.tanh(apply(mixed_stack, weights[candidate_name]) + biases[candidate_name])
    result = state_wide + update * (candidate - state_wide)
    return (result, (joined_stack, mixed_stack, update, reset, candidate, state_wide))


def gru_backward(result_grad, kept, weights, grads, gate_name, candidate_name, tall, wide, padder):
    joined_stack, mixed_stack, update, reset, candidate, state_wide = kept
    hidden = update.shape[-1]
    candidate_grad = (result_grad * update * (1.0 - candidate * candidate)).astype(jnp.bfloat16)
    record(grads, candidate_name, mixed_stack, candidate_grad)
    mixed_grad = apply(
        patches(padder(candidate_grad, tall, wide), tall, wide),
        flipped(weights[candidate_name], tall, wide),
    )
    reset_grad = mixed_grad[..., :hidden]
    gate_grad = jnp.concatenate(
        [
            result_grad * (candidate - state_wide) * update * (1.0 - update),
            reset_grad * state_wide * reset * (1.0 - reset),
        ],
        -1,
    ).astype(jnp.bfloat16)
    record(grads, gate_name, joined_stack, gate_grad)
    joined_grad = apply(
        patches(padder(gate_grad, tall, wide), tall, wide), flipped(weights[gate_name], tall, wide)
    )
    state_grad = result_grad * (1.0 - update) + reset_grad * reset + joined_grad[..., :hidden]
    inputs_grad = joined_grad[..., hidden:] + mixed_grad[..., hidden:]
    return (state_grad, inputs_grad)


def shards(net, context, corr, flow, target, valid, grad_net, grad_mask, params):
    flow_start = CTX + MOT - 2
    plane = jnp.float32(target.shape[2] * net.shape[2])
    counts = lax.psum(jnp.sum(valid, axis=(1, 2)).astype(jnp.float32), SPACE)
    divisor = jnp.maximum(counts, 1.0)
    weights, biases = unpack(gather_params(params))
    grads = {}
    flow_rows = jnp.transpose(flow, (0, 2, 3, 1))
    corr_pre = apply(corr, weights[CORR_IN]) + biases[CORR_IN]
    corr_one = jax.nn.silu(corr_pre).astype(jnp.bfloat16)
    corr_stack = patches(row_pad(corr_one, 3), 3, 3)
    corr_mix_pre = apply(corr_stack, weights[CORR_MIX]) + biases[CORR_MIX]
    corr_two = jax.nn.silu(corr_mix_pre).astype(jnp.bfloat16)
    flow_stack = patches(row_pad(flow_rows, 7), 7, 7)
    flow_pre = apply(flow_stack, weights[FLOW_IN]) + biases[FLOW_IN]
    flow_one = jax.nn.silu(flow_pre).astype(jnp.bfloat16)
    flow_mix_stack = patches(row_pad(flow_one, 3), 3, 3)
    flow_mix_pre = apply(flow_mix_stack, weights[FLOW_MIX]) + biases[FLOW_MIX]
    flow_two = jax.nn.silu(flow_mix_pre).astype(jnp.bfloat16)
    joint_stack = patches(row_pad(jnp.concatenate([corr_two, flow_two], -1), 3), 3, 3)
    motion_pre = apply(joint_stack, weights[MOTION_MIX]) + biases[MOTION_MIX]
    motion = jax.nn.silu(motion_pre).astype(jnp.bfloat16)
    inputs = jnp.concatenate([context, motion, flow_rows], -1)
    state, rows_kept = gru_forward(
        net, inputs, weights, biases, ROWS_GATES, ROWS_CANDIDATE, 1, 5, local_pad
    )
    state_columns, inputs_columns = (
        lax.all_to_all(
            state.astype(jnp.bfloat16), SPACE, split_axis=2, concat_axis=1, tiled=True
        ),
        lax.all_to_all(inputs, SPACE, split_axis=2, concat_axis=1, tiled=True),
    )
    target_here = jnp.transpose(target, (0, 2, 3, 1))
    valid_here = valid.astype(jnp.float32)
    net_cotangent = grad_net
    mask_cotangent = grad_mask
    final, columns_kept = gru_forward(
        state_columns,
        inputs_columns,
        weights,
        biases,
        COLUMNS_GATES,
        COLUMNS_CANDIDATE,
        5,
        1,
        local_pad,
    )
    final_low = final.astype(jnp.bfloat16)
    heads_weight = jnp.concatenate([weights[FLOW_HIDDEN], weights[MASK_HIDDEN]], 1)
    heads_bias = jnp.concatenate([biases[FLOW_HIDDEN], biases[MASK_HIDDEN]])
    net_stack = patches(column_pad(final_low, 3, 3), 3, 3)
    heads_pre = apply(net_stack, heads_weight) + heads_bias
    heads_act = jax.nn.silu(heads_pre).astype(jnp.bfloat16)
    flow_features = heads_act[..., :HEAD]
    mask_features = heads_act[..., HEAD:]
    hidden_stack = patches(column_pad(flow_features, 3, 3), 3, 3)
    delta = apply(hidden_stack, weights[FLOW_OUT]) + biases[FLOW_OUT]
    mask_full = 0.25 * (apply(mask_features, weights[MASK_OUT]) + biases[MASK_OUT])
    new_flow = inputs_columns[..., flow_start:].astype(jnp.float32) + delta
    error = new_flow - target_here
    root = jnp.sqrt(error * error + 1.0)
    partials = jnp.sum(valid_here * jnp.sum(root, axis=-1), axis=(1, 2))
    flow_grad = plane / divisor[:, None, None, None] * valid_here[..., None] * error / root
    mask_low = mask_full.astype(jnp.bfloat16)
    nets_out = final_low
    flows_out = jnp.transpose(new_flow, (0, 3, 1, 2))
    masks_out = mask_low
    delta_grad = flow_grad.astype(jnp.bfloat16)
    mask_grad = (0.25 * mask_cotangent.astype(jnp.float32)).astype(jnp.bfloat16)
    record(grads, MASK_OUT, mask_features, mask_grad)
    record(grads, FLOW_OUT, hidden_stack, delta_grad)
    from_flow = apply(
        patches(column_pad(delta_grad, 3, 3), 3, 3), flipped(weights[FLOW_OUT], 3, 3)
    )
    from_mask = apply_back(mask_grad, weights[MASK_OUT])
    heads_grad = (jnp.concatenate([from_flow, from_mask], -1) * slope(heads_pre)).astype(
        jnp.bfloat16
    )
    heads_wgrad = weight_grad(net_stack, heads_grad)
    heads_bgrad = jnp.sum(heads_grad, axis=(0, 1, 2), dtype=jnp.float32)
    grads[FLOW_HIDDEN] = (heads_wgrad[:, :HEAD], heads_bgrad[:HEAD])
    grads[MASK_HIDDEN] = (heads_wgrad[:, HEAD:], heads_bgrad[HEAD:])
    final_grad = net_cotangent.astype(jnp.float32) + apply(
        patches(column_pad(heads_grad, 3, 3), 3, 3), flipped(heads_weight, 3, 3)
    )
    state_grad_columns, inputs_grad_columns = gru_backward(
        final_grad,
        columns_kept,
        weights,
        grads,
        COLUMNS_GATES,
        COLUMNS_CANDIDATE,
        5,
        1,
        local_pad,
    )
    inputs_grad_columns = jnp.concatenate(
        [
            inputs_grad_columns[..., :flow_start],
            inputs_grad_columns[..., flow_start:] + flow_grad,
        ],
        -1,
    )
    state_back, inputs_back = (
        lax.all_to_all(
            state_grad_columns.astype(jnp.bfloat16),
            SPACE,
            split_axis=1,
            concat_axis=2,
            tiled=True,
        ),
        lax.all_to_all(
            inputs_grad_columns.astype(jnp.bfloat16),
            SPACE,
            split_axis=1,
            concat_axis=2,
            tiled=True,
        ),
    )
    net_grad, inputs_grad = gru_backward(
        state_back.astype(jnp.float32),
        rows_kept,
        weights,
        grads,
        ROWS_GATES,
        ROWS_CANDIDATE,
        1,
        5,
        local_pad,
    )
    inputs_total = inputs_grad + inputs_back.astype(jnp.float32)
    motion_grad = (inputs_total[..., CTX:flow_start] * slope(motion_pre)).astype(jnp.bfloat16)
    record(grads, MOTION_MIX, joint_stack, motion_grad)
    joint_grad = apply(
        patches(row_pad(motion_grad, 3), 3, 3), flipped(weights[MOTION_MIX], 3, 3)
    )
    branch_grad = jnp.concatenate(
        [
            joint_grad[..., :C2] * slope(corr_mix_pre),
            joint_grad[..., C2:] * slope(flow_mix_pre),
        ],
        -1,
    ).astype(jnp.bfloat16)
    record(grads, CORR_MIX, corr_stack, branch_grad[..., :C2])
    record(grads, FLOW_MIX, flow_mix_stack, branch_grad[..., C2:])
    branch_pad = row_pad(branch_grad, 3)
    corr_one_grad = apply(
        patches(branch_pad[..., :C2], 3, 3), flipped(weights[CORR_MIX], 3, 3)
    )
    flow_one_grad = apply(
        patches(branch_pad[..., C2:], 3, 3), flipped(weights[FLOW_MIX], 3, 3)
    )
    corr_pre_grad = (corr_one_grad * slope(corr_pre)).astype(jnp.bfloat16)
    flow_pre_grad = (flow_one_grad * slope(flow_pre)).astype(jnp.bfloat16)
    record(grads, CORR_IN, corr, corr_pre_grad)
    record(grads, FLOW_IN, flow_stack, flow_pre_grad)
    corr_grads = apply_back(corr_pre_grad, weights[CORR_IN])
    flow_total = inputs_total[..., flow_start:] + apply(
        patches(row_pad(flow_pre_grad, 7), 7, 7), flipped(weights[FLOW_IN], 7, 7)
    )
    flow_grads = jnp.transpose(flow_total, (0, 3, 1, 2))
    net_grads = net_grad
    context_grads = inputs_total[..., :CTX]
    count = params.shape[0]
    local = pack(grads, 3 * count // (LANES * 16) * 16 + BLOCK)
    collected = reduce_grads(local, lax.axis_size(SPACE), count)
    losses = lax.psum(partials, SPACE) / divisor
    return (
        nets_out,
        flows_out,
        masks_out,
        losses,
        collected,
        net_grads,
        context_grads,
        corr_grads,
        flow_grads,
    )


BATCH = 2
ROWS = 5
WIDE = 128
TALL = 40
COLS = 16
AREA = 640
PITCH = 20
SPREAD = TALL * PITCH
SPAN = 896
EDGE = 64


def mm(a, b):
    return jnp.dot(a, b, preferred_element_type=jnp.float32)


def nt(a, b):
    return lax.dot_general(a, b, (((1,), (1,)), ((), ())), preferred_element_type=jnp.float32)


def tn(a, b):
    return lax.dot_general(a, b, (((0,), (0,)), ((), ())), preferred_element_type=jnp.float32)


def half_of(value):
    return value.astype(jnp.bfloat16)


def full_of(value):
    return value.astype(jnp.float32)


def quarter_of(value):
    return half_of(0.25 * full_of(value))


def lane_index(shape):
    return lax.broadcasted_iota(jnp.int32, shape, 1)


def row_index(shape):
    return lax.broadcasted_iota(jnp.int32, shape, 0)


def act_slope(pre):
    sigma = jax.nn.sigmoid(pre)
    act = pre * sigma
    return act, sigma + act * (1.0 - sigma)


def flat_rows():
    table = shapes()
    offset = 0
    starts = {}
    for name, height, width in table:
        starts[name] = offset // LANES
        offset += height * width
    bias_row = offset // LANES
    spots = {}
    inner = 0
    for name, height, width in table:
        spots[name] = inner
        inner += width
    return starts, bias_row, spots, inner


def cast_rows(dst, to, src, start, count, kind):
    big = 256
    whole = count // big

    if whole > 1:

        def body(step, carry):
            at = pl.multiple_of(step * big, big)
            dst[pl.ds(to + at, big), :] = src[pl.ds(start + at, big), :].astype(kind)
            return carry

        lax.fori_loop(0, whole, body, 0)
    elif whole == 1:
        dst[to : to + big, :] = src[start : start + big, :].astype(kind)
    rest = count - whole * big
    if rest:
        low = whole * big
        dst[to + low : to + count, :] = src[start + low : start + count, :].astype(kind)


MARGIN = 16


def stage_plan(count, start, rows):
    stop = start + rows
    pieces, fill = [], 0
    for rank in range(4):
        first = rank * count // LANES
        last = -(-(rank + 1) * count // LANES)
        low, high = max(start, first), min(stop, last)
        if low >= high:
            continue
        place = low - first + rank * BLOCK
        base = place // 16 * 16
        length = -(-(place - base + high - low) // 16) * 16
        to = MARGIN + low - start - (place - base)
        seam = MARGIN + low - start if start < first else None
        pieces.append((base, length, fill, to, seam))
        fill += length
    return pieces


class Stages:
    def __init__(self, v, count, segments):
        self.v, self.at = v, 0
        self.plans = [stage_plan(count, start, rows) for start, rows in segments]
        self.fetch(0)

    def copies(self, index):
        v, slot = self.v, index % 2
        return [
            pltpu.make_async_copy(
                v.gathered.at[base : base + length], v.stage.at[slot, fill : fill + length], v.ssem.at[slot, number]
            )
            for number, (base, length, fill, to, seam) in enumerate(self.plans[index])
        ]

    def fetch(self, index):
        if index < len(self.plans):
            for copy in self.copies(index):
                copy.start()

    def take(self):
        v, index = self.v, self.at
        self.at += 1
        for copy in self.copies(index):
            copy.wait()
        self.fetch(index + 1)
        for base, length, fill, to, seam in self.plans[index]:
            saved = None if seam is None else v.flat[seam : seam + 1, :]
            cast_rows(v.flat, to, v.stage.at[index % 2], fill, length, jnp.float32)
            if seam is not None:
                v.flat[seam : seam + 1, :] = v.flat[seam : seam + 1, :] + saved


def strided(ref, start, count, stride):
    if stride == 1:
        return ref[pl.ds(start, count), :]
    return ref[pl.ds(start, count, stride=stride), :]


def unpack_pairs(flat, row, count, dst, to, lane):
    dst[to : to + count, lane : lane + LANES] = half_of(strided(flat, MARGIN + 2 * row, count, 2))
    dst[to : to + count, lane + LANES : lane + 2 * LANES] = half_of(strided(flat, MARGIN + 2 * row + 1, count, 2))


def pack_pairs(flat, row, count, low, high):
    flat[pl.ds(MARGIN + 2 * row, count, stride=2), :] = low
    flat[pl.ds(MARGIN + 2 * row + 1, count, stride=2), :] = high


def split_pick(which, quarter):
    source = lax.broadcasted_iota(jnp.int32, (LANES, HEAD), 0)
    target = lax.broadcasted_iota(jnp.int32, (LANES, HEAD), 1)
    return jnp.where(source == 2 * (target - 64 * quarter) + which, 1.0, 0.0).astype(jnp.bfloat16)


def unpack_all(v, count):
    starts, bias_row, spots, inner = flat_rows()
    flat = v.flat
    order = (
        (CORR_IN, 648), (CORR_MIX, 3456), (FLOW_IN, 98), (FLOW_MIX, 576), (MOTION_MIX, 2268),
        (ROWS_GATES, 3840), (ROWS_CANDIDATE, 1920), (COLUMNS_GATES, 3840), (COLUMNS_CANDIDATE, 1920),
        (FLOW_HIDDEN, 2304), (MASK_HIDDEN, 2304), (FLOW_OUT, 36), (MASK_OUT, 1152),
    )
    stages = Stages(v, count, [(starts[name], rows) for name, rows in order] + [(bias_row, 21)])

    def stage(name, rows):
        assert order[stages.at] == (name, rows)
        stages.take()

    stage(CORR_IN, 648)
    unpack_pairs(flat, 0, 324, v.w_ci, 0, 0)

    stage(CORR_MIX, 3456)
    lane = lane_index((128, LANES))
    low_half = lane < 64

    def mix_step(step, carry):
        at = MARGIN + 384 * step
        r0, r1, r2 = (strided(flat, at + i, 128, 3) for i in range(3))
        r1s, r2s = pltpu.roll(r1, 64, 1), pltpu.roll(r2, 64, 1)
        v.pair_a[pl.ds(0, 128, stride=2), :] = r0
        v.pair_a[pl.ds(1, 128, stride=2), :] = jnp.where(low_half, r1s, r2s)
        v.pair_b[pl.ds(0, 128, stride=2), :] = jnp.where(low_half, r1, 0.0)
        v.pair_b[pl.ds(1, 128, stride=2), :] = jnp.where(low_half, r2s, 0.0)
        to = pl.ds(pl.multiple_of(step * 256, 256), 256)
        v.w_cm[to, 0:128] = half_of(v.pair_a[...])
        v.w_cm[to, 128:256] = half_of(v.pair_b[...])
        return carry

    lax.fori_loop(0, 9, mix_step, 0)

    stage(FLOW_IN, 98)
    v.flow_tmp[...] = jnp.zeros_like(v.flow_tmp)
    for across in range(7):
        for comp in range(2):
            v.flow_tmp[pl.ds(across * 16 + comp, 7, stride=2), :] = strided(
                flat, MARGIN + across * 2 + comp, 7, 14
            )
    v.w_fi[...] = half_of(v.flow_tmp[...])

    stage(FLOW_MIX, 576)
    for step in range(9):
        r0 = strided(flat, MARGIN + 64 * step, 64, 1)
        high_half = lane_index((64, LANES)) >= 64
        v.pair_a[pl.ds(0, 64, stride=2), :] = jnp.where(high_half, pltpu.roll(r0, 64, 1), 0.0)
        v.pair_a[pl.ds(1, 64, stride=2), :] = jnp.where(high_half, r0, 0.0)
        v.w_fm[step * 128 : (step + 1) * 128, :] = half_of(v.pair_a[0:128, :])

    stage(MOTION_MIX, 2268)
    lane36 = lane_index((36, LANES))
    for i in range(64):
        if i == 0:
            value = strided(flat, MARGIN, 36, 63)
        elif i == 63:
            value = pltpu.roll(strided(flat, MARGIN + 62, 36, 63), 126, 1)
        else:
            low = pltpu.roll(strided(flat, MARGIN + i - 1, 36, 63), 2 * i, 1)
            high = pltpu.roll(strided(flat, MARGIN + i, 36, 63), 2 * i, 1)
            value = jnp.where(lane36 < 2 * i, low, high)
        v.mm_tmp[pl.ds(i, 36, stride=64), :] = jnp.where(lane36 < 126, value, 0.0)
    for step in range(9):
        v.w_mm[step * 256 : (step + 1) * 256, :] = half_of(v.mm_tmp[step * 256 : (step + 1) * 256, :])

    for gates_name, cand_name, w_i, w_s in ((ROWS_GATES, ROWS_CANDIDATE, v.w_ri, v.w_rs), (COLUMNS_GATES, COLUMNS_CANDIDATE, v.w_li, v.w_ls)):
        stage(gates_name, 3840)
        for tap in range(5):
            unpack_pairs(flat, tap * 384, 128, w_s, tap * 128, 0)
            unpack_pairs(flat, tap * 384 + 128, 256, w_i, tap * 256, 0)
        stage(cand_name, 1920)
        for tap in range(5):
            w_s[tap * 128 : (tap + 1) * 128, 256:384] = half_of(strided(flat, MARGIN + tap * 384, 128, 1))
            w_i[tap * 256 : (tap + 1) * 256, 256:384] = half_of(strided(flat, MARGIN + tap * 384 + 128, 256, 1))

    for name, lane0 in ((FLOW_HIDDEN, 0), (MASK_HIDDEN, 256)):
        stage(name, 2304)
        for tap in range(9):
            unpack_pairs(flat, tap * 128, 128, v.w_h, tap * 128, lane0)

    stage(FLOW_OUT, 36)
    v.fo_tmp[...] = jnp.zeros_like(v.fo_tmp)
    for which in range(2):
        total = jnp.zeros((9, HEAD), jnp.float32)
        for quarter in range(4):
            total = total + mm(half_of(strided(flat, MARGIN + quarter, 9, 4)), split_pick(which, quarter))
        v.fo_tmp[pl.ds(which, 9, stride=2), 0:128] = total[:, :128]
        v.fo_tmp2[pl.ds(which, 9, stride=2), 0:128] = total[:, 128:]
    v.fo_tmp2[18:32, :] = jnp.zeros((14, LANES), jnp.float32)
    v.w_fo[:, 0:128] = half_of(v.fo_tmp[...])
    v.w_fo[:, 128:256] = half_of(v.fo_tmp2[...])

    stage(MASK_OUT, 1152)
    r = [strided(flat, MARGIN + i, 128, 9) for i in range(9)]
    rs = [pltpu.roll(r[i], 64, 1) for i in range(4, 9)]
    for block in range(5):
        even = r[block] if block < 4 else jnp.where(low_half, r[4], 0.0)
        odd = jnp.where(low_half, rs[block], rs[block + 1]) if block < 4 else jnp.where(low_half, rs[4], 0.0)
        v.pair_a[pl.ds(0, 128, stride=2), :] = even
        v.pair_a[pl.ds(1, 128, stride=2), :] = odd
        v.w_mo[:, block * 128 : (block + 1) * 128] = half_of(v.pair_a[...])

    stages.take()
    place = 0
    lane1 = lane_index((1, LANES))
    for name, height, width in shapes():
        spot = spots[name]
        for block in range(-(-width // LANES)):
            at = spot + block * LANES
            row, shift = at // LANES, at % LANES
            value = flat[MARGIN + row : MARGIN + row + 1, :]
            if shift:
                after = flat[MARGIN + row + 1 : MARGIN + row + 2, :]
                value = jnp.where(
                    lane1 < LANES - shift, pltpu.roll(value, LANES - shift, 1), pltpu.roll(after, LANES - shift, 1)
                )
            left = width - block * LANES
            if left < LANES:
                value = jnp.where(lane1 < left, value, 0.0)
            if name == FLOW_MIX:
                value = pltpu.roll(value, 64, 1)
            v.bias[place : place + 1, :] = value
            place += 1


BIAS_AT = {}
_place = 0
for _name, _height, _width in shapes():
    BIAS_AT[_name] = _place
    _place += -(-_width // 128)
BIAS_ROWS = 32


def bias_of(v, name, blocks):
    at = BIAS_AT[name]
    return jnp.concatenate([v.bias[at + i : at + i + 1, :] for i in range(blocks)], axis=1)


class Halo:
    def __init__(self, v, sem, up_src, down_src, from_down, from_up):
        up = {SPACE: jnp.maximum(v.spot - 1, 0)}
        down = {SPACE: jnp.minimum(v.spot + 1, v.space - 1)}
        self.v = v
        self.up = remote(up_src, from_down, v.hsend.at[sem, 0], v.hrecv.at[sem, 0], up)
        self.down = remote(down_src, from_up, v.hsend.at[sem, 1], v.hrecv.at[sem, 1], down)

    def start(self):
        pl.when(self.v.spot > 0)(self.up.start)
        pl.when(self.v.spot < self.v.space - 1)(self.down.start)

    def receive(self):
        pl.when(self.v.spot < self.v.space - 1)(self.up.wait_recv)
        pl.when(self.v.spot > 0)(self.down.wait_recv)

    def sent(self):
        pl.when(self.v.spot > 0)(self.up.wait_send)
        pl.when(self.v.spot < self.v.space - 1)(self.down.wait_send)


class Swap:
    def __init__(self, v, sem, src, dst, broadcast=False):
        self.v, self.sem, self.src, self.dst, self.broadcast = v, sem, src, dst, broadcast

    def copy(self, step):
        v = self.v
        to = lax.rem(v.spot + step, v.space)
        src = self.src if self.broadcast else self.src.at[to]
        return remote(src, self.dst.at[v.spot], v.asend.at[self.sem, step], v.arecv.at[self.sem, step], {SPACE: to})

    def each(self, what):
        def body(step, carry):
            what(self.copy(step))
            return carry

        lax.fori_loop(1, self.v.space, body, 0)

    def start(self):
        self.each(lambda copy: copy.start())

    def receive(self):
        self.each(lambda copy: copy.wait_recv())

    def sent(self):
        self.each(lambda copy: copy.wait_send())


def spread_rows(v, b, acts, rows, dst, row0, width, backward=False):
    x = lax.rem(row_index((rows, LANES)), WIDE)
    for block, act in enumerate(acts):
        v.tmp[8 : 8 + rows, :] = act
        for tap in range(3):
            d = (1 - tap) if backward else (tap - 1)
            value = act if d == 0 else v.tmp[8 + d : 8 + d + rows, :]
            if d == -1:
                value = jnp.where(x > 0, value, 0.0)
            if d == 1:
                value = jnp.where(x < WIDE - 1, value, 0.0)
            lane = tap * width + block * LANES
            if backward:
                dst[row0 : row0 + rows, b + lane : b + lane + LANES] = half_of(value)
            else:
                dst[b, row0 : row0 + rows, lane : lane + LANES] = half_of(value)


def spread_five(v, value, dst, lane_of, backward=False):
    x = lax.rem(row_index((AREA, LANES)), WIDE)
    v.tmp[8 : 8 + AREA, :] = value
    for tap in range(5):
        d = (2 - tap) if backward else (tap - 2)
        moved = value if d == 0 else v.tmp[8 + d : 8 + d + AREA, :]
        if d:
            moved = jnp.where((x + d >= 0) & (x + d < WIDE), moved, 0.0)
        if backward:
            taps_part(v, tap, lane_of, lane_of + LANES)[...] = half_of(moved)
        else:
            lane = lane_of(tap)
            dst[:, lane : lane + LANES] = half_of(moved)


def lines_of(ref, b, lines):
    return jnp.concatenate([ref[b, y] for y in range(lines)], axis=1)


def edge_rows(v, value, rows):
    low = jnp.where(v.spot > 0, value[0:rows], 0.0)
    high = jnp.where(v.spot < v.space - 1, value[-rows:], 0.0)
    return jnp.concatenate([low, value[rows:-rows], high], axis=0)


def forward_rows(v):
    spot, last = v.spot, v.space - 1
    def image(b, carry):
        pieces = (
            (v.corr_up, 0, 256, 2, spot > 0),
            (v.corr, 256, 640, 5, None),
            (v.corr_down, 896, 256, 2, spot < last),
        )
        bias = bias_of(v, CORR_IN, 2)
        for ref, row0, rows, lines, seen in pieces:
            act, slope = act_slope(tn(lines_of(ref, b, lines), v.w_ci[...]) + bias)
            if seen is None:
                v.slope_ci[b] = half_of(slope)
            else:
                act = jnp.where(seen, act, 0.0)
            spread_rows(v, b, (act[:, :128], act[:, 128:]), rows, v.hx_c, row0, 256)

        up = jnp.where(spot > 0, v.flow_up[b], 0.0)
        down = jnp.where(spot < last, v.flow_down[b], 0.0)
        lane = lane_index((16, LANES))
        v.fs[...] = jnp.zeros_like(v.fs)
        for across in range(7):
            d = across - 3
            for part, value in enumerate((up, v.flow[b], down)):
                moved = value
                if d:
                    moved = pltpu.roll(value, (-d) % LANES, 1)
                    moved = jnp.where((lane + d >= 0) & (lane + d < WIDE), moved, 0.0)
                v.fs[across, part * 10 : part * 10 + 10, :] = moved[0:10, :]
        for y in range(9):
            for across in range(7):
                v.flow_tmp[across * 16 : across * 16 + 16, :] = v.fs[across, 2 * y : 2 * y + 16, :]
            v.xt[b, :, y * 128 : (y + 1) * 128] = half_of(v.flow_tmp[...])
        act, slope = act_slope(tn(v.xt[b], v.w_fi[...]) + bias_of(v, FLOW_IN, 1))
        v.slope_fi[b] = half_of(slope[256:896])
        spread_rows(v, b, (edge_rows(v, act, 2 * WIDE),), 9 * WIDE, v.hx_f, 0, 128)

        pre = bias_of(v, CORR_MIX, 2)
        flow_pre = bias_of(v, FLOW_MIX, 1)
        for a in range(3):
            pre = pre + mm(v.hx_c[b, a * 128 : a * 128 + 896, :], v.w_cm[a * 768 : (a + 1) * 768, :])
            flow_pre = flow_pre + mm(v.hx_f[b, a * 128 : a * 128 + 896, :], v.w_fm[a * 384 : (a + 1) * 384, :])
        low, low_slope = act_slope(pre[:, :128])
        high, high_slope = act_slope(pre[:, 128:] + flow_pre)
        v.slope_j[b, :, 0:128] = half_of(low_slope)
        v.slope_j[b, :, 128:256] = half_of(high_slope)
        spread_rows(v, b, (edge_rows(v, low, WIDE), edge_rows(v, high, WIDE)), 896, v.hx_j, 0, 256)

        pre = bias_of(v, MOTION_MIX, 1)
        for a in range(3):
            pre = pre + mm(v.hx_j[b, a * 128 : a * 128 + 640, :], v.w_mm[a * 768 : (a + 1) * 768, :])
        act, slope = act_slope(pre)
        v.slope_m[b] = half_of(jnp.where(lane_index((AREA, LANES)) < 126, slope, 0.0))
        pick = jnp.where(lane_index((16, LANES)) == row_index((16, LANES)) + 126, 1.0, 0.0)
        own_flow = v.flow[b]
        for y in range(ROWS):
            v.tmp2[0:2, :] = own_flow[2 * y : 2 * y + 2, :]
            v.tmp2[2:16, :] = jnp.zeros((14, LANES), jnp.float32)
            v.motion[b, y * 128 : (y + 1) * 128, :] = act[y * 128 : (y + 1) * 128, :] + tn(
                half_of(v.tmp2[0:16, :]), half_of(pick)
            )
        v.motion[b] = full_of(half_of(v.motion[b]))
        pack_rows(v, v.motion, b, v.a_motion)
        return carry

    lax.fori_loop(0, BATCH, image, 0)
    v.swap_motion.start()

    def gru(b, carry):
        at = pl.ds(pl.multiple_of(b * AREA, AREA), AREA)
        s = full_of(v.net[b])
        spread_five(v, full_of(v.context[b]), v.xi.at[at], lambda t: t * 256)
        spread_five(v, v.motion[b], v.xi.at[at], lambda t: t * 256 + 128)
        spread_five(v, s, v.xs.at[at], lambda t: t * 128)
        both = mm(v.xi[at, :], v.w_ri[...])
        gates = jax.nn.sigmoid(both[:, :256] + mm(v.xs[at, :], v.w_rs[:, :256]) + bias_of(v, ROWS_GATES, 2))
        update, reset = gates[:, :128], gates[:, 128:]
        v.ru[b] = update
        v.rr[b] = reset
        spread_five(v, full_of(half_of(reset * s)), v.xr.at[at], lambda t: t * 128)
        cand = jnp.tanh(both[:, 256:] + mm(v.xr[at, :], v.w_rs[:, 256:]) + bias_of(v, ROWS_CANDIDATE, 1))
        v.rc[b] = cand
        v.state[b] = s + update * (cand - s)
        pack_rows(v, v.state, b, v.a_state)
        return carry

    lax.fori_loop(0, BATCH, gru, 0)
    v.swap_state.start()


def pack_rows(v, src, b, dst):
    def peer(t, carry):
        for y in range(ROWS):
            at = pl.multiple_of(y * WIDE + t * COLS, COLS)
            dst[t, b, y * COLS : (y + 1) * COLS, :] = half_of(src[b, pl.ds(at, COLS), :])
        return carry

    lax.fori_loop(0, v.space, peer, 0)


def take_own(v, src, dst):
    dst[v.spot] = src[v.spot]


def columns_in(v):
    def zero(b, carry):
        for ref, wide in ((v.xc, 384), (v.xcr, 128), (v.gc, 384)):
            for low in (0, 32 + AREA):
                ref[b, low : low + 32, :] = jnp.zeros((32, wide), jnp.bfloat16)
        return carry

    lax.fori_loop(0, BATCH, zero, 0)

    def peer(t, carry):
        at = pl.ds(pl.multiple_of(32 + t * ROWS * COLS, 16), ROWS * COLS)
        for b in range(BATCH):
            v.xc[b, at, 0:128] = v.b_state[t, b]
            v.xc[b, at, 128:256] = v.b_context[t, b]
            v.xc[b, at, 256:384] = v.b_motion[t, b]
        return carry

    lax.fori_loop(0, v.space, peer, 0)


FX_ROWS = 16 + (TALL + 2) * PITCH


def fx_base(b):
    return pl.multiple_of(b * FX_ROWS, 8)


def columns_forward(v):
    def gru(b, carry):
        s = full_of(v.xc[b, 32 : 32 + AREA, 0:128])
        both = bias_of(v, COLUMNS_GATES, 2)
        both = jnp.concatenate([both, bias_of(v, COLUMNS_CANDIDATE, 1)], axis=1)
        gates = 0.0
        for t in range(5):
            rows = slice(t * COLS, t * COLS + AREA)
            both = both + mm(v.xc[b, rows, 128:384], v.w_li[t * 256 : (t + 1) * 256, :])
            gates = gates + mm(v.xc[b, rows, 0:128], v.w_ls[t * 128 : (t + 1) * 128, 0:256])
        gates = jax.nn.sigmoid(gates + both[:, :256])
        update, reset = gates[:, :128], gates[:, 128:]
        v.lu[b] = update
        v.lr[b] = reset
        v.xcr[b, 32 : 32 + AREA, :] = half_of(reset * s)
        cand = both[:, 256:]
        for t in range(5):
            rows = slice(t * COLS, t * COLS + AREA)
            cand = cand + mm(v.xcr[b, rows, :], v.w_ls[t * 128 : (t + 1) * 128, 256:384])
        cand = jnp.tanh(cand)
        v.lc[b] = cand
        final = s + update * (cand - s)
        v.out_net[b] = half_of(final)
        v.final[...] = full_of(half_of(final))
        fx = fx_base(b)
        v.mm_tmp[pl.ds(fx, FX_ROWS), :] = jnp.zeros((FX_ROWS, LANES), jnp.float32)
        for x in range(COLS):
            v.mm_tmp[pl.ds(fx + 8 + PITCH + 2 + x, TALL, stride=PITCH), :] = v.final[pl.ds(x, TALL, stride=COLS), :]
        for j in range(2):
            v.e_left[b, j, 0:TALL, :] = half_of(v.final[pl.ds(j, TALL, stride=COLS), :])
            v.e_right[b, j, 0:TALL, :] = half_of(v.final[pl.ds(COLS - 2 + j, TALL, stride=COLS), :])
        return carry

    lax.fori_loop(0, BATCH, gru, 0)
    v.halo_final.start()


def ring_masks(v, shape):
    x = lax.rem(row_index(shape), PITCH)
    place = v.spot * COLS + x - 2
    seen = (place >= 0) & (place < WIDE) & (x >= 1) & (x < PITCH - 1)
    own = (x >= 2) & (x < PITCH - 2)
    return seen, own


def mask_gradient(v):
    def image(b, carry):
        value = nt(quarter_of(v.grad_mask[b]), v.w_mo[:, 0:MASK])
        for block in range(2):
            v.final[...] = value[:, block * 128 : (block + 1) * 128]
            v.tmp[0:SPREAD, :] = jnp.zeros((SPREAD, LANES), jnp.float32)
            for x in range(COLS):
                v.tmp[pl.ds(2 + x, TALL, stride=PITCH), :] = v.final[pl.ds(x, TALL, stride=COLS), :]
            v.hgo[b, :, 256 + block * 128 : 384 + block * 128] = half_of(v.tmp[0:SPREAD, :])
            v.m_left[b, block, 0:TALL, :] = half_of(v.final[pl.ds(0, TALL, stride=COLS), :])
            v.m_right[b, block, 0:TALL, :] = half_of(v.final[pl.ds(COLS - 1, TALL, stride=COLS), :])
        return carry

    lax.fori_loop(0, BATCH, image, 0)
    v.halo_mask.start()


def heads_part(v, b, tap):
    ref = v.hx_c if tap < 6 else v.hx_f
    lane = tap % 6 * 128
    return ref.at[b, 0:SPREAD, lane : lane + 128]


def taps_part(v, t, low, high):
    ref = v.hx_f if t % 3 == 2 else v.hx_c
    lane = (t % 3) % 2 * 384
    return ref.at[t // 3, 0:AREA, lane + low : lane + high]


def heads(v):
    spot, last = v.spot, v.space - 1
    v.halo_final.receive()
    v.halo_mask.receive()
    v.swap_count.receive()
    v.counts[v.spot] = v.count_out[...]
    counts = jnp.sum(v.counts[...], axis=0)
    seen, own = ring_masks(v, (SPREAD, LANES))
    steps = [(a - 1) * PITCH + (c - 1) for a in range(3) for c in range(3)]
    plane = jnp.float32(TALL * WIDE)

    def image(b, carry):
        fx = fx_base(b)
        for j in range(2):
            left = jnp.where(spot > 0, full_of(v.f_left[b, j, 0:TALL, :]), 0.0)
            right = jnp.where(spot < last, full_of(v.f_right[b, j, 0:TALL, :]), 0.0)
            v.mm_tmp[pl.ds(fx + 8 + PITCH + j, TALL, stride=PITCH), :] = left
            v.mm_tmp[pl.ds(fx + 8 + PITCH + PITCH - 2 + j, TALL, stride=PITCH), :] = right
        for block in range(2):
            left = jnp.where(spot > 0, full_of(v.n_left[b, block, 0:TALL, :]), 0.0)
            right = jnp.where(spot < last, full_of(v.n_right[b, block, 0:TALL, :]), 0.0)
            v.tmp[0:SPREAD, :] = full_of(v.hgo[b, :, 256 + block * 128 : 384 + block * 128])
            v.tmp[pl.ds(1, TALL, stride=PITCH), :] = left
            v.tmp[pl.ds(PITCH - 2, TALL, stride=PITCH), :] = right
            v.hgo[b, :, 256 + block * 128 : 384 + block * 128] = half_of(v.tmp[0:SPREAD, :])
        for tap in range(9):
            at = 8 + PITCH + steps[tap]
            heads_part(v, b, tap)[...] = half_of(v.mm_tmp[pl.ds(fx + at, SPREAD), :])
        for part in range(2):
            name = (FLOW_HIDDEN, MASK_HIDDEN)[part]
            lanes = slice(part * 256, (part + 1) * 256)
            act, slope = act_slope(mm(v.hx_c[b, 0:SPREAD, :], v.w_h[0:768, lanes]) + mm(v.hx_f[b, 0:SPREAD, :], v.w_h[768:1152, lanes]) + bias_of(v, name, 2))
            v.slope_h[b, :, lanes] = half_of(slope)
            if part == 0:
                for block in range(2):
                    value = jnp.where(seen, act[:, block * 128 : (block + 1) * 128], 0.0)
                    v.feat[b, 0:SPREAD, block * 128 : (block + 1) * 128] = half_of(value)
                v.feat[b, SPREAD:SPAN, :] = jnp.zeros((SPAN - SPREAD, HEAD), jnp.bfloat16)
            else:
                for block in range(2):
                    v.tmp[0:SPREAD, :] = act[:, block * 128 : (block + 1) * 128]
                    for x in range(COLS):
                        v.final[pl.ds(x, TALL, stride=COLS), :] = v.tmp[pl.ds(2 + x, TALL, stride=PITCH), :]
                    v.mf[b, :, block * 128 : (block + 1) * 128] = half_of(v.final[...])
        moved = nt(v.w_fo[...], v.feat[b])
        v.zt[...] = moved
        delta = jnp.zeros((8, SPAN), jnp.float32)
        for tap in range(9):
            pair = jnp.concatenate([v.zt[2 * tap : 2 * tap + 2, :], jnp.zeros((6, SPAN), jnp.float32)], axis=0)
            delta = delta + pltpu.roll(pair, (-steps[tap]) % SPAN, 1)
        v.tmp[0:SPAN, :] = jnp.zeros((SPAN, LANES), jnp.float32)
        v.final[...] = full_of(v.xc[b, 32 : 32 + AREA, 256:384])
        for x in range(COLS):
            v.tmp[pl.ds(2 + x, TALL, stride=PITCH), :] = v.final[pl.ds(x, TALL, stride=COLS), :]
        pick = jnp.where(lane_index((16, LANES)) == row_index((16, LANES)) + 126, 1.0, 0.0)
        base = nt(half_of(pick), half_of(v.tmp[0:SPAN, :]))[0:8, :]
        bias = v.bias[BIAS_AT[FLOW_OUT] : BIAS_AT[FLOW_OUT] + 1, :]
        first = row_index((8, SPAN)) == 0
        second = row_index((8, SPAN)) == 1
        shift = jnp.where(first, bias[0:1, 0:1], jnp.where(second, bias[0:1, 1:2], 0.0))
        new = base + delta + shift
        v.out_flow[b] = new
        error = new - v.target[b]
        root = jnp.sqrt(error * error + 1.0)
        valid = jnp.where(first | second, v.valid[b], 0.0)
        piece = jnp.sum(valid * root)
        divisor = jnp.maximum(v.pick_count(counts, b), 1.0)
        gradient = plane / divisor * valid * error / root
        v.dg[b] = gradient
        v.losses[...] = jnp.where(row_index((8, LANES)) == b, piece, v.losses[...])
        return carry

    v.losses[...] = jnp.zeros((8, LANES), jnp.float32)
    lax.fori_loop(0, BATCH, image, 0)
    v.halo_dg.start()
    v.swap_loss.start()


def mask_output(v):
    def image(b, carry):
        store = pltpu.make_async_copy(v.mask_low, v.out_mask.at[b], v.osem.at[3])
        pl.when(b > 0)(store.wait)
        for block in range(5):
            wide = min(128, MASK - block * 128)
            lanes = slice(block * 128, block * 128 + wide)
            at = BIAS_AT[MASK_OUT] + block
            value = mm(v.mf[b], v.w_mo[:, lanes]) + v.bias[at : at + 1, 0:wide]
            v.mask_low[:, lanes] = half_of(0.25 * value)
        store.start()
        return carry

    lax.fori_loop(0, BATCH, image, 0)


def heads_back(v):
    spot, last = v.spot, v.space - 1
    seen, own = ring_masks(v, (SPREAD, LANES))
    steps = [(a - 1) * PITCH + (c - 1) for a in range(3) for c in range(3)]
    v.halo_dg.receive()

    def zb(c, low, rows):
        at = c * (2 * EDGE + SPREAD) + low
        return v.mm_tmp.at[at : at + rows]

    def image(b, carry):
        x = lax.rem(lane_index((8, SPAN)), PITCH)
        own_dg = v.dg[b]
        left = jnp.where((x < 2) & (spot > 0), pltpu.roll(v.dg_left[b], SPAN - COLS, 1), 0.0)
        right = jnp.where((x >= PITCH - 2) & (spot < last), pltpu.roll(v.dg_right[b], COLS, 1), 0.0)
        inside = lane_index((8, SPAN)) < SPREAD
        wide_dg = full_of(half_of(jnp.where(inside, own_dg + left + right, 0.0)))
        own_low = full_of(half_of(own_dg))
        v.dt[...] = jnp.zeros_like(v.dt)
        v.dto[...] = jnp.zeros_like(v.dto)
        for tap in range(9):
            v.dt[2 * tap : 2 * tap + 2, :] = pltpu.roll(wide_dg, steps[tap] % SPAN, 1)[0:2, :]
            v.dto[2 * tap : 2 * tap + 2, :] = pltpu.roll(own_low, steps[tap] % SPAN, 1)[0:2, :]
        v.dtb[b] = half_of(v.dto[...])
        from_flow = tn(half_of(v.dt[...]), v.w_fo[...])
        for block in range(4):
            lanes = slice(block * 128, (block + 1) * 128)
            value = from_flow[0:SPREAD, lanes] if block < 2 else full_of(v.hgo[b, :, lanes])
            value = value * full_of(v.slope_h[b, :, lanes])
            v.hgo[b, :, lanes] = half_of(jnp.where(seen, value, 0.0))
        total = jnp.zeros((SPREAD, LANES), jnp.float32)
        for a in range(3):
            value = nt(v.hgo[b], v.w_h[a * 384 : (a + 1) * 384, :])
            for c in range(3):
                zb(c, EDGE, SPREAD)[...] = value[:, c * 128 : (c + 1) * 128]
            for c in range(3):
                at = EDGE - steps[a * 3 + c]
                total = total + zb(c, at, SPREAD)[...]
        for block in range(4):
            lanes = slice(block * 128, (block + 1) * 128)
            v.hgo[b, :, lanes] = half_of(jnp.where(own, full_of(v.hgo[b, :, lanes]), 0.0))
        v.tmp[0:SPREAD, :] = total
        for x in range(COLS):
            v.final[pl.ds(x, TALL, stride=COLS), :] = v.tmp[pl.ds(2 + x, TALL, stride=PITCH), :]
        r = v.final[...] + full_of(v.grad_net[b])

        s = full_of(v.xc[b, 32 : 32 + AREA, 0:128])
        update, reset, cand = v.lu[b], v.lr[b], v.lc[b]
        cg = half_of(r * update * (1.0 - cand * cand))
        v.gc[b, 32 : 32 + AREA, 256:384] = cg
        reset_grad = 0.0
        for t in range(5):
            rows = slice((4 - t) * COLS, (4 - t) * COLS + AREA)
            reset_grad = reset_grad + nt(v.gc[b, rows, 256:384], v.w_ls[t * 128 : (t + 1) * 128, 256:384])
        v.gc[b, 32 : 32 + AREA, 0:128] = half_of(r * (cand - s) * update * (1.0 - update))
        v.gc[b, 32 : 32 + AREA, 128:256] = half_of(reset_grad * s * reset * (1.0 - reset))
        state_grad = r * (1.0 - update) + reset_grad * reset
        inputs_grad = 0.0
        for t in range(5):
            rows = slice((4 - t) * COLS, (4 - t) * COLS + AREA)
            state_grad = state_grad + nt(v.gc[b, rows, 0:256], v.w_ls[t * 128 : (t + 1) * 128, 0:256])
            inputs_grad = inputs_grad + nt(v.gc[b, rows, :], v.w_li[t * 256 : (t + 1) * 256, :])
        high = half_of(own_dg)
        low = half_of(own_dg - full_of(high))
        pick = half_of(jnp.where(lane_index((8, LANES)) == row_index((8, LANES)) + 126, 1.0, 0.0))
        v.tmp[0:SPAN, :] = tn(high, pick) + tn(low, pick)
        for x in range(COLS):
            v.final[pl.ds(x, TALL, stride=COLS), :] = v.tmp[pl.ds(2 + x, TALL, stride=PITCH), :]
        v.lu[b] = state_grad
        v.lr[b] = inputs_grad[:, 0:128]
        v.lc[b] = inputs_grad[:, 128:256] + v.final[...]

        def peer(t, carry):
            at = pl.ds(pl.multiple_of(t * ROWS * COLS, 16), ROWS * COLS)
            v.a_state[t, b] = half_of(v.lu[b, at, :])
            v.a_context[t, b] = half_of(v.lr[b, at, :])
            v.a_motion[t, b] = half_of(v.lc[b, at, :])
            return carry

        lax.fori_loop(0, v.space, peer, 0)
        return carry

    for c in range(3):
        zb(c, 0, EDGE)[...] = jnp.zeros((EDGE, LANES), jnp.float32)
        zb(c, EDGE + SPREAD, EDGE)[...] = jnp.zeros((EDGE, LANES), jnp.float32)
    lax.fori_loop(0, BATCH, image, 0)
    v.swap_loss.receive()
    v.back_state.start()
    v.back_context.start()
    v.back_motion.start()


def unpack_back(v, src, dst):
    def peer(t, carry):
        for b in range(BATCH):
            value = full_of(src[t, b])
            for y in range(ROWS):
                at = pl.multiple_of(y * WIDE + t * COLS, COLS)
                dst[b, pl.ds(at, COLS), :] = value[y * COLS : (y + 1) * COLS, :]
        return carry

    lax.fori_loop(0, v.space, peer, 0)


def seams():
    starts, bias_row, _, _ = flat_rows()
    edges = sorted(starts.values()) + [bias_row]
    tiles = sorted({row // 16 for row in edges if row % 16})
    parts = {}
    for low, high in zip(edges, edges[1:]):
        for tile in tiles:
            if low < (tile + 1) * 16 and high > tile * 16:
                parts[tile] = parts.get(tile, 0) + 1
    return {tile: (index, parts[tile]) for index, tile in enumerate(tiles)}


class Flush:
    def __init__(self, v):
        self.v, self.at, self.busy, self.small = v, 0, {}, []
        self.tiles = seams()
        self.left = {tile: parts for tile, (_, parts) in self.tiles.items()}
        v.seam[...] = jnp.zeros_like(v.seam)
        top = (max(self.tiles) + 1) * 16
        rest = v.out_flat.shape[0] - top
        v.seam_low[16 * 16 : 16 * 16 + rest, :] = jnp.zeros((rest, LANES), jnp.bfloat16)
        self.write(16, rest, top)

    def write(self, index, rows, base):
        v = self.v
        copy = pltpu.make_async_copy(
            v.seam_low.at[index * 16 : index * 16 + rows], v.out_flat.at[base : base + rows], v.fsem.at[index]
        )
        copy.start()
        self.small.append(copy)

    def send(self, low, length, base):
        v, slot = self.v, self.at % 2
        self.at += 1
        if slot in self.busy:
            self.busy[slot].wait()
        cast_rows(v.stage.at[slot], 0, v.flat, low, length, jnp.bfloat16)
        copy = pltpu.make_async_copy(
            v.stage.at[slot, 0:length], v.out_flat.at[base : base + length], v.ssem.at[slot, 0]
        )
        copy.start()
        self.busy[slot] = copy

    def layer(self, start, rows):
        v, stop = self.v, start + rows
        for tile in self.tiles:
            low, high = max(start, tile * 16), min(stop, tile * 16 + 16)
            if low >= high:
                continue
            index = self.tiles[tile][0]
            v.seam[index, low - tile * 16 : high - tile * 16, :] = v.flat[MARGIN + low - start : MARGIN + high - start, :]
            self.left[tile] -= 1
            if not self.left[tile]:
                v.seam_low[index * 16 : index * 16 + 16, :] = half_of(v.seam[index])
                self.write(index, 16, tile * 16)
        low, high = -(-start // 16) * 16, stop // 16 * 16
        if high > low:
            self.send(MARGIN + low - start, high - low, low)

    def settle(self):
        for copy in list(self.busy.values()) + self.small:
            copy.wait()
        self.busy, self.small = {}, []


SHARE = 3072


class Reduce:
    ORDER = (
        (3, 3072, 3072), (3, 0, 3072), (2, 3072, 3072), (2, 0, 3072), (1, 3072, 3072), (1, 0, 3072),
        (0, 1024, 3072), (0, 4096, 2048), (0, 0, 1024),
    )

    def __init__(self, v, count):
        self.v, self.count = v, count
        self.flying, self.queue = [], []
        self.copies = {}
        rank = v.rank
        self.lower, self.upper = lax.rem(rank, 2), lax.div(rank, 2)
        self.side, self.depth = lax.rem(v.spot, 2), lax.div(v.spot, 2)
        self.group = v.space // 2

    def part(self, k):
        return self.ORDER[k][2] // 4 // self.v.space

    def slice_at(self, k, spot):
        return lax.rem(spot, 2) * (self.ORDER[k][2] // 8) + lax.div(spot, 2) * self.part(k)

    def offer(self, *numbers):
        self.v.flush.settle()
        self.queue += list(numbers)

    def tick(self):
        stages = (self.core, self.across, self.stripes, self.along, self.beside)
        for entry in self.flying:
            stages[entry[1]](entry[0])
            entry[1] += 1
        self.flying = [entry for entry in self.flying if entry[1] < len(stages)]
        if self.queue:
            number = self.queue.pop(0)
            self.begin(number)
            self.flying.append([number, 0])

    def begin(self, k):
        v, slot = self.v, k % 2
        quarter, low, size = self.ORDER[k]
        start = quarter * self.count // (LANES * 16) * 16 + low
        half = size // 2

        def rows(which):
            return v.out_flat.at[pl.ds(pl.multiple_of(start + which * half, 16), half)]

        copy = remote(
            rows(1 - self.lower), v.rcore.at[slot, 0:half], v.rsend.at[0, slot], v.rrecv.at[0, slot], {DP: v.mate}
        )
        own = pltpu.make_async_copy(rows(self.lower), v.own.at[slot, 0:half], v.rlocal.at[slot])
        copy.start()
        own.start()
        self.copies[k] = (copy, own)

    def core(self, k):
        v, slot = self.v, k % 2
        copy, own = self.copies[k]
        copy.wait()
        own.wait()
        if k >= 2:
            self.x_copy(k - 2).wait_send()
        quarter = self.ORDER[k][2] // 4

        def add(step, carry):
            at = pl.multiple_of(step * 128, 128)
            near = pl.ds(pl.multiple_of(self.upper * quarter + at, 128), 128)
            far = pl.ds(pl.multiple_of((1 - self.upper) * quarter + at, 128), 128)
            to = pl.ds(at, 128)
            v.tx[slot, to, :] = half_of(full_of(v.own[slot, far, :]) + full_of(v.rcore[slot, far, :]))
            v.ks[slot, to, :] = full_of(v.own[slot, near, :]) + full_of(v.rcore[slot, near, :])
            return carry

        lax.fori_loop(0, quarter // 128, add, 0)
        self.x_copy(k).start()

    def x_copy(self, k):
        v, slot = self.v, k % 2
        rows = slice(0, self.ORDER[k][2] // 4)
        return remote(
            v.tx.at[slot, rows], v.rx.at[slot, rows], v.rsend.at[1, slot], v.rrecv.at[1, slot], {DP: v.other}
        )

    def s_copy(self, k, step):
        v, slot, part = self.v, k % 2, self.part(k)
        to = lax.rem(v.spot + step, v.space)
        src = v.ts.at[slot, pl.ds(pl.multiple_of(self.slice_at(k, to), 16), part)]
        dst = v.rs.at[slot, v.spot, 0:part]
        return remote(src, dst, v.s2send.at[slot, step], v.s2recv.at[slot, step], {SPACE: to})

    def each(self, what, start, stop):
        def body(step, carry):
            what(step)
            return carry

        lax.fori_loop(start, stop, body, 0)

    def across(self, k):
        v, slot = self.v, k % 2
        self.x_copy(k).wait_recv()
        if k >= 2:
            self.each(lambda step: self.s_copy(k - 2, step).wait_send(), 1, v.space)

        def add(step, carry):
            to = pl.ds(pl.multiple_of(step * 128, 128), 128)
            value = v.ks[slot, to, :] + full_of(v.rx[slot, to, :])
            v.ks[slot, to, :] = value
            v.ts[slot, to, :] = half_of(value)
            return carry

        lax.fori_loop(0, self.ORDER[k][2] // 4 // 128, add, 0)
        part = self.part(k)
        v.acc[slot, 0:part, :] = v.ks[slot, pl.ds(pl.multiple_of(self.slice_at(k, v.spot), 16), part), :]
        self.each(lambda step: self.s_copy(k, step).start(), 1, v.space)

    def place(self, k, lower, upper, spot):
        quarter, low, size = self.ORDER[k]
        at = low + lower * (size // 2) + upper * (size // 4) + self.slice_at(k, spot)
        return pl.ds(pl.multiple_of(at, 16), self.part(k))

    def f_copy(self, k, step):
        v, slot = self.v, k % 2
        quarter = self.ORDER[k][0]
        to = lax.rem(self.depth + step, self.group) * 2 + self.side
        return remote(
            v.fin.at[slot, 0 : self.part(k)], v.gath.at[self.place(k, self.lower, self.upper, v.spot)],
            v.fsend.at[slot, step], v.frecv.at[k, v.rank, self.depth], {DP: quarter, SPACE: to},
        )

    def f_all(self, k, what):
        v = self.v
        pl.when(v.rank != self.ORDER[k][0])(lambda: what(self.f_copy(k, 0)))
        self.each(lambda step: what(self.f_copy(k, step)), 1, self.group)

    def stripes(self, k):
        v, slot, part = self.v, k % 2, self.part(k)
        quarter = self.ORDER[k][0]
        self.each(lambda step: self.s_copy(k, step).wait_recv(), 1, v.space)

        def add(step, value):
            return value + full_of(v.rs[slot, lax.rem(v.spot + step, v.space), 0:part])

        value = half_of(lax.fori_loop(1, v.space, add, v.acc[slot, 0:part, :]))
        if k >= 2:
            self.f_all(k - 2, lambda copy: copy.wait_send())
        v.fin[slot, 0:part, :] = value

        @pl.when(v.rank == quarter)
        def _():
            v.gath[self.place(k, self.lower, self.upper, v.spot), :] = v.fin[slot, 0:part, :]

        self.f_all(k, lambda copy: copy.start())

    def f_wait(self, k, source, step):
        v = self.v
        depth = lax.rem(self.depth + step, self.group)
        spot = depth * 2 + self.side
        remote(
            v.fin.at[0, 0 : self.part(k)], v.gath.at[self.place(k, source % 2, source // 2, spot)],
            v.fsend.at[0, 0], v.frecv.at[k, source, depth], {SPACE: v.twin},
        ).wait_recv()

    def y_copies(self, k):
        v = self.v
        quarter, low, size = self.ORDER[k]
        out = []
        for i in range(4):
            at = pl.multiple_of(low + i * (size // 4) + self.side * (size // 8), 16)
            block = v.gath.at[pl.ds(at, size // 8)]
            out.append(remote(block, block, v.ysend.at[k, i], v.yrecv.at[k, i], {SPACE: v.twin}))
        return out

    def along(self, k):
        v = self.v
        quarter = self.ORDER[k][0]

        @pl.when(v.rank == quarter)
        def _():
            for source in range(4):
                self.each(
                    lambda step: self.f_wait(k, source, step), 1 if source == quarter else 0, self.group
                )
            for copy in self.y_copies(k):
                copy.start()

    def beside(self, k):
        v = self.v

        @pl.when(v.rank == self.ORDER[k][0])
        def _():
            for copy in self.y_copies(k):
                copy.wait()

    def settle(self):
        v = self.v
        for k in range(len(self.ORDER) - 2, len(self.ORDER)):
            self.x_copy(k).wait_send()
            self.each(lambda step: self.s_copy(k, step).wait_send(), 1, v.space)
            self.f_all(k, lambda copy: copy.wait_send())

    def ready(self):
        v, count = self.v, self.count
        v.gath[2 * SHARE :, :] = jnp.zeros((32, LANES), jnp.bfloat16)

        @pl.when(v.rank == 3)
        def _():
            at = self.bias_base() - 3 * count // (LANES * 16) * 16
            v.gath[at : at + 32, :] = half_of(full_of(v.gath[at : at + 32, :]) + v.bsum[...])

    def lay(self, first, last):
        v, count = self.v, self.count
        offset = v.rank * count - quarter_base(v.rank, count) * LANES
        skip = lax.div(offset, LANES)
        matrix = lane_matrix(lax.rem(offset, LANES), False)

        def out(step):
            at = pl.multiple_of(step * 256, 256)
            slot = lax.rem(step, 2)
            return pltpu.make_async_copy(v.gout.at[slot], v.out_grads.at[pl.ds(at, 256)], v.osem.at[4 + slot])

        def place(step, carry):
            at = pl.multiple_of(step * 256, 256)
            both = mm(v.gath[pl.ds(at, 288), :], matrix)
            v.tmp[0:288, :] = both[:, 0:LANES]
            v.tmp[288:576, :] = both[:, LANES:]
            pl.when(step > first + 1)(out(step - 2).wait)
            v.gout[lax.rem(step, 2)] = v.tmp[pl.ds(skip, 256), :] + v.tmp[pl.ds(skip + 289, 256), :]
            out(step).start()
            return carry

        lax.fori_loop(first, last, place, 0)
        for step in (last - 2, last - 1):
            out(step).wait()

    def bias_base(self):
        return flat_rows()[1] // 16 * 16

    def bias_core(self):
        v = self.v
        self.b1 = remote(v.bown, v.bcore, v.bsend.at[0], v.brecv.at[0], {DP: v.mate})
        self.b1.start()

    def bias_across(self):
        v = self.v
        self.b1.wait()
        v.btwo[...] = v.bown[...] + v.bcore[...]
        self.b2 = remote(v.btwo, v.bacross, v.bsend.at[1], v.brecv.at[1], {DP: v.other})
        self.b2.start()

    def bias_stripes(self):
        v = self.v
        self.b2.wait()
        v.bfour[...] = v.btwo[...] + v.bacross[...]
        self.b3 = Swap(v, 8, v.bfour, v.ball, True)
        self.b3.start()

    def bias_end(self):
        v = self.v
        self.b3.receive()
        self.b3.sent()
        v.ball[v.spot] = v.bfour[...]
        v.bsum[...] = jnp.sum(v.ball[...], axis=0)


def ones_sum(g):
    return mm(jnp.ones((8, g.shape[0]), jnp.bfloat16), g)[0:1, :]


def keep_bias(v, name, value):
    for block in range(-(-value.shape[1] // 128)):
        at = BIAS_AT[name] + block
        v.gbias[at : at + 1, :] = value[:, block * 128 : (block + 1) * 128]


def gradients_gru(v, gates_name, cand_name, parts, g_of):
    starts, _, _, _ = flat_rows()
    total = 0.0
    for b in range(BATCH):
        total = total + ones_sum(g_of(b))
    keep_bias(v, gates_name, total[:, 0:256])
    keep_bias(v, cand_name, total[:, 256:384])

    for t in range(5):
        s_part, i_part, r_part = parts(t)
        state = tn_all(s_part, g_of, 0, 256)
        v.mm_tmp[pl.ds(MARGIN + t * 384, 128), :] = tn_all(r_part, g_of, 256, 384)
        inputs = tn_all(i_part, g_of, 0, 384)
        pack_pairs(v.flat, t * 384, 128, state[:, 0:128], state[:, 128:256])
        pack_pairs(v.flat, t * 384 + 128, 256, inputs[:, 0:128], inputs[:, 128:256])
        v.mm_tmp[pl.ds(MARGIN + t * 384 + 128, 256), :] = inputs[:, 256:384]
    v.flush.layer(starts[gates_name], 3840)
    cast_rows(v.flat, MARGIN, v.mm_tmp, MARGIN, 1920, jnp.float32)
    v.flush.layer(starts[cand_name], 1920)


def tn_all(part, g_of, low, high):
    total = 0.0
    for b in range(BATCH):
        total = total + tn(part(b), g_of(b, low, high))
    return total


def gradients_heads(v):
    starts, _, _, _ = flat_rows()
    total = 0.0
    for b in range(BATCH):
        total = total + ones_sum(v.hgo[b])
    keep_bias(v, FLOW_HIDDEN, total[:, 0:256])
    keep_bias(v, MASK_HIDDEN, total[:, 256:512])
    for name, lane in ((FLOW_HIDDEN, 0), (MASK_HIDDEN, 256)):
        for tap in range(9):
            value = 0.0
            for b in range(BATCH):
                value = value + tn(heads_part(v, b, tap)[...], v.hgo[b, :, lane : lane + 256])
            pack_pairs(v.flat, tap * 128, 128, value[:, 0:128], value[:, 128:256])
        v.flush.layer(starts[name], 2304)

    total = 0.0
    sums = 0.0
    for b in range(BATCH):
        total = total + mm(v.dtb[b], v.feat[b])
        sums = sums + jnp.sum(full_of(half_of(v.dg[b])), axis=1, keepdims=True)
    lane1 = lane_index((1, LANES))
    at = BIAS_AT[FLOW_OUT]
    v.gbias[at : at + 1, :] = jnp.where(lane1 == 0, sums[0:1, :], jnp.where(lane1 == 1, sums[1:2, :], 0.0))
    v.fo_tmp[...] = total[:, 0:128]
    v.fo_tmp2[...] = total[:, 128:256]
    for quarter in range(4):
        value = 0.0
        for which in range(2):
            rows = jnp.concatenate(
                [v.fo_tmp[pl.ds(which, 9, stride=2), :], v.fo_tmp2[pl.ds(which, 9, stride=2), :]], axis=1
            )
            value = value + nt(half_of(rows), split_pick(which, quarter))
        v.flat[pl.ds(MARGIN + quarter, 9, stride=4), :] = value
    v.flush.layer(starts[FLOW_OUT], 36)

    lane = lane_index((128, LANES))
    low_half = lane < 64
    even, odd = [], []
    total = 0.0
    for b in range(BATCH):
        total = total + ones_sum(quarter_of(v.grad_mask[b]))
    for block in range(5):
        wide = min(128, MASK - block * 128)
        at = BIAS_AT[MASK_OUT] + block
        v.gbias[at : at + 1, 0:wide] = total[:, block * 128 : block * 128 + wide]
        value = 0.0
        for b in range(BATCH):
            value = value + tn(v.mf[b], quarter_of(v.grad_mask[b, :, block * 128 : block * 128 + wide]))
        v.pair_a[:, 0:wide] = value
        even.append(v.pair_a[pl.ds(0, 128, stride=2), :])
        odd.append(pltpu.roll(v.pair_a[pl.ds(1, 128, stride=2), :], 64, 1))
    for i in range(4):
        v.flat[pl.ds(MARGIN + i, 128, stride=9), :] = even[i]
    v.flat[pl.ds(MARGIN + 4, 128, stride=9), :] = jnp.where(low_half, even[4], odd[0])
    for i in range(4):
        v.flat[pl.ds(MARGIN + 5 + i, 128, stride=9), :] = jnp.where(low_half, odd[i], odd[i + 1])
    v.flush.layer(starts[MASK_OUT], 1152)


def rows_back(v):
    v.back_state.receive()
    take_own(v, v.a_state, v.b_state)
    unpack_back(v, v.b_state, v.state)
    v.reduce.tick()
    v.back_context.receive()
    v.back_motion.receive()
    take_own(v, v.a_context, v.b_context)
    take_own(v, v.a_motion, v.b_motion)
    unpack_back(v, v.b_context, v.lr)
    unpack_back(v, v.b_motion, v.lu)

    def image(b, carry):
        at = pl.ds(pl.multiple_of(b * AREA, AREA), AREA)
        r = v.state[b]
        s = full_of(v.net[b])
        update, reset, cand = v.ru[b], v.rr[b], v.rc[b]
        cg = full_of(half_of(r * update * (1.0 - cand * cand)))
        spread_five(v, cg, None, 256, True)
        reset_grad = 0.0
        for t in range(5):
            reset_grad = reset_grad + nt(
                taps_part(v, t, 256, 384)[...], v.w_rs[t * 128 : (t + 1) * 128, 256:384]
            )
        low = full_of(half_of(r * (cand - s) * update * (1.0 - update)))
        high = full_of(half_of(reset_grad * s * reset * (1.0 - reset)))
        spread_five(v, low, None, 0, True)
        spread_five(v, high, None, 128, True)
        v.gr[b] = taps_part(v, 2, 0, 384)[...]
        state_grad = r * (1.0 - update) + reset_grad * reset
        inputs_grad = jnp.concatenate([v.lr[b], v.lu[b]], axis=1)
        for t in range(5):
            state_grad = state_grad + nt(taps_part(v, t, 0, 256)[...], v.w_rs[t * 128 : (t + 1) * 128, 0:256])
            inputs_grad = inputs_grad + nt(taps_part(v, t, 0, 384)[...], v.w_ri[t * 256 : (t + 1) * 256, :])
        v.ru[b] = state_grad
        v.rr[b] = inputs_grad[:, 0:128]
        motion = inputs_grad[:, 128:256]
        grad = half_of(motion * full_of(v.slope_m[b]))
        v.mge[b, 256:896, :] = grad
        high = half_of(motion)
        low = half_of(motion - full_of(high))
        pick = half_of(jnp.where(lane_index((16, LANES)) == row_index((16, LANES)) + 126, 1.0, 0.0))
        v.gf_base[b] = (nt(pick, high) + nt(pick, low))[0:8, :]
        return carry

    lax.fori_loop(0, BATCH, image, 0)
    v.halo_mg.start()
    v.store_gnet.start()
    v.store_gctx.start()


def gcorr_stores(v, b):
    return [
        pltpu.make_async_copy(v.mm_tmp.at[y * 328 : y * 328 + CORR], v.out_gcorr.at[b, y], v.gsem.at[y])
        for y in range(ROWS)
    ]


def branch_back(v):
    v.halo_mg.receive()

    def image(b, carry):
        up = jnp.where(v.spot > 0, full_of(v.mge[b, 0:256, :]), 0.0)
        own = full_of(v.mge[b, 256:896, :])
        down = jnp.where(v.spot < v.space - 1, full_of(v.mge[b, 896:1152, :]), 0.0)
        spread_rows(v, 0, (jnp.concatenate([up, own, down], axis=0),), 1152, v.xi, 0, 128, True)
        joint = 0.0
        for a in range(3):
            for c in range(3):
                k = (a * 3 + c) * 256
                joint = joint + nt(
                    v.xi[(2 - a) * 128 : (2 - a) * 128 + 896, c * 128 : (c + 1) * 128], v.w_mm[k : k + 256, :]
                )
        branch = joint * full_of(v.slope_j[b])
        low = full_of(half_of(edge_rows(v, branch[:, 0:128], WIDE)))
        high = full_of(half_of(edge_rows(v, branch[:, 128:256], WIDE)))
        spread_rows(v, 0, (low, high), 896, v.hx_j.at[b], 0, 256, True)
        return carry

    lax.fori_loop(0, BATCH, image, 0)


def branch_own(v, b, low=0, high=256):
    return v.hx_j[b, 128:768, 256 + low : 256 + high]


def flow_back(v):
    def image(b, carry):
        flow_grad = 0.0
        for a in range(3):
            rows = slice((2 - a) * 128, (2 - a) * 128 + 640)
            for c in range(3):
                k = a * 3 + c
                flow_grad = flow_grad + nt(
                    v.hx_j[b, rows, c * 256 + 128 : (c + 1) * 256], v.w_fm[k * 128 : (k + 1) * 128, :]
                )
        v.fpg[b] = half_of(flow_grad * full_of(v.slope_fi[b]))
        z = nt(v.w_fi[...], v.fpg[b])
        total = jnp.zeros((32, LANES), jnp.float32)
        lane = lane_index((32, LANES))
        for across in range(7):
            v.fs[across] = jnp.zeros((32, LANES), jnp.float32)
            for y in range(ROWS):
                v.fs[across, 2 * y : 2 * y + 16, :] += z[across * 16 : across * 16 + 16, y * 128 : (y + 1) * 128]
            d = across - 3
            value = v.fs[across]
            if d:
                value = pltpu.roll(value, d % LANES, 1)
                value = jnp.where((lane - d >= 0) & (lane - d < WIDE), value, 0.0)
            total = total + value
        v.gf[b] = total
        return carry

    lax.fori_loop(0, BATCH, image, 0)
    v.halo_gf.start()


def corr_back(v):
    def image(b, carry):
        corr_grad = 0.0
        for a in range(3):
            rows = slice((2 - a) * 128, (2 - a) * 128 + 640)
            for c in range(3):
                k = a * 3 + c
                corr_grad = corr_grad + nt(v.hx_j[b, rows, c * 256 : (c + 1) * 256], v.w_cm[k * 256 : (k + 1) * 256, :])
        v.cpg[b] = half_of(corr_grad * full_of(v.slope_ci[b]))
        stores = gcorr_stores(v, b)
        for store in stores:
            pl.when(b > 0)(store.wait)
        gcorr = nt(v.w_ci[...], v.cpg[b])
        for y in range(ROWS):
            v.mm_tmp[y * 328 : y * 328 + CORR, :] = gcorr[:, y * WIDE : (y + 1) * WIDE]
        for store in stores:
            store.start()
        return carry

    lax.fori_loop(0, BATCH, image, 0)


def summed(v, ref, name):
    total = 0.0
    for b in range(BATCH):
        total = total + ones_sum(ref(b))
    keep_bias(v, name, total)


def gradients_motion(v):
    starts = flat_rows()[0]
    summed(v, lambda b: v.mge[b, 256:896, :], MOTION_MIX)
    for k in range(9):
        a, c = k // 3, k % 3
        value = 0.0
        for b in range(BATCH):
            value = value + tn(
                v.hx_j[b, a * 128 : a * 128 + 640, c * 256 : (c + 1) * 256], v.mge[b, 256:896, :]
            )
        v.mm_tmp[k * 256 : (k + 1) * 256, :] = value
    lane36 = lane_index((36, LANES))
    for r in range(63):
        first = v.mm_tmp[pl.ds(r, 36, stride=64), :]
        second = v.mm_tmp[pl.ds(r + 1, 36, stride=64), :]
        if r:
            first = pltpu.roll(first, LANES - 2 * r, 1)
        second = pltpu.roll(second, 126 - 2 * r, 1)
        v.flat[pl.ds(MARGIN + r, 36, stride=63), :] = jnp.where(lane36 < 126 - 2 * r, first, second)
    v.flush.layer(starts[MOTION_MIX], 2268)


def gradients_branches(v):
    starts = flat_rows()[0]
    summed(v, lambda b: branch_own(v, b), CORR_MIX)
    summed(v, lambda b: branch_own(v, b, 128, 256), FLOW_MIX)
    for k in range(9):
        a, c = k // 3, k % 3
        value = 0.0
        for b in range(BATCH):
            value = value + tn(
                v.hx_f[b, (a + 1) * 128 : (a + 1) * 128 + 640, c * 128 : (c + 1) * 128], branch_own(v, b, 128, 256)
            )
        v.pair_a[0:128, :] = value
        even, odd = (v.pair_a[pl.ds(i, 64, stride=2), :] for i in range(2))
        v.flat[MARGIN + 64 * k : MARGIN + 64 * (k + 1), :] = jnp.where(
            lane_index((64, LANES)) < 64, pltpu.roll(even, 64, 1), odd
        )
    v.flush.layer(starts[FLOW_MIX], 576)

    low_half = lane_index((128, LANES)) < 64
    for k in range(9):
        a, c = k // 3, k % 3
        value = 0.0
        for b in range(BATCH):
            value = value + tn(
                v.hx_c[b, (a + 1) * 128 : (a + 1) * 128 + 640, c * 256 : (c + 1) * 256], branch_own(v, b)
            )
        v.pair_a[...] = value[:, 0:128]
        v.pair_b[...] = value[:, 128:256]
        even, odd = (v.pair_a[pl.ds(i, 128, stride=2), :] for i in range(2))
        even_high, odd_high = (v.pair_b[pl.ds(i, 128, stride=2), :] for i in range(2))
        odd, odd_high = pltpu.roll(odd, 64, 1), pltpu.roll(odd_high, 64, 1)
        at = MARGIN + 384 * k
        v.flat[pl.ds(at, 128, stride=3), :] = even
        v.flat[pl.ds(at + 1, 128, stride=3), :] = jnp.where(low_half, even_high, odd)
        v.flat[pl.ds(at + 2, 128, stride=3), :] = jnp.where(low_half, odd, odd_high)
        if k == 4:
            v.reduce.tick()
    v.flush.layer(starts[CORR_MIX], 3456)


def gradients_flow_in(v):
    starts = flat_rows()[0]
    summed(v, lambda b: v.fpg[b], FLOW_IN)
    value = 0.0
    for b in range(BATCH):
        value = value + mm(v.xt[b, :, 256:896], v.fpg[b])
    v.flow_tmp[...] = value
    for across in range(7):
        for comp in range(2):
            v.flat[pl.ds(MARGIN + across * 2 + comp, 7, stride=14), :] = v.flow_tmp[
                pl.ds(across * 16 + comp, 7, stride=2), :
            ]
    v.flush.layer(starts[FLOW_IN], 98)


def gradients_corr_in(v):
    starts = flat_rows()[0]
    summed(v, lambda b: v.cpg[b], CORR_IN)
    value = 0.0
    for b in range(BATCH):
        value = value + mm(lines_of(v.corr, b, ROWS), v.cpg[b])
    pack_pairs(v.flat, 0, 324, value[:, 0:128], value[:, 128:256])
    v.flush.layer(starts[CORR_IN], 648)


def bias_tile(v):
    starts, bias_row, spots, inner = flat_rows()
    lead = bias_row % 16
    lane1 = lane_index((1, LANES))
    v.bown[...] = jnp.zeros_like(v.bown)
    for name, height, width in shapes():
        for block in range(-(-width // LANES)):
            value = v.gbias[BIAS_AT[name] + block : BIAS_AT[name] + block + 1, :]
            if name == FLOW_MIX:
                value = pltpu.roll(value, 64, 1)
            left = width - block * LANES
            if left < LANES:
                value = jnp.where(lane1 < left, value, 0.0)
            at = spots[name] + block * LANES
            row, shift = lead + at // LANES, at % LANES
            moved = pltpu.roll(value, shift, 1) if shift else value
            v.bown[row : row + 1, :] = v.bown[row : row + 1, :] + jnp.where(lane1 >= shift, moved, 0.0)
            if shift:
                v.bown[row + 1 : row + 2, :] = v.bown[row + 1 : row + 2, :] + jnp.where(lane1 < shift, moved, 0.0)


def finish(v):
    spot, last = v.spot, v.space - 1
    v.halo_gf.receive()
    for b in range(BATCH):
        v.tmp2[...] = v.gf[b]
        up = jnp.where(spot > 0, v.gf_up[b], 0.0)
        down = jnp.where(spot < last, v.gf_down[b], 0.0)
        v.tmp2[6:12, :] += up[16:22, :]
        v.tmp2[10:16, :] += down[0:6, :]
        for y in range(ROWS):
            v.out_gflow[b, 2 * y : 2 * y + 2, :] = (
                v.tmp2[6 + 2 * y : 8 + 2 * y, :] + v.gf_base[b, 0:2, y * 128 : (y + 1) * 128]
            )
    v.loss_in[v.spot] = v.losses[...]
    total = jnp.sum(v.loss_in[...], axis=0)
    counts = jnp.sum(v.counts[...], axis=0)
    v.out_loss[...] = total / jnp.maximum(counts, 1.0)


class View:
    pass


def main_kernel(names, space, count, *refs):
    v = View()
    for name, ref in zip(names, refs):
        setattr(v, name, ref)
    v.space = space
    v.lu, v.lc = v.motion, v.state
    v.spot = lax.axis_index(SPACE)
    v.rank = lax.axis_index(DP)
    v.mate, v.other, v.twin = mate_of(v.rank), lax.rem(v.rank + 2, 4), mate_of(v.spot)
    spot = v.spot
    barrier = pltpu.get_barrier_semaphore()

    def hello(step, carry):
        pl.semaphore_signal(barrier, inc=1, device_id={SPACE: lax.rem(spot + step, space)}, device_id_type=MESH)
        return carry

    lax.fori_loop(1, space, hello, 0)
    for turn in range(1, 4):

        def greet_rank(step, carry):
            place = lax.rem(spot + 2 * step, space)
            device = {DP: lax.rem(v.rank + turn, 4), SPACE: place}
            pl.semaphore_signal(barrier, inc=1, device_id=device, device_id_type=MESH)
            return carry

        lax.fori_loop(0, space // 2, greet_rank, 0)
    pl.semaphore_wait(barrier, space - 1 + 3 * (space // 2))

    v.store_gnet = pltpu.make_async_copy(v.ru, v.out_gnet, v.osem.at[0])
    v.store_gctx = pltpu.make_async_copy(v.rr, v.out_gctx, v.osem.at[1])
    rows = row_index((8, LANES))
    counted = jnp.zeros((8, LANES), jnp.float32)
    for b in range(BATCH):
        counted = jnp.where(rows == b, jnp.sum(v.valid[b, 0:1, :]), counted)
    v.count_out[...] = counted
    v.pick_count = lambda counts, b: jnp.sum(jnp.where((rows == b) & (lane_index((8, LANES)) == 0), counts, 0.0))
    v.swap_count = Swap(v, 0, v.count_out, v.counts, True)
    v.swap_context = Swap(v, 1, v.a_context, v.b_context)
    v.swap_motion = Swap(v, 2, v.a_motion, v.b_motion)
    v.swap_state = Swap(v, 3, v.a_state, v.b_state)
    v.back_context = Swap(v, 4, v.a_context, v.b_context)
    v.back_motion = Swap(v, 5, v.a_motion, v.b_motion)
    v.back_state = Swap(v, 6, v.a_state, v.b_state)
    v.swap_loss = Swap(v, 7, v.losses, v.loss_in, True)
    v.halo_corr = Halo(v, 0, v.corr.at[:, 0:2], v.corr.at[:, 3:5], v.corr_down, v.corr_up)
    v.halo_flow = Halo(v, 1, v.flow, v.flow, v.flow_down, v.flow_up)
    v.halo_final = Halo(v, 2, v.e_left, v.e_right, v.f_right, v.f_left)
    v.halo_mask = Halo(v, 3, v.m_left, v.m_right, v.n_right, v.n_left)
    v.halo_dg = Halo(v, 4, v.dg, v.dg, v.dg_right, v.dg_left)
    v.halo_mg = Halo(v, 5, v.mge.at[:, 256:512], v.mge.at[:, 640:896], v.mge.at[:, 896:1152], v.mge.at[:, 0:256])
    v.halo_gf = Halo(v, 6, v.gf, v.gf, v.gf_down, v.gf_up)

    v.halo_corr.start()
    v.halo_flow.start()
    v.swap_count.start()

    def first(b, carry):
        v.state[b] = full_of(v.context[b])
        pack_rows(v, v.state, b, v.a_context)
        return carry

    lax.fori_loop(0, BATCH, first, 0)
    v.swap_context.start()
    unpack_all(v, count)
    v.halo_flow.receive()
    v.halo_corr.receive()
    forward_rows(v)
    keep = [pltpu.make_async_copy(v.hx_c, v.out_keep_c, v.ksem.at[0]), pltpu.make_async_copy(v.hx_f, v.out_keep_f, v.ksem.at[1])]
    for copy in keep:
        copy.start()
    mask_gradient(v)
    v.swap_context.receive()
    v.swap_motion.receive()
    v.swap_state.receive()
    take_own(v, v.a_context, v.b_context)
    take_own(v, v.a_motion, v.b_motion)
    take_own(v, v.a_state, v.b_state)
    columns_in(v)
    columns_forward(v)
    for copy in keep:
        copy.wait()
    heads(v)
    mask_output(v)
    v.swap_context.sent()
    v.swap_motion.sent()
    v.swap_state.sent()
    heads_back(v)
    v.flush = Flush(v)
    red = v.reduce = Reduce(v, count)
    gradients_heads(v)
    red.offer(0)
    red.tick()
    gradients_gru(
        v,
        COLUMNS_GATES,
        COLUMNS_CANDIDATE,
        lambda t: (
            lambda b: v.xc[b, t * COLS : t * COLS + AREA, 0:128],
            lambda b: v.xc[b, t * COLS : t * COLS + AREA, 128:384],
            lambda b: v.xcr[b, t * COLS : t * COLS + AREA, :],
        ),
        lambda b, low=0, high=384: v.gc[b, 32 : 32 + AREA, low:high],
    )
    red.offer(1, 2)
    red.tick()
    rows_back(v)
    red.tick()
    keep = [
        pltpu.make_async_copy(v.out_keep_c, v.hx_c, v.ksem.at[0]),
        pltpu.make_async_copy(v.out_keep_f, v.hx_f, v.ksem.at[1]),
    ]
    for copy in keep:
        copy.start()
    gradients_gru(
        v,
        ROWS_GATES,
        ROWS_CANDIDATE,
        lambda t: (
            lambda b: v.xs[b * AREA : (b + 1) * AREA, t * 128 : (t + 1) * 128],
            lambda b: v.xi[b * AREA : (b + 1) * AREA, t * 256 : (t + 1) * 256],
            lambda b: v.xr[b * AREA : (b + 1) * AREA, t * 128 : (t + 1) * 128],
        ),
        lambda b, low=0, high=384: v.gr[b, :, low:high],
    )
    red.offer(3, 4)
    red.tick()
    gradients_motion(v)
    red.offer(5)
    red.tick()
    branch_back(v)
    red.tick()
    for copy in keep:
        copy.wait()
    gradients_branches(v)
    red.offer(6)
    red.tick()
    flow_back(v)
    gradients_flow_in(v)
    red.offer(7)
    red.tick()
    corr_back(v)
    gradients_corr_in(v)
    bias_tile(v)
    red.bias_core()
    red.offer(8)
    red.tick()
    for store in gcorr_stores(v, 0):
        store.wait()
    finish(v)
    red.bias_across()
    red.tick()
    red.bias_stripes()
    red.tick()
    red.bias_end()
    red.ready()
    red.tick()
    pl.when(v.rank > 0)(lambda: red.lay(0, 24))
    red.tick()
    pl.when(v.rank == 0)(lambda: red.lay(5, 24))
    red.tick()
    assert not red.flying and not red.queue
    pl.when(v.rank == 0)(lambda: red.lay(0, 5))
    red.settle()
    for swap in (v.swap_count, v.back_context, v.back_motion, v.back_state, v.swap_loss):
        swap.sent()
    for halo in (v.halo_corr, v.halo_flow, v.halo_final, v.halo_mask, v.halo_dg, v.halo_mg, v.halo_gf):
        halo.sent()
    v.store_gnet.wait()
    v.store_gctx.wait()
    pltpu.make_async_copy(v.mask_low, v.out_mask.at[0], v.osem.at[3]).wait()


def main_call(space, count, gathered, net, context, corr, flow, target, valid, grad_net, grad_mask):
    total = 3 * count // (LANES * 16) * 16 + BLOCK
    low, wide = jnp.bfloat16, jnp.float32
    peers = (space, BATCH, ROWS * COLS, LANES)
    ins = dict(
        gathered=gathered, net=net, context=context, corr=corr, flow=flow, target=target, valid=valid,
        grad_net=grad_net, grad_mask=grad_mask,
    )
    outs = dict(
        out_net=((BATCH, AREA, 128), low),
        out_flow=((BATCH, 8, SPAN), wide),
        out_mask=((BATCH, AREA, MASK), low),
        out_loss=((8, 128), wide),
        out_flat=((total, 128), low),
        out_gnet=((BATCH, AREA, 128), wide),
        out_gctx=((BATCH, AREA, 128), wide),
        out_gcorr=((BATCH, ROWS, CORR, 128), wide),
        out_gflow=((BATCH, 16, 128), wide),
        out_keep_c=((BATCH, 1152, 768), low),
        out_keep_f=((BATCH, 1152, 384), low),
        out_grads=((BLOCK, 128), wide),
    )
    scratch = dict(
        stage=((2, 3904, 128), low),
        seam=((16, 16, 128), wide),
        mask_low=((AREA, MASK), low),
        gout=((2, 256, 128), wide),
        seam_low=((16 * 20, 128), low),
        own=((2, SHARE // 2, 128), low),
        rcore=((2, SHARE // 2, 128), low),
        tx=((2, SHARE // 4, 128), low),
        rx=((2, SHARE // 4, 128), low),
        ks=((2, SHARE // 4, 128), wide),
        ts=((2, SHARE // 4, 128), low),
        acc=((2, SHARE // 4 // space, 128), wide),
        rs=((2, space, SHARE // 4 // space, 128), low),
        fin=((2, SHARE // 4 // space, 128), low),
        gath=((2 * SHARE + 32, 128), low),
        bown=((32, 128), wide), bcore=((32, 128), wide), btwo=((32, 128), wide), bacross=((32, 128), wide),
        bfour=((32, 128), wide), ball=((space, 32, 128), wide), bsum=((32, 128), wide),
        flat=((3904, 128), wide),
        pair_a=((256, 128), wide),
        pair_b=((256, 128), wide),
        flow_tmp=((112, 128), wide),
        mm_tmp=((3 * (2 * EDGE + SPREAD), 128), wide),
        fo_tmp=((32, 128), wide),
        fo_tmp2=((32, 128), wide),
        w_ci=((CORR, 256), low),
        w_cm=((2304, 256), low),
        w_fi=((112, 128), low),
        w_fm=((1152, 128), low),
        w_mm=((2304, 128), low),
        w_ri=((1280, 384), low),
        w_rs=((640, 384), low),
        w_li=((1280, 384), low),
        w_ls=((640, 384), low),
        w_h=((1152, 512), low),
        w_fo=((32, 256), low),
        w_mo=((256, 640), low),
        bias=((BIAS_ROWS, 128), wide),
        gbias=((BIAS_ROWS, 128), wide),
        corr_up=((BATCH, 2, CORR, 128), low),
        corr_down=((BATCH, 2, CORR, 128), low),
        flow_up=((BATCH, 16, 128), wide),
        flow_down=((BATCH, 16, 128), wide),
        fs=((7, 32, 128), wide),
        xt=((BATCH, 112, 1152), low),
        tmp=((1168, 128), wide),
        tmp2=((32, 128), wide),
        hx_c=((BATCH, 1152, 768), low),
        hx_f=((BATCH, 1152, 384), low),
        hx_j=((BATCH, 896, 768), low),
        slope_ci=((BATCH, AREA, 256), low),
        slope_fi=((BATCH, AREA, 128), low),
        slope_j=((BATCH, 896, 256), low),
        slope_m=((BATCH, AREA, 128), low),
        motion=((BATCH, AREA, 128), wide),
        state=((BATCH, AREA, 128), wide),
        xi=((BATCH * AREA, 1280), low),
        xs=((BATCH * AREA, 640), low),
        xr=((BATCH * AREA, 640), low),
        ru=((BATCH, AREA, 128), wide),
        rr=((BATCH, AREA, 128), wide),
        rc=((BATCH, AREA, 128), wide),
        lr=((BATCH, AREA, 128), wide),
        a_state=(peers, low), a_context=(peers, low), a_motion=(peers, low),
        b_state=(peers, low), b_context=(peers, low), b_motion=(peers, low),
        xc=((BATCH, AREA + 64, 384), low),
        xcr=((BATCH, AREA + 64, 128), low),
        gc=((BATCH, AREA + 64, 384), low),
        final=((AREA, 128), wide),
        e_left=((BATCH, 2, 48, 128), low), e_right=((BATCH, 2, 48, 128), low),
        f_left=((BATCH, 2, 48, 128), low), f_right=((BATCH, 2, 48, 128), low),
        m_left=((BATCH, 2, 48, 128), low), m_right=((BATCH, 2, 48, 128), low),
        n_left=((BATCH, 2, 48, 128), low), n_right=((BATCH, 2, 48, 128), low),
        slope_h=((BATCH, SPREAD, 512), low),
        feat=((BATCH, SPAN, 256), low),
        mf=((BATCH, AREA, 256), low),
        zt=((32, SPAN), wide),
        dg=((BATCH, 8, SPAN), wide),
        dg_left=((BATCH, 8, SPAN), wide), dg_right=((BATCH, 8, SPAN), wide),
        dt=((32, SPAN), wide),
        dto=((32, SPAN), wide),
        dtb=((BATCH, 32, SPAN), low),
        hgo=((BATCH, SPREAD, 512), low),
        gr=((BATCH, AREA, 384), low),
        mge=((BATCH, 1152, 128), low),
        cpg=((BATCH, AREA, 256), low),
        fpg=((BATCH, AREA, 128), low),
        gf_base=((BATCH, 8, AREA), wide),
        gf=((BATCH, 32, 128), wide), gf_up=((BATCH, 32, 128), wide), gf_down=((BATCH, 32, 128), wide),
        count_out=((8, 128), wide), counts=((space, 8, 128), wide),
        losses=((8, 128), wide), loss_in=((space, 8, 128), wide),
    )
    sems = dict(
        hsend=pltpu.SemaphoreType.DMA((7, 2)), hrecv=pltpu.SemaphoreType.DMA((7, 2)),
        asend=pltpu.SemaphoreType.DMA((9, space)), arecv=pltpu.SemaphoreType.DMA((9, space)),
        ssem=pltpu.SemaphoreType.DMA((2, 2)),
        fsem=pltpu.SemaphoreType.DMA((17,)),
        rsend=pltpu.SemaphoreType.DMA((2, 2)), rrecv=pltpu.SemaphoreType.DMA((2, 2)),
        rlocal=pltpu.SemaphoreType.DMA((2,)),
        s2send=pltpu.SemaphoreType.DMA((2, space)), s2recv=pltpu.SemaphoreType.DMA((2, space)),
        fsend=pltpu.SemaphoreType.DMA((2, space // 2)), frecv=pltpu.SemaphoreType.DMA((9, 4, space // 2)),
        ysend=pltpu.SemaphoreType.DMA((9, 4)), yrecv=pltpu.SemaphoreType.DMA((9, 4)),
        bsend=pltpu.SemaphoreType.DMA((2,)), brecv=pltpu.SemaphoreType.DMA((2,)),
        ksem=pltpu.SemaphoreType.DMA((2,)),
        gsem=pltpu.SemaphoreType.DMA((ROWS,)),
        osem=pltpu.SemaphoreType.DMA((6,)),
    )
    vmem = pl.BlockSpec(memory_space=pltpu.VMEM)
    hbm = pl.BlockSpec(memory_space=pl.ANY)
    names = list(ins) + list(outs) + list(scratch) + list(sems)
    return pl.pallas_call(
        functools.partial(main_kernel, names, space, count),
        out_shape=[jax.ShapeDtypeStruct(*entry) for entry in outs.values()],
        in_specs=[hbm if name == "gathered" else vmem for name in ins],
        out_specs=[hbm if name in ("out_flat", "out_gnet", "out_gctx", "out_gcorr", "out_keep_c", "out_keep_f", "out_mask", "out_grads") else vmem for name in outs],
        scratch_shapes=[pltpu.VMEM(*entry) for entry in scratch.values()] + list(sems.values()),
        compiler_params=pltpu.CompilerParams(
            collective_id=2, has_side_effects=True, vmem_limit_bytes=VMEM_LIMIT
        ),
    )(*ins.values())


VMEM_LIMIT = 64 * 2**20 - 2**17


def shards_wide(net, context, corr, flow, target, valid, grad_net, grad_mask, params):
    space = lax.axis_size(SPACE)
    count = params.shape[0]
    gathered = gather_blocks(params).reshape(4 * BLOCK, LANES)
    flow_rows = jnp.transpose(flow.astype(jnp.float32), (0, 2, 1, 3)).reshape(BATCH, 2 * ROWS, WIDE)
    flow_rows = jnp.pad(flow_rows, ((0, 0), (0, 16 - 2 * ROWS), (0, 0)))
    pad = ((0, 0), (0, 0), (0, 0), (2, 2))
    target_ext = jnp.pad(target, pad).reshape(BATCH, 2, SPREAD)
    target_ext = jnp.pad(target_ext, ((0, 0), (0, 6), (0, SPAN - SPREAD)))
    valid_ext = jnp.pad(valid.astype(jnp.float32)[:, None], pad).reshape(BATCH, 1, SPREAD)
    valid_ext = jnp.broadcast_to(jnp.pad(valid_ext, ((0, 0), (0, 0), (0, SPAN - SPREAD))), (BATCH, 8, SPAN))
    outs = main_call(
        space, count, gathered, net.reshape(BATCH, AREA, HID), context.reshape(BATCH, AREA, CTX),
        jnp.transpose(corr, (0, 1, 3, 2)), flow_rows, target_ext, valid_ext,
        grad_net.reshape(BATCH, AREA, HID), grad_mask.reshape(BATCH, AREA, MASK),
    )
    new_net, new_flow, mask, loss, _, gnet, gctx, gcorr, gflow = outs[:9]
    new_flow = new_flow[:, 0:2, 0:SPREAD].reshape(BATCH, 2, TALL, PITCH)[..., 2 : 2 + COLS]
    grads = outs[-1].reshape(-1)[:count]
    return (
        new_net.reshape(BATCH, TALL, COLS, HID),
        new_flow,
        mask.reshape(BATCH, TALL, COLS, MASK),
        loss[0:BATCH, 0],
        grads,
        gnet.reshape(BATCH, ROWS, WIDE, HID),
        gctx.reshape(BATCH, ROWS, WIDE, CTX),
        jnp.transpose(gcorr, (0, 1, 3, 2)),
        jnp.transpose(gflow[:, 0 : 2 * ROWS].reshape(BATCH, ROWS, 2, WIDE), (0, 2, 1, 3)),
    )


def solution(mesh):
    def plan(*arrays):
        net, valid = arrays[0], arrays[5]
        if (net.shape[1:3], valid.shape[1:]) == ((ROWS, WIDE), (TALL, COLS)):
            return shards_wide(*arrays)
        return shards(*arrays)

    return jax.shard_map(
        plan,
        mesh=mesh,
        in_specs=(
            P(DP, SPACE, None, None),
            P(DP, SPACE, None, None),
            P(DP, SPACE, None, None),
            P(DP, None, SPACE, None),
            P(DP, None, None, SPACE),
            P(DP, None, SPACE),
            P(DP, None, SPACE, None),
            P(DP, None, SPACE, None),
            P(DP),
        ),
        out_specs=(
            P(DP, None, SPACE, None),
            P(DP, None, None, SPACE),
            P(DP, None, SPACE, None),
            P(DP),
            P(DP),
            P(DP, SPACE, None, None),
            P(DP, SPACE, None, None),
            P(DP, SPACE, None, None),
            P(DP, None, SPACE, None),
        ),
        check_vma=False,
    )
```

```python
import functools

import jax
import jax.numpy as jnp
from jax import lax
from jax.experimental import pallas as pl
from jax.experimental.pallas import tpu as pltpu
from jax.sharding import PartitionSpec as P

HID = 128
CTX = 128
MOT = 128
CORR = 324
SPACE = "space"
DP = "dp"
(
    CORR_IN,
    CORR_MIX,
    FLOW_IN,
    FLOW_MIX,
    MOTION_MIX,
    ROWS_GATES,
    ROWS_CANDIDATE,
    COLUMNS_GATES,
    COLUMNS_CANDIDATE,
    FLOW_HIDDEN,
    FLOW_OUT,
    MASK_HIDDEN,
    MASK_OUT,
) = range(13)
C1 = 256
C2 = 192
F1 = 128
F2 = 64
HEAD = 256
MASK = 576


def with_halo(block, sides, width):
    for axis, dim in sides:
        count = lax.axis_size(axis)
        forward = [(i, i + 1) for i in range(count - 1)]
        backward = [(target, source) for source, target in forward]
        low = lax.ppermute(
            lax.slice_in_dim(block, block.shape[dim] - width, None, axis=dim), axis, forward
        )
        high = lax.ppermute(lax.slice_in_dim(block, 0, width, axis=dim), axis, backward)
        block = jnp.concatenate([low, block, high], axis=dim)
    return block


def shapes():
    inputs_width = HID + CTX + MOT
    return [
        (CORR_IN, CORR, C1),
        (CORR_MIX, 9 * C1, C2),
        (FLOW_IN, 98, F1),
        (FLOW_MIX, 9 * F1, F2),
        (MOTION_MIX, 9 * (C2 + F2), MOT - 2),
        (ROWS_GATES, 5 * inputs_width, 2 * HID),
        (ROWS_CANDIDATE, 5 * inputs_width, HID),
        (COLUMNS_GATES, 5 * inputs_width, 2 * HID),
        (COLUMNS_CANDIDATE, 5 * inputs_width, HID),
        (FLOW_HIDDEN, 9 * HID, HEAD),
        (FLOW_OUT, 9 * HEAD, 2),
        (MASK_HIDDEN, 9 * HID, HEAD),
        (MASK_OUT, HEAD, MASK),
    ]


def unpack(flat):
    weights = {}
    biases = {}
    offset = 0
    table = shapes()
    for name, height, width in table:
        weights[name] = flat[offset // LANES : (offset + height * width) // LANES].reshape(height, width)
        offset = offset + height * width
    rest = flat[offset // LANES :].reshape(-1)
    offset = 0
    for name, height, width in table:
        biases[name] = rest[offset : offset + width].astype(jnp.float32)
        offset = offset + width
    return (weights, biases)


def pack(grads, total):
    table = shapes()
    rows = [grads[entry[0]][0].astype(jnp.bfloat16).reshape(-1, LANES) for entry in table]
    biases = jnp.concatenate([grads[entry[0]][1] for entry in table]).astype(jnp.bfloat16)
    left = total * LANES - sum(entry[1] * entry[2] for entry in table) - biases.shape[0]
    return jnp.concatenate(rows + [jnp.pad(biases, (0, left)).reshape(-1, LANES)])


def patches(padded, tall, wide):
    out_rows = padded.shape[1] - tall + 1
    out_columns = padded.shape[2] - wide + 1
    return jnp.concatenate(
        [
            padded[:, down : down + out_rows, across : across + out_columns]
            for down in range(tall)
            for across in range(wide)
        ],
        axis=-1,
    )


def apply(stacked, weight):
    return jnp.einsum("bhwk,ko->bhwo", stacked, weight, preferred_element_type=jnp.float32)


def apply_back(grad, weight):
    return jnp.einsum("bhwo,ko->bhwk", grad, weight, preferred_element_type=jnp.float32)


def weight_grad(stacked, pre_grad):
    return jnp.einsum("bhwk,bhwo->ko", stacked, pre_grad, preferred_element_type=jnp.float32)


def record(grads, name, stacked, pre_grad):
    grads[name] = (
        weight_grad(stacked, pre_grad),
        jnp.sum(pre_grad, axis=(0, 1, 2), dtype=jnp.float32),
    )


def flipped(weight, tall, wide):
    inner = weight.shape[0] // (tall * wide)
    shaped = weight.reshape(tall, wide, inner, weight.shape[1])[::-1, ::-1]
    return jnp.transpose(shaped, (0, 1, 3, 2)).reshape(-1, inner)


def slope(pre):
    sigma = jax.nn.sigmoid(pre)
    return sigma * (1.0 + pre * (1.0 - sigma))


def local_pad(field, tall, wide):
    return jnp.pad(field, ((0, 0), (tall // 2, tall // 2), (wide // 2, wide // 2), (0, 0)))


def row_pad(field, tall):
    field = with_halo(field, ((SPACE, 1),), tall // 2)
    return jnp.pad(field, ((0, 0), (0, 0), (tall // 2, tall // 2), (0, 0)))


def column_pad(field, tall, wide):
    field = with_halo(field, ((SPACE, 2),), wide // 2)
    return jnp.pad(field, ((0, 0), (tall // 2, tall // 2), (0, 0), (0, 0)))


MESH = pl.DeviceIdType.MESH
LANES = 128
BLOCK = 6144


def quarter_start(rank, count):
    return lax.div(rank * count, LANES)


def quarter_base(rank, count):
    return lax.div(rank * count, LANES * 16) * 16


def mate_of(rank):
    return rank + 1 - 2 * lax.rem(rank, 2)


def remote(src, dst, send, recv, device):
    return pltpu.make_async_remote_copy(
        src_ref=src, dst_ref=dst, send_sem=send, recv_sem=recv, device_id=device, device_id_type=MESH
    )


def greet(devices):
    barrier = pltpu.get_barrier_semaphore()
    for device in devices:
        pl.semaphore_signal(barrier, inc=1, device_id=device, device_id_type=MESH)
    pl.semaphore_wait(barrier, len(devices))


def lane_matrix(shift, forward):
    source = lax.broadcasted_iota(jnp.int32, (LANES, 2 * LANES), 0)
    target = lax.broadcasted_iota(jnp.int32, (LANES, 2 * LANES), 1)
    if forward:
        return jnp.where(target == source + shift, 1.0, 0.0).astype(jnp.bfloat16)
    return jnp.where(lax.rem(target + LANES, 2 * LANES) == source - shift + LANES, 1.0, 0.0).astype(jnp.bfloat16)


def gather_kernel(count, local_ref, out_ref, own_ref, send, recv):
    rank, spot = lax.axis_index(DP), lax.axis_index(SPACE)
    mate, across, twin = mate_of(rank), lax.rem(rank + 2, 4), mate_of(spot)
    pieces = 4
    rows = BLOCK // 2 // pieces
    peers = ({DP: mate}, {DP: across}, {SPACE: twin})
    greet(peers)
    matrix = lane_matrix(lax.rem(rank * count, LANES), True)
    first = lax.broadcasted_iota(jnp.int32, (256, LANES), 0) == 0

    def rotate(step, carry):
        at = pl.ds(pl.multiple_of(step * 256, 256), 256)
        both = jnp.dot(local_ref[at, :], matrix, preferred_element_type=jnp.float32)
        spill = pltpu.roll(both[:, LANES:], 1, 0)
        own_ref[at, :] = (both[:, :LANES] + jnp.where(first, carry, spill)).astype(jnp.bfloat16)
        return spill[0:1]

    lax.fori_loop(0, BLOCK // 256, rotate, jnp.zeros((1, LANES), jnp.float32))

    half, other_half = lax.rem(spot, 2), lax.rem(spot + 1, 2)

    def piece(which, index):
        return pl.ds(pl.multiple_of(which * (BLOCK // 2) + index * rows, 16), rows)

    own_x = [
        remote(own_ref.at[piece(half, k)], out_ref.at[rank, piece(half, k)], send.at[0, k], recv.at[0, k], peers[1])
        for k in range(pieces)
    ]
    own_c = remote(own_ref, out_ref.at[rank], send.at[4, 0], recv.at[4, 0], peers[0])
    for copy in own_x:
        copy.start()
    own_c.start()
    later = []
    for k in range(pieces):
        own_x[k].wait_recv()
        block = out_ref.at[across, piece(half, k)]
        to_twin = remote(block, block, send.at[1, k], recv.at[1, k], peers[2])
        to_mate = remote(block, block, send.at[2, k], recv.at[2, k], peers[0])
        to_twin.start()
        to_mate.start()
        later.append((to_twin, to_mate))
    for at in range(BLOCK // 256):
        out_ref[rank, at * 256 : (at + 1) * 256, :] = own_ref[at * 256 : (at + 1) * 256, :]
    for k in range(pieces):
        later[k][0].wait_recv()
        block = out_ref.at[across, piece(other_half, k)]
        to_mate = remote(block, block, send.at[3, k], recv.at[3, k], peers[0])
        to_mate.start()
        later.append((to_mate,))
    for k in range(pieces):
        own_x[k].wait_send()
        later[k][0].wait_send()
        later[k][1].wait()
        later[pieces + k][0].wait()
    own_c.wait()


def gather_blocks(params):
    count = params.shape[0]
    local = jnp.pad(params, (0, BLOCK * LANES - count)).reshape(BLOCK, LANES)
    return pl.pallas_call(
        functools.partial(gather_kernel, count),
        out_shape=jax.ShapeDtypeStruct((4, BLOCK, LANES), jnp.bfloat16),
        in_specs=[pl.BlockSpec(memory_space=pltpu.VMEM)],
        out_specs=pl.BlockSpec(memory_space=pltpu.VMEM),
        scratch_shapes=[
            pltpu.VMEM((BLOCK, LANES), jnp.bfloat16),
            pltpu.SemaphoreType.DMA((5, 4)),
            pltpu.SemaphoreType.DMA((5, 4)),
        ],
        compiler_params=pltpu.CompilerParams(
            collective_id=0, has_side_effects=True, vmem_limit_bytes=32 * 2**20
        ),
    )(local)


def gather_params(params):
    count = params.shape[0]
    blocks = gather_blocks(params)
    pieces = []
    reach = 0
    for rank in range(4):
        start = rank * count // LANES
        stop = -(-(rank + 1) * count // LANES)
        head = blocks[rank, :1] if rank == 0 else blocks[rank, :1] + pieces.pop()
        pieces += [head, blocks[rank, 1 : stop - start - 1], blocks[rank, stop - start - 1 : stop - start]]
    return jnp.concatenate(pieces)


def reduce_kernel(count, space, pieces, grads_ref, out_ref, rc, tx, rx, acc, ty, ry, tz, rz, gath, send, recv, zsend, zrecv):
    rank, spot = lax.axis_index(DP), lax.axis_index(SPACE)
    mate, across, twin = mate_of(rank), lax.rem(rank + 2, 4), mate_of(spot)
    group = space // 2
    side, depth = lax.rem(spot, 2), lax.div(spot, 2)
    rows = BLOCK // pieces
    half = rows // 2
    part = half // group

    def partner(step):
        return lax.rem(depth + step, group)

    peers = [{DP: mate}, {DP: across}, {SPACE: twin}]
    barrier = pltpu.get_barrier_semaphore()
    for device in peers:
        pl.semaphore_signal(barrier, inc=1, device_id=device, device_id_type=MESH)

    def hello(step, carry):
        pl.semaphore_signal(barrier, inc=1, device_id={SPACE: partner(step) * 2 + side}, device_id_type=MESH)
        return carry

    lax.fori_loop(1, group, hello, 0)
    pl.semaphore_wait(barrier, 3 + group - 1)

    gath[BLOCK:, :] = jnp.zeros((32, LANES), jnp.bfloat16)
    lower = lax.rem(rank, 2)
    upper = lax.div(rank, 2)

    def base(who):
        return pl.multiple_of(quarter_base(who, count), 16)

    def rows_of(start, index, length):
        return pl.ds(pl.multiple_of(start + index, 16), length)

    core = []
    for p in range(pieces):
        for high in range(2):
            copy = remote(
                grads_ref.at[rows_of(base(2 * high + 1 - lower), p * rows, rows)],
                rc.at[p, high],
                send.at[high, p],
                recv.at[high, p],
                peers[0],
            )
            copy.start()
            core.append(copy)
    step_rows = 192 if half % 192 == 0 else 16
    xs, ys, gs = [], [], []

    def z_copy(p, step):
        to = partner(step)
        return remote(
            tz.at[p, pl.ds(pl.multiple_of(to * part, 16), part)],
            rz.at[p, pl.ds(pl.multiple_of(depth * part, 16), part)],
            zsend.at[0, p, step],
            zrecv.at[0, p, step],
            {SPACE: to * 2 + side},
        )

    def home(p, which, slot):
        return pl.ds(pl.multiple_of(p * rows + which * half + slot * part, 16), part)

    def g_copy(p, step):
        block = gath.at[home(p, side, depth)]
        return remote(block, block, zsend.at[1, p, step], zrecv.at[1, p, step], {SPACE: partner(step) * 2 + side})

    def each(body):
        def run(step, carry):
            body(step)
            return carry

        lax.fori_loop(1, group, run, 0)

    def stage_core(p):
        core[2 * p].wait_recv()
        core[2 * p + 1].wait_recv()
        far = 1 - upper

        def add(step, carry):
            at = pl.multiple_of(step * step_rows, 16)
            mine = grads_ref[rows_of(base(2 * far + lower), p * rows + at, step_rows), :].astype(jnp.float32)
            tx[p, pl.ds(at, step_rows), :] = (
                mine + rc[p, far, pl.ds(at, step_rows), :].astype(jnp.float32)
            ).astype(jnp.bfloat16)
            return carry

        lax.fori_loop(0, rows // step_rows, add, 0)
        copy = remote(tx.at[p], rx.at[p], send.at[2, p], recv.at[2, p], peers[1])
        copy.start()
        xs.append(copy)

    def stage_x(p):
        xs[p].wait_recv()

        def total(at):
            return (
                grads_ref[rows_of(base(rank), p * rows + at, step_rows), :].astype(jnp.float32)
                + rc[p, upper, pl.ds(at, step_rows), :].astype(jnp.float32)
                + rx[p, pl.ds(at, step_rows), :].astype(jnp.float32)
            )

        def add(step, carry):
            at = pl.multiple_of(step * step_rows, 16)
            far = pl.multiple_of((1 - side) * half + at, 16)
            near = pl.multiple_of(side * half + at, 16)
            ty[p, pl.ds(at, step_rows), :] = total(far).astype(jnp.bfloat16)
            acc[p, pl.ds(at, step_rows), :] = total(near)
            return carry

        lax.fori_loop(0, half // step_rows, add, 0)
        copy = remote(ty.at[p], ry.at[p], send.at[3, p], recv.at[3, p], peers[2])
        copy.start()
        ys.append(copy)

    def stage_y(p):
        ys[p].wait_recv()

        def add(step, carry):
            at = pl.ds(pl.multiple_of(step * step_rows, 16), step_rows)
            value = acc[p, at, :] + ry[p, at, :].astype(jnp.float32)
            acc[p, at, :] = value
            tz[p, at, :] = value.astype(jnp.bfloat16)
            return carry

        lax.fori_loop(0, half // step_rows, add, 0)
        each(lambda step: z_copy(p, step).start())

    def stage_z(p):
        each(lambda step: z_copy(p, step).wait_recv())
        value = acc[p, pl.ds(pl.multiple_of(depth * part, 16), part), :]

        def add(step, value):
            other = lax.rem(depth + group - step, group)
            return value + rz[p, pl.ds(pl.multiple_of(other * part, 16), part), :].astype(jnp.float32)

        value = lax.fori_loop(1, group, add, value)
        gath[home(p, side, depth), :] = value.astype(jnp.bfloat16)
        each(lambda step: g_copy(p, step).start())

    def stage_zg(p):
        each(lambda step: g_copy(p, step).wait_recv())
        block = gath.at[pl.ds(pl.multiple_of(p * rows + side * half, 16), half)]
        copy = remote(block, block, send.at[4, p], recv.at[4, p], peers[2])
        copy.start()
        gs.append(copy)

    def stage_yg(p):
        gs[p].wait_recv()

    stages = [stage_core, stage_x, stage_y, stage_z, stage_zg, stage_yg]
    for tick in range(pieces + len(stages) - 1):
        for number in reversed(range(len(stages))):
            if 0 <= tick - number < pieces:
                stages[number](tick - number)

    for copy in core + xs + ys + gs:
        copy.wait_send()
    for p in range(pieces):

        def done(step):
            z_copy(p, step).wait_send()
            g_copy(p, step).wait_send()

        each(done)

    offset = rank * count - quarter_base(rank, count) * LANES
    skip = lax.div(offset, LANES)
    matrix = lane_matrix(lax.rem(offset, LANES), False)
    wide = jnp.where(
        lax.broadcasted_iota(jnp.int32, (256, 288), 1)
        == lax.broadcasted_iota(jnp.int32, (256, 288), 0) + skip,
        1.0,
        0.0,
    ).astype(jnp.bfloat16)
    wide_next = jnp.where(
        lax.broadcasted_iota(jnp.int32, (256, 288), 1)
        == lax.broadcasted_iota(jnp.int32, (256, 288), 0) + skip + 1,
        1.0,
        0.0,
    ).astype(jnp.bfloat16)

    def place(step, carry):
        at = pl.multiple_of(step * 256, 256)
        block = gath[pl.ds(at, 288), :]
        both = jnp.dot(block, matrix, preferred_element_type=jnp.float32).astype(jnp.bfloat16)
        out_ref[pl.ds(at, 256), :] = jnp.dot(wide, both[:, :LANES], preferred_element_type=jnp.float32) + jnp.dot(
            wide_next, both[:, LANES:], preferred_element_type=jnp.float32
        )
        return carry

    lax.fori_loop(0, BLOCK // 256, place, 0)


def reduce_grads(flat, space, count):
    pieces = next(k for k in (4, 2, 1) if BLOCK // (k * space) % 16 == 0)
    rows = BLOCK // pieces
    half = rows // 2
    out = pl.pallas_call(
        functools.partial(reduce_kernel, count, space, pieces),
        out_shape=jax.ShapeDtypeStruct((BLOCK, LANES), jnp.float32),
        in_specs=[pl.BlockSpec(memory_space=pltpu.VMEM)],
        out_specs=pl.BlockSpec(memory_space=pltpu.VMEM),
        scratch_shapes=[
            pltpu.VMEM((pieces, 2, rows, LANES), jnp.bfloat16),
            pltpu.VMEM((pieces, rows, LANES), jnp.bfloat16),
            pltpu.VMEM((pieces, rows, LANES), jnp.bfloat16),
            pltpu.VMEM((pieces, half, LANES), jnp.float32),
            pltpu.VMEM((pieces, half, LANES), jnp.bfloat16),
            pltpu.VMEM((pieces, half, LANES), jnp.bfloat16),
            pltpu.VMEM((pieces, half, LANES), jnp.bfloat16),
            pltpu.VMEM((pieces, half, LANES), jnp.bfloat16),
            pltpu.VMEM((BLOCK + 32, LANES), jnp.bfloat16),
            pltpu.SemaphoreType.DMA((5, pieces)),
            pltpu.SemaphoreType.DMA((5, pieces)),
            pltpu.SemaphoreType.DMA((2, pieces, space // 2)),
            pltpu.SemaphoreType.DMA((2, pieces, space // 2)),
        ],
        compiler_params=pltpu.CompilerParams(
            collective_id=1, has_side_effects=True, vmem_limit_bytes=48 * 2**20
        ),
    )(flat)
    return out.reshape(-1)[:count]


def gru_forward(state, inputs, weights, biases, gate_name, candidate_name, tall, wide, padder):
    joined_stack = patches(padder(jnp.concatenate([state, inputs], -1), tall, wide), tall, wide)
    gates = jax.nn.sigmoid(apply(joined_stack, weights[gate_name]) + biases[gate_name])
    hidden = state.shape[-1]
    update = gates[..., :hidden]
    reset = gates[..., hidden:]
    state_wide = state.astype(jnp.float32)
    mixed = jnp.concatenate([(reset * state_wide).astype(jnp.bfloat16), inputs], -1)
    mixed_stack = patches(padder(mixed, tall, wide), tall, wide)
    candidate = jnp.tanh(apply(mixed_stack, weights[candidate_name]) + biases[candidate_name])
    result = state_wide + update * (candidate - state_wide)
    return (result, (joined_stack, mixed_stack, update, reset, candidate, state_wide))


def gru_backward(result_grad, kept, weights, grads, gate_name, candidate_name, tall, wide, padder):
    joined_stack, mixed_stack, update, reset, candidate, state_wide = kept
    hidden = update.shape[-1]
    candidate_grad = (result_grad * update * (1.0 - candidate * candidate)).astype(jnp.bfloat16)
    record(grads, candidate_name, mixed_stack, candidate_grad)
    mixed_grad = apply(
        patches(padder(candidate_grad, tall, wide), tall, wide),
        flipped(weights[candidate_name], tall, wide),
    )
    reset_grad = mixed_grad[..., :hidden]
    gate_grad = jnp.concatenate(
        [
            result_grad * (candidate - state_wide) * update * (1.0 - update),
            reset_grad * state_wide * reset * (1.0 - reset),
        ],
        -1,
    ).astype(jnp.bfloat16)
    record(grads, gate_name, joined_stack, gate_grad)
    joined_grad = apply(
        patches(padder(gate_grad, tall, wide), tall, wide), flipped(weights[gate_name], tall, wide)
    )
    state_grad = result_grad * (1.0 - update) + reset_grad * reset + joined_grad[..., :hidden]
    inputs_grad = joined_grad[..., hidden:] + mixed_grad[..., hidden:]
    return (state_grad, inputs_grad)


def shards(net, context, corr, flow, target, valid, grad_net, grad_mask, params):
    flow_start = CTX + MOT - 2
    plane = jnp.float32(target.shape[2] * net.shape[2])
    counts = lax.psum(jnp.sum(valid, axis=(1, 2)).astype(jnp.float32), SPACE)
    divisor = jnp.maximum(counts, 1.0)
    weights, biases = unpack(gather_params(params))
    grads = {}
    flow_rows = jnp.transpose(flow, (0, 2, 3, 1))
    corr_pre = apply(corr, weights[CORR_IN]) + biases[CORR_IN]
    corr_one = jax.nn.silu(corr_pre).astype(jnp.bfloat16)
    corr_stack = patches(row_pad(corr_one, 3), 3, 3)
    corr_mix_pre = apply(corr_stack, weights[CORR_MIX]) + biases[CORR_MIX]
    corr_two = jax.nn.silu(corr_mix_pre).astype(jnp.bfloat16)
    flow_stack = patches(row_pad(flow_rows, 7), 7, 7)
    flow_pre = apply(flow_stack, weights[FLOW_IN]) + biases[FLOW_IN]
    flow_one = jax.nn.silu(flow_pre).astype(jnp.bfloat16)
    flow_mix_stack = patches(row_pad(flow_one, 3), 3, 3)
    flow_mix_pre = apply(flow_mix_stack, weights[FLOW_MIX]) + biases[FLOW_MIX]
    flow_two = jax.nn.silu(flow_mix_pre).astype(jnp.bfloat16)
    joint_stack = patches(row_pad(jnp.concatenate([corr_two, flow_two], -1), 3), 3, 3)
    motion_pre = apply(joint_stack, weights[MOTION_MIX]) + biases[MOTION_MIX]
    motion = jax.nn.silu(motion_pre).astype(jnp.bfloat16)
    inputs = jnp.concatenate([context, motion, flow_rows], -1)
    state, rows_kept = gru_forward(
        net, inputs, weights, biases, ROWS_GATES, ROWS_CANDIDATE, 1, 5, local_pad
    )
    state_columns, inputs_columns = (
        lax.all_to_all(
            state.astype(jnp.bfloat16), SPACE, split_axis=2, concat_axis=1, tiled=True
        ),
        lax.all_to_all(inputs, SPACE, split_axis=2, concat_axis=1, tiled=True),
    )
    target_here = jnp.transpose(target, (0, 2, 3, 1))
    valid_here = valid.astype(jnp.float32)
    net_cotangent = grad_net
    mask_cotangent = grad_mask
    final, columns_kept = gru_forward(
        state_columns,
        inputs_columns,
        weights,
        biases,
        COLUMNS_GATES,
        COLUMNS_CANDIDATE,
        5,
        1,
        local_pad,
    )
    final_low = final.astype(jnp.bfloat16)
    heads_weight = jnp.concatenate([weights[FLOW_HIDDEN], weights[MASK_HIDDEN]], 1)
    heads_bias = jnp.concatenate([biases[FLOW_HIDDEN], biases[MASK_HIDDEN]])
    net_stack = patches(column_pad(final_low, 3, 3), 3, 3)
    heads_pre = apply(net_stack, heads_weight) + heads_bias
    heads_act = jax.nn.silu(heads_pre).astype(jnp.bfloat16)
    flow_features = heads_act[..., :HEAD]
    mask_features = heads_act[..., HEAD:]
    hidden_stack = patches(column_pad(flow_features, 3, 3), 3, 3)
    delta = apply(hidden_stack, weights[FLOW_OUT]) + biases[FLOW_OUT]
    mask_full = 0.25 * (apply(mask_features, weights[MASK_OUT]) + biases[MASK_OUT])
    new_flow = inputs_columns[..., flow_start:].astype(jnp.float32) + delta
    error = new_flow - target_here
    root = jnp.sqrt(error * error + 1.0)
    partials = jnp.sum(valid_here * jnp.sum(root, axis=-1), axis=(1, 2))
    flow_grad = plane / divisor[:, None, None, None] * valid_here[..., None] * error / root
    mask_low = mask_full.astype(jnp.bfloat16)
    nets_out = final_low
    flows_out = jnp.transpose(new_flow, (0, 3, 1, 2))
    masks_out = mask_low
    delta_grad = flow_grad.astype(jnp.bfloat16)
    mask_grad = (0.25 * mask_cotangent.astype(jnp.float32)).astype(jnp.bfloat16)
    record(grads, MASK_OUT, mask_features, mask_grad)
    record(grads, FLOW_OUT, hidden_stack, delta_grad)
    from_flow = apply(
        patches(column_pad(delta_grad, 3, 3), 3, 3), flipped(weights[FLOW_OUT], 3, 3)
    )
    from_mask = apply_back(mask_grad, weights[MASK_OUT])
    heads_grad = (jnp.concatenate([from_flow, from_mask], -1) * slope(heads_pre)).astype(
        jnp.bfloat16
    )
    heads_wgrad = weight_grad(net_stack, heads_grad)
    heads_bgrad = jnp.sum(heads_grad, axis=(0, 1, 2), dtype=jnp.float32)
    grads[FLOW_HIDDEN] = (heads_wgrad[:, :HEAD], heads_bgrad[:HEAD])
    grads[MASK_HIDDEN] = (heads_wgrad[:, HEAD:], heads_bgrad[HEAD:])
    final_grad = net_cotangent.astype(jnp.float32) + apply(
        patches(column_pad(heads_grad, 3, 3), 3, 3), flipped(heads_weight, 3, 3)
    )
    state_grad_columns, inputs_grad_columns = gru_backward(
        final_grad,
        columns_kept,
        weights,
        grads,
        COLUMNS_GATES,
        COLUMNS_CANDIDATE,
        5,
        1,
        local_pad,
    )
    inputs_grad_columns = jnp.concatenate(
        [
            inputs_grad_columns[..., :flow_start],
            inputs_grad_columns[..., flow_start:] + flow_grad,
        ],
        -1,
    )
    state_back, inputs_back = (
        lax.all_to_all(
            state_grad_columns.astype(jnp.bfloat16),
            SPACE,
            split_axis=1,
            concat_axis=2,
            tiled=True,
        ),
        lax.all_to_all(
            inputs_grad_columns.astype(jnp.bfloat16),
            SPACE,
            split_axis=1,
            concat_axis=2,
            tiled=True,
        ),
    )
    net_grad, inputs_grad = gru_backward(
        state_back.astype(jnp.float32),
        rows_kept,
        weights,
        grads,
        ROWS_GATES,
        ROWS_CANDIDATE,
        1,
        5,
        local_pad,
    )
    inputs_total = inputs_grad + inputs_back.astype(jnp.float32)
    motion_grad = (inputs_total[..., CTX:flow_start] * slope(motion_pre)).astype(jnp.bfloat16)
    record(grads, MOTION_MIX, joint_stack, motion_grad)
    joint_grad = apply(
        patches(row_pad(motion_grad, 3), 3, 3), flipped(weights[MOTION_MIX], 3, 3)
    )
    branch_grad = jnp.concatenate(
        [
            joint_grad[..., :C2] * slope(corr_mix_pre),
            joint_grad[..., C2:] * slope(flow_mix_pre),
        ],
        -1,
    ).astype(jnp.bfloat16)
    record(grads, CORR_MIX, corr_stack, branch_grad[..., :C2])
    record(grads, FLOW_MIX, flow_mix_stack, branch_grad[..., C2:])
    branch_pad = row_pad(branch_grad, 3)
    corr_one_grad = apply(
        patches(branch_pad[..., :C2], 3, 3), flipped(weights[CORR_MIX], 3, 3)
    )
    flow_one_grad = apply(
        patches(branch_pad[..., C2:], 3, 3), flipped(weights[FLOW_MIX], 3, 3)
    )
    corr_pre_grad = (corr_one_grad * slope(corr_pre)).astype(jnp.bfloat16)
    flow_pre_grad = (flow_one_grad * slope(flow_pre)).astype(jnp.bfloat16)
    record(grads, CORR_IN, corr, corr_pre_grad)
    record(grads, FLOW_IN, flow_stack, flow_pre_grad)
    corr_grads = apply_back(corr_pre_grad, weights[CORR_IN])
    flow_total = inputs_total[..., flow_start:] + apply(
        patches(row_pad(flow_pre_grad, 7), 7, 7), flipped(weights[FLOW_IN], 7, 7)
    )
    flow_grads = jnp.transpose(flow_total, (0, 3, 1, 2))
    net_grads = net_grad
    context_grads = inputs_total[..., :CTX]
    count = params.shape[0]
    local = pack(grads, 3 * count // (LANES * 16) * 16 + BLOCK)
    collected = reduce_grads(local, lax.axis_size(SPACE), count)
    losses = lax.psum(partials, SPACE) / divisor
    return (
        nets_out,
        flows_out,
        masks_out,
        losses,
        collected,
        net_grads,
        context_grads,
        corr_grads,
        flow_grads,
    )


BATCH = 2
ROWS = 5
WIDE = 128
TALL = 40
COLS = 16
AREA = 640
PITCH = 20
SPREAD = TALL * PITCH
SPAN = 896
EDGE = 64


def mm(a, b):
    return jnp.dot(a, b, preferred_element_type=jnp.float32)


def nt(a, b):
    return lax.dot_general(a, b, (((1,), (1,)), ((), ())), preferred_element_type=jnp.float32)


def tn(a, b):
    return lax.dot_general(a, b, (((0,), (0,)), ((), ())), preferred_element_type=jnp.float32)


def half_of(value):
    return value.astype(jnp.bfloat16)


def full_of(value):
    return value.astype(jnp.float32)


def quarter_of(value):
    return half_of(0.25 * full_of(value))


def lane_index(shape):
    return lax.broadcasted_iota(jnp.int32, shape, 1)


def row_index(shape):
    return lax.broadcasted_iota(jnp.int32, shape, 0)


def act_slope(pre):
    sigma = jax.nn.sigmoid(pre)
    act = pre * sigma
    return act, sigma + act * (1.0 - sigma)


def flat_rows():
    table = shapes()
    offset = 0
    starts = {}
    for name, height, width in table:
        starts[name] = offset // LANES
        offset += height * width
    bias_row = offset // LANES
    spots = {}
    inner = 0
    for name, height, width in table:
        spots[name] = inner
        inner += width
    return starts, bias_row, spots, inner


def cast_rows(dst, to, src, start, count, kind):
    big = 256
    whole = count // big

    if whole > 1:

        def body(step, carry):
            at = pl.multiple_of(step * big, big)
            dst[pl.ds(to + at, big), :] = src[pl.ds(start + at, big), :].astype(kind)
            return carry

        lax.fori_loop(0, whole, body, 0)
    elif whole == 1:
        dst[to : to + big, :] = src[start : start + big, :].astype(kind)
    rest = count - whole * big
    if rest:
        low = whole * big
        dst[to + low : to + count, :] = src[start + low : start + count, :].astype(kind)


MARGIN = 16


def stage_plan(count, start, rows):
    stop = start + rows
    pieces, fill = [], 0
    for rank in range(4):
        first = rank * count // LANES
        last = -(-(rank + 1) * count // LANES)
        low, high = max(start, first), min(stop, last)
        if low >= high:
            continue
        place = low - first + rank * BLOCK
        base = place // 16 * 16
        length = -(-(place - base + high - low) // 16) * 16
        to = MARGIN + low - start - (place - base)
        seam = MARGIN + low - start if start < first else None
        pieces.append((base, length, fill, to, seam))
        fill += length
    return pieces


class Stages:
    def __init__(self, v, count, segments):
        self.v, self.at = v, 0
        self.plans = [stage_plan(count, start, rows) for start, rows in segments]
        self.fetch(0)

    def copies(self, index):
        v, slot = self.v, index % 2
        return [
            pltpu.make_async_copy(
                v.out_all.at[base : base + length], v.stage.at[slot, fill : fill + length], v.ssem.at[slot, number]
            )
            for number, (base, length, fill, to, seam) in enumerate(self.plans[index])
        ]

    def fetch(self, index):
        if index < len(self.plans):
            for copy in self.copies(index):
                copy.start()

    def take(self):
        v, index = self.v, self.at
        self.at += 1
        for copy in self.copies(index):
            copy.wait()
        self.fetch(index + 1)
        for base, length, fill, to, seam in self.plans[index]:
            saved = None if seam is None else v.flat[seam : seam + 1, :]
            cast_rows(v.flat, to, v.stage.at[index % 2], fill, length, jnp.float32)
            if seam is not None:
                v.flat[seam : seam + 1, :] = v.flat[seam : seam + 1, :] + saved


def strided(ref, start, count, stride):
    if stride == 1:
        return ref[pl.ds(start, count), :]
    return ref[pl.ds(start, count, stride=stride), :]


def unpack_pairs(flat, row, count, dst, to, lane):
    dst[to : to + count, lane : lane + LANES] = half_of(strided(flat, MARGIN + 2 * row, count, 2))
    dst[to : to + count, lane + LANES : lane + 2 * LANES] = half_of(strided(flat, MARGIN + 2 * row + 1, count, 2))


def pack_pairs(flat, row, count, low, high):
    flat[pl.ds(MARGIN + 2 * row, count, stride=2), :] = low
    flat[pl.ds(MARGIN + 2 * row + 1, count, stride=2), :] = high


def split_pick(which, quarter):
    source = lax.broadcasted_iota(jnp.int32, (LANES, HEAD), 0)
    target = lax.broadcasted_iota(jnp.int32, (LANES, HEAD), 1)
    return jnp.where(source == 2 * (target - 64 * quarter) + which, 1.0, 0.0).astype(jnp.bfloat16)


UNPACK = (
    (CORR_IN, 648), (CORR_MIX, 3456), (FLOW_IN, 98), (FLOW_MIX, 576), (MOTION_MIX, 2268),
    (ROWS_GATES, 3840), (ROWS_CANDIDATE, 1920), (None, 21), (COLUMNS_GATES, 3840), (COLUMNS_CANDIDATE, 1920),
    (FLOW_HIDDEN, 2304), (MASK_HIDDEN, 2304), (FLOW_OUT, 36), (MASK_OUT, 1152),
)


def stage_of(v, name, rows):
    assert UNPACK[v.stages.at] == (name, rows)
    v.stages.take()


def unpack_gru(v, gates_name, cand_name, w_i, w_s):
    flat = v.flat
    stage_of(v, gates_name, 3840)
    for tap in range(5):
        unpack_pairs(flat, tap * 384, 128, w_s, tap * 128, 0)
        unpack_pairs(flat, tap * 384 + 128, 256, w_i, tap * 256, 0)
    stage_of(v, cand_name, 1920)
    for tap in range(5):
        w_s[tap * 128 : (tap + 1) * 128, 256:384] = half_of(strided(flat, MARGIN + tap * 384, 128, 1))
        w_i[tap * 256 : (tap + 1) * 256, 256:384] = half_of(strided(flat, MARGIN + tap * 384 + 128, 256, 1))


def unpack_encoder(v, count):
    starts, bias_row, spots, inner = flat_rows()
    flat = v.flat
    v.stages = Stages(v, count, [(bias_row if name is None else starts[name], rows) for name, rows in UNPACK])

    def stage(name, rows):
        stage_of(v, name, rows)

    stage(CORR_IN, 648)
    unpack_pairs(flat, 0, 324, v.w_ci, 0, 0)

    stage(CORR_MIX, 3456)
    lane = lane_index((128, LANES))
    low_half = lane < 64

    def mix_step(step, carry):
        at = MARGIN + 384 * step
        r0, r1, r2 = (strided(flat, at + i, 128, 3) for i in range(3))
        r1s, r2s = pltpu.roll(r1, 64, 1), pltpu.roll(r2, 64, 1)
        v.pair_a[pl.ds(0, 128, stride=2), :] = r0
        v.pair_a[pl.ds(1, 128, stride=2), :] = jnp.where(low_half, r1s, r2s)
        v.pair_b[pl.ds(0, 128, stride=2), :] = jnp.where(low_half, r1, 0.0)
        v.pair_b[pl.ds(1, 128, stride=2), :] = jnp.where(low_half, r2s, 0.0)
        to = pl.ds(pl.multiple_of(step * 256, 256), 256)
        v.w_cm[to, 0:128] = half_of(v.pair_a[...])
        v.w_cm[to, 128:256] = half_of(v.pair_b[...])
        return carry

    lax.fori_loop(0, 9, mix_step, 0)

    stage(FLOW_IN, 98)
    v.flow_tmp[...] = jnp.zeros_like(v.flow_tmp)
    for across in range(7):
        for comp in range(2):
            v.flow_tmp[pl.ds(across * 16 + comp, 7, stride=2), :] = strided(
                flat, MARGIN + across * 2 + comp, 7, 14
            )
    v.w_fi[...] = half_of(v.flow_tmp[...])

    stage(FLOW_MIX, 576)
    for step in range(9):
        r0 = strided(flat, MARGIN + 64 * step, 64, 1)
        high_half = lane_index((64, LANES)) >= 64
        v.pair_a[pl.ds(0, 64, stride=2), :] = jnp.where(high_half, pltpu.roll(r0, 64, 1), 0.0)
        v.pair_a[pl.ds(1, 64, stride=2), :] = jnp.where(high_half, r0, 0.0)
        v.w_fm[step * 128 : (step + 1) * 128, :] = half_of(v.pair_a[0:128, :])

    stage(MOTION_MIX, 2268)
    lane36 = lane_index((36, LANES))
    for i in range(64):
        if i == 0:
            value = strided(flat, MARGIN, 36, 63)
        elif i == 63:
            value = pltpu.roll(strided(flat, MARGIN + 62, 36, 63), 126, 1)
        else:
            low = pltpu.roll(strided(flat, MARGIN + i - 1, 36, 63), 2 * i, 1)
            high = pltpu.roll(strided(flat, MARGIN + i, 36, 63), 2 * i, 1)
            value = jnp.where(lane36 < 2 * i, low, high)
        v.mm_tmp[pl.ds(i, 36, stride=64), :] = jnp.where(lane36 < 126, value, 0.0)
    for step in range(9):
        v.w_mm[step * 256 : (step + 1) * 256, :] = half_of(v.mm_tmp[step * 256 : (step + 1) * 256, :])

    unpack_gru(v, ROWS_GATES, ROWS_CANDIDATE, v.w_ri, v.w_rs)

    stage(None, 21)
    place = 0
    lane1 = lane_index((1, LANES))
    for name, height, width in shapes():
        spot = spots[name]
        for block in range(-(-width // LANES)):
            at = spot + block * LANES
            row, shift = at // LANES, at % LANES
            value = flat[MARGIN + row : MARGIN + row + 1, :]
            if shift:
                after = flat[MARGIN + row + 1 : MARGIN + row + 2, :]
                value = jnp.where(
                    lane1 < LANES - shift, pltpu.roll(value, LANES - shift, 1), pltpu.roll(after, LANES - shift, 1)
                )
            left = width - block * LANES
            if left < LANES:
                value = jnp.where(lane1 < left, value, 0.0)
            if name == FLOW_MIX:
                value = pltpu.roll(value, 64, 1)
            v.bias[place : place + 1, :] = value
            place += 1


def unpack_heads(v):
    flat = v.flat
    low_half = lane_index((128, LANES)) < 64

    def stage(name, rows):
        stage_of(v, name, rows)

    unpack_gru(v, COLUMNS_GATES, COLUMNS_CANDIDATE, v.w_li, v.w_ls)

    for name, lane0 in ((FLOW_HIDDEN, 0), (MASK_HIDDEN, 256)):
        stage(name, 2304)
        for tap in range(9):
            unpack_pairs(flat, tap * 128, 128, v.w_h, tap * 128, lane0)

    stage(FLOW_OUT, 36)
    v.fo_tmp[...] = jnp.zeros_like(v.fo_tmp)
    for which in range(2):
        total = jnp.zeros((9, HEAD), jnp.float32)
        for quarter in range(4):
            total = total + mm(half_of(strided(flat, MARGIN + quarter, 9, 4)), split_pick(which, quarter))
        v.fo_tmp[pl.ds(which, 9, stride=2), 0:128] = total[:, :128]
        v.fo_tmp2[pl.ds(which, 9, stride=2), 0:128] = total[:, 128:]
    v.fo_tmp2[18:32, :] = jnp.zeros((14, LANES), jnp.float32)
    v.w_fo[:, 0:128] = half_of(v.fo_tmp[...])
    v.w_fo[:, 128:256] = half_of(v.fo_tmp2[...])

    stage(MASK_OUT, 1152)
    r = [strided(flat, MARGIN + i, 128, 9) for i in range(9)]
    rs = [pltpu.roll(r[i], 64, 1) for i in range(4, 9)]
    for block in range(5):
        even = r[block] if block < 4 else jnp.where(low_half, r[4], 0.0)
        odd = jnp.where(low_half, rs[block], rs[block + 1]) if block < 4 else jnp.where(low_half, rs[4], 0.0)
        v.pair_a[pl.ds(0, 128, stride=2), :] = even
        v.pair_a[pl.ds(1, 128, stride=2), :] = odd
        v.w_mo[:, block * 128 : (block + 1) * 128] = half_of(v.pair_a[...])


BIAS_AT = {}
_place = 0
for _name, _height, _width in shapes():
    BIAS_AT[_name] = _place
    _place += -(-_width // 128)
BIAS_ROWS = 32


def bias_of(v, name, blocks):
    at = BIAS_AT[name]
    return jnp.concatenate([v.bias[at + i : at + i + 1, :] for i in range(blocks)], axis=1)


class Halo:
    def __init__(self, v, sem, up_src, down_src, from_down, from_up):
        up = {SPACE: jnp.maximum(v.spot - 1, 0)}
        down = {SPACE: jnp.minimum(v.spot + 1, v.space - 1)}
        self.v = v
        self.up = remote(up_src, from_down, v.hsend.at[sem, 0], v.hrecv.at[sem, 0], up)
        self.down = remote(down_src, from_up, v.hsend.at[sem, 1], v.hrecv.at[sem, 1], down)

    def start(self):
        pl.when(self.v.spot > 0)(self.up.start)
        pl.when(self.v.spot < self.v.space - 1)(self.down.start)

    def receive(self):
        pl.when(self.v.spot < self.v.space - 1)(self.up.wait_recv)
        pl.when(self.v.spot > 0)(self.down.wait_recv)

    def sent(self):
        pl.when(self.v.spot > 0)(self.up.wait_send)
        pl.when(self.v.spot < self.v.space - 1)(self.down.wait_send)


class Swap:
    def __init__(self, v, sem, src, dst, broadcast=False):
        self.v, self.sem, self.src, self.dst, self.broadcast = v, sem, src, dst, broadcast

    def copy(self, step):
        v = self.v
        to = lax.rem(v.spot + step, v.space)
        src = self.src if self.broadcast else self.src.at[to]
        return remote(src, self.dst.at[v.spot], v.asend.at[self.sem, step], v.arecv.at[self.sem, step], {SPACE: to})

    def each(self, what):
        def body(step, carry):
            what(self.copy(step))
            return carry

        lax.fori_loop(1, self.v.space, body, 0)

    def start(self):
        self.each(lambda copy: copy.start())

    def receive(self):
        self.each(lambda copy: copy.wait_recv())

    def sent(self):
        self.each(lambda copy: copy.wait_send())


def spread_rows(v, b, acts, rows, dst, row0, width, backward=False):
    x = lax.rem(row_index((rows, LANES)), WIDE)
    for block, act in enumerate(acts):
        v.tmp[8 : 8 + rows, :] = act
        for tap in range(3):
            d = (1 - tap) if backward else (tap - 1)
            value = act if d == 0 else v.tmp[8 + d : 8 + d + rows, :]
            if d == -1:
                value = jnp.where(x > 0, value, 0.0)
            if d == 1:
                value = jnp.where(x < WIDE - 1, value, 0.0)
            lane = tap * width + block * LANES
            if backward:
                dst[row0 : row0 + rows, b + lane : b + lane + LANES] = half_of(value)
            else:
                dst[b, row0 : row0 + rows, lane : lane + LANES] = half_of(value)


def spread_five(v, value, dst, lane_of, backward=False):
    x = lax.rem(row_index((AREA, LANES)), WIDE)
    v.tmp[8 : 8 + AREA, :] = value
    for tap in range(5):
        d = (2 - tap) if backward else (tap - 2)
        moved = value if d == 0 else v.tmp[8 + d : 8 + d + AREA, :]
        if d:
            moved = jnp.where((x + d >= 0) & (x + d < WIDE), moved, 0.0)
        if backward:
            taps_part(v, tap, lane_of, lane_of + LANES)[...] = half_of(moved)
        else:
            lane = lane_of(tap)
            dst[:, lane : lane + LANES] = half_of(moved)


def lines_of(ref, b, lines):
    return jnp.concatenate([ref[b, y] for y in range(lines)], axis=1)


def edge_rows(v, value, rows):
    low = jnp.where(v.spot > 0, value[0:rows], 0.0)
    high = jnp.where(v.spot < v.space - 1, value[-rows:], 0.0)
    return jnp.concatenate([low, value[rows:-rows], high], axis=0)


def early_taps(v):
    def flow(b, carry):
        up = jnp.where(v.spot > 0, v.flow_up[b], 0.0)
        down = jnp.where(v.spot < v.space - 1, v.flow_down[b], 0.0)
        lane = lane_index((16, LANES))
        v.fs[...] = jnp.zeros_like(v.fs)
        for across in range(7):
            d = across - 3
            for part, value in enumerate((up, v.flow[b], down)):
                moved = value
                if d:
                    moved = pltpu.roll(value, (-d) % LANES, 1)
                    moved = jnp.where((lane + d >= 0) & (lane + d < WIDE), moved, 0.0)
                v.fs[across, part * 10 : part * 10 + 10, :] = moved[0:10, :]
        for y in range(9):
            for across in range(7):
                v.flow_tmp[across * 16 : across * 16 + 16, :] = v.fs[across, 2 * y : 2 * y + 16, :]
            v.xt[b, :, y * 128 : (y + 1) * 128] = half_of(v.flow_tmp[...])
        return carry

    lax.fori_loop(0, BATCH, flow, 0)

    def image(b, carry):
        at = pl.ds(pl.multiple_of(b * AREA, AREA), AREA)
        spread_five(v, full_of(v.context[b]), v.xi.at[at], lambda t: t * 256)
        spread_five(v, full_of(v.net[b]), v.xs.at[at], lambda t: t * 128)
        return carry

    lax.fori_loop(0, BATCH, image, 0)


def gather_start(v, count):
    pieces = 4
    rows = BLOCK // 2 // pieces
    half = lax.rem(v.spot, 2)
    matrix = lane_matrix(lax.rem(v.rank * count, LANES), True)
    first = row_index((256, LANES)) == 0

    def rotate(step, carry):
        at = pl.ds(pl.multiple_of(step * 256, 256), 256)
        both = mm(v.gath[at, :], matrix)
        spill = pltpu.roll(both[:, LANES:], 1, 0)
        v.gath[at, :] = half_of(both[:, :LANES] + jnp.where(first, carry, spill))
        return spill[0:1]

    lax.fori_loop(0, BLOCK // 256, rotate, jnp.zeros((1, LANES), jnp.float32))

    def piece(rank, which, index):
        return pl.ds(pl.multiple_of(rank * BLOCK + which * (BLOCK // 2) + index * rows, 16), rows)

    mine = pl.ds(pl.multiple_of(v.rank * BLOCK, 16), BLOCK)
    own = v.gath.at[0:BLOCK]
    v.g_x = [
        remote(
            v.gath.at[piece(0, half, k)], v.out_all.at[piece(v.rank, half, k)], v.gsend.at[0, k], v.grecv.at[0, k],
            {DP: v.other},
        )
        for k in range(pieces)
    ]
    v.g_own = remote(own, v.out_all.at[mine], v.gsend.at[4, 0], v.grecv.at[4, 0], {DP: v.mate})
    v.g_here = pltpu.make_async_copy(own, v.out_all.at[mine], v.gsend.at[4, 1])

    def forward(number, which, k, device):
        block = v.out_all.at[piece(v.other, which, k)]
        return remote(block, block, v.gsend.at[number, k], v.grecv.at[number, k], device)

    v.g_twin = [forward(1, half, k, {SPACE: v.twin}) for k in range(pieces)]
    v.g_mate = [forward(2, half, k, {DP: v.mate}) for k in range(pieces)]
    v.g_last = [forward(3, 1 - half, k, {DP: v.mate}) for k in range(pieces)]
    for copy in v.g_x:
        copy.start()
    v.g_own.start()
    v.g_here.start()


def gather_pass(v, first, last):
    for k in range(first, last):
        v.g_x[k].wait_recv()
        v.g_twin[k].start()
        v.g_mate[k].start()


def gather_end(v):
    for k in range(len(v.g_x)):
        v.g_twin[k].wait_recv()
        v.g_last[k].start()
    for k in range(len(v.g_x)):
        v.g_x[k].wait_send()
        v.g_twin[k].wait_send()
        v.g_mate[k].wait()
        v.g_last[k].wait()
    v.g_own.wait()
    v.g_here.wait()


def forward_rows(v):
    spot, last = v.spot, v.space - 1
    def image(b, carry):
        pieces = (
            (v.corr_up, 0, 256, 2, spot > 0),
            (v.corr, 256, 640, 5, None),
            (v.corr_down, 896, 256, 2, spot < last),
        )
        bias = bias_of(v, CORR_IN, 2)
        for ref, row0, rows, lines, seen in pieces:
            act, slope = act_slope(tn(lines_of(ref, b, lines), v.w_ci[...]) + bias)
            if seen is None:
                v.slope_ci[b] = half_of(slope)
            else:
                act = jnp.where(seen, act, 0.0)
            spread_rows(v, b, (act[:, :128], act[:, 128:]), rows, v.hx_c, row0, 256)

        act, slope = act_slope(tn(v.xt[b], v.w_fi[...]) + bias_of(v, FLOW_IN, 1))
        v.slope_fi[b] = half_of(slope[256:896])
        spread_rows(v, b, (edge_rows(v, act, 2 * WIDE),), 9 * WIDE, v.hx_f, 0, 128)

        pre = bias_of(v, CORR_MIX, 2)
        flow_pre = bias_of(v, FLOW_MIX, 1)
        for a in range(3):
            pre = pre + mm(v.hx_c[b, a * 128 : a * 128 + 896, :], v.w_cm[a * 768 : (a + 1) * 768, :])
            flow_pre = flow_pre + mm(v.hx_f[b, a * 128 : a * 128 + 896, :], v.w_fm[a * 384 : (a + 1) * 384, :])
        low, low_slope = act_slope(pre[:, :128])
        high, high_slope = act_slope(pre[:, 128:] + flow_pre)
        v.slope_j[b, :, 0:128] = half_of(low_slope)
        v.slope_j[b, :, 128:256] = half_of(high_slope)
        spread_rows(v, b, (edge_rows(v, low, WIDE), edge_rows(v, high, WIDE)), 896, v.hx_j, 0, 256)

        pre = bias_of(v, MOTION_MIX, 1)
        for a in range(3):
            pre = pre + mm(v.hx_j[b, a * 128 : a * 128 + 640, :], v.w_mm[a * 768 : (a + 1) * 768, :])
        act, slope = act_slope(pre)
        v.slope_m[b] = half_of(jnp.where(lane_index((AREA, LANES)) < 126, slope, 0.0))
        pick = jnp.where(lane_index((16, LANES)) == row_index((16, LANES)) + 126, 1.0, 0.0)
        own_flow = v.flow[b]
        for y in range(ROWS):
            v.tmp2[0:2, :] = own_flow[2 * y : 2 * y + 2, :]
            v.tmp2[2:16, :] = jnp.zeros((14, LANES), jnp.float32)
            v.motion[b, y * 128 : (y + 1) * 128, :] = act[y * 128 : (y + 1) * 128, :] + tn(
                half_of(v.tmp2[0:16, :]), half_of(pick)
            )
        v.motion[b] = full_of(half_of(v.motion[b]))
        pack_rows(v, v.motion, b, v.a_motion)
        return carry

    lax.fori_loop(0, BATCH, image, 0)
    v.swap_motion.start()

    def gru(b, carry):
        at = pl.ds(pl.multiple_of(b * AREA, AREA), AREA)
        s = full_of(v.net[b])
        spread_five(v, v.motion[b], v.xi.at[at], lambda t: t * 256 + 128)
        both = mm(v.xi[at, :], v.w_ri[...])
        gates = jax.nn.sigmoid(both[:, :256] + mm(v.xs[at, :], v.w_rs[:, :256]) + bias_of(v, ROWS_GATES, 2))
        update, reset = gates[:, :128], gates[:, 128:]
        v.ru[b] = update
        v.rr[b] = reset
        spread_five(v, full_of(half_of(reset * s)), v.xr.at[at], lambda t: t * 128)
        cand = jnp.tanh(both[:, 256:] + mm(v.xr[at, :], v.w_rs[:, 256:]) + bias_of(v, ROWS_CANDIDATE, 1))
        v.rc[b] = cand
        v.state[b] = s + update * (cand - s)
        pack_rows(v, v.state, b, v.a_state)
        return carry

    lax.fori_loop(0, BATCH, gru, 0)
    v.swap_state.start()


def pack_rows(v, src, b, dst):
    def peer(t, carry):
        for y in range(ROWS):
            at = pl.multiple_of(y * WIDE + t * COLS, COLS)
            dst[t, b, y * COLS : (y + 1) * COLS, :] = half_of(src[b, pl.ds(at, COLS), :])
        return carry

    lax.fori_loop(0, v.space, peer, 0)


def take_own(v, src, dst):
    dst[v.spot] = src[v.spot]


def columns_zero(v):
    def zero(b, carry):
        for ref, wide in ((v.xc, 384), (v.xcr, 128), (v.gc, 384)):
            for low in (0, 32 + AREA):
                ref[b, low : low + 32, :] = jnp.zeros((32, wide), jnp.bfloat16)
        return carry

    lax.fori_loop(0, BATCH, zero, 0)


def columns_in(v):
    def peer(t, carry):
        at = pl.ds(pl.multiple_of(32 + t * ROWS * COLS, 16), ROWS * COLS)
        for b in range(BATCH):
            v.xc[b, at, 0:128] = v.b_state[t, b]
            v.xc[b, at, 128:256] = v.b_context[t, b]
            v.xc[b, at, 256:384] = v.b_motion[t, b]
        return carry

    lax.fori_loop(0, v.space, peer, 0)


FX_ROWS = 16 + (TALL + 2) * PITCH


def fx_base(b):
    return pl.multiple_of(b * FX_ROWS, 8)


def columns_forward(v):
    def gru(b, carry):
        s = full_of(v.xc[b, 32 : 32 + AREA, 0:128])
        both = bias_of(v, COLUMNS_GATES, 2)
        both = jnp.concatenate([both, bias_of(v, COLUMNS_CANDIDATE, 1)], axis=1)
        gates = 0.0
        for t in range(5):
            rows = slice(t * COLS, t * COLS + AREA)
            both = both + mm(v.xc[b, rows, 128:384], v.w_li[t * 256 : (t + 1) * 256, :])
            gates = gates + mm(v.xc[b, rows, 0:128], v.w_ls[t * 128 : (t + 1) * 128, 0:256])
        gates = jax.nn.sigmoid(gates + both[:, :256])
        update, reset = gates[:, :128], gates[:, 128:]
        v.lu[b] = update
        v.lr[b] = reset
        v.xcr[b, 32 : 32 + AREA, :] = half_of(reset * s)
        cand = both[:, 256:]
        for t in range(5):
            rows = slice(t * COLS, t * COLS + AREA)
            cand = cand + mm(v.xcr[b, rows, :], v.w_ls[t * 128 : (t + 1) * 128, 256:384])
        cand = jnp.tanh(cand)
        v.lc[b] = cand
        final = s + update * (cand - s)
        v.out_net[b] = half_of(final)
        v.final[...] = full_of(half_of(final))
        fx = fx_base(b)
        v.mm_tmp[pl.ds(fx, FX_ROWS), :] = jnp.zeros((FX_ROWS, LANES), jnp.float32)
        for x in range(COLS):
            v.mm_tmp[pl.ds(fx + 8 + PITCH + 2 + x, TALL, stride=PITCH), :] = v.final[pl.ds(x, TALL, stride=COLS), :]
        for j in range(2):
            v.e_left[b, j, 0:TALL, :] = half_of(v.final[pl.ds(j, TALL, stride=COLS), :])
            v.e_right[b, j, 0:TALL, :] = half_of(v.final[pl.ds(COLS - 2 + j, TALL, stride=COLS), :])
        return carry

    lax.fori_loop(0, BATCH, gru, 0)
    v.halo_final.start()


def ring_masks(v, shape):
    x = lax.rem(row_index(shape), PITCH)
    place = v.spot * COLS + x - 2
    seen = (place >= 0) & (place < WIDE) & (x >= 1) & (x < PITCH - 1)
    own = (x >= 2) & (x < PITCH - 2)
    return seen, own


def mask_gradient(v):
    def image(b, carry):
        value = nt(quarter_of(v.grad_mask[b]), v.w_mo[:, 0:MASK])
        for block in range(2):
            v.final[...] = value[:, block * 128 : (block + 1) * 128]
            v.tmp[0:SPREAD, :] = jnp.zeros((SPREAD, LANES), jnp.float32)
            for x in range(COLS):
                v.tmp[pl.ds(2 + x, TALL, stride=PITCH), :] = v.final[pl.ds(x, TALL, stride=COLS), :]
            v.hgo[b, :, 256 + block * 128 : 384 + block * 128] = half_of(v.tmp[0:SPREAD, :])
            v.m_left[b, block, 0:TALL, :] = half_of(v.final[pl.ds(0, TALL, stride=COLS), :])
            v.m_right[b, block, 0:TALL, :] = half_of(v.final[pl.ds(COLS - 1, TALL, stride=COLS), :])
        return carry

    lax.fori_loop(0, BATCH, image, 0)
    v.halo_mask.start()


def heads_part(v, b, tap):
    ref = v.hx_c if tap < 6 else v.hx_f
    lane = tap % 6 * 128
    return ref.at[b, 0:SPREAD, lane : lane + 128]


def taps_part(v, t, low, high):
    ref = v.hx_f if t % 3 == 2 else v.hx_c
    lane = (t % 3) % 2 * 384
    return ref.at[t // 3, 0:AREA, lane + low : lane + high]


def heads(v):
    spot, last = v.spot, v.space - 1
    v.halo_final.receive()
    v.halo_mask.receive()
    v.swap_count.receive()
    v.counts[v.spot] = v.count_out[...]
    counts = jnp.sum(v.counts[...], axis=0)
    seen, own = ring_masks(v, (SPREAD, LANES))
    steps = [(a - 1) * PITCH + (c - 1) for a in range(3) for c in range(3)]
    plane = jnp.float32(TALL * WIDE)

    def image(b, carry):
        fx = fx_base(b)
        for j in range(2):
            left = jnp.where(spot > 0, full_of(v.f_left[b, j, 0:TALL, :]), 0.0)
            right = jnp.where(spot < last, full_of(v.f_right[b, j, 0:TALL, :]), 0.0)
            v.mm_tmp[pl.ds(fx + 8 + PITCH + j, TALL, stride=PITCH), :] = left
            v.mm_tmp[pl.ds(fx + 8 + PITCH + PITCH - 2 + j, TALL, stride=PITCH), :] = right
        for block in range(2):
            left = jnp.where(spot > 0, full_of(v.n_left[b, block, 0:TALL, :]), 0.0)
            right = jnp.where(spot < last, full_of(v.n_right[b, block, 0:TALL, :]), 0.0)
            v.tmp[0:SPREAD, :] = full_of(v.hgo[b, :, 256 + block * 128 : 384 + block * 128])
            v.tmp[pl.ds(1, TALL, stride=PITCH), :] = left
            v.tmp[pl.ds(PITCH - 2, TALL, stride=PITCH), :] = right
            v.hgo[b, :, 256 + block * 128 : 384 + block * 128] = half_of(v.tmp[0:SPREAD, :])
        for tap in range(9):
            at = 8 + PITCH + steps[tap]
            heads_part(v, b, tap)[...] = half_of(v.mm_tmp[pl.ds(fx + at, SPREAD), :])
        for part in range(2):
            name = (FLOW_HIDDEN, MASK_HIDDEN)[part]
            lanes = slice(part * 256, (part + 1) * 256)
            act, slope = act_slope(mm(v.hx_c[b, 0:SPREAD, :], v.w_h[0:768, lanes]) + mm(v.hx_f[b, 0:SPREAD, :], v.w_h[768:1152, lanes]) + bias_of(v, name, 2))
            v.slope_h[b, :, lanes] = half_of(slope)
            if part == 0:
                for block in range(2):
                    value = jnp.where(seen, act[:, block * 128 : (block + 1) * 128], 0.0)
                    v.feat[b, 0:SPREAD, block * 128 : (block + 1) * 128] = half_of(value)
                v.feat[b, SPREAD:SPAN, :] = jnp.zeros((SPAN - SPREAD, HEAD), jnp.bfloat16)
            else:
                for block in range(2):
                    v.tmp[0:SPREAD, :] = act[:, block * 128 : (block + 1) * 128]
                    for x in range(COLS):
                        v.final[pl.ds(x, TALL, stride=COLS), :] = v.tmp[pl.ds(2 + x, TALL, stride=PITCH), :]
                    v.mf[b, :, block * 128 : (block + 1) * 128] = half_of(v.final[...])
        moved = nt(v.w_fo[...], v.feat[b])
        v.zt[...] = moved
        delta = jnp.zeros((8, SPAN), jnp.float32)
        for tap in range(9):
            pair = jnp.concatenate([v.zt[2 * tap : 2 * tap + 2, :], jnp.zeros((6, SPAN), jnp.float32)], axis=0)
            delta = delta + pltpu.roll(pair, (-steps[tap]) % SPAN, 1)
        v.tmp[0:SPAN, :] = jnp.zeros((SPAN, LANES), jnp.float32)
        v.final[...] = full_of(v.xc[b, 32 : 32 + AREA, 256:384])
        for x in range(COLS):
            v.tmp[pl.ds(2 + x, TALL, stride=PITCH), :] = v.final[pl.ds(x, TALL, stride=COLS), :]
        pick = jnp.where(lane_index((16, LANES)) == row_index((16, LANES)) + 126, 1.0, 0.0)
        base = nt(half_of(pick), half_of(v.tmp[0:SPAN, :]))[0:8, :]
        bias = v.bias[BIAS_AT[FLOW_OUT] : BIAS_AT[FLOW_OUT] + 1, :]
        first = row_index((8, SPAN)) == 0
        second = row_index((8, SPAN)) == 1
        shift = jnp.where(first, bias[0:1, 0:1], jnp.where(second, bias[0:1, 1:2], 0.0))
        new = base + delta + shift
        v.out_flow[b] = new
        error = new - v.target[b]
        root = jnp.sqrt(error * error + 1.0)
        valid = jnp.where(first | second, v.valid[b], 0.0)
        piece = jnp.sum(valid * root)
        divisor = jnp.maximum(v.pick_count(counts, b), 1.0)
        gradient = plane / divisor * valid * error / root
        v.dg[b] = gradient
        v.losses[...] = jnp.where(row_index((8, LANES)) == b, piece, v.losses[...])
        return carry

    v.losses[...] = jnp.zeros((8, LANES), jnp.float32)
    lax.fori_loop(0, BATCH, image, 0)
    v.halo_dg.start()
    v.swap_loss.start()


def mask_output(v):
    def image(b, carry):
        store = pltpu.make_async_copy(v.mask_low, v.out_mask.at[b], v.osem.at[3])
        pl.when(b > 0)(store.wait)
        for block in range(5):
            wide = min(128, MASK - block * 128)
            lanes = slice(block * 128, block * 128 + wide)
            at = BIAS_AT[MASK_OUT] + block
            value = mm(v.mf[b], v.w_mo[:, lanes]) + v.bias[at : at + 1, 0:wide]
            v.mask_low[:, lanes] = half_of(0.25 * value)
        store.start()
        return carry

    lax.fori_loop(0, BATCH, image, 0)


def heads_back(v):
    spot, last = v.spot, v.space - 1
    seen, own = ring_masks(v, (SPREAD, LANES))
    steps = [(a - 1) * PITCH + (c - 1) for a in range(3) for c in range(3)]
    v.halo_dg.receive()

    def zb(c, low, rows):
        at = c * (2 * EDGE + SPREAD) + low
        return v.mm_tmp.at[at : at + rows]

    def image(b, carry):
        x = lax.rem(lane_index((8, SPAN)), PITCH)
        own_dg = v.dg[b]
        left = jnp.where((x < 2) & (spot > 0), pltpu.roll(v.dg_left[b], SPAN - COLS, 1), 0.0)
        right = jnp.where((x >= PITCH - 2) & (spot < last), pltpu.roll(v.dg_right[b], COLS, 1), 0.0)
        inside = lane_index((8, SPAN)) < SPREAD
        wide_dg = full_of(half_of(jnp.where(inside, own_dg + left + right, 0.0)))
        own_low = full_of(half_of(own_dg))
        v.dt[...] = jnp.zeros_like(v.dt)
        v.dto[...] = jnp.zeros_like(v.dto)
        for tap in range(9):
            v.dt[2 * tap : 2 * tap + 2, :] = pltpu.roll(wide_dg, steps[tap] % SPAN, 1)[0:2, :]
            v.dto[2 * tap : 2 * tap + 2, :] = pltpu.roll(own_low, steps[tap] % SPAN, 1)[0:2, :]
        v.dtb[b] = half_of(v.dto[...])
        from_flow = tn(half_of(v.dt[...]), v.w_fo[...])
        for block in range(4):
            lanes = slice(block * 128, (block + 1) * 128)
            value = from_flow[0:SPREAD, lanes] if block < 2 else full_of(v.hgo[b, :, lanes])
            value = value * full_of(v.slope_h[b, :, lanes])
            v.hgo[b, :, lanes] = half_of(jnp.where(seen, value, 0.0))
        total = jnp.zeros((SPREAD, LANES), jnp.float32)
        for a in range(3):
            value = nt(v.hgo[b], v.w_h[a * 384 : (a + 1) * 384, :])
            for c in range(3):
                zb(c, EDGE, SPREAD)[...] = value[:, c * 128 : (c + 1) * 128]
            for c in range(3):
                at = EDGE - steps[a * 3 + c]
                total = total + zb(c, at, SPREAD)[...]
        for block in range(4):
            lanes = slice(block * 128, (block + 1) * 128)
            v.hgo[b, :, lanes] = half_of(jnp.where(own, full_of(v.hgo[b, :, lanes]), 0.0))
        v.tmp[0:SPREAD, :] = total
        for x in range(COLS):
            v.final[pl.ds(x, TALL, stride=COLS), :] = v.tmp[pl.ds(2 + x, TALL, stride=PITCH), :]
        r = v.final[...] + full_of(v.grad_net[b])

        s = full_of(v.xc[b, 32 : 32 + AREA, 0:128])
        update, reset, cand = v.lu[b], v.lr[b], v.lc[b]
        cg = half_of(r * update * (1.0 - cand * cand))
        v.gc[b, 32 : 32 + AREA, 256:384] = cg
        reset_grad = 0.0
        for t in range(5):
            rows = slice((4 - t) * COLS, (4 - t) * COLS + AREA)
            reset_grad = reset_grad + nt(v.gc[b, rows, 256:384], v.w_ls[t * 128 : (t + 1) * 128, 256:384])
        v.gc[b, 32 : 32 + AREA, 0:128] = half_of(r * (cand - s) * update * (1.0 - update))
        v.gc[b, 32 : 32 + AREA, 128:256] = half_of(reset_grad * s * reset * (1.0 - reset))
        state_grad = r * (1.0 - update) + reset_grad * reset
        inputs_grad = 0.0
        for t in range(5):
            rows = slice((4 - t) * COLS, (4 - t) * COLS + AREA)
            state_grad = state_grad + nt(v.gc[b, rows, 0:256], v.w_ls[t * 128 : (t + 1) * 128, 0:256])
            inputs_grad = inputs_grad + nt(v.gc[b, rows, :], v.w_li[t * 256 : (t + 1) * 256, :])
        high = half_of(own_dg)
        low = half_of(own_dg - full_of(high))
        pick = half_of(jnp.where(lane_index((8, LANES)) == row_index((8, LANES)) + 126, 1.0, 0.0))
        v.tmp[0:SPAN, :] = tn(high, pick) + tn(low, pick)
        for x in range(COLS):
            v.final[pl.ds(x, TALL, stride=COLS), :] = v.tmp[pl.ds(2 + x, TALL, stride=PITCH), :]
        v.lu[b] = state_grad
        v.lr[b] = inputs_grad[:, 0:128]
        v.lc[b] = inputs_grad[:, 128:256] + v.final[...]

        def peer(t, carry):
            at = pl.ds(pl.multiple_of(t * ROWS * COLS, 16), ROWS * COLS)
            v.a_state[t, b] = half_of(v.lu[b, at, :])
            v.a_context[t, b] = half_of(v.lr[b, at, :])
            v.a_motion[t, b] = half_of(v.lc[b, at, :])
            return carry

        lax.fori_loop(0, v.space, peer, 0)
        return carry

    for c in range(3):
        zb(c, 0, EDGE)[...] = jnp.zeros((EDGE, LANES), jnp.float32)
        zb(c, EDGE + SPREAD, EDGE)[...] = jnp.zeros((EDGE, LANES), jnp.float32)
    lax.fori_loop(0, BATCH, image, 0)
    v.swap_loss.receive()
    v.back_state.start()
    v.back_context.start()
    v.back_motion.start()


def unpack_back(v, src, dst):
    def peer(t, carry):
        for b in range(BATCH):
            value = full_of(src[t, b])
            for y in range(ROWS):
                at = pl.multiple_of(y * WIDE + t * COLS, COLS)
                dst[b, pl.ds(at, COLS), :] = value[y * COLS : (y + 1) * COLS, :]
        return carry

    lax.fori_loop(0, v.space, peer, 0)


def seams():
    starts, bias_row, _, _ = flat_rows()
    edges = sorted(starts.values()) + [bias_row]
    tiles = sorted({row // 16 for row in edges if row % 16})
    parts = {}
    for low, high in zip(edges, edges[1:]):
        for tile in tiles:
            if low < (tile + 1) * 16 and high > tile * 16:
                parts[tile] = parts.get(tile, 0) + 1
    return {tile: (index, parts[tile]) for index, tile in enumerate(tiles)}


class Flush:
    def __init__(self, v):
        self.v, self.at, self.busy, self.small = v, 0, {}, []
        self.tiles = seams()
        self.left = {tile: parts for tile, (_, parts) in self.tiles.items()}
        v.seam[...] = jnp.zeros_like(v.seam)
        top = (max(self.tiles) + 1) * 16
        rest = v.out_flat.shape[0] - top
        v.seam_low[16 * 16 : 16 * 16 + rest, :] = jnp.zeros((rest, LANES), jnp.bfloat16)
        self.write(16, rest, top)

    def write(self, index, rows, base):
        v = self.v
        copy = pltpu.make_async_copy(
            v.seam_low.at[index * 16 : index * 16 + rows], v.out_flat.at[base : base + rows], v.fsem.at[index]
        )
        copy.start()
        self.small.append(copy)

    def send(self, low, length, base):
        v, slot = self.v, self.at % 2
        self.at += 1
        if slot in self.busy:
            self.busy[slot].wait()
        cast_rows(v.stage.at[slot], 0, v.flat, low, length, jnp.bfloat16)
        copy = pltpu.make_async_copy(
            v.stage.at[slot, 0:length], v.out_flat.at[base : base + length], v.ssem.at[slot, 0]
        )
        copy.start()
        self.busy[slot] = copy

    def layer(self, start, rows):
        v, stop = self.v, start + rows
        for tile in self.tiles:
            low, high = max(start, tile * 16), min(stop, tile * 16 + 16)
            if low >= high:
                continue
            index = self.tiles[tile][0]
            v.seam[index, low - tile * 16 : high - tile * 16, :] = v.flat[MARGIN + low - start : MARGIN + high - start, :]
            self.left[tile] -= 1
            if not self.left[tile]:
                v.seam_low[index * 16 : index * 16 + 16, :] = half_of(v.seam[index])
                self.write(index, 16, tile * 16)
        low, high = -(-start // 16) * 16, stop // 16 * 16
        if high > low:
            self.send(MARGIN + low - start, high - low, low)

    def settle(self):
        for copy in list(self.busy.values()) + self.small:
            copy.wait()
        self.busy, self.small = {}, []


SHARE = 3072


class Reduce:
    ORDER = (
        (3, 3072, 3072), (3, 0, 3072), (2, 3072, 3072), (2, 0, 3072), (1, 3072, 3072), (1, 0, 3072),
        (0, 1024, 3072), (0, 4096, 2048), (0, 0, 1024),
    )

    def __init__(self, v, count):
        self.v, self.count = v, count
        self.flying, self.queue = [], []
        self.copies = {}
        rank = v.rank
        self.lower, self.upper = lax.rem(rank, 2), lax.div(rank, 2)
        self.side, self.depth = lax.rem(v.spot, 2), lax.div(v.spot, 2)
        self.group = v.space // 2

    def part(self, k):
        return self.ORDER[k][2] // 4 // self.v.space

    def slice_at(self, k, spot):
        return lax.rem(spot, 2) * (self.ORDER[k][2] // 8) + lax.div(spot, 2) * self.part(k)

    def offer(self, *numbers):
        self.v.flush.settle()
        self.queue += list(numbers)

    def tick(self):
        stages = (self.core, self.across, self.stripes, self.along, self.beside)
        for entry in self.flying:
            stages[entry[1]](entry[0])
            entry[1] += 1
        self.flying = [entry for entry in self.flying if entry[1] < len(stages)]
        if self.queue:
            number = self.queue.pop(0)
            self.begin(number)
            self.flying.append([number, 0])

    def begin(self, k):
        v, slot = self.v, k % 2
        quarter, low, size = self.ORDER[k]
        start = quarter * self.count // (LANES * 16) * 16 + low
        half = size // 2

        def rows(which):
            return v.out_flat.at[pl.ds(pl.multiple_of(start + which * half, 16), half)]

        copy = remote(
            rows(1 - self.lower), v.rcore.at[slot, 0:half], v.rsend.at[0, slot], v.rrecv.at[0, slot], {DP: v.mate}
        )
        own = pltpu.make_async_copy(rows(self.lower), v.own.at[slot, 0:half], v.rlocal.at[slot])
        copy.start()
        own.start()
        self.copies[k] = (copy, own)

    def core(self, k):
        v, slot = self.v, k % 2
        copy, own = self.copies[k]
        copy.wait()
        own.wait()
        if k >= 2:
            self.x_copy(k - 2).wait_send()
        quarter = self.ORDER[k][2] // 4

        def add(step, carry):
            at = pl.multiple_of(step * 128, 128)
            near = pl.ds(pl.multiple_of(self.upper * quarter + at, 128), 128)
            far = pl.ds(pl.multiple_of((1 - self.upper) * quarter + at, 128), 128)
            to = pl.ds(at, 128)
            v.tx[slot, to, :] = half_of(full_of(v.own[slot, far, :]) + full_of(v.rcore[slot, far, :]))
            v.ks[slot, to, :] = full_of(v.own[slot, near, :]) + full_of(v.rcore[slot, near, :])
            return carry

        lax.fori_loop(0, quarter // 128, add, 0)
        self.x_copy(k).start()

    def x_copy(self, k):
        v, slot = self.v, k % 2
        rows = slice(0, self.ORDER[k][2] // 4)
        return remote(
            v.tx.at[slot, rows], v.rx.at[slot, rows], v.rsend.at[1, slot], v.rrecv.at[1, slot], {DP: v.other}
        )

    def s_copy(self, k, step):
        v, slot, part = self.v, k % 2, self.part(k)
        to = lax.rem(v.spot + step, v.space)
        src = v.ts.at[slot, pl.ds(pl.multiple_of(self.slice_at(k, to), 16), part)]
        dst = v.rs.at[slot, v.spot, 0:part]
        return remote(src, dst, v.s2send.at[slot, step], v.s2recv.at[slot, step], {SPACE: to})

    def each(self, what, start, stop):
        def body(step, carry):
            what(step)
            return carry

        lax.fori_loop(start, stop, body, 0)

    def across(self, k):
        v, slot = self.v, k % 2
        self.x_copy(k).wait_recv()
        if k >= 2:
            self.each(lambda step: self.s_copy(k - 2, step).wait_send(), 1, v.space)

        def add(step, carry):
            to = pl.ds(pl.multiple_of(step * 128, 128), 128)
            value = v.ks[slot, to, :] + full_of(v.rx[slot, to, :])
            v.ks[slot, to, :] = value
            v.ts[slot, to, :] = half_of(value)
            return carry

        lax.fori_loop(0, self.ORDER[k][2] // 4 // 128, add, 0)
        part = self.part(k)
        v.acc[slot, 0:part, :] = v.ks[slot, pl.ds(pl.multiple_of(self.slice_at(k, v.spot), 16), part), :]
        self.each(lambda step: self.s_copy(k, step).start(), 1, v.space)

    def place(self, k, lower, upper, spot):
        quarter, low, size = self.ORDER[k]
        at = low + lower * (size // 2) + upper * (size // 4) + self.slice_at(k, spot)
        return pl.ds(pl.multiple_of(at, 16), self.part(k))

    def f_copy(self, k, step):
        v, slot = self.v, k % 2
        quarter = self.ORDER[k][0]
        to = lax.rem(self.depth + step, self.group) * 2 + self.side
        return remote(
            v.fin.at[slot, 0 : self.part(k)], v.gath.at[self.place(k, self.lower, self.upper, v.spot)],
            v.fsend.at[slot, step], v.frecv.at[k, v.rank, self.depth], {DP: quarter, SPACE: to},
        )

    def f_all(self, k, what):
        v = self.v
        pl.when(v.rank != self.ORDER[k][0])(lambda: what(self.f_copy(k, 0)))
        self.each(lambda step: what(self.f_copy(k, step)), 1, self.group)

    def stripes(self, k):
        v, slot, part = self.v, k % 2, self.part(k)
        quarter = self.ORDER[k][0]
        self.each(lambda step: self.s_copy(k, step).wait_recv(), 1, v.space)

        def add(step, value):
            return value + full_of(v.rs[slot, lax.rem(v.spot + step, v.space), 0:part])

        value = half_of(lax.fori_loop(1, v.space, add, v.acc[slot, 0:part, :]))
        if k >= 2:
            self.f_all(k - 2, lambda copy: copy.wait_send())
        v.fin[slot, 0:part, :] = value

        @pl.when(v.rank == quarter)
        def _():
            v.gath[self.place(k, self.lower, self.upper, v.spot), :] = v.fin[slot, 0:part, :]

        self.f_all(k, lambda copy: copy.start())

    def f_wait(self, k, source, step):
        v = self.v
        depth = lax.rem(self.depth + step, self.group)
        spot = depth * 2 + self.side
        remote(
            v.fin.at[0, 0 : self.part(k)], v.gath.at[self.place(k, source % 2, source // 2, spot)],
            v.fsend.at[0, 0], v.frecv.at[k, source, depth], {SPACE: v.twin},
        ).wait_recv()

    def y_copies(self, k):
        v = self.v
        quarter, low, size = self.ORDER[k]
        out = []
        for i in range(4):
            at = pl.multiple_of(low + i * (size // 4) + self.side * (size // 8), 16)
            block = v.gath.at[pl.ds(at, size // 8)]
            out.append(remote(block, block, v.ysend.at[k, i], v.yrecv.at[k, i], {SPACE: v.twin}))
        return out

    def along(self, k):
        v = self.v
        quarter = self.ORDER[k][0]

        @pl.when(v.rank == quarter)
        def _():
            for source in range(4):
                self.each(
                    lambda step: self.f_wait(k, source, step), 1 if source == quarter else 0, self.group
                )
            for copy in self.y_copies(k):
                copy.start()

    def beside(self, k):
        v = self.v

        @pl.when(v.rank == self.ORDER[k][0])
        def _():
            for copy in self.y_copies(k):
                copy.wait()

    def settle(self):
        v = self.v
        for k in range(len(self.ORDER) - 2, len(self.ORDER)):
            self.x_copy(k).wait_send()
            self.each(lambda step: self.s_copy(k, step).wait_send(), 1, v.space)
            self.f_all(k, lambda copy: copy.wait_send())

    def ready(self):
        v, count = self.v, self.count
        v.gath[2 * SHARE :, :] = jnp.zeros((32, LANES), jnp.bfloat16)

        @pl.when(v.rank == 3)
        def _():
            at = self.bias_base() - 3 * count // (LANES * 16) * 16
            v.gath[at : at + 32, :] = half_of(full_of(v.gath[at : at + 32, :]) + v.bsum[...])

    def lay(self, first, last):
        v, count = self.v, self.count
        offset = v.rank * count - quarter_base(v.rank, count) * LANES
        skip = lax.div(offset, LANES)
        matrix = lane_matrix(lax.rem(offset, LANES), False)

        def out(step):
            at = pl.multiple_of(step * 256, 256)
            slot = lax.rem(step, 2)
            return pltpu.make_async_copy(v.gout.at[slot], v.out_grads.at[pl.ds(at, 256)], v.osem.at[4 + slot])

        def place(step, carry):
            at = pl.multiple_of(step * 256, 256)
            both = mm(v.gath[pl.ds(at, 288), :], matrix)
            v.tmp[0:288, :] = both[:, 0:LANES]
            v.tmp[288:576, :] = both[:, LANES:]
            pl.when(step > first + 1)(out(step - 2).wait)
            v.gout[lax.rem(step, 2)] = v.tmp[pl.ds(skip, 256), :] + v.tmp[pl.ds(skip + 289, 256), :]
            out(step).start()
            return carry

        lax.fori_loop(first, last, place, 0)
        for step in (last - 2, last - 1):
            out(step).wait()

    def bias_base(self):
        return flat_rows()[1] // 16 * 16

    def bias_core(self):
        v = self.v
        self.b1 = remote(v.bown, v.bcore, v.bsend.at[0], v.brecv.at[0], {DP: v.mate})
        self.b1.start()

    def bias_across(self):
        v = self.v
        self.b1.wait()
        v.btwo[...] = v.bown[...] + v.bcore[...]
        self.b2 = remote(v.btwo, v.bacross, v.bsend.at[1], v.brecv.at[1], {DP: v.other})
        self.b2.start()

    def bias_stripes(self):
        v = self.v
        self.b2.wait()
        v.bfour[...] = v.btwo[...] + v.bacross[...]
        self.b3 = Swap(v, 8, v.bfour, v.ball, True)
        self.b3.start()

    def bias_end(self):
        v = self.v
        self.b3.receive()
        self.b3.sent()
        v.ball[v.spot] = v.bfour[...]
        v.bsum[...] = jnp.sum(v.ball[...], axis=0)


def ones_sum(g):
    return mm(jnp.ones((8, g.shape[0]), jnp.bfloat16), g)[0:1, :]


def keep_bias(v, name, value):
    for block in range(-(-value.shape[1] // 128)):
        at = BIAS_AT[name] + block
        v.gbias[at : at + 1, :] = value[:, block * 128 : (block + 1) * 128]


def gradients_gru(v, gates_name, cand_name, parts, g_of):
    starts, _, _, _ = flat_rows()
    total = 0.0
    for b in range(BATCH):
        total = total + ones_sum(g_of(b))
    keep_bias(v, gates_name, total[:, 0:256])
    keep_bias(v, cand_name, total[:, 256:384])

    for t in range(5):
        s_part, i_part, r_part = parts(t)
        state = tn_all(s_part, g_of, 0, 256)
        v.mm_tmp[pl.ds(MARGIN + t * 384, 128), :] = tn_all(r_part, g_of, 256, 384)
        inputs = tn_all(i_part, g_of, 0, 384)
        pack_pairs(v.flat, t * 384, 128, state[:, 0:128], state[:, 128:256])
        pack_pairs(v.flat, t * 384 + 128, 256, inputs[:, 0:128], inputs[:, 128:256])
        v.mm_tmp[pl.ds(MARGIN + t * 384 + 128, 256), :] = inputs[:, 256:384]
    v.flush.layer(starts[gates_name], 3840)
    cast_rows(v.flat, MARGIN, v.mm_tmp, MARGIN, 1920, jnp.float32)
    v.flush.layer(starts[cand_name], 1920)


def tn_all(part, g_of, low, high):
    total = 0.0
    for b in range(BATCH):
        total = total + tn(part(b), g_of(b, low, high))
    return total


def gradients_heads(v):
    starts, _, _, _ = flat_rows()
    total = 0.0
    for b in range(BATCH):
        total = total + ones_sum(v.hgo[b])
    keep_bias(v, FLOW_HIDDEN, total[:, 0:256])
    keep_bias(v, MASK_HIDDEN, total[:, 256:512])
    for name, lane in ((FLOW_HIDDEN, 0), (MASK_HIDDEN, 256)):
        for tap in range(9):
            value = 0.0
            for b in range(BATCH):
                value = value + tn(heads_part(v, b, tap)[...], v.hgo[b, :, lane : lane + 256])
            pack_pairs(v.flat, tap * 128, 128, value[:, 0:128], value[:, 128:256])
        v.flush.layer(starts[name], 2304)

    total = 0.0
    sums = 0.0
    for b in range(BATCH):
        total = total + mm(v.dtb[b], v.feat[b])
        sums = sums + jnp.sum(full_of(half_of(v.dg[b])), axis=1, keepdims=True)
    lane1 = lane_index((1, LANES))
    at = BIAS_AT[FLOW_OUT]
    v.gbias[at : at + 1, :] = jnp.where(lane1 == 0, sums[0:1, :], jnp.where(lane1 == 1, sums[1:2, :], 0.0))
    v.fo_tmp[...] = total[:, 0:128]
    v.fo_tmp2[...] = total[:, 128:256]
    for quarter in range(4):
        value = 0.0
        for which in range(2):
            rows = jnp.concatenate(
                [v.fo_tmp[pl.ds(which, 9, stride=2), :], v.fo_tmp2[pl.ds(which, 9, stride=2), :]], axis=1
            )
            value = value + nt(half_of(rows), split_pick(which, quarter))
        v.flat[pl.ds(MARGIN + quarter, 9, stride=4), :] = value
    v.flush.layer(starts[FLOW_OUT], 36)

    lane = lane_index((128, LANES))
    low_half = lane < 64
    even, odd = [], []
    total = 0.0
    for b in range(BATCH):
        total = total + ones_sum(quarter_of(v.grad_mask[b]))
    for block in range(5):
        wide = min(128, MASK - block * 128)
        at = BIAS_AT[MASK_OUT] + block
        v.gbias[at : at + 1, 0:wide] = total[:, block * 128 : block * 128 + wide]
        value = 0.0
        for b in range(BATCH):
            value = value + tn(v.mf[b], quarter_of(v.grad_mask[b, :, block * 128 : block * 128 + wide]))
        v.pair_a[:, 0:wide] = value
        even.append(v.pair_a[pl.ds(0, 128, stride=2), :])
        odd.append(pltpu.roll(v.pair_a[pl.ds(1, 128, stride=2), :], 64, 1))
    for i in range(4):
        v.flat[pl.ds(MARGIN + i, 128, stride=9), :] = even[i]
    v.flat[pl.ds(MARGIN + 4, 128, stride=9), :] = jnp.where(low_half, even[4], odd[0])
    for i in range(4):
        v.flat[pl.ds(MARGIN + 5 + i, 128, stride=9), :] = jnp.where(low_half, odd[i], odd[i + 1])
    v.flush.layer(starts[MASK_OUT], 1152)


def rows_back(v):
    v.back_state.receive()
    take_own(v, v.a_state, v.b_state)
    unpack_back(v, v.b_state, v.state)
    v.reduce.tick()
    v.back_context.receive()
    v.back_motion.receive()
    take_own(v, v.a_context, v.b_context)
    take_own(v, v.a_motion, v.b_motion)
    unpack_back(v, v.b_context, v.lr)
    unpack_back(v, v.b_motion, v.lu)

    def image(b, carry):
        at = pl.ds(pl.multiple_of(b * AREA, AREA), AREA)
        r = v.state[b]
        s = full_of(v.net[b])
        update, reset, cand = v.ru[b], v.rr[b], v.rc[b]
        cg = full_of(half_of(r * update * (1.0 - cand * cand)))
        spread_five(v, cg, None, 256, True)
        reset_grad = 0.0
        for t in range(5):
            reset_grad = reset_grad + nt(
                taps_part(v, t, 256, 384)[...], v.w_rs[t * 128 : (t + 1) * 128, 256:384]
            )
        low = full_of(half_of(r * (cand - s) * update * (1.0 - update)))
        high = full_of(half_of(reset_grad * s * reset * (1.0 - reset)))
        spread_five(v, low, None, 0, True)
        spread_five(v, high, None, 128, True)
        v.gr[b] = taps_part(v, 2, 0, 384)[...]
        state_grad = r * (1.0 - update) + reset_grad * reset
        inputs_grad = jnp.concatenate([v.lr[b], v.lu[b]], axis=1)
        for t in range(5):
            state_grad = state_grad + nt(taps_part(v, t, 0, 256)[...], v.w_rs[t * 128 : (t + 1) * 128, 0:256])
            inputs_grad = inputs_grad + nt(taps_part(v, t, 0, 384)[...], v.w_ri[t * 256 : (t + 1) * 256, :])
        v.ru[b] = state_grad
        v.rr[b] = inputs_grad[:, 0:128]
        motion = inputs_grad[:, 128:256]
        grad = half_of(motion * full_of(v.slope_m[b]))
        v.mge[b, 256:896, :] = grad
        high = half_of(motion)
        low = half_of(motion - full_of(high))
        pick = half_of(jnp.where(lane_index((16, LANES)) == row_index((16, LANES)) + 126, 1.0, 0.0))
        v.gf_base[b] = (nt(pick, high) + nt(pick, low))[0:8, :]
        return carry

    lax.fori_loop(0, BATCH, image, 0)
    v.halo_mg.start()
    v.store_gnet.start()
    v.store_gctx.start()


def gcorr_stores(v, b):
    return [
        pltpu.make_async_copy(v.mm_tmp.at[y * 328 : y * 328 + CORR], v.out_gcorr.at[b, y], v.gsem.at[y])
        for y in range(ROWS)
    ]


def branch_back(v):
    v.halo_mg.receive()

    def image(b, carry):
        up = jnp.where(v.spot > 0, full_of(v.mge[b, 0:256, :]), 0.0)
        own = full_of(v.mge[b, 256:896, :])
        down = jnp.where(v.spot < v.space - 1, full_of(v.mge[b, 896:1152, :]), 0.0)
        spread_rows(v, 0, (jnp.concatenate([up, own, down], axis=0),), 1152, v.xi, 0, 128, True)
        joint = 0.0
        for a in range(3):
            for c in range(3):
                k = (a * 3 + c) * 256
                joint = joint + nt(
                    v.xi[(2 - a) * 128 : (2 - a) * 128 + 896, c * 128 : (c + 1) * 128], v.w_mm[k : k + 256, :]
                )
        branch = joint * full_of(v.slope_j[b])
        low = full_of(half_of(edge_rows(v, branch[:, 0:128], WIDE)))
        high = full_of(half_of(edge_rows(v, branch[:, 128:256], WIDE)))
        spread_rows(v, 0, (low, high), 896, v.hx_j.at[b], 0, 256, True)
        return carry

    lax.fori_loop(0, BATCH, image, 0)


def branch_own(v, b, low=0, high=256):
    return v.hx_j[b, 128:768, 256 + low : 256 + high]


def flow_back(v):
    def image(b, carry):
        flow_grad = 0.0
        for a in range(3):
            rows = slice((2 - a) * 128, (2 - a) * 128 + 640)
            for c in range(3):
                k = a * 3 + c
                flow_grad = flow_grad + nt(
                    v.hx_j[b, rows, c * 256 + 128 : (c + 1) * 256], v.w_fm[k * 128 : (k + 1) * 128, :]
                )
        v.fpg[b] = half_of(flow_grad * full_of(v.slope_fi[b]))
        z = nt(v.w_fi[...], v.fpg[b])
        total = jnp.zeros((32, LANES), jnp.float32)
        lane = lane_index((32, LANES))
        for across in range(7):
            v.fs[across] = jnp.zeros((32, LANES), jnp.float32)
            for y in range(ROWS):
                v.fs[across, 2 * y : 2 * y + 16, :] += z[across * 16 : across * 16 + 16, y * 128 : (y + 1) * 128]
            d = across - 3
            value = v.fs[across]
            if d:
                value = pltpu.roll(value, d % LANES, 1)
                value = jnp.where((lane - d >= 0) & (lane - d < WIDE), value, 0.0)
            total = total + value
        v.gf[b] = total
        return carry

    lax.fori_loop(0, BATCH, image, 0)
    v.halo_gf.start()


def corr_back(v):
    def image(b, carry):
        corr_grad = 0.0
        for a in range(3):
            rows = slice((2 - a) * 128, (2 - a) * 128 + 640)
            for c in range(3):
                k = a * 3 + c
                corr_grad = corr_grad + nt(v.hx_j[b, rows, c * 256 : (c + 1) * 256], v.w_cm[k * 256 : (k + 1) * 256, :])
        v.cpg[b] = half_of(corr_grad * full_of(v.slope_ci[b]))
        stores = gcorr_stores(v, b)
        for store in stores:
            pl.when(b > 0)(store.wait)
        gcorr = nt(v.w_ci[...], v.cpg[b])
        for y in range(ROWS):
            v.mm_tmp[y * 328 : y * 328 + CORR, :] = gcorr[:, y * WIDE : (y + 1) * WIDE]
        for store in stores:
            store.start()
        return carry

    lax.fori_loop(0, BATCH, image, 0)


def summed(v, ref, name):
    total = 0.0
    for b in range(BATCH):
        total = total + ones_sum(ref(b))
    keep_bias(v, name, total)


def gradients_motion(v):
    starts = flat_rows()[0]
    summed(v, lambda b: v.mge[b, 256:896, :], MOTION_MIX)
    for k in range(9):
        a, c = k // 3, k % 3
        value = 0.0
        for b in range(BATCH):
            value = value + tn(
                v.hx_j[b, a * 128 : a * 128 + 640, c * 256 : (c + 1) * 256], v.mge[b, 256:896, :]
            )
        v.mm_tmp[k * 256 : (k + 1) * 256, :] = value
    lane36 = lane_index((36, LANES))
    for r in range(63):
        first = v.mm_tmp[pl.ds(r, 36, stride=64), :]
        second = v.mm_tmp[pl.ds(r + 1, 36, stride=64), :]
        if r:
            first = pltpu.roll(first, LANES - 2 * r, 1)
        second = pltpu.roll(second, 126 - 2 * r, 1)
        v.flat[pl.ds(MARGIN + r, 36, stride=63), :] = jnp.where(lane36 < 126 - 2 * r, first, second)
    v.flush.layer(starts[MOTION_MIX], 2268)


def gradients_branches(v):
    starts = flat_rows()[0]
    summed(v, lambda b: branch_own(v, b), CORR_MIX)
    summed(v, lambda b: branch_own(v, b, 128, 256), FLOW_MIX)
    for k in range(9):
        a, c = k // 3, k % 3
        value = 0.0
        for b in range(BATCH):
            value = value + tn(
                v.hx_f[b, (a + 1) * 128 : (a + 1) * 128 + 640, c * 128 : (c + 1) * 128], branch_own(v, b, 128, 256)
            )
        v.pair_a[0:128, :] = value
        even, odd = (v.pair_a[pl.ds(i, 64, stride=2), :] for i in range(2))
        v.flat[MARGIN + 64 * k : MARGIN + 64 * (k + 1), :] = jnp.where(
            lane_index((64, LANES)) < 64, pltpu.roll(even, 64, 1), odd
        )
    v.flush.layer(starts[FLOW_MIX], 576)

    low_half = lane_index((128, LANES)) < 64
    for k in range(9):
        a, c = k // 3, k % 3
        value = 0.0
        for b in range(BATCH):
            value = value + tn(
                v.hx_c[b, (a + 1) * 128 : (a + 1) * 128 + 640, c * 256 : (c + 1) * 256], branch_own(v, b)
            )
        v.pair_a[...] = value[:, 0:128]
        v.pair_b[...] = value[:, 128:256]
        even, odd = (v.pair_a[pl.ds(i, 128, stride=2), :] for i in range(2))
        even_high, odd_high = (v.pair_b[pl.ds(i, 128, stride=2), :] for i in range(2))
        odd, odd_high = pltpu.roll(odd, 64, 1), pltpu.roll(odd_high, 64, 1)
        at = MARGIN + 384 * k
        v.flat[pl.ds(at, 128, stride=3), :] = even
        v.flat[pl.ds(at + 1, 128, stride=3), :] = jnp.where(low_half, even_high, odd)
        v.flat[pl.ds(at + 2, 128, stride=3), :] = jnp.where(low_half, odd, odd_high)
        if k == 4:
            v.reduce.tick()
    v.flush.layer(starts[CORR_MIX], 3456)


def gradients_flow_in(v):
    starts = flat_rows()[0]
    summed(v, lambda b: v.fpg[b], FLOW_IN)
    value = 0.0
    for b in range(BATCH):
        value = value + mm(v.xt[b, :, 256:896], v.fpg[b])
    v.flow_tmp[...] = value
    for across in range(7):
        for comp in range(2):
            v.flat[pl.ds(MARGIN + across * 2 + comp, 7, stride=14), :] = v.flow_tmp[
                pl.ds(across * 16 + comp, 7, stride=2), :
            ]
    v.flush.layer(starts[FLOW_IN], 98)


def gradients_corr_in(v):
    starts = flat_rows()[0]
    summed(v, lambda b: v.cpg[b], CORR_IN)
    value = 0.0
    for b in range(BATCH):
        value = value + mm(lines_of(v.corr, b, ROWS), v.cpg[b])
    pack_pairs(v.flat, 0, 324, value[:, 0:128], value[:, 128:256])
    v.flush.layer(starts[CORR_IN], 648)


def bias_tile(v):
    starts, bias_row, spots, inner = flat_rows()
    lead = bias_row % 16
    lane1 = lane_index((1, LANES))
    v.bown[...] = jnp.zeros_like(v.bown)
    for name, height, width in shapes():
        for block in range(-(-width // LANES)):
            value = v.gbias[BIAS_AT[name] + block : BIAS_AT[name] + block + 1, :]
            if name == FLOW_MIX:
                value = pltpu.roll(value, 64, 1)
            left = width - block * LANES
            if left < LANES:
                value = jnp.where(lane1 < left, value, 0.0)
            at = spots[name] + block * LANES
            row, shift = lead + at // LANES, at % LANES
            moved = pltpu.roll(value, shift, 1) if shift else value
            v.bown[row : row + 1, :] = v.bown[row : row + 1, :] + jnp.where(lane1 >= shift, moved, 0.0)
            if shift:
                v.bown[row + 1 : row + 2, :] = v.bown[row + 1 : row + 2, :] + jnp.where(lane1 < shift, moved, 0.0)


def finish(v):
    spot, last = v.spot, v.space - 1
    v.halo_gf.receive()
    for b in range(BATCH):
        v.tmp2[...] = v.gf[b]
        up = jnp.where(spot > 0, v.gf_up[b], 0.0)
        down = jnp.where(spot < last, v.gf_down[b], 0.0)
        v.tmp2[6:12, :] += up[16:22, :]
        v.tmp2[10:16, :] += down[0:6, :]
        for y in range(ROWS):
            v.out_gflow[b, 2 * y : 2 * y + 2, :] = (
                v.tmp2[6 + 2 * y : 8 + 2 * y, :] + v.gf_base[b, 0:2, y * 128 : (y + 1) * 128]
            )
    v.loss_in[v.spot] = v.losses[...]
    total = jnp.sum(v.loss_in[...], axis=0)
    counts = jnp.sum(v.counts[...], axis=0)
    v.out_loss[...] = total / jnp.maximum(counts, 1.0)


class View:
    pass


def main_kernel(names, space, count, *refs):
    v = View()
    for name, ref in zip(names, refs):
        setattr(v, name, ref)
    v.space = space
    v.lu, v.lc = v.motion, v.state
    v.spot = lax.axis_index(SPACE)
    v.rank = lax.axis_index(DP)
    v.mate, v.other, v.twin = mate_of(v.rank), lax.rem(v.rank + 2, 4), mate_of(v.spot)
    spot = v.spot
    barrier = pltpu.get_barrier_semaphore()

    def hello(step, carry):
        pl.semaphore_signal(barrier, inc=1, device_id={SPACE: lax.rem(spot + step, space)}, device_id_type=MESH)
        return carry

    lax.fori_loop(1, space, hello, 0)
    for turn in range(1, 4):

        def greet_rank(step, carry):
            place = lax.rem(spot + 2 * step, space)
            device = {DP: lax.rem(v.rank + turn, 4), SPACE: place}
            pl.semaphore_signal(barrier, inc=1, device_id=device, device_id_type=MESH)
            return carry

        lax.fori_loop(0, space // 2, greet_rank, 0)
    pl.semaphore_wait(barrier, space - 1 + 3 * (space // 2))

    v.store_gnet = pltpu.make_async_copy(v.ru, v.out_gnet, v.osem.at[0])
    v.store_gctx = pltpu.make_async_copy(v.rr, v.out_gctx, v.osem.at[1])
    rows = row_index((8, LANES))
    counted = jnp.zeros((8, LANES), jnp.float32)
    for b in range(BATCH):
        counted = jnp.where(rows == b, jnp.sum(v.valid[b, 0:1, :]), counted)
    v.count_out[...] = counted
    v.pick_count = lambda counts, b: jnp.sum(jnp.where((rows == b) & (lane_index((8, LANES)) == 0), counts, 0.0))
    v.swap_count = Swap(v, 0, v.count_out, v.counts, True)
    v.swap_context = Swap(v, 1, v.a_context, v.b_context)
    v.swap_motion = Swap(v, 2, v.a_motion, v.b_motion)
    v.swap_state = Swap(v, 3, v.a_state, v.b_state)
    v.back_context = Swap(v, 4, v.a_context, v.b_context)
    v.back_motion = Swap(v, 5, v.a_motion, v.b_motion)
    v.back_state = Swap(v, 6, v.a_state, v.b_state)
    v.swap_loss = Swap(v, 7, v.losses, v.loss_in, True)
    v.halo_corr = Halo(v, 0, v.corr.at[:, 0:2], v.corr.at[:, 3:5], v.corr_down, v.corr_up)
    v.halo_flow = Halo(v, 1, v.flow, v.flow, v.flow_down, v.flow_up)
    v.halo_final = Halo(v, 2, v.e_left, v.e_right, v.f_right, v.f_left)
    v.halo_mask = Halo(v, 3, v.m_left, v.m_right, v.n_right, v.n_left)
    v.halo_dg = Halo(v, 4, v.dg, v.dg, v.dg_right, v.dg_left)
    v.halo_mg = Halo(v, 5, v.mge.at[:, 256:512], v.mge.at[:, 640:896], v.mge.at[:, 896:1152], v.mge.at[:, 0:256])
    v.halo_gf = Halo(v, 6, v.gf, v.gf, v.gf_down, v.gf_up)

    load = pltpu.make_async_copy(v.local, v.gath.at[0:BLOCK], v.gsend.at[4, 2])
    load.start()
    v.halo_flow.start()
    v.halo_corr.start()
    v.swap_count.start()
    load.wait()
    gather_start(v, count)

    def first(b, carry):
        v.state[b] = full_of(v.context[b])
        pack_rows(v, v.state, b, v.a_context)
        return carry

    lax.fori_loop(0, BATCH, first, 0)
    v.swap_context.start()
    v.halo_flow.receive()
    gather_pass(v, 0, 2)
    early_taps(v)
    gather_pass(v, 2, 4)
    columns_zero(v)
    gather_end(v)
    unpack_encoder(v, count)
    v.halo_corr.receive()
    forward_rows(v)
    keep = [pltpu.make_async_copy(v.hx_c, v.out_keep_c, v.ksem.at[0]), pltpu.make_async_copy(v.hx_f, v.out_keep_f, v.ksem.at[1])]
    for copy in keep:
        copy.start()
    unpack_heads(v)
    mask_gradient(v)
    v.swap_context.receive()
    v.swap_motion.receive()
    v.swap_state.receive()
    take_own(v, v.a_context, v.b_context)
    take_own(v, v.a_motion, v.b_motion)
    take_own(v, v.a_state, v.b_state)
    columns_in(v)
    columns_forward(v)
    for copy in keep:
        copy.wait()
    heads(v)
    mask_output(v)
    v.swap_context.sent()
    v.swap_motion.sent()
    v.swap_state.sent()
    heads_back(v)
    v.flush = Flush(v)
    red = v.reduce = Reduce(v, count)
    gradients_heads(v)
    red.offer(0)
    red.tick()
    gradients_gru(
        v,
        COLUMNS_GATES,
        COLUMNS_CANDIDATE,
        lambda t: (
            lambda b: v.xc[b, t * COLS : t * COLS + AREA, 0:128],
            lambda b: v.xc[b, t * COLS : t * COLS + AREA, 128:384],
            lambda b: v.xcr[b, t * COLS : t * COLS + AREA, :],
        ),
        lambda b, low=0, high=384: v.gc[b, 32 : 32 + AREA, low:high],
    )
    red.offer(1, 2)
    red.tick()
    rows_back(v)
    red.tick()
    keep = [
        pltpu.make_async_copy(v.out_keep_c, v.hx_c, v.ksem.at[0]),
        pltpu.make_async_copy(v.out_keep_f, v.hx_f, v.ksem.at[1]),
    ]
    for copy in keep:
        copy.start()
    gradients_gru(
        v,
        ROWS_GATES,
        ROWS_CANDIDATE,
        lambda t: (
            lambda b: v.xs[b * AREA : (b + 1) * AREA, t * 128 : (t + 1) * 128],
            lambda b: v.xi[b * AREA : (b + 1) * AREA, t * 256 : (t + 1) * 256],
            lambda b: v.xr[b * AREA : (b + 1) * AREA, t * 128 : (t + 1) * 128],
        ),
        lambda b, low=0, high=384: v.gr[b, :, low:high],
    )
    red.offer(3, 4)
    red.tick()
    gradients_motion(v)
    red.offer(5)
    red.tick()
    branch_back(v)
    red.tick()
    for copy in keep:
        copy.wait()
    gradients_branches(v)
    red.offer(6)
    red.tick()
    flow_back(v)
    gradients_flow_in(v)
    red.offer(7)
    red.tick()
    corr_back(v)
    gradients_corr_in(v)
    bias_tile(v)
    red.bias_core()
    red.offer(8)
    red.tick()
    for store in gcorr_stores(v, 0):
        store.wait()
    finish(v)
    red.bias_across()
    red.tick()
    red.bias_stripes()
    red.tick()
    red.bias_end()
    red.ready()
    red.tick()
    pl.when(v.rank > 0)(lambda: red.lay(0, 24))
    red.tick()
    pl.when(v.rank == 0)(lambda: red.lay(5, 24))
    red.tick()
    assert not red.flying and not red.queue
    pl.when(v.rank == 0)(lambda: red.lay(0, 5))
    red.settle()
    for swap in (v.swap_count, v.back_context, v.back_motion, v.back_state, v.swap_loss):
        swap.sent()
    for halo in (v.halo_corr, v.halo_flow, v.halo_final, v.halo_mask, v.halo_dg, v.halo_mg, v.halo_gf):
        halo.sent()
    v.store_gnet.wait()
    v.store_gctx.wait()
    pltpu.make_async_copy(v.mask_low, v.out_mask.at[0], v.osem.at[3]).wait()


def main_call(space, count, local, net, context, corr, flow, target, valid, grad_net, grad_mask):
    total = 3 * count // (LANES * 16) * 16 + BLOCK
    low, wide = jnp.bfloat16, jnp.float32
    peers = (space, BATCH, ROWS * COLS, LANES)
    ins = dict(
        local=local, net=net, context=context, corr=corr, flow=flow, target=target, valid=valid,
        grad_net=grad_net, grad_mask=grad_mask,
    )
    outs = dict(
        out_net=((BATCH, AREA, 128), low),
        out_flow=((BATCH, 8, SPAN), wide),
        out_mask=((BATCH, AREA, MASK), low),
        out_loss=((8, 128), wide),
        out_flat=((total, 128), low),
        out_gnet=((BATCH, AREA, 128), wide),
        out_gctx=((BATCH, AREA, 128), wide),
        out_gcorr=((BATCH, ROWS, CORR, 128), wide),
        out_gflow=((BATCH, 16, 128), wide),
        out_keep_c=((BATCH, 1152, 768), low),
        out_keep_f=((BATCH, 1152, 384), low),
        out_all=((4 * BLOCK, 128), low),
        out_grads=((BLOCK, 128), wide),
    )
    scratch = dict(
        stage=((2, 3904, 128), low),
        seam=((16, 16, 128), wide),
        mask_low=((AREA, MASK), low),
        gout=((2, 256, 128), wide),
        seam_low=((16 * 20, 128), low),
        own=((2, SHARE // 2, 128), low),
        rcore=((2, SHARE // 2, 128), low),
        tx=((2, SHARE // 4, 128), low),
        rx=((2, SHARE // 4, 128), low),
        ks=((2, SHARE // 4, 128), wide),
        ts=((2, SHARE // 4, 128), low),
        acc=((2, SHARE // 4 // space, 128), wide),
        rs=((2, space, SHARE // 4 // space, 128), low),
        fin=((2, SHARE // 4 // space, 128), low),
        gath=((2 * SHARE + 32, 128), low),
        bown=((32, 128), wide), bcore=((32, 128), wide), btwo=((32, 128), wide), bacross=((32, 128), wide),
        bfour=((32, 128), wide), ball=((space, 32, 128), wide), bsum=((32, 128), wide),
        flat=((3904, 128), wide),
        pair_a=((256, 128), wide),
        pair_b=((256, 128), wide),
        flow_tmp=((112, 128), wide),
        mm_tmp=((3 * (2 * EDGE + SPREAD), 128), wide),
        fo_tmp=((32, 128), wide),
        fo_tmp2=((32, 128), wide),
        w_ci=((CORR, 256), low),
        w_cm=((2304, 256), low),
        w_fi=((112, 128), low),
        w_fm=((1152, 128), low),
        w_mm=((2304, 128), low),
        w_ri=((1280, 384), low),
        w_rs=((640, 384), low),
        w_li=((1280, 384), low),
        w_ls=((640, 384), low),
        w_h=((1152, 512), low),
        w_fo=((32, 256), low),
        w_mo=((256, 640), low),
        bias=((BIAS_ROWS, 128), wide),
        gbias=((BIAS_ROWS, 128), wide),
        corr_up=((BATCH, 2, CORR, 128), low),
        corr_down=((BATCH, 2, CORR, 128), low),
        flow_up=((BATCH, 16, 128), wide),
        flow_down=((BATCH, 16, 128), wide),
        fs=((7, 32, 128), wide),
        xt=((BATCH, 112, 1152), low),
        tmp=((1168, 128), wide),
        tmp2=((32, 128), wide),
        hx_c=((BATCH, 1152, 768), low),
        hx_f=((BATCH, 1152, 384), low),
        hx_j=((BATCH, 896, 768), low),
        slope_ci=((BATCH, AREA, 256), low),
        slope_fi=((BATCH, AREA, 128), low),
        slope_j=((BATCH, 896, 256), low),
        slope_m=((BATCH, AREA, 128), low),
        motion=((BATCH, AREA, 128), wide),
        state=((BATCH, AREA, 128), wide),
        xi=((BATCH * AREA, 1280), low),
        xs=((BATCH * AREA, 640), low),
        xr=((BATCH * AREA, 640), low),
        ru=((BATCH, AREA, 128), wide),
        rr=((BATCH, AREA, 128), wide),
        rc=((BATCH, AREA, 128), wide),
        lr=((BATCH, AREA, 128), wide),
        a_state=(peers, low), a_context=(peers, low), a_motion=(peers, low),
        b_state=(peers, low), b_context=(peers, low), b_motion=(peers, low),
        xc=((BATCH, AREA + 64, 384), low),
        xcr=((BATCH, AREA + 64, 128), low),
        gc=((BATCH, AREA + 64, 384), low),
        final=((AREA, 128), wide),
        e_left=((BATCH, 2, 48, 128), low), e_right=((BATCH, 2, 48, 128), low),
        f_left=((BATCH, 2, 48, 128), low), f_right=((BATCH, 2, 48, 128), low),
        m_left=((BATCH, 2, 48, 128), low), m_right=((BATCH, 2, 48, 128), low),
        n_left=((BATCH, 2, 48, 128), low), n_right=((BATCH, 2, 48, 128), low),
        slope_h=((BATCH, SPREAD, 512), low),
        feat=((BATCH, SPAN, 256), low),
        mf=((BATCH, AREA, 256), low),
        zt=((32, SPAN), wide),
        dg=((BATCH, 8, SPAN), wide),
        dg_left=((BATCH, 8, SPAN), wide), dg_right=((BATCH, 8, SPAN), wide),
        dt=((32, SPAN), wide),
        dto=((32, SPAN), wide),
        dtb=((BATCH, 32, SPAN), low),
        hgo=((BATCH, SPREAD, 512), low),
        gr=((BATCH, AREA, 384), low),
        mge=((BATCH, 1152, 128), low),
        cpg=((BATCH, AREA, 256), low),
        fpg=((BATCH, AREA, 128), low),
        gf_base=((BATCH, 8, AREA), wide),
        gf=((BATCH, 32, 128), wide), gf_up=((BATCH, 32, 128), wide), gf_down=((BATCH, 32, 128), wide),
        count_out=((8, 128), wide), counts=((space, 8, 128), wide),
        losses=((8, 128), wide), loss_in=((space, 8, 128), wide),
    )
    sems = dict(
        hsend=pltpu.SemaphoreType.DMA((7, 2)), hrecv=pltpu.SemaphoreType.DMA((7, 2)),
        asend=pltpu.SemaphoreType.DMA((9, space)), arecv=pltpu.SemaphoreType.DMA((9, space)),
        ssem=pltpu.SemaphoreType.DMA((2, 2)),
        fsem=pltpu.SemaphoreType.DMA((17,)),
        rsend=pltpu.SemaphoreType.DMA((2, 2)), rrecv=pltpu.SemaphoreType.DMA((2, 2)),
        rlocal=pltpu.SemaphoreType.DMA((2,)),
        s2send=pltpu.SemaphoreType.DMA((2, space)), s2recv=pltpu.SemaphoreType.DMA((2, space)),
        fsend=pltpu.SemaphoreType.DMA((2, space // 2)), frecv=pltpu.SemaphoreType.DMA((9, 4, space // 2)),
        ysend=pltpu.SemaphoreType.DMA((9, 4)), yrecv=pltpu.SemaphoreType.DMA((9, 4)),
        bsend=pltpu.SemaphoreType.DMA((2,)), brecv=pltpu.SemaphoreType.DMA((2,)),
        ksem=pltpu.SemaphoreType.DMA((2,)),
        gsend=pltpu.SemaphoreType.DMA((5, 4)), grecv=pltpu.SemaphoreType.DMA((5, 4)),
        gsem=pltpu.SemaphoreType.DMA((ROWS,)),
        osem=pltpu.SemaphoreType.DMA((6,)),
    )
    vmem = pl.BlockSpec(memory_space=pltpu.VMEM)
    hbm = pl.BlockSpec(memory_space=pl.ANY)
    names = list(ins) + list(outs) + list(scratch) + list(sems)
    return pl.pallas_call(
        functools.partial(main_kernel, names, space, count),
        out_shape=[jax.ShapeDtypeStruct(*entry) for entry in outs.values()],
        in_specs=[hbm if name == "local" else vmem for name in ins],
        out_specs=[hbm if name in ("out_flat", "out_gnet", "out_gctx", "out_gcorr", "out_keep_c", "out_keep_f", "out_mask", "out_grads", "out_all") else vmem for name in outs],
        scratch_shapes=[pltpu.VMEM(*entry) for entry in scratch.values()] + list(sems.values()),
        compiler_params=pltpu.CompilerParams(
            collective_id=2, has_side_effects=True, vmem_limit_bytes=VMEM_LIMIT
        ),
    )(*ins.values())


VMEM_LIMIT = 64 * 2**20 - 2**17


def shards_wide(net, context, corr, flow, target, valid, grad_net, grad_mask, params):
    space = lax.axis_size(SPACE)
    count = params.shape[0]
    local = jnp.pad(params, (0, BLOCK * LANES - count)).reshape(BLOCK, LANES)
    flow_rows = jnp.transpose(flow.astype(jnp.float32), (0, 2, 1, 3)).reshape(BATCH, 2 * ROWS, WIDE)
    flow_rows = jnp.pad(flow_rows, ((0, 0), (0, 16 - 2 * ROWS), (0, 0)))
    pad = ((0, 0), (0, 0), (0, 0), (2, 2))
    target_ext = jnp.pad(target, pad).reshape(BATCH, 2, SPREAD)
    target_ext = jnp.pad(target_ext, ((0, 0), (0, 6), (0, SPAN - SPREAD)))
    valid_ext = jnp.pad(valid.astype(jnp.float32)[:, None], pad).reshape(BATCH, 1, SPREAD)
    valid_ext = jnp.broadcast_to(jnp.pad(valid_ext, ((0, 0), (0, 0), (0, SPAN - SPREAD))), (BATCH, 8, SPAN))
    outs = main_call(
        space, count, local, net.reshape(BATCH, AREA, HID), context.reshape(BATCH, AREA, CTX),
        jnp.transpose(corr, (0, 1, 3, 2)), flow_rows, target_ext, valid_ext,
        grad_net.reshape(BATCH, AREA, HID), grad_mask.reshape(BATCH, AREA, MASK),
    )
    new_net, new_flow, mask, loss, _, gnet, gctx, gcorr, gflow = outs[:9]
    new_flow = new_flow[:, 0:2, 0:SPREAD].reshape(BATCH, 2, TALL, PITCH)[..., 2 : 2 + COLS]
    grads = outs[-1].reshape(-1)[:count]
    return (
        new_net.reshape(BATCH, TALL, COLS, HID),
        new_flow,
        mask.reshape(BATCH, TALL, COLS, MASK),
        loss[0:BATCH, 0],
        grads,
        gnet.reshape(BATCH, ROWS, WIDE, HID),
        gctx.reshape(BATCH, ROWS, WIDE, CTX),
        jnp.transpose(gcorr, (0, 1, 3, 2)),
        jnp.transpose(gflow[:, 0 : 2 * ROWS].reshape(BATCH, ROWS, 2, WIDE), (0, 2, 1, 3)),
    )


def solution(mesh):
    def plan(*arrays):
        net, valid = arrays[0], arrays[5]
        if (net.shape[1:3], valid.shape[1:]) == ((ROWS, WIDE), (TALL, COLS)):
            return shards_wide(*arrays)
        return shards(*arrays)

    return jax.shard_map(
        plan,
        mesh=mesh,
        in_specs=(
            P(DP, SPACE, None, None),
            P(DP, SPACE, None, None),
            P(DP, SPACE, None, None),
            P(DP, None, SPACE, None),
            P(DP, None, None, SPACE),
            P(DP, None, SPACE),
            P(DP, None, SPACE, None),
            P(DP, None, SPACE, None),
            P(DP),
        ),
        out_specs=(
            P(DP, None, SPACE, None),
            P(DP, None, None, SPACE),
            P(DP, None, SPACE, None),
            P(DP),
            P(DP),
            P(DP, SPACE, None, None),
            P(DP, SPACE, None, None),
            P(DP, SPACE, None, None),
            P(DP, None, SPACE, None),
        ),
        check_vma=False,
    )
```

```python
import functools

import jax
import jax.numpy as jnp
from jax import lax
from jax.experimental import pallas as pl
from jax.experimental.pallas import tpu as pltpu
from jax.sharding import PartitionSpec as P

HID = 128
CTX = 128
MOT = 128
CORR = 324
SPACE = "space"
DP = "dp"
(
    CORR_IN,
    CORR_MIX,
    FLOW_IN,
    FLOW_MIX,
    MOTION_MIX,
    ROWS_GATES,
    ROWS_CANDIDATE,
    COLUMNS_GATES,
    COLUMNS_CANDIDATE,
    FLOW_HIDDEN,
    FLOW_OUT,
    MASK_HIDDEN,
    MASK_OUT,
) = range(13)
C1 = 256
C2 = 192
F1 = 128
F2 = 64
HEAD = 256
MASK = 576


def with_halo(block, sides, width):
    for axis, dim in sides:
        count = lax.axis_size(axis)
        forward = [(i, i + 1) for i in range(count - 1)]
        backward = [(target, source) for source, target in forward]
        low = lax.ppermute(
            lax.slice_in_dim(block, block.shape[dim] - width, None, axis=dim), axis, forward
        )
        high = lax.ppermute(lax.slice_in_dim(block, 0, width, axis=dim), axis, backward)
        block = jnp.concatenate([low, block, high], axis=dim)
    return block


def shapes():
    inputs_width = HID + CTX + MOT
    return [
        (CORR_IN, CORR, C1),
        (CORR_MIX, 9 * C1, C2),
        (FLOW_IN, 98, F1),
        (FLOW_MIX, 9 * F1, F2),
        (MOTION_MIX, 9 * (C2 + F2), MOT - 2),
        (ROWS_GATES, 5 * inputs_width, 2 * HID),
        (ROWS_CANDIDATE, 5 * inputs_width, HID),
        (COLUMNS_GATES, 5 * inputs_width, 2 * HID),
        (COLUMNS_CANDIDATE, 5 * inputs_width, HID),
        (FLOW_HIDDEN, 9 * HID, HEAD),
        (FLOW_OUT, 9 * HEAD, 2),
        (MASK_HIDDEN, 9 * HID, HEAD),
        (MASK_OUT, HEAD, MASK),
    ]


def unpack(flat):
    weights = {}
    biases = {}
    offset = 0
    table = shapes()
    for name, height, width in table:
        weights[name] = flat[offset // LANES : (offset + height * width) // LANES].reshape(height, width)
        offset = offset + height * width
    rest = flat[offset // LANES :].reshape(-1)
    offset = 0
    for name, height, width in table:
        biases[name] = rest[offset : offset + width].astype(jnp.float32)
        offset = offset + width
    return (weights, biases)


def pack(grads, total):
    table = shapes()
    rows = [grads[entry[0]][0].astype(jnp.bfloat16).reshape(-1, LANES) for entry in table]
    biases = jnp.concatenate([grads[entry[0]][1] for entry in table]).astype(jnp.bfloat16)
    left = total * LANES - sum(entry[1] * entry[2] for entry in table) - biases.shape[0]
    return jnp.concatenate(rows + [jnp.pad(biases, (0, left)).reshape(-1, LANES)])


def patches(padded, tall, wide):
    out_rows = padded.shape[1] - tall + 1
    out_columns = padded.shape[2] - wide + 1
    return jnp.concatenate(
        [
            padded[:, down : down + out_rows, across : across + out_columns]
            for down in range(tall)
            for across in range(wide)
        ],
        axis=-1,
    )


def apply(stacked, weight):
    return jnp.einsum("bhwk,ko->bhwo", stacked, weight, preferred_element_type=jnp.float32)


def apply_back(grad, weight):
    return jnp.einsum("bhwo,ko->bhwk", grad, weight, preferred_element_type=jnp.float32)


def weight_grad(stacked, pre_grad):
    return jnp.einsum("bhwk,bhwo->ko", stacked, pre_grad, preferred_element_type=jnp.float32)


def record(grads, name, stacked, pre_grad):
    grads[name] = (
        weight_grad(stacked, pre_grad),
        jnp.sum(pre_grad, axis=(0, 1, 2), dtype=jnp.float32),
    )


def flipped(weight, tall, wide):
    inner = weight.shape[0] // (tall * wide)
    shaped = weight.reshape(tall, wide, inner, weight.shape[1])[::-1, ::-1]
    return jnp.transpose(shaped, (0, 1, 3, 2)).reshape(-1, inner)


def slope(pre):
    sigma = jax.nn.sigmoid(pre)
    return sigma * (1.0 + pre * (1.0 - sigma))


def local_pad(field, tall, wide):
    return jnp.pad(field, ((0, 0), (tall // 2, tall // 2), (wide // 2, wide // 2), (0, 0)))


def row_pad(field, tall):
    field = with_halo(field, ((SPACE, 1),), tall // 2)
    return jnp.pad(field, ((0, 0), (0, 0), (tall // 2, tall // 2), (0, 0)))


def column_pad(field, tall, wide):
    field = with_halo(field, ((SPACE, 2),), wide // 2)
    return jnp.pad(field, ((0, 0), (tall // 2, tall // 2), (0, 0), (0, 0)))


MESH = pl.DeviceIdType.MESH
LANES = 128
BLOCK = 6144


def quarter_start(rank, count):
    return lax.div(rank * count, LANES)


def quarter_base(rank, count):
    return lax.div(rank * count, LANES * 16) * 16


def mate_of(rank):
    return rank + 1 - 2 * lax.rem(rank, 2)


def remote(src, dst, send, recv, device):
    return pltpu.make_async_remote_copy(
        src_ref=src, dst_ref=dst, send_sem=send, recv_sem=recv, device_id=device, device_id_type=MESH
    )


def greet(devices):
    barrier = pltpu.get_barrier_semaphore()
    for device in devices:
        pl.semaphore_signal(barrier, inc=1, device_id=device, device_id_type=MESH)
    pl.semaphore_wait(barrier, len(devices))


def lane_matrix(shift, forward):
    source = lax.broadcasted_iota(jnp.int32, (LANES, 2 * LANES), 0)
    target = lax.broadcasted_iota(jnp.int32, (LANES, 2 * LANES), 1)
    if forward:
        return jnp.where(target == source + shift, 1.0, 0.0).astype(jnp.bfloat16)
    return jnp.where(lax.rem(target + LANES, 2 * LANES) == source - shift + LANES, 1.0, 0.0).astype(jnp.bfloat16)


def gather_kernel(count, local_ref, out_ref, own_ref, send, recv):
    rank, spot = lax.axis_index(DP), lax.axis_index(SPACE)
    mate, across, twin = mate_of(rank), lax.rem(rank + 2, 4), mate_of(spot)
    pieces = 4
    rows = BLOCK // 2 // pieces
    peers = ({DP: mate}, {DP: across}, {SPACE: twin})
    greet(peers)
    matrix = lane_matrix(lax.rem(rank * count, LANES), True)
    first = lax.broadcasted_iota(jnp.int32, (256, LANES), 0) == 0

    def rotate(step, carry):
        at = pl.ds(pl.multiple_of(step * 256, 256), 256)
        both = jnp.dot(local_ref[at, :], matrix, preferred_element_type=jnp.float32)
        spill = pltpu.roll(both[:, LANES:], 1, 0)
        own_ref[at, :] = (both[:, :LANES] + jnp.where(first, carry, spill)).astype(jnp.bfloat16)
        return spill[0:1]

    lax.fori_loop(0, BLOCK // 256, rotate, jnp.zeros((1, LANES), jnp.float32))

    half, other_half = lax.rem(spot, 2), lax.rem(spot + 1, 2)

    def piece(which, index):
        return pl.ds(pl.multiple_of(which * (BLOCK // 2) + index * rows, 16), rows)

    own_x = [
        remote(own_ref.at[piece(half, k)], out_ref.at[rank, piece(half, k)], send.at[0, k], recv.at[0, k], peers[1])
        for k in range(pieces)
    ]
    own_c = remote(own_ref, out_ref.at[rank], send.at[4, 0], recv.at[4, 0], peers[0])
    for copy in own_x:
        copy.start()
    own_c.start()
    later = []
    for k in range(pieces):
        own_x[k].wait_recv()
        block = out_ref.at[across, piece(half, k)]
        to_twin = remote(block, block, send.at[1, k], recv.at[1, k], peers[2])
        to_mate = remote(block, block, send.at[2, k], recv.at[2, k], peers[0])
        to_twin.start()
        to_mate.start()
        later.append((to_twin, to_mate))
    for at in range(BLOCK // 256):
        out_ref[rank, at * 256 : (at + 1) * 256, :] = own_ref[at * 256 : (at + 1) * 256, :]
    for k in range(pieces):
        later[k][0].wait_recv()
        block = out_ref.at[across, piece(other_half, k)]
        to_mate = remote(block, block, send.at[3, k], recv.at[3, k], peers[0])
        to_mate.start()
        later.append((to_mate,))
    for k in range(pieces):
        own_x[k].wait_send()
        later[k][0].wait_send()
        later[k][1].wait()
        later[pieces + k][0].wait()
    own_c.wait()


def gather_blocks(params):
    count = params.shape[0]
    local = jnp.pad(params, (0, BLOCK * LANES - count)).reshape(BLOCK, LANES)
    return pl.pallas_call(
        functools.partial(gather_kernel, count),
        out_shape=jax.ShapeDtypeStruct((4, BLOCK, LANES), jnp.bfloat16),
        in_specs=[pl.BlockSpec(memory_space=pltpu.VMEM)],
        out_specs=pl.BlockSpec(memory_space=pltpu.VMEM),
        scratch_shapes=[
            pltpu.VMEM((BLOCK, LANES), jnp.bfloat16),
            pltpu.SemaphoreType.DMA((5, 4)),
            pltpu.SemaphoreType.DMA((5, 4)),
        ],
        compiler_params=pltpu.CompilerParams(
            collective_id=0, has_side_effects=True, vmem_limit_bytes=32 * 2**20
        ),
    )(local)


def gather_params(params):
    count = params.shape[0]
    blocks = gather_blocks(params)
    pieces = []
    reach = 0
    for rank in range(4):
        start = rank * count // LANES
        stop = -(-(rank + 1) * count // LANES)
        head = blocks[rank, :1] if rank == 0 else blocks[rank, :1] + pieces.pop()
        pieces += [head, blocks[rank, 1 : stop - start - 1], blocks[rank, stop - start - 1 : stop - start]]
    return jnp.concatenate(pieces)


def reduce_kernel(count, space, pieces, grads_ref, out_ref, rc, tx, rx, acc, ty, ry, tz, rz, gath, send, recv, zsend, zrecv):
    rank, spot = lax.axis_index(DP), lax.axis_index(SPACE)
    mate, across, twin = mate_of(rank), lax.rem(rank + 2, 4), mate_of(spot)
    group = space // 2
    side, depth = lax.rem(spot, 2), lax.div(spot, 2)
    rows = BLOCK // pieces
    half = rows // 2
    part = half // group

    def partner(step):
        return lax.rem(depth + step, group)

    peers = [{DP: mate}, {DP: across}, {SPACE: twin}]
    barrier = pltpu.get_barrier_semaphore()
    for device in peers:
        pl.semaphore_signal(barrier, inc=1, device_id=device, device_id_type=MESH)

    def hello(step, carry):
        pl.semaphore_signal(barrier, inc=1, device_id={SPACE: partner(step) * 2 + side}, device_id_type=MESH)
        return carry

    lax.fori_loop(1, group, hello, 0)
    pl.semaphore_wait(barrier, 3 + group - 1)

    gath[BLOCK:, :] = jnp.zeros((32, LANES), jnp.bfloat16)
    lower = lax.rem(rank, 2)
    upper = lax.div(rank, 2)

    def base(who):
        return pl.multiple_of(quarter_base(who, count), 16)

    def rows_of(start, index, length):
        return pl.ds(pl.multiple_of(start + index, 16), length)

    core = []
    for p in range(pieces):
        for high in range(2):
            copy = remote(
                grads_ref.at[rows_of(base(2 * high + 1 - lower), p * rows, rows)],
                rc.at[p, high],
                send.at[high, p],
                recv.at[high, p],
                peers[0],
            )
            copy.start()
            core.append(copy)
    step_rows = 192 if half % 192 == 0 else 16
    xs, ys, gs = [], [], []

    def z_copy(p, step):
        to = partner(step)
        return remote(
            tz.at[p, pl.ds(pl.multiple_of(to * part, 16), part)],
            rz.at[p, pl.ds(pl.multiple_of(depth * part, 16), part)],
            zsend.at[0, p, step],
            zrecv.at[0, p, step],
            {SPACE: to * 2 + side},
        )

    def home(p, which, slot):
        return pl.ds(pl.multiple_of(p * rows + which * half + slot * part, 16), part)

    def g_copy(p, step):
        block = gath.at[home(p, side, depth)]
        return remote(block, block, zsend.at[1, p, step], zrecv.at[1, p, step], {SPACE: partner(step) * 2 + side})

    def each(body):
        def run(step, carry):
            body(step)
            return carry

        lax.fori_loop(1, group, run, 0)

    def stage_core(p):
        core[2 * p].wait_recv()
        core[2 * p + 1].wait_recv()
        far = 1 - upper

        def add(step, carry):
            at = pl.multiple_of(step * step_rows, 16)
            mine = grads_ref[rows_of(base(2 * far + lower), p * rows + at, step_rows), :].astype(jnp.float32)
            tx[p, pl.ds(at, step_rows), :] = (
                mine + rc[p, far, pl.ds(at, step_rows), :].astype(jnp.float32)
            ).astype(jnp.bfloat16)
            return carry

        lax.fori_loop(0, rows // step_rows, add, 0)
        copy = remote(tx.at[p], rx.at[p], send.at[2, p], recv.at[2, p], peers[1])
        copy.start()
        xs.append(copy)

    def stage_x(p):
        xs[p].wait_recv()

        def total(at):
            return (
                grads_ref[rows_of(base(rank), p * rows + at, step_rows), :].astype(jnp.float32)
                + rc[p, upper, pl.ds(at, step_rows), :].astype(jnp.float32)
                + rx[p, pl.ds(at, step_rows), :].astype(jnp.float32)
            )

        def add(step, carry):
            at = pl.multiple_of(step * step_rows, 16)
            far = pl.multiple_of((1 - side) * half + at, 16)
            near = pl.multiple_of(side * half + at, 16)
            ty[p, pl.ds(at, step_rows), :] = total(far).astype(jnp.bfloat16)
            acc[p, pl.ds(at, step_rows), :] = total(near)
            return carry

        lax.fori_loop(0, half // step_rows, add, 0)
        copy = remote(ty.at[p], ry.at[p], send.at[3, p], recv.at[3, p], peers[2])
        copy.start()
        ys.append(copy)

    def stage_y(p):
        ys[p].wait_recv()

        def add(step, carry):
            at = pl.ds(pl.multiple_of(step * step_rows, 16), step_rows)
            value = acc[p, at, :] + ry[p, at, :].astype(jnp.float32)
            acc[p, at, :] = value
            tz[p, at, :] = value.astype(jnp.bfloat16)
            return carry

        lax.fori_loop(0, half // step_rows, add, 0)
        each(lambda step: z_copy(p, step).start())

    def stage_z(p):
        each(lambda step: z_copy(p, step).wait_recv())
        value = acc[p, pl.ds(pl.multiple_of(depth * part, 16), part), :]

        def add(step, value):
            other = lax.rem(depth + group - step, group)
            return value + rz[p, pl.ds(pl.multiple_of(other * part, 16), part), :].astype(jnp.float32)

        value = lax.fori_loop(1, group, add, value)
        gath[home(p, side, depth), :] = value.astype(jnp.bfloat16)
        each(lambda step: g_copy(p, step).start())

    def stage_zg(p):
        each(lambda step: g_copy(p, step).wait_recv())
        block = gath.at[pl.ds(pl.multiple_of(p * rows + side * half, 16), half)]
        copy = remote(block, block, send.at[4, p], recv.at[4, p], peers[2])
        copy.start()
        gs.append(copy)

    def stage_yg(p):
        gs[p].wait_recv()

    stages = [stage_core, stage_x, stage_y, stage_z, stage_zg, stage_yg]
    for tick in range(pieces + len(stages) - 1):
        for number in reversed(range(len(stages))):
            if 0 <= tick - number < pieces:
                stages[number](tick - number)

    for copy in core + xs + ys + gs:
        copy.wait_send()
    for p in range(pieces):

        def done(step):
            z_copy(p, step).wait_send()
            g_copy(p, step).wait_send()

        each(done)

    offset = rank * count - quarter_base(rank, count) * LANES
    skip = lax.div(offset, LANES)
    matrix = lane_matrix(lax.rem(offset, LANES), False)
    wide = jnp.where(
        lax.broadcasted_iota(jnp.int32, (256, 288), 1)
        == lax.broadcasted_iota(jnp.int32, (256, 288), 0) + skip,
        1.0,
        0.0,
    ).astype(jnp.bfloat16)
    wide_next = jnp.where(
        lax.broadcasted_iota(jnp.int32, (256, 288), 1)
        == lax.broadcasted_iota(jnp.int32, (256, 288), 0) + skip + 1,
        1.0,
        0.0,
    ).astype(jnp.bfloat16)

    def place(step, carry):
        at = pl.multiple_of(step * 256, 256)
        block = gath[pl.ds(at, 288), :]
        both = jnp.dot(block, matrix, preferred_element_type=jnp.float32).astype(jnp.bfloat16)
        out_ref[pl.ds(at, 256), :] = jnp.dot(wide, both[:, :LANES], preferred_element_type=jnp.float32) + jnp.dot(
            wide_next, both[:, LANES:], preferred_element_type=jnp.float32
        )
        return carry

    lax.fori_loop(0, BLOCK // 256, place, 0)


def reduce_grads(flat, space, count):
    pieces = next(k for k in (4, 2, 1) if BLOCK // (k * space) % 16 == 0)
    rows = BLOCK // pieces
    half = rows // 2
    out = pl.pallas_call(
        functools.partial(reduce_kernel, count, space, pieces),
        out_shape=jax.ShapeDtypeStruct((BLOCK, LANES), jnp.float32),
        in_specs=[pl.BlockSpec(memory_space=pltpu.VMEM)],
        out_specs=pl.BlockSpec(memory_space=pltpu.VMEM),
        scratch_shapes=[
            pltpu.VMEM((pieces, 2, rows, LANES), jnp.bfloat16),
            pltpu.VMEM((pieces, rows, LANES), jnp.bfloat16),
            pltpu.VMEM((pieces, rows, LANES), jnp.bfloat16),
            pltpu.VMEM((pieces, half, LANES), jnp.float32),
            pltpu.VMEM((pieces, half, LANES), jnp.bfloat16),
            pltpu.VMEM((pieces, half, LANES), jnp.bfloat16),
            pltpu.VMEM((pieces, half, LANES), jnp.bfloat16),
            pltpu.VMEM((pieces, half, LANES), jnp.bfloat16),
            pltpu.VMEM((BLOCK + 32, LANES), jnp.bfloat16),
            pltpu.SemaphoreType.DMA((5, pieces)),
            pltpu.SemaphoreType.DMA((5, pieces)),
            pltpu.SemaphoreType.DMA((2, pieces, space // 2)),
            pltpu.SemaphoreType.DMA((2, pieces, space // 2)),
        ],
        compiler_params=pltpu.CompilerParams(
            collective_id=1, has_side_effects=True, vmem_limit_bytes=48 * 2**20
        ),
    )(flat)
    return out.reshape(-1)[:count]


def gru_forward(state, inputs, weights, biases, gate_name, candidate_name, tall, wide, padder):
    joined_stack = patches(padder(jnp.concatenate([state, inputs], -1), tall, wide), tall, wide)
    gates = jax.nn.sigmoid(apply(joined_stack, weights[gate_name]) + biases[gate_name])
    hidden = state.shape[-1]
    update = gates[..., :hidden]
    reset = gates[..., hidden:]
    state_wide = state.astype(jnp.float32)
    mixed = jnp.concatenate([(reset * state_wide).astype(jnp.bfloat16), inputs], -1)
    mixed_stack = patches(padder(mixed, tall, wide), tall, wide)
    candidate = jnp.tanh(apply(mixed_stack, weights[candidate_name]) + biases[candidate_name])
    result = state_wide + update * (candidate - state_wide)
    return (result, (joined_stack, mixed_stack, update, reset, candidate, state_wide))


def gru_backward(result_grad, kept, weights, grads, gate_name, candidate_name, tall, wide, padder):
    joined_stack, mixed_stack, update, reset, candidate, state_wide = kept
    hidden = update.shape[-1]
    candidate_grad = (result_grad * update * (1.0 - candidate * candidate)).astype(jnp.bfloat16)
    record(grads, candidate_name, mixed_stack, candidate_grad)
    mixed_grad = apply(
        patches(padder(candidate_grad, tall, wide), tall, wide),
        flipped(weights[candidate_name], tall, wide),
    )
    reset_grad = mixed_grad[..., :hidden]
    gate_grad = jnp.concatenate(
        [
            result_grad * (candidate - state_wide) * update * (1.0 - update),
            reset_grad * state_wide * reset * (1.0 - reset),
        ],
        -1,
    ).astype(jnp.bfloat16)
    record(grads, gate_name, joined_stack, gate_grad)
    joined_grad = apply(
        patches(padder(gate_grad, tall, wide), tall, wide), flipped(weights[gate_name], tall, wide)
    )
    state_grad = result_grad * (1.0 - update) + reset_grad * reset + joined_grad[..., :hidden]
    inputs_grad = joined_grad[..., hidden:] + mixed_grad[..., hidden:]
    return (state_grad, inputs_grad)


def shards(net, context, corr, flow, target, valid, grad_net, grad_mask, params):
    flow_start = CTX + MOT - 2
    plane = jnp.float32(target.shape[2] * net.shape[2])
    counts = lax.psum(jnp.sum(valid, axis=(1, 2)).astype(jnp.float32), SPACE)
    divisor = jnp.maximum(counts, 1.0)
    weights, biases = unpack(gather_params(params))
    grads = {}
    flow_rows = jnp.transpose(flow, (0, 2, 3, 1))
    corr_pre = apply(corr, weights[CORR_IN]) + biases[CORR_IN]
    corr_one = jax.nn.silu(corr_pre).astype(jnp.bfloat16)
    corr_stack = patches(row_pad(corr_one, 3), 3, 3)
    corr_mix_pre = apply(corr_stack, weights[CORR_MIX]) + biases[CORR_MIX]
    corr_two = jax.nn.silu(corr_mix_pre).astype(jnp.bfloat16)
    flow_stack = patches(row_pad(flow_rows, 7), 7, 7)
    flow_pre = apply(flow_stack, weights[FLOW_IN]) + biases[FLOW_IN]
    flow_one = jax.nn.silu(flow_pre).astype(jnp.bfloat16)
    flow_mix_stack = patches(row_pad(flow_one, 3), 3, 3)
    flow_mix_pre = apply(flow_mix_stack, weights[FLOW_MIX]) + biases[FLOW_MIX]
    flow_two = jax.nn.silu(flow_mix_pre).astype(jnp.bfloat16)
    joint_stack = patches(row_pad(jnp.concatenate([corr_two, flow_two], -1), 3), 3, 3)
    motion_pre = apply(joint_stack, weights[MOTION_MIX]) + biases[MOTION_MIX]
    motion = jax.nn.silu(motion_pre).astype(jnp.bfloat16)
    inputs = jnp.concatenate([context, motion, flow_rows], -1)
    state, rows_kept = gru_forward(
        net, inputs, weights, biases, ROWS_GATES, ROWS_CANDIDATE, 1, 5, local_pad
    )
    state_columns, inputs_columns = (
        lax.all_to_all(
            state.astype(jnp.bfloat16), SPACE, split_axis=2, concat_axis=1, tiled=True
        ),
        lax.all_to_all(inputs, SPACE, split_axis=2, concat_axis=1, tiled=True),
    )
    target_here = jnp.transpose(target, (0, 2, 3, 1))
    valid_here = valid.astype(jnp.float32)
    net_cotangent = grad_net
    mask_cotangent = grad_mask
    final, columns_kept = gru_forward(
        state_columns,
        inputs_columns,
        weights,
        biases,
        COLUMNS_GATES,
        COLUMNS_CANDIDATE,
        5,
        1,
        local_pad,
    )
    final_low = final.astype(jnp.bfloat16)
    heads_weight = jnp.concatenate([weights[FLOW_HIDDEN], weights[MASK_HIDDEN]], 1)
    heads_bias = jnp.concatenate([biases[FLOW_HIDDEN], biases[MASK_HIDDEN]])
    net_stack = patches(column_pad(final_low, 3, 3), 3, 3)
    heads_pre = apply(net_stack, heads_weight) + heads_bias
    heads_act = jax.nn.silu(heads_pre).astype(jnp.bfloat16)
    flow_features = heads_act[..., :HEAD]
    mask_features = heads_act[..., HEAD:]
    hidden_stack = patches(column_pad(flow_features, 3, 3), 3, 3)
    delta = apply(hidden_stack, weights[FLOW_OUT]) + biases[FLOW_OUT]
    mask_full = 0.25 * (apply(mask_features, weights[MASK_OUT]) + biases[MASK_OUT])
    new_flow = inputs_columns[..., flow_start:].astype(jnp.float32) + delta
    error = new_flow - target_here
    root = jnp.sqrt(error * error + 1.0)
    partials = jnp.sum(valid_here * jnp.sum(root, axis=-1), axis=(1, 2))
    flow_grad = plane / divisor[:, None, None, None] * valid_here[..., None] * error / root
    mask_low = mask_full.astype(jnp.bfloat16)
    nets_out = final_low
    flows_out = jnp.transpose(new_flow, (0, 3, 1, 2))
    masks_out = mask_low
    delta_grad = flow_grad.astype(jnp.bfloat16)
    mask_grad = (0.25 * mask_cotangent.astype(jnp.float32)).astype(jnp.bfloat16)
    record(grads, MASK_OUT, mask_features, mask_grad)
    record(grads, FLOW_OUT, hidden_stack, delta_grad)
    from_flow = apply(
        patches(column_pad(delta_grad, 3, 3), 3, 3), flipped(weights[FLOW_OUT], 3, 3)
    )
    from_mask = apply_back(mask_grad, weights[MASK_OUT])
    heads_grad = (jnp.concatenate([from_flow, from_mask], -1) * slope(heads_pre)).astype(
        jnp.bfloat16
    )
    heads_wgrad = weight_grad(net_stack, heads_grad)
    heads_bgrad = jnp.sum(heads_grad, axis=(0, 1, 2), dtype=jnp.float32)
    grads[FLOW_HIDDEN] = (heads_wgrad[:, :HEAD], heads_bgrad[:HEAD])
    grads[MASK_HIDDEN] = (heads_wgrad[:, HEAD:], heads_bgrad[HEAD:])
    final_grad = net_cotangent.astype(jnp.float32) + apply(
        patches(column_pad(heads_grad, 3, 3), 3, 3), flipped(heads_weight, 3, 3)
    )
    state_grad_columns, inputs_grad_columns = gru_backward(
        final_grad,
        columns_kept,
        weights,
        grads,
        COLUMNS_GATES,
        COLUMNS_CANDIDATE,
        5,
        1,
        local_pad,
    )
    inputs_grad_columns = jnp.concatenate(
        [
            inputs_grad_columns[..., :flow_start],
            inputs_grad_columns[..., flow_start:] + flow_grad,
        ],
        -1,
    )
    state_back, inputs_back = (
        lax.all_to_all(
            state_grad_columns.astype(jnp.bfloat16),
            SPACE,
            split_axis=1,
            concat_axis=2,
            tiled=True,
        ),
        lax.all_to_all(
            inputs_grad_columns.astype(jnp.bfloat16),
            SPACE,
            split_axis=1,
            concat_axis=2,
            tiled=True,
        ),
    )
    net_grad, inputs_grad = gru_backward(
        state_back.astype(jnp.float32),
        rows_kept,
        weights,
        grads,
        ROWS_GATES,
        ROWS_CANDIDATE,
        1,
        5,
        local_pad,
    )
    inputs_total = inputs_grad + inputs_back.astype(jnp.float32)
    motion_grad = (inputs_total[..., CTX:flow_start] * slope(motion_pre)).astype(jnp.bfloat16)
    record(grads, MOTION_MIX, joint_stack, motion_grad)
    joint_grad = apply(
        patches(row_pad(motion_grad, 3), 3, 3), flipped(weights[MOTION_MIX], 3, 3)
    )
    branch_grad = jnp.concatenate(
        [
            joint_grad[..., :C2] * slope(corr_mix_pre),
            joint_grad[..., C2:] * slope(flow_mix_pre),
        ],
        -1,
    ).astype(jnp.bfloat16)
    record(grads, CORR_MIX, corr_stack, branch_grad[..., :C2])
    record(grads, FLOW_MIX, flow_mix_stack, branch_grad[..., C2:])
    branch_pad = row_pad(branch_grad, 3)
    corr_one_grad = apply(
        patches(branch_pad[..., :C2], 3, 3), flipped(weights[CORR_MIX], 3, 3)
    )
    flow_one_grad = apply(
        patches(branch_pad[..., C2:], 3, 3), flipped(weights[FLOW_MIX], 3, 3)
    )
    corr_pre_grad = (corr_one_grad * slope(corr_pre)).astype(jnp.bfloat16)
    flow_pre_grad = (flow_one_grad * slope(flow_pre)).astype(jnp.bfloat16)
    record(grads, CORR_IN, corr, corr_pre_grad)
    record(grads, FLOW_IN, flow_stack, flow_pre_grad)
    corr_grads = apply_back(corr_pre_grad, weights[CORR_IN])
    flow_total = inputs_total[..., flow_start:] + apply(
        patches(row_pad(flow_pre_grad, 7), 7, 7), flipped(weights[FLOW_IN], 7, 7)
    )
    flow_grads = jnp.transpose(flow_total, (0, 3, 1, 2))
    net_grads = net_grad
    context_grads = inputs_total[..., :CTX]
    count = params.shape[0]
    local = pack(grads, 3 * count // (LANES * 16) * 16 + BLOCK)
    collected = reduce_grads(local, lax.axis_size(SPACE), count)
    losses = lax.psum(partials, SPACE) / divisor
    return (
        nets_out,
        flows_out,
        masks_out,
        losses,
        collected,
        net_grads,
        context_grads,
        corr_grads,
        flow_grads,
    )


BATCH = 2
ROWS = 5
WIDE = 128
TALL = 40
COLS = 16
AREA = 640
PITCH = 20
SPREAD = TALL * PITCH
SPAN = 896
EDGE = 64


def mm(a, b):
    return jnp.dot(a, b, preferred_element_type=jnp.float32)


def nt(a, b):
    return lax.dot_general(a, b, (((1,), (1,)), ((), ())), preferred_element_type=jnp.float32)


def tn(a, b):
    return lax.dot_general(a, b, (((0,), (0,)), ((), ())), preferred_element_type=jnp.float32)


def half_of(value):
    return value.astype(jnp.bfloat16)


def full_of(value):
    return value.astype(jnp.float32)


def quarter_of(value):
    return half_of(0.25 * full_of(value))


def lane_index(shape):
    return lax.broadcasted_iota(jnp.int32, shape, 1)


def row_index(shape):
    return lax.broadcasted_iota(jnp.int32, shape, 0)


def act_slope(pre):
    sigma = jax.nn.sigmoid(pre)
    act = pre * sigma
    return act, sigma + act * (1.0 - sigma)


def flat_rows():
    table = shapes()
    offset = 0
    starts = {}
    for name, height, width in table:
        starts[name] = offset // LANES
        offset += height * width
    bias_row = offset // LANES
    spots = {}
    inner = 0
    for name, height, width in table:
        spots[name] = inner
        inner += width
    return starts, bias_row, spots, inner


def cast_rows(dst, to, src, start, count, kind):
    big = 256
    whole = count // big

    if whole > 1:

        def body(step, carry):
            at = pl.multiple_of(step * big, big)
            dst[pl.ds(to + at, big), :] = src[pl.ds(start + at, big), :].astype(kind)
            return carry

        lax.fori_loop(0, whole, body, 0)
    elif whole == 1:
        dst[to : to + big, :] = src[start : start + big, :].astype(kind)
    rest = count - whole * big
    if rest:
        low = whole * big
        dst[to + low : to + count, :] = src[start + low : start + count, :].astype(kind)


MARGIN = 16


def stage_plan(count, start, rows):
    stop = start + rows
    pieces, fill = [], 0
    for rank in range(4):
        first = rank * count // LANES
        last = -(-(rank + 1) * count // LANES)
        low, high = max(start, first), min(stop, last)
        if low >= high:
            continue
        place = low - first + rank * BLOCK
        base = place // 16 * 16
        length = -(-(place - base + high - low) // 16) * 16
        to = MARGIN + low - start - (place - base)
        seam = MARGIN + low - start if start < first else None
        pieces.append((base, length, fill, to, seam))
        fill += length
    return pieces


class Stages:
    def __init__(self, v, count, segments):
        self.v, self.at = v, 0
        self.plans = [stage_plan(count, start, rows) for start, rows in segments]
        self.fetch(0)

    def copies(self, index):
        v, slot = self.v, index % 2
        return [
            pltpu.make_async_copy(
                v.out_all.at[base : base + length], v.stage.at[slot, fill : fill + length], v.ssem.at[slot, number]
            )
            for number, (base, length, fill, to, seam) in enumerate(self.plans[index])
        ]

    def fetch(self, index):
        if index < len(self.plans):
            for copy in self.copies(index):
                copy.start()

    def take(self):
        v, index = self.v, self.at
        self.at += 1
        for copy in self.copies(index):
            copy.wait()
        self.fetch(index + 1)
        for base, length, fill, to, seam in self.plans[index]:
            saved = None if seam is None else v.flat[seam : seam + 1, :]
            cast_rows(v.flat, to, v.stage.at[index % 2], fill, length, jnp.float32)
            if seam is not None:
                v.flat[seam : seam + 1, :] = v.flat[seam : seam + 1, :] + saved


def strided(ref, start, count, stride):
    if stride == 1:
        return ref[pl.ds(start, count), :]
    return ref[pl.ds(start, count, stride=stride), :]


def unpack_pairs(flat, row, count, dst, to, lane):
    dst[to : to + count, lane : lane + LANES] = half_of(strided(flat, MARGIN + 2 * row, count, 2))
    dst[to : to + count, lane + LANES : lane + 2 * LANES] = half_of(strided(flat, MARGIN + 2 * row + 1, count, 2))


def pack_pairs(flat, row, count, low, high):
    flat[pl.ds(MARGIN + 2 * row, count, stride=2), :] = low
    flat[pl.ds(MARGIN + 2 * row + 1, count, stride=2), :] = high


def split_pick(which, quarter):
    source = lax.broadcasted_iota(jnp.int32, (LANES, HEAD), 0)
    target = lax.broadcasted_iota(jnp.int32, (LANES, HEAD), 1)
    return jnp.where(source == 2 * (target - 64 * quarter) + which, 1.0, 0.0).astype(jnp.bfloat16)


UNPACK = (
    (CORR_IN, 648), (CORR_MIX, 3456), (FLOW_IN, 98), (FLOW_MIX, 576), (MOTION_MIX, 2268),
    (ROWS_GATES, 3840), (ROWS_CANDIDATE, 1920), (None, 21), (COLUMNS_GATES, 3840), (COLUMNS_CANDIDATE, 1920),
    (FLOW_HIDDEN, 2304), (MASK_HIDDEN, 2304), (FLOW_OUT, 36), (MASK_OUT, 1152),
)


def stage_of(v, name, rows):
    assert UNPACK[v.stages.at] == (name, rows)
    v.stages.take()


def unpack_gru(v, gates_name, cand_name, w_i, w_s):
    flat = v.flat
    stage_of(v, gates_name, 3840)
    for tap in range(5):
        unpack_pairs(flat, tap * 384, 128, w_s, tap * 128, 0)
        unpack_pairs(flat, tap * 384 + 128, 256, w_i, tap * 256, 0)
    stage_of(v, cand_name, 1920)
    for tap in range(5):
        w_s[tap * 128 : (tap + 1) * 128, 256:384] = half_of(strided(flat, MARGIN + tap * 384, 128, 1))
        w_i[tap * 256 : (tap + 1) * 256, 256:384] = half_of(strided(flat, MARGIN + tap * 384 + 128, 256, 1))


def unpack_encoder(v, count):
    starts, bias_row, spots, inner = flat_rows()
    flat = v.flat
    v.stages = Stages(v, count, [(bias_row if name is None else starts[name], rows) for name, rows in UNPACK])

    def stage(name, rows):
        stage_of(v, name, rows)

    stage(CORR_IN, 648)
    unpack_pairs(flat, 0, 324, v.w_ci, 0, 0)

    stage(CORR_MIX, 3456)
    lane = lane_index((128, LANES))
    low_half = lane < 64

    def mix_step(step, carry):
        at = MARGIN + 384 * step
        r0, r1, r2 = (strided(flat, at + i, 128, 3) for i in range(3))
        r1s, r2s = pltpu.roll(r1, 64, 1), pltpu.roll(r2, 64, 1)
        v.pair_a[pl.ds(0, 128, stride=2), :] = r0
        v.pair_a[pl.ds(1, 128, stride=2), :] = jnp.where(low_half, r1s, r2s)
        v.pair_b[pl.ds(0, 128, stride=2), :] = jnp.where(low_half, r1, 0.0)
        v.pair_b[pl.ds(1, 128, stride=2), :] = jnp.where(low_half, r2s, 0.0)
        to = pl.ds(pl.multiple_of(step * 256, 256), 256)
        v.w_cm[to, 0:128] = half_of(v.pair_a[...])
        v.w_cm[to, 128:256] = half_of(v.pair_b[...])
        return carry

    lax.fori_loop(0, 9, mix_step, 0)

    stage(FLOW_IN, 98)
    v.flow_tmp[...] = jnp.zeros_like(v.flow_tmp)
    for across in range(7):
        for comp in range(2):
            v.flow_tmp[pl.ds(across * 16 + comp, 7, stride=2), :] = strided(
                flat, MARGIN + across * 2 + comp, 7, 14
            )
    v.w_fi[...] = half_of(v.flow_tmp[...])

    stage(FLOW_MIX, 576)
    for step in range(9):
        r0 = strided(flat, MARGIN + 64 * step, 64, 1)
        high_half = lane_index((64, LANES)) >= 64
        v.pair_a[pl.ds(0, 64, stride=2), :] = jnp.where(high_half, pltpu.roll(r0, 64, 1), 0.0)
        v.pair_a[pl.ds(1, 64, stride=2), :] = jnp.where(high_half, r0, 0.0)
        v.w_fm[step * 128 : (step + 1) * 128, :] = half_of(v.pair_a[0:128, :])

    stage(MOTION_MIX, 2268)
    lane36 = lane_index((36, LANES))
    for i in range(64):
        if i == 0:
            value = strided(flat, MARGIN, 36, 63)
        elif i == 63:
            value = pltpu.roll(strided(flat, MARGIN + 62, 36, 63), 126, 1)
        else:
            low = pltpu.roll(strided(flat, MARGIN + i - 1, 36, 63), 2 * i, 1)
            high = pltpu.roll(strided(flat, MARGIN + i, 36, 63), 2 * i, 1)
            value = jnp.where(lane36 < 2 * i, low, high)
        v.mm_tmp[pl.ds(i, 36, stride=64), :] = jnp.where(lane36 < 126, value, 0.0)
    for step in range(9):
        v.w_mm[step * 256 : (step + 1) * 256, :] = half_of(v.mm_tmp[step * 256 : (step + 1) * 256, :])

    unpack_gru(v, ROWS_GATES, ROWS_CANDIDATE, v.w_ri, v.w_rs)

    stage(None, 21)
    place = 0
    lane1 = lane_index((1, LANES))
    for name, height, width in shapes():
        spot = spots[name]
        for block in range(-(-width // LANES)):
            at = spot + block * LANES
            row, shift = at // LANES, at % LANES
            value = flat[MARGIN + row : MARGIN + row + 1, :]
            if shift:
                after = flat[MARGIN + row + 1 : MARGIN + row + 2, :]
                value = jnp.where(
                    lane1 < LANES - shift, pltpu.roll(value, LANES - shift, 1), pltpu.roll(after, LANES - shift, 1)
                )
            left = width - block * LANES
            if left < LANES:
                value = jnp.where(lane1 < left, value, 0.0)
            if name == FLOW_MIX:
                value = pltpu.roll(value, 64, 1)
            v.bias[place : place + 1, :] = value
            place += 1


def unpack_heads(v):
    flat = v.flat
    low_half = lane_index((128, LANES)) < 64

    def stage(name, rows):
        stage_of(v, name, rows)

    unpack_gru(v, COLUMNS_GATES, COLUMNS_CANDIDATE, v.w_li, v.w_ls)

    for name, lane0 in ((FLOW_HIDDEN, 0), (MASK_HIDDEN, 256)):
        stage(name, 2304)
        for tap in range(9):
            unpack_pairs(flat, tap * 128, 128, v.w_h, tap * 128, lane0)

    stage(FLOW_OUT, 36)
    v.fo_tmp[...] = jnp.zeros_like(v.fo_tmp)
    for which in range(2):
        total = jnp.zeros((9, HEAD), jnp.float32)
        for quarter in range(4):
            total = total + mm(half_of(strided(flat, MARGIN + quarter, 9, 4)), split_pick(which, quarter))
        v.fo_tmp[pl.ds(which, 9, stride=2), 0:128] = total[:, :128]
        v.fo_tmp2[pl.ds(which, 9, stride=2), 0:128] = total[:, 128:]
    v.fo_tmp2[18:32, :] = jnp.zeros((14, LANES), jnp.float32)
    v.w_fo[:, 0:128] = half_of(v.fo_tmp[...])
    v.w_fo[:, 128:256] = half_of(v.fo_tmp2[...])

    stage(MASK_OUT, 1152)
    r = [strided(flat, MARGIN + i, 128, 9) for i in range(9)]
    rs = [pltpu.roll(r[i], 64, 1) for i in range(4, 9)]
    for block in range(5):
        even = r[block] if block < 4 else jnp.where(low_half, r[4], 0.0)
        odd = jnp.where(low_half, rs[block], rs[block + 1]) if block < 4 else jnp.where(low_half, rs[4], 0.0)
        v.pair_a[pl.ds(0, 128, stride=2), :] = even
        v.pair_a[pl.ds(1, 128, stride=2), :] = odd
        v.w_mo[:, block * 128 : (block + 1) * 128] = half_of(v.pair_a[...])


BIAS_AT = {}
_place = 0
for _name, _height, _width in shapes():
    BIAS_AT[_name] = _place
    _place += -(-_width // 128)
BIAS_ROWS = 32


def bias_of(v, name, blocks):
    at = BIAS_AT[name]
    return jnp.concatenate([v.bias[at + i : at + i + 1, :] for i in range(blocks)], axis=1)


class Halo:
    def __init__(self, v, sem, up_src, down_src, from_down, from_up):
        up = {SPACE: jnp.maximum(v.spot - 1, 0)}
        down = {SPACE: jnp.minimum(v.spot + 1, v.space - 1)}
        self.v = v
        self.up = remote(up_src, from_down, v.hsend.at[sem, 0], v.hrecv.at[sem, 0], up)
        self.down = remote(down_src, from_up, v.hsend.at[sem, 1], v.hrecv.at[sem, 1], down)

    def start(self):
        pl.when(self.v.spot > 0)(self.up.start)
        pl.when(self.v.spot < self.v.space - 1)(self.down.start)

    def receive(self):
        pl.when(self.v.spot < self.v.space - 1)(self.up.wait_recv)
        pl.when(self.v.spot > 0)(self.down.wait_recv)

    def sent(self):
        pl.when(self.v.spot > 0)(self.up.wait_send)
        pl.when(self.v.spot < self.v.space - 1)(self.down.wait_send)


class Swap:
    def __init__(self, v, sem, src, dst, broadcast=False):
        self.v, self.sem, self.src, self.dst, self.broadcast = v, sem, src, dst, broadcast

    def copy(self, step):
        v = self.v
        to = lax.rem(v.spot + step, v.space)
        src = self.src if self.broadcast else self.src.at[to]
        return remote(src, self.dst.at[v.spot], v.asend.at[self.sem, step], v.arecv.at[self.sem, step], {SPACE: to})

    def each(self, what):
        def body(step, carry):
            what(self.copy(step))
            return carry

        lax.fori_loop(1, self.v.space, body, 0)

    def start(self):
        self.each(lambda copy: copy.start())

    def receive(self):
        self.each(lambda copy: copy.wait_recv())

    def sent(self):
        self.each(lambda copy: copy.wait_send())


def spread_rows(v, b, acts, rows, dst, row0, width, backward=False):
    x = lax.rem(row_index((rows, LANES)), WIDE)
    for block, act in enumerate(acts):
        v.tmp[8 : 8 + rows, :] = act
        for tap in range(3):
            d = (1 - tap) if backward else (tap - 1)
            value = act if d == 0 else v.tmp[8 + d : 8 + d + rows, :]
            if d == -1:
                value = jnp.where(x > 0, value, 0.0)
            if d == 1:
                value = jnp.where(x < WIDE - 1, value, 0.0)
            lane = tap * width + block * LANES
            if backward:
                dst[row0 : row0 + rows, b + lane : b + lane + LANES] = half_of(value)
            else:
                dst[b, row0 : row0 + rows, lane : lane + LANES] = half_of(value)


def spread_five(v, value, dst, lane_of, backward=False):
    x = lax.rem(row_index((AREA, LANES)), WIDE)
    v.tmp[8 : 8 + AREA, :] = value
    for tap in range(5):
        d = (2 - tap) if backward else (tap - 2)
        moved = value if d == 0 else v.tmp[8 + d : 8 + d + AREA, :]
        if d:
            moved = jnp.where((x + d >= 0) & (x + d < WIDE), moved, 0.0)
        if backward:
            taps_part(v, tap, lane_of, lane_of + LANES)[...] = half_of(moved)
        else:
            lane = lane_of(tap)
            dst[:, lane : lane + LANES] = half_of(moved)


def lines_of(ref, b, lines):
    return jnp.concatenate([ref[b, y] for y in range(lines)], axis=1)


def edge_rows(v, value, rows):
    low = jnp.where(v.spot > 0, value[0:rows], 0.0)
    high = jnp.where(v.spot < v.space - 1, value[-rows:], 0.0)
    return jnp.concatenate([low, value[rows:-rows], high], axis=0)


def early_taps(v):
    def flow(b, carry):
        up = jnp.where(v.spot > 0, v.flow_up[b], 0.0)
        down = jnp.where(v.spot < v.space - 1, v.flow_down[b], 0.0)
        lane = lane_index((16, LANES))
        v.fs[...] = jnp.zeros_like(v.fs)
        for across in range(7):
            d = across - 3
            for part, value in enumerate((up, v.flow[b], down)):
                moved = value
                if d:
                    moved = pltpu.roll(value, (-d) % LANES, 1)
                    moved = jnp.where((lane + d >= 0) & (lane + d < WIDE), moved, 0.0)
                v.fs[across, part * 10 : part * 10 + 10, :] = moved[0:10, :]
        for y in range(9):
            for across in range(7):
                v.flow_tmp[across * 16 : across * 16 + 16, :] = v.fs[across, 2 * y : 2 * y + 16, :]
            v.xt[b, :, y * 128 : (y + 1) * 128] = half_of(v.flow_tmp[...])
        return carry

    lax.fori_loop(0, BATCH, flow, 0)

    def image(b, carry):
        at = pl.ds(pl.multiple_of(b * AREA, AREA), AREA)
        spread_five(v, full_of(v.context[b]), v.xi.at[at], lambda t: t * 256)
        spread_five(v, full_of(v.net[b]), v.xs.at[at], lambda t: t * 128)
        return carry

    lax.fori_loop(0, BATCH, image, 0)


def gather_start(v, count):
    pieces = 4
    rows = BLOCK // 2 // pieces
    half = lax.rem(v.spot, 2)
    matrix = lane_matrix(lax.rem(v.rank * count, LANES), True)
    first = row_index((256, LANES)) == 0

    def rotate(step, carry):
        at = pl.ds(pl.multiple_of(step * 256, 256), 256)
        both = mm(v.gath[at, :], matrix)
        spill = pltpu.roll(both[:, LANES:], 1, 0)
        v.gath[at, :] = half_of(both[:, :LANES] + jnp.where(first, carry, spill))
        return spill[0:1]

    lax.fori_loop(0, BLOCK // 256, rotate, jnp.zeros((1, LANES), jnp.float32))

    def piece(rank, which, index):
        return pl.ds(pl.multiple_of(rank * BLOCK + which * (BLOCK // 2) + index * rows, 16), rows)

    mine = pl.ds(pl.multiple_of(v.rank * BLOCK, 16), BLOCK)
    own = v.gath.at[0:BLOCK]
    v.g_x = [
        remote(
            v.gath.at[piece(0, half, k)], v.out_all.at[piece(v.rank, half, k)], v.gsend.at[0, k], v.grecv.at[0, k],
            {DP: v.other},
        )
        for k in range(pieces)
    ]
    v.g_own = remote(own, v.out_all.at[mine], v.gsend.at[4, 0], v.grecv.at[4, 0], {DP: v.mate})
    v.g_here = pltpu.make_async_copy(own, v.out_all.at[mine], v.gsend.at[4, 1])

    def forward(number, which, k, device):
        block = v.out_all.at[piece(v.other, which, k)]
        return remote(block, block, v.gsend.at[number, k], v.grecv.at[number, k], device)

    v.g_twin = [forward(1, half, k, {SPACE: v.twin}) for k in range(pieces)]
    v.g_mate = [forward(2, half, k, {DP: v.mate}) for k in range(pieces)]
    v.g_last = [forward(3, 1 - half, k, {DP: v.mate}) for k in range(pieces)]
    for copy in v.g_x:
        copy.start()
    v.g_own.start()
    v.g_here.start()


def gather_pass(v, first, last):
    for k in range(first, last):
        v.g_x[k].wait_recv()
        v.g_twin[k].start()
        v.g_mate[k].start()


def gather_end(v):
    for k in range(len(v.g_x)):
        v.g_twin[k].wait_recv()
        v.g_last[k].start()
    for k in range(len(v.g_x)):
        v.g_x[k].wait_send()
        v.g_twin[k].wait_send()
        v.g_mate[k].wait()
        v.g_last[k].wait()
    v.g_own.wait()
    v.g_here.wait()


def forward_rows(v):
    spot, last = v.spot, v.space - 1
    def image(b, carry):
        pieces = (
            (v.corr_up, 0, 256, 2, spot > 0),
            (v.corr, 256, 640, 5, None),
            (v.corr_down, 896, 256, 2, spot < last),
        )
        bias = bias_of(v, CORR_IN, 2)
        for ref, row0, rows, lines, seen in pieces:
            act, slope = act_slope(tn(lines_of(ref, b, lines), v.w_ci[...]) + bias)
            if seen is None:
                v.slope_ci[b] = half_of(slope)
            else:
                act = jnp.where(seen, act, 0.0)
            spread_rows(v, b, (act[:, :128], act[:, 128:]), rows, v.hx_c, row0, 256)

        act, slope = act_slope(tn(v.xt[b], v.w_fi[...]) + bias_of(v, FLOW_IN, 1))
        v.slope_fi[b] = half_of(slope[256:896])
        spread_rows(v, b, (edge_rows(v, act, 2 * WIDE),), 9 * WIDE, v.hx_f, 0, 128)

        pre = bias_of(v, CORR_MIX, 2)
        flow_pre = bias_of(v, FLOW_MIX, 1)
        for a in range(3):
            pre = pre + mm(v.hx_c[b, a * 128 : a * 128 + 896, :], v.w_cm[a * 768 : (a + 1) * 768, :])
            flow_pre = flow_pre + mm(v.hx_f[b, a * 128 : a * 128 + 896, :], v.w_fm[a * 384 : (a + 1) * 384, :])
        low, low_slope = act_slope(pre[:, :128])
        high, high_slope = act_slope(pre[:, 128:] + flow_pre)
        v.slope_j[b, :, 0:128] = half_of(low_slope)
        v.slope_j[b, :, 128:256] = half_of(high_slope)
        spread_rows(v, b, (edge_rows(v, low, WIDE), edge_rows(v, high, WIDE)), 896, v.hx_j, 0, 256)

        pre = bias_of(v, MOTION_MIX, 1)
        for a in range(3):
            pre = pre + mm(v.hx_j[b, a * 128 : a * 128 + 640, :], v.w_mm[a * 768 : (a + 1) * 768, :])
        act, slope = act_slope(pre)
        v.slope_m[b] = half_of(jnp.where(lane_index((AREA, LANES)) < 126, slope, 0.0))
        pick = jnp.where(lane_index((16, LANES)) == row_index((16, LANES)) + 126, 1.0, 0.0)
        own_flow = v.flow[b]
        for y in range(ROWS):
            v.tmp2[0:2, :] = own_flow[2 * y : 2 * y + 2, :]
            v.tmp2[2:16, :] = jnp.zeros((14, LANES), jnp.float32)
            v.motion[b, y * 128 : (y + 1) * 128, :] = act[y * 128 : (y + 1) * 128, :] + tn(
                half_of(v.tmp2[0:16, :]), half_of(pick)
            )
        v.motion[b] = full_of(half_of(v.motion[b]))
        pack_rows(v, v.motion, b, v.a_motion)
        return carry

    lax.fori_loop(0, BATCH, image, 0)
    v.swap_motion.start()

    def gru(b, carry):
        at = pl.ds(pl.multiple_of(b * AREA, AREA), AREA)
        s = full_of(v.net[b])
        spread_five(v, v.motion[b], v.xi.at[at], lambda t: t * 256 + 128)
        both = mm(v.xi[at, :], v.w_ri[...])
        gates = jax.nn.sigmoid(both[:, :256] + mm(v.xs[at, :], v.w_rs[:, :256]) + bias_of(v, ROWS_GATES, 2))
        update, reset = gates[:, :128], gates[:, 128:]
        v.ru[b] = update
        v.rr[b] = reset
        spread_five(v, full_of(half_of(reset * s)), v.xr.at[at], lambda t: t * 128)
        cand = jnp.tanh(both[:, 256:] + mm(v.xr[at, :], v.w_rs[:, 256:]) + bias_of(v, ROWS_CANDIDATE, 1))
        v.rc[b] = cand
        v.state[b] = s + update * (cand - s)
        pack_rows(v, v.state, b, v.a_state)
        return carry

    lax.fori_loop(0, BATCH, gru, 0)
    v.swap_state.start()


def pack_rows(v, src, b, dst):
    def peer(t, carry):
        for y in range(ROWS):
            at = pl.multiple_of(y * WIDE + t * COLS, COLS)
            dst[t, b, y * COLS : (y + 1) * COLS, :] = half_of(src[b, pl.ds(at, COLS), :])
        return carry

    lax.fori_loop(0, v.space, peer, 0)


def take_own(v, src, dst):
    dst[v.spot] = src[v.spot]


def columns_zero(v):
    def zero(b, carry):
        for ref, wide in ((v.xc, 384), (v.xcr, 128), (v.gc, 384)):
            for low in (0, 32 + AREA):
                ref[b, low : low + 32, :] = jnp.zeros((32, wide), jnp.bfloat16)
        return carry

    lax.fori_loop(0, BATCH, zero, 0)


def columns_in(v):
    def peer(t, carry):
        at = pl.ds(pl.multiple_of(32 + t * ROWS * COLS, 16), ROWS * COLS)
        for b in range(BATCH):
            v.xc[b, at, 0:128] = v.b_state[t, b]
            v.xc[b, at, 128:256] = v.b_context[t, b]
            v.xc[b, at, 256:384] = v.b_motion[t, b]
        return carry

    lax.fori_loop(0, v.space, peer, 0)


FX_ROWS = 16 + (TALL + 2) * PITCH


def fx_base(b):
    return pl.multiple_of(b * FX_ROWS, 8)


def columns_forward(v):
    def gru(b, carry):
        s = full_of(v.xc[b, 32 : 32 + AREA, 0:128])
        both = bias_of(v, COLUMNS_GATES, 2)
        both = jnp.concatenate([both, bias_of(v, COLUMNS_CANDIDATE, 1)], axis=1)
        gates = 0.0
        for t in range(5):
            rows = slice(t * COLS, t * COLS + AREA)
            both = both + mm(v.xc[b, rows, 128:384], v.w_li[t * 256 : (t + 1) * 256, :])
            gates = gates + mm(v.xc[b, rows, 0:128], v.w_ls[t * 128 : (t + 1) * 128, 0:256])
        gates = jax.nn.sigmoid(gates + both[:, :256])
        update, reset = gates[:, :128], gates[:, 128:]
        v.lu[b] = update
        v.lr[b] = reset
        v.xcr[b, 32 : 32 + AREA, :] = half_of(reset * s)
        cand = both[:, 256:]
        for t in range(5):
            rows = slice(t * COLS, t * COLS + AREA)
            cand = cand + mm(v.xcr[b, rows, :], v.w_ls[t * 128 : (t + 1) * 128, 256:384])
        cand = jnp.tanh(cand)
        v.lc[b] = cand
        final = s + update * (cand - s)
        v.out_net[b] = half_of(final)
        v.final[...] = full_of(half_of(final))
        fx = fx_base(b)
        v.mm_tmp[pl.ds(fx, FX_ROWS), :] = jnp.zeros((FX_ROWS, LANES), jnp.float32)
        for x in range(COLS):
            v.mm_tmp[pl.ds(fx + 8 + PITCH + 2 + x, TALL, stride=PITCH), :] = v.final[pl.ds(x, TALL, stride=COLS), :]
        for j in range(2):
            v.e_left[b, j, 0:TALL, :] = half_of(v.final[pl.ds(j, TALL, stride=COLS), :])
            v.e_right[b, j, 0:TALL, :] = half_of(v.final[pl.ds(COLS - 2 + j, TALL, stride=COLS), :])
        return carry

    lax.fori_loop(0, BATCH, gru, 0)
    v.halo_final.start()


def ring_masks(v, shape):
    x = lax.rem(row_index(shape), PITCH)
    place = v.spot * COLS + x - 2
    seen = (place >= 0) & (place < WIDE) & (x >= 1) & (x < PITCH - 1)
    own = (x >= 2) & (x < PITCH - 2)
    return seen, own


def mask_gradient(v):
    def image(b, carry):
        value = nt(quarter_of(v.grad_mask[b]), v.w_mo[:, 0:MASK])
        for block in range(2):
            v.final[...] = value[:, block * 128 : (block + 1) * 128]
            v.tmp[0:SPREAD, :] = jnp.zeros((SPREAD, LANES), jnp.float32)
            for x in range(COLS):
                v.tmp[pl.ds(2 + x, TALL, stride=PITCH), :] = v.final[pl.ds(x, TALL, stride=COLS), :]
            v.hgo[b, :, 256 + block * 128 : 384 + block * 128] = half_of(v.tmp[0:SPREAD, :])
            v.m_left[b, block, 0:TALL, :] = half_of(v.final[pl.ds(0, TALL, stride=COLS), :])
            v.m_right[b, block, 0:TALL, :] = half_of(v.final[pl.ds(COLS - 1, TALL, stride=COLS), :])
        return carry

    lax.fori_loop(0, BATCH, image, 0)
    v.halo_mask.start()


def heads_part(v, b, tap):
    ref = v.hx_c if tap < 6 else v.hx_f
    lane = tap % 6 * 128
    return ref.at[b, 0:SPREAD, lane : lane + 128]


def taps_part(v, t, low, high):
    ref = v.hx_f if t % 3 == 2 else v.hx_c
    lane = (t % 3) % 2 * 384
    return ref.at[t // 3, 0:AREA, lane + low : lane + high]


def heads(v):
    spot, last = v.spot, v.space - 1
    v.halo_final.receive()
    v.halo_mask.receive()
    v.swap_count.receive()
    v.counts[v.spot] = v.count_out[...]
    counts = jnp.sum(v.counts[...], axis=0)
    seen, own = ring_masks(v, (SPREAD, LANES))
    steps = [(a - 1) * PITCH + (c - 1) for a in range(3) for c in range(3)]
    plane = jnp.float32(TALL * WIDE)

    def image(b, carry):
        fx = fx_base(b)
        for j in range(2):
            left = jnp.where(spot > 0, full_of(v.f_left[b, j, 0:TALL, :]), 0.0)
            right = jnp.where(spot < last, full_of(v.f_right[b, j, 0:TALL, :]), 0.0)
            v.mm_tmp[pl.ds(fx + 8 + PITCH + j, TALL, stride=PITCH), :] = left
            v.mm_tmp[pl.ds(fx + 8 + PITCH + PITCH - 2 + j, TALL, stride=PITCH), :] = right
        for block in range(2):
            left = jnp.where(spot > 0, full_of(v.n_left[b, block, 0:TALL, :]), 0.0)
            right = jnp.where(spot < last, full_of(v.n_right[b, block, 0:TALL, :]), 0.0)
            v.tmp[0:SPREAD, :] = full_of(v.hgo[b, :, 256 + block * 128 : 384 + block * 128])
            v.tmp[pl.ds(1, TALL, stride=PITCH), :] = left
            v.tmp[pl.ds(PITCH - 2, TALL, stride=PITCH), :] = right
            v.hgo[b, :, 256 + block * 128 : 384 + block * 128] = half_of(v.tmp[0:SPREAD, :])
        for tap in range(9):
            at = 8 + PITCH + steps[tap]
            heads_part(v, b, tap)[...] = half_of(v.mm_tmp[pl.ds(fx + at, SPREAD), :])
        for part in range(2):
            name = (FLOW_HIDDEN, MASK_HIDDEN)[part]
            lanes = slice(part * 256, (part + 1) * 256)
            act, slope = act_slope(mm(v.hx_c[b, 0:SPREAD, :], v.w_h[0:768, lanes]) + mm(v.hx_f[b, 0:SPREAD, :], v.w_h[768:1152, lanes]) + bias_of(v, name, 2))
            v.slope_h[b, :, lanes] = half_of(slope)
            if part == 0:
                for block in range(2):
                    value = jnp.where(seen, act[:, block * 128 : (block + 1) * 128], 0.0)
                    v.feat[b, 0:SPREAD, block * 128 : (block + 1) * 128] = half_of(value)
                v.feat[b, SPREAD:SPAN, :] = jnp.zeros((SPAN - SPREAD, HEAD), jnp.bfloat16)
            else:
                for block in range(2):
                    v.tmp[0:SPREAD, :] = act[:, block * 128 : (block + 1) * 128]
                    for x in range(COLS):
                        v.final[pl.ds(x, TALL, stride=COLS), :] = v.tmp[pl.ds(2 + x, TALL, stride=PITCH), :]
                    v.mf[b, :, block * 128 : (block + 1) * 128] = half_of(v.final[...])
        moved = nt(v.w_fo[...], v.feat[b])
        v.zt[...] = moved
        delta = jnp.zeros((8, SPAN), jnp.float32)
        for tap in range(9):
            pair = jnp.concatenate([v.zt[2 * tap : 2 * tap + 2, :], jnp.zeros((6, SPAN), jnp.float32)], axis=0)
            delta = delta + pltpu.roll(pair, (-steps[tap]) % SPAN, 1)
        v.tmp[0:SPAN, :] = jnp.zeros((SPAN, LANES), jnp.float32)
        v.final[...] = full_of(v.xc[b, 32 : 32 + AREA, 256:384])
        for x in range(COLS):
            v.tmp[pl.ds(2 + x, TALL, stride=PITCH), :] = v.final[pl.ds(x, TALL, stride=COLS), :]
        pick = jnp.where(lane_index((16, LANES)) == row_index((16, LANES)) + 126, 1.0, 0.0)
        base = nt(half_of(pick), half_of(v.tmp[0:SPAN, :]))[0:8, :]
        bias = v.bias[BIAS_AT[FLOW_OUT] : BIAS_AT[FLOW_OUT] + 1, :]
        first = row_index((8, SPAN)) == 0
        second = row_index((8, SPAN)) == 1
        shift = jnp.where(first, bias[0:1, 0:1], jnp.where(second, bias[0:1, 1:2], 0.0))
        new = base + delta + shift
        v.out_flow[b] = new
        error = new - v.target[b]
        root = jnp.sqrt(error * error + 1.0)
        valid = jnp.where(first | second, v.valid[b], 0.0)
        piece = jnp.sum(valid * root)
        divisor = jnp.maximum(v.pick_count(counts, b), 1.0)
        gradient = plane / divisor * valid * error / root
        v.dg[b] = gradient
        v.losses[...] = jnp.where(row_index((8, LANES)) == b, piece, v.losses[...])
        return carry

    v.losses[...] = jnp.zeros((8, LANES), jnp.float32)
    lax.fori_loop(0, BATCH, image, 0)
    v.halo_dg.start()
    v.swap_loss.start()


def mask_output(v):
    def image(b, carry):
        store = pltpu.make_async_copy(v.mask_low, v.out_mask.at[b], v.osem.at[3])
        pl.when(b > 0)(store.wait)
        for block in range(5):
            wide = min(128, MASK - block * 128)
            lanes = slice(block * 128, block * 128 + wide)
            at = BIAS_AT[MASK_OUT] + block
            value = mm(v.mf[b], v.w_mo[:, lanes]) + v.bias[at : at + 1, 0:wide]
            v.mask_low[:, lanes] = half_of(0.25 * value)
        store.start()
        return carry

    lax.fori_loop(0, BATCH, image, 0)


def heads_back(v):
    spot, last = v.spot, v.space - 1
    seen, own = ring_masks(v, (SPREAD, LANES))
    steps = [(a - 1) * PITCH + (c - 1) for a in range(3) for c in range(3)]
    v.halo_dg.receive()

    def zb(c, low, rows):
        at = c * (2 * EDGE + SPREAD) + low
        return v.mm_tmp.at[at : at + rows]

    def image(b, carry):
        x = lax.rem(lane_index((8, SPAN)), PITCH)
        own_dg = v.dg[b]
        left = jnp.where((x < 2) & (spot > 0), pltpu.roll(v.dg_left[b], SPAN - COLS, 1), 0.0)
        right = jnp.where((x >= PITCH - 2) & (spot < last), pltpu.roll(v.dg_right[b], COLS, 1), 0.0)
        inside = lane_index((8, SPAN)) < SPREAD
        wide_dg = full_of(half_of(jnp.where(inside, own_dg + left + right, 0.0)))
        own_low = full_of(half_of(own_dg))
        v.dt[...] = jnp.zeros_like(v.dt)
        v.dto[...] = jnp.zeros_like(v.dto)
        for tap in range(9):
            v.dt[2 * tap : 2 * tap + 2, :] = pltpu.roll(wide_dg, steps[tap] % SPAN, 1)[0:2, :]
            v.dto[2 * tap : 2 * tap + 2, :] = pltpu.roll(own_low, steps[tap] % SPAN, 1)[0:2, :]
        v.dtb[b] = half_of(v.dto[...])
        from_flow = tn(half_of(v.dt[...]), v.w_fo[...])
        for block in range(4):
            lanes = slice(block * 128, (block + 1) * 128)
            value = from_flow[0:SPREAD, lanes] if block < 2 else full_of(v.hgo[b, :, lanes])
            value = value * full_of(v.slope_h[b, :, lanes])
            v.hgo[b, :, lanes] = half_of(jnp.where(seen, value, 0.0))
        total = jnp.zeros((SPREAD, LANES), jnp.float32)
        for a in range(3):
            value = nt(v.hgo[b], v.w_h[a * 384 : (a + 1) * 384, :])
            for c in range(3):
                zb(c, EDGE, SPREAD)[...] = value[:, c * 128 : (c + 1) * 128]
            for c in range(3):
                at = EDGE - steps[a * 3 + c]
                total = total + zb(c, at, SPREAD)[...]
        for block in range(4):
            lanes = slice(block * 128, (block + 1) * 128)
            v.hgo[b, :, lanes] = half_of(jnp.where(own, full_of(v.hgo[b, :, lanes]), 0.0))
        v.tmp[0:SPREAD, :] = total
        for x in range(COLS):
            v.final[pl.ds(x, TALL, stride=COLS), :] = v.tmp[pl.ds(2 + x, TALL, stride=PITCH), :]
        r = v.final[...] + full_of(v.grad_net[b])

        s = full_of(v.xc[b, 32 : 32 + AREA, 0:128])
        update, reset, cand = v.lu[b], v.lr[b], v.lc[b]
        cg = half_of(r * update * (1.0 - cand * cand))
        v.gc[b, 32 : 32 + AREA, 256:384] = cg
        reset_grad = 0.0
        for t in range(5):
            rows = slice((4 - t) * COLS, (4 - t) * COLS + AREA)
            reset_grad = reset_grad + nt(v.gc[b, rows, 256:384], v.w_ls[t * 128 : (t + 1) * 128, 256:384])
        v.gc[b, 32 : 32 + AREA, 0:128] = half_of(r * (cand - s) * update * (1.0 - update))
        v.gc[b, 32 : 32 + AREA, 128:256] = half_of(reset_grad * s * reset * (1.0 - reset))
        state_grad = r * (1.0 - update) + reset_grad * reset
        inputs_grad = 0.0
        for t in range(5):
            rows = slice((4 - t) * COLS, (4 - t) * COLS + AREA)
            state_grad = state_grad + nt(v.gc[b, rows, 0:256], v.w_ls[t * 128 : (t + 1) * 128, 0:256])
            inputs_grad = inputs_grad + nt(v.gc[b, rows, :], v.w_li[t * 256 : (t + 1) * 256, :])
        high = half_of(own_dg)
        low = half_of(own_dg - full_of(high))
        pick = half_of(jnp.where(lane_index((8, LANES)) == row_index((8, LANES)) + 126, 1.0, 0.0))
        v.tmp[0:SPAN, :] = tn(high, pick) + tn(low, pick)
        for x in range(COLS):
            v.final[pl.ds(x, TALL, stride=COLS), :] = v.tmp[pl.ds(2 + x, TALL, stride=PITCH), :]
        v.lu[b] = state_grad
        v.lr[b] = inputs_grad[:, 0:128]
        v.lc[b] = inputs_grad[:, 128:256] + v.final[...]

        def peer(t, carry):
            at = pl.ds(pl.multiple_of(t * ROWS * COLS, 16), ROWS * COLS)
            v.a_state[t, b] = half_of(v.lu[b, at, :])
            v.a_context[t, b] = half_of(v.lr[b, at, :])
            v.a_motion[t, b] = half_of(v.lc[b, at, :])
            return carry

        lax.fori_loop(0, v.space, peer, 0)
        return carry

    for c in range(3):
        zb(c, 0, EDGE)[...] = jnp.zeros((EDGE, LANES), jnp.float32)
        zb(c, EDGE + SPREAD, EDGE)[...] = jnp.zeros((EDGE, LANES), jnp.float32)
    lax.fori_loop(0, BATCH, image, 0)
    v.swap_loss.receive()
    v.back_state.start()
    v.back_context.start()
    v.back_motion.start()


def unpack_back(v, src, dst):
    def peer(t, carry):
        for b in range(BATCH):
            value = full_of(src[t, b])
            for y in range(ROWS):
                at = pl.multiple_of(y * WIDE + t * COLS, COLS)
                dst[b, pl.ds(at, COLS), :] = value[y * COLS : (y + 1) * COLS, :]
        return carry

    lax.fori_loop(0, v.space, peer, 0)


def seams():
    starts, bias_row, _, _ = flat_rows()
    edges = sorted(starts.values()) + [bias_row]
    tiles = sorted({row // 16 for row in edges if row % 16})
    parts = {}
    for low, high in zip(edges, edges[1:]):
        for tile in tiles:
            if low < (tile + 1) * 16 and high > tile * 16:
                parts[tile] = parts.get(tile, 0) + 1
    return {tile: (index, parts[tile]) for index, tile in enumerate(tiles)}


class Flush:
    def __init__(self, v):
        self.v, self.at, self.busy, self.small = v, 0, {}, []
        self.tiles = seams()
        self.left = {tile: parts for tile, (_, parts) in self.tiles.items()}
        v.seam[...] = jnp.zeros_like(v.seam)
        top = (max(self.tiles) + 1) * 16
        rest = v.out_flat.shape[0] - top
        v.seam_low[16 * 16 : 16 * 16 + rest, :] = jnp.zeros((rest, LANES), jnp.bfloat16)
        self.write(16, rest, top)

    def write(self, index, rows, base):
        v = self.v
        copy = pltpu.make_async_copy(
            v.seam_low.at[index * 16 : index * 16 + rows], v.out_flat.at[base : base + rows], v.fsem.at[index]
        )
        copy.start()
        self.small.append(copy)

    def send(self, low, length, base):
        v, slot = self.v, self.at % 2
        self.at += 1
        if slot in self.busy:
            self.busy[slot].wait()
        cast_rows(v.stage.at[slot], 0, v.flat, low, length, jnp.bfloat16)
        copy = pltpu.make_async_copy(
            v.stage.at[slot, 0:length], v.out_flat.at[base : base + length], v.ssem.at[slot, 0]
        )
        copy.start()
        self.busy[slot] = copy

    def layer(self, start, rows):
        v, stop = self.v, start + rows
        for tile in self.tiles:
            low, high = max(start, tile * 16), min(stop, tile * 16 + 16)
            if low >= high:
                continue
            index = self.tiles[tile][0]
            v.seam[index, low - tile * 16 : high - tile * 16, :] = v.flat[MARGIN + low - start : MARGIN + high - start, :]
            self.left[tile] -= 1
            if not self.left[tile]:
                v.seam_low[index * 16 : index * 16 + 16, :] = half_of(v.seam[index])
                self.write(index, 16, tile * 16)
        low, high = -(-start // 16) * 16, stop // 16 * 16
        if high > low:
            self.send(MARGIN + low - start, high - low, low)

    def settle(self):
        for copy in list(self.busy.values()) + self.small:
            copy.wait()
        self.busy, self.small = {}, []


SHARE = 3072


class Reduce:
    ORDER = (
        (3, 3072, 3072), (3, 0, 3072), (2, 3072, 3072), (2, 0, 3072), (1, 3072, 3072), (1, 0, 3072),
        (0, 1024, 3072), (0, 4096, 2048), (0, 0, 1024),
    )

    def __init__(self, v, count):
        self.v, self.count = v, count
        self.flying, self.queue = [], []
        self.copies = {}
        rank = v.rank
        self.lower, self.upper = lax.rem(rank, 2), lax.div(rank, 2)
        self.side, self.depth = lax.rem(v.spot, 2), lax.div(v.spot, 2)
        self.group = v.space // 2

    def part(self, k):
        return self.ORDER[k][2] // 4 // self.v.space

    def slice_at(self, k, spot):
        return lax.rem(spot, 2) * (self.ORDER[k][2] // 8) + lax.div(spot, 2) * self.part(k)

    def offer(self, *numbers):
        self.queue += list(numbers)

    LONG = 7

    def stages(self, k):
        if k < self.LONG:
            return (self.core, self.across, self.side_sum, self.deep_sum, self.deep_out, self.owner, self.beside)
        return (self.core, self.across, self.stripes, self.along, self.beside)

    def tick(self):
        for entry in self.flying:
            self.stages(entry[0])[entry[1]](entry[0])
            entry[1] += 1
        self.flying = [entry for entry in self.flying if entry[1] < len(self.stages(entry[0]))]
        if self.queue:
            number = self.queue.pop(0)
            self.v.flush.settle()
            self.begin(number)
            self.flying.append([number, 0])

    def begin(self, k):
        v, slot = self.v, k % 2
        quarter, low, size = self.ORDER[k]
        start = quarter * self.count // (LANES * 16) * 16 + low
        half = size // 2

        def rows(which):
            return v.out_flat.at[pl.ds(pl.multiple_of(start + which * half, 16), half)]

        copy = remote(
            rows(1 - self.lower), v.rcore.at[slot, 0:half], v.rsend.at[0, slot], v.rrecv.at[0, slot], {DP: v.mate}
        )
        own = pltpu.make_async_copy(rows(self.lower), v.own.at[slot, 0:half], v.rlocal.at[slot])
        copy.start()
        own.start()
        self.copies[k] = (copy, own)

    def core(self, k):
        v, slot = self.v, k % 2
        copy, own = self.copies[k]
        copy.wait()
        own.wait()
        if k >= 2:
            self.x_copy(k - 2).wait_send()
        quarter = self.ORDER[k][2] // 4

        def add(step, carry):
            at = pl.multiple_of(step * 128, 128)
            near = pl.ds(pl.multiple_of(self.upper * quarter + at, 128), 128)
            far = pl.ds(pl.multiple_of((1 - self.upper) * quarter + at, 128), 128)
            to = pl.ds(at, 128)
            v.tx[slot, to, :] = half_of(full_of(v.own[slot, far, :]) + full_of(v.rcore[slot, far, :]))
            v.ks[slot, to, :] = full_of(v.own[slot, near, :]) + full_of(v.rcore[slot, near, :])
            return carry

        lax.fori_loop(0, quarter // 128, add, 0)
        self.x_copy(k).start()

    def x_copy(self, k):
        v, slot = self.v, k % 2
        rows = slice(0, self.ORDER[k][2] // 4)
        return remote(
            v.tx.at[slot, rows], v.rx.at[slot, rows], v.rsend.at[1, slot], v.rrecv.at[1, slot], {DP: v.other}
        )

    def s_copy(self, k, step):
        v, slot, part = self.v, k % 2, self.part(k)
        to = lax.rem(v.spot + step, v.space)
        src = v.ts.at[slot, pl.ds(pl.multiple_of(self.slice_at(k, to), 16), part)]
        dst = v.rs.at[slot, v.spot, 0:part]
        return remote(src, dst, v.s2send.at[slot, step], v.s2recv.at[slot, step], {SPACE: to})

    def each(self, what, start, stop):
        def body(step, carry):
            what(step)
            return carry

        lax.fori_loop(start, stop, body, 0)

    def across(self, k):
        v, slot = self.v, k % 2
        self.x_copy(k).wait_recv()
        if k < self.LONG:
            self.across_long(k)
            return

        def add(step, carry):
            to = pl.ds(pl.multiple_of(step * 128, 128), 128)
            value = v.ks[slot, to, :] + full_of(v.rx[slot, to, :])
            v.ks[slot, to, :] = value
            v.ts[slot, to, :] = half_of(value)
            return carry

        lax.fori_loop(0, self.ORDER[k][2] // 4 // 128, add, 0)
        part = self.part(k)
        v.acc[slot, 0:part, :] = v.ks[slot, pl.ds(pl.multiple_of(self.slice_at(k, v.spot), 16), part), :]
        self.each(lambda step: self.s_copy(k, step).start(), 1, v.space)

    def across_long(self, k):
        v, slot = self.v, k % 2
        if k >= 2:
            self.side_copy(k - 2).wait_send()
        rows = self.ORDER[k][2] // 8

        def add(step, carry):
            at = pl.multiple_of(step * 128, 128)
            near = pl.ds(pl.multiple_of(self.side * rows + at, 128), 128)
            far = pl.ds(pl.multiple_of((1 - self.side) * rows + at, 128), 128)
            to = pl.ds(at, 128)
            v.ty[slot, to, :] = half_of(v.ks[slot, far, :] + full_of(v.rx[slot, far, :]))
            v.ky[slot, to, :] = v.ks[slot, near, :] + full_of(v.rx[slot, near, :])
            return carry

        lax.fori_loop(0, rows // 128, add, 0)
        self.side_copy(k).start()

    def side_copy(self, k):
        v, slot = self.v, k % 2
        return remote(v.ty.at[slot], v.ry.at[slot], v.rsend.at[2, slot], v.rrecv.at[2, slot], {SPACE: v.twin})

    def deep_at(self, k, depth):
        return pl.ds(pl.multiple_of(depth * self.part(k), 16), self.part(k))

    def deep_copy(self, k, step):
        v, slot = self.v, k % 2
        to = lax.rem(self.depth + step, self.group)
        return remote(
            v.tz.at[slot, self.deep_at(k, to)], v.rz.at[slot, self.depth], v.z1send.at[slot, step],
            v.z1recv.at[slot, step], {SPACE: to * 2 + self.side},
        )

    def side_sum(self, k):
        v, slot = self.v, k % 2
        self.side_copy(k).wait_recv()
        if k >= 2:
            self.each(lambda step: self.deep_copy(k - 2, step).wait_send(), 1, self.group)
        value = v.ky[slot] + full_of(v.ry[slot])
        v.tz[slot] = half_of(value)
        v.ky[slot] = value
        v.kz[slot] = v.ky[slot, self.deep_at(k, self.depth), :]
        self.each(lambda step: self.deep_copy(k, step).start(), 1, self.group)

    def out_copy(self, k, step):
        v, slot = self.v, k % 3
        to = lax.rem(self.depth + step, self.group)
        block = v.az.at[slot, self.deep_at(k, self.depth)]
        return remote(
            block, block, v.z2send.at[slot, step], v.z2recv.at[slot, step], {SPACE: to * 2 + self.side}
        )

    def deep_sum(self, k):
        v, slot = self.v, k % 2
        self.each(lambda step: self.deep_copy(k, step).wait_recv(), 1, self.group)

        def add(step, value):
            return value + full_of(v.rz[slot, lax.rem(self.depth + step, self.group)])

        value = lax.fori_loop(1, self.group, add, v.kz[slot])
        if k >= 2:
            self.own_wait(k - 2)
        v.az[k % 3, self.deep_at(k, self.depth), :] = half_of(value)
        self.each(lambda step: self.out_copy(k, step).start(), 1, self.group)

    def own_rows(self, k, lower, upper):
        quarter, low, size = self.ORDER[k]
        at = low + lower * (size // 2) + upper * (size // 4) + self.side * (size // 8)
        return pl.ds(pl.multiple_of(at, 16), size // 8)

    def own_copy(self, k, source=None):
        v = self.v
        quarter = self.ORDER[k][0]
        if source is None:
            rows, sem = self.own_rows(k, self.lower, self.upper), v.orecv.at[k, v.rank]
        else:
            rows, sem = self.own_rows(k, source % 2, source // 2), v.orecv.at[k, source]
        return remote(v.az.at[k % 3], v.gath.at[rows], v.osend.at[k % 3], sem, {DP: quarter if source is None else source})

    def own_wait(self, k):
        pl.when(self.v.rank != self.ORDER[k][0])(self.own_copy(k).wait_send)

    def deep_out(self, k):
        v = self.v
        self.each(lambda step: self.out_copy(k, step).wait(), 1, self.group)
        pl.when(v.rank != self.ORDER[k][0])(self.own_copy(k).start)

        @pl.when(v.rank == self.ORDER[k][0])
        def _():
            v.gath[self.own_rows(k, self.lower, self.upper), :] = v.az[k % 3]

    def owner(self, k):
        v = self.v

        @pl.when(v.rank == self.ORDER[k][0])
        def _():
            for source in range(4):
                if source != self.ORDER[k][0]:
                    self.own_copy(k, source).wait_recv()
            for copy in self.y_copies(k):
                copy.start()

    def place(self, k, lower, upper, spot):
        quarter, low, size = self.ORDER[k]
        at = low + lower * (size // 2) + upper * (size // 4) + self.slice_at(k, spot)
        return pl.ds(pl.multiple_of(at, 16), self.part(k))

    def f_copy(self, k, step):
        v, slot = self.v, k % 2
        quarter = self.ORDER[k][0]
        to = lax.rem(self.depth + step, self.group) * 2 + self.side
        return remote(
            v.fin.at[slot, 0 : self.part(k)], v.gath.at[self.place(k, self.lower, self.upper, v.spot)],
            v.fsend.at[slot, step], v.frecv.at[k, v.rank, self.depth], {DP: quarter, SPACE: to},
        )

    def f_all(self, k, what):
        v = self.v
        pl.when(v.rank != self.ORDER[k][0])(lambda: what(self.f_copy(k, 0)))
        self.each(lambda step: what(self.f_copy(k, step)), 1, self.group)

    def stripes(self, k):
        v, slot, part = self.v, k % 2, self.part(k)
        quarter = self.ORDER[k][0]
        self.each(lambda step: self.s_copy(k, step).wait_recv(), 1, v.space)

        def add(step, value):
            return value + full_of(v.rs[slot, lax.rem(v.spot + step, v.space), 0:part])

        value = half_of(lax.fori_loop(1, v.space, add, v.acc[slot, 0:part, :]))
        v.fin[slot, 0:part, :] = value

        @pl.when(v.rank == quarter)
        def _():
            v.gath[self.place(k, self.lower, self.upper, v.spot), :] = v.fin[slot, 0:part, :]

        self.f_all(k, lambda copy: copy.start())

    def f_wait(self, k, source, step):
        v = self.v
        depth = lax.rem(self.depth + step, self.group)
        spot = depth * 2 + self.side
        remote(
            v.fin.at[0, 0 : self.part(k)], v.gath.at[self.place(k, source % 2, source // 2, spot)],
            v.fsend.at[0, 0], v.frecv.at[k, source, depth], {SPACE: v.twin},
        ).wait_recv()

    def y_copies(self, k):
        v = self.v
        quarter, low, size = self.ORDER[k]
        out = []
        for i in range(4):
            at = pl.multiple_of(low + i * (size // 4) + self.side * (size // 8), 16)
            block = v.gath.at[pl.ds(at, size // 8)]
            out.append(remote(block, block, v.ysend.at[k, i], v.yrecv.at[k, i], {SPACE: v.twin}))
        return out

    def along(self, k):
        v = self.v
        quarter = self.ORDER[k][0]

        @pl.when(v.rank == quarter)
        def _():
            for source in range(4):
                self.each(
                    lambda step: self.f_wait(k, source, step), 1 if source == quarter else 0, self.group
                )
            for copy in self.y_copies(k):
                copy.start()

    def beside(self, k):
        v = self.v

        @pl.when(v.rank == self.ORDER[k][0])
        def _():
            for copy in self.y_copies(k):
                copy.wait()

    def settle(self):
        v = self.v
        for k in range(self.LONG - 2, self.LONG):
            self.side_copy(k).wait_send()
            self.each(lambda step: self.deep_copy(k, step).wait_send(), 1, self.group)
            self.own_wait(k)
        for k in range(self.LONG, len(self.ORDER)):
            self.x_copy(k).wait_send()
            self.each(lambda step: self.s_copy(k, step).wait_send(), 1, v.space)
            self.f_all(k, lambda copy: copy.wait_send())

    def ready(self):
        v, count = self.v, self.count
        v.gath[2 * SHARE :, :] = jnp.zeros((32, LANES), jnp.bfloat16)

        @pl.when(v.rank == 3)
        def _():
            at = self.bias_base() - 3 * count // (LANES * 16) * 16
            v.gath[at : at + 32, :] = half_of(full_of(v.gath[at : at + 32, :]) + v.bsum[...])

    def lay(self, first, last):
        v, count = self.v, self.count
        offset = v.rank * count - quarter_base(v.rank, count) * LANES
        skip = lax.div(offset, LANES)
        matrix = lane_matrix(lax.rem(offset, LANES), False)

        def out(step):
            at = pl.multiple_of(step * 256, 256)
            slot = lax.rem(step, 2)
            return pltpu.make_async_copy(v.gout.at[slot], v.out_grads.at[pl.ds(at, 256)], v.osem.at[4 + slot])

        def place(step, carry):
            at = pl.multiple_of(step * 256, 256)
            both = mm(v.gath[pl.ds(at, 288), :], matrix)
            v.tmp[0:288, :] = both[:, 0:LANES]
            v.tmp[288:576, :] = both[:, LANES:]
            pl.when(step > first + 1)(out(step - 2).wait)
            v.gout[lax.rem(step, 2)] = v.tmp[pl.ds(skip, 256), :] + v.tmp[pl.ds(skip + 289, 256), :]
            out(step).start()
            return carry

        lax.fori_loop(first, last, place, 0)
        for step in (last - 2, last - 1):
            out(step).wait()

    def bias_base(self):
        return flat_rows()[1] // 16 * 16

    def bias_core(self):
        v = self.v
        self.b1 = remote(v.bown, v.bcore, v.bsend.at[0], v.brecv.at[0], {DP: v.mate})
        self.b1.start()

    def bias_across(self):
        v = self.v
        self.b1.wait()
        v.btwo[...] = v.bown[...] + v.bcore[...]
        self.b2 = remote(v.btwo, v.bacross, v.bsend.at[1], v.brecv.at[1], {DP: v.other})
        self.b2.start()

    def bias_stripes(self):
        v = self.v
        self.b2.wait()
        v.bfour[...] = v.btwo[...] + v.bacross[...]
        self.b3 = Swap(v, 8, v.bfour, v.ball, True)
        self.b3.start()

    def bias_end(self):
        v = self.v
        self.b3.receive()
        self.b3.sent()
        v.ball[v.spot] = v.bfour[...]
        v.bsum[...] = jnp.sum(v.ball[...], axis=0)


def ones_sum(g):
    return mm(jnp.ones((8, g.shape[0]), jnp.bfloat16), g)[0:1, :]


def keep_bias(v, name, value):
    for block in range(-(-value.shape[1] // 128)):
        at = BIAS_AT[name] + block
        v.gbias[at : at + 1, :] = value[:, block * 128 : (block + 1) * 128]


def gradients_gru(v, gates_name, cand_name, parts, g_of):
    starts, _, _, _ = flat_rows()
    total = 0.0
    for b in range(BATCH):
        total = total + ones_sum(g_of(b))
    keep_bias(v, gates_name, total[:, 0:256])
    keep_bias(v, cand_name, total[:, 256:384])

    for t in range(5):
        s_part, i_part, r_part = parts(t)
        state = tn_all(s_part, g_of, 0, 256)
        v.mm_tmp[pl.ds(MARGIN + t * 384, 128), :] = tn_all(r_part, g_of, 256, 384)
        inputs = tn_all(i_part, g_of, 0, 384)
        pack_pairs(v.flat, t * 384, 128, state[:, 0:128], state[:, 128:256])
        pack_pairs(v.flat, t * 384 + 128, 256, inputs[:, 0:128], inputs[:, 128:256])
        v.mm_tmp[pl.ds(MARGIN + t * 384 + 128, 256), :] = inputs[:, 256:384]
    v.flush.layer(starts[gates_name], 3840)
    cast_rows(v.flat, MARGIN, v.mm_tmp, MARGIN, 1920, jnp.float32)
    v.flush.layer(starts[cand_name], 1920)


def tn_all(part, g_of, low, high):
    total = 0.0
    for b in range(BATCH):
        total = total + tn(part(b), g_of(b, low, high))
    return total


def gradients_heads(v):
    starts, _, _, _ = flat_rows()
    total = 0.0
    for b in range(BATCH):
        total = total + ones_sum(v.hgo[b])
    keep_bias(v, FLOW_HIDDEN, total[:, 0:256])
    keep_bias(v, MASK_HIDDEN, total[:, 256:512])
    for name, lane in ((FLOW_HIDDEN, 0), (MASK_HIDDEN, 256)):
        for tap in range(9):
            value = 0.0
            for b in range(BATCH):
                value = value + tn(heads_part(v, b, tap)[...], v.hgo[b, :, lane : lane + 256])
            pack_pairs(v.flat, tap * 128, 128, value[:, 0:128], value[:, 128:256])
        v.flush.layer(starts[name], 2304)

    total = 0.0
    sums = 0.0
    for b in range(BATCH):
        total = total + mm(v.dtb[b], v.feat[b])
        sums = sums + jnp.sum(full_of(half_of(v.dg[b])), axis=1, keepdims=True)
    lane1 = lane_index((1, LANES))
    at = BIAS_AT[FLOW_OUT]
    v.gbias[at : at + 1, :] = jnp.where(lane1 == 0, sums[0:1, :], jnp.where(lane1 == 1, sums[1:2, :], 0.0))
    v.fo_tmp[...] = total[:, 0:128]
    v.fo_tmp2[...] = total[:, 128:256]
    for quarter in range(4):
        value = 0.0
        for which in range(2):
            rows = jnp.concatenate(
                [v.fo_tmp[pl.ds(which, 9, stride=2), :], v.fo_tmp2[pl.ds(which, 9, stride=2), :]], axis=1
            )
            value = value + nt(half_of(rows), split_pick(which, quarter))
        v.flat[pl.ds(MARGIN + quarter, 9, stride=4), :] = value
    v.flush.layer(starts[FLOW_OUT], 36)

    lane = lane_index((128, LANES))
    low_half = lane < 64
    even, odd = [], []
    total = 0.0
    for b in range(BATCH):
        total = total + ones_sum(quarter_of(v.grad_mask[b]))
    for block in range(5):
        wide = min(128, MASK - block * 128)
        at = BIAS_AT[MASK_OUT] + block
        v.gbias[at : at + 1, 0:wide] = total[:, block * 128 : block * 128 + wide]
        value = 0.0
        for b in range(BATCH):
            value = value + tn(v.mf[b], quarter_of(v.grad_mask[b, :, block * 128 : block * 128 + wide]))
        v.pair_a[:, 0:wide] = value
        even.append(v.pair_a[pl.ds(0, 128, stride=2), :])
        odd.append(pltpu.roll(v.pair_a[pl.ds(1, 128, stride=2), :], 64, 1))
    for i in range(4):
        v.flat[pl.ds(MARGIN + i, 128, stride=9), :] = even[i]
    v.flat[pl.ds(MARGIN + 4, 128, stride=9), :] = jnp.where(low_half, even[4], odd[0])
    for i in range(4):
        v.flat[pl.ds(MARGIN + 5 + i, 128, stride=9), :] = jnp.where(low_half, odd[i], odd[i + 1])
    v.flush.layer(starts[MASK_OUT], 1152)


def rows_back(v):
    v.back_state.receive()
    take_own(v, v.a_state, v.b_state)
    unpack_back(v, v.b_state, v.state)
    v.reduce.tick()
    v.back_context.receive()
    v.back_motion.receive()
    take_own(v, v.a_context, v.b_context)
    take_own(v, v.a_motion, v.b_motion)
    unpack_back(v, v.b_context, v.lr)
    unpack_back(v, v.b_motion, v.lu)

    def image(b, carry):
        at = pl.ds(pl.multiple_of(b * AREA, AREA), AREA)
        r = v.state[b]
        s = full_of(v.net[b])
        update, reset, cand = v.ru[b], v.rr[b], v.rc[b]
        cg = full_of(half_of(r * update * (1.0 - cand * cand)))
        spread_five(v, cg, None, 256, True)
        reset_grad = 0.0
        for t in range(5):
            reset_grad = reset_grad + nt(
                taps_part(v, t, 256, 384)[...], v.w_rs[t * 128 : (t + 1) * 128, 256:384]
            )
        low = full_of(half_of(r * (cand - s) * update * (1.0 - update)))
        high = full_of(half_of(reset_grad * s * reset * (1.0 - reset)))
        spread_five(v, low, None, 0, True)
        spread_five(v, high, None, 128, True)
        v.gr[b] = taps_part(v, 2, 0, 384)[...]
        state_grad = r * (1.0 - update) + reset_grad * reset
        inputs_grad = jnp.concatenate([v.lr[b], v.lu[b]], axis=1)
        for t in range(5):
            state_grad = state_grad + nt(taps_part(v, t, 0, 256)[...], v.w_rs[t * 128 : (t + 1) * 128, 0:256])
            inputs_grad = inputs_grad + nt(taps_part(v, t, 0, 384)[...], v.w_ri[t * 256 : (t + 1) * 256, :])
        v.ru[b] = state_grad
        v.rr[b] = inputs_grad[:, 0:128]
        motion = inputs_grad[:, 128:256]
        grad = half_of(motion * full_of(v.slope_m[b]))
        v.mge[b, 256:896, :] = grad
        high = half_of(motion)
        low = half_of(motion - full_of(high))
        pick = half_of(jnp.where(lane_index((16, LANES)) == row_index((16, LANES)) + 126, 1.0, 0.0))
        v.gf_base[b] = (nt(pick, high) + nt(pick, low))[0:8, :]
        return carry

    lax.fori_loop(0, BATCH, image, 0)
    v.halo_mg.start()
    v.store_gnet.start()
    v.store_gctx.start()


def gcorr_stores(v, b):
    return [
        pltpu.make_async_copy(v.mm_tmp.at[y * 328 : y * 328 + CORR], v.out_gcorr.at[b, y], v.gsem.at[y])
        for y in range(ROWS)
    ]


def branch_back(v):
    v.halo_mg.receive()

    def image(b, carry):
        up = jnp.where(v.spot > 0, full_of(v.mge[b, 0:256, :]), 0.0)
        own = full_of(v.mge[b, 256:896, :])
        down = jnp.where(v.spot < v.space - 1, full_of(v.mge[b, 896:1152, :]), 0.0)
        spread_rows(v, 0, (jnp.concatenate([up, own, down], axis=0),), 1152, v.xi, 0, 128, True)
        joint = 0.0
        for a in range(3):
            for c in range(3):
                k = (a * 3 + c) * 256
                joint = joint + nt(
                    v.xi[(2 - a) * 128 : (2 - a) * 128 + 896, c * 128 : (c + 1) * 128], v.w_mm[k : k + 256, :]
                )
        branch = joint * full_of(v.slope_j[b])
        low = full_of(half_of(edge_rows(v, branch[:, 0:128], WIDE)))
        high = full_of(half_of(edge_rows(v, branch[:, 128:256], WIDE)))
        spread_rows(v, 0, (low, high), 896, v.hx_j.at[b], 0, 256, True)
        return carry

    lax.fori_loop(0, BATCH, image, 0)


def branch_own(v, b, low=0, high=256):
    return v.hx_j[b, 128:768, 256 + low : 256 + high]


def flow_back(v):
    def image(b, carry):
        flow_grad = 0.0
        for a in range(3):
            rows = slice((2 - a) * 128, (2 - a) * 128 + 640)
            for c in range(3):
                k = a * 3 + c
                flow_grad = flow_grad + nt(
                    v.hx_j[b, rows, c * 256 + 128 : (c + 1) * 256], v.w_fm[k * 128 : (k + 1) * 128, :]
                )
        v.fpg[b] = half_of(flow_grad * full_of(v.slope_fi[b]))
        z = nt(v.w_fi[...], v.fpg[b])
        total = jnp.zeros((32, LANES), jnp.float32)
        lane = lane_index((32, LANES))
        for across in range(7):
            v.fs[across] = jnp.zeros((32, LANES), jnp.float32)
            for y in range(ROWS):
                v.fs[across, 2 * y : 2 * y + 16, :] += z[across * 16 : across * 16 + 16, y * 128 : (y + 1) * 128]
            d = across - 3
            value = v.fs[across]
            if d:
                value = pltpu.roll(value, d % LANES, 1)
                value = jnp.where((lane - d >= 0) & (lane - d < WIDE), value, 0.0)
            total = total + value
        v.gf[b] = total
        return carry

    lax.fori_loop(0, BATCH, image, 0)
    v.halo_gf.start()


def corr_back(v):
    def image(b, carry):
        corr_grad = 0.0
        for a in range(3):
            rows = slice((2 - a) * 128, (2 - a) * 128 + 640)
            for c in range(3):
                k = a * 3 + c
                corr_grad = corr_grad + nt(v.hx_j[b, rows, c * 256 : (c + 1) * 256], v.w_cm[k * 256 : (k + 1) * 256, :])
        v.cpg[b] = half_of(corr_grad * full_of(v.slope_ci[b]))
        stores = gcorr_stores(v, b)
        for store in stores:
            pl.when(b > 0)(store.wait)
        gcorr = nt(v.w_ci[...], v.cpg[b])
        for y in range(ROWS):
            v.mm_tmp[y * 328 : y * 328 + CORR, :] = gcorr[:, y * WIDE : (y + 1) * WIDE]
        for store in stores:
            store.start()
        return carry

    lax.fori_loop(0, BATCH, image, 0)


def summed(v, ref, name):
    total = 0.0
    for b in range(BATCH):
        total = total + ones_sum(ref(b))
    keep_bias(v, name, total)


def gradients_motion(v):
    starts = flat_rows()[0]
    summed(v, lambda b: v.mge[b, 256:896, :], MOTION_MIX)
    for k in range(9):
        a, c = k // 3, k % 3
        value = 0.0
        for b in range(BATCH):
            value = value + tn(
                v.hx_j[b, a * 128 : a * 128 + 640, c * 256 : (c + 1) * 256], v.mge[b, 256:896, :]
            )
        v.mm_tmp[k * 256 : (k + 1) * 256, :] = value
    lane36 = lane_index((36, LANES))
    for r in range(63):
        first = v.mm_tmp[pl.ds(r, 36, stride=64), :]
        second = v.mm_tmp[pl.ds(r + 1, 36, stride=64), :]
        if r:
            first = pltpu.roll(first, LANES - 2 * r, 1)
        second = pltpu.roll(second, 126 - 2 * r, 1)
        v.flat[pl.ds(MARGIN + r, 36, stride=63), :] = jnp.where(lane36 < 126 - 2 * r, first, second)
    v.flush.layer(starts[MOTION_MIX], 2268)


def gradients_branches(v):
    starts = flat_rows()[0]
    summed(v, lambda b: branch_own(v, b), CORR_MIX)
    summed(v, lambda b: branch_own(v, b, 128, 256), FLOW_MIX)
    for k in range(9):
        a, c = k // 3, k % 3
        value = 0.0
        for b in range(BATCH):
            value = value + tn(
                v.hx_f[b, (a + 1) * 128 : (a + 1) * 128 + 640, c * 128 : (c + 1) * 128], branch_own(v, b, 128, 256)
            )
        v.pair_a[0:128, :] = value
        even, odd = (v.pair_a[pl.ds(i, 64, stride=2), :] for i in range(2))
        v.flat[MARGIN + 64 * k : MARGIN + 64 * (k + 1), :] = jnp.where(
            lane_index((64, LANES)) < 64, pltpu.roll(even, 64, 1), odd
        )
    v.flush.layer(starts[FLOW_MIX], 576)

    low_half = lane_index((128, LANES)) < 64
    for k in range(9):
        a, c = k // 3, k % 3
        value = 0.0
        for b in range(BATCH):
            value = value + tn(
                v.hx_c[b, (a + 1) * 128 : (a + 1) * 128 + 640, c * 256 : (c + 1) * 256], branch_own(v, b)
            )
        v.pair_a[...] = value[:, 0:128]
        v.pair_b[...] = value[:, 128:256]
        even, odd = (v.pair_a[pl.ds(i, 128, stride=2), :] for i in range(2))
        even_high, odd_high = (v.pair_b[pl.ds(i, 128, stride=2), :] for i in range(2))
        odd, odd_high = pltpu.roll(odd, 64, 1), pltpu.roll(odd_high, 64, 1)
        at = MARGIN + 384 * k
        v.flat[pl.ds(at, 128, stride=3), :] = even
        v.flat[pl.ds(at + 1, 128, stride=3), :] = jnp.where(low_half, even_high, odd)
        v.flat[pl.ds(at + 2, 128, stride=3), :] = jnp.where(low_half, odd, odd_high)
        if k == 4:
            v.reduce.tick()
    v.flush.layer(starts[CORR_MIX], 3456)


def gradients_flow_in(v):
    starts = flat_rows()[0]
    summed(v, lambda b: v.fpg[b], FLOW_IN)
    value = 0.0
    for b in range(BATCH):
        value = value + mm(v.xt[b, :, 256:896], v.fpg[b])
    v.flow_tmp[...] = value
    for across in range(7):
        for comp in range(2):
            v.flat[pl.ds(MARGIN + across * 2 + comp, 7, stride=14), :] = v.flow_tmp[
                pl.ds(across * 16 + comp, 7, stride=2), :
            ]
    v.flush.layer(starts[FLOW_IN], 98)


def gradients_corr_in(v):
    starts = flat_rows()[0]
    summed(v, lambda b: v.cpg[b], CORR_IN)
    value = 0.0
    for b in range(BATCH):
        value = value + mm(lines_of(v.corr, b, ROWS), v.cpg[b])
    pack_pairs(v.flat, 0, 324, value[:, 0:128], value[:, 128:256])
    v.flush.layer(starts[CORR_IN], 648)


def bias_tile(v):
    starts, bias_row, spots, inner = flat_rows()
    lead = bias_row % 16
    lane1 = lane_index((1, LANES))
    v.bown[...] = jnp.zeros_like(v.bown)
    for name, height, width in shapes():
        for block in range(-(-width // LANES)):
            value = v.gbias[BIAS_AT[name] + block : BIAS_AT[name] + block + 1, :]
            if name == FLOW_MIX:
                value = pltpu.roll(value, 64, 1)
            left = width - block * LANES
            if left < LANES:
                value = jnp.where(lane1 < left, value, 0.0)
            at = spots[name] + block * LANES
            row, shift = lead + at // LANES, at % LANES
            moved = pltpu.roll(value, shift, 1) if shift else value
            v.bown[row : row + 1, :] = v.bown[row : row + 1, :] + jnp.where(lane1 >= shift, moved, 0.0)
            if shift:
                v.bown[row + 1 : row + 2, :] = v.bown[row + 1 : row + 2, :] + jnp.where(lane1 < shift, moved, 0.0)


def finish(v):
    spot, last = v.spot, v.space - 1
    v.halo_gf.receive()
    for b in range(BATCH):
        v.tmp2[...] = v.gf[b]
        up = jnp.where(spot > 0, v.gf_up[b], 0.0)
        down = jnp.where(spot < last, v.gf_down[b], 0.0)
        v.tmp2[6:12, :] += up[16:22, :]
        v.tmp2[10:16, :] += down[0:6, :]
        for y in range(ROWS):
            v.out_gflow[b, 2 * y : 2 * y + 2, :] = (
                v.tmp2[6 + 2 * y : 8 + 2 * y, :] + v.gf_base[b, 0:2, y * 128 : (y + 1) * 128]
            )
    v.loss_in[v.spot] = v.losses[...]
    total = jnp.sum(v.loss_in[...], axis=0)
    counts = jnp.sum(v.counts[...], axis=0)
    v.out_loss[...] = total / jnp.maximum(counts, 1.0)


class View:
    pass


def main_kernel(names, space, count, *refs):
    v = View()
    for name, ref in zip(names, refs):
        setattr(v, name, ref)
    v.space = space
    v.lu, v.lc = v.motion, v.state
    v.spot = lax.axis_index(SPACE)
    v.rank = lax.axis_index(DP)
    v.mate, v.other, v.twin = mate_of(v.rank), lax.rem(v.rank + 2, 4), mate_of(v.spot)
    spot = v.spot
    barrier = pltpu.get_barrier_semaphore()

    def hello(step, carry):
        pl.semaphore_signal(barrier, inc=1, device_id={SPACE: lax.rem(spot + step, space)}, device_id_type=MESH)
        return carry

    lax.fori_loop(1, space, hello, 0)
    for turn in range(1, 4):

        def greet_rank(step, carry):
            place = lax.rem(spot + 2 * step, space)
            device = {DP: lax.rem(v.rank + turn, 4), SPACE: place}
            pl.semaphore_signal(barrier, inc=1, device_id=device, device_id_type=MESH)
            return carry

        lax.fori_loop(0, space // 2, greet_rank, 0)
    pl.semaphore_wait(barrier, space - 1 + 3 * (space // 2))

    v.store_gnet = pltpu.make_async_copy(v.ru, v.out_gnet, v.osem.at[0])
    v.store_gctx = pltpu.make_async_copy(v.rr, v.out_gctx, v.osem.at[1])
    rows = row_index((8, LANES))
    counted = jnp.zeros((8, LANES), jnp.float32)
    for b in range(BATCH):
        counted = jnp.where(rows == b, jnp.sum(v.valid[b, 0:1, :]), counted)
    v.count_out[...] = counted
    v.pick_count = lambda counts, b: jnp.sum(jnp.where((rows == b) & (lane_index((8, LANES)) == 0), counts, 0.0))
    v.swap_count = Swap(v, 0, v.count_out, v.counts, True)
    v.swap_context = Swap(v, 1, v.a_context, v.b_context)
    v.swap_motion = Swap(v, 2, v.a_motion, v.b_motion)
    v.swap_state = Swap(v, 3, v.a_state, v.b_state)
    v.back_context = Swap(v, 4, v.a_context, v.b_context)
    v.back_motion = Swap(v, 5, v.a_motion, v.b_motion)
    v.back_state = Swap(v, 6, v.a_state, v.b_state)
    v.swap_loss = Swap(v, 7, v.losses, v.loss_in, True)
    v.halo_corr = Halo(v, 0, v.corr.at[:, 0:2], v.corr.at[:, 3:5], v.corr_down, v.corr_up)
    v.halo_flow = Halo(v, 1, v.flow, v.flow, v.flow_down, v.flow_up)
    v.halo_final = Halo(v, 2, v.e_left, v.e_right, v.f_right, v.f_left)
    v.halo_mask = Halo(v, 3, v.m_left, v.m_right, v.n_right, v.n_left)
    v.halo_dg = Halo(v, 4, v.dg, v.dg, v.dg_right, v.dg_left)
    v.halo_mg = Halo(v, 5, v.mge.at[:, 256:512], v.mge.at[:, 640:896], v.mge.at[:, 896:1152], v.mge.at[:, 0:256])
    v.halo_gf = Halo(v, 6, v.gf, v.gf, v.gf_down, v.gf_up)

    load = pltpu.make_async_copy(v.local, v.gath.at[0:BLOCK], v.gsend.at[4, 2])
    load.start()
    v.halo_flow.start()
    v.halo_corr.start()
    v.swap_count.start()
    load.wait()
    gather_start(v, count)

    def first(b, carry):
        v.state[b] = full_of(v.context[b])
        pack_rows(v, v.state, b, v.a_context)
        return carry

    lax.fori_loop(0, BATCH, first, 0)
    v.swap_context.start()
    v.halo_flow.receive()
    gather_pass(v, 0, 2)
    early_taps(v)
    gather_pass(v, 2, 4)
    columns_zero(v)
    gather_end(v)
    unpack_encoder(v, count)
    v.halo_corr.receive()
    forward_rows(v)
    keep = [pltpu.make_async_copy(v.hx_c, v.out_keep_c, v.ksem.at[0]), pltpu.make_async_copy(v.hx_f, v.out_keep_f, v.ksem.at[1])]
    for copy in keep:
        copy.start()
    unpack_heads(v)
    mask_gradient(v)
    v.swap_context.receive()
    v.swap_motion.receive()
    v.swap_state.receive()
    take_own(v, v.a_context, v.b_context)
    take_own(v, v.a_motion, v.b_motion)
    take_own(v, v.a_state, v.b_state)
    columns_in(v)
    columns_forward(v)
    for copy in keep:
        copy.wait()
    heads(v)
    mask_output(v)
    v.swap_context.sent()
    v.swap_motion.sent()
    v.swap_state.sent()
    heads_back(v)
    v.flush = Flush(v)
    red = v.reduce = Reduce(v, count)
    gradients_heads(v)
    red.offer(0)
    red.tick()
    gradients_gru(
        v,
        COLUMNS_GATES,
        COLUMNS_CANDIDATE,
        lambda t: (
            lambda b: v.xc[b, t * COLS : t * COLS + AREA, 0:128],
            lambda b: v.xc[b, t * COLS : t * COLS + AREA, 128:384],
            lambda b: v.xcr[b, t * COLS : t * COLS + AREA, :],
        ),
        lambda b, low=0, high=384: v.gc[b, 32 : 32 + AREA, low:high],
    )
    red.offer(1, 2)
    red.tick()
    rows_back(v)
    red.tick()
    keep = [
        pltpu.make_async_copy(v.out_keep_c, v.hx_c, v.ksem.at[0]),
        pltpu.make_async_copy(v.out_keep_f, v.hx_f, v.ksem.at[1]),
    ]
    for copy in keep:
        copy.start()
    gradients_gru(
        v,
        ROWS_GATES,
        ROWS_CANDIDATE,
        lambda t: (
            lambda b: v.xs[b * AREA : (b + 1) * AREA, t * 128 : (t + 1) * 128],
            lambda b: v.xi[b * AREA : (b + 1) * AREA, t * 256 : (t + 1) * 256],
            lambda b: v.xr[b * AREA : (b + 1) * AREA, t * 128 : (t + 1) * 128],
        ),
        lambda b, low=0, high=384: v.gr[b, :, low:high],
    )
    red.offer(3, 4)
    red.tick()
    gradients_motion(v)
    red.offer(5)
    red.tick()
    branch_back(v)
    red.tick()
    for copy in keep:
        copy.wait()
    gradients_branches(v)
    red.offer(6)
    red.tick()
    flow_back(v)
    red.tick()
    gradients_flow_in(v)
    red.offer(7)
    red.tick()
    corr_back(v)
    red.tick()
    gradients_corr_in(v)
    bias_tile(v)
    red.bias_core()
    red.offer(8)
    red.tick()
    for store in gcorr_stores(v, 0):
        store.wait()
    finish(v)
    red.bias_across()
    red.tick()
    red.bias_stripes()
    red.tick()
    red.bias_end()
    red.ready()
    red.tick()
    pl.when(v.rank > 0)(lambda: red.lay(0, 24))
    red.tick()
    pl.when(v.rank == 0)(lambda: red.lay(5, 24))
    red.tick()
    assert not red.flying and not red.queue
    pl.when(v.rank == 0)(lambda: red.lay(0, 5))
    red.settle()
    for swap in (v.swap_count, v.back_context, v.back_motion, v.back_state, v.swap_loss):
        swap.sent()
    for halo in (v.halo_corr, v.halo_flow, v.halo_final, v.halo_mask, v.halo_dg, v.halo_mg, v.halo_gf):
        halo.sent()
    v.store_gnet.wait()
    v.store_gctx.wait()
    pltpu.make_async_copy(v.mask_low, v.out_mask.at[0], v.osem.at[3]).wait()


def main_call(space, count, local, net, context, corr, flow, target, valid, grad_net, grad_mask):
    total = 3 * count // (LANES * 16) * 16 + BLOCK
    low, wide = jnp.bfloat16, jnp.float32
    peers = (space, BATCH, ROWS * COLS, LANES)
    ins = dict(
        local=local, net=net, context=context, corr=corr, flow=flow, target=target, valid=valid,
        grad_net=grad_net, grad_mask=grad_mask,
    )
    outs = dict(
        out_net=((BATCH, AREA, 128), low),
        out_flow=((BATCH, 8, SPAN), wide),
        out_mask=((BATCH, AREA, MASK), low),
        out_loss=((8, 128), wide),
        out_flat=((total, 128), low),
        out_gnet=((BATCH, AREA, 128), wide),
        out_gctx=((BATCH, AREA, 128), wide),
        out_gcorr=((BATCH, ROWS, CORR, 128), wide),
        out_gflow=((BATCH, 16, 128), wide),
        out_keep_c=((BATCH, 1152, 768), low),
        out_keep_f=((BATCH, 1152, 384), low),
        out_all=((4 * BLOCK, 128), low),
        out_grads=((BLOCK, 128), wide),
    )
    scratch = dict(
        stage=((2, 3904, 128), low),
        seam=((16, 16, 128), wide),
        mask_low=((AREA, MASK), low),
        gout=((2, 256, 128), wide),
        seam_low=((16 * 20, 128), low),
        own=((2, SHARE // 2, 128), low),
        rcore=((2, SHARE // 2, 128), low),
        tx=((2, SHARE // 4, 128), low),
        rx=((2, SHARE // 4, 128), low),
        ks=((2, SHARE // 4, 128), wide),
        ts=((2, 512, 128), low),
        acc=((2, 512 // space, 128), wide),
        rs=((2, space, 512 // space, 128), low),
        fin=((2, 512 // space, 128), low),
        ty=((2, SHARE // 8, 128), low),
        ry=((2, SHARE // 8, 128), low),
        ky=((2, SHARE // 8, 128), wide),
        tz=((2, SHARE // 8, 128), low),
        rz=((2, space // 2, SHARE // 4 // space, 128), low),
        kz=((2, SHARE // 4 // space, 128), wide),
        az=((3, SHARE // 8, 128), low),
        gath=((2 * SHARE + 32, 128), low),
        bown=((32, 128), wide), bcore=((32, 128), wide), btwo=((32, 128), wide), bacross=((32, 128), wide),
        bfour=((32, 128), wide), ball=((space, 32, 128), wide), bsum=((32, 128), wide),
        flat=((3904, 128), wide),
        pair_a=((256, 128), wide),
        pair_b=((256, 128), wide),
        flow_tmp=((112, 128), wide),
        mm_tmp=((3 * (2 * EDGE + SPREAD), 128), wide),
        fo_tmp=((32, 128), wide),
        fo_tmp2=((32, 128), wide),
        w_ci=((CORR, 256), low),
        w_cm=((2304, 256), low),
        w_fi=((112, 128), low),
        w_fm=((1152, 128), low),
        w_mm=((2304, 128), low),
        w_ri=((1280, 384), low),
        w_rs=((640, 384), low),
        w_li=((1280, 384), low),
        w_ls=((640, 384), low),
        w_h=((1152, 512), low),
        w_fo=((32, 256), low),
        w_mo=((256, 640), low),
        bias=((BIAS_ROWS, 128), wide),
        gbias=((BIAS_ROWS, 128), wide),
        corr_up=((BATCH, 2, CORR, 128), low),
        corr_down=((BATCH, 2, CORR, 128), low),
        flow_up=((BATCH, 16, 128), wide),
        flow_down=((BATCH, 16, 128), wide),
        fs=((7, 32, 128), wide),
        xt=((BATCH, 112, 1152), low),
        tmp=((1168, 128), wide),
        tmp2=((32, 128), wide),
        hx_c=((BATCH, 1152, 768), low),
        hx_f=((BATCH, 1152, 384), low),
        hx_j=((BATCH, 896, 768), low),
        slope_ci=((BATCH, AREA, 256), low),
        slope_fi=((BATCH, AREA, 128), low),
        slope_j=((BATCH, 896, 256), low),
        slope_m=((BATCH, AREA, 128), low),
        motion=((BATCH, AREA, 128), wide),
        state=((BATCH, AREA, 128), wide),
        xi=((BATCH * AREA, 1280), low),
        xs=((BATCH * AREA, 640), low),
        xr=((BATCH * AREA, 640), low),
        ru=((BATCH, AREA, 128), wide),
        rr=((BATCH, AREA, 128), wide),
        rc=((BATCH, AREA, 128), wide),
        lr=((BATCH, AREA, 128), wide),
        a_state=(peers, low), a_context=(peers, low), a_motion=(peers, low),
        b_state=(peers, low), b_context=(peers, low), b_motion=(peers, low),
        xc=((BATCH, AREA + 64, 384), low),
        xcr=((BATCH, AREA + 64, 128), low),
        gc=((BATCH, AREA + 64, 384), low),
        final=((AREA, 128), wide),
        e_left=((BATCH, 2, 48, 128), low), e_right=((BATCH, 2, 48, 128), low),
        f_left=((BATCH, 2, 48, 128), low), f_right=((BATCH, 2, 48, 128), low),
        m_left=((BATCH, 2, 48, 128), low), m_right=((BATCH, 2, 48, 128), low),
        n_left=((BATCH, 2, 48, 128), low), n_right=((BATCH, 2, 48, 128), low),
        slope_h=((BATCH, SPREAD, 512), low),
        feat=((BATCH, SPAN, 256), low),
        mf=((BATCH, AREA, 256), low),
        zt=((32, SPAN), wide),
        dg=((BATCH, 8, SPAN), wide),
        dg_left=((BATCH, 8, SPAN), wide), dg_right=((BATCH, 8, SPAN), wide),
        dt=((32, SPAN), wide),
        dto=((32, SPAN), wide),
        dtb=((BATCH, 32, SPAN), low),
        hgo=((BATCH, SPREAD, 512), low),
        gr=((BATCH, AREA, 384), low),
        mge=((BATCH, 1152, 128), low),
        cpg=((BATCH, AREA, 256), low),
        fpg=((BATCH, AREA, 128), low),
        gf_base=((BATCH, 8, AREA), wide),
        gf=((BATCH, 32, 128), wide), gf_up=((BATCH, 32, 128), wide), gf_down=((BATCH, 32, 128), wide),
        count_out=((8, 128), wide), counts=((space, 8, 128), wide),
        losses=((8, 128), wide), loss_in=((space, 8, 128), wide),
    )
    sems = dict(
        hsend=pltpu.SemaphoreType.DMA((7, 2)), hrecv=pltpu.SemaphoreType.DMA((7, 2)),
        asend=pltpu.SemaphoreType.DMA((9, space)), arecv=pltpu.SemaphoreType.DMA((9, space)),
        ssem=pltpu.SemaphoreType.DMA((2, 2)),
        fsem=pltpu.SemaphoreType.DMA((17,)),
        rsend=pltpu.SemaphoreType.DMA((3, 2)), rrecv=pltpu.SemaphoreType.DMA((3, 2)),
        z1send=pltpu.SemaphoreType.DMA((2, space // 2)), z1recv=pltpu.SemaphoreType.DMA((2, space // 2)),
        z2send=pltpu.SemaphoreType.DMA((3, space // 2)), z2recv=pltpu.SemaphoreType.DMA((3, space // 2)),
        osend=pltpu.SemaphoreType.DMA((3,)), orecv=pltpu.SemaphoreType.DMA((9, 4)),
        rlocal=pltpu.SemaphoreType.DMA((2,)),
        s2send=pltpu.SemaphoreType.DMA((2, space)), s2recv=pltpu.SemaphoreType.DMA((2, space)),
        fsend=pltpu.SemaphoreType.DMA((2, space // 2)), frecv=pltpu.SemaphoreType.DMA((9, 4, space // 2)),
        ysend=pltpu.SemaphoreType.DMA((9, 4)), yrecv=pltpu.SemaphoreType.DMA((9, 4)),
        bsend=pltpu.SemaphoreType.DMA((2,)), brecv=pltpu.SemaphoreType.DMA((2,)),
        ksem=pltpu.SemaphoreType.DMA((2,)),
        gsend=pltpu.SemaphoreType.DMA((5, 4)), grecv=pltpu.SemaphoreType.DMA((5, 4)),
        gsem=pltpu.SemaphoreType.DMA((ROWS,)),
        osem=pltpu.SemaphoreType.DMA((6,)),
    )
    vmem = pl.BlockSpec(memory_space=pltpu.VMEM)
    hbm = pl.BlockSpec(memory_space=pl.ANY)
    names = list(ins) + list(outs) + list(scratch) + list(sems)
    return pl.pallas_call(
        functools.partial(main_kernel, names, space, count),
        out_shape=[jax.ShapeDtypeStruct(*entry) for entry in outs.values()],
        in_specs=[hbm if name == "local" else vmem for name in ins],
        out_specs=[hbm if name in ("out_flat", "out_gnet", "out_gctx", "out_gcorr", "out_keep_c", "out_keep_f", "out_mask", "out_grads", "out_all") else vmem for name in outs],
        scratch_shapes=[pltpu.VMEM(*entry) for entry in scratch.values()] + list(sems.values()),
        compiler_params=pltpu.CompilerParams(
            collective_id=2, has_side_effects=True, vmem_limit_bytes=VMEM_LIMIT
        ),
    )(*ins.values())


VMEM_LIMIT = 64 * 2**20 - 2**17


def shards_wide(net, context, corr, flow, target, valid, grad_net, grad_mask, params):
    space = lax.axis_size(SPACE)
    count = params.shape[0]
    local = jnp.pad(params, (0, BLOCK * LANES - count)).reshape(BLOCK, LANES)
    flow_rows = jnp.transpose(flow.astype(jnp.float32), (0, 2, 1, 3)).reshape(BATCH, 2 * ROWS, WIDE)
    flow_rows = jnp.pad(flow_rows, ((0, 0), (0, 16 - 2 * ROWS), (0, 0)))
    pad = ((0, 0), (0, 0), (0, 0), (2, 2))
    target_ext = jnp.pad(target, pad).reshape(BATCH, 2, SPREAD)
    target_ext = jnp.pad(target_ext, ((0, 0), (0, 6), (0, SPAN - SPREAD)))
    valid_ext = jnp.pad(valid.astype(jnp.float32)[:, None], pad).reshape(BATCH, 1, SPREAD)
    valid_ext = jnp.broadcast_to(jnp.pad(valid_ext, ((0, 0), (0, 0), (0, SPAN - SPREAD))), (BATCH, 8, SPAN))
    outs = main_call(
        space, count, local, net.reshape(BATCH, AREA, HID), context.reshape(BATCH, AREA, CTX),
        jnp.transpose(corr, (0, 1, 3, 2)), flow_rows, target_ext, valid_ext,
        grad_net.reshape(BATCH, AREA, HID), grad_mask.reshape(BATCH, AREA, MASK),
    )
    new_net, new_flow, mask, loss, _, gnet, gctx, gcorr, gflow = outs[:9]
    new_flow = new_flow[:, 0:2, 0:SPREAD].reshape(BATCH, 2, TALL, PITCH)[..., 2 : 2 + COLS]
    grads = outs[-1].reshape(-1)[:count]
    return (
        new_net.reshape(BATCH, TALL, COLS, HID),
        new_flow,
        mask.reshape(BATCH, TALL, COLS, MASK),
        loss[0:BATCH, 0],
        grads,
        gnet.reshape(BATCH, ROWS, WIDE, HID),
        gctx.reshape(BATCH, ROWS, WIDE, CTX),
        jnp.transpose(gcorr, (0, 1, 3, 2)),
        jnp.transpose(gflow[:, 0 : 2 * ROWS].reshape(BATCH, ROWS, 2, WIDE), (0, 2, 1, 3)),
    )


def solution(mesh):
    def plan(*arrays):
        net, valid = arrays[0], arrays[5]
        if (net.shape[1:3], valid.shape[1:]) == ((ROWS, WIDE), (TALL, COLS)):
            return shards_wide(*arrays)
        return shards(*arrays)

    return jax.shard_map(
        plan,
        mesh=mesh,
        in_specs=(
            P(DP, SPACE, None, None),
            P(DP, SPACE, None, None),
            P(DP, SPACE, None, None),
            P(DP, None, SPACE, None),
            P(DP, None, None, SPACE),
            P(DP, None, SPACE),
            P(DP, None, SPACE, None),
            P(DP, None, SPACE, None),
            P(DP),
        ),
        out_specs=(
            P(DP, None, SPACE, None),
            P(DP, None, None, SPACE),
            P(DP, None, SPACE, None),
            P(DP),
            P(DP),
            P(DP, SPACE, None, None),
            P(DP, SPACE, None, None),
            P(DP, SPACE, None, None),
            P(DP, None, SPACE, None),
        ),
        check_vma=False,
    )
```

```python
import functools

import jax
import jax.numpy as jnp
from jax import lax
from jax.experimental import pallas as pl
from jax.experimental.pallas import tpu as pltpu
from jax.sharding import PartitionSpec as P

HID = 128
CTX = 128
MOT = 128
CORR = 324
SPACE = "space"
DP = "dp"
(
    CORR_IN,
    CORR_MIX,
    FLOW_IN,
    FLOW_MIX,
    MOTION_MIX,
    ROWS_GATES,
    ROWS_CANDIDATE,
    COLUMNS_GATES,
    COLUMNS_CANDIDATE,
    FLOW_HIDDEN,
    FLOW_OUT,
    MASK_HIDDEN,
    MASK_OUT,
) = range(13)
C1 = 256
C2 = 192
F1 = 128
F2 = 64
HEAD = 256
MASK = 576


def with_halo(block, sides, width):
    for axis, dim in sides:
        count = lax.axis_size(axis)
        forward = [(i, i + 1) for i in range(count - 1)]
        backward = [(target, source) for source, target in forward]
        low = lax.ppermute(
            lax.slice_in_dim(block, block.shape[dim] - width, None, axis=dim), axis, forward
        )
        high = lax.ppermute(lax.slice_in_dim(block, 0, width, axis=dim), axis, backward)
        block = jnp.concatenate([low, block, high], axis=dim)
    return block


def shapes():
    inputs_width = HID + CTX + MOT
    return [
        (CORR_IN, CORR, C1),
        (CORR_MIX, 9 * C1, C2),
        (FLOW_IN, 98, F1),
        (FLOW_MIX, 9 * F1, F2),
        (MOTION_MIX, 9 * (C2 + F2), MOT - 2),
        (ROWS_GATES, 5 * inputs_width, 2 * HID),
        (ROWS_CANDIDATE, 5 * inputs_width, HID),
        (COLUMNS_GATES, 5 * inputs_width, 2 * HID),
        (COLUMNS_CANDIDATE, 5 * inputs_width, HID),
        (FLOW_HIDDEN, 9 * HID, HEAD),
        (FLOW_OUT, 9 * HEAD, 2),
        (MASK_HIDDEN, 9 * HID, HEAD),
        (MASK_OUT, HEAD, MASK),
    ]


def unpack(flat):
    weights = {}
    biases = {}
    offset = 0
    table = shapes()
    for name, height, width in table:
        weights[name] = flat[offset // LANES : (offset + height * width) // LANES].reshape(height, width)
        offset = offset + height * width
    rest = flat[offset // LANES :].reshape(-1)
    offset = 0
    for name, height, width in table:
        biases[name] = rest[offset : offset + width].astype(jnp.float32)
        offset = offset + width
    return (weights, biases)


def pack(grads, total):
    table = shapes()
    rows = [grads[entry[0]][0].astype(jnp.bfloat16).reshape(-1, LANES) for entry in table]
    biases = jnp.concatenate([grads[entry[0]][1] for entry in table]).astype(jnp.bfloat16)
    left = total * LANES - sum(entry[1] * entry[2] for entry in table) - biases.shape[0]
    return jnp.concatenate(rows + [jnp.pad(biases, (0, left)).reshape(-1, LANES)])


def patches(padded, tall, wide):
    out_rows = padded.shape[1] - tall + 1
    out_columns = padded.shape[2] - wide + 1
    return jnp.concatenate(
        [
            padded[:, down : down + out_rows, across : across + out_columns]
            for down in range(tall)
            for across in range(wide)
        ],
        axis=-1,
    )


def apply(stacked, weight):
    return jnp.einsum("bhwk,ko->bhwo", stacked, weight, preferred_element_type=jnp.float32)


def apply_back(grad, weight):
    return jnp.einsum("bhwo,ko->bhwk", grad, weight, preferred_element_type=jnp.float32)


def weight_grad(stacked, pre_grad):
    return jnp.einsum("bhwk,bhwo->ko", stacked, pre_grad, preferred_element_type=jnp.float32)


def record(grads, name, stacked, pre_grad):
    grads[name] = (
        weight_grad(stacked, pre_grad),
        jnp.sum(pre_grad, axis=(0, 1, 2), dtype=jnp.float32),
    )


def flipped(weight, tall, wide):
    inner = weight.shape[0] // (tall * wide)
    shaped = weight.reshape(tall, wide, inner, weight.shape[1])[::-1, ::-1]
    return jnp.transpose(shaped, (0, 1, 3, 2)).reshape(-1, inner)


def slope(pre):
    sigma = jax.nn.sigmoid(pre)
    return sigma * (1.0 + pre * (1.0 - sigma))


def local_pad(field, tall, wide):
    return jnp.pad(field, ((0, 0), (tall // 2, tall // 2), (wide // 2, wide // 2), (0, 0)))


def row_pad(field, tall):
    field = with_halo(field, ((SPACE, 1),), tall // 2)
    return jnp.pad(field, ((0, 0), (0, 0), (tall // 2, tall // 2), (0, 0)))


def column_pad(field, tall, wide):
    field = with_halo(field, ((SPACE, 2),), wide // 2)
    return jnp.pad(field, ((0, 0), (tall // 2, tall // 2), (0, 0), (0, 0)))


MESH = pl.DeviceIdType.MESH
LANES = 128
BLOCK = 6144


def quarter_start(rank, count):
    return lax.div(rank * count, LANES)


def quarter_base(rank, count):
    return lax.div(rank * count, LANES * 16) * 16


def mate_of(rank):
    return rank + 1 - 2 * lax.rem(rank, 2)


def remote(src, dst, send, recv, device):
    return pltpu.make_async_remote_copy(
        src_ref=src, dst_ref=dst, send_sem=send, recv_sem=recv, device_id=device, device_id_type=MESH
    )


def greet(devices):
    barrier = pltpu.get_barrier_semaphore()
    for device in devices:
        pl.semaphore_signal(barrier, inc=1, device_id=device, device_id_type=MESH)
    pl.semaphore_wait(barrier, len(devices))


def lane_matrix(shift, forward):
    source = lax.broadcasted_iota(jnp.int32, (LANES, 2 * LANES), 0)
    target = lax.broadcasted_iota(jnp.int32, (LANES, 2 * LANES), 1)
    if forward:
        return jnp.where(target == source + shift, 1.0, 0.0).astype(jnp.bfloat16)
    return jnp.where(lax.rem(target + LANES, 2 * LANES) == source - shift + LANES, 1.0, 0.0).astype(jnp.bfloat16)


def gather_kernel(count, local_ref, out_ref, own_ref, send, recv):
    rank, spot = lax.axis_index(DP), lax.axis_index(SPACE)
    mate, across, twin = mate_of(rank), lax.rem(rank + 2, 4), mate_of(spot)
    pieces = 4
    rows = BLOCK // 2 // pieces
    peers = ({DP: mate}, {DP: across}, {SPACE: twin})
    greet(peers)
    matrix = lane_matrix(lax.rem(rank * count, LANES), True)
    first = lax.broadcasted_iota(jnp.int32, (256, LANES), 0) == 0

    def rotate(step, carry):
        at = pl.ds(pl.multiple_of(step * 256, 256), 256)
        both = jnp.dot(local_ref[at, :], matrix, preferred_element_type=jnp.float32)
        spill = pltpu.roll(both[:, LANES:], 1, 0)
        own_ref[at, :] = (both[:, :LANES] + jnp.where(first, carry, spill)).astype(jnp.bfloat16)
        return spill[0:1]

    lax.fori_loop(0, BLOCK // 256, rotate, jnp.zeros((1, LANES), jnp.float32))

    half, other_half = lax.rem(spot, 2), lax.rem(spot + 1, 2)

    def piece(which, index):
        return pl.ds(pl.multiple_of(which * (BLOCK // 2) + index * rows, 16), rows)

    own_x = [
        remote(own_ref.at[piece(half, k)], out_ref.at[rank, piece(half, k)], send.at[0, k], recv.at[0, k], peers[1])
        for k in range(pieces)
    ]
    own_c = remote(own_ref, out_ref.at[rank], send.at[4, 0], recv.at[4, 0], peers[0])
    for copy in own_x:
        copy.start()
    own_c.start()
    later = []
    for k in range(pieces):
        own_x[k].wait_recv()
        block = out_ref.at[across, piece(half, k)]
        to_twin = remote(block, block, send.at[1, k], recv.at[1, k], peers[2])
        to_mate = remote(block, block, send.at[2, k], recv.at[2, k], peers[0])
        to_twin.start()
        to_mate.start()
        later.append((to_twin, to_mate))
    for at in range(BLOCK // 256):
        out_ref[rank, at * 256 : (at + 1) * 256, :] = own_ref[at * 256 : (at + 1) * 256, :]
    for k in range(pieces):
        later[k][0].wait_recv()
        block = out_ref.at[across, piece(other_half, k)]
        to_mate = remote(block, block, send.at[3, k], recv.at[3, k], peers[0])
        to_mate.start()
        later.append((to_mate,))
    for k in range(pieces):
        own_x[k].wait_send()
        later[k][0].wait_send()
        later[k][1].wait()
        later[pieces + k][0].wait()
    own_c.wait()


def gather_blocks(params):
    count = params.shape[0]
    local = jnp.pad(params, (0, BLOCK * LANES - count)).reshape(BLOCK, LANES)
    return pl.pallas_call(
        functools.partial(gather_kernel, count),
        out_shape=jax.ShapeDtypeStruct((4, BLOCK, LANES), jnp.bfloat16),
        in_specs=[pl.BlockSpec(memory_space=pltpu.VMEM)],
        out_specs=pl.BlockSpec(memory_space=pltpu.VMEM),
        scratch_shapes=[
            pltpu.VMEM((BLOCK, LANES), jnp.bfloat16),
            pltpu.SemaphoreType.DMA((5, 4)),
            pltpu.SemaphoreType.DMA((5, 4)),
        ],
        compiler_params=pltpu.CompilerParams(
            collective_id=0, has_side_effects=True, vmem_limit_bytes=32 * 2**20
        ),
    )(local)


def gather_params(params):
    count = params.shape[0]
    blocks = gather_blocks(params)
    pieces = []
    reach = 0
    for rank in range(4):
        start = rank * count // LANES
        stop = -(-(rank + 1) * count // LANES)
        head = blocks[rank, :1] if rank == 0 else blocks[rank, :1] + pieces.pop()
        pieces += [head, blocks[rank, 1 : stop - start - 1], blocks[rank, stop - start - 1 : stop - start]]
    return jnp.concatenate(pieces)


def reduce_kernel(count, space, pieces, grads_ref, out_ref, rc, tx, rx, acc, ty, ry, tz, rz, gath, send, recv, zsend, zrecv):
    rank, spot = lax.axis_index(DP), lax.axis_index(SPACE)
    mate, across, twin = mate_of(rank), lax.rem(rank + 2, 4), mate_of(spot)
    group = space // 2
    side, depth = lax.rem(spot, 2), lax.div(spot, 2)
    rows = BLOCK // pieces
    half = rows // 2
    part = half // group

    def partner(step):
        return lax.rem(depth + step, group)

    peers = [{DP: mate}, {DP: across}, {SPACE: twin}]
    barrier = pltpu.get_barrier_semaphore()
    for device in peers:
        pl.semaphore_signal(barrier, inc=1, device_id=device, device_id_type=MESH)

    def hello(step, carry):
        pl.semaphore_signal(barrier, inc=1, device_id={SPACE: partner(step) * 2 + side}, device_id_type=MESH)
        return carry

    lax.fori_loop(1, group, hello, 0)
    pl.semaphore_wait(barrier, 3 + group - 1)

    gath[BLOCK:, :] = jnp.zeros((32, LANES), jnp.bfloat16)
    lower = lax.rem(rank, 2)
    upper = lax.div(rank, 2)

    def base(who):
        return pl.multiple_of(quarter_base(who, count), 16)

    def rows_of(start, index, length):
        return pl.ds(pl.multiple_of(start + index, 16), length)

    core = []
    for p in range(pieces):
        for high in range(2):
            copy = remote(
                grads_ref.at[rows_of(base(2 * high + 1 - lower), p * rows, rows)],
                rc.at[p, high],
                send.at[high, p],
                recv.at[high, p],
                peers[0],
            )
            copy.start()
            core.append(copy)
    step_rows = 192 if half % 192 == 0 else 16
    xs, ys, gs = [], [], []

    def z_copy(p, step):
        to = partner(step)
        return remote(
            tz.at[p, pl.ds(pl.multiple_of(to * part, 16), part)],
            rz.at[p, pl.ds(pl.multiple_of(depth * part, 16), part)],
            zsend.at[0, p, step],
            zrecv.at[0, p, step],
            {SPACE: to * 2 + side},
        )

    def home(p, which, slot):
        return pl.ds(pl.multiple_of(p * rows + which * half + slot * part, 16), part)

    def g_copy(p, step):
        block = gath.at[home(p, side, depth)]
        return remote(block, block, zsend.at[1, p, step], zrecv.at[1, p, step], {SPACE: partner(step) * 2 + side})

    def each(body):
        def run(step, carry):
            body(step)
            return carry

        lax.fori_loop(1, group, run, 0)

    def stage_core(p):
        core[2 * p].wait_recv()
        core[2 * p + 1].wait_recv()
        far = 1 - upper

        def add(step, carry):
            at = pl.multiple_of(step * step_rows, 16)
            mine = grads_ref[rows_of(base(2 * far + lower), p * rows + at, step_rows), :].astype(jnp.float32)
            tx[p, pl.ds(at, step_rows), :] = (
                mine + rc[p, far, pl.ds(at, step_rows), :].astype(jnp.float32)
            ).astype(jnp.bfloat16)
            return carry

        lax.fori_loop(0, rows // step_rows, add, 0)
        copy = remote(tx.at[p], rx.at[p], send.at[2, p], recv.at[2, p], peers[1])
        copy.start()
        xs.append(copy)

    def stage_x(p):
        xs[p].wait_recv()

        def total(at):
            return (
                grads_ref[rows_of(base(rank), p * rows + at, step_rows), :].astype(jnp.float32)
                + rc[p, upper, pl.ds(at, step_rows), :].astype(jnp.float32)
                + rx[p, pl.ds(at, step_rows), :].astype(jnp.float32)
            )

        def add(step, carry):
            at = pl.multiple_of(step * step_rows, 16)
            far = pl.multiple_of((1 - side) * half + at, 16)
            near = pl.multiple_of(side * half + at, 16)
            ty[p, pl.ds(at, step_rows), :] = total(far).astype(jnp.bfloat16)
            acc[p, pl.ds(at, step_rows), :] = total(near)
            return carry

        lax.fori_loop(0, half // step_rows, add, 0)
        copy = remote(ty.at[p], ry.at[p], send.at[3, p], recv.at[3, p], peers[2])
        copy.start()
        ys.append(copy)

    def stage_y(p):
        ys[p].wait_recv()

        def add(step, carry):
            at = pl.ds(pl.multiple_of(step * step_rows, 16), step_rows)
            value = acc[p, at, :] + ry[p, at, :].astype(jnp.float32)
            acc[p, at, :] = value
            tz[p, at, :] = value.astype(jnp.bfloat16)
            return carry

        lax.fori_loop(0, half // step_rows, add, 0)
        each(lambda step: z_copy(p, step).start())

    def stage_z(p):
        each(lambda step: z_copy(p, step).wait_recv())
        value = acc[p, pl.ds(pl.multiple_of(depth * part, 16), part), :]

        def add(step, value):
            other = lax.rem(depth + group - step, group)
            return value + rz[p, pl.ds(pl.multiple_of(other * part, 16), part), :].astype(jnp.float32)

        value = lax.fori_loop(1, group, add, value)
        gath[home(p, side, depth), :] = value.astype(jnp.bfloat16)
        each(lambda step: g_copy(p, step).start())

    def stage_zg(p):
        each(lambda step: g_copy(p, step).wait_recv())
        block = gath.at[pl.ds(pl.multiple_of(p * rows + side * half, 16), half)]
        copy = remote(block, block, send.at[4, p], recv.at[4, p], peers[2])
        copy.start()
        gs.append(copy)

    def stage_yg(p):
        gs[p].wait_recv()

    stages = [stage_core, stage_x, stage_y, stage_z, stage_zg, stage_yg]
    for tick in range(pieces + len(stages) - 1):
        for number in reversed(range(len(stages))):
            if 0 <= tick - number < pieces:
                stages[number](tick - number)

    for copy in core + xs + ys + gs:
        copy.wait_send()
    for p in range(pieces):

        def done(step):
            z_copy(p, step).wait_send()
            g_copy(p, step).wait_send()

        each(done)

    offset = rank * count - quarter_base(rank, count) * LANES
    skip = lax.div(offset, LANES)
    matrix = lane_matrix(lax.rem(offset, LANES), False)
    wide = jnp.where(
        lax.broadcasted_iota(jnp.int32, (256, 288), 1)
        == lax.broadcasted_iota(jnp.int32, (256, 288), 0) + skip,
        1.0,
        0.0,
    ).astype(jnp.bfloat16)
    wide_next = jnp.where(
        lax.broadcasted_iota(jnp.int32, (256, 288), 1)
        == lax.broadcasted_iota(jnp.int32, (256, 288), 0) + skip + 1,
        1.0,
        0.0,
    ).astype(jnp.bfloat16)

    def place(step, carry):
        at = pl.multiple_of(step * 256, 256)
        block = gath[pl.ds(at, 288), :]
        both = jnp.dot(block, matrix, preferred_element_type=jnp.float32).astype(jnp.bfloat16)
        out_ref[pl.ds(at, 256), :] = jnp.dot(wide, both[:, :LANES], preferred_element_type=jnp.float32) + jnp.dot(
            wide_next, both[:, LANES:], preferred_element_type=jnp.float32
        )
        return carry

    lax.fori_loop(0, BLOCK // 256, place, 0)


def reduce_grads(flat, space, count):
    pieces = next(k for k in (4, 2, 1) if BLOCK // (k * space) % 16 == 0)
    rows = BLOCK // pieces
    half = rows // 2
    out = pl.pallas_call(
        functools.partial(reduce_kernel, count, space, pieces),
        out_shape=jax.ShapeDtypeStruct((BLOCK, LANES), jnp.float32),
        in_specs=[pl.BlockSpec(memory_space=pltpu.VMEM)],
        out_specs=pl.BlockSpec(memory_space=pltpu.VMEM),
        scratch_shapes=[
            pltpu.VMEM((pieces, 2, rows, LANES), jnp.bfloat16),
            pltpu.VMEM((pieces, rows, LANES), jnp.bfloat16),
            pltpu.VMEM((pieces, rows, LANES), jnp.bfloat16),
            pltpu.VMEM((pieces, half, LANES), jnp.float32),
            pltpu.VMEM((pieces, half, LANES), jnp.bfloat16),
            pltpu.VMEM((pieces, half, LANES), jnp.bfloat16),
            pltpu.VMEM((pieces, half, LANES), jnp.bfloat16),
            pltpu.VMEM((pieces, half, LANES), jnp.bfloat16),
            pltpu.VMEM((BLOCK + 32, LANES), jnp.bfloat16),
            pltpu.SemaphoreType.DMA((5, pieces)),
            pltpu.SemaphoreType.DMA((5, pieces)),
            pltpu.SemaphoreType.DMA((2, pieces, space // 2)),
            pltpu.SemaphoreType.DMA((2, pieces, space // 2)),
        ],
        compiler_params=pltpu.CompilerParams(
            collective_id=1, has_side_effects=True, vmem_limit_bytes=48 * 2**20
        ),
    )(flat)
    return out.reshape(-1)[:count]


def gru_forward(state, inputs, weights, biases, gate_name, candidate_name, tall, wide, padder):
    joined_stack = patches(padder(jnp.concatenate([state, inputs], -1), tall, wide), tall, wide)
    gates = jax.nn.sigmoid(apply(joined_stack, weights[gate_name]) + biases[gate_name])
    hidden = state.shape[-1]
    update = gates[..., :hidden]
    reset = gates[..., hidden:]
    state_wide = state.astype(jnp.float32)
    mixed = jnp.concatenate([(reset * state_wide).astype(jnp.bfloat16), inputs], -1)
    mixed_stack = patches(padder(mixed, tall, wide), tall, wide)
    candidate = jnp.tanh(apply(mixed_stack, weights[candidate_name]) + biases[candidate_name])
    result = state_wide + update * (candidate - state_wide)
    return (result, (joined_stack, mixed_stack, update, reset, candidate, state_wide))


def gru_backward(result_grad, kept, weights, grads, gate_name, candidate_name, tall, wide, padder):
    joined_stack, mixed_stack, update, reset, candidate, state_wide = kept
    hidden = update.shape[-1]
    candidate_grad = (result_grad * update * (1.0 - candidate * candidate)).astype(jnp.bfloat16)
    record(grads, candidate_name, mixed_stack, candidate_grad)
    mixed_grad = apply(
        patches(padder(candidate_grad, tall, wide), tall, wide),
        flipped(weights[candidate_name], tall, wide),
    )
    reset_grad = mixed_grad[..., :hidden]
    gate_grad = jnp.concatenate(
        [
            result_grad * (candidate - state_wide) * update * (1.0 - update),
            reset_grad * state_wide * reset * (1.0 - reset),
        ],
        -1,
    ).astype(jnp.bfloat16)
    record(grads, gate_name, joined_stack, gate_grad)
    joined_grad = apply(
        patches(padder(gate_grad, tall, wide), tall, wide), flipped(weights[gate_name], tall, wide)
    )
    state_grad = result_grad * (1.0 - update) + reset_grad * reset + joined_grad[..., :hidden]
    inputs_grad = joined_grad[..., hidden:] + mixed_grad[..., hidden:]
    return (state_grad, inputs_grad)


def shards(net, context, corr, flow, target, valid, grad_net, grad_mask, params):
    flow_start = CTX + MOT - 2
    plane = jnp.float32(target.shape[2] * net.shape[2])
    counts = lax.psum(jnp.sum(valid, axis=(1, 2)).astype(jnp.float32), SPACE)
    divisor = jnp.maximum(counts, 1.0)
    weights, biases = unpack(gather_params(params))
    grads = {}
    flow_rows = jnp.transpose(flow, (0, 2, 3, 1))
    corr_pre = apply(corr, weights[CORR_IN]) + biases[CORR_IN]
    corr_one = jax.nn.silu(corr_pre).astype(jnp.bfloat16)
    corr_stack = patches(row_pad(corr_one, 3), 3, 3)
    corr_mix_pre = apply(corr_stack, weights[CORR_MIX]) + biases[CORR_MIX]
    corr_two = jax.nn.silu(corr_mix_pre).astype(jnp.bfloat16)
    flow_stack = patches(row_pad(flow_rows, 7), 7, 7)
    flow_pre = apply(flow_stack, weights[FLOW_IN]) + biases[FLOW_IN]
    flow_one = jax.nn.silu(flow_pre).astype(jnp.bfloat16)
    flow_mix_stack = patches(row_pad(flow_one, 3), 3, 3)
    flow_mix_pre = apply(flow_mix_stack, weights[FLOW_MIX]) + biases[FLOW_MIX]
    flow_two = jax.nn.silu(flow_mix_pre).astype(jnp.bfloat16)
    joint_stack = patches(row_pad(jnp.concatenate([corr_two, flow_two], -1), 3), 3, 3)
    motion_pre = apply(joint_stack, weights[MOTION_MIX]) + biases[MOTION_MIX]
    motion = jax.nn.silu(motion_pre).astype(jnp.bfloat16)
    inputs = jnp.concatenate([context, motion, flow_rows], -1)
    state, rows_kept = gru_forward(
        net, inputs, weights, biases, ROWS_GATES, ROWS_CANDIDATE, 1, 5, local_pad
    )
    state_columns, inputs_columns = (
        lax.all_to_all(
            state.astype(jnp.bfloat16), SPACE, split_axis=2, concat_axis=1, tiled=True
        ),
        lax.all_to_all(inputs, SPACE, split_axis=2, concat_axis=1, tiled=True),
    )
    target_here = jnp.transpose(target, (0, 2, 3, 1))
    valid_here = valid.astype(jnp.float32)
    net_cotangent = grad_net
    mask_cotangent = grad_mask
    final, columns_kept = gru_forward(
        state_columns,
        inputs_columns,
        weights,
        biases,
        COLUMNS_GATES,
        COLUMNS_CANDIDATE,
        5,
        1,
        local_pad,
    )
    final_low = final.astype(jnp.bfloat16)
    heads_weight = jnp.concatenate([weights[FLOW_HIDDEN], weights[MASK_HIDDEN]], 1)
    heads_bias = jnp.concatenate([biases[FLOW_HIDDEN], biases[MASK_HIDDEN]])
    net_stack = patches(column_pad(final_low, 3, 3), 3, 3)
    heads_pre = apply(net_stack, heads_weight) + heads_bias
    heads_act = jax.nn.silu(heads_pre).astype(jnp.bfloat16)
    flow_features = heads_act[..., :HEAD]
    mask_features = heads_act[..., HEAD:]
    hidden_stack = patches(column_pad(flow_features, 3, 3), 3, 3)
    delta = apply(hidden_stack, weights[FLOW_OUT]) + biases[FLOW_OUT]
    mask_full = 0.25 * (apply(mask_features, weights[MASK_OUT]) + biases[MASK_OUT])
    new_flow = inputs_columns[..., flow_start:].astype(jnp.float32) + delta
    error = new_flow - target_here
    root = jnp.sqrt(error * error + 1.0)
    partials = jnp.sum(valid_here * jnp.sum(root, axis=-1), axis=(1, 2))
    flow_grad = plane / divisor[:, None, None, None] * valid_here[..., None] * error / root
    mask_low = mask_full.astype(jnp.bfloat16)
    nets_out = final_low
    flows_out = jnp.transpose(new_flow, (0, 3, 1, 2))
    masks_out = mask_low
    delta_grad = flow_grad.astype(jnp.bfloat16)
    mask_grad = (0.25 * mask_cotangent.astype(jnp.float32)).astype(jnp.bfloat16)
    record(grads, MASK_OUT, mask_features, mask_grad)
    record(grads, FLOW_OUT, hidden_stack, delta_grad)
    from_flow = apply(
        patches(column_pad(delta_grad, 3, 3), 3, 3), flipped(weights[FLOW_OUT], 3, 3)
    )
    from_mask = apply_back(mask_grad, weights[MASK_OUT])
    heads_grad = (jnp.concatenate([from_flow, from_mask], -1) * slope(heads_pre)).astype(
        jnp.bfloat16
    )
    heads_wgrad = weight_grad(net_stack, heads_grad)
    heads_bgrad = jnp.sum(heads_grad, axis=(0, 1, 2), dtype=jnp.float32)
    grads[FLOW_HIDDEN] = (heads_wgrad[:, :HEAD], heads_bgrad[:HEAD])
    grads[MASK_HIDDEN] = (heads_wgrad[:, HEAD:], heads_bgrad[HEAD:])
    final_grad = net_cotangent.astype(jnp.float32) + apply(
        patches(column_pad(heads_grad, 3, 3), 3, 3), flipped(heads_weight, 3, 3)
    )
    state_grad_columns, inputs_grad_columns = gru_backward(
        final_grad,
        columns_kept,
        weights,
        grads,
        COLUMNS_GATES,
        COLUMNS_CANDIDATE,
        5,
        1,
        local_pad,
    )
    inputs_grad_columns = jnp.concatenate(
        [
            inputs_grad_columns[..., :flow_start],
            inputs_grad_columns[..., flow_start:] + flow_grad,
        ],
        -1,
    )
    state_back, inputs_back = (
        lax.all_to_all(
            state_grad_columns.astype(jnp.bfloat16),
            SPACE,
            split_axis=1,
            concat_axis=2,
            tiled=True,
        ),
        lax.all_to_all(
            inputs_grad_columns.astype(jnp.bfloat16),
            SPACE,
            split_axis=1,
            concat_axis=2,
            tiled=True,
        ),
    )
    net_grad, inputs_grad = gru_backward(
        state_back.astype(jnp.float32),
        rows_kept,
        weights,
        grads,
        ROWS_GATES,
        ROWS_CANDIDATE,
        1,
        5,
        local_pad,
    )
    inputs_total = inputs_grad + inputs_back.astype(jnp.float32)
    motion_grad = (inputs_total[..., CTX:flow_start] * slope(motion_pre)).astype(jnp.bfloat16)
    record(grads, MOTION_MIX, joint_stack, motion_grad)
    joint_grad = apply(
        patches(row_pad(motion_grad, 3), 3, 3), flipped(weights[MOTION_MIX], 3, 3)
    )
    branch_grad = jnp.concatenate(
        [
            joint_grad[..., :C2] * slope(corr_mix_pre),
            joint_grad[..., C2:] * slope(flow_mix_pre),
        ],
        -1,
    ).astype(jnp.bfloat16)
    record(grads, CORR_MIX, corr_stack, branch_grad[..., :C2])
    record(grads, FLOW_MIX, flow_mix_stack, branch_grad[..., C2:])
    branch_pad = row_pad(branch_grad, 3)
    corr_one_grad = apply(
        patches(branch_pad[..., :C2], 3, 3), flipped(weights[CORR_MIX], 3, 3)
    )
    flow_one_grad = apply(
        patches(branch_pad[..., C2:], 3, 3), flipped(weights[FLOW_MIX], 3, 3)
    )
    corr_pre_grad = (corr_one_grad * slope(corr_pre)).astype(jnp.bfloat16)
    flow_pre_grad = (flow_one_grad * slope(flow_pre)).astype(jnp.bfloat16)
    record(grads, CORR_IN, corr, corr_pre_grad)
    record(grads, FLOW_IN, flow_stack, flow_pre_grad)
    corr_grads = apply_back(corr_pre_grad, weights[CORR_IN])
    flow_total = inputs_total[..., flow_start:] + apply(
        patches(row_pad(flow_pre_grad, 7), 7, 7), flipped(weights[FLOW_IN], 7, 7)
    )
    flow_grads = jnp.transpose(flow_total, (0, 3, 1, 2))
    net_grads = net_grad
    context_grads = inputs_total[..., :CTX]
    count = params.shape[0]
    local = pack(grads, 3 * count // (LANES * 16) * 16 + BLOCK)
    collected = reduce_grads(local, lax.axis_size(SPACE), count)
    losses = lax.psum(partials, SPACE) / divisor
    return (
        nets_out,
        flows_out,
        masks_out,
        losses,
        collected,
        net_grads,
        context_grads,
        corr_grads,
        flow_grads,
    )


BATCH = 2
ROWS = 5
WIDE = 128
TALL = 40
COLS = 16
AREA = 640
PITCH = 20
SPREAD = TALL * PITCH
SPAN = 896
EDGE = 64


def mm(a, b):
    return jnp.dot(a, b, preferred_element_type=jnp.float32)


def nt(a, b):
    return lax.dot_general(a, b, (((1,), (1,)), ((), ())), preferred_element_type=jnp.float32)


def tn(a, b):
    return lax.dot_general(a, b, (((0,), (0,)), ((), ())), preferred_element_type=jnp.float32)


def half_of(value):
    return value.astype(jnp.bfloat16)


def full_of(value):
    return value.astype(jnp.float32)


def join(parts, axis=1):
    return jnp.concatenate(list(parts), axis=axis)


def quarter_of(value):
    return half_of(0.25 * full_of(value))


def lane_index(shape):
    return lax.broadcasted_iota(jnp.int32, shape, 1)


def row_index(shape):
    return lax.broadcasted_iota(jnp.int32, shape, 0)


def act_slope(pre):
    sigma = jax.nn.sigmoid(pre)
    act = pre * sigma
    return act, sigma + act * (1.0 - sigma)


def flat_rows():
    table = shapes()
    offset = 0
    starts = {}
    for name, height, width in table:
        starts[name] = offset // LANES
        offset += height * width
    bias_row = offset // LANES
    spots = {}
    inner = 0
    for name, height, width in table:
        spots[name] = inner
        inner += width
    return starts, bias_row, spots, inner


def cast_rows(dst, to, src, start, count, kind):
    big = 256
    whole = count // big

    if whole > 1:

        def body(step, carry):
            at = pl.multiple_of(step * big, big)
            dst[pl.ds(to + at, big), :] = src[pl.ds(start + at, big), :].astype(kind)
            return carry

        lax.fori_loop(0, whole, body, 0)
    elif whole == 1:
        dst[to : to + big, :] = src[start : start + big, :].astype(kind)
    rest = count - whole * big
    if rest:
        low = whole * big
        dst[to + low : to + count, :] = src[start + low : start + count, :].astype(kind)


MARGIN = 16


def stage_plan(count, start, rows):
    stop = start + rows
    pieces, fill = [], 0
    for rank in range(4):
        first = rank * count // LANES
        last = -(-(rank + 1) * count // LANES)
        low, high = max(start, first), min(stop, last)
        if low >= high:
            continue
        place = low - first + rank * BLOCK
        base = place // 16 * 16
        length = -(-(place - base + high - low) // 16) * 16
        to = MARGIN + low - start - (place - base)
        seam = MARGIN + low - start if start < first else None
        pieces.append((base, length, fill, to, seam))
        fill += length
    return pieces


class Stages:
    def __init__(self, v, count, segments):
        self.v, self.at = v, 0
        self.plans = [stage_plan(count, start, rows) for start, rows in segments]
        self.fetch(0)

    def copies(self, index):
        v, slot = self.v, index % 2
        return [
            pltpu.make_async_copy(
                v.out_all.at[base : base + length], v.stage.at[slot, fill : fill + length], v.ssem.at[slot, number]
            )
            for number, (base, length, fill, to, seam) in enumerate(self.plans[index])
        ]

    def fetch(self, index):
        if index < len(self.plans):
            for copy in self.copies(index):
                copy.start()

    def take(self):
        v, index = self.v, self.at
        self.at += 1
        for copy in self.copies(index):
            copy.wait()
        self.fetch(index + 1)
        for base, length, fill, to, seam in self.plans[index]:
            saved = None if seam is None else v.flat[seam : seam + 1, :]
            cast_rows(v.flat, to, v.stage.at[index % 2], fill, length, jnp.float32)
            if seam is not None:
                v.flat[seam : seam + 1, :] = v.flat[seam : seam + 1, :] + saved


def strided(ref, start, count, stride):
    if stride == 1:
        return ref[pl.ds(start, count), :]
    return ref[pl.ds(start, count, stride=stride), :]


def unpack_pairs(flat, row, count, dst, to, lane):
    dst[to : to + count, lane : lane + LANES] = half_of(strided(flat, MARGIN + 2 * row, count, 2))
    dst[to : to + count, lane + LANES : lane + 2 * LANES] = half_of(strided(flat, MARGIN + 2 * row + 1, count, 2))


def pack_pairs(flat, row, count, low, high):
    flat[pl.ds(MARGIN + 2 * row, count, stride=2), :] = low
    flat[pl.ds(MARGIN + 2 * row + 1, count, stride=2), :] = high


def split_pick(which, quarter):
    source = lax.broadcasted_iota(jnp.int32, (LANES, HEAD), 0)
    target = lax.broadcasted_iota(jnp.int32, (LANES, HEAD), 1)
    return jnp.where(source == 2 * (target - 64 * quarter) + which, 1.0, 0.0).astype(jnp.bfloat16)


UNPACK = (
    (CORR_IN, 648), (CORR_MIX, 3456), (FLOW_IN, 98), (FLOW_MIX, 576), (MOTION_MIX, 2268),
    (ROWS_GATES, 3840), (ROWS_CANDIDATE, 1920), (None, 21), (COLUMNS_GATES, 3840), (COLUMNS_CANDIDATE, 1920),
    (FLOW_HIDDEN, 2304), (MASK_HIDDEN, 2304), (FLOW_OUT, 36), (MASK_OUT, 1152),
)


def stage_of(v, name, rows):
    assert UNPACK[v.stages.at] == (name, rows)
    v.stages.take()


def unpack_gru(v, gates_name, cand_name, w_i, w_s):
    flat = v.flat
    stage_of(v, gates_name, 3840)
    for tap in range(5):
        unpack_pairs(flat, tap * 384, 128, w_s, tap * 128, 0)
        unpack_pairs(flat, tap * 384 + 128, 256, w_i, tap * 256, 0)
    stage_of(v, cand_name, 1920)
    for tap in range(5):
        w_s[tap * 128 : (tap + 1) * 128, 256:384] = half_of(strided(flat, MARGIN + tap * 384, 128, 1))
        w_i[tap * 256 : (tap + 1) * 256, 256:384] = half_of(strided(flat, MARGIN + tap * 384 + 128, 256, 1))


def unpack_encoder(v, count):
    starts, bias_row, spots, inner = flat_rows()
    flat = v.flat
    v.stages = Stages(v, count, [(bias_row if name is None else starts[name], rows) for name, rows in UNPACK])

    def stage(name, rows):
        stage_of(v, name, rows)

    stage(CORR_IN, 648)
    unpack_pairs(flat, 0, 324, v.w_ci, 0, 0)

    stage(CORR_MIX, 3456)
    lane = lane_index((128, LANES))
    low_half = lane < 64

    def mix_step(step, carry):
        at = MARGIN + 384 * step
        r0, r1, r2 = (strided(flat, at + i, 128, 3) for i in range(3))
        r1s, r2s = pltpu.roll(r1, 64, 1), pltpu.roll(r2, 64, 1)
        v.pair_a[pl.ds(0, 128, stride=2), :] = r0
        v.pair_a[pl.ds(1, 128, stride=2), :] = jnp.where(low_half, r1s, r2s)
        v.pair_b[pl.ds(0, 128, stride=2), :] = jnp.where(low_half, r1, 0.0)
        v.pair_b[pl.ds(1, 128, stride=2), :] = jnp.where(low_half, r2s, 0.0)
        to = pl.ds(pl.multiple_of(step * 256, 256), 256)
        v.w_cm[to, 0:128] = half_of(v.pair_a[...])
        v.w_cm[to, 128:256] = half_of(v.pair_b[...])
        return carry

    lax.fori_loop(0, 9, mix_step, 0)

    stage(FLOW_IN, 98)
    v.flow_tmp[...] = jnp.zeros_like(v.flow_tmp)
    for across in range(7):
        for comp in range(2):
            v.flow_tmp[pl.ds(across * 16 + comp, 7, stride=2), :] = strided(
                flat, MARGIN + across * 2 + comp, 7, 14
            )
    v.w_fi[...] = half_of(v.flow_tmp[...])

    stage(FLOW_MIX, 576)
    for step in range(9):
        r0 = strided(flat, MARGIN + 64 * step, 64, 1)
        high_half = lane_index((64, LANES)) >= 64
        v.pair_a[pl.ds(0, 64, stride=2), :] = jnp.where(high_half, pltpu.roll(r0, 64, 1), 0.0)
        v.pair_a[pl.ds(1, 64, stride=2), :] = jnp.where(high_half, r0, 0.0)
        v.w_fm[step * 128 : (step + 1) * 128, :] = half_of(v.pair_a[0:128, :])

    stage(MOTION_MIX, 2268)
    lane36 = lane_index((36, LANES))
    for i in range(64):
        if i == 0:
            value = strided(flat, MARGIN, 36, 63)
        elif i == 63:
            value = pltpu.roll(strided(flat, MARGIN + 62, 36, 63), 126, 1)
        else:
            low = pltpu.roll(strided(flat, MARGIN + i - 1, 36, 63), 2 * i, 1)
            high = pltpu.roll(strided(flat, MARGIN + i, 36, 63), 2 * i, 1)
            value = jnp.where(lane36 < 2 * i, low, high)
        v.mm_tmp[pl.ds(i, 36, stride=64), :] = jnp.where(lane36 < 126, value, 0.0)
    for step in range(9):
        v.w_mm[step * 256 : (step + 1) * 256, :] = half_of(v.mm_tmp[step * 256 : (step + 1) * 256, :])

    unpack_gru(v, ROWS_GATES, ROWS_CANDIDATE, v.w_ri, v.w_rs)

    stage(None, 21)
    place = 0
    lane1 = lane_index((1, LANES))
    for name, height, width in shapes():
        spot = spots[name]
        for block in range(-(-width // LANES)):
            at = spot + block * LANES
            row, shift = at // LANES, at % LANES
            value = flat[MARGIN + row : MARGIN + row + 1, :]
            if shift:
                after = flat[MARGIN + row + 1 : MARGIN + row + 2, :]
                value = jnp.where(
                    lane1 < LANES - shift, pltpu.roll(value, LANES - shift, 1), pltpu.roll(after, LANES - shift, 1)
                )
            left = width - block * LANES
            if left < LANES:
                value = jnp.where(lane1 < left, value, 0.0)
            if name == FLOW_MIX:
                value = pltpu.roll(value, 64, 1)
            v.bias[place : place + 1, :] = value
            place += 1


def unpack_heads(v):
    flat = v.flat
    low_half = lane_index((128, LANES)) < 64

    def stage(name, rows):
        stage_of(v, name, rows)

    unpack_gru(v, COLUMNS_GATES, COLUMNS_CANDIDATE, v.w_li, v.w_ls)

    for name, lane0 in ((FLOW_HIDDEN, 0), (MASK_HIDDEN, 256)):
        stage(name, 2304)
        for tap in range(9):
            unpack_pairs(flat, tap * 128, 128, v.w_h, tap * 128, lane0)

    stage(FLOW_OUT, 36)
    v.fo_tmp[...] = jnp.zeros_like(v.fo_tmp)
    for which in range(2):
        total = jnp.zeros((9, HEAD), jnp.float32)
        for quarter in range(4):
            total = total + mm(half_of(strided(flat, MARGIN + quarter, 9, 4)), split_pick(which, quarter))
        v.fo_tmp[pl.ds(which, 9, stride=2), 0:128] = total[:, :128]
        v.fo_tmp2[pl.ds(which, 9, stride=2), 0:128] = total[:, 128:]
    v.fo_tmp2[18:32, :] = jnp.zeros((14, LANES), jnp.float32)
    v.w_fo[:, 0:128] = half_of(v.fo_tmp[...])
    v.w_fo[:, 128:256] = half_of(v.fo_tmp2[...])

    stage(MASK_OUT, 1152)
    r = [strided(flat, MARGIN + i, 128, 9) for i in range(9)]
    rs = [pltpu.roll(r[i], 64, 1) for i in range(4, 9)]
    for block in range(5):
        even = r[block] if block < 4 else jnp.where(low_half, r[4], 0.0)
        odd = jnp.where(low_half, rs[block], rs[block + 1]) if block < 4 else jnp.where(low_half, rs[4], 0.0)
        v.pair_a[pl.ds(0, 128, stride=2), :] = even
        v.pair_a[pl.ds(1, 128, stride=2), :] = odd
        v.w_mo[:, block * 128 : (block + 1) * 128] = half_of(v.pair_a[...])


BIAS_AT = {}
_place = 0
for _name, _height, _width in shapes():
    BIAS_AT[_name] = _place
    _place += -(-_width // 128)
BIAS_ROWS = 32


def bias_of(v, name, blocks):
    at = BIAS_AT[name]
    return jnp.concatenate([v.bias[at + i : at + i + 1, :] for i in range(blocks)], axis=1)


class Halo:
    def __init__(self, v, sem, up_src, down_src, from_down, from_up):
        up = {SPACE: jnp.maximum(v.spot - 1, 0)}
        down = {SPACE: jnp.minimum(v.spot + 1, v.space - 1)}
        self.v = v
        self.up = remote(up_src, from_down, v.hsend.at[sem, 0], v.hrecv.at[sem, 0], up)
        self.down = remote(down_src, from_up, v.hsend.at[sem, 1], v.hrecv.at[sem, 1], down)

    def start(self):
        pl.when(self.v.spot > 0)(self.up.start)
        pl.when(self.v.spot < self.v.space - 1)(self.down.start)

    def receive(self):
        pl.when(self.v.spot < self.v.space - 1)(self.up.wait_recv)
        pl.when(self.v.spot > 0)(self.down.wait_recv)

    def sent(self):
        pl.when(self.v.spot > 0)(self.up.wait_send)
        pl.when(self.v.spot < self.v.space - 1)(self.down.wait_send)


def drain_bytes(ref, sem):
    pltpu.make_async_copy(ref, ref, sem).wait()


class Swap:
    def __init__(self, v, sem, src, dst, broadcast=False):
        self.v, self.sem, self.src, self.dst, self.broadcast = v, sem, src, dst, broadcast

    def copy(self, step):
        v = self.v
        to = lax.rem(v.spot + step, v.space)
        src = self.src if self.broadcast else self.src.at[to]
        return remote(src, self.dst.at[v.spot], v.asend.at[self.sem], v.arecv.at[self.sem], {SPACE: to})

    def each(self, what):
        def body(step, carry):
            what(self.copy(step))
            return carry

        lax.fori_loop(1, self.v.space, body, 0)

    def start(self):
        self.each(lambda copy: copy.start())

    def receive(self):
        drain_bytes(self.dst.at[0 : self.v.space - 1], self.v.arecv.at[self.sem])

    def sent(self):
        drain_bytes(self.dst.at[0 : self.v.space - 1], self.v.asend.at[self.sem])


def spread_rows(v, b, acts, rows, dst, row0, width, backward=False):
    x = lax.rem(row_index((rows, LANES)), WIDE)
    for block, act in enumerate(acts):
        v.tmp[8 : 8 + rows, :] = act
        for tap in range(3):
            d = (1 - tap) if backward else (tap - 1)
            value = act if d == 0 else v.tmp[8 + d : 8 + d + rows, :]
            if d == -1:
                value = jnp.where(x > 0, value, 0.0)
            if d == 1:
                value = jnp.where(x < WIDE - 1, value, 0.0)
            lane = tap * width + block * LANES
            if backward:
                dst[row0 : row0 + rows, b + lane : b + lane + LANES] = half_of(value)
            else:
                dst[b, row0 : row0 + rows, lane : lane + LANES] = half_of(value)


def spread_five(v, value, dst, lane_of, backward=False):
    x = lax.rem(row_index((AREA, LANES)), WIDE)
    v.tmp[8 : 8 + AREA, :] = value
    for tap in range(5):
        d = (2 - tap) if backward else (tap - 2)
        moved = value if d == 0 else v.tmp[8 + d : 8 + d + AREA, :]
        if d:
            moved = jnp.where((x + d >= 0) & (x + d < WIDE), moved, 0.0)
        if backward:
            taps_part(v, tap, lane_of, lane_of + LANES)[...] = half_of(moved)
        else:
            lane = lane_of(tap)
            dst[:, lane : lane + LANES] = half_of(moved)


def lines_of(ref, b, lines):
    return jnp.concatenate([ref[b, y] for y in range(lines)], axis=1)


def edge_rows(v, value, rows):
    low = jnp.where(v.spot > 0, value[0:rows], 0.0)
    high = jnp.where(v.spot < v.space - 1, value[-rows:], 0.0)
    return jnp.concatenate([low, value[rows:-rows], high], axis=0)


def early_taps(v):
    def flow(b, carry):
        up = jnp.where(v.spot > 0, v.flow_up[b], 0.0)
        down = jnp.where(v.spot < v.space - 1, v.flow_down[b], 0.0)
        lane = lane_index((16, LANES))
        v.fs[...] = jnp.zeros_like(v.fs)
        for across in range(7):
            d = across - 3
            for part, value in enumerate((up, v.flow[b], down)):
                moved = value
                if d:
                    moved = pltpu.roll(value, (-d) % LANES, 1)
                    moved = jnp.where((lane + d >= 0) & (lane + d < WIDE), moved, 0.0)
                v.fs[across, part * 10 : part * 10 + 10, :] = moved[0:10, :]
        for y in range(9):
            for across in range(7):
                v.flow_tmp[across * 16 : across * 16 + 16, :] = v.fs[across, 2 * y : 2 * y + 16, :]
            v.xt[b, :, y * 128 : (y + 1) * 128] = half_of(v.flow_tmp[...])
        return carry

    lax.fori_loop(0, BATCH, flow, 0)

    def image(b, carry):
        at = pl.ds(pl.multiple_of(b * AREA, AREA), AREA)
        spread_five(v, full_of(v.context[b]), v.xi.at[at], lambda t: t * 256)
        spread_five(v, full_of(v.net[b]), v.xs.at[at], lambda t: t * 128)
        return carry

    lax.fori_loop(0, BATCH, image, 0)


def gather_start(v, count):
    pieces = 4
    rows = BLOCK // 2 // pieces
    half = lax.rem(v.spot, 2)
    shift = lax.rem(v.rank * count, LANES)
    chunk = 512
    keep = lane_index((chunk, LANES)) >= shift
    v.tmp[7:8, :] = jnp.zeros((1, LANES), jnp.float32)

    def rotate(step, carry):
        at = pl.ds(pl.multiple_of(step * chunk, chunk), chunk)
        moved = pltpu.roll(full_of(v.gath[at, :]), shift, 1)
        v.tmp[8 : 8 + chunk, :] = moved
        v.gath[at, :] = half_of(jnp.where(keep, moved, v.tmp[7 : 7 + chunk, :]))
        v.tmp[7:8, :] = v.tmp[7 + chunk : 8 + chunk, :]
        return carry

    lax.fori_loop(0, BLOCK // chunk, rotate, 0)

    def piece(rank, which, index):
        return pl.ds(pl.multiple_of(rank * BLOCK + which * (BLOCK // 2) + index * rows, 16), rows)

    mine = pl.ds(pl.multiple_of(v.rank * BLOCK, 16), BLOCK)
    own = v.gath.at[0:BLOCK]
    v.g_x = [
        remote(
            v.gath.at[piece(0, half, k)], v.out_all.at[piece(v.rank, half, k)], v.gsend.at[0, k], v.grecv.at[0, k],
            {DP: v.other},
        )
        for k in range(pieces)
    ]
    v.g_own = remote(own, v.out_all.at[mine], v.gsend.at[4, 0], v.grecv.at[4, 0], {DP: v.mate})
    v.g_here = pltpu.make_async_copy(own, v.out_all.at[mine], v.gsend.at[4, 1])

    def forward(number, which, k, device):
        block = v.out_all.at[piece(v.other, which, k)]
        return remote(block, block, v.gsend.at[number, k], v.grecv.at[number, k], device)

    v.g_twin = [forward(1, half, k, {SPACE: v.twin}) for k in range(pieces)]
    v.g_mate = [forward(2, half, k, {DP: v.mate}) for k in range(pieces)]
    v.g_last = [forward(3, 1 - half, k, {DP: v.mate}) for k in range(pieces)]
    for copy in v.g_x:
        copy.start()
    v.g_own.start()
    v.g_here.start()


def gather_pass(v, first, last):
    for k in range(first, last):
        v.g_x[k].wait_recv()
        v.g_twin[k].start()
        v.g_mate[k].start()


def gather_end(v):
    for k in range(len(v.g_x)):
        v.g_twin[k].wait_recv()
        v.g_last[k].start()
    for k in range(len(v.g_x)):
        v.g_x[k].wait_send()
        v.g_twin[k].wait_send()
        v.g_mate[k].wait()
        v.g_last[k].wait()
    v.g_own.wait()
    v.g_here.wait()


def forward_rows(v):
    spot, last = v.spot, v.space - 1
    def image(b, carry):
        pieces = (
            (v.corr_up, 0, 256, 2, spot > 0),
            (v.corr, 256, 640, 5, None),
            (v.corr_down, 896, 256, 2, spot < last),
        )
        bias = bias_of(v, CORR_IN, 2)
        for ref, row0, rows, lines, seen in pieces:
            act, slope = act_slope(tn(lines_of(ref, b, lines), v.w_ci[...]) + bias)
            if seen is None:
                v.slope_ci[b] = half_of(slope)
            else:
                act = jnp.where(seen, act, 0.0)
            spread_rows(v, b, (act[:, :128], act[:, 128:]), rows, v.hx_c, row0, 256)

        act, slope = act_slope(tn(v.xt[b], v.w_fi[...]) + bias_of(v, FLOW_IN, 1))
        v.slope_fi[b] = half_of(slope[256:896])
        spread_rows(v, b, (edge_rows(v, act, 2 * WIDE),), 9 * WIDE, v.hx_f, 0, 128)

        pre = mm(join(v.hx_c[b, a * 128 : a * 128 + 896, :] for a in range(3)), v.w_cm[...]) + bias_of(v, CORR_MIX, 2)
        flow_pre = mm(join(v.hx_f[b, a * 128 : a * 128 + 896, :] for a in range(3)), v.w_fm[...])
        flow_pre = flow_pre + bias_of(v, FLOW_MIX, 1)
        low, low_slope = act_slope(pre[:, :128])
        high, high_slope = act_slope(pre[:, 128:] + flow_pre)
        v.slope_j[b, :, 0:128] = half_of(low_slope)
        v.slope_j[b, :, 128:256] = half_of(high_slope)
        spread_rows(v, b, (edge_rows(v, low, WIDE), edge_rows(v, high, WIDE)), 896, v.hx_j, 0, 256)

        pre = mm(join(v.hx_j[b, a * 128 : a * 128 + 640, :] for a in range(3)), v.w_mm[...])
        pre = pre + bias_of(v, MOTION_MIX, 1)
        act, slope = act_slope(pre)
        v.slope_m[b] = half_of(jnp.where(lane_index((AREA, LANES)) < 126, slope, 0.0))
        pick = jnp.where(lane_index((16, LANES)) == row_index((16, LANES)) + 126, 1.0, 0.0)
        own_flow = v.flow[b]
        for y in range(ROWS):
            v.tmp2[0:2, :] = own_flow[2 * y : 2 * y + 2, :]
            v.tmp2[2:16, :] = jnp.zeros((14, LANES), jnp.float32)
            v.motion[b, y * 128 : (y + 1) * 128, :] = act[y * 128 : (y + 1) * 128, :] + tn(
                half_of(v.tmp2[0:16, :]), half_of(pick)
            )
        v.motion[b] = full_of(half_of(v.motion[b]))
        pack_rows(v, v.motion, b, v.a_motion)
        return carry

    lax.fori_loop(0, BATCH, image, 0)
    v.swap_motion.start()

    def gru(b, carry):
        at = pl.ds(pl.multiple_of(b * AREA, AREA), AREA)
        s = full_of(v.net[b])
        spread_five(v, v.motion[b], v.xi.at[at], lambda t: t * 256 + 128)
        both = mm(v.xi[at, :], v.w_ri[...])
        gates = jax.nn.sigmoid(both[:, :256] + mm(v.xs[at, :], v.w_rs[:, :256]) + bias_of(v, ROWS_GATES, 2))
        update, reset = gates[:, :128], gates[:, 128:]
        v.ru[b] = update
        v.rr[b] = reset
        spread_five(v, full_of(half_of(reset * s)), v.xr.at[at], lambda t: t * 128)
        cand = jnp.tanh(both[:, 256:] + mm(v.xr[at, :], v.w_rs[:, 256:]) + bias_of(v, ROWS_CANDIDATE, 1))
        v.rc[b] = cand
        v.state[b] = s + update * (cand - s)
        pack_rows(v, v.state, b, v.a_state)
        return carry

    lax.fori_loop(0, BATCH, gru, 0)
    v.swap_state.start()


def pack_rows(v, src, b, dst):
    def peer(t, carry):
        for y in range(ROWS):
            at = pl.multiple_of(y * WIDE + t * COLS, COLS)
            dst[t, b, y * COLS : (y + 1) * COLS, :] = half_of(src[b, pl.ds(at, COLS), :])
        return carry

    lax.fori_loop(0, v.space, peer, 0)


def take_own(v, src, dst):
    dst[v.spot] = src[v.spot]


def columns_zero(v):
    def zero(b, carry):
        for ref, wide in ((v.xc, 384), (v.xcr, 128), (v.gc, 384)):
            for low in (0, 32 + AREA):
                ref[b, low : low + 32, :] = jnp.zeros((32, wide), jnp.bfloat16)
        return carry

    lax.fori_loop(0, BATCH, zero, 0)


def columns_in(v):
    def peer(t, carry):
        at = pl.ds(pl.multiple_of(32 + t * ROWS * COLS, 16), ROWS * COLS)
        for b in range(BATCH):
            v.xc[b, at, 0:128] = v.b_state[t, b]
            v.xc[b, at, 128:256] = v.b_context[t, b]
            v.xc[b, at, 256:384] = v.b_motion[t, b]
        return carry

    lax.fori_loop(0, v.space, peer, 0)


FX_ROWS = 16 + (TALL + 2) * PITCH


def fx_base(b):
    return pl.multiple_of(b * FX_ROWS, 8)


def columns_forward(v):
    def gru(b, carry):
        s = full_of(v.xc[b, 32 : 32 + AREA, 0:128])
        bias = join((bias_of(v, COLUMNS_GATES, 2), bias_of(v, COLUMNS_CANDIDATE, 1)))
        rows = [slice(t * COLS, t * COLS + AREA) for t in range(5)]
        both = mm(join(v.xc[b, rows[t], 128:384] for t in range(5)), v.w_li[...]) + bias
        gates = mm(join(v.xc[b, rows[t], 0:128] for t in range(5)), v.w_ls[:, 0:256])
        gates = jax.nn.sigmoid(gates + both[:, :256])
        update, reset = gates[:, :128], gates[:, 128:]
        v.lu[b] = update
        v.lr[b] = reset
        v.xcr[b, 32 : 32 + AREA, :] = half_of(reset * s)
        cand = jnp.tanh(both[:, 256:] + mm(join(v.xcr[b, rows[t], :] for t in range(5)), v.w_ls[:, 256:384]))
        v.lc[b] = cand
        final = s + update * (cand - s)
        v.out_net[b] = half_of(final)
        v.final[...] = full_of(half_of(final))
        fx = fx_base(b)
        v.mm_tmp[pl.ds(fx, FX_ROWS), :] = jnp.zeros((FX_ROWS, LANES), jnp.float32)
        for x in range(COLS):
            v.mm_tmp[pl.ds(fx + 8 + PITCH + 2 + x, TALL, stride=PITCH), :] = v.final[pl.ds(x, TALL, stride=COLS), :]
        for j in range(2):
            v.e_left[b, j, 0:TALL, :] = half_of(v.final[pl.ds(j, TALL, stride=COLS), :])
            v.e_right[b, j, 0:TALL, :] = half_of(v.final[pl.ds(COLS - 2 + j, TALL, stride=COLS), :])
        return carry

    lax.fori_loop(0, BATCH, gru, 0)
    v.halo_final.start()


def ring_masks(v, shape):
    x = lax.rem(row_index(shape), PITCH)
    place = v.spot * COLS + x - 2
    seen = (place >= 0) & (place < WIDE) & (x >= 1) & (x < PITCH - 1)
    own = (x >= 2) & (x < PITCH - 2)
    return seen, own


def mask_gradient(v):
    def image(b, carry):
        value = nt(quarter_of(v.grad_mask[b]), v.w_mo[:, 0:MASK])
        for block in range(2):
            v.final[...] = value[:, block * 128 : (block + 1) * 128]
            v.tmp[0:SPREAD, :] = jnp.zeros((SPREAD, LANES), jnp.float32)
            for x in range(COLS):
                v.tmp[pl.ds(2 + x, TALL, stride=PITCH), :] = v.final[pl.ds(x, TALL, stride=COLS), :]
            v.hgo[b, :, 256 + block * 128 : 384 + block * 128] = half_of(v.tmp[0:SPREAD, :])
            v.m_left[b, block, 0:TALL, :] = half_of(v.final[pl.ds(0, TALL, stride=COLS), :])
            v.m_right[b, block, 0:TALL, :] = half_of(v.final[pl.ds(COLS - 1, TALL, stride=COLS), :])
        return carry

    lax.fori_loop(0, BATCH, image, 0)
    v.halo_mask.start()


def heads_part(v, b, tap):
    ref = v.hx_c if tap < 6 else v.hx_f
    lane = tap % 6 * 128
    return ref.at[b, 0:SPREAD, lane : lane + 128]


def taps_part(v, t, low, high):
    ref = v.hx_f if t % 3 == 2 else v.hx_c
    lane = (t % 3) % 2 * 384
    return ref.at[t // 3, 0:AREA, lane + low : lane + high]


def heads(v):
    spot, last = v.spot, v.space - 1
    v.halo_final.receive()
    v.halo_mask.receive()
    v.swap_count.receive()
    v.counts[v.spot] = v.count_out[...]
    counts = jnp.sum(v.counts[...], axis=0)
    seen, own = ring_masks(v, (SPREAD, LANES))
    steps = [(a - 1) * PITCH + (c - 1) for a in range(3) for c in range(3)]
    plane = jnp.float32(TALL * WIDE)

    def image(b, carry):
        fx = fx_base(b)
        for j in range(2):
            left = jnp.where(spot > 0, full_of(v.f_left[b, j, 0:TALL, :]), 0.0)
            right = jnp.where(spot < last, full_of(v.f_right[b, j, 0:TALL, :]), 0.0)
            v.mm_tmp[pl.ds(fx + 8 + PITCH + j, TALL, stride=PITCH), :] = left
            v.mm_tmp[pl.ds(fx + 8 + PITCH + PITCH - 2 + j, TALL, stride=PITCH), :] = right
        for block in range(2):
            left = jnp.where(spot > 0, full_of(v.n_left[b, block, 0:TALL, :]), 0.0)
            right = jnp.where(spot < last, full_of(v.n_right[b, block, 0:TALL, :]), 0.0)
            v.tmp[0:SPREAD, :] = full_of(v.hgo[b, :, 256 + block * 128 : 384 + block * 128])
            v.tmp[pl.ds(1, TALL, stride=PITCH), :] = left
            v.tmp[pl.ds(PITCH - 2, TALL, stride=PITCH), :] = right
            v.hgo[b, :, 256 + block * 128 : 384 + block * 128] = half_of(v.tmp[0:SPREAD, :])
        for tap in range(9):
            at = 8 + PITCH + steps[tap]
            heads_part(v, b, tap)[...] = half_of(v.mm_tmp[pl.ds(fx + at, SPREAD), :])
        for part in range(2):
            name = (FLOW_HIDDEN, MASK_HIDDEN)[part]
            lanes = slice(part * 256, (part + 1) * 256)
            act, slope = act_slope(mm(join((v.hx_c[b, 0:SPREAD, :], v.hx_f[b, 0:SPREAD, :])), v.w_h[:, lanes]) + bias_of(v, name, 2))
            v.slope_h[b, :, lanes] = half_of(slope)
            if part == 0:
                for block in range(2):
                    value = jnp.where(seen, act[:, block * 128 : (block + 1) * 128], 0.0)
                    v.feat[b, 0:SPREAD, block * 128 : (block + 1) * 128] = half_of(value)
                v.feat[b, SPREAD:SPAN, :] = jnp.zeros((SPAN - SPREAD, HEAD), jnp.bfloat16)
            else:
                for block in range(2):
                    v.tmp[0:SPREAD, :] = act[:, block * 128 : (block + 1) * 128]
                    for x in range(COLS):
                        v.final[pl.ds(x, TALL, stride=COLS), :] = v.tmp[pl.ds(2 + x, TALL, stride=PITCH), :]
                    v.mf[b, :, block * 128 : (block + 1) * 128] = half_of(v.final[...])
        moved = nt(v.w_fo[...], v.feat[b])
        v.zt[...] = moved
        delta = jnp.zeros((8, SPAN), jnp.float32)
        for tap in range(9):
            pair = jnp.concatenate([v.zt[2 * tap : 2 * tap + 2, :], jnp.zeros((6, SPAN), jnp.float32)], axis=0)
            delta = delta + pltpu.roll(pair, (-steps[tap]) % SPAN, 1)
        v.tmp[0:SPAN, :] = jnp.zeros((SPAN, LANES), jnp.float32)
        v.final[...] = full_of(v.xc[b, 32 : 32 + AREA, 256:384])
        for x in range(COLS):
            v.tmp[pl.ds(2 + x, TALL, stride=PITCH), :] = v.final[pl.ds(x, TALL, stride=COLS), :]
        pick = jnp.where(lane_index((16, LANES)) == row_index((16, LANES)) + 126, 1.0, 0.0)
        base = nt(half_of(pick), half_of(v.tmp[0:SPAN, :]))[0:8, :]
        bias = v.bias[BIAS_AT[FLOW_OUT] : BIAS_AT[FLOW_OUT] + 1, :]
        first = row_index((8, SPAN)) == 0
        second = row_index((8, SPAN)) == 1
        shift = jnp.where(first, bias[0:1, 0:1], jnp.where(second, bias[0:1, 1:2], 0.0))
        new = base + delta + shift
        v.out_flow[b] = new
        error = new - v.target[b]
        root = jnp.sqrt(error * error + 1.0)
        valid = jnp.where(first | second, v.valid[b], 0.0)
        piece = jnp.sum(valid * root)
        divisor = jnp.maximum(v.pick_count(counts, b), 1.0)
        gradient = plane / divisor * valid * error / root
        v.dg[b] = gradient
        v.losses[...] = jnp.where(row_index((8, LANES)) == b, piece, v.losses[...])
        return carry

    v.losses[...] = jnp.zeros((8, LANES), jnp.float32)
    lax.fori_loop(0, BATCH, image, 0)
    v.halo_dg.start()
    v.swap_loss.start()


def mask_output(v):
    def image(b, carry):
        store = pltpu.make_async_copy(v.mask_low, v.out_mask.at[b], v.osem.at[3])
        pl.when(b > 0)(store.wait)
        for block in range(5):
            wide = min(128, MASK - block * 128)
            lanes = slice(block * 128, block * 128 + wide)
            at = BIAS_AT[MASK_OUT] + block
            value = mm(v.mf[b], v.w_mo[:, lanes]) + v.bias[at : at + 1, 0:wide]
            v.mask_low[:, lanes] = half_of(0.25 * value)
        store.start()
        return carry

    lax.fori_loop(0, BATCH, image, 0)


def heads_back(v):
    spot, last = v.spot, v.space - 1
    seen, own = ring_masks(v, (SPREAD, LANES))
    steps = [(a - 1) * PITCH + (c - 1) for a in range(3) for c in range(3)]
    v.halo_dg.receive()

    def zb(c, low, rows):
        at = c * (2 * EDGE + SPREAD) + low
        return v.mm_tmp.at[at : at + rows]

    def image(b, carry):
        x = lax.rem(lane_index((8, SPAN)), PITCH)
        own_dg = v.dg[b]
        left = jnp.where((x < 2) & (spot > 0), pltpu.roll(v.dg_left[b], SPAN - COLS, 1), 0.0)
        right = jnp.where((x >= PITCH - 2) & (spot < last), pltpu.roll(v.dg_right[b], COLS, 1), 0.0)
        inside = lane_index((8, SPAN)) < SPREAD
        wide_dg = full_of(half_of(jnp.where(inside, own_dg + left + right, 0.0)))
        own_low = full_of(half_of(own_dg))
        v.dt[...] = jnp.zeros_like(v.dt)
        v.dto[...] = jnp.zeros_like(v.dto)
        for tap in range(9):
            v.dt[2 * tap : 2 * tap + 2, :] = pltpu.roll(wide_dg, steps[tap] % SPAN, 1)[0:2, :]
            v.dto[2 * tap : 2 * tap + 2, :] = pltpu.roll(own_low, steps[tap] % SPAN, 1)[0:2, :]
        v.dtb[b] = half_of(v.dto[...])
        from_flow = tn(half_of(v.dt[...]), v.w_fo[...])
        for block in range(4):
            lanes = slice(block * 128, (block + 1) * 128)
            value = from_flow[0:SPREAD, lanes] if block < 2 else full_of(v.hgo[b, :, lanes])
            value = value * full_of(v.slope_h[b, :, lanes])
            v.hgo[b, :, lanes] = half_of(jnp.where(seen, value, 0.0))
        total = jnp.zeros((SPREAD, LANES), jnp.float32)
        for a in range(3):
            value = nt(v.hgo[b], v.w_h[a * 384 : (a + 1) * 384, :])
            for c in range(3):
                zb(c, EDGE, SPREAD)[...] = value[:, c * 128 : (c + 1) * 128]
            for c in range(3):
                at = EDGE - steps[a * 3 + c]
                total = total + zb(c, at, SPREAD)[...]
        for block in range(4):
            lanes = slice(block * 128, (block + 1) * 128)
            v.hgo[b, :, lanes] = half_of(jnp.where(own, full_of(v.hgo[b, :, lanes]), 0.0))
        v.tmp[0:SPREAD, :] = total
        for x in range(COLS):
            v.final[pl.ds(x, TALL, stride=COLS), :] = v.tmp[pl.ds(2 + x, TALL, stride=PITCH), :]
        r = v.final[...] + full_of(v.grad_net[b])

        s = full_of(v.xc[b, 32 : 32 + AREA, 0:128])
        update, reset, cand = v.lu[b], v.lr[b], v.lc[b]
        cg = half_of(r * update * (1.0 - cand * cand))
        v.gc[b, 32 : 32 + AREA, 256:384] = cg
        rows = [slice((4 - t) * COLS, (4 - t) * COLS + AREA) for t in range(5)]
        reset_grad = nt(
            join(v.gc[b, rows[t], 256:384] for t in range(5)),
            join(v.w_ls[t * 128 : (t + 1) * 128, 256:384] for t in range(5)),
        )
        v.gc[b, 32 : 32 + AREA, 0:128] = half_of(r * (cand - s) * update * (1.0 - update))
        v.gc[b, 32 : 32 + AREA, 128:256] = half_of(reset_grad * s * reset * (1.0 - reset))
        state_grad = r * (1.0 - update) + reset_grad * reset
        state_grad = state_grad + nt(
            join(v.gc[b, rows[t], 0:256] for t in range(5)),
            join(v.w_ls[t * 128 : (t + 1) * 128, 0:256] for t in range(5)),
        )
        inputs_grad = nt(
            join(v.gc[b, rows[t], :] for t in range(5)), join(v.w_li[t * 256 : (t + 1) * 256, :] for t in range(5))
        )
        high = half_of(own_dg)
        low = half_of(own_dg - full_of(high))
        pick = half_of(jnp.where(lane_index((8, LANES)) == row_index((8, LANES)) + 126, 1.0, 0.0))
        v.tmp[0:SPAN, :] = tn(high, pick) + tn(low, pick)
        for x in range(COLS):
            v.final[pl.ds(x, TALL, stride=COLS), :] = v.tmp[pl.ds(2 + x, TALL, stride=PITCH), :]
        v.lu[b] = state_grad
        v.lr[b] = inputs_grad[:, 0:128]
        v.lc[b] = inputs_grad[:, 128:256] + v.final[...]

        def peer(t, carry):
            at = pl.ds(pl.multiple_of(t * ROWS * COLS, 16), ROWS * COLS)
            v.a_state[t, b] = half_of(v.lu[b, at, :])
            v.a_context[t, b] = half_of(v.lr[b, at, :])
            v.a_motion[t, b] = half_of(v.lc[b, at, :])
            return carry

        lax.fori_loop(0, v.space, peer, 0)
        return carry

    for c in range(3):
        zb(c, 0, EDGE)[...] = jnp.zeros((EDGE, LANES), jnp.float32)
        zb(c, EDGE + SPREAD, EDGE)[...] = jnp.zeros((EDGE, LANES), jnp.float32)
    lax.fori_loop(0, BATCH, image, 0)
    v.swap_loss.receive()
    v.back_state.start()


def unpack_back(v, src, dst):
    def peer(t, carry):
        for b in range(BATCH):
            value = full_of(src[t, b])
            for y in range(ROWS):
                at = pl.multiple_of(y * WIDE + t * COLS, COLS)
                dst[b, pl.ds(at, COLS), :] = value[y * COLS : (y + 1) * COLS, :]
        return carry

    lax.fori_loop(0, v.space, peer, 0)


def seams():
    starts, bias_row, _, _ = flat_rows()
    edges = sorted(starts.values()) + [bias_row]
    tiles = sorted({row // 16 for row in edges if row % 16})
    parts = {}
    for low, high in zip(edges, edges[1:]):
        for tile in tiles:
            if low < (tile + 1) * 16 and high > tile * 16:
                parts[tile] = parts.get(tile, 0) + 1
    return {tile: (index, parts[tile]) for index, tile in enumerate(tiles)}


class Flush:
    def __init__(self, v):
        self.v, self.at, self.busy, self.small = v, 0, {}, []
        self.tiles = seams()
        self.left = {tile: parts for tile, (_, parts) in self.tiles.items()}
        v.seam[...] = jnp.zeros_like(v.seam)
        top = (max(self.tiles) + 1) * 16
        rest = v.out_flat.shape[0] - top
        v.seam_low[16 * 16 : 16 * 16 + rest, :] = jnp.zeros((rest, LANES), jnp.bfloat16)
        self.write(16, rest, top)

    def write(self, index, rows, base):
        v = self.v
        copy = pltpu.make_async_copy(
            v.seam_low.at[index * 16 : index * 16 + rows], v.out_flat.at[base : base + rows], v.fsem.at[index]
        )
        copy.start()
        self.small.append(copy)

    def send(self, low, length, base):
        v, slot = self.v, self.at % 2
        self.at += 1
        if slot in self.busy:
            self.busy[slot].wait()
        cast_rows(v.stage.at[slot], 0, v.flat, low, length, jnp.bfloat16)
        copy = pltpu.make_async_copy(
            v.stage.at[slot, 0:length], v.out_flat.at[base : base + length], v.ssem.at[slot, 0]
        )
        copy.start()
        self.busy[slot] = copy

    def layer(self, start, rows):
        v, stop = self.v, start + rows
        for tile in self.tiles:
            low, high = max(start, tile * 16), min(stop, tile * 16 + 16)
            if low >= high:
                continue
            index = self.tiles[tile][0]
            v.seam[index, low - tile * 16 : high - tile * 16, :] = v.flat[MARGIN + low - start : MARGIN + high - start, :]
            self.left[tile] -= 1
            if not self.left[tile]:
                v.seam_low[index * 16 : index * 16 + 16, :] = half_of(v.seam[index])
                self.write(index, 16, tile * 16)
        low, high = -(-start // 16) * 16, stop // 16 * 16
        if high > low:
            self.send(MARGIN + low - start, high - low, low)

    def settle(self):
        for copy in list(self.busy.values()) + self.small:
            copy.wait()
        self.busy, self.small = {}, []


SHARE = 3072


class Reduce:
    ORDER = (
        (3, 3072, 3072), (3, 0, 3072), (2, 3072, 3072), (2, 0, 3072), (1, 3072, 3072), (1, 0, 3072),
        (0, 1024, 3072), (0, 4096, 2048), (0, 0, 1024),
    )

    def __init__(self, v, count):
        self.v, self.count = v, count
        self.flying, self.queue = [], []
        self.copies = {}
        rank = v.rank
        self.lower, self.upper = lax.rem(rank, 2), lax.div(rank, 2)
        self.side, self.depth = lax.rem(v.spot, 2), lax.div(v.spot, 2)
        self.group = v.space // 2

    def part(self, k):
        return self.ORDER[k][2] // 4 // self.v.space

    def slice_at(self, k, spot):
        return lax.rem(spot, 2) * (self.ORDER[k][2] // 8) + lax.div(spot, 2) * self.part(k)

    def offer(self, *numbers):
        self.queue += list(numbers)

    LONG = 6

    def stages(self, k):
        if k < self.LONG:
            return (self.core, self.across, self.side_sum, self.deep_sum, self.deep_out, self.owner, self.beside)
        if k < len(self.ORDER) - 1:
            return (self.core, self.across, self.stripes, self.along, self.beside)
        return (self.ranks, self.stripes, self.along, self.beside)

    def tick(self):
        for entry in self.flying:
            self.stages(entry[0])[entry[1]](entry[0])
            entry[1] += 1
        self.flying = [entry for entry in self.flying if entry[1] < len(self.stages(entry[0]))]
        if self.queue:
            number = self.queue.pop(0)
            self.v.flush.settle()
            self.begin(number)
            self.flying.append([number, 0])

    def begin(self, k):
        v, slot = self.v, k % 2
        quarter, low, size = self.ORDER[k]
        start = quarter * self.count // (LANES * 16) * 16 + low
        half = size // 2
        if k == len(self.ORDER) - 1:
            self.begin_ranks(start, size // 4)
            return

        def rows(which):
            return v.out_flat.at[pl.ds(pl.multiple_of(start + which * half, 16), half)]

        copy = remote(
            rows(1 - self.lower), v.rcore.at[slot, 0:half], v.rsend.at[0, slot], v.rrecv.at[0, slot], {DP: v.mate}
        )
        own = pltpu.make_async_copy(rows(self.lower), v.own.at[slot, 0:half], v.rlocal.at[slot])
        copy.start()
        own.start()
        self.copies[k] = (copy, own)

    def begin_ranks(self, start, rows):
        v = self.v

        def block(rank):
            at = start + lax.rem(rank, 2) * (2 * rows) + lax.div(rank, 2) * rows
            return v.out_flat.at[pl.ds(pl.multiple_of(at, 16), rows)]

        for turn in range(1, 4):
            to = lax.rem(v.rank + turn, 4)
            remote(block(to), v.dall.at[v.rank], v.dsend, v.drecv, {DP: to}).start()
        self.mine = pltpu.make_async_copy(block(v.rank), v.dall.at[v.rank], v.rlocal.at[0])
        self.mine.start()

    def ranks(self, k):
        v, slot, part = self.v, k % 2, self.part(k)
        self.mine.wait()
        drain_bytes(v.dall.at[0:3], v.dsend)
        drain_bytes(v.dall.at[0:3], v.drecv)
        self.finish_f(k)
        value = full_of(v.dall[0]) + full_of(v.dall[1]) + full_of(v.dall[2]) + full_of(v.dall[3])
        rows = self.ORDER[k][2] // 4
        v.ks[slot, 0:rows, :] = value
        v.ts[slot, 0:rows, :] = half_of(value)
        v.acc[slot, 0:part, :] = v.ks[slot, pl.ds(pl.multiple_of(self.slice_at(k, v.spot), 16), part), :]
        self.each(lambda step: self.s_copy(k, step).start(), 1, v.space)

    def finish_f(self, k):
        drain_bytes(self.s_all(k - 2), self.v.s2send.at[k % 2])
        self.f_sent(k - 2)

    def core(self, k):
        v, slot = self.v, k % 2
        copy, own = self.copies[k]
        copy.wait()
        own.wait()
        if k >= 2:
            self.x_copy(k - 2).wait_send()
        quarter = self.ORDER[k][2] // 4

        def add(step, carry):
            at = pl.multiple_of(step * 128, 128)
            near = pl.ds(pl.multiple_of(self.upper * quarter + at, 128), 128)
            far = pl.ds(pl.multiple_of((1 - self.upper) * quarter + at, 128), 128)
            to = pl.ds(at, 128)
            v.tx[slot, to, :] = half_of(full_of(v.own[slot, far, :]) + full_of(v.rcore[slot, far, :]))
            v.ks[slot, to, :] = full_of(v.own[slot, near, :]) + full_of(v.rcore[slot, near, :])
            return carry

        lax.fori_loop(0, quarter // 128, add, 0)
        self.x_copy(k).start()

    def x_copy(self, k):
        v, slot = self.v, k % 2
        rows = slice(0, self.ORDER[k][2] // 4)
        return remote(
            v.tx.at[slot, rows], v.rx.at[slot, rows], v.rsend.at[1, slot], v.rrecv.at[1, slot], {DP: v.other}
        )

    def s_copy(self, k, step):
        v, slot, part = self.v, k % 2, self.part(k)
        to = lax.rem(v.spot + step, v.space)
        src = v.ts.at[slot, pl.ds(pl.multiple_of(self.slice_at(k, to), 16), part)]
        dst = v.rs.at[slot, v.spot, 0:part]
        return remote(src, dst, v.s2send.at[slot], v.s2recv.at[slot], {SPACE: to})

    def s_all(self, k):
        return self.v.rs.at[k % 2, 0 : self.v.space - 1, 0 : self.part(k)]

    def each(self, what, start, stop):
        def body(step, carry):
            what(step)
            return carry

        lax.fori_loop(start, stop, body, 0)

    def across(self, k):
        v, slot = self.v, k % 2
        self.x_copy(k).wait_recv()
        if k < self.LONG:
            self.across_long(k)
            return

        def add(step, carry):
            to = pl.ds(pl.multiple_of(step * 128, 128), 128)
            value = v.ks[slot, to, :] + full_of(v.rx[slot, to, :])
            v.ks[slot, to, :] = value
            v.ts[slot, to, :] = half_of(value)
            return carry

        lax.fori_loop(0, self.ORDER[k][2] // 4 // 128, add, 0)
        part = self.part(k)
        v.acc[slot, 0:part, :] = v.ks[slot, pl.ds(pl.multiple_of(self.slice_at(k, v.spot), 16), part), :]
        self.each(lambda step: self.s_copy(k, step).start(), 1, v.space)

    def across_long(self, k):
        v, slot = self.v, k % 2
        if k >= 2:
            self.side_copy(k - 2).wait_send()
        rows = self.ORDER[k][2] // 8

        def add(step, carry):
            at = pl.multiple_of(step * 128, 128)
            near = pl.ds(pl.multiple_of(self.side * rows + at, 128), 128)
            far = pl.ds(pl.multiple_of((1 - self.side) * rows + at, 128), 128)
            to = pl.ds(at, 128)
            v.ty[slot, to, :] = half_of(v.ks[slot, far, :] + full_of(v.rx[slot, far, :]))
            v.ky[slot, to, :] = v.ks[slot, near, :] + full_of(v.rx[slot, near, :])
            return carry

        lax.fori_loop(0, rows // 128, add, 0)
        self.side_copy(k).start()

    def side_copy(self, k):
        v, slot = self.v, k % 2
        return remote(v.ty.at[slot], v.ry.at[slot], v.rsend.at[2, slot], v.rrecv.at[2, slot], {SPACE: v.twin})

    def deep_at(self, k, depth):
        return pl.ds(pl.multiple_of(depth * self.part(k), 16), self.part(k))

    def deep_copy(self, k, step):
        v, slot = self.v, k % 2
        to = lax.rem(self.depth + step, self.group)
        return remote(
            v.tz.at[slot, self.deep_at(k, to)], v.rz.at[slot, self.depth], v.z1send.at[slot],
            v.z1recv.at[slot], {SPACE: to * 2 + self.side},
        )

    def deep_all(self, k):
        return self.v.rz.at[k % 2, 0 : self.group - 1]

    def side_sum(self, k):
        v, slot = self.v, k % 2
        self.side_copy(k).wait_recv()
        if k >= 2:
            drain_bytes(self.deep_all(k - 2), v.z1send.at[slot])
        value = v.ky[slot] + full_of(v.ry[slot])
        v.tz[slot] = half_of(value)
        v.ky[slot] = value
        v.kz[slot] = v.ky[slot, self.deep_at(k, self.depth), :]
        self.each(lambda step: self.deep_copy(k, step).start(), 1, self.group)

    def out_copy(self, k, step):
        v, slot = self.v, k % 3
        to = lax.rem(self.depth + step, self.group)
        block = v.az.at[slot, self.deep_at(k, self.depth)]
        return remote(
            block, block, v.z2send.at[slot], v.z2recv.at[slot], {SPACE: to * 2 + self.side}
        )

    def deep_sum(self, k):
        v, slot = self.v, k % 2
        drain_bytes(self.deep_all(k), v.z1recv.at[slot])

        def add(step, value):
            return value + full_of(v.rz[slot, lax.rem(self.depth + step, self.group)])

        value = lax.fori_loop(1, self.group, add, v.kz[slot])
        if k >= 2:
            self.own_wait(k - 2)
        v.az[k % 3, self.deep_at(k, self.depth), :] = half_of(value)
        self.each(lambda step: self.out_copy(k, step).start(), 1, self.group)

    def own_rows(self, k, lower, upper):
        quarter, low, size = self.ORDER[k]
        at = low + lower * (size // 2) + upper * (size // 4) + self.side * (size // 8)
        return pl.ds(pl.multiple_of(at, 16), size // 8)

    def own_copy(self, k):
        v = self.v
        rows = self.own_rows(k, self.lower, self.upper)
        return remote(v.az.at[k % 3], v.gath.at[rows], v.osend.at[k % 3], v.orecv.at[k], {DP: self.ORDER[k][0]})

    def own_wait(self, k):
        pl.when(self.v.rank != self.ORDER[k][0])(self.own_copy(k).wait_send)

    def deep_out(self, k):
        v = self.v
        several = v.az.at[k % 3, 0 : (self.group - 1) * self.part(k)]
        drain_bytes(several, v.z2send.at[k % 3])
        drain_bytes(several, v.z2recv.at[k % 3])
        pl.when(v.rank != self.ORDER[k][0])(self.own_copy(k).start)

        @pl.when(v.rank == self.ORDER[k][0])
        def _():
            v.gath[self.own_rows(k, self.lower, self.upper), :] = v.az[k % 3]

    def owner(self, k):
        v = self.v

        @pl.when(v.rank == self.ORDER[k][0])
        def _():
            drain_bytes(v.gath.at[0 : 3 * (self.ORDER[k][2] // 8)], v.orecv.at[k])
            for copy in self.y_copies(k):
                copy.start()

    def place(self, k, lower, upper, spot):
        quarter, low, size = self.ORDER[k]
        at = low + lower * (size // 2) + upper * (size // 4) + self.slice_at(k, spot)
        return pl.ds(pl.multiple_of(at, 16), self.part(k))

    def f_copy(self, k, step):
        v, slot = self.v, k % 2
        quarter = self.ORDER[k][0]
        to = lax.rem(self.depth + step, self.group) * 2 + self.side
        return remote(
            v.fin.at[slot, 0 : self.part(k)], v.gath.at[self.place(k, self.lower, self.upper, v.spot)],
            v.fsend.at[slot], v.frecv.at[k], {DP: quarter, SPACE: to},
        )

    def f_all(self, k, what):
        v = self.v
        pl.when(v.rank != self.ORDER[k][0])(lambda: what(self.f_copy(k, 0)))
        self.each(lambda step: what(self.f_copy(k, step)), 1, self.group)

    def f_sent(self, k):
        v = self.v
        quarter = self.ORDER[k][0]
        pl.when(v.rank != quarter)(lambda: self.f_copy(k, 0).wait_send())
        drain_bytes(v.gath.at[0 : (self.group - 1) * self.part(k)], v.fsend.at[k % 2])

    def stripes(self, k):
        v, slot, part = self.v, k % 2, self.part(k)
        quarter = self.ORDER[k][0]
        drain_bytes(self.s_all(k), v.s2recv.at[slot])

        def add(step, value):
            return value + full_of(v.rs[slot, lax.rem(v.spot + step, v.space), 0:part])

        value = half_of(lax.fori_loop(1, v.space, add, v.acc[slot, 0:part, :]))
        v.fin[slot, 0:part, :] = value

        @pl.when(v.rank == quarter)
        def _():
            v.gath[self.place(k, self.lower, self.upper, v.spot), :] = v.fin[slot, 0:part, :]

        self.f_all(k, lambda copy: copy.start())

    def y_copies(self, k):
        v = self.v
        quarter, low, size = self.ORDER[k]
        out = []
        for i in range(4):
            at = pl.multiple_of(low + i * (size // 4) + self.side * (size // 8), 16)
            block = v.gath.at[pl.ds(at, size // 8)]
            out.append(remote(block, block, v.ysend.at[k], v.yrecv.at[k], {SPACE: v.twin}))
        return out

    def along(self, k):
        v = self.v
        quarter = self.ORDER[k][0]

        @pl.when(v.rank == quarter)
        def _():
            drain_bytes(v.gath.at[0 : (4 * self.group - 1) * self.part(k)], v.frecv.at[k])
            for copy in self.y_copies(k):
                copy.start()

    def beside(self, k):
        v = self.v

        @pl.when(v.rank == self.ORDER[k][0])
        def _():
            several = v.gath.at[0 : self.ORDER[k][2] // 2]
            drain_bytes(several, v.ysend.at[k])
            drain_bytes(several, v.yrecv.at[k])

    def settle(self):
        v = self.v
        for k in range(self.LONG - 2, self.LONG):
            self.side_copy(k).wait_send()
            drain_bytes(self.deep_all(k), v.z1send.at[k % 2])
            self.own_wait(k)
        for k in range(len(self.ORDER) - 3, len(self.ORDER) - 1):
            self.x_copy(k).wait_send()
        for k in range(len(self.ORDER) - 2, len(self.ORDER)):
            drain_bytes(self.s_all(k), v.s2send.at[k % 2])
            self.f_sent(k)

    def ready(self):
        v, count = self.v, self.count
        v.gath[2 * SHARE :, :] = jnp.zeros((32, LANES), jnp.bfloat16)

        @pl.when(v.rank == 3)
        def _():
            at = self.bias_base() - 3 * count // (LANES * 16) * 16
            v.gath[at : at + 32, :] = half_of(full_of(v.gath[at : at + 32, :]) + v.bsum[...])

    def lay(self, first, last):
        v, count = self.v, self.count
        offset = v.rank * count - quarter_base(v.rank, count) * LANES
        skip = lax.div(offset, LANES)
        shift = lax.rem(offset, LANES)
        near = lane_index((256, LANES)) < LANES - shift

        def staged(slot):
            return v.mm_tmp.at[pl.ds(pl.multiple_of(slot * 256, 256), 256)]

        def out(step):
            at = pl.multiple_of(step * 256, 256)
            slot = lax.rem(step, 2)
            return pltpu.make_async_copy(staged(slot), v.out_grads.at[pl.ds(at, 256)], v.osem.at[4 + slot])

        def place(step, carry):
            at = pl.multiple_of(step * 256, 256)
            v.tmp[0:288, :] = pltpu.roll(full_of(v.gath[pl.ds(at, 288), :]), lax.rem(LANES - shift, LANES), 1)
            pl.when(step > first + 1)(out(step - 2).wait)
            staged(lax.rem(step, 2))[...] = jnp.where(near, v.tmp[pl.ds(skip, 256), :], v.tmp[pl.ds(skip + 1, 256), :])
            out(step).start()
            return carry

        lax.fori_loop(first, last, place, 0)
        for step in (last - 2, last - 1):
            out(step).wait()

    def bias_base(self):
        return flat_rows()[1] // 16 * 16

    def bias_core(self):
        v = self.v
        self.b1 = remote(v.bown, v.bcore, v.bsend.at[0], v.brecv.at[0], {DP: v.mate})
        self.b1.start()

    def bias_across(self):
        v = self.v
        self.b1.wait()
        v.btwo[...] = v.bown[...] + v.bcore[...]
        self.b2 = remote(v.btwo, v.bacross, v.bsend.at[1], v.brecv.at[1], {DP: v.other})
        self.b2.start()

    def bias_stripes(self):
        v = self.v
        self.b2.wait()
        v.bfour[...] = v.btwo[...] + v.bacross[...]
        self.b3 = Swap(v, 8, v.bfour, v.ball, True)
        self.b3.start()

    def bias_end(self):
        v = self.v
        self.b3.receive()
        self.b3.sent()
        v.ball[v.spot] = v.bfour[...]
        v.bsum[...] = jnp.sum(v.ball[...], axis=0)


def ones_sum(g):
    return mm(jnp.ones((8, g.shape[0]), jnp.bfloat16), g)[0:1, :]


def keep_bias(v, name, value):
    for block in range(-(-value.shape[1] // 128)):
        at = BIAS_AT[name] + block
        v.gbias[at : at + 1, :] = value[:, block * 128 : (block + 1) * 128]


def gradients_gru(v, gates_name, cand_name, parts, g_of):
    starts, _, _, _ = flat_rows()
    total = 0.0
    for b in range(BATCH):
        total = total + ones_sum(g_of(b))
    keep_bias(v, gates_name, total[:, 0:256])
    keep_bias(v, cand_name, total[:, 256:384])

    def taps(number, first, last):
        return lambda b: join(parts(t)[number](b) for t in range(first, last))

    state = tn_all(taps(0, 0, 5), g_of, 0, 256)
    for t in range(5):
        pack_pairs(v.flat, t * 384, 128, state[t * 128 : (t + 1) * 128, 0:128], state[t * 128 : (t + 1) * 128, 128:256])
    state = tn_all(taps(2, 0, 5), g_of, 256, 384)
    for t in range(5):
        v.mm_tmp[pl.ds(MARGIN + t * 384, 128), :] = state[t * 128 : (t + 1) * 128, :]
    for first, last in ((0, 2), (2, 4), (4, 5)):
        inputs = tn_all(taps(1, first, last), g_of, 0, 384)
        for t in range(first, last):
            rows = slice((t - first) * 256, (t - first + 1) * 256)
            pack_pairs(v.flat, t * 384 + 128, 256, inputs[rows, 0:128], inputs[rows, 128:256])
            v.mm_tmp[pl.ds(MARGIN + t * 384 + 128, 256), :] = inputs[rows, 256:384]
    v.flush.layer(starts[gates_name], 3840)
    cast_rows(v.flat, MARGIN, v.mm_tmp, MARGIN, 1920, jnp.float32)
    v.flush.layer(starts[cand_name], 1920)


def tn_all(part, g_of, low, high):
    return tn(join((part(b) for b in range(BATCH)), 0), join((g_of(b, low, high) for b in range(BATCH)), 0))


def gradients_heads(v):
    starts, _, _, _ = flat_rows()
    total = 0.0
    for b in range(BATCH):
        total = total + ones_sum(v.hgo[b])
    keep_bias(v, FLOW_HIDDEN, total[:, 0:256])
    keep_bias(v, MASK_HIDDEN, total[:, 256:512])
    for name, lane in ((FLOW_HIDDEN, 0), (MASK_HIDDEN, 256)):
        grads = join((v.hgo[b, :, lane : lane + 256] for b in range(BATCH)), 0)
        for group in range(3):
            taps = [join(heads_part(v, b, group * 3 + c)[...] for c in range(3)) for b in range(BATCH)]
            value = tn(join(taps, 0), grads)
            for c in range(3):
                rows = slice(c * 128, (c + 1) * 128)
                pack_pairs(v.flat, (group * 3 + c) * 128, 128, value[rows, 0:128], value[rows, 128:256])
        v.flush.layer(starts[name], 2304)

    total = 0.0
    sums = 0.0
    for b in range(BATCH):
        total = total + mm(v.dtb[b], v.feat[b])
        sums = sums + jnp.sum(full_of(half_of(v.dg[b])), axis=1, keepdims=True)
    lane1 = lane_index((1, LANES))
    at = BIAS_AT[FLOW_OUT]
    v.gbias[at : at + 1, :] = jnp.where(lane1 == 0, sums[0:1, :], jnp.where(lane1 == 1, sums[1:2, :], 0.0))
    v.fo_tmp[...] = total[:, 0:128]
    v.fo_tmp2[...] = total[:, 128:256]
    for quarter in range(4):
        value = 0.0
        for which in range(2):
            rows = jnp.concatenate(
                [v.fo_tmp[pl.ds(which, 9, stride=2), :], v.fo_tmp2[pl.ds(which, 9, stride=2), :]], axis=1
            )
            value = value + nt(half_of(rows), split_pick(which, quarter))
        v.flat[pl.ds(MARGIN + quarter, 9, stride=4), :] = value
    v.flush.layer(starts[FLOW_OUT], 36)

    lane = lane_index((128, LANES))
    low_half = lane < 64
    even, odd = [], []
    total = 0.0
    for b in range(BATCH):
        total = total + ones_sum(quarter_of(v.grad_mask[b]))
    for block in range(5):
        wide = min(128, MASK - block * 128)
        at = BIAS_AT[MASK_OUT] + block
        v.gbias[at : at + 1, 0:wide] = total[:, block * 128 : block * 128 + wide]
        value = 0.0
        for b in range(BATCH):
            value = value + tn(v.mf[b], quarter_of(v.grad_mask[b, :, block * 128 : block * 128 + wide]))
        v.pair_a[:, 0:wide] = value
        even.append(v.pair_a[pl.ds(0, 128, stride=2), :])
        odd.append(pltpu.roll(v.pair_a[pl.ds(1, 128, stride=2), :], 64, 1))
    for i in range(4):
        v.flat[pl.ds(MARGIN + i, 128, stride=9), :] = even[i]
    v.flat[pl.ds(MARGIN + 4, 128, stride=9), :] = jnp.where(low_half, even[4], odd[0])
    for i in range(4):
        v.flat[pl.ds(MARGIN + 5 + i, 128, stride=9), :] = jnp.where(low_half, odd[i], odd[i + 1])
    v.flush.layer(starts[MASK_OUT], 1152)


def rows_back(v):
    v.back_state.receive()
    take_own(v, v.a_state, v.b_state)
    unpack_back(v, v.b_state, v.state)
    v.reduce.tick()

    def image(b, carry):
        r = v.state[b]
        s = full_of(v.net[b])
        update, reset, cand = v.ru[b], v.rr[b], v.rc[b]
        cg = full_of(half_of(r * update * (1.0 - cand * cand)))
        spread_five(v, cg, None, 256, True)
        reset_grad = nt(
            join(taps_part(v, t, 256, 384)[...] for t in range(5)),
            join(v.w_rs[t * 128 : (t + 1) * 128, 256:384] for t in range(5)),
        )
        low = full_of(half_of(r * (cand - s) * update * (1.0 - update)))
        high = full_of(half_of(reset_grad * s * reset * (1.0 - reset)))
        spread_five(v, low, None, 0, True)
        spread_five(v, high, None, 128, True)
        v.gr[b] = taps_part(v, 2, 0, 384)[...]
        state_grad = r * (1.0 - update) + reset_grad * reset
        state_grad = state_grad + nt(
            join(taps_part(v, t, 0, 256)[...] for t in range(5)),
            join(v.w_rs[t * 128 : (t + 1) * 128, 0:256] for t in range(5)),
        )
        v.ru[b] = state_grad
        inputs_grad = nt(
            join(taps_part(v, t, 0, 384)[...] for t in range(5)),
            join(v.w_ri[t * 256 : (t + 1) * 256, :] for t in range(5)),
        )
        v.rr[b] = inputs_grad[:, 0:128]
        v.rc[b] = inputs_grad[:, 128:256]
        return carry

    lax.fori_loop(0, BATCH, image, 0)
    v.store_gnet.start()
    v.back_context.receive()
    v.back_motion.receive()
    take_own(v, v.a_context, v.b_context)
    take_own(v, v.a_motion, v.b_motion)
    unpack_back(v, v.b_context, v.lr)
    unpack_back(v, v.b_motion, v.lu)

    def total(b, carry):
        v.rr[b] = v.rr[b] + v.lr[b]
        motion = v.rc[b] + v.lu[b]
        v.mge[b, 256:896, :] = half_of(motion * full_of(v.slope_m[b]))
        high = half_of(motion)
        low = half_of(motion - full_of(high))
        pick = half_of(jnp.where(lane_index((16, LANES)) == row_index((16, LANES)) + 126, 1.0, 0.0))
        v.gf_base[b] = (nt(pick, high) + nt(pick, low))[0:8, :]
        return carry

    lax.fori_loop(0, BATCH, total, 0)
    v.halo_mg.start()
    v.store_gctx.start()


def gcorr_stores(v, b):
    return [
        pltpu.make_async_copy(v.mm_tmp.at[y * 328 : y * 328 + CORR], v.out_gcorr.at[b, y], v.gsem.at[y])
        for y in range(ROWS)
    ]


def branch_back(v):
    v.halo_mg.receive()

    def image(b, carry):
        up = jnp.where(v.spot > 0, full_of(v.mge[b, 0:256, :]), 0.0)
        own = full_of(v.mge[b, 256:896, :])
        down = jnp.where(v.spot < v.space - 1, full_of(v.mge[b, 896:1152, :]), 0.0)
        spread_rows(v, 0, (jnp.concatenate([up, own, down], axis=0),), 1152, v.xi, 0, 128, True)
        joint = nt(
            join(v.xi[(2 - a) * 128 : (2 - a) * 128 + 896, 0:384] for a in range(3)),
            join(v.w_mm[k * 256 : (k + 1) * 256, :] for k in range(9)),
        )
        branch = joint * full_of(v.slope_j[b])
        low = full_of(half_of(edge_rows(v, branch[:, 0:128], WIDE)))
        high = full_of(half_of(edge_rows(v, branch[:, 128:256], WIDE)))
        spread_rows(v, 0, (low, high), 896, v.hx_j.at[b], 0, 256, True)
        return carry

    lax.fori_loop(0, BATCH, image, 0)


def branch_own(v, b, low=0, high=256):
    return v.hx_j[b, 128:768, 256 + low : 256 + high]


def flow_back(v):
    def image(b, carry):
        rows = [slice((2 - a) * 128, (2 - a) * 128 + 640) for a in range(3)]
        flow_grad = nt(
            join(v.hx_j[b, rows[a], c * 256 + 128 : (c + 1) * 256] for a in range(3) for c in range(3)),
            join(v.w_fm[k * 128 : (k + 1) * 128, :] for k in range(9)),
        )
        v.fpg[b] = half_of(flow_grad * full_of(v.slope_fi[b]))
        z = nt(v.w_fi[...], v.fpg[b])
        total = jnp.zeros((32, LANES), jnp.float32)
        lane = lane_index((32, LANES))
        for across in range(7):
            v.fs[across] = jnp.zeros((32, LANES), jnp.float32)
            for y in range(ROWS):
                v.fs[across, 2 * y : 2 * y + 16, :] += z[across * 16 : across * 16 + 16, y * 128 : (y + 1) * 128]
            d = across - 3
            value = v.fs[across]
            if d:
                value = pltpu.roll(value, d % LANES, 1)
                value = jnp.where((lane - d >= 0) & (lane - d < WIDE), value, 0.0)
            total = total + value
        v.gf[b] = total
        return carry

    lax.fori_loop(0, BATCH, image, 0)
    v.halo_gf.start()


def corr_back(v):
    def image(b, carry):
        corr_grad = nt(
            join(v.hx_j[b, (2 - a) * 128 : (2 - a) * 128 + 640, :] for a in range(3)),
            join(v.w_cm[k * 256 : (k + 1) * 256, :] for k in range(9)),
        )
        v.cpg[b] = half_of(corr_grad * full_of(v.slope_ci[b]))
        stores = gcorr_stores(v, b)
        for store in stores:
            pl.when(b > 0)(store.wait)
        gcorr = nt(v.w_ci[...], v.cpg[b])
        for y in range(ROWS):
            v.mm_tmp[y * 328 : y * 328 + CORR, :] = gcorr[:, y * WIDE : (y + 1) * WIDE]
        for store in stores:
            store.start()
        return carry

    lax.fori_loop(0, BATCH, image, 0)


def summed(v, ref, name):
    total = 0.0
    for b in range(BATCH):
        total = total + ones_sum(ref(b))
    keep_bias(v, name, total)


def gradients_motion(v):
    starts = flat_rows()[0]
    summed(v, lambda b: v.mge[b, 256:896, :], MOTION_MIX)
    grads = join((v.mge[b, 256:896, :] for b in range(BATCH)), 0)
    for a in range(3):
        taps = join((v.hx_j[b, a * 128 : a * 128 + 640, :] for b in range(BATCH)), 0)
        v.mm_tmp[a * 768 : (a + 1) * 768, :] = tn(taps, grads)
    lane36 = lane_index((36, LANES))
    for r in range(63):
        first = v.mm_tmp[pl.ds(r, 36, stride=64), :]
        second = v.mm_tmp[pl.ds(r + 1, 36, stride=64), :]
        if r:
            first = pltpu.roll(first, LANES - 2 * r, 1)
        second = pltpu.roll(second, 126 - 2 * r, 1)
        v.flat[pl.ds(MARGIN + r, 36, stride=63), :] = jnp.where(lane36 < 126 - 2 * r, first, second)
    v.flush.layer(starts[MOTION_MIX], 2268)


def gradients_branches(v):
    starts = flat_rows()[0]
    summed(v, lambda b: branch_own(v, b), CORR_MIX)
    summed(v, lambda b: branch_own(v, b, 128, 256), FLOW_MIX)
    grads = join((branch_own(v, b, 128, 256) for b in range(BATCH)), 0)
    for k in range(9):
        a, c = k // 3, k % 3
        if c == 0:
            taps = join((v.hx_f[b, (a + 1) * 128 : (a + 1) * 128 + 640, :] for b in range(BATCH)), 0)
            group = tn(taps, grads)
        v.pair_a[0:128, :] = group[c * 128 : (c + 1) * 128]
        even, odd = (v.pair_a[pl.ds(i, 64, stride=2), :] for i in range(2))
        v.flat[MARGIN + 64 * k : MARGIN + 64 * (k + 1), :] = jnp.where(
            lane_index((64, LANES)) < 64, pltpu.roll(even, 64, 1), odd
        )
    v.flush.layer(starts[FLOW_MIX], 576)

    low_half = lane_index((128, LANES)) < 64
    grads = join((branch_own(v, b) for b in range(BATCH)), 0)
    for k in range(9):
        a, c = k // 3, k % 3
        if c == 0:
            taps = join((v.hx_c[b, (a + 1) * 128 : (a + 1) * 128 + 640, :] for b in range(BATCH)), 0)
            group = tn(taps, grads)
        v.pair_a[...] = group[c * 256 : (c + 1) * 256, 0:128]
        v.pair_b[...] = group[c * 256 : (c + 1) * 256, 128:256]
        even, odd = (v.pair_a[pl.ds(i, 128, stride=2), :] for i in range(2))
        even_high, odd_high = (v.pair_b[pl.ds(i, 128, stride=2), :] for i in range(2))
        odd, odd_high = pltpu.roll(odd, 64, 1), pltpu.roll(odd_high, 64, 1)
        at = MARGIN + 384 * k
        v.flat[pl.ds(at, 128, stride=3), :] = even
        v.flat[pl.ds(at + 1, 128, stride=3), :] = jnp.where(low_half, even_high, odd)
        v.flat[pl.ds(at + 2, 128, stride=3), :] = jnp.where(low_half, odd, odd_high)
        if k == 4:
            v.reduce.tick()
    v.flush.layer(starts[CORR_MIX], 3456)


def gradients_flow_in(v):
    starts = flat_rows()[0]
    summed(v, lambda b: v.fpg[b], FLOW_IN)
    value = 0.0
    for b in range(BATCH):
        value = value + mm(v.xt[b, :, 256:896], v.fpg[b])
    v.flow_tmp[...] = value
    for across in range(7):
        for comp in range(2):
            v.flat[pl.ds(MARGIN + across * 2 + comp, 7, stride=14), :] = v.flow_tmp[
                pl.ds(across * 16 + comp, 7, stride=2), :
            ]
    v.flush.layer(starts[FLOW_IN], 98)


def gradients_corr_in(v):
    starts = flat_rows()[0]
    summed(v, lambda b: v.cpg[b], CORR_IN)
    value = 0.0
    for b in range(BATCH):
        value = value + mm(lines_of(v.corr, b, ROWS), v.cpg[b])
    pack_pairs(v.flat, 0, 324, value[:, 0:128], value[:, 128:256])
    v.flush.layer(starts[CORR_IN], 648)


def bias_tile(v):
    starts, bias_row, spots, inner = flat_rows()
    lead = bias_row % 16
    lane1 = lane_index((1, LANES))
    v.bown[...] = jnp.zeros_like(v.bown)
    for name, height, width in shapes():
        for block in range(-(-width // LANES)):
            value = v.gbias[BIAS_AT[name] + block : BIAS_AT[name] + block + 1, :]
            if name == FLOW_MIX:
                value = pltpu.roll(value, 64, 1)
            left = width - block * LANES
            if left < LANES:
                value = jnp.where(lane1 < left, value, 0.0)
            at = spots[name] + block * LANES
            row, shift = lead + at // LANES, at % LANES
            moved = pltpu.roll(value, shift, 1) if shift else value
            v.bown[row : row + 1, :] = v.bown[row : row + 1, :] + jnp.where(lane1 >= shift, moved, 0.0)
            if shift:
                v.bown[row + 1 : row + 2, :] = v.bown[row + 1 : row + 2, :] + jnp.where(lane1 < shift, moved, 0.0)


def finish(v):
    spot, last = v.spot, v.space - 1
    v.halo_gf.receive()
    for b in range(BATCH):
        v.tmp2[...] = v.gf[b]
        up = jnp.where(spot > 0, v.gf_up[b], 0.0)
        down = jnp.where(spot < last, v.gf_down[b], 0.0)
        v.tmp2[6:12, :] += up[16:22, :]
        v.tmp2[10:16, :] += down[0:6, :]
        for y in range(ROWS):
            v.out_gflow[b, 2 * y : 2 * y + 2, :] = (
                v.tmp2[6 + 2 * y : 8 + 2 * y, :] + v.gf_base[b, 0:2, y * 128 : (y + 1) * 128]
            )
    v.loss_in[v.spot] = v.losses[...]
    total = jnp.sum(v.loss_in[...], axis=0)
    counts = jnp.sum(v.counts[...], axis=0)
    v.out_loss[...] = total / jnp.maximum(counts, 1.0)


class View:
    pass


def main_kernel(names, space, count, *refs):
    v = View()
    for name, ref in zip(names, refs):
        setattr(v, name, ref)
    v.space = space
    v.lu, v.lc = v.motion, v.state
    v.spot = lax.axis_index(SPACE)
    v.rank = lax.axis_index(DP)
    v.mate, v.other, v.twin = mate_of(v.rank), lax.rem(v.rank + 2, 4), mate_of(v.spot)
    spot = v.spot
    barrier = pltpu.get_barrier_semaphore()

    def hello(step, carry):
        pl.semaphore_signal(barrier, inc=1, device_id={SPACE: lax.rem(spot + step, space)}, device_id_type=MESH)
        return carry

    lax.fori_loop(1, space, hello, 0)
    for turn in range(1, 4):

        def greet_rank(step, carry):
            place = lax.rem(spot + 2 * step, space)
            device = {DP: lax.rem(v.rank + turn, 4), SPACE: place}
            pl.semaphore_signal(barrier, inc=1, device_id=device, device_id_type=MESH)
            return carry

        lax.fori_loop(0, space // 2, greet_rank, 0)
    pl.semaphore_wait(barrier, space - 1 + 3 * (space // 2))

    v.store_gnet = pltpu.make_async_copy(v.ru, v.out_gnet, v.osem.at[0])
    v.store_gctx = pltpu.make_async_copy(v.rr, v.out_gctx, v.osem.at[1])
    rows = row_index((8, LANES))
    counted = jnp.zeros((8, LANES), jnp.float32)
    for b in range(BATCH):
        counted = jnp.where(rows == b, jnp.sum(v.valid[b, 0:1, :]), counted)
    v.count_out[...] = counted
    v.pick_count = lambda counts, b: jnp.sum(jnp.where((rows == b) & (lane_index((8, LANES)) == 0), counts, 0.0))
    v.swap_count = Swap(v, 0, v.count_out, v.counts, True)
    v.swap_context = Swap(v, 1, v.a_context, v.b_context)
    v.swap_motion = Swap(v, 2, v.a_motion, v.b_motion)
    v.swap_state = Swap(v, 3, v.a_state, v.b_state)
    v.back_context = Swap(v, 4, v.a_context, v.b_context)
    v.back_motion = Swap(v, 5, v.a_motion, v.b_motion)
    v.back_state = Swap(v, 6, v.a_state, v.b_state)
    v.swap_loss = Swap(v, 7, v.losses, v.loss_in, True)
    v.halo_corr = Halo(v, 0, v.corr.at[:, 0:2], v.corr.at[:, 3:5], v.corr_down, v.corr_up)
    v.halo_flow = Halo(v, 1, v.flow, v.flow, v.flow_down, v.flow_up)
    v.halo_final = Halo(v, 2, v.e_left, v.e_right, v.f_right, v.f_left)
    v.halo_mask = Halo(v, 3, v.m_left, v.m_right, v.n_right, v.n_left)
    v.halo_dg = Halo(v, 4, v.dg, v.dg, v.dg_right, v.dg_left)
    v.halo_mg = Halo(v, 5, v.mge.at[:, 256:512], v.mge.at[:, 640:896], v.mge.at[:, 896:1152], v.mge.at[:, 0:256])
    v.halo_gf = Halo(v, 6, v.gf, v.gf, v.gf_down, v.gf_up)

    load = pltpu.make_async_copy(v.local, v.gath.at[0:BLOCK], v.gsend.at[4, 2])
    load.start()
    v.halo_flow.start()
    v.halo_corr.start()
    v.swap_count.start()
    load.wait()
    gather_start(v, count)

    def first(b, carry):
        v.state[b] = full_of(v.context[b])
        pack_rows(v, v.state, b, v.a_context)
        return carry

    lax.fori_loop(0, BATCH, first, 0)
    v.swap_context.start()
    v.halo_flow.receive()
    gather_pass(v, 0, 2)
    early_taps(v)
    gather_pass(v, 2, 4)
    columns_zero(v)
    gather_end(v)
    unpack_encoder(v, count)
    v.halo_corr.receive()
    forward_rows(v)
    keep = [pltpu.make_async_copy(v.hx_c, v.out_keep_c, v.ksem.at[0]), pltpu.make_async_copy(v.hx_f, v.out_keep_f, v.ksem.at[1])]
    for copy in keep:
        copy.start()
    unpack_heads(v)
    mask_gradient(v)
    v.swap_context.receive()
    v.swap_motion.receive()
    v.swap_state.receive()
    take_own(v, v.a_context, v.b_context)
    take_own(v, v.a_motion, v.b_motion)
    take_own(v, v.a_state, v.b_state)
    columns_in(v)
    columns_forward(v)
    for copy in keep:
        copy.wait()
    heads(v)
    mask_output(v)
    v.swap_context.sent()
    v.swap_motion.sent()
    v.swap_state.sent()
    heads_back(v)
    v.flush = Flush(v)
    red = v.reduce = Reduce(v, count)
    gradients_heads(v)
    v.back_context.start()
    v.back_motion.start()
    red.offer(0)
    red.tick()
    gradients_gru(
        v,
        COLUMNS_GATES,
        COLUMNS_CANDIDATE,
        lambda t: (
            lambda b: v.xc[b, t * COLS : t * COLS + AREA, 0:128],
            lambda b: v.xc[b, t * COLS : t * COLS + AREA, 128:384],
            lambda b: v.xcr[b, t * COLS : t * COLS + AREA, :],
        ),
        lambda b, low=0, high=384: v.gc[b, 32 : 32 + AREA, low:high],
    )
    red.offer(1, 2)
    red.tick()
    rows_back(v)
    red.tick()
    keep = [
        pltpu.make_async_copy(v.out_keep_c, v.hx_c, v.ksem.at[0]),
        pltpu.make_async_copy(v.out_keep_f, v.hx_f, v.ksem.at[1]),
    ]
    for copy in keep:
        copy.start()
    gradients_gru(
        v,
        ROWS_GATES,
        ROWS_CANDIDATE,
        lambda t: (
            lambda b: v.xs[b * AREA : (b + 1) * AREA, t * 128 : (t + 1) * 128],
            lambda b: v.xi[b * AREA : (b + 1) * AREA, t * 256 : (t + 1) * 256],
            lambda b: v.xr[b * AREA : (b + 1) * AREA, t * 128 : (t + 1) * 128],
        ),
        lambda b, low=0, high=384: v.gr[b, :, low:high],
    )
    red.offer(3, 4)
    red.tick()
    gradients_motion(v)
    red.offer(5)
    red.tick()
    branch_back(v)
    red.tick()
    for copy in keep:
        copy.wait()
    gradients_branches(v)
    red.offer(6)
    red.tick()
    flow_back(v)
    red.tick()
    gradients_flow_in(v)
    red.offer(7)
    red.tick()
    corr_back(v)
    red.tick()
    gradients_corr_in(v)
    bias_tile(v)
    red.bias_core()
    red.offer(8)
    red.tick()
    for store in gcorr_stores(v, 0):
        store.wait()
    finish(v)
    red.bias_across()
    red.tick()
    red.bias_stripes()
    pl.when(v.rank == 0)(lambda: red.lay(4, 15))
    red.tick()
    red.bias_end()
    red.ready()
    pl.when(v.rank > 0)(lambda: red.lay(0, 24))
    red.tick()
    pl.when(v.rank == 0)(lambda: red.lay(15, 24))
    red.tick()
    assert not red.flying and not red.queue
    pl.when(v.rank == 0)(lambda: red.lay(0, 4))
    red.settle()
    for swap in (v.swap_count, v.back_context, v.back_motion, v.back_state, v.swap_loss):
        swap.sent()
    for halo in (v.halo_corr, v.halo_flow, v.halo_final, v.halo_mask, v.halo_dg, v.halo_mg, v.halo_gf):
        halo.sent()
    v.store_gnet.wait()
    v.store_gctx.wait()
    pltpu.make_async_copy(v.mask_low, v.out_mask.at[0], v.osem.at[3]).wait()


def main_call(space, count, local, net, context, corr, flow, target, valid, grad_net, grad_mask):
    total = 3 * count // (LANES * 16) * 16 + BLOCK
    low, wide = jnp.bfloat16, jnp.float32
    peers = (space, BATCH, ROWS * COLS, LANES)
    ins = dict(
        local=local, net=net, context=context, corr=corr, flow=flow, target=target, valid=valid,
        grad_net=grad_net, grad_mask=grad_mask,
    )
    outs = dict(
        out_net=((BATCH, AREA, 128), low),
        out_flow=((BATCH, 8, SPAN), wide),
        out_mask=((BATCH, AREA, MASK), low),
        out_loss=((8, 128), wide),
        out_flat=((total, 128), low),
        out_gnet=((BATCH, AREA, 128), wide),
        out_gctx=((BATCH, AREA, 128), wide),
        out_gcorr=((BATCH, ROWS, CORR, 128), wide),
        out_gflow=((BATCH, 16, 128), wide),
        out_keep_c=((BATCH, 1152, 768), low),
        out_keep_f=((BATCH, 1152, 384), low),
        out_all=((4 * BLOCK, 128), low),
        out_grads=((BLOCK, 128), wide),
    )
    scratch = dict(
        stage=((2, 3904, 128), low),
        seam=((16, 16, 128), wide),
        mask_low=((AREA, MASK), low),
        seam_low=((16 * 20, 128), low),
        own=((2, SHARE // 2, 128), low),
        rcore=((2, SHARE // 2, 128), low),
        tx=((2, SHARE // 4, 128), low),
        rx=((2, SHARE // 4, 128), low),
        ks=((2, SHARE // 4, 128), wide),
        ts=((2, SHARE // 4, 128), low),
        acc=((2, SHARE // 4 // space, 128), wide),
        rs=((2, space, SHARE // 4 // space, 128), low),
        fin=((2, SHARE // 4 // space, 128), low),
        dall=((4, 256, 128), low),
        ty=((2, SHARE // 8, 128), low),
        ry=((2, SHARE // 8, 128), low),
        ky=((2, SHARE // 8, 128), wide),
        tz=((2, SHARE // 8, 128), low),
        rz=((2, space // 2, SHARE // 4 // space, 128), low),
        kz=((2, SHARE // 4 // space, 128), wide),
        az=((3, SHARE // 8, 128), low),
        gath=((2 * SHARE + 32, 128), low),
        bown=((32, 128), wide), bcore=((32, 128), wide), btwo=((32, 128), wide), bacross=((32, 128), wide),
        bfour=((32, 128), wide), ball=((space, 32, 128), wide), bsum=((32, 128), wide),
        flat=((3904, 128), wide),
        pair_a=((256, 128), wide),
        pair_b=((256, 128), wide),
        flow_tmp=((112, 128), wide),
        mm_tmp=((3 * (2 * EDGE + SPREAD), 128), wide),
        fo_tmp=((32, 128), wide),
        fo_tmp2=((32, 128), wide),
        w_ci=((CORR, 256), low),
        w_cm=((2304, 256), low),
        w_fi=((112, 128), low),
        w_fm=((1152, 128), low),
        w_mm=((2304, 128), low),
        w_ri=((1280, 384), low),
        w_rs=((640, 384), low),
        w_li=((1280, 384), low),
        w_ls=((640, 384), low),
        w_h=((1152, 512), low),
        w_fo=((32, 256), low),
        w_mo=((256, 640), low),
        bias=((BIAS_ROWS, 128), wide),
        gbias=((BIAS_ROWS, 128), wide),
        corr_up=((BATCH, 2, CORR, 128), low),
        corr_down=((BATCH, 2, CORR, 128), low),
        flow_up=((BATCH, 16, 128), wide),
        flow_down=((BATCH, 16, 128), wide),
        fs=((7, 32, 128), wide),
        xt=((BATCH, 112, 1152), low),
        tmp=((1168, 128), wide),
        tmp2=((32, 128), wide),
        hx_c=((BATCH, 1152, 768), low),
        hx_f=((BATCH, 1152, 384), low),
        hx_j=((BATCH, 896, 768), low),
        slope_ci=((BATCH, AREA, 256), low),
        slope_fi=((BATCH, AREA, 128), low),
        slope_j=((BATCH, 896, 256), low),
        slope_m=((BATCH, AREA, 128), low),
        motion=((BATCH, AREA, 128), wide),
        state=((BATCH, AREA, 128), wide),
        xi=((BATCH * AREA, 1280), low),
        xs=((BATCH * AREA, 640), low),
        xr=((BATCH * AREA, 640), low),
        ru=((BATCH, AREA, 128), wide),
        rr=((BATCH, AREA, 128), wide),
        rc=((BATCH, AREA, 128), wide),
        lr=((BATCH, AREA, 128), wide),
        a_state=(peers, low), a_context=(peers, low), a_motion=(peers, low),
        b_state=(peers, low), b_context=(peers, low), b_motion=(peers, low),
        xc=((BATCH, AREA + 64, 384), low),
        xcr=((BATCH, AREA + 64, 128), low),
        gc=((BATCH, AREA + 64, 384), low),
        final=((AREA, 128), wide),
        e_left=((BATCH, 2, 48, 128), low), e_right=((BATCH, 2, 48, 128), low),
        f_left=((BATCH, 2, 48, 128), low), f_right=((BATCH, 2, 48, 128), low),
        m_left=((BATCH, 2, 48, 128), low), m_right=((BATCH, 2, 48, 128), low),
        n_left=((BATCH, 2, 48, 128), low), n_right=((BATCH, 2, 48, 128), low),
        slope_h=((BATCH, SPREAD, 512), low),
        feat=((BATCH, SPAN, 256), low),
        mf=((BATCH, AREA, 256), low),
        zt=((32, SPAN), wide),
        dg=((BATCH, 8, SPAN), wide),
        dg_left=((BATCH, 8, SPAN), wide), dg_right=((BATCH, 8, SPAN), wide),
        dt=((32, SPAN), wide),
        dto=((32, SPAN), wide),
        dtb=((BATCH, 32, SPAN), low),
        hgo=((BATCH, SPREAD, 512), low),
        gr=((BATCH, AREA, 384), low),
        mge=((BATCH, 1152, 128), low),
        cpg=((BATCH, AREA, 256), low),
        fpg=((BATCH, AREA, 128), low),
        gf_base=((BATCH, 8, AREA), wide),
        gf=((BATCH, 32, 128), wide), gf_up=((BATCH, 32, 128), wide), gf_down=((BATCH, 32, 128), wide),
        count_out=((8, 128), wide), counts=((space, 8, 128), wide),
        losses=((8, 128), wide), loss_in=((space, 8, 128), wide),
    )
    sems = dict(
        hsend=pltpu.SemaphoreType.DMA((7, 2)), hrecv=pltpu.SemaphoreType.DMA((7, 2)),
        asend=pltpu.SemaphoreType.DMA((9,)), arecv=pltpu.SemaphoreType.DMA((9,)),
        ssem=pltpu.SemaphoreType.DMA((2, 2)),
        fsem=pltpu.SemaphoreType.DMA((17,)),
        rsend=pltpu.SemaphoreType.DMA((3, 2)), rrecv=pltpu.SemaphoreType.DMA((3, 2)),
        z1send=pltpu.SemaphoreType.DMA((2,)), z1recv=pltpu.SemaphoreType.DMA((2,)),
        z2send=pltpu.SemaphoreType.DMA((3,)), z2recv=pltpu.SemaphoreType.DMA((3,)),
        osend=pltpu.SemaphoreType.DMA((3,)), orecv=pltpu.SemaphoreType.DMA((9,)),
        rlocal=pltpu.SemaphoreType.DMA((2,)),
        s2send=pltpu.SemaphoreType.DMA((2,)), s2recv=pltpu.SemaphoreType.DMA((2,)),
        fsend=pltpu.SemaphoreType.DMA((2,)), frecv=pltpu.SemaphoreType.DMA((9,)),
        ysend=pltpu.SemaphoreType.DMA((9,)), yrecv=pltpu.SemaphoreType.DMA((9,)),
        dsend=pltpu.SemaphoreType.DMA, drecv=pltpu.SemaphoreType.DMA,
        bsend=pltpu.SemaphoreType.DMA((2,)), brecv=pltpu.SemaphoreType.DMA((2,)),
        ksem=pltpu.SemaphoreType.DMA((2,)),
        gsend=pltpu.SemaphoreType.DMA((5, 4)), grecv=pltpu.SemaphoreType.DMA((5, 4)),
        gsem=pltpu.SemaphoreType.DMA((ROWS,)),
        osem=pltpu.SemaphoreType.DMA((6,)),
    )
    vmem = pl.BlockSpec(memory_space=pltpu.VMEM)
    hbm = pl.BlockSpec(memory_space=pl.ANY)
    names = list(ins) + list(outs) + list(scratch) + list(sems)
    return pl.pallas_call(
        functools.partial(main_kernel, names, space, count),
        out_shape=[jax.ShapeDtypeStruct(*entry) for entry in outs.values()],
        in_specs=[hbm if name == "local" else vmem for name in ins],
        out_specs=[hbm if name in ("out_flat", "out_gnet", "out_gctx", "out_gcorr", "out_keep_c", "out_keep_f", "out_mask", "out_grads", "out_all") else vmem for name in outs],
        scratch_shapes=[pltpu.VMEM(*entry) for entry in scratch.values()] + list(sems.values()),
        compiler_params=pltpu.CompilerParams(
            collective_id=2, has_side_effects=True, vmem_limit_bytes=VMEM_LIMIT
        ),
    )(*ins.values())


VMEM_LIMIT = 64 * 2**20 - 2**17


def shards_wide(net, context, corr, flow, target, valid, grad_net, grad_mask, params):
    space = lax.axis_size(SPACE)
    count = params.shape[0]
    local = jnp.pad(params, (0, BLOCK * LANES - count)).reshape(BLOCK, LANES)
    flow_rows = jnp.transpose(flow.astype(jnp.float32), (0, 2, 1, 3)).reshape(BATCH, 2 * ROWS, WIDE)
    flow_rows = jnp.pad(flow_rows, ((0, 0), (0, 16 - 2 * ROWS), (0, 0)))
    pad = ((0, 0), (0, 0), (0, 0), (2, 2))
    target_ext = jnp.pad(target, pad).reshape(BATCH, 2, SPREAD)
    target_ext = jnp.pad(target_ext, ((0, 0), (0, 6), (0, SPAN - SPREAD)))
    valid_ext = jnp.pad(valid.astype(jnp.float32)[:, None], pad).reshape(BATCH, 1, SPREAD)
    valid_ext = jnp.broadcast_to(jnp.pad(valid_ext, ((0, 0), (0, 0), (0, SPAN - SPREAD))), (BATCH, 8, SPAN))
    outs = main_call(
        space, count, local, net.reshape(BATCH, AREA, HID), context.reshape(BATCH, AREA, CTX),
        jnp.transpose(corr, (0, 1, 3, 2)), flow_rows, target_ext, valid_ext,
        grad_net.reshape(BATCH, AREA, HID), grad_mask.reshape(BATCH, AREA, MASK),
    )
    new_net, new_flow, mask, loss, _, gnet, gctx, gcorr, gflow = outs[:9]
    new_flow = new_flow[:, 0:2, 0:SPREAD].reshape(BATCH, 2, TALL, PITCH)[..., 2 : 2 + COLS]
    grads = outs[-1].reshape(-1)[:count]
    return (
        new_net.reshape(BATCH, TALL, COLS, HID),
        new_flow,
        mask.reshape(BATCH, TALL, COLS, MASK),
        loss[0:BATCH, 0],
        grads,
        gnet.reshape(BATCH, ROWS, WIDE, HID),
        gctx.reshape(BATCH, ROWS, WIDE, CTX),
        jnp.transpose(gcorr, (0, 1, 3, 2)),
        jnp.transpose(gflow[:, 0 : 2 * ROWS].reshape(BATCH, ROWS, 2, WIDE), (0, 2, 1, 3)),
    )


def solution(mesh):
    def plan(*arrays):
        net, valid = arrays[0], arrays[5]
        if (net.shape[1:3], valid.shape[1:]) == ((ROWS, WIDE), (TALL, COLS)):
            return shards_wide(*arrays)
        return shards(*arrays)

    return jax.shard_map(
        plan,
        mesh=mesh,
        in_specs=(
            P(DP, SPACE, None, None),
            P(DP, SPACE, None, None),
            P(DP, SPACE, None, None),
            P(DP, None, SPACE, None),
            P(DP, None, None, SPACE),
            P(DP, None, SPACE),
            P(DP, None, SPACE, None),
            P(DP, None, SPACE, None),
            P(DP),
        ),
        out_specs=(
            P(DP, None, SPACE, None),
            P(DP, None, None, SPACE),
            P(DP, None, SPACE, None),
            P(DP),
            P(DP),
            P(DP, SPACE, None, None),
            P(DP, SPACE, None, None),
            P(DP, SPACE, None, None),
            P(DP, None, SPACE, None),
        ),
        check_vma=False,
    )
```

```python
import functools

import jax
import jax.numpy as jnp
from jax import lax
from jax.experimental import pallas as pl
from jax.experimental.pallas import tpu as pltpu
from jax.sharding import PartitionSpec as P

HID = 128
CTX = 128
MOT = 128
CORR = 324
SPACE = "space"
DP = "dp"
(
    CORR_IN,
    CORR_MIX,
    FLOW_IN,
    FLOW_MIX,
    MOTION_MIX,
    ROWS_GATES,
    ROWS_CANDIDATE,
    COLUMNS_GATES,
    COLUMNS_CANDIDATE,
    FLOW_HIDDEN,
    FLOW_OUT,
    MASK_HIDDEN,
    MASK_OUT,
) = range(13)
C1 = 256
C2 = 192
F1 = 128
F2 = 64
HEAD = 256
MASK = 576


def with_halo(block, sides, width):
    for axis, dim in sides:
        count = lax.axis_size(axis)
        forward = [(i, i + 1) for i in range(count - 1)]
        backward = [(target, source) for source, target in forward]
        low = lax.ppermute(
            lax.slice_in_dim(block, block.shape[dim] - width, None, axis=dim), axis, forward
        )
        high = lax.ppermute(lax.slice_in_dim(block, 0, width, axis=dim), axis, backward)
        block = jnp.concatenate([low, block, high], axis=dim)
    return block


def shapes():
    inputs_width = HID + CTX + MOT
    return [
        (CORR_IN, CORR, C1),
        (CORR_MIX, 9 * C1, C2),
        (FLOW_IN, 98, F1),
        (FLOW_MIX, 9 * F1, F2),
        (MOTION_MIX, 9 * (C2 + F2), MOT - 2),
        (ROWS_GATES, 5 * inputs_width, 2 * HID),
        (ROWS_CANDIDATE, 5 * inputs_width, HID),
        (COLUMNS_GATES, 5 * inputs_width, 2 * HID),
        (COLUMNS_CANDIDATE, 5 * inputs_width, HID),
        (FLOW_HIDDEN, 9 * HID, HEAD),
        (FLOW_OUT, 9 * HEAD, 2),
        (MASK_HIDDEN, 9 * HID, HEAD),
        (MASK_OUT, HEAD, MASK),
    ]


def unpack(flat):
    weights = {}
    biases = {}
    offset = 0
    table = shapes()
    for name, height, width in table:
        weights[name] = flat[offset // LANES : (offset + height * width) // LANES].reshape(height, width)
        offset = offset + height * width
    rest = flat[offset // LANES :].reshape(-1)
    offset = 0
    for name, height, width in table:
        biases[name] = rest[offset : offset + width].astype(jnp.float32)
        offset = offset + width
    return (weights, biases)


def pack(grads, total):
    table = shapes()
    rows = [grads[entry[0]][0].astype(jnp.bfloat16).reshape(-1, LANES) for entry in table]
    biases = jnp.concatenate([grads[entry[0]][1] for entry in table]).astype(jnp.bfloat16)
    left = total * LANES - sum(entry[1] * entry[2] for entry in table) - biases.shape[0]
    return jnp.concatenate(rows + [jnp.pad(biases, (0, left)).reshape(-1, LANES)])


def patches(padded, tall, wide):
    out_rows = padded.shape[1] - tall + 1
    out_columns = padded.shape[2] - wide + 1
    return jnp.concatenate(
        [
            padded[:, down : down + out_rows, across : across + out_columns]
            for down in range(tall)
            for across in range(wide)
        ],
        axis=-1,
    )


def apply(stacked, weight):
    return jnp.einsum("bhwk,ko->bhwo", stacked, weight, preferred_element_type=jnp.float32)


def apply_back(grad, weight):
    return jnp.einsum("bhwo,ko->bhwk", grad, weight, preferred_element_type=jnp.float32)


def weight_grad(stacked, pre_grad):
    return jnp.einsum("bhwk,bhwo->ko", stacked, pre_grad, preferred_element_type=jnp.float32)


def record(grads, name, stacked, pre_grad):
    grads[name] = (
        weight_grad(stacked, pre_grad),
        jnp.sum(pre_grad, axis=(0, 1, 2), dtype=jnp.float32),
    )


def flipped(weight, tall, wide):
    inner = weight.shape[0] // (tall * wide)
    shaped = weight.reshape(tall, wide, inner, weight.shape[1])[::-1, ::-1]
    return jnp.transpose(shaped, (0, 1, 3, 2)).reshape(-1, inner)


def slope(pre):
    sigma = jax.nn.sigmoid(pre)
    return sigma * (1.0 + pre * (1.0 - sigma))


def local_pad(field, tall, wide):
    return jnp.pad(field, ((0, 0), (tall // 2, tall // 2), (wide // 2, wide // 2), (0, 0)))


def row_pad(field, tall):
    field = with_halo(field, ((SPACE, 1),), tall // 2)
    return jnp.pad(field, ((0, 0), (0, 0), (tall // 2, tall // 2), (0, 0)))


def column_pad(field, tall, wide):
    field = with_halo(field, ((SPACE, 2),), wide // 2)
    return jnp.pad(field, ((0, 0), (tall // 2, tall // 2), (0, 0), (0, 0)))


MESH = pl.DeviceIdType.MESH
LANES = 128
BLOCK = 6144


def quarter_start(rank, count):
    return lax.div(rank * count, LANES)


def quarter_base(rank, count):
    return lax.div(rank * count, LANES * 16) * 16


def mate_of(rank):
    return rank + 1 - 2 * lax.rem(rank, 2)


def remote(src, dst, send, recv, device):
    return pltpu.make_async_remote_copy(
        src_ref=src, dst_ref=dst, send_sem=send, recv_sem=recv, device_id=device, device_id_type=MESH
    )


def greet(devices):
    barrier = pltpu.get_barrier_semaphore()
    for device in devices:
        pl.semaphore_signal(barrier, inc=1, device_id=device, device_id_type=MESH)
    pl.semaphore_wait(barrier, len(devices))


def lane_matrix(shift, forward):
    source = lax.broadcasted_iota(jnp.int32, (LANES, 2 * LANES), 0)
    target = lax.broadcasted_iota(jnp.int32, (LANES, 2 * LANES), 1)
    if forward:
        return jnp.where(target == source + shift, 1.0, 0.0).astype(jnp.bfloat16)
    return jnp.where(lax.rem(target + LANES, 2 * LANES) == source - shift + LANES, 1.0, 0.0).astype(jnp.bfloat16)


def gather_kernel(count, local_ref, out_ref, own_ref, send, recv):
    rank, spot = lax.axis_index(DP), lax.axis_index(SPACE)
    mate, across, twin = mate_of(rank), lax.rem(rank + 2, 4), mate_of(spot)
    pieces = 4
    rows = BLOCK // 2 // pieces
    peers = ({DP: mate}, {DP: across}, {SPACE: twin})
    greet(peers)
    matrix = lane_matrix(lax.rem(rank * count, LANES), True)
    first = lax.broadcasted_iota(jnp.int32, (256, LANES), 0) == 0

    def rotate(step, carry):
        at = pl.ds(pl.multiple_of(step * 256, 256), 256)
        both = jnp.dot(local_ref[at, :], matrix, preferred_element_type=jnp.float32)
        spill = pltpu.roll(both[:, LANES:], 1, 0)
        own_ref[at, :] = (both[:, :LANES] + jnp.where(first, carry, spill)).astype(jnp.bfloat16)
        return spill[0:1]

    lax.fori_loop(0, BLOCK // 256, rotate, jnp.zeros((1, LANES), jnp.float32))

    half, other_half = lax.rem(spot, 2), lax.rem(spot + 1, 2)

    def piece(which, index):
        return pl.ds(pl.multiple_of(which * (BLOCK // 2) + index * rows, 16), rows)

    own_x = [
        remote(own_ref.at[piece(half, k)], out_ref.at[rank, piece(half, k)], send.at[0, k], recv.at[0, k], peers[1])
        for k in range(pieces)
    ]
    own_c = remote(own_ref, out_ref.at[rank], send.at[4, 0], recv.at[4, 0], peers[0])
    for copy in own_x:
        copy.start()
    own_c.start()
    later = []
    for k in range(pieces):
        own_x[k].wait_recv()
        block = out_ref.at[across, piece(half, k)]
        to_twin = remote(block, block, send.at[1, k], recv.at[1, k], peers[2])
        to_mate = remote(block, block, send.at[2, k], recv.at[2, k], peers[0])
        to_twin.start()
        to_mate.start()
        later.append((to_twin, to_mate))
    for at in range(BLOCK // 256):
        out_ref[rank, at * 256 : (at + 1) * 256, :] = own_ref[at * 256 : (at + 1) * 256, :]
    for k in range(pieces):
        later[k][0].wait_recv()
        block = out_ref.at[across, piece(other_half, k)]
        to_mate = remote(block, block, send.at[3, k], recv.at[3, k], peers[0])
        to_mate.start()
        later.append((to_mate,))
    for k in range(pieces):
        own_x[k].wait_send()
        later[k][0].wait_send()
        later[k][1].wait()
        later[pieces + k][0].wait()
    own_c.wait()


def gather_blocks(params):
    count = params.shape[0]
    local = jnp.pad(params, (0, BLOCK * LANES - count)).reshape(BLOCK, LANES)
    return pl.pallas_call(
        functools.partial(gather_kernel, count),
        out_shape=jax.ShapeDtypeStruct((4, BLOCK, LANES), jnp.bfloat16),
        in_specs=[pl.BlockSpec(memory_space=pltpu.VMEM)],
        out_specs=pl.BlockSpec(memory_space=pltpu.VMEM),
        scratch_shapes=[
            pltpu.VMEM((BLOCK, LANES), jnp.bfloat16),
            pltpu.SemaphoreType.DMA((5, 4)),
            pltpu.SemaphoreType.DMA((5, 4)),
        ],
        compiler_params=pltpu.CompilerParams(
            collective_id=0, has_side_effects=True, vmem_limit_bytes=32 * 2**20
        ),
    )(local)


def gather_params(params):
    count = params.shape[0]
    blocks = gather_blocks(params)
    pieces = []
    reach = 0
    for rank in range(4):
        start = rank * count // LANES
        stop = -(-(rank + 1) * count // LANES)
        head = blocks[rank, :1] if rank == 0 else blocks[rank, :1] + pieces.pop()
        pieces += [head, blocks[rank, 1 : stop - start - 1], blocks[rank, stop - start - 1 : stop - start]]
    return jnp.concatenate(pieces)


def reduce_kernel(count, space, pieces, grads_ref, out_ref, rc, tx, rx, acc, ty, ry, tz, rz, gath, send, recv, zsend, zrecv):
    rank, spot = lax.axis_index(DP), lax.axis_index(SPACE)
    mate, across, twin = mate_of(rank), lax.rem(rank + 2, 4), mate_of(spot)
    group = space // 2
    side, depth = lax.rem(spot, 2), lax.div(spot, 2)
    rows = BLOCK // pieces
    half = rows // 2
    part = half // group

    def partner(step):
        return lax.rem(depth + step, group)

    peers = [{DP: mate}, {DP: across}, {SPACE: twin}]
    barrier = pltpu.get_barrier_semaphore()
    for device in peers:
        pl.semaphore_signal(barrier, inc=1, device_id=device, device_id_type=MESH)

    def hello(step, carry):
        pl.semaphore_signal(barrier, inc=1, device_id={SPACE: partner(step) * 2 + side}, device_id_type=MESH)
        return carry

    lax.fori_loop(1, group, hello, 0)
    pl.semaphore_wait(barrier, 3 + group - 1)

    gath[BLOCK:, :] = jnp.zeros((32, LANES), jnp.bfloat16)
    lower = lax.rem(rank, 2)
    upper = lax.div(rank, 2)

    def base(who):
        return pl.multiple_of(quarter_base(who, count), 16)

    def rows_of(start, index, length):
        return pl.ds(pl.multiple_of(start + index, 16), length)

    core = []
    for p in range(pieces):
        for high in range(2):
            copy = remote(
                grads_ref.at[rows_of(base(2 * high + 1 - lower), p * rows, rows)],
                rc.at[p, high],
                send.at[high, p],
                recv.at[high, p],
                peers[0],
            )
            copy.start()
            core.append(copy)
    step_rows = 192 if half % 192 == 0 else 16
    xs, ys, gs = [], [], []

    def z_copy(p, step):
        to = partner(step)
        return remote(
            tz.at[p, pl.ds(pl.multiple_of(to * part, 16), part)],
            rz.at[p, pl.ds(pl.multiple_of(depth * part, 16), part)],
            zsend.at[0, p, step],
            zrecv.at[0, p, step],
            {SPACE: to * 2 + side},
        )

    def home(p, which, slot):
        return pl.ds(pl.multiple_of(p * rows + which * half + slot * part, 16), part)

    def g_copy(p, step):
        block = gath.at[home(p, side, depth)]
        return remote(block, block, zsend.at[1, p, step], zrecv.at[1, p, step], {SPACE: partner(step) * 2 + side})

    def each(body):
        def run(step, carry):
            body(step)
            return carry

        lax.fori_loop(1, group, run, 0)

    def stage_core(p):
        core[2 * p].wait_recv()
        core[2 * p + 1].wait_recv()
        far = 1 - upper

        def add(step, carry):
            at = pl.multiple_of(step * step_rows, 16)
            mine = grads_ref[rows_of(base(2 * far + lower), p * rows + at, step_rows), :].astype(jnp.float32)
            tx[p, pl.ds(at, step_rows), :] = (
                mine + rc[p, far, pl.ds(at, step_rows), :].astype(jnp.float32)
            ).astype(jnp.bfloat16)
            return carry

        lax.fori_loop(0, rows // step_rows, add, 0)
        copy = remote(tx.at[p], rx.at[p], send.at[2, p], recv.at[2, p], peers[1])
        copy.start()
        xs.append(copy)

    def stage_x(p):
        xs[p].wait_recv()

        def total(at):
            return (
                grads_ref[rows_of(base(rank), p * rows + at, step_rows), :].astype(jnp.float32)
                + rc[p, upper, pl.ds(at, step_rows), :].astype(jnp.float32)
                + rx[p, pl.ds(at, step_rows), :].astype(jnp.float32)
            )

        def add(step, carry):
            at = pl.multiple_of(step * step_rows, 16)
            far = pl.multiple_of((1 - side) * half + at, 16)
            near = pl.multiple_of(side * half + at, 16)
            ty[p, pl.ds(at, step_rows), :] = total(far).astype(jnp.bfloat16)
            acc[p, pl.ds(at, step_rows), :] = total(near)
            return carry

        lax.fori_loop(0, half // step_rows, add, 0)
        copy = remote(ty.at[p], ry.at[p], send.at[3, p], recv.at[3, p], peers[2])
        copy.start()
        ys.append(copy)

    def stage_y(p):
        ys[p].wait_recv()

        def add(step, carry):
            at = pl.ds(pl.multiple_of(step * step_rows, 16), step_rows)
            value = acc[p, at, :] + ry[p, at, :].astype(jnp.float32)
            acc[p, at, :] = value
            tz[p, at, :] = value.astype(jnp.bfloat16)
            return carry

        lax.fori_loop(0, half // step_rows, add, 0)
        each(lambda step: z_copy(p, step).start())

    def stage_z(p):
        each(lambda step: z_copy(p, step).wait_recv())
        value = acc[p, pl.ds(pl.multiple_of(depth * part, 16), part), :]

        def add(step, value):
            other = lax.rem(depth + group - step, group)
            return value + rz[p, pl.ds(pl.multiple_of(other * part, 16), part), :].astype(jnp.float32)

        value = lax.fori_loop(1, group, add, value)
        gath[home(p, side, depth), :] = value.astype(jnp.bfloat16)
        each(lambda step: g_copy(p, step).start())

    def stage_zg(p):
        each(lambda step: g_copy(p, step).wait_recv())
        block = gath.at[pl.ds(pl.multiple_of(p * rows + side * half, 16), half)]
        copy = remote(block, block, send.at[4, p], recv.at[4, p], peers[2])
        copy.start()
        gs.append(copy)

    def stage_yg(p):
        gs[p].wait_recv()

    stages = [stage_core, stage_x, stage_y, stage_z, stage_zg, stage_yg]
    for tick in range(pieces + len(stages) - 1):
        for number in reversed(range(len(stages))):
            if 0 <= tick - number < pieces:
                stages[number](tick - number)

    for copy in core + xs + ys + gs:
        copy.wait_send()
    for p in range(pieces):

        def done(step):
            z_copy(p, step).wait_send()
            g_copy(p, step).wait_send()

        each(done)

    offset = rank * count - quarter_base(rank, count) * LANES
    skip = lax.div(offset, LANES)
    matrix = lane_matrix(lax.rem(offset, LANES), False)
    wide = jnp.where(
        lax.broadcasted_iota(jnp.int32, (256, 288), 1)
        == lax.broadcasted_iota(jnp.int32, (256, 288), 0) + skip,
        1.0,
        0.0,
    ).astype(jnp.bfloat16)
    wide_next = jnp.where(
        lax.broadcasted_iota(jnp.int32, (256, 288), 1)
        == lax.broadcasted_iota(jnp.int32, (256, 288), 0) + skip + 1,
        1.0,
        0.0,
    ).astype(jnp.bfloat16)

    def place(step, carry):
        at = pl.multiple_of(step * 256, 256)
        block = gath[pl.ds(at, 288), :]
        both = jnp.dot(block, matrix, preferred_element_type=jnp.float32).astype(jnp.bfloat16)
        out_ref[pl.ds(at, 256), :] = jnp.dot(wide, both[:, :LANES], preferred_element_type=jnp.float32) + jnp.dot(
            wide_next, both[:, LANES:], preferred_element_type=jnp.float32
        )
        return carry

    lax.fori_loop(0, BLOCK // 256, place, 0)


def reduce_grads(flat, space, count):
    pieces = next(k for k in (4, 2, 1) if BLOCK // (k * space) % 16 == 0)
    rows = BLOCK // pieces
    half = rows // 2
    out = pl.pallas_call(
        functools.partial(reduce_kernel, count, space, pieces),
        out_shape=jax.ShapeDtypeStruct((BLOCK, LANES), jnp.float32),
        in_specs=[pl.BlockSpec(memory_space=pltpu.VMEM)],
        out_specs=pl.BlockSpec(memory_space=pltpu.VMEM),
        scratch_shapes=[
            pltpu.VMEM((pieces, 2, rows, LANES), jnp.bfloat16),
            pltpu.VMEM((pieces, rows, LANES), jnp.bfloat16),
            pltpu.VMEM((pieces, rows, LANES), jnp.bfloat16),
            pltpu.VMEM((pieces, half, LANES), jnp.float32),
            pltpu.VMEM((pieces, half, LANES), jnp.bfloat16),
            pltpu.VMEM((pieces, half, LANES), jnp.bfloat16),
            pltpu.VMEM((pieces, half, LANES), jnp.bfloat16),
            pltpu.VMEM((pieces, half, LANES), jnp.bfloat16),
            pltpu.VMEM((BLOCK + 32, LANES), jnp.bfloat16),
            pltpu.SemaphoreType.DMA((5, pieces)),
            pltpu.SemaphoreType.DMA((5, pieces)),
            pltpu.SemaphoreType.DMA((2, pieces, space // 2)),
            pltpu.SemaphoreType.DMA((2, pieces, space // 2)),
        ],
        compiler_params=pltpu.CompilerParams(
            collective_id=1, has_side_effects=True, vmem_limit_bytes=48 * 2**20
        ),
    )(flat)
    return out.reshape(-1)[:count]


def gru_forward(state, inputs, weights, biases, gate_name, candidate_name, tall, wide, padder):
    joined_stack = patches(padder(jnp.concatenate([state, inputs], -1), tall, wide), tall, wide)
    gates = jax.nn.sigmoid(apply(joined_stack, weights[gate_name]) + biases[gate_name])
    hidden = state.shape[-1]
    update = gates[..., :hidden]
    reset = gates[..., hidden:]
    state_wide = state.astype(jnp.float32)
    mixed = jnp.concatenate([(reset * state_wide).astype(jnp.bfloat16), inputs], -1)
    mixed_stack = patches(padder(mixed, tall, wide), tall, wide)
    candidate = jnp.tanh(apply(mixed_stack, weights[candidate_name]) + biases[candidate_name])
    result = state_wide + update * (candidate - state_wide)
    return (result, (joined_stack, mixed_stack, update, reset, candidate, state_wide))


def gru_backward(result_grad, kept, weights, grads, gate_name, candidate_name, tall, wide, padder):
    joined_stack, mixed_stack, update, reset, candidate, state_wide = kept
    hidden = update.shape[-1]
    candidate_grad = (result_grad * update * (1.0 - candidate * candidate)).astype(jnp.bfloat16)
    record(grads, candidate_name, mixed_stack, candidate_grad)
    mixed_grad = apply(
        patches(padder(candidate_grad, tall, wide), tall, wide),
        flipped(weights[candidate_name], tall, wide),
    )
    reset_grad = mixed_grad[..., :hidden]
    gate_grad = jnp.concatenate(
        [
            result_grad * (candidate - state_wide) * update * (1.0 - update),
            reset_grad * state_wide * reset * (1.0 - reset),
        ],
        -1,
    ).astype(jnp.bfloat16)
    record(grads, gate_name, joined_stack, gate_grad)
    joined_grad = apply(
        patches(padder(gate_grad, tall, wide), tall, wide), flipped(weights[gate_name], tall, wide)
    )
    state_grad = result_grad * (1.0 - update) + reset_grad * reset + joined_grad[..., :hidden]
    inputs_grad = joined_grad[..., hidden:] + mixed_grad[..., hidden:]
    return (state_grad, inputs_grad)


def shards(net, context, corr, flow, target, valid, grad_net, grad_mask, params):
    flow_start = CTX + MOT - 2
    plane = jnp.float32(target.shape[2] * net.shape[2])
    counts = lax.psum(jnp.sum(valid, axis=(1, 2)).astype(jnp.float32), SPACE)
    divisor = jnp.maximum(counts, 1.0)
    weights, biases = unpack(gather_params(params))
    grads = {}
    flow_rows = jnp.transpose(flow, (0, 2, 3, 1))
    corr_pre = apply(corr, weights[CORR_IN]) + biases[CORR_IN]
    corr_one = jax.nn.silu(corr_pre).astype(jnp.bfloat16)
    corr_stack = patches(row_pad(corr_one, 3), 3, 3)
    corr_mix_pre = apply(corr_stack, weights[CORR_MIX]) + biases[CORR_MIX]
    corr_two = jax.nn.silu(corr_mix_pre).astype(jnp.bfloat16)
    flow_stack = patches(row_pad(flow_rows, 7), 7, 7)
    flow_pre = apply(flow_stack, weights[FLOW_IN]) + biases[FLOW_IN]
    flow_one = jax.nn.silu(flow_pre).astype(jnp.bfloat16)
    flow_mix_stack = patches(row_pad(flow_one, 3), 3, 3)
    flow_mix_pre = apply(flow_mix_stack, weights[FLOW_MIX]) + biases[FLOW_MIX]
    flow_two = jax.nn.silu(flow_mix_pre).astype(jnp.bfloat16)
    joint_stack = patches(row_pad(jnp.concatenate([corr_two, flow_two], -1), 3), 3, 3)
    motion_pre = apply(joint_stack, weights[MOTION_MIX]) + biases[MOTION_MIX]
    motion = jax.nn.silu(motion_pre).astype(jnp.bfloat16)
    inputs = jnp.concatenate([context, motion, flow_rows], -1)
    state, rows_kept = gru_forward(
        net, inputs, weights, biases, ROWS_GATES, ROWS_CANDIDATE, 1, 5, local_pad
    )
    state_columns, inputs_columns = (
        lax.all_to_all(
            state.astype(jnp.bfloat16), SPACE, split_axis=2, concat_axis=1, tiled=True
        ),
        lax.all_to_all(inputs, SPACE, split_axis=2, concat_axis=1, tiled=True),
    )
    target_here = jnp.transpose(target, (0, 2, 3, 1))
    valid_here = valid.astype(jnp.float32)
    net_cotangent = grad_net
    mask_cotangent = grad_mask
    final, columns_kept = gru_forward(
        state_columns,
        inputs_columns,
        weights,
        biases,
        COLUMNS_GATES,
        COLUMNS_CANDIDATE,
        5,
        1,
        local_pad,
    )
    final_low = final.astype(jnp.bfloat16)
    heads_weight = jnp.concatenate([weights[FLOW_HIDDEN], weights[MASK_HIDDEN]], 1)
    heads_bias = jnp.concatenate([biases[FLOW_HIDDEN], biases[MASK_HIDDEN]])
    net_stack = patches(column_pad(final_low, 3, 3), 3, 3)
    heads_pre = apply(net_stack, heads_weight) + heads_bias
    heads_act = jax.nn.silu(heads_pre).astype(jnp.bfloat16)
    flow_features = heads_act[..., :HEAD]
    mask_features = heads_act[..., HEAD:]
    hidden_stack = patches(column_pad(flow_features, 3, 3), 3, 3)
    delta = apply(hidden_stack, weights[FLOW_OUT]) + biases[FLOW_OUT]
    mask_full = 0.25 * (apply(mask_features, weights[MASK_OUT]) + biases[MASK_OUT])
    new_flow = inputs_columns[..., flow_start:].astype(jnp.float32) + delta
    error = new_flow - target_here
    root = jnp.sqrt(error * error + 1.0)
    partials = jnp.sum(valid_here * jnp.sum(root, axis=-1), axis=(1, 2))
    flow_grad = plane / divisor[:, None, None, None] * valid_here[..., None] * error / root
    mask_low = mask_full.astype(jnp.bfloat16)
    nets_out = final_low
    flows_out = jnp.transpose(new_flow, (0, 3, 1, 2))
    masks_out = mask_low
    delta_grad = flow_grad.astype(jnp.bfloat16)
    mask_grad = (0.25 * mask_cotangent.astype(jnp.float32)).astype(jnp.bfloat16)
    record(grads, MASK_OUT, mask_features, mask_grad)
    record(grads, FLOW_OUT, hidden_stack, delta_grad)
    from_flow = apply(
        patches(column_pad(delta_grad, 3, 3), 3, 3), flipped(weights[FLOW_OUT], 3, 3)
    )
    from_mask = apply_back(mask_grad, weights[MASK_OUT])
    heads_grad = (jnp.concatenate([from_flow, from_mask], -1) * slope(heads_pre)).astype(
        jnp.bfloat16
    )
    heads_wgrad = weight_grad(net_stack, heads_grad)
    heads_bgrad = jnp.sum(heads_grad, axis=(0, 1, 2), dtype=jnp.float32)
    grads[FLOW_HIDDEN] = (heads_wgrad[:, :HEAD], heads_bgrad[:HEAD])
    grads[MASK_HIDDEN] = (heads_wgrad[:, HEAD:], heads_bgrad[HEAD:])
    final_grad = net_cotangent.astype(jnp.float32) + apply(
        patches(column_pad(heads_grad, 3, 3), 3, 3), flipped(heads_weight, 3, 3)
    )
    state_grad_columns, inputs_grad_columns = gru_backward(
        final_grad,
        columns_kept,
        weights,
        grads,
        COLUMNS_GATES,
        COLUMNS_CANDIDATE,
        5,
        1,
        local_pad,
    )
    inputs_grad_columns = jnp.concatenate(
        [
            inputs_grad_columns[..., :flow_start],
            inputs_grad_columns[..., flow_start:] + flow_grad,
        ],
        -1,
    )
    state_back, inputs_back = (
        lax.all_to_all(
            state_grad_columns.astype(jnp.bfloat16),
            SPACE,
            split_axis=1,
            concat_axis=2,
            tiled=True,
        ),
        lax.all_to_all(
            inputs_grad_columns.astype(jnp.bfloat16),
            SPACE,
            split_axis=1,
            concat_axis=2,
            tiled=True,
        ),
    )
    net_grad, inputs_grad = gru_backward(
        state_back.astype(jnp.float32),
        rows_kept,
        weights,
        grads,
        ROWS_GATES,
        ROWS_CANDIDATE,
        1,
        5,
        local_pad,
    )
    inputs_total = inputs_grad + inputs_back.astype(jnp.float32)
    motion_grad = (inputs_total[..., CTX:flow_start] * slope(motion_pre)).astype(jnp.bfloat16)
    record(grads, MOTION_MIX, joint_stack, motion_grad)
    joint_grad = apply(
        patches(row_pad(motion_grad, 3), 3, 3), flipped(weights[MOTION_MIX], 3, 3)
    )
    branch_grad = jnp.concatenate(
        [
            joint_grad[..., :C2] * slope(corr_mix_pre),
            joint_grad[..., C2:] * slope(flow_mix_pre),
        ],
        -1,
    ).astype(jnp.bfloat16)
    record(grads, CORR_MIX, corr_stack, branch_grad[..., :C2])
    record(grads, FLOW_MIX, flow_mix_stack, branch_grad[..., C2:])
    branch_pad = row_pad(branch_grad, 3)
    corr_one_grad = apply(
        patches(branch_pad[..., :C2], 3, 3), flipped(weights[CORR_MIX], 3, 3)
    )
    flow_one_grad = apply(
        patches(branch_pad[..., C2:], 3, 3), flipped(weights[FLOW_MIX], 3, 3)
    )
    corr_pre_grad = (corr_one_grad * slope(corr_pre)).astype(jnp.bfloat16)
    flow_pre_grad = (flow_one_grad * slope(flow_pre)).astype(jnp.bfloat16)
    record(grads, CORR_IN, corr, corr_pre_grad)
    record(grads, FLOW_IN, flow_stack, flow_pre_grad)
    corr_grads = apply_back(corr_pre_grad, weights[CORR_IN])
    flow_total = inputs_total[..., flow_start:] + apply(
        patches(row_pad(flow_pre_grad, 7), 7, 7), flipped(weights[FLOW_IN], 7, 7)
    )
    flow_grads = jnp.transpose(flow_total, (0, 3, 1, 2))
    net_grads = net_grad
    context_grads = inputs_total[..., :CTX]
    count = params.shape[0]
    local = pack(grads, 3 * count // (LANES * 16) * 16 + BLOCK)
    collected = reduce_grads(local, lax.axis_size(SPACE), count)
    losses = lax.psum(partials, SPACE) / divisor
    return (
        nets_out,
        flows_out,
        masks_out,
        losses,
        collected,
        net_grads,
        context_grads,
        corr_grads,
        flow_grads,
    )


BATCH = 2
ROWS = 5
WIDE = 128
TALL = 40
COLS = 16
AREA = 640
PITCH = 20
SPREAD = TALL * PITCH
SPAN = 896
EDGE = 64


def mm(a, b):
    return jnp.dot(a, b, preferred_element_type=jnp.float32)


def nt(a, b):
    return lax.dot_general(a, b, (((1,), (1,)), ((), ())), preferred_element_type=jnp.float32)


def tn(a, b):
    return lax.dot_general(a, b, (((0,), (0,)), ((), ())), preferred_element_type=jnp.float32)


def half_of(value):
    return value.astype(jnp.bfloat16)


def full_of(value):
    return value.astype(jnp.float32)


def join(parts, axis=1):
    return jnp.concatenate(list(parts), axis=axis)


def quarter_of(value):
    return half_of(0.25 * full_of(value))


def lane_index(shape):
    return lax.broadcasted_iota(jnp.int32, shape, 1)


def row_index(shape):
    return lax.broadcasted_iota(jnp.int32, shape, 0)


def act_slope(pre):
    sigma = jax.nn.sigmoid(pre)
    act = pre * sigma
    return act, sigma + act * (1.0 - sigma)


def flat_rows():
    table = shapes()
    offset = 0
    starts = {}
    for name, height, width in table:
        starts[name] = offset // LANES
        offset += height * width
    bias_row = offset // LANES
    spots = {}
    inner = 0
    for name, height, width in table:
        spots[name] = inner
        inner += width
    return starts, bias_row, spots, inner


def cast_rows(dst, to, src, start, count, kind):
    big = 256
    whole = count // big

    if whole > 1:

        def body(step, carry):
            at = pl.multiple_of(step * big, big)
            dst[pl.ds(to + at, big), :] = src[pl.ds(start + at, big), :].astype(kind)
            return carry

        lax.fori_loop(0, whole, body, 0)
    elif whole == 1:
        dst[to : to + big, :] = src[start : start + big, :].astype(kind)
    rest = count - whole * big
    if rest:
        low = whole * big
        dst[to + low : to + count, :] = src[start + low : start + count, :].astype(kind)


MARGIN = 16


def stage_plan(count, start, rows):
    stop = start + rows
    pieces, fill = [], 0
    for rank in range(4):
        first = rank * count // LANES
        last = -(-(rank + 1) * count // LANES)
        low, high = max(start, first), min(stop, last)
        if low >= high:
            continue
        place = low - first + rank * BLOCK
        base = place // 16 * 16
        length = -(-(place - base + high - low) // 16) * 16
        to = MARGIN + low - start - (place - base)
        seam = MARGIN + low - start if start < first else None
        pieces.append((base, length, fill, to, seam))
        fill += length
    return pieces


class Stages:
    def __init__(self, v, count, segments):
        self.v, self.at = v, 0
        self.plans = [stage_plan(count, start, rows) for start, rows in segments]
        self.fetch(0)

    def copies(self, index):
        v, slot = self.v, index % 2
        return [
            pltpu.make_async_copy(
                v.out_all.at[base : base + length], v.stage.at[slot, fill : fill + length], v.ssem.at[slot, number]
            )
            for number, (base, length, fill, to, seam) in enumerate(self.plans[index])
        ]

    def fetch(self, index):
        if index < len(self.plans):
            for copy in self.copies(index):
                copy.start()

    def take(self):
        v, index = self.v, self.at
        self.at += 1
        for copy in self.copies(index):
            copy.wait()
        self.fetch(index + 1)
        for base, length, fill, to, seam in self.plans[index]:
            saved = None if seam is None else v.flat[seam : seam + 1, :]
            cast_rows(v.flat, to, v.stage.at[index % 2], fill, length, jnp.float32)
            if seam is not None:
                v.flat[seam : seam + 1, :] = v.flat[seam : seam + 1, :] + saved


def strided(ref, start, count, stride):
    if stride == 1:
        return ref[pl.ds(start, count), :]
    return ref[pl.ds(start, count, stride=stride), :]


def unpack_pairs(flat, row, count, dst, to, lane):
    dst[to : to + count, lane : lane + LANES] = half_of(strided(flat, MARGIN + 2 * row, count, 2))
    dst[to : to + count, lane + LANES : lane + 2 * LANES] = half_of(strided(flat, MARGIN + 2 * row + 1, count, 2))


def pack_pairs(flat, row, count, low, high):
    flat[pl.ds(MARGIN + 2 * row, count, stride=2), :] = low
    flat[pl.ds(MARGIN + 2 * row + 1, count, stride=2), :] = high


def split_pick(which, quarter):
    source = lax.broadcasted_iota(jnp.int32, (LANES, HEAD), 0)
    target = lax.broadcasted_iota(jnp.int32, (LANES, HEAD), 1)
    return jnp.where(source == 2 * (target - 64 * quarter) + which, 1.0, 0.0).astype(jnp.bfloat16)


UNPACK = (
    (CORR_IN, 648), (CORR_MIX, 3456), (FLOW_IN, 98), (FLOW_MIX, 576), (MOTION_MIX, 2268),
    (ROWS_GATES, 3840), (ROWS_CANDIDATE, 1920), (None, 21), (COLUMNS_GATES, 3840), (COLUMNS_CANDIDATE, 1920),
    (FLOW_HIDDEN, 2304), (MASK_HIDDEN, 2304), (FLOW_OUT, 36), (MASK_OUT, 1152),
)


def stage_of(v, name, rows):
    assert UNPACK[v.stages.at] == (name, rows)
    v.stages.take()


def unpack_gru(v, gates_name, cand_name, w_i, w_s):
    flat = v.flat
    stage_of(v, gates_name, 3840)
    for tap in range(5):
        unpack_pairs(flat, tap * 384, 128, w_s, tap * 128, 0)
        unpack_pairs(flat, tap * 384 + 128, 256, w_i, tap * 256, 0)
    stage_of(v, cand_name, 1920)
    for tap in range(5):
        w_s[tap * 128 : (tap + 1) * 128, 256:384] = half_of(strided(flat, MARGIN + tap * 384, 128, 1))
        w_i[tap * 256 : (tap + 1) * 256, 256:384] = half_of(strided(flat, MARGIN + tap * 384 + 128, 256, 1))


def unpack_encoder(v, count):
    starts, bias_row, spots, inner = flat_rows()
    flat = v.flat
    v.stages = Stages(v, count, [(bias_row if name is None else starts[name], rows) for name, rows in UNPACK])

    def stage(name, rows):
        stage_of(v, name, rows)

    stage(CORR_IN, 648)
    unpack_pairs(flat, 0, 324, v.w_ci, 0, 0)

    stage(CORR_MIX, 3456)
    lane = lane_index((128, LANES))
    low_half = lane < 64

    def mix_step(step, carry):
        at = MARGIN + 384 * step
        r0, r1, r2 = (strided(flat, at + i, 128, 3) for i in range(3))
        r1s, r2s = pltpu.roll(r1, 64, 1), pltpu.roll(r2, 64, 1)
        v.pair_a[pl.ds(0, 128, stride=2), :] = r0
        v.pair_a[pl.ds(1, 128, stride=2), :] = jnp.where(low_half, r1s, r2s)
        v.pair_b[pl.ds(0, 128, stride=2), :] = jnp.where(low_half, r1, 0.0)
        v.pair_b[pl.ds(1, 128, stride=2), :] = jnp.where(low_half, r2s, 0.0)
        to = pl.ds(pl.multiple_of(step * 256, 256), 256)
        v.w_cm[to, 0:128] = half_of(v.pair_a[...])
        v.w_cm[to, 128:256] = half_of(v.pair_b[...])
        return carry

    lax.fori_loop(0, 9, mix_step, 0)

    stage(FLOW_IN, 98)
    v.flow_tmp[...] = jnp.zeros_like(v.flow_tmp)
    for across in range(7):
        for comp in range(2):
            v.flow_tmp[pl.ds(across * 16 + comp, 7, stride=2), :] = strided(
                flat, MARGIN + across * 2 + comp, 7, 14
            )
    v.w_fi[...] = half_of(v.flow_tmp[...])

    stage(FLOW_MIX, 576)
    for step in range(9):
        r0 = strided(flat, MARGIN + 64 * step, 64, 1)
        high_half = lane_index((64, LANES)) >= 64
        v.pair_a[pl.ds(0, 64, stride=2), :] = jnp.where(high_half, pltpu.roll(r0, 64, 1), 0.0)
        v.pair_a[pl.ds(1, 64, stride=2), :] = jnp.where(high_half, r0, 0.0)
        v.w_fm[step * 128 : (step + 1) * 128, :] = half_of(v.pair_a[0:128, :])

    stage(MOTION_MIX, 2268)
    lane36 = lane_index((36, LANES))
    for i in range(64):
        if i == 0:
            value = strided(flat, MARGIN, 36, 63)
        elif i == 63:
            value = pltpu.roll(strided(flat, MARGIN + 62, 36, 63), 126, 1)
        else:
            low = pltpu.roll(strided(flat, MARGIN + i - 1, 36, 63), 2 * i, 1)
            high = pltpu.roll(strided(flat, MARGIN + i, 36, 63), 2 * i, 1)
            value = jnp.where(lane36 < 2 * i, low, high)
        v.mm_tmp[pl.ds(i, 36, stride=64), :] = jnp.where(lane36 < 126, value, 0.0)
    for step in range(9):
        v.w_mm[step * 256 : (step + 1) * 256, :] = half_of(v.mm_tmp[step * 256 : (step + 1) * 256, :])

    unpack_gru(v, ROWS_GATES, ROWS_CANDIDATE, v.w_ri, v.w_rs)

    stage(None, 21)
    place = 0
    lane1 = lane_index((1, LANES))
    for name, height, width in shapes():
        spot = spots[name]
        for block in range(-(-width // LANES)):
            at = spot + block * LANES
            row, shift = at // LANES, at % LANES
            value = flat[MARGIN + row : MARGIN + row + 1, :]
            if shift:
                after = flat[MARGIN + row + 1 : MARGIN + row + 2, :]
                value = jnp.where(
                    lane1 < LANES - shift, pltpu.roll(value, LANES - shift, 1), pltpu.roll(after, LANES - shift, 1)
                )
            left = width - block * LANES
            if left < LANES:
                value = jnp.where(lane1 < left, value, 0.0)
            if name == FLOW_MIX:
                value = pltpu.roll(value, 64, 1)
            v.bias[place : place + 1, :] = value
            place += 1


def unpack_heads(v):
    flat = v.flat
    low_half = lane_index((128, LANES)) < 64

    def stage(name, rows):
        stage_of(v, name, rows)

    unpack_gru(v, COLUMNS_GATES, COLUMNS_CANDIDATE, v.w_li, v.w_ls)

    for name, lane0 in ((FLOW_HIDDEN, 0), (MASK_HIDDEN, 256)):
        stage(name, 2304)
        for tap in range(9):
            unpack_pairs(flat, tap * 128, 128, v.w_h, tap * 128, lane0)

    stage(FLOW_OUT, 36)
    v.fo_tmp[...] = jnp.zeros_like(v.fo_tmp)
    for which in range(2):
        total = jnp.zeros((9, HEAD), jnp.float32)
        for quarter in range(4):
            total = total + mm(half_of(strided(flat, MARGIN + quarter, 9, 4)), split_pick(which, quarter))
        v.fo_tmp[pl.ds(which, 9, stride=2), 0:128] = total[:, :128]
        v.fo_tmp2[pl.ds(which, 9, stride=2), 0:128] = total[:, 128:]
    v.fo_tmp2[18:32, :] = jnp.zeros((14, LANES), jnp.float32)
    v.w_fo[:, 0:128] = half_of(v.fo_tmp[...])
    v.w_fo[:, 128:256] = half_of(v.fo_tmp2[...])

    stage(MASK_OUT, 1152)
    r = [strided(flat, MARGIN + i, 128, 9) for i in range(9)]
    rs = [pltpu.roll(r[i], 64, 1) for i in range(4, 9)]
    for block in range(5):
        even = r[block] if block < 4 else jnp.where(low_half, r[4], 0.0)
        odd = jnp.where(low_half, rs[block], rs[block + 1]) if block < 4 else jnp.where(low_half, rs[4], 0.0)
        v.pair_a[pl.ds(0, 128, stride=2), :] = even
        v.pair_a[pl.ds(1, 128, stride=2), :] = odd
        v.w_mo[:, block * 128 : (block + 1) * 128] = half_of(v.pair_a[...])


BIAS_AT = {}
_place = 0
for _name, _height, _width in shapes():
    BIAS_AT[_name] = _place
    _place += -(-_width // 128)
BIAS_ROWS = 32


def bias_of(v, name, blocks):
    at = BIAS_AT[name]
    return jnp.concatenate([v.bias[at + i : at + i + 1, :] for i in range(blocks)], axis=1)


class Halo:
    def __init__(self, v, sem, up_src, down_src, from_down, from_up):
        up = {SPACE: jnp.maximum(v.spot - 1, 0)}
        down = {SPACE: jnp.minimum(v.spot + 1, v.space - 1)}
        self.v = v
        self.up = remote(up_src, from_down, v.hsend.at[sem, 0], v.hrecv.at[sem, 0], up)
        self.down = remote(down_src, from_up, v.hsend.at[sem, 1], v.hrecv.at[sem, 1], down)

    def start(self):
        pl.when(self.v.spot > 0)(self.up.start)
        pl.when(self.v.spot < self.v.space - 1)(self.down.start)

    def receive(self):
        pl.when(self.v.spot < self.v.space - 1)(self.up.wait_recv)
        pl.when(self.v.spot > 0)(self.down.wait_recv)

    def sent(self):
        pl.when(self.v.spot > 0)(self.up.wait_send)
        pl.when(self.v.spot < self.v.space - 1)(self.down.wait_send)


def drain_bytes(ref, sem):
    pltpu.make_async_copy(ref, ref, sem).wait()


class Swap:
    def __init__(self, v, sem, src, dst, broadcast=False):
        self.v, self.sem, self.src, self.dst, self.broadcast = v, sem, src, dst, broadcast

    def copy(self, step):
        v = self.v
        to = lax.rem(v.spot + step, v.space)
        src = self.src if self.broadcast else self.src.at[to]
        return remote(src, self.dst.at[v.spot], v.asend.at[self.sem], v.arecv.at[self.sem], {SPACE: to})

    def each(self, what):
        def body(step, carry):
            what(self.copy(step))
            return carry

        lax.fori_loop(1, self.v.space, body, 0)

    def start(self):
        self.each(lambda copy: copy.start())

    def receive(self):
        drain_bytes(self.dst.at[0 : self.v.space - 1], self.v.arecv.at[self.sem])

    def sent(self):
        drain_bytes(self.dst.at[0 : self.v.space - 1], self.v.asend.at[self.sem])


def spread_rows(v, b, acts, rows, dst, row0, width, backward=False):
    x = lax.rem(row_index((rows, LANES)), WIDE)
    for block, act in enumerate(acts):
        v.tmp[8 : 8 + rows, :] = act
        for tap in range(3):
            d = (1 - tap) if backward else (tap - 1)
            value = act if d == 0 else v.tmp[8 + d : 8 + d + rows, :]
            if d == -1:
                value = jnp.where(x > 0, value, 0.0)
            if d == 1:
                value = jnp.where(x < WIDE - 1, value, 0.0)
            lane = tap * width + block * LANES
            if backward:
                dst[row0 : row0 + rows, b + lane : b + lane + LANES] = half_of(value)
            else:
                dst[b, row0 : row0 + rows, lane : lane + LANES] = half_of(value)


def spread_five(v, value, dst, lane_of, backward=False):
    x = lax.rem(row_index((AREA, LANES)), WIDE)
    v.tmp[8 : 8 + AREA, :] = value
    for tap in range(5):
        d = (2 - tap) if backward else (tap - 2)
        moved = value if d == 0 else v.tmp[8 + d : 8 + d + AREA, :]
        if d:
            moved = jnp.where((x + d >= 0) & (x + d < WIDE), moved, 0.0)
        if backward:
            taps_part(v, tap, lane_of, lane_of + LANES)[...] = half_of(moved)
        else:
            lane = lane_of(tap)
            dst[:, lane : lane + LANES] = half_of(moved)


def lines_of(ref, b, lines):
    return jnp.concatenate([ref[b, y] for y in range(lines)], axis=1)


def edge_rows(v, value, rows):
    low = jnp.where(v.spot > 0, value[0:rows], 0.0)
    high = jnp.where(v.spot < v.space - 1, value[-rows:], 0.0)
    return jnp.concatenate([low, value[rows:-rows], high], axis=0)


def early_taps(v):
    def flow(b, carry):
        up = jnp.where(v.spot > 0, v.flow_up[b], 0.0)
        down = jnp.where(v.spot < v.space - 1, v.flow_down[b], 0.0)
        lane = lane_index((16, LANES))
        v.fs[...] = jnp.zeros_like(v.fs)
        for across in range(7):
            d = across - 3
            for part, value in enumerate((up, v.flow[b], down)):
                moved = value
                if d:
                    moved = pltpu.roll(value, (-d) % LANES, 1)
                    moved = jnp.where((lane + d >= 0) & (lane + d < WIDE), moved, 0.0)
                v.fs[across, part * 10 : part * 10 + 10, :] = moved[0:10, :]
        for y in range(9):
            for across in range(7):
                v.flow_tmp[across * 16 : across * 16 + 16, :] = v.fs[across, 2 * y : 2 * y + 16, :]
            v.xt[b, :, y * 128 : (y + 1) * 128] = half_of(v.flow_tmp[...])
        return carry

    lax.fori_loop(0, BATCH, flow, 0)

    def image(b, carry):
        at = pl.ds(pl.multiple_of(b * AREA, AREA), AREA)
        spread_five(v, full_of(v.context[b]), v.xi.at[at], lambda t: t * 256)
        spread_five(v, full_of(v.net[b]), v.xs.at[at], lambda t: t * 128)
        return carry

    lax.fori_loop(0, BATCH, image, 0)


def gather_start(v, count):
    pieces = 4
    rows = BLOCK // 2 // pieces
    half = lax.rem(v.spot, 2)
    shift = lax.rem(v.rank * count, LANES)
    chunk = 512
    keep = lane_index((chunk, LANES)) >= shift
    v.tmp[7:8, :] = jnp.zeros((1, LANES), jnp.float32)

    def rotate(step, carry):
        at = pl.ds(pl.multiple_of(step * chunk, chunk), chunk)
        moved = pltpu.roll(full_of(v.gath[at, :]), shift, 1)
        v.tmp[8 : 8 + chunk, :] = moved
        v.gath[at, :] = half_of(jnp.where(keep, moved, v.tmp[7 : 7 + chunk, :]))
        v.tmp[7:8, :] = v.tmp[7 + chunk : 8 + chunk, :]
        return carry

    lax.fori_loop(0, BLOCK // chunk, rotate, 0)

    def piece(rank, which, index):
        return pl.ds(pl.multiple_of(rank * BLOCK + which * (BLOCK // 2) + index * rows, 16), rows)

    mine = pl.ds(pl.multiple_of(v.rank * BLOCK, 16), BLOCK)
    own = v.gath.at[0:BLOCK]
    v.g_x = [
        remote(
            v.gath.at[piece(0, half, k)], v.out_all.at[piece(v.rank, half, k)], v.gsend.at[0, k], v.grecv.at[0, k],
            {DP: v.other},
        )
        for k in range(pieces)
    ]
    v.g_own = remote(own, v.out_all.at[mine], v.gsend.at[4, 0], v.grecv.at[4, 0], {DP: v.mate})
    v.g_here = pltpu.make_async_copy(own, v.out_all.at[mine], v.gsend.at[4, 1])

    def forward(number, which, k, device):
        block = v.out_all.at[piece(v.other, which, k)]
        return remote(block, block, v.gsend.at[number, k], v.grecv.at[number, k], device)

    v.g_twin = [forward(1, half, k, {SPACE: v.twin}) for k in range(pieces)]
    v.g_mate = [forward(2, half, k, {DP: v.mate}) for k in range(pieces)]
    v.g_last = [forward(3, 1 - half, k, {DP: v.mate}) for k in range(pieces)]
    for copy in v.g_x:
        copy.start()
    v.g_own.start()
    v.g_here.start()


def gather_pass(v, first, last):
    for k in range(first, last):
        v.g_x[k].wait_recv()
        v.g_twin[k].start()
        v.g_mate[k].start()


def gather_end(v):
    for k in range(len(v.g_x)):
        v.g_twin[k].wait_recv()
        v.g_last[k].start()
    for k in range(len(v.g_x)):
        v.g_x[k].wait_send()
        v.g_twin[k].wait_send()
        v.g_mate[k].wait()
        v.g_last[k].wait()
    v.g_own.wait()
    v.g_here.wait()


def forward_rows(v):
    spot, last = v.spot, v.space - 1
    def image(b, carry):
        pieces = (
            (v.corr_up, 0, 256, 2, spot > 0),
            (v.corr, 256, 640, 5, None),
            (v.corr_down, 896, 256, 2, spot < last),
        )
        bias = bias_of(v, CORR_IN, 2)
        for ref, row0, rows, lines, seen in pieces:
            act, slope = act_slope(tn(lines_of(ref, b, lines), v.w_ci[...]) + bias)
            if seen is None:
                v.slope_ci[b] = half_of(slope)
            else:
                act = jnp.where(seen, act, 0.0)
            spread_rows(v, b, (act[:, :128], act[:, 128:]), rows, v.hx_c, row0, 256)

        act, slope = act_slope(tn(v.xt[b], v.w_fi[...]) + bias_of(v, FLOW_IN, 1))
        v.slope_fi[b] = half_of(slope[256:896])
        spread_rows(v, b, (edge_rows(v, act, 2 * WIDE),), 9 * WIDE, v.hx_f, 0, 128)

        pre = mm(join(v.hx_c[b, a * 128 : a * 128 + 896, :] for a in range(3)), v.w_cm[...]) + bias_of(v, CORR_MIX, 2)
        flow_pre = mm(join(v.hx_f[b, a * 128 : a * 128 + 896, :] for a in range(3)), v.w_fm[...])
        flow_pre = flow_pre + bias_of(v, FLOW_MIX, 1)
        low, low_slope = act_slope(pre[:, :128])
        high, high_slope = act_slope(pre[:, 128:] + flow_pre)
        v.slope_j[b, :, 0:128] = half_of(low_slope)
        v.slope_j[b, :, 128:256] = half_of(high_slope)
        spread_rows(v, b, (edge_rows(v, low, WIDE), edge_rows(v, high, WIDE)), 896, v.hx_j, 0, 256)

        pre = mm(join(v.hx_j[b, a * 128 : a * 128 + 640, :] for a in range(3)), v.w_mm[...])
        pre = pre + bias_of(v, MOTION_MIX, 1)
        act, slope = act_slope(pre)
        v.slope_m[b] = half_of(jnp.where(lane_index((AREA, LANES)) < 126, slope, 0.0))
        pick = jnp.where(lane_index((16, LANES)) == row_index((16, LANES)) + 126, 1.0, 0.0)
        own_flow = v.flow[b]
        for y in range(ROWS):
            v.tmp2[0:2, :] = own_flow[2 * y : 2 * y + 2, :]
            v.tmp2[2:16, :] = jnp.zeros((14, LANES), jnp.float32)
            v.motion[b, y * 128 : (y + 1) * 128, :] = act[y * 128 : (y + 1) * 128, :] + tn(
                half_of(v.tmp2[0:16, :]), half_of(pick)
            )
        v.motion[b] = full_of(half_of(v.motion[b]))
        pack_rows(v, v.motion, b, v.a_motion)
        return carry

    lax.fori_loop(0, BATCH, image, 0)
    v.swap_motion.start()

    def gru(b, carry):
        at = pl.ds(pl.multiple_of(b * AREA, AREA), AREA)
        s = full_of(v.net[b])
        spread_five(v, v.motion[b], v.xi.at[at], lambda t: t * 256 + 128)
        both = mm(v.xi[at, :], v.w_ri[...])
        gates = jax.nn.sigmoid(both[:, :256] + mm(v.xs[at, :], v.w_rs[:, :256]) + bias_of(v, ROWS_GATES, 2))
        update, reset = gates[:, :128], gates[:, 128:]
        v.ru[b] = update
        v.rr[b] = reset
        spread_five(v, full_of(half_of(reset * s)), v.xr.at[at], lambda t: t * 128)
        cand = jnp.tanh(both[:, 256:] + mm(v.xr[at, :], v.w_rs[:, 256:]) + bias_of(v, ROWS_CANDIDATE, 1))
        v.rc[b] = cand
        v.state[b] = s + update * (cand - s)
        pack_rows(v, v.state, b, v.a_state)
        return carry

    lax.fori_loop(0, BATCH, gru, 0)
    v.swap_state.start()


def pack_rows(v, src, b, dst):
    def peer(t, carry):
        for y in range(ROWS):
            at = pl.multiple_of(y * WIDE + t * COLS, COLS)
            dst[t, b, y * COLS : (y + 1) * COLS, :] = half_of(src[b, pl.ds(at, COLS), :])
        return carry

    lax.fori_loop(0, v.space, peer, 0)


def take_own(v, src, dst):
    dst[v.spot] = src[v.spot]


def columns_zero(v):
    def zero(b, carry):
        for ref, wide in ((v.xc, 384), (v.xcr, 128), (v.gc, 384)):
            for low in (0, 32 + AREA):
                ref[b, low : low + 32, :] = jnp.zeros((32, wide), jnp.bfloat16)
        return carry

    lax.fori_loop(0, BATCH, zero, 0)


def columns_in(v):
    def peer(t, carry):
        at = pl.ds(pl.multiple_of(32 + t * ROWS * COLS, 16), ROWS * COLS)
        for b in range(BATCH):
            v.xc[b, at, 0:128] = v.b_state[t, b]
            v.xc[b, at, 128:256] = v.b_context[t, b]
            v.xc[b, at, 256:384] = v.b_motion[t, b]
        return carry

    lax.fori_loop(0, v.space, peer, 0)


FX_ROWS = 16 + (TALL + 2) * PITCH


def fx_base(b):
    return pl.multiple_of(b * FX_ROWS, 8)


def columns_forward(v):
    def gru(b, carry):
        s = full_of(v.xc[b, 32 : 32 + AREA, 0:128])
        bias = join((bias_of(v, COLUMNS_GATES, 2), bias_of(v, COLUMNS_CANDIDATE, 1)))
        rows = [slice(t * COLS, t * COLS + AREA) for t in range(5)]
        both = mm(join(v.xc[b, rows[t], 128:384] for t in range(5)), v.w_li[...]) + bias
        gates = mm(join(v.xc[b, rows[t], 0:128] for t in range(5)), v.w_ls[:, 0:256])
        gates = jax.nn.sigmoid(gates + both[:, :256])
        update, reset = gates[:, :128], gates[:, 128:]
        v.lu[b] = update
        v.lr[b] = reset
        v.xcr[b, 32 : 32 + AREA, :] = half_of(reset * s)
        cand = jnp.tanh(both[:, 256:] + mm(join(v.xcr[b, rows[t], :] for t in range(5)), v.w_ls[:, 256:384]))
        v.lc[b] = cand
        final = s + update * (cand - s)
        v.out_net[b] = half_of(final)
        v.final[...] = full_of(half_of(final))
        fx = fx_base(b)
        v.mm_tmp[pl.ds(fx, FX_ROWS), :] = jnp.zeros((FX_ROWS, LANES), jnp.float32)
        for x in range(COLS):
            v.mm_tmp[pl.ds(fx + 8 + PITCH + 2 + x, TALL, stride=PITCH), :] = v.final[pl.ds(x, TALL, stride=COLS), :]
        for j in range(2):
            v.e_left[b, j, 0:TALL, :] = half_of(v.final[pl.ds(j, TALL, stride=COLS), :])
            v.e_right[b, j, 0:TALL, :] = half_of(v.final[pl.ds(COLS - 2 + j, TALL, stride=COLS), :])
        return carry

    lax.fori_loop(0, BATCH, gru, 0)
    v.halo_final.start()


def ring_masks(v, shape):
    x = lax.rem(row_index(shape), PITCH)
    place = v.spot * COLS + x - 2
    seen = (place >= 0) & (place < WIDE) & (x >= 1) & (x < PITCH - 1)
    own = (x >= 2) & (x < PITCH - 2)
    return seen, own


def mask_gradient(v):
    def image(b, carry):
        value = nt(quarter_of(v.grad_mask[b]), v.w_mo[:, 0:MASK])
        for block in range(2):
            v.final[...] = value[:, block * 128 : (block + 1) * 128]
            v.tmp[0:SPREAD, :] = jnp.zeros((SPREAD, LANES), jnp.float32)
            for x in range(COLS):
                v.tmp[pl.ds(2 + x, TALL, stride=PITCH), :] = v.final[pl.ds(x, TALL, stride=COLS), :]
            v.hgo[b, :, 256 + block * 128 : 384 + block * 128] = half_of(v.tmp[0:SPREAD, :])
            v.m_left[b, block, 0:TALL, :] = half_of(v.final[pl.ds(0, TALL, stride=COLS), :])
            v.m_right[b, block, 0:TALL, :] = half_of(v.final[pl.ds(COLS - 1, TALL, stride=COLS), :])
        return carry

    lax.fori_loop(0, BATCH, image, 0)
    v.halo_mask.start()


def heads_part(v, b, tap):
    ref = v.hx_c if tap < 6 else v.hx_f
    lane = tap % 6 * 128
    return ref.at[b, 0:SPREAD, lane : lane + 128]


def taps_part(v, t, low, high):
    ref = v.hx_f if t % 3 == 2 else v.hx_c
    lane = (t % 3) % 2 * 384
    return ref.at[t // 3, 0:AREA, lane + low : lane + high]


def split_three(value):
    first = half_of(value)
    second = half_of(value - full_of(first))
    third = half_of(value - full_of(first) - full_of(second))
    return first, second, third


def column_grid():
    lane = lane_index((COLS, SPAN))
    columns = jnp.where((lax.rem(lane, PITCH) == row_index((COLS, SPAN)) + 2) & (lane < SPREAD), 1.0, 0.0)
    lane = lane_index((TALL, SPAN))
    rows = jnp.where(lax.div(lane, PITCH) == row_index((TALL, SPAN)), 1.0, 0.0)
    return columns, half_of(rows)


def widen(value, columns, rows, parts):
    spread = 0.0
    for piece in split_three(value)[:parts]:
        spread = spread + mm(piece, rows)
    return jnp.sum(spread * columns, axis=0, keepdims=True)


def widen_all(v):
    columns, rows = column_grid()
    first = row_index((8, SPAN)) == 0
    second = row_index((8, SPAN)) == 1
    for b in range(BATCH):
        low, high = (widen(v.target[b, c], columns, rows, 3) for c in range(2))
        v.target_wide[b] = jnp.where(first, low, jnp.where(second, high, 0.0))
        v.valid_wide[b] = jnp.broadcast_to(widen(v.valid[b].astype(jnp.float32), columns, rows, 1), (8, SPAN))


def narrow(v, b, wide, columns, rows):
    for c in range(2):
        total = 0.0
        for piece in split_three(wide[c : c + 1, :] * columns):
            total = total + nt(piece, rows)
        v.out_flow[b, c] = total


def heads(v):
    spot, last = v.spot, v.space - 1
    v.halo_final.receive()
    v.halo_mask.receive()
    v.swap_count.receive()
    v.counts[v.spot] = v.count_out[...]
    counts = jnp.sum(v.counts[...], axis=0)
    seen, own = ring_masks(v, (SPREAD, LANES))
    steps = [(a - 1) * PITCH + (c - 1) for a in range(3) for c in range(3)]
    plane = jnp.float32(TALL * WIDE)
    columns, rows = column_grid()

    def image(b, carry):
        fx = fx_base(b)
        for j in range(2):
            left = jnp.where(spot > 0, full_of(v.f_left[b, j, 0:TALL, :]), 0.0)
            right = jnp.where(spot < last, full_of(v.f_right[b, j, 0:TALL, :]), 0.0)
            v.mm_tmp[pl.ds(fx + 8 + PITCH + j, TALL, stride=PITCH), :] = left
            v.mm_tmp[pl.ds(fx + 8 + PITCH + PITCH - 2 + j, TALL, stride=PITCH), :] = right
        for block in range(2):
            left = jnp.where(spot > 0, full_of(v.n_left[b, block, 0:TALL, :]), 0.0)
            right = jnp.where(spot < last, full_of(v.n_right[b, block, 0:TALL, :]), 0.0)
            v.tmp[0:SPREAD, :] = full_of(v.hgo[b, :, 256 + block * 128 : 384 + block * 128])
            v.tmp[pl.ds(1, TALL, stride=PITCH), :] = left
            v.tmp[pl.ds(PITCH - 2, TALL, stride=PITCH), :] = right
            v.hgo[b, :, 256 + block * 128 : 384 + block * 128] = half_of(v.tmp[0:SPREAD, :])
        for tap in range(9):
            at = 8 + PITCH + steps[tap]
            heads_part(v, b, tap)[...] = half_of(v.mm_tmp[pl.ds(fx + at, SPREAD), :])
        for part in range(2):
            name = (FLOW_HIDDEN, MASK_HIDDEN)[part]
            lanes = slice(part * 256, (part + 1) * 256)
            act, slope = act_slope(mm(join((v.hx_c[b, 0:SPREAD, :], v.hx_f[b, 0:SPREAD, :])), v.w_h[:, lanes]) + bias_of(v, name, 2))
            v.slope_h[b, :, lanes] = half_of(slope)
            if part == 0:
                for block in range(2):
                    value = jnp.where(seen, act[:, block * 128 : (block + 1) * 128], 0.0)
                    v.feat[b, 0:SPREAD, block * 128 : (block + 1) * 128] = half_of(value)
                v.feat[b, SPREAD:SPAN, :] = jnp.zeros((SPAN - SPREAD, HEAD), jnp.bfloat16)
            else:
                for block in range(2):
                    v.tmp[0:SPREAD, :] = act[:, block * 128 : (block + 1) * 128]
                    for x in range(COLS):
                        v.final[pl.ds(x, TALL, stride=COLS), :] = v.tmp[pl.ds(2 + x, TALL, stride=PITCH), :]
                    v.mf[b, :, block * 128 : (block + 1) * 128] = half_of(v.final[...])
        moved = nt(v.w_fo[...], v.feat[b])
        v.dt[...] = moved
        delta = jnp.zeros((8, SPAN), jnp.float32)
        for tap in range(9):
            pair = jnp.concatenate([v.dt[2 * tap : 2 * tap + 2, :], jnp.zeros((6, SPAN), jnp.float32)], axis=0)
            delta = delta + pltpu.roll(pair, (-steps[tap]) % SPAN, 1)
        v.tmp[0:SPAN, :] = jnp.zeros((SPAN, LANES), jnp.float32)
        v.final[...] = full_of(v.xc[b, 32 : 32 + AREA, 256:384])
        for x in range(COLS):
            v.tmp[pl.ds(2 + x, TALL, stride=PITCH), :] = v.final[pl.ds(x, TALL, stride=COLS), :]
        pick = jnp.where(lane_index((16, LANES)) == row_index((16, LANES)) + 126, 1.0, 0.0)
        base = nt(half_of(pick), half_of(v.tmp[0:SPAN, :]))[0:8, :]
        bias = v.bias[BIAS_AT[FLOW_OUT] : BIAS_AT[FLOW_OUT] + 1, :]
        first = row_index((8, SPAN)) == 0
        second = row_index((8, SPAN)) == 1
        shift = jnp.where(first, bias[0:1, 0:1], jnp.where(second, bias[0:1, 1:2], 0.0))
        new = base + delta + shift
        narrow(v, b, new, columns, rows)
        error = new - v.target_wide[b]
        root = jnp.sqrt(error * error + 1.0)
        valid = jnp.where(first | second, v.valid_wide[b], 0.0)
        piece = jnp.sum(valid * root)
        divisor = jnp.maximum(v.pick_count(counts, b), 1.0)
        gradient = plane / divisor * valid * error / root
        v.dg[b] = gradient
        v.losses[...] = jnp.where(row_index((8, LANES)) == b, piece, v.losses[...])
        return carry

    v.losses[...] = jnp.zeros((8, LANES), jnp.float32)
    lax.fori_loop(0, BATCH, image, 0)
    v.halo_dg.start()
    v.swap_loss.start()


def mask_output(v):
    def image(b, carry):
        store = pltpu.make_async_copy(v.mask_low, v.out_mask.at[b], v.osem.at[3])
        pl.when(b > 0)(store.wait)
        for block in range(5):
            wide = min(128, MASK - block * 128)
            lanes = slice(block * 128, block * 128 + wide)
            at = BIAS_AT[MASK_OUT] + block
            value = mm(v.mf[b], v.w_mo[:, lanes]) + v.bias[at : at + 1, 0:wide]
            v.mask_low[:, lanes] = half_of(0.25 * value)
        store.start()
        return carry

    lax.fori_loop(0, BATCH, image, 0)


def heads_back(v):
    spot, last = v.spot, v.space - 1
    seen, own = ring_masks(v, (SPREAD, LANES))
    steps = [(a - 1) * PITCH + (c - 1) for a in range(3) for c in range(3)]
    v.halo_dg.receive()

    def zb(c, low, rows):
        at = c * (2 * EDGE + SPREAD) + low
        return v.mm_tmp.at[at : at + rows]

    def image(b, carry):
        x = lax.rem(lane_index((8, SPAN)), PITCH)
        own_dg = v.dg[b]
        left = jnp.where((x < 2) & (spot > 0), pltpu.roll(v.dg_left[b], SPAN - COLS, 1), 0.0)
        right = jnp.where((x >= PITCH - 2) & (spot < last), pltpu.roll(v.dg_right[b], COLS, 1), 0.0)
        inside = lane_index((8, SPAN)) < SPREAD
        wide_dg = full_of(half_of(jnp.where(inside, own_dg + left + right, 0.0)))
        own_low = full_of(half_of(own_dg))
        v.dt[...] = jnp.zeros_like(v.dt)
        v.dto[...] = jnp.zeros_like(v.dto)
        for tap in range(9):
            v.dt[2 * tap : 2 * tap + 2, :] = pltpu.roll(wide_dg, steps[tap] % SPAN, 1)[0:2, :]
            v.dto[2 * tap : 2 * tap + 2, :] = pltpu.roll(own_low, steps[tap] % SPAN, 1)[0:2, :]
        v.dtb[b] = half_of(v.dto[...])
        from_flow = tn(half_of(v.dt[...]), v.w_fo[...])
        for block in range(4):
            lanes = slice(block * 128, (block + 1) * 128)
            value = from_flow[0:SPREAD, lanes] if block < 2 else full_of(v.hgo[b, :, lanes])
            value = value * full_of(v.slope_h[b, :, lanes])
            v.hgo[b, :, lanes] = half_of(jnp.where(seen, value, 0.0))
        total = jnp.zeros((SPREAD, LANES), jnp.float32)
        for a in range(3):
            value = nt(v.hgo[b], v.w_h[a * 384 : (a + 1) * 384, :])
            for c in range(3):
                zb(c, EDGE, SPREAD)[...] = value[:, c * 128 : (c + 1) * 128]
            for c in range(3):
                at = EDGE - steps[a * 3 + c]
                total = total + zb(c, at, SPREAD)[...]
        for block in range(4):
            lanes = slice(block * 128, (block + 1) * 128)
            v.hgo[b, :, lanes] = half_of(jnp.where(own, full_of(v.hgo[b, :, lanes]), 0.0))
        v.tmp[0:SPREAD, :] = total
        for x in range(COLS):
            v.final[pl.ds(x, TALL, stride=COLS), :] = v.tmp[pl.ds(2 + x, TALL, stride=PITCH), :]
        r = v.final[...] + full_of(v.grad_net[b])

        s = full_of(v.xc[b, 32 : 32 + AREA, 0:128])
        update, reset, cand = v.lu[b], v.lr[b], v.lc[b]
        cg = half_of(r * update * (1.0 - cand * cand))
        v.gc[b, 32 : 32 + AREA, 256:384] = cg
        rows = [slice((4 - t) * COLS, (4 - t) * COLS + AREA) for t in range(5)]
        reset_grad = nt(
            join(v.gc[b, rows[t], 256:384] for t in range(5)),
            join(v.w_ls[t * 128 : (t + 1) * 128, 256:384] for t in range(5)),
        )
        v.gc[b, 32 : 32 + AREA, 0:128] = half_of(r * (cand - s) * update * (1.0 - update))
        v.gc[b, 32 : 32 + AREA, 128:256] = half_of(reset_grad * s * reset * (1.0 - reset))
        state_grad = r * (1.0 - update) + reset_grad * reset
        state_grad = state_grad + nt(
            join(v.gc[b, rows[t], 0:256] for t in range(5)),
            join(v.w_ls[t * 128 : (t + 1) * 128, 0:256] for t in range(5)),
        )
        inputs_grad = nt(
            join(v.gc[b, rows[t], :] for t in range(5)), join(v.w_li[t * 256 : (t + 1) * 256, :] for t in range(5))
        )
        high = half_of(own_dg)
        low = half_of(own_dg - full_of(high))
        pick = half_of(jnp.where(lane_index((8, LANES)) == row_index((8, LANES)) + 126, 1.0, 0.0))
        v.tmp[0:SPAN, :] = tn(high, pick) + tn(low, pick)
        for x in range(COLS):
            v.final[pl.ds(x, TALL, stride=COLS), :] = v.tmp[pl.ds(2 + x, TALL, stride=PITCH), :]
        v.lu[b] = state_grad
        v.lr[b] = inputs_grad[:, 0:128]
        v.lc[b] = inputs_grad[:, 128:256] + v.final[...]

        def peer(t, carry):
            at = pl.ds(pl.multiple_of(t * ROWS * COLS, 16), ROWS * COLS)
            v.a_state[t, b] = half_of(v.lu[b, at, :])
            v.a_context[t, b] = half_of(v.lr[b, at, :])
            v.a_motion[t, b] = half_of(v.lc[b, at, :])
            return carry

        lax.fori_loop(0, v.space, peer, 0)
        return carry

    for c in range(3):
        zb(c, 0, EDGE)[...] = jnp.zeros((EDGE, LANES), jnp.float32)
        zb(c, EDGE + SPREAD, EDGE)[...] = jnp.zeros((EDGE, LANES), jnp.float32)
    lax.fori_loop(0, BATCH, image, 0)
    v.swap_loss.receive()
    v.back_state.start()


def unpack_back(v, src, dst):
    def peer(t, carry):
        for b in range(BATCH):
            value = full_of(src[t, b])
            for y in range(ROWS):
                at = pl.multiple_of(y * WIDE + t * COLS, COLS)
                dst[b, pl.ds(at, COLS), :] = value[y * COLS : (y + 1) * COLS, :]
        return carry

    lax.fori_loop(0, v.space, peer, 0)


def seams():
    starts, bias_row, _, _ = flat_rows()
    edges = sorted(starts.values()) + [bias_row]
    tiles = sorted({row // 16 for row in edges if row % 16})
    parts = {}
    for low, high in zip(edges, edges[1:]):
        for tile in tiles:
            if low < (tile + 1) * 16 and high > tile * 16:
                parts[tile] = parts.get(tile, 0) + 1
    return {tile: (index, parts[tile]) for index, tile in enumerate(tiles)}


class Flush:
    def __init__(self, v):
        self.v, self.at, self.busy, self.small = v, 0, {}, []
        self.tiles = seams()
        self.left = {tile: parts for tile, (_, parts) in self.tiles.items()}
        v.seam[...] = jnp.zeros_like(v.seam)
        top = (max(self.tiles) + 1) * 16
        rest = v.out_flat.shape[0] - top
        v.seam_low[16 * 16 : 16 * 16 + rest, :] = jnp.zeros((rest, LANES), jnp.bfloat16)
        self.write(16, rest, top)

    def write(self, index, rows, base):
        v = self.v
        copy = pltpu.make_async_copy(
            v.seam_low.at[index * 16 : index * 16 + rows], v.out_flat.at[base : base + rows], v.fsem.at[index]
        )
        copy.start()
        self.small.append(copy)

    def send(self, low, length, base):
        v, slot = self.v, self.at % 2
        self.at += 1
        if slot in self.busy:
            self.busy[slot].wait()
        cast_rows(v.stage.at[slot], 0, v.flat, low, length, jnp.bfloat16)
        copy = pltpu.make_async_copy(
            v.stage.at[slot, 0:length], v.out_flat.at[base : base + length], v.ssem.at[slot, 0]
        )
        copy.start()
        self.busy[slot] = copy

    def layer(self, start, rows):
        v, stop = self.v, start + rows
        for tile in self.tiles:
            low, high = max(start, tile * 16), min(stop, tile * 16 + 16)
            if low >= high:
                continue
            index = self.tiles[tile][0]
            v.seam[index, low - tile * 16 : high - tile * 16, :] = v.flat[MARGIN + low - start : MARGIN + high - start, :]
            self.left[tile] -= 1
            if not self.left[tile]:
                v.seam_low[index * 16 : index * 16 + 16, :] = half_of(v.seam[index])
                self.write(index, 16, tile * 16)
        low, high = -(-start // 16) * 16, stop // 16 * 16
        if high > low:
            self.send(MARGIN + low - start, high - low, low)

    def settle(self):
        for copy in list(self.busy.values()) + self.small:
            copy.wait()
        self.busy, self.small = {}, []


SHARE = 3072


class Reduce:
    ORDER = (
        (3, 3072, 3072), (3, 0, 3072), (2, 3072, 3072), (2, 0, 3072), (1, 3072, 3072), (1, 0, 3072),
        (0, 1024, 3072), (0, 4096, 2048), (0, 0, 1024),
    )

    def __init__(self, v, count):
        self.v, self.count = v, count
        self.flying, self.queue = [], []
        self.copies = {}
        rank = v.rank
        self.lower, self.upper = lax.rem(rank, 2), lax.div(rank, 2)
        self.side, self.depth = lax.rem(v.spot, 2), lax.div(v.spot, 2)
        self.group = v.space // 2

    def part(self, k):
        return self.ORDER[k][2] // 4 // self.v.space

    def slice_at(self, k, spot):
        return lax.rem(spot, 2) * (self.ORDER[k][2] // 8) + lax.div(spot, 2) * self.part(k)

    def offer(self, *numbers):
        self.queue += list(numbers)

    LONG = 6

    def stages(self, k):
        if k < self.LONG:
            return (self.core, self.across, self.side_sum, self.deep_sum, self.deep_out, self.owner, self.beside)
        if k < len(self.ORDER) - 1:
            return (self.core, self.across, self.stripes, self.along, self.beside)
        return (self.ranks, self.stripes, self.along, self.beside)

    def tick(self):
        for entry in self.flying:
            self.stages(entry[0])[entry[1]](entry[0])
            entry[1] += 1
        self.flying = [entry for entry in self.flying if entry[1] < len(self.stages(entry[0]))]
        if self.queue:
            number = self.queue.pop(0)
            self.v.flush.settle()
            self.begin(number)
            self.flying.append([number, 0])

    def begin(self, k):
        v, slot = self.v, k % 2
        quarter, low, size = self.ORDER[k]
        start = quarter * self.count // (LANES * 16) * 16 + low
        half = size // 2
        if k == len(self.ORDER) - 1:
            self.begin_ranks(start, size // 4)
            return

        def rows(which):
            return v.out_flat.at[pl.ds(pl.multiple_of(start + which * half, 16), half)]

        copy = remote(
            rows(1 - self.lower), v.rcore.at[slot, 0:half], v.rsend.at[0, slot], v.rrecv.at[0, slot], {DP: v.mate}
        )
        own = pltpu.make_async_copy(rows(self.lower), v.own.at[slot, 0:half], v.rlocal.at[slot])
        copy.start()
        own.start()
        self.copies[k] = (copy, own)

    def begin_ranks(self, start, rows):
        v = self.v

        def block(rank):
            at = start + lax.rem(rank, 2) * (2 * rows) + lax.div(rank, 2) * rows
            return v.out_flat.at[pl.ds(pl.multiple_of(at, 16), rows)]

        for turn in range(1, 4):
            to = lax.rem(v.rank + turn, 4)
            remote(block(to), v.dall.at[v.rank], v.dsend, v.drecv, {DP: to}).start()
        self.mine = pltpu.make_async_copy(block(v.rank), v.dall.at[v.rank], v.rlocal.at[0])
        self.mine.start()

    def ranks(self, k):
        v, slot, part = self.v, k % 2, self.part(k)
        self.mine.wait()
        drain_bytes(v.dall.at[0:3], v.dsend)
        drain_bytes(v.dall.at[0:3], v.drecv)
        self.finish_f(k)
        value = full_of(v.dall[0]) + full_of(v.dall[1]) + full_of(v.dall[2]) + full_of(v.dall[3])
        rows = self.ORDER[k][2] // 4
        v.ks[slot, 0:rows, :] = value
        v.ts[slot, 0:rows, :] = half_of(value)
        v.acc[slot, 0:part, :] = v.ks[slot, pl.ds(pl.multiple_of(self.slice_at(k, v.spot), 16), part), :]
        self.each(lambda step: self.s_copy(k, step).start(), 1, v.space)

    def finish_f(self, k):
        drain_bytes(self.s_all(k - 2), self.v.s2send.at[k % 2])
        self.f_sent(k - 2)

    def core(self, k):
        v, slot = self.v, k % 2
        copy, own = self.copies[k]
        copy.wait()
        own.wait()
        if k >= 2:
            self.x_copy(k - 2).wait_send()
        quarter = self.ORDER[k][2] // 4

        def add(step, carry):
            at = pl.multiple_of(step * 128, 128)
            near = pl.ds(pl.multiple_of(self.upper * quarter + at, 128), 128)
            far = pl.ds(pl.multiple_of((1 - self.upper) * quarter + at, 128), 128)
            to = pl.ds(at, 128)
            v.tx[slot, to, :] = half_of(full_of(v.own[slot, far, :]) + full_of(v.rcore[slot, far, :]))
            v.ks[slot, to, :] = full_of(v.own[slot, near, :]) + full_of(v.rcore[slot, near, :])
            return carry

        lax.fori_loop(0, quarter // 128, add, 0)
        self.x_copy(k).start()

    def x_copy(self, k):
        v, slot = self.v, k % 2
        rows = slice(0, self.ORDER[k][2] // 4)
        return remote(
            v.tx.at[slot, rows], v.rx.at[slot, rows], v.rsend.at[1, slot], v.rrecv.at[1, slot], {DP: v.other}
        )

    def s_copy(self, k, step):
        v, slot, part = self.v, k % 2, self.part(k)
        to = lax.rem(v.spot + step, v.space)
        src = v.ts.at[slot, pl.ds(pl.multiple_of(self.slice_at(k, to), 16), part)]
        dst = v.rs.at[slot, v.spot, 0:part]
        return remote(src, dst, v.s2send.at[slot], v.s2recv.at[slot], {SPACE: to})

    def s_all(self, k):
        return self.v.rs.at[k % 2, 0 : self.v.space - 1, 0 : self.part(k)]

    def each(self, what, start, stop):
        def body(step, carry):
            what(step)
            return carry

        lax.fori_loop(start, stop, body, 0)

    def across(self, k):
        v, slot = self.v, k % 2
        self.x_copy(k).wait_recv()
        if k < self.LONG:
            self.across_long(k)
            return

        def add(step, carry):
            to = pl.ds(pl.multiple_of(step * 128, 128), 128)
            value = v.ks[slot, to, :] + full_of(v.rx[slot, to, :])
            v.ks[slot, to, :] = value
            v.ts[slot, to, :] = half_of(value)
            return carry

        lax.fori_loop(0, self.ORDER[k][2] // 4 // 128, add, 0)
        part = self.part(k)
        v.acc[slot, 0:part, :] = v.ks[slot, pl.ds(pl.multiple_of(self.slice_at(k, v.spot), 16), part), :]
        self.each(lambda step: self.s_copy(k, step).start(), 1, v.space)

    def across_long(self, k):
        v, slot = self.v, k % 2
        if k >= 2:
            self.side_copy(k - 2).wait_send()
        rows = self.ORDER[k][2] // 8

        def add(step, carry):
            at = pl.multiple_of(step * 128, 128)
            near = pl.ds(pl.multiple_of(self.side * rows + at, 128), 128)
            far = pl.ds(pl.multiple_of((1 - self.side) * rows + at, 128), 128)
            to = pl.ds(at, 128)
            v.ty[slot, to, :] = half_of(v.ks[slot, far, :] + full_of(v.rx[slot, far, :]))
            v.ky[slot, to, :] = v.ks[slot, near, :] + full_of(v.rx[slot, near, :])
            return carry

        lax.fori_loop(0, rows // 128, add, 0)
        self.side_copy(k).start()

    def side_copy(self, k):
        v, slot = self.v, k % 2
        return remote(v.ty.at[slot], v.ry.at[slot], v.rsend.at[2, slot], v.rrecv.at[2, slot], {SPACE: v.twin})

    def deep_at(self, k, depth):
        return pl.ds(pl.multiple_of(depth * self.part(k), 16), self.part(k))

    def deep_copy(self, k, step):
        v, slot = self.v, k % 2
        to = lax.rem(self.depth + step, self.group)
        return remote(
            v.tz.at[slot, self.deep_at(k, to)], v.rz.at[slot, self.depth], v.z1send.at[slot],
            v.z1recv.at[slot], {SPACE: to * 2 + self.side},
        )

    def deep_all(self, k):
        return self.v.rz.at[k % 2, 0 : self.group - 1]

    def side_sum(self, k):
        v, slot = self.v, k % 2
        self.side_copy(k).wait_recv()
        if k >= 2:
            drain_bytes(self.deep_all(k - 2), v.z1send.at[slot])
        value = v.ky[slot] + full_of(v.ry[slot])
        v.tz[slot] = half_of(value)
        v.ky[slot] = value
        v.kz[slot] = v.ky[slot, self.deep_at(k, self.depth), :]
        self.each(lambda step: self.deep_copy(k, step).start(), 1, self.group)

    def out_copy(self, k, step):
        v, slot = self.v, k % 3
        to = lax.rem(self.depth + step, self.group)
        block = v.az.at[slot, self.deep_at(k, self.depth)]
        return remote(
            block, block, v.z2send.at[slot], v.z2recv.at[slot], {SPACE: to * 2 + self.side}
        )

    def deep_sum(self, k):
        v, slot = self.v, k % 2
        drain_bytes(self.deep_all(k), v.z1recv.at[slot])

        def add(step, value):
            return value + full_of(v.rz[slot, lax.rem(self.depth + step, self.group)])

        value = lax.fori_loop(1, self.group, add, v.kz[slot])
        if k >= 2:
            self.own_wait(k - 2)
        v.az[k % 3, self.deep_at(k, self.depth), :] = half_of(value)
        self.each(lambda step: self.out_copy(k, step).start(), 1, self.group)

    def own_rows(self, k, lower, upper):
        quarter, low, size = self.ORDER[k]
        at = low + lower * (size // 2) + upper * (size // 4) + self.side * (size // 8)
        return pl.ds(pl.multiple_of(at, 16), size // 8)

    def own_copy(self, k):
        v = self.v
        rows = self.own_rows(k, self.lower, self.upper)
        return remote(v.az.at[k % 3], v.gath.at[rows], v.osend.at[k % 3], v.orecv.at[k], {DP: self.ORDER[k][0]})

    def own_wait(self, k):
        pl.when(self.v.rank != self.ORDER[k][0])(self.own_copy(k).wait_send)

    def deep_out(self, k):
        v = self.v
        several = v.az.at[k % 3, 0 : (self.group - 1) * self.part(k)]
        drain_bytes(several, v.z2send.at[k % 3])
        drain_bytes(several, v.z2recv.at[k % 3])
        pl.when(v.rank != self.ORDER[k][0])(self.own_copy(k).start)

        @pl.when(v.rank == self.ORDER[k][0])
        def _():
            v.gath[self.own_rows(k, self.lower, self.upper), :] = v.az[k % 3]

    def owner(self, k):
        v = self.v

        @pl.when(v.rank == self.ORDER[k][0])
        def _():
            drain_bytes(v.gath.at[0 : 3 * (self.ORDER[k][2] // 8)], v.orecv.at[k])
            for copy in self.y_copies(k):
                copy.start()

    def place(self, k, lower, upper, spot):
        quarter, low, size = self.ORDER[k]
        at = low + lower * (size // 2) + upper * (size // 4) + self.slice_at(k, spot)
        return pl.ds(pl.multiple_of(at, 16), self.part(k))

    def f_copy(self, k, step):
        v, slot = self.v, k % 2
        quarter = self.ORDER[k][0]
        to = lax.rem(self.depth + step, self.group) * 2 + self.side
        return remote(
            v.fin.at[slot, 0 : self.part(k)], v.gath.at[self.place(k, self.lower, self.upper, v.spot)],
            v.fsend.at[slot], v.frecv.at[k], {DP: quarter, SPACE: to},
        )

    def f_all(self, k, what):
        v = self.v
        pl.when(v.rank != self.ORDER[k][0])(lambda: what(self.f_copy(k, 0)))
        self.each(lambda step: what(self.f_copy(k, step)), 1, self.group)

    def f_sent(self, k):
        v = self.v
        quarter = self.ORDER[k][0]
        pl.when(v.rank != quarter)(lambda: self.f_copy(k, 0).wait_send())
        drain_bytes(v.gath.at[0 : (self.group - 1) * self.part(k)], v.fsend.at[k % 2])

    def stripes(self, k):
        v, slot, part = self.v, k % 2, self.part(k)
        quarter = self.ORDER[k][0]
        drain_bytes(self.s_all(k), v.s2recv.at[slot])

        def add(step, value):
            return value + full_of(v.rs[slot, lax.rem(v.spot + step, v.space), 0:part])

        value = half_of(lax.fori_loop(1, v.space, add, v.acc[slot, 0:part, :]))
        v.fin[slot, 0:part, :] = value

        @pl.when(v.rank == quarter)
        def _():
            v.gath[self.place(k, self.lower, self.upper, v.spot), :] = v.fin[slot, 0:part, :]

        self.f_all(k, lambda copy: copy.start())

    def y_copies(self, k):
        v = self.v
        quarter, low, size = self.ORDER[k]
        out = []
        for i in range(4):
            at = pl.multiple_of(low + i * (size // 4) + self.side * (size // 8), 16)
            block = v.gath.at[pl.ds(at, size // 8)]
            out.append(remote(block, block, v.ysend.at[k], v.yrecv.at[k], {SPACE: v.twin}))
        return out

    def along(self, k):
        v = self.v
        quarter = self.ORDER[k][0]

        @pl.when(v.rank == quarter)
        def _():
            drain_bytes(v.gath.at[0 : (4 * self.group - 1) * self.part(k)], v.frecv.at[k])
            for copy in self.y_copies(k):
                copy.start()

    def beside(self, k):
        v = self.v

        @pl.when(v.rank == self.ORDER[k][0])
        def _():
            several = v.gath.at[0 : self.ORDER[k][2] // 2]
            drain_bytes(several, v.ysend.at[k])
            drain_bytes(several, v.yrecv.at[k])

    def settle(self):
        v = self.v
        for k in range(self.LONG - 2, self.LONG):
            self.side_copy(k).wait_send()
            drain_bytes(self.deep_all(k), v.z1send.at[k % 2])
            self.own_wait(k)
        for k in range(len(self.ORDER) - 3, len(self.ORDER) - 1):
            self.x_copy(k).wait_send()
        for k in range(len(self.ORDER) - 2, len(self.ORDER)):
            drain_bytes(self.s_all(k), v.s2send.at[k % 2])
            self.f_sent(k)

    def ready(self):
        v, count = self.v, self.count
        v.gath[2 * SHARE :, :] = jnp.zeros((32, LANES), jnp.bfloat16)

        @pl.when(v.rank == 3)
        def _():
            at = self.bias_base() - 3 * count // (LANES * 16) * 16
            v.gath[at : at + 32, :] = half_of(full_of(v.gath[at : at + 32, :]) + v.bsum[...])

    def lay(self, first, last):
        v, count = self.v, self.count
        offset = v.rank * count - quarter_base(v.rank, count) * LANES
        skip = lax.div(offset, LANES)
        shift = lax.rem(offset, LANES)
        near = lane_index((256, LANES)) < LANES - shift

        def staged(slot):
            return v.mm_tmp.at[pl.ds(pl.multiple_of(slot * 256, 256), 256)]

        def out(step):
            at = pl.multiple_of(step * 256, 256)
            slot = lax.rem(step, 2)
            return pltpu.make_async_copy(staged(slot), v.out_grads.at[pl.ds(at, 256)], v.osem.at[4 + slot])

        def place(step, carry):
            at = pl.multiple_of(step * 256, 256)
            v.tmp[0:288, :] = pltpu.roll(full_of(v.gath[pl.ds(at, 288), :]), lax.rem(LANES - shift, LANES), 1)
            pl.when(step > first + 1)(out(step - 2).wait)
            staged(lax.rem(step, 2))[...] = jnp.where(near, v.tmp[pl.ds(skip, 256), :], v.tmp[pl.ds(skip + 1, 256), :])
            out(step).start()
            return carry

        lax.fori_loop(first, last, place, 0)
        for step in (last - 2, last - 1):
            out(step).wait()

    def bias_base(self):
        return flat_rows()[1] // 16 * 16

    def bias_core(self):
        v = self.v
        self.b1 = remote(v.bown, v.bcore, v.bsend.at[0], v.brecv.at[0], {DP: v.mate})
        self.b1.start()

    def bias_across(self):
        v = self.v
        self.b1.wait()
        v.btwo[...] = v.bown[...] + v.bcore[...]
        self.b2 = remote(v.btwo, v.bacross, v.bsend.at[1], v.brecv.at[1], {DP: v.other})
        self.b2.start()

    def bias_stripes(self):
        v = self.v
        self.b2.wait()
        v.bfour[...] = v.btwo[...] + v.bacross[...]
        self.b3 = Swap(v, 8, v.bfour, v.ball, True)
        self.b3.start()

    def bias_end(self):
        v = self.v
        self.b3.receive()
        self.b3.sent()
        v.ball[v.spot] = v.bfour[...]
        v.bsum[...] = jnp.sum(v.ball[...], axis=0)


def ones_sum(g):
    return mm(jnp.ones((8, g.shape[0]), jnp.bfloat16), g)[0:1, :]


def keep_bias(v, name, value):
    for block in range(-(-value.shape[1] // 128)):
        at = BIAS_AT[name] + block
        v.gbias[at : at + 1, :] = value[:, block * 128 : (block + 1) * 128]


def gradients_gru(v, gates_name, cand_name, parts, g_of):
    starts, _, _, _ = flat_rows()
    total = 0.0
    for b in range(BATCH):
        total = total + ones_sum(g_of(b))
    keep_bias(v, gates_name, total[:, 0:256])
    keep_bias(v, cand_name, total[:, 256:384])

    def taps(number, first, last):
        return lambda b: join(parts(t)[number](b) for t in range(first, last))

    state = tn_all(taps(0, 0, 5), g_of, 0, 256)
    for t in range(5):
        pack_pairs(v.flat, t * 384, 128, state[t * 128 : (t + 1) * 128, 0:128], state[t * 128 : (t + 1) * 128, 128:256])
    state = tn_all(taps(2, 0, 5), g_of, 256, 384)
    for t in range(5):
        v.mm_tmp[pl.ds(MARGIN + t * 384, 128), :] = state[t * 128 : (t + 1) * 128, :]
    for first, last in ((0, 2), (2, 4), (4, 5)):
        inputs = tn_all(taps(1, first, last), g_of, 0, 384)
        for t in range(first, last):
            rows = slice((t - first) * 256, (t - first + 1) * 256)
            pack_pairs(v.flat, t * 384 + 128, 256, inputs[rows, 0:128], inputs[rows, 128:256])
            v.mm_tmp[pl.ds(MARGIN + t * 384 + 128, 256), :] = inputs[rows, 256:384]
    v.flush.layer(starts[gates_name], 3840)
    cast_rows(v.flat, MARGIN, v.mm_tmp, MARGIN, 1920, jnp.float32)
    v.flush.layer(starts[cand_name], 1920)


def tn_all(part, g_of, low, high):
    return tn(join((part(b) for b in range(BATCH)), 0), join((g_of(b, low, high) for b in range(BATCH)), 0))


def gradients_heads(v):
    starts, _, _, _ = flat_rows()
    total = 0.0
    for b in range(BATCH):
        total = total + ones_sum(v.hgo[b])
    keep_bias(v, FLOW_HIDDEN, total[:, 0:256])
    keep_bias(v, MASK_HIDDEN, total[:, 256:512])
    for name, lane in ((FLOW_HIDDEN, 0), (MASK_HIDDEN, 256)):
        grads = join((v.hgo[b, :, lane : lane + 256] for b in range(BATCH)), 0)
        for group in range(3):
            taps = [join(heads_part(v, b, group * 3 + c)[...] for c in range(3)) for b in range(BATCH)]
            value = tn(join(taps, 0), grads)
            for c in range(3):
                rows = slice(c * 128, (c + 1) * 128)
                pack_pairs(v.flat, (group * 3 + c) * 128, 128, value[rows, 0:128], value[rows, 128:256])
        v.flush.layer(starts[name], 2304)

    total = 0.0
    sums = 0.0
    for b in range(BATCH):
        total = total + mm(v.dtb[b], v.feat[b])
        sums = sums + jnp.sum(full_of(half_of(v.dg[b])), axis=1, keepdims=True)
    lane1 = lane_index((1, LANES))
    at = BIAS_AT[FLOW_OUT]
    v.gbias[at : at + 1, :] = jnp.where(lane1 == 0, sums[0:1, :], jnp.where(lane1 == 1, sums[1:2, :], 0.0))
    v.fo_tmp[...] = total[:, 0:128]
    v.fo_tmp2[...] = total[:, 128:256]
    for quarter in range(4):
        value = 0.0
        for which in range(2):
            rows = jnp.concatenate(
                [v.fo_tmp[pl.ds(which, 9, stride=2), :], v.fo_tmp2[pl.ds(which, 9, stride=2), :]], axis=1
            )
            value = value + nt(half_of(rows), split_pick(which, quarter))
        v.flat[pl.ds(MARGIN + quarter, 9, stride=4), :] = value
    v.flush.layer(starts[FLOW_OUT], 36)

    lane = lane_index((128, LANES))
    low_half = lane < 64
    even, odd = [], []
    total = 0.0
    for b in range(BATCH):
        total = total + ones_sum(quarter_of(v.grad_mask[b]))
    for block in range(5):
        wide = min(128, MASK - block * 128)
        at = BIAS_AT[MASK_OUT] + block
        v.gbias[at : at + 1, 0:wide] = total[:, block * 128 : block * 128 + wide]
        value = 0.0
        for b in range(BATCH):
            value = value + tn(v.mf[b], quarter_of(v.grad_mask[b, :, block * 128 : block * 128 + wide]))
        v.pair_a[:, 0:wide] = value
        even.append(v.pair_a[pl.ds(0, 128, stride=2), :])
        odd.append(pltpu.roll(v.pair_a[pl.ds(1, 128, stride=2), :], 64, 1))
    for i in range(4):
        v.flat[pl.ds(MARGIN + i, 128, stride=9), :] = even[i]
    v.flat[pl.ds(MARGIN + 4, 128, stride=9), :] = jnp.where(low_half, even[4], odd[0])
    for i in range(4):
        v.flat[pl.ds(MARGIN + 5 + i, 128, stride=9), :] = jnp.where(low_half, odd[i], odd[i + 1])
    v.flush.layer(starts[MASK_OUT], 1152)


def rows_back(v):
    v.back_state.receive()
    take_own(v, v.a_state, v.b_state)
    unpack_back(v, v.b_state, v.state)
    v.reduce.tick()

    def image(b, carry):
        r = v.state[b]
        s = full_of(v.net[b])
        update, reset, cand = v.ru[b], v.rr[b], v.rc[b]
        cg = full_of(half_of(r * update * (1.0 - cand * cand)))
        spread_five(v, cg, None, 256, True)
        reset_grad = nt(
            join(taps_part(v, t, 256, 384)[...] for t in range(5)),
            join(v.w_rs[t * 128 : (t + 1) * 128, 256:384] for t in range(5)),
        )
        low = full_of(half_of(r * (cand - s) * update * (1.0 - update)))
        high = full_of(half_of(reset_grad * s * reset * (1.0 - reset)))
        spread_five(v, low, None, 0, True)
        spread_five(v, high, None, 128, True)
        v.gr[b] = taps_part(v, 2, 0, 384)[...]
        state_grad = r * (1.0 - update) + reset_grad * reset
        state_grad = state_grad + nt(
            join(taps_part(v, t, 0, 256)[...] for t in range(5)),
            join(v.w_rs[t * 128 : (t + 1) * 128, 0:256] for t in range(5)),
        )
        v.ru[b] = state_grad
        inputs_grad = nt(
            join(taps_part(v, t, 0, 384)[...] for t in range(5)),
            join(v.w_ri[t * 256 : (t + 1) * 256, :] for t in range(5)),
        )
        v.rr[b] = inputs_grad[:, 0:128]
        v.rc[b] = inputs_grad[:, 128:256]
        return carry

    lax.fori_loop(0, BATCH, image, 0)
    v.store_gnet.start()
    v.back_context.receive()
    v.back_motion.receive()
    take_own(v, v.a_context, v.b_context)
    take_own(v, v.a_motion, v.b_motion)
    unpack_back(v, v.b_context, v.lr)
    unpack_back(v, v.b_motion, v.lu)

    def total(b, carry):
        v.rr[b] = v.rr[b] + v.lr[b]
        motion = v.rc[b] + v.lu[b]
        v.mge[b, 256:896, :] = half_of(motion * full_of(v.slope_m[b]))
        high = half_of(motion)
        low = half_of(motion - full_of(high))
        pick = half_of(jnp.where(lane_index((16, LANES)) == row_index((16, LANES)) + 126, 1.0, 0.0))
        v.gf_base[b] = (nt(pick, high) + nt(pick, low))[0:8, :]
        return carry

    lax.fori_loop(0, BATCH, total, 0)
    v.halo_mg.start()
    v.store_gctx.start()


def gcorr_stores(v, b):
    return [
        pltpu.make_async_copy(v.mm_tmp.at[y * 328 : y * 328 + CORR], v.out_gcorr.at[b, y], v.gsem.at[y])
        for y in range(ROWS)
    ]


def branch_back(v):
    v.halo_mg.receive()

    def image(b, carry):
        up = jnp.where(v.spot > 0, full_of(v.mge[b, 0:256, :]), 0.0)
        own = full_of(v.mge[b, 256:896, :])
        down = jnp.where(v.spot < v.space - 1, full_of(v.mge[b, 896:1152, :]), 0.0)
        spread_rows(v, 0, (jnp.concatenate([up, own, down], axis=0),), 1152, v.xi, 0, 128, True)
        joint = nt(
            join(v.xi[(2 - a) * 128 : (2 - a) * 128 + 896, 0:384] for a in range(3)),
            join(v.w_mm[k * 256 : (k + 1) * 256, :] for k in range(9)),
        )
        branch = joint * full_of(v.slope_j[b])
        low = full_of(half_of(edge_rows(v, branch[:, 0:128], WIDE)))
        high = full_of(half_of(edge_rows(v, branch[:, 128:256], WIDE)))
        spread_rows(v, 0, (low, high), 896, v.hx_j.at[b], 0, 256, True)
        return carry

    lax.fori_loop(0, BATCH, image, 0)


def branch_own(v, b, low=0, high=256):
    return v.hx_j[b, 128:768, 256 + low : 256 + high]


def flow_back(v):
    def image(b, carry):
        rows = [slice((2 - a) * 128, (2 - a) * 128 + 640) for a in range(3)]
        flow_grad = nt(
            join(v.hx_j[b, rows[a], c * 256 + 128 : (c + 1) * 256] for a in range(3) for c in range(3)),
            join(v.w_fm[k * 128 : (k + 1) * 128, :] for k in range(9)),
        )
        v.fpg[b] = half_of(flow_grad * full_of(v.slope_fi[b]))
        z = nt(v.w_fi[...], v.fpg[b])
        total = jnp.zeros((32, LANES), jnp.float32)
        lane = lane_index((32, LANES))
        for across in range(7):
            v.fs[across] = jnp.zeros((32, LANES), jnp.float32)
            for y in range(ROWS):
                v.fs[across, 2 * y : 2 * y + 16, :] += z[across * 16 : across * 16 + 16, y * 128 : (y + 1) * 128]
            d = across - 3
            value = v.fs[across]
            if d:
                value = pltpu.roll(value, d % LANES, 1)
                value = jnp.where((lane - d >= 0) & (lane - d < WIDE), value, 0.0)
            total = total + value
        v.gf[b] = total
        return carry

    lax.fori_loop(0, BATCH, image, 0)
    v.halo_gf.start()


def corr_back(v):
    def image(b, carry):
        corr_grad = nt(
            join(v.hx_j[b, (2 - a) * 128 : (2 - a) * 128 + 640, :] for a in range(3)),
            join(v.w_cm[k * 256 : (k + 1) * 256, :] for k in range(9)),
        )
        v.cpg[b] = half_of(corr_grad * full_of(v.slope_ci[b]))
        stores = gcorr_stores(v, b)
        for store in stores:
            pl.when(b > 0)(store.wait)
        gcorr = nt(v.w_ci[...], v.cpg[b])
        for y in range(ROWS):
            v.mm_tmp[y * 328 : y * 328 + CORR, :] = gcorr[:, y * WIDE : (y + 1) * WIDE]
        for store in stores:
            store.start()
        return carry

    lax.fori_loop(0, BATCH, image, 0)


def summed(v, ref, name):
    total = 0.0
    for b in range(BATCH):
        total = total + ones_sum(ref(b))
    keep_bias(v, name, total)


def gradients_motion(v):
    starts = flat_rows()[0]
    summed(v, lambda b: v.mge[b, 256:896, :], MOTION_MIX)
    grads = join((v.mge[b, 256:896, :] for b in range(BATCH)), 0)
    for a in range(3):
        taps = join((v.hx_j[b, a * 128 : a * 128 + 640, :] for b in range(BATCH)), 0)
        v.mm_tmp[a * 768 : (a + 1) * 768, :] = tn(taps, grads)
    lane36 = lane_index((36, LANES))
    for r in range(63):
        first = v.mm_tmp[pl.ds(r, 36, stride=64), :]
        second = v.mm_tmp[pl.ds(r + 1, 36, stride=64), :]
        if r:
            first = pltpu.roll(first, LANES - 2 * r, 1)
        second = pltpu.roll(second, 126 - 2 * r, 1)
        v.flat[pl.ds(MARGIN + r, 36, stride=63), :] = jnp.where(lane36 < 126 - 2 * r, first, second)
    v.flush.layer(starts[MOTION_MIX], 2268)


def gradients_branches(v):
    starts = flat_rows()[0]
    summed(v, lambda b: branch_own(v, b), CORR_MIX)
    summed(v, lambda b: branch_own(v, b, 128, 256), FLOW_MIX)
    grads = join((branch_own(v, b, 128, 256) for b in range(BATCH)), 0)
    for k in range(9):
        a, c = k // 3, k % 3
        if c == 0:
            taps = join((v.hx_f[b, (a + 1) * 128 : (a + 1) * 128 + 640, :] for b in range(BATCH)), 0)
            group = tn(taps, grads)
        v.pair_a[0:128, :] = group[c * 128 : (c + 1) * 128]
        even, odd = (v.pair_a[pl.ds(i, 64, stride=2), :] for i in range(2))
        v.flat[MARGIN + 64 * k : MARGIN + 64 * (k + 1), :] = jnp.where(
            lane_index((64, LANES)) < 64, pltpu.roll(even, 64, 1), odd
        )
    v.flush.layer(starts[FLOW_MIX], 576)

    low_half = lane_index((128, LANES)) < 64
    grads = join((branch_own(v, b) for b in range(BATCH)), 0)
    for k in range(9):
        a, c = k // 3, k % 3
        if c == 0:
            taps = join((v.hx_c[b, (a + 1) * 128 : (a + 1) * 128 + 640, :] for b in range(BATCH)), 0)
            group = tn(taps, grads)
        v.pair_a[...] = group[c * 256 : (c + 1) * 256, 0:128]
        v.pair_b[...] = group[c * 256 : (c + 1) * 256, 128:256]
        even, odd = (v.pair_a[pl.ds(i, 128, stride=2), :] for i in range(2))
        even_high, odd_high = (v.pair_b[pl.ds(i, 128, stride=2), :] for i in range(2))
        odd, odd_high = pltpu.roll(odd, 64, 1), pltpu.roll(odd_high, 64, 1)
        at = MARGIN + 384 * k
        v.flat[pl.ds(at, 128, stride=3), :] = even
        v.flat[pl.ds(at + 1, 128, stride=3), :] = jnp.where(low_half, even_high, odd)
        v.flat[pl.ds(at + 2, 128, stride=3), :] = jnp.where(low_half, odd, odd_high)
        if k == 4:
            v.reduce.tick()
    v.flush.layer(starts[CORR_MIX], 3456)


def gradients_flow_in(v):
    starts = flat_rows()[0]
    summed(v, lambda b: v.fpg[b], FLOW_IN)
    value = 0.0
    for b in range(BATCH):
        value = value + mm(v.xt[b, :, 256:896], v.fpg[b])
    v.flow_tmp[...] = value
    for across in range(7):
        for comp in range(2):
            v.flat[pl.ds(MARGIN + across * 2 + comp, 7, stride=14), :] = v.flow_tmp[
                pl.ds(across * 16 + comp, 7, stride=2), :
            ]
    v.flush.layer(starts[FLOW_IN], 98)


def gradients_corr_in(v):
    starts = flat_rows()[0]
    summed(v, lambda b: v.cpg[b], CORR_IN)
    value = 0.0
    for b in range(BATCH):
        value = value + mm(lines_of(v.corr, b, ROWS), v.cpg[b])
    pack_pairs(v.flat, 0, 324, value[:, 0:128], value[:, 128:256])
    v.flush.layer(starts[CORR_IN], 648)


def bias_tile(v):
    starts, bias_row, spots, inner = flat_rows()
    lead = bias_row % 16
    lane1 = lane_index((1, LANES))
    v.bown[...] = jnp.zeros_like(v.bown)
    for name, height, width in shapes():
        for block in range(-(-width // LANES)):
            value = v.gbias[BIAS_AT[name] + block : BIAS_AT[name] + block + 1, :]
            if name == FLOW_MIX:
                value = pltpu.roll(value, 64, 1)
            left = width - block * LANES
            if left < LANES:
                value = jnp.where(lane1 < left, value, 0.0)
            at = spots[name] + block * LANES
            row, shift = lead + at // LANES, at % LANES
            moved = pltpu.roll(value, shift, 1) if shift else value
            v.bown[row : row + 1, :] = v.bown[row : row + 1, :] + jnp.where(lane1 >= shift, moved, 0.0)
            if shift:
                v.bown[row + 1 : row + 2, :] = v.bown[row + 1 : row + 2, :] + jnp.where(lane1 < shift, moved, 0.0)


def finish(v):
    spot, last = v.spot, v.space - 1
    v.halo_gf.receive()
    for b in range(BATCH):
        v.tmp2[...] = v.gf[b]
        up = jnp.where(spot > 0, v.gf_up[b], 0.0)
        down = jnp.where(spot < last, v.gf_down[b], 0.0)
        v.tmp2[6:12, :] += up[16:22, :]
        v.tmp2[10:16, :] += down[0:6, :]
        for y in range(ROWS):
            v.out_gflow[b, 2 * y : 2 * y + 2, :] = (
                v.tmp2[6 + 2 * y : 8 + 2 * y, :] + v.gf_base[b, 0:2, y * 128 : (y + 1) * 128]
            )
    v.loss_in[v.spot] = v.losses[...]
    total = jnp.sum(v.loss_in[...], axis=0)
    counts = jnp.sum(v.counts[...], axis=0)
    value = total / jnp.maximum(counts, 1.0)
    for b in range(BATCH):
        v.out_loss[b] = v.pick_count(value, b)


class View:
    pass


def main_kernel(names, space, count, *refs):
    v = View()
    for name, ref in zip(names, refs):
        setattr(v, name, ref)
    v.space = space
    v.lu, v.lc = v.motion, v.state
    v.spot = lax.axis_index(SPACE)
    v.rank = lax.axis_index(DP)
    v.mate, v.other, v.twin = mate_of(v.rank), lax.rem(v.rank + 2, 4), mate_of(v.spot)
    spot = v.spot
    barrier = pltpu.get_barrier_semaphore()

    def hello(step, carry):
        pl.semaphore_signal(barrier, inc=1, device_id={SPACE: lax.rem(spot + step, space)}, device_id_type=MESH)
        return carry

    lax.fori_loop(1, space, hello, 0)
    for turn in range(1, 4):

        def greet_rank(step, carry):
            place = lax.rem(spot + 2 * step, space)
            device = {DP: lax.rem(v.rank + turn, 4), SPACE: place}
            pl.semaphore_signal(barrier, inc=1, device_id=device, device_id_type=MESH)
            return carry

        lax.fori_loop(0, space // 2, greet_rank, 0)
    pl.semaphore_wait(barrier, space - 1 + 3 * (space // 2))

    v.store_gnet = pltpu.make_async_copy(v.ru, v.out_gnet, v.osem.at[0])
    v.store_gctx = pltpu.make_async_copy(v.rr, v.out_gctx, v.osem.at[1])
    rows = row_index((8, LANES))
    counted = jnp.zeros((8, LANES), jnp.float32)
    for b in range(BATCH):
        counted = jnp.where(rows == b, jnp.sum(v.valid[b].astype(jnp.float32)), counted)
    v.count_out[...] = counted
    v.pick_count = lambda counts, b: jnp.sum(jnp.where((rows == b) & (lane_index((8, LANES)) == 0), counts, 0.0))
    v.swap_count = Swap(v, 0, v.count_out, v.counts, True)
    v.swap_context = Swap(v, 1, v.a_context, v.b_context)
    v.swap_motion = Swap(v, 2, v.a_motion, v.b_motion)
    v.swap_state = Swap(v, 3, v.a_state, v.b_state)
    v.back_context = Swap(v, 4, v.a_context, v.b_context)
    v.back_motion = Swap(v, 5, v.a_motion, v.b_motion)
    v.back_state = Swap(v, 6, v.a_state, v.b_state)
    v.swap_loss = Swap(v, 7, v.losses, v.loss_in, True)
    v.halo_corr = Halo(v, 0, v.corr.at[:, 0:2], v.corr.at[:, 3:5], v.corr_down, v.corr_up)
    v.halo_flow = Halo(v, 1, v.flow, v.flow, v.flow_down, v.flow_up)
    v.halo_final = Halo(v, 2, v.e_left, v.e_right, v.f_right, v.f_left)
    v.halo_mask = Halo(v, 3, v.m_left, v.m_right, v.n_right, v.n_left)
    v.halo_dg = Halo(v, 4, v.dg, v.dg, v.dg_right, v.dg_left)
    v.halo_mg = Halo(v, 5, v.mge.at[:, 256:512], v.mge.at[:, 640:896], v.mge.at[:, 896:1152], v.mge.at[:, 0:256])
    v.halo_gf = Halo(v, 6, v.gf, v.gf, v.gf_down, v.gf_up)

    load = pltpu.make_async_copy(v.local, v.gath.at[0:BLOCK], v.gsend.at[4, 2])
    load.start()
    for b in range(BATCH):
        for y in range(ROWS):
            v.flow[b, 2 * y : 2 * y + 2, :] = full_of(v.flow_in[b, y])
        v.flow[b, 2 * ROWS : 16, :] = jnp.zeros((16 - 2 * ROWS, LANES), jnp.float32)
    v.halo_flow.start()
    v.halo_corr.start()
    v.swap_count.start()
    load.wait()
    gather_start(v, count)

    def first(b, carry):
        v.state[b] = full_of(v.context[b])
        pack_rows(v, v.state, b, v.a_context)
        return carry

    lax.fori_loop(0, BATCH, first, 0)
    v.swap_context.start()
    v.halo_flow.receive()
    gather_pass(v, 0, 2)
    widen_all(v)
    early_taps(v)
    gather_pass(v, 2, 4)
    columns_zero(v)
    gather_end(v)
    unpack_encoder(v, count)
    v.halo_corr.receive()
    forward_rows(v)
    keep = [pltpu.make_async_copy(v.hx_c, v.out_keep_c, v.ksem.at[0]), pltpu.make_async_copy(v.hx_f, v.out_keep_f, v.ksem.at[1])]
    for copy in keep:
        copy.start()
    unpack_heads(v)
    mask_gradient(v)
    v.swap_context.receive()
    v.swap_motion.receive()
    v.swap_state.receive()
    take_own(v, v.a_context, v.b_context)
    take_own(v, v.a_motion, v.b_motion)
    take_own(v, v.a_state, v.b_state)
    columns_in(v)
    columns_forward(v)
    for copy in keep:
        copy.wait()
    heads(v)
    mask_output(v)
    v.swap_context.sent()
    v.swap_motion.sent()
    v.swap_state.sent()
    heads_back(v)
    v.flush = Flush(v)
    red = v.reduce = Reduce(v, count)
    gradients_heads(v)
    v.back_context.start()
    v.back_motion.start()
    red.offer(0)
    red.tick()
    gradients_gru(
        v,
        COLUMNS_GATES,
        COLUMNS_CANDIDATE,
        lambda t: (
            lambda b: v.xc[b, t * COLS : t * COLS + AREA, 0:128],
            lambda b: v.xc[b, t * COLS : t * COLS + AREA, 128:384],
            lambda b: v.xcr[b, t * COLS : t * COLS + AREA, :],
        ),
        lambda b, low=0, high=384: v.gc[b, 32 : 32 + AREA, low:high],
    )
    red.offer(1, 2)
    red.tick()
    rows_back(v)
    red.tick()
    keep = [
        pltpu.make_async_copy(v.out_keep_c, v.hx_c, v.ksem.at[0]),
        pltpu.make_async_copy(v.out_keep_f, v.hx_f, v.ksem.at[1]),
    ]
    for copy in keep:
        copy.start()
    gradients_gru(
        v,
        ROWS_GATES,
        ROWS_CANDIDATE,
        lambda t: (
            lambda b: v.xs[b * AREA : (b + 1) * AREA, t * 128 : (t + 1) * 128],
            lambda b: v.xi[b * AREA : (b + 1) * AREA, t * 256 : (t + 1) * 256],
            lambda b: v.xr[b * AREA : (b + 1) * AREA, t * 128 : (t + 1) * 128],
        ),
        lambda b, low=0, high=384: v.gr[b, :, low:high],
    )
    red.offer(3, 4)
    red.tick()
    gradients_motion(v)
    red.offer(5)
    red.tick()
    branch_back(v)
    red.tick()
    for copy in keep:
        copy.wait()
    gradients_branches(v)
    red.offer(6)
    red.tick()
    flow_back(v)
    red.tick()
    gradients_flow_in(v)
    red.offer(7)
    red.tick()
    corr_back(v)
    red.tick()
    gradients_corr_in(v)
    bias_tile(v)
    red.bias_core()
    red.offer(8)
    red.tick()
    for store in gcorr_stores(v, 0):
        store.wait()
    finish(v)
    red.bias_across()
    red.tick()
    red.bias_stripes()
    pl.when(v.rank == 0)(lambda: red.lay(4, 15))
    red.tick()
    red.bias_end()
    red.ready()
    pl.when(v.rank > 0)(lambda: red.lay(0, 24))
    red.tick()
    pl.when(v.rank == 0)(lambda: red.lay(15, 24))
    red.tick()
    assert not red.flying and not red.queue
    pl.when(v.rank == 0)(lambda: red.lay(0, 4))
    red.settle()
    for swap in (v.swap_count, v.back_context, v.back_motion, v.back_state, v.swap_loss):
        swap.sent()
    for halo in (v.halo_corr, v.halo_flow, v.halo_final, v.halo_mask, v.halo_dg, v.halo_mg, v.halo_gf):
        halo.sent()
    v.store_gnet.wait()
    v.store_gctx.wait()
    pltpu.make_async_copy(v.mask_low, v.out_mask.at[0], v.osem.at[3]).wait()


def main_call(space, count, local, net, context, corr, flow, target, valid, grad_net, grad_mask):
    total = 3 * count // (LANES * 16) * 16 + BLOCK
    low, wide = jnp.bfloat16, jnp.float32
    peers = (space, BATCH, ROWS * COLS, LANES)
    ins = dict(
        local=local, net=net, context=context, corr=corr, flow_in=flow, target=target, valid=valid,
        grad_net=grad_net, grad_mask=grad_mask,
    )
    outs = dict(
        out_net=((BATCH, AREA, 128), low),
        out_flow=((BATCH, 2, COLS, TALL), wide),
        out_mask=((BATCH, AREA, MASK), low),
        out_loss=((BATCH,), wide),
        out_flat=((total, 128), low),
        out_gnet=((BATCH, AREA, 128), wide),
        out_gctx=((BATCH, AREA, 128), wide),
        out_gcorr=((BATCH, ROWS, CORR, 128), wide),
        out_gflow=((BATCH, 16, 128), wide),
        out_keep_c=((BATCH, 1152, 768), low),
        out_keep_f=((BATCH, 1152, 384), low),
        out_all=((4 * BLOCK, 128), low),
        out_grads=((BLOCK, 128), wide),
    )
    scratch = dict(
        stage=((2, 3904, 128), low),
        seam=((16, 16, 128), wide),
        mask_low=((AREA, MASK), low),
        seam_low=((16 * 20, 128), low),
        own=((2, SHARE // 2, 128), low),
        rcore=((2, SHARE // 2, 128), low),
        tx=((2, SHARE // 4, 128), low),
        rx=((2, SHARE // 4, 128), low),
        ks=((2, SHARE // 4, 128), wide),
        ts=((2, SHARE // 4, 128), low),
        acc=((2, SHARE // 4 // space, 128), wide),
        rs=((2, space, SHARE // 4 // space, 128), low),
        fin=((2, SHARE // 4 // space, 128), low),
        dall=((4, 256, 128), low),
        ty=((2, SHARE // 8, 128), low),
        ry=((2, SHARE // 8, 128), low),
        ky=((2, SHARE // 8, 128), wide),
        tz=((2, SHARE // 8, 128), low),
        rz=((2, space // 2, SHARE // 4 // space, 128), low),
        kz=((2, SHARE // 4 // space, 128), wide),
        az=((3, SHARE // 8, 128), low),
        gath=((2 * SHARE + 32, 128), low),
        bown=((32, 128), wide), bcore=((32, 128), wide), btwo=((32, 128), wide), bacross=((32, 128), wide),
        bfour=((32, 128), wide), ball=((space, 32, 128), wide), bsum=((32, 128), wide),
        flat=((3904, 128), wide),
        pair_a=((256, 128), wide),
        pair_b=((256, 128), wide),
        flow_tmp=((112, 128), wide),
        mm_tmp=((3 * (2 * EDGE + SPREAD), 128), wide),
        fo_tmp=((32, 128), wide),
        fo_tmp2=((32, 128), wide),
        w_ci=((CORR, 256), low),
        w_cm=((2304, 256), low),
        w_fi=((112, 128), low),
        w_fm=((1152, 128), low),
        w_mm=((2304, 128), low),
        w_ri=((1280, 384), low),
        w_rs=((640, 384), low),
        w_li=((1280, 384), low),
        w_ls=((640, 384), low),
        w_h=((1152, 512), low),
        w_fo=((32, 256), low),
        w_mo=((256, 640), low),
        bias=((BIAS_ROWS, 128), wide),
        gbias=((BIAS_ROWS, 128), wide),
        corr_up=((BATCH, 2, CORR, 128), low),
        corr_down=((BATCH, 2, CORR, 128), low),
        flow_up=((BATCH, 16, 128), wide),
        flow_down=((BATCH, 16, 128), wide),
        fs=((7, 32, 128), wide),
        xt=((BATCH, 112, 1152), low),
        tmp=((1168, 128), wide),
        tmp2=((32, 128), wide),
        hx_c=((BATCH, 1152, 768), low),
        hx_f=((BATCH, 1152, 384), low),
        hx_j=((BATCH, 896, 768), low),
        slope_ci=((BATCH, AREA, 256), low),
        slope_fi=((BATCH, AREA, 128), low),
        slope_j=((BATCH, 896, 256), low),
        slope_m=((BATCH, AREA, 128), low),
        motion=((BATCH, AREA, 128), wide),
        state=((BATCH, AREA, 128), wide),
        xi=((BATCH * AREA, 1280), low),
        xs=((BATCH * AREA, 640), low),
        xr=((BATCH * AREA, 640), low),
        ru=((BATCH, AREA, 128), wide),
        rr=((BATCH, AREA, 128), wide),
        rc=((BATCH, AREA, 128), wide),
        lr=((BATCH, AREA, 128), wide),
        a_state=(peers, low), a_context=(peers, low), a_motion=(peers, low),
        b_state=(peers, low), b_context=(peers, low), b_motion=(peers, low),
        xc=((BATCH, AREA + 64, 384), low),
        xcr=((BATCH, AREA + 64, 128), low),
        gc=((BATCH, AREA + 64, 384), low),
        final=((AREA, 128), wide),
        e_left=((BATCH, 2, 48, 128), low), e_right=((BATCH, 2, 48, 128), low),
        f_left=((BATCH, 2, 48, 128), low), f_right=((BATCH, 2, 48, 128), low),
        m_left=((BATCH, 2, 48, 128), low), m_right=((BATCH, 2, 48, 128), low),
        n_left=((BATCH, 2, 48, 128), low), n_right=((BATCH, 2, 48, 128), low),
        slope_h=((BATCH, SPREAD, 512), low),
        feat=((BATCH, SPAN, 256), low),
        mf=((BATCH, AREA, 256), low),
        dg=((BATCH, 8, SPAN), wide),
        target_wide=((BATCH, 8, SPAN), wide),
        valid_wide=((BATCH, 8, SPAN), wide),
        flow=((BATCH, 16, 128), wide),
        dg_left=((BATCH, 8, SPAN), wide), dg_right=((BATCH, 8, SPAN), wide),
        dt=((32, SPAN), wide),
        dto=((32, SPAN), wide),
        dtb=((BATCH, 32, SPAN), low),
        hgo=((BATCH, SPREAD, 512), low),
        gr=((BATCH, AREA, 384), low),
        mge=((BATCH, 1152, 128), low),
        cpg=((BATCH, AREA, 256), low),
        fpg=((BATCH, AREA, 128), low),
        gf_base=((BATCH, 8, AREA), wide),
        gf=((BATCH, 32, 128), wide), gf_up=((BATCH, 32, 128), wide), gf_down=((BATCH, 32, 128), wide),
        count_out=((8, 128), wide), counts=((space, 8, 128), wide),
        losses=((8, 128), wide), loss_in=((space, 8, 128), wide),
    )
    sems = dict(
        hsend=pltpu.SemaphoreType.DMA((7, 2)), hrecv=pltpu.SemaphoreType.DMA((7, 2)),
        asend=pltpu.SemaphoreType.DMA((9,)), arecv=pltpu.SemaphoreType.DMA((9,)),
        ssem=pltpu.SemaphoreType.DMA((2, 2)),
        fsem=pltpu.SemaphoreType.DMA((17,)),
        rsend=pltpu.SemaphoreType.DMA((3, 2)), rrecv=pltpu.SemaphoreType.DMA((3, 2)),
        z1send=pltpu.SemaphoreType.DMA((2,)), z1recv=pltpu.SemaphoreType.DMA((2,)),
        z2send=pltpu.SemaphoreType.DMA((3,)), z2recv=pltpu.SemaphoreType.DMA((3,)),
        osend=pltpu.SemaphoreType.DMA((3,)), orecv=pltpu.SemaphoreType.DMA((9,)),
        rlocal=pltpu.SemaphoreType.DMA((2,)),
        s2send=pltpu.SemaphoreType.DMA((2,)), s2recv=pltpu.SemaphoreType.DMA((2,)),
        fsend=pltpu.SemaphoreType.DMA((2,)), frecv=pltpu.SemaphoreType.DMA((9,)),
        ysend=pltpu.SemaphoreType.DMA((9,)), yrecv=pltpu.SemaphoreType.DMA((9,)),
        dsend=pltpu.SemaphoreType.DMA, drecv=pltpu.SemaphoreType.DMA,
        bsend=pltpu.SemaphoreType.DMA((2,)), brecv=pltpu.SemaphoreType.DMA((2,)),
        ksem=pltpu.SemaphoreType.DMA((2,)),
        gsend=pltpu.SemaphoreType.DMA((5, 4)), grecv=pltpu.SemaphoreType.DMA((5, 4)),
        gsem=pltpu.SemaphoreType.DMA((ROWS,)),
        osem=pltpu.SemaphoreType.DMA((6,)),
    )
    vmem = pl.BlockSpec(memory_space=pltpu.VMEM)
    hbm = pl.BlockSpec(memory_space=pl.ANY)
    names = list(ins) + list(outs) + list(scratch) + list(sems)
    return pl.pallas_call(
        functools.partial(main_kernel, names, space, count),
        out_shape=[jax.ShapeDtypeStruct(*entry) for entry in outs.values()],
        in_specs=[hbm if name == "local" else vmem for name in ins],
        out_specs=[pl.BlockSpec(memory_space=pltpu.SMEM) if name == "out_loss" else hbm if name in ("out_flat", "out_gnet", "out_gctx", "out_gcorr", "out_keep_c", "out_keep_f", "out_mask", "out_grads", "out_all") else vmem for name in outs],
        scratch_shapes=[pltpu.VMEM(*entry) for entry in scratch.values()] + list(sems.values()),
        compiler_params=pltpu.CompilerParams(
            collective_id=2, has_side_effects=True, vmem_limit_bytes=VMEM_LIMIT
        ),
    )(*ins.values())


VMEM_LIMIT = 64 * 2**20 - 2**17


def shards_wide(net, context, corr, flow, target, valid, grad_net, grad_mask, params):
    space = lax.axis_size(SPACE)
    count = params.shape[0]
    local = jnp.pad(params, (0, BLOCK * LANES - count)).reshape(BLOCK, LANES)
    outs = main_call(
        space, count, local, net.reshape(BATCH, AREA, HID), context.reshape(BATCH, AREA, CTX),
        jnp.transpose(corr, (0, 1, 3, 2)), jnp.transpose(flow, (0, 2, 1, 3)), jnp.transpose(target, (0, 1, 3, 2)),
        jnp.transpose(valid, (0, 2, 1)),
        grad_net.reshape(BATCH, AREA, HID), grad_mask.reshape(BATCH, AREA, MASK),
    )
    new_net, new_flow, mask, loss, _, gnet, gctx, gcorr, gflow = outs[:9]
    new_flow = jnp.transpose(new_flow, (0, 1, 3, 2))
    grads = outs[-1].reshape(-1)[:count]
    return (
        new_net.reshape(BATCH, TALL, COLS, HID),
        new_flow,
        mask.reshape(BATCH, TALL, COLS, MASK),
        loss,
        grads,
        gnet.reshape(BATCH, ROWS, WIDE, HID),
        gctx.reshape(BATCH, ROWS, WIDE, CTX),
        jnp.transpose(gcorr, (0, 1, 3, 2)),
        jnp.transpose(gflow[:, 0 : 2 * ROWS].reshape(BATCH, ROWS, 2, WIDE), (0, 2, 1, 3)),
    )


def solution(mesh):
    def plan(*arrays):
        net, valid = arrays[0], arrays[5]
        if (net.shape[1:3], valid.shape[1:]) == ((ROWS, WIDE), (TALL, COLS)):
            return shards_wide(*arrays)
        return shards(*arrays)

    return jax.shard_map(
        plan,
        mesh=mesh,
        in_specs=(
            P(DP, SPACE, None, None),
            P(DP, SPACE, None, None),
            P(DP, SPACE, None, None),
            P(DP, None, SPACE, None),
            P(DP, None, None, SPACE),
            P(DP, None, SPACE),
            P(DP, None, SPACE, None),
            P(DP, None, SPACE, None),
            P(DP),
        ),
        out_specs=(
            P(DP, None, SPACE, None),
            P(DP, None, None, SPACE),
            P(DP, None, SPACE, None),
            P(DP),
            P(DP),
            P(DP, SPACE, None, None),
            P(DP, SPACE, None, None),
            P(DP, SPACE, None, None),
            P(DP, None, SPACE, None),
        ),
        check_vma=False,
    )
```

```python
import functools

import jax
import jax.numpy as jnp
from jax import lax
from jax.experimental import pallas as pl
from jax.experimental.pallas import tpu as pltpu
from jax.sharding import PartitionSpec as P

HID = 128
CTX = 128
MOT = 128
CORR = 324
SPACE = "space"
DP = "dp"
(
    CORR_IN,
    CORR_MIX,
    FLOW_IN,
    FLOW_MIX,
    MOTION_MIX,
    ROWS_GATES,
    ROWS_CANDIDATE,
    COLUMNS_GATES,
    COLUMNS_CANDIDATE,
    FLOW_HIDDEN,
    FLOW_OUT,
    MASK_HIDDEN,
    MASK_OUT,
) = range(13)
C1 = 256
C2 = 192
F1 = 128
F2 = 64
HEAD = 256
MASK = 576


def with_halo(block, sides, width):
    for axis, dim in sides:
        count = lax.axis_size(axis)
        forward = [(i, i + 1) for i in range(count - 1)]
        backward = [(target, source) for source, target in forward]
        low = lax.ppermute(
            lax.slice_in_dim(block, block.shape[dim] - width, None, axis=dim), axis, forward
        )
        high = lax.ppermute(lax.slice_in_dim(block, 0, width, axis=dim), axis, backward)
        block = jnp.concatenate([low, block, high], axis=dim)
    return block


def shapes():
    inputs_width = HID + CTX + MOT
    return [
        (CORR_IN, CORR, C1),
        (CORR_MIX, 9 * C1, C2),
        (FLOW_IN, 98, F1),
        (FLOW_MIX, 9 * F1, F2),
        (MOTION_MIX, 9 * (C2 + F2), MOT - 2),
        (ROWS_GATES, 5 * inputs_width, 2 * HID),
        (ROWS_CANDIDATE, 5 * inputs_width, HID),
        (COLUMNS_GATES, 5 * inputs_width, 2 * HID),
        (COLUMNS_CANDIDATE, 5 * inputs_width, HID),
        (FLOW_HIDDEN, 9 * HID, HEAD),
        (FLOW_OUT, 9 * HEAD, 2),
        (MASK_HIDDEN, 9 * HID, HEAD),
        (MASK_OUT, HEAD, MASK),
    ]


def unpack(flat):
    weights = {}
    biases = {}
    offset = 0
    table = shapes()
    for name, height, width in table:
        weights[name] = flat[offset // LANES : (offset + height * width) // LANES].reshape(height, width)
        offset = offset + height * width
    rest = flat[offset // LANES :].reshape(-1)
    offset = 0
    for name, height, width in table:
        biases[name] = rest[offset : offset + width].astype(jnp.float32)
        offset = offset + width
    return (weights, biases)


def pack(grads, total):
    table = shapes()
    rows = [grads[entry[0]][0].astype(jnp.bfloat16).reshape(-1, LANES) for entry in table]
    biases = jnp.concatenate([grads[entry[0]][1] for entry in table]).astype(jnp.bfloat16)
    left = total * LANES - sum(entry[1] * entry[2] for entry in table) - biases.shape[0]
    return jnp.concatenate(rows + [jnp.pad(biases, (0, left)).reshape(-1, LANES)])


def patches(padded, tall, wide):
    out_rows = padded.shape[1] - tall + 1
    out_columns = padded.shape[2] - wide + 1
    return jnp.concatenate(
        [
            padded[:, down : down + out_rows, across : across + out_columns]
            for down in range(tall)
            for across in range(wide)
        ],
        axis=-1,
    )


def apply(stacked, weight):
    return jnp.einsum("bhwk,ko->bhwo", stacked, weight, preferred_element_type=jnp.float32)


def apply_back(grad, weight):
    return jnp.einsum("bhwo,ko->bhwk", grad, weight, preferred_element_type=jnp.float32)


def weight_grad(stacked, pre_grad):
    return jnp.einsum("bhwk,bhwo->ko", stacked, pre_grad, preferred_element_type=jnp.float32)


def record(grads, name, stacked, pre_grad):
    grads[name] = (
        weight_grad(stacked, pre_grad),
        jnp.sum(pre_grad, axis=(0, 1, 2), dtype=jnp.float32),
    )


def flipped(weight, tall, wide):
    inner = weight.shape[0] // (tall * wide)
    shaped = weight.reshape(tall, wide, inner, weight.shape[1])[::-1, ::-1]
    return jnp.transpose(shaped, (0, 1, 3, 2)).reshape(-1, inner)


def slope(pre):
    sigma = jax.nn.sigmoid(pre)
    return sigma * (1.0 + pre * (1.0 - sigma))


def local_pad(field, tall, wide):
    return jnp.pad(field, ((0, 0), (tall // 2, tall // 2), (wide // 2, wide // 2), (0, 0)))


def row_pad(field, tall):
    field = with_halo(field, ((SPACE, 1),), tall // 2)
    return jnp.pad(field, ((0, 0), (0, 0), (tall // 2, tall // 2), (0, 0)))


def column_pad(field, tall, wide):
    field = with_halo(field, ((SPACE, 2),), wide // 2)
    return jnp.pad(field, ((0, 0), (tall // 2, tall // 2), (0, 0), (0, 0)))


MESH = pl.DeviceIdType.MESH
LANES = 128
BLOCK = 6144


def quarter_start(rank, count):
    return lax.div(rank * count, LANES)


def quarter_base(rank, count):
    return lax.div(rank * count, LANES * 16) * 16


def mate_of(rank):
    return rank + 1 - 2 * lax.rem(rank, 2)


def remote(src, dst, send, recv, device):
    return pltpu.make_async_remote_copy(
        src_ref=src, dst_ref=dst, send_sem=send, recv_sem=recv, device_id=device, device_id_type=MESH
    )


def greet(devices):
    barrier = pltpu.get_barrier_semaphore()
    for device in devices:
        pl.semaphore_signal(barrier, inc=1, device_id=device, device_id_type=MESH)
    pl.semaphore_wait(barrier, len(devices))


def lane_matrix(shift, forward):
    source = lax.broadcasted_iota(jnp.int32, (LANES, 2 * LANES), 0)
    target = lax.broadcasted_iota(jnp.int32, (LANES, 2 * LANES), 1)
    if forward:
        return jnp.where(target == source + shift, 1.0, 0.0).astype(jnp.bfloat16)
    return jnp.where(lax.rem(target + LANES, 2 * LANES) == source - shift + LANES, 1.0, 0.0).astype(jnp.bfloat16)


def gather_kernel(count, local_ref, out_ref, own_ref, send, recv):
    rank, spot = lax.axis_index(DP), lax.axis_index(SPACE)
    mate, across, twin = mate_of(rank), lax.rem(rank + 2, 4), mate_of(spot)
    pieces = 4
    rows = BLOCK // 2 // pieces
    peers = ({DP: mate}, {DP: across}, {SPACE: twin})
    greet(peers)
    matrix = lane_matrix(lax.rem(rank * count, LANES), True)
    first = lax.broadcasted_iota(jnp.int32, (256, LANES), 0) == 0

    def rotate(step, carry):
        at = pl.ds(pl.multiple_of(step * 256, 256), 256)
        both = jnp.dot(local_ref[at, :], matrix, preferred_element_type=jnp.float32)
        spill = pltpu.roll(both[:, LANES:], 1, 0)
        own_ref[at, :] = (both[:, :LANES] + jnp.where(first, carry, spill)).astype(jnp.bfloat16)
        return spill[0:1]

    lax.fori_loop(0, BLOCK // 256, rotate, jnp.zeros((1, LANES), jnp.float32))

    half, other_half = lax.rem(spot, 2), lax.rem(spot + 1, 2)

    def piece(which, index):
        return pl.ds(pl.multiple_of(which * (BLOCK // 2) + index * rows, 16), rows)

    own_x = [
        remote(own_ref.at[piece(half, k)], out_ref.at[rank, piece(half, k)], send.at[0, k], recv.at[0, k], peers[1])
        for k in range(pieces)
    ]
    own_c = remote(own_ref, out_ref.at[rank], send.at[4, 0], recv.at[4, 0], peers[0])
    for copy in own_x:
        copy.start()
    own_c.start()
    later = []
    for k in range(pieces):
        own_x[k].wait_recv()
        block = out_ref.at[across, piece(half, k)]
        to_twin = remote(block, block, send.at[1, k], recv.at[1, k], peers[2])
        to_mate = remote(block, block, send.at[2, k], recv.at[2, k], peers[0])
        to_twin.start()
        to_mate.start()
        later.append((to_twin, to_mate))
    for at in range(BLOCK // 256):
        out_ref[rank, at * 256 : (at + 1) * 256, :] = own_ref[at * 256 : (at + 1) * 256, :]
    for k in range(pieces):
        later[k][0].wait_recv()
        block = out_ref.at[across, piece(other_half, k)]
        to_mate = remote(block, block, send.at[3, k], recv.at[3, k], peers[0])
        to_mate.start()
        later.append((to_mate,))
    for k in range(pieces):
        own_x[k].wait_send()
        later[k][0].wait_send()
        later[k][1].wait()
        later[pieces + k][0].wait()
    own_c.wait()


def gather_blocks(params):
    count = params.shape[0]
    local = jnp.pad(params, (0, BLOCK * LANES - count)).reshape(BLOCK, LANES)
    return pl.pallas_call(
        functools.partial(gather_kernel, count),
        out_shape=jax.ShapeDtypeStruct((4, BLOCK, LANES), jnp.bfloat16),
        in_specs=[pl.BlockSpec(memory_space=pltpu.VMEM)],
        out_specs=pl.BlockSpec(memory_space=pltpu.VMEM),
        scratch_shapes=[
            pltpu.VMEM((BLOCK, LANES), jnp.bfloat16),
            pltpu.SemaphoreType.DMA((5, 4)),
            pltpu.SemaphoreType.DMA((5, 4)),
        ],
        compiler_params=pltpu.CompilerParams(
            collective_id=0, has_side_effects=True, vmem_limit_bytes=32 * 2**20
        ),
    )(local)


def gather_params(params):
    count = params.shape[0]
    blocks = gather_blocks(params)
    pieces = []
    reach = 0
    for rank in range(4):
        start = rank * count // LANES
        stop = -(-(rank + 1) * count // LANES)
        head = blocks[rank, :1] if rank == 0 else blocks[rank, :1] + pieces.pop()
        pieces += [head, blocks[rank, 1 : stop - start - 1], blocks[rank, stop - start - 1 : stop - start]]
    return jnp.concatenate(pieces)


def reduce_kernel(count, space, pieces, grads_ref, out_ref, rc, tx, rx, acc, ty, ry, tz, rz, gath, send, recv, zsend, zrecv):
    rank, spot = lax.axis_index(DP), lax.axis_index(SPACE)
    mate, across, twin = mate_of(rank), lax.rem(rank + 2, 4), mate_of(spot)
    group = space // 2
    side, depth = lax.rem(spot, 2), lax.div(spot, 2)
    rows = BLOCK // pieces
    half = rows // 2
    part = half // group

    def partner(step):
        return lax.rem(depth + step, group)

    peers = [{DP: mate}, {DP: across}, {SPACE: twin}]
    barrier = pltpu.get_barrier_semaphore()
    for device in peers:
        pl.semaphore_signal(barrier, inc=1, device_id=device, device_id_type=MESH)

    def hello(step, carry):
        pl.semaphore_signal(barrier, inc=1, device_id={SPACE: partner(step) * 2 + side}, device_id_type=MESH)
        return carry

    lax.fori_loop(1, group, hello, 0)
    pl.semaphore_wait(barrier, 3 + group - 1)

    gath[BLOCK:, :] = jnp.zeros((32, LANES), jnp.bfloat16)
    lower = lax.rem(rank, 2)
    upper = lax.div(rank, 2)

    def base(who):
        return pl.multiple_of(quarter_base(who, count), 16)

    def rows_of(start, index, length):
        return pl.ds(pl.multiple_of(start + index, 16), length)

    core = []
    for p in range(pieces):
        for high in range(2):
            copy = remote(
                grads_ref.at[rows_of(base(2 * high + 1 - lower), p * rows, rows)],
                rc.at[p, high],
                send.at[high, p],
                recv.at[high, p],
                peers[0],
            )
            copy.start()
            core.append(copy)
    step_rows = 192 if half % 192 == 0 else 16
    xs, ys, gs = [], [], []

    def z_copy(p, step):
        to = partner(step)
        return remote(
            tz.at[p, pl.ds(pl.multiple_of(to * part, 16), part)],
            rz.at[p, pl.ds(pl.multiple_of(depth * part, 16), part)],
            zsend.at[0, p, step],
            zrecv.at[0, p, step],
            {SPACE: to * 2 + side},
        )

    def home(p, which, slot):
        return pl.ds(pl.multiple_of(p * rows + which * half + slot * part, 16), part)

    def g_copy(p, step):
        block = gath.at[home(p, side, depth)]
        return remote(block, block, zsend.at[1, p, step], zrecv.at[1, p, step], {SPACE: partner(step) * 2 + side})

    def each(body):
        def run(step, carry):
            body(step)
            return carry

        lax.fori_loop(1, group, run, 0)

    def stage_core(p):
        core[2 * p].wait_recv()
        core[2 * p + 1].wait_recv()
        far = 1 - upper

        def add(step, carry):
            at = pl.multiple_of(step * step_rows, 16)
            mine = grads_ref[rows_of(base(2 * far + lower), p * rows + at, step_rows), :].astype(jnp.float32)
            tx[p, pl.ds(at, step_rows), :] = (
                mine + rc[p, far, pl.ds(at, step_rows), :].astype(jnp.float32)
            ).astype(jnp.bfloat16)
            return carry

        lax.fori_loop(0, rows // step_rows, add, 0)
        copy = remote(tx.at[p], rx.at[p], send.at[2, p], recv.at[2, p], peers[1])
        copy.start()
        xs.append(copy)

    def stage_x(p):
        xs[p].wait_recv()

        def total(at):
            return (
                grads_ref[rows_of(base(rank), p * rows + at, step_rows), :].astype(jnp.float32)
                + rc[p, upper, pl.ds(at, step_rows), :].astype(jnp.float32)
                + rx[p, pl.ds(at, step_rows), :].astype(jnp.float32)
            )

        def add(step, carry):
            at = pl.multiple_of(step * step_rows, 16)
            far = pl.multiple_of((1 - side) * half + at, 16)
            near = pl.multiple_of(side * half + at, 16)
            ty[p, pl.ds(at, step_rows), :] = total(far).astype(jnp.bfloat16)
            acc[p, pl.ds(at, step_rows), :] = total(near)
            return carry

        lax.fori_loop(0, half // step_rows, add, 0)
        copy = remote(ty.at[p], ry.at[p], send.at[3, p], recv.at[3, p], peers[2])
        copy.start()
        ys.append(copy)

    def stage_y(p):
        ys[p].wait_recv()

        def add(step, carry):
            at = pl.ds(pl.multiple_of(step * step_rows, 16), step_rows)
            value = acc[p, at, :] + ry[p, at, :].astype(jnp.float32)
            acc[p, at, :] = value
            tz[p, at, :] = value.astype(jnp.bfloat16)
            return carry

        lax.fori_loop(0, half // step_rows, add, 0)
        each(lambda step: z_copy(p, step).start())

    def stage_z(p):
        each(lambda step: z_copy(p, step).wait_recv())
        value = acc[p, pl.ds(pl.multiple_of(depth * part, 16), part), :]

        def add(step, value):
            other = lax.rem(depth + group - step, group)
            return value + rz[p, pl.ds(pl.multiple_of(other * part, 16), part), :].astype(jnp.float32)

        value = lax.fori_loop(1, group, add, value)
        gath[home(p, side, depth), :] = value.astype(jnp.bfloat16)
        each(lambda step: g_copy(p, step).start())

    def stage_zg(p):
        each(lambda step: g_copy(p, step).wait_recv())
        block = gath.at[pl.ds(pl.multiple_of(p * rows + side * half, 16), half)]
        copy = remote(block, block, send.at[4, p], recv.at[4, p], peers[2])
        copy.start()
        gs.append(copy)

    def stage_yg(p):
        gs[p].wait_recv()

    stages = [stage_core, stage_x, stage_y, stage_z, stage_zg, stage_yg]
    for tick in range(pieces + len(stages) - 1):
        for number in reversed(range(len(stages))):
            if 0 <= tick - number < pieces:
                stages[number](tick - number)

    for copy in core + xs + ys + gs:
        copy.wait_send()
    for p in range(pieces):

        def done(step):
            z_copy(p, step).wait_send()
            g_copy(p, step).wait_send()

        each(done)

    offset = rank * count - quarter_base(rank, count) * LANES
    skip = lax.div(offset, LANES)
    matrix = lane_matrix(lax.rem(offset, LANES), False)
    wide = jnp.where(
        lax.broadcasted_iota(jnp.int32, (256, 288), 1)
        == lax.broadcasted_iota(jnp.int32, (256, 288), 0) + skip,
        1.0,
        0.0,
    ).astype(jnp.bfloat16)
    wide_next = jnp.where(
        lax.broadcasted_iota(jnp.int32, (256, 288), 1)
        == lax.broadcasted_iota(jnp.int32, (256, 288), 0) + skip + 1,
        1.0,
        0.0,
    ).astype(jnp.bfloat16)

    def place(step, carry):
        at = pl.multiple_of(step * 256, 256)
        block = gath[pl.ds(at, 288), :]
        both = jnp.dot(block, matrix, preferred_element_type=jnp.float32).astype(jnp.bfloat16)
        out_ref[pl.ds(at, 256), :] = jnp.dot(wide, both[:, :LANES], preferred_element_type=jnp.float32) + jnp.dot(
            wide_next, both[:, LANES:], preferred_element_type=jnp.float32
        )
        return carry

    lax.fori_loop(0, BLOCK // 256, place, 0)


def reduce_grads(flat, space, count):
    pieces = next(k for k in (4, 2, 1) if BLOCK // (k * space) % 16 == 0)
    rows = BLOCK // pieces
    half = rows // 2
    out = pl.pallas_call(
        functools.partial(reduce_kernel, count, space, pieces),
        out_shape=jax.ShapeDtypeStruct((BLOCK, LANES), jnp.float32),
        in_specs=[pl.BlockSpec(memory_space=pltpu.VMEM)],
        out_specs=pl.BlockSpec(memory_space=pltpu.VMEM),
        scratch_shapes=[
            pltpu.VMEM((pieces, 2, rows, LANES), jnp.bfloat16),
            pltpu.VMEM((pieces, rows, LANES), jnp.bfloat16),
            pltpu.VMEM((pieces, rows, LANES), jnp.bfloat16),
            pltpu.VMEM((pieces, half, LANES), jnp.float32),
            pltpu.VMEM((pieces, half, LANES), jnp.bfloat16),
            pltpu.VMEM((pieces, half, LANES), jnp.bfloat16),
            pltpu.VMEM((pieces, half, LANES), jnp.bfloat16),
            pltpu.VMEM((pieces, half, LANES), jnp.bfloat16),
            pltpu.VMEM((BLOCK + 32, LANES), jnp.bfloat16),
            pltpu.SemaphoreType.DMA((5, pieces)),
            pltpu.SemaphoreType.DMA((5, pieces)),
            pltpu.SemaphoreType.DMA((2, pieces, space // 2)),
            pltpu.SemaphoreType.DMA((2, pieces, space // 2)),
        ],
        compiler_params=pltpu.CompilerParams(
            collective_id=1, has_side_effects=True, vmem_limit_bytes=48 * 2**20
        ),
    )(flat)
    return out.reshape(-1)[:count]


def gru_forward(state, inputs, weights, biases, gate_name, candidate_name, tall, wide, padder):
    joined_stack = patches(padder(jnp.concatenate([state, inputs], -1), tall, wide), tall, wide)
    gates = jax.nn.sigmoid(apply(joined_stack, weights[gate_name]) + biases[gate_name])
    hidden = state.shape[-1]
    update = gates[..., :hidden]
    reset = gates[..., hidden:]
    state_wide = state.astype(jnp.float32)
    mixed = jnp.concatenate([(reset * state_wide).astype(jnp.bfloat16), inputs], -1)
    mixed_stack = patches(padder(mixed, tall, wide), tall, wide)
    candidate = jnp.tanh(apply(mixed_stack, weights[candidate_name]) + biases[candidate_name])
    result = state_wide + update * (candidate - state_wide)
    return (result, (joined_stack, mixed_stack, update, reset, candidate, state_wide))


def gru_backward(result_grad, kept, weights, grads, gate_name, candidate_name, tall, wide, padder):
    joined_stack, mixed_stack, update, reset, candidate, state_wide = kept
    hidden = update.shape[-1]
    candidate_grad = (result_grad * update * (1.0 - candidate * candidate)).astype(jnp.bfloat16)
    record(grads, candidate_name, mixed_stack, candidate_grad)
    mixed_grad = apply(
        patches(padder(candidate_grad, tall, wide), tall, wide),
        flipped(weights[candidate_name], tall, wide),
    )
    reset_grad = mixed_grad[..., :hidden]
    gate_grad = jnp.concatenate(
        [
            result_grad * (candidate - state_wide) * update * (1.0 - update),
            reset_grad * state_wide * reset * (1.0 - reset),
        ],
        -1,
    ).astype(jnp.bfloat16)
    record(grads, gate_name, joined_stack, gate_grad)
    joined_grad = apply(
        patches(padder(gate_grad, tall, wide), tall, wide), flipped(weights[gate_name], tall, wide)
    )
    state_grad = result_grad * (1.0 - update) + reset_grad * reset + joined_grad[..., :hidden]
    inputs_grad = joined_grad[..., hidden:] + mixed_grad[..., hidden:]
    return (state_grad, inputs_grad)


def shards(net, context, corr, flow, target, valid, grad_net, grad_mask, params):
    flow_start = CTX + MOT - 2
    plane = jnp.float32(target.shape[2] * net.shape[2])
    counts = lax.psum(jnp.sum(valid, axis=(1, 2)).astype(jnp.float32), SPACE)
    divisor = jnp.maximum(counts, 1.0)
    weights, biases = unpack(gather_params(params))
    grads = {}
    flow_rows = jnp.transpose(flow, (0, 2, 3, 1))
    corr_pre = apply(corr, weights[CORR_IN]) + biases[CORR_IN]
    corr_one = jax.nn.silu(corr_pre).astype(jnp.bfloat16)
    corr_stack = patches(row_pad(corr_one, 3), 3, 3)
    corr_mix_pre = apply(corr_stack, weights[CORR_MIX]) + biases[CORR_MIX]
    corr_two = jax.nn.silu(corr_mix_pre).astype(jnp.bfloat16)
    flow_stack = patches(row_pad(flow_rows, 7), 7, 7)
    flow_pre = apply(flow_stack, weights[FLOW_IN]) + biases[FLOW_IN]
    flow_one = jax.nn.silu(flow_pre).astype(jnp.bfloat16)
    flow_mix_stack = patches(row_pad(flow_one, 3), 3, 3)
    flow_mix_pre = apply(flow_mix_stack, weights[FLOW_MIX]) + biases[FLOW_MIX]
    flow_two = jax.nn.silu(flow_mix_pre).astype(jnp.bfloat16)
    joint_stack = patches(row_pad(jnp.concatenate([corr_two, flow_two], -1), 3), 3, 3)
    motion_pre = apply(joint_stack, weights[MOTION_MIX]) + biases[MOTION_MIX]
    motion = jax.nn.silu(motion_pre).astype(jnp.bfloat16)
    inputs = jnp.concatenate([context, motion, flow_rows], -1)
    state, rows_kept = gru_forward(
        net, inputs, weights, biases, ROWS_GATES, ROWS_CANDIDATE, 1, 5, local_pad
    )
    state_columns, inputs_columns = (
        lax.all_to_all(
            state.astype(jnp.bfloat16), SPACE, split_axis=2, concat_axis=1, tiled=True
        ),
        lax.all_to_all(inputs, SPACE, split_axis=2, concat_axis=1, tiled=True),
    )
    target_here = jnp.transpose(target, (0, 2, 3, 1))
    valid_here = valid.astype(jnp.float32)
    net_cotangent = grad_net
    mask_cotangent = grad_mask
    final, columns_kept = gru_forward(
        state_columns,
        inputs_columns,
        weights,
        biases,
        COLUMNS_GATES,
        COLUMNS_CANDIDATE,
        5,
        1,
        local_pad,
    )
    final_low = final.astype(jnp.bfloat16)
    heads_weight = jnp.concatenate([weights[FLOW_HIDDEN], weights[MASK_HIDDEN]], 1)
    heads_bias = jnp.concatenate([biases[FLOW_HIDDEN], biases[MASK_HIDDEN]])
    net_stack = patches(column_pad(final_low, 3, 3), 3, 3)
    heads_pre = apply(net_stack, heads_weight) + heads_bias
    heads_act = jax.nn.silu(heads_pre).astype(jnp.bfloat16)
    flow_features = heads_act[..., :HEAD]
    mask_features = heads_act[..., HEAD:]
    hidden_stack = patches(column_pad(flow_features, 3, 3), 3, 3)
    delta = apply(hidden_stack, weights[FLOW_OUT]) + biases[FLOW_OUT]
    mask_full = 0.25 * (apply(mask_features, weights[MASK_OUT]) + biases[MASK_OUT])
    new_flow = inputs_columns[..., flow_start:].astype(jnp.float32) + delta
    error = new_flow - target_here
    root = jnp.sqrt(error * error + 1.0)
    partials = jnp.sum(valid_here * jnp.sum(root, axis=-1), axis=(1, 2))
    flow_grad = plane / divisor[:, None, None, None] * valid_here[..., None] * error / root
    mask_low = mask_full.astype(jnp.bfloat16)
    nets_out = final_low
    flows_out = jnp.transpose(new_flow, (0, 3, 1, 2))
    masks_out = mask_low
    delta_grad = flow_grad.astype(jnp.bfloat16)
    mask_grad = (0.25 * mask_cotangent.astype(jnp.float32)).astype(jnp.bfloat16)
    record(grads, MASK_OUT, mask_features, mask_grad)
    record(grads, FLOW_OUT, hidden_stack, delta_grad)
    from_flow = apply(
        patches(column_pad(delta_grad, 3, 3), 3, 3), flipped(weights[FLOW_OUT], 3, 3)
    )
    from_mask = apply_back(mask_grad, weights[MASK_OUT])
    heads_grad = (jnp.concatenate([from_flow, from_mask], -1) * slope(heads_pre)).astype(
        jnp.bfloat16
    )
    heads_wgrad = weight_grad(net_stack, heads_grad)
    heads_bgrad = jnp.sum(heads_grad, axis=(0, 1, 2), dtype=jnp.float32)
    grads[FLOW_HIDDEN] = (heads_wgrad[:, :HEAD], heads_bgrad[:HEAD])
    grads[MASK_HIDDEN] = (heads_wgrad[:, HEAD:], heads_bgrad[HEAD:])
    final_grad = net_cotangent.astype(jnp.float32) + apply(
        patches(column_pad(heads_grad, 3, 3), 3, 3), flipped(heads_weight, 3, 3)
    )
    state_grad_columns, inputs_grad_columns = gru_backward(
        final_grad,
        columns_kept,
        weights,
        grads,
        COLUMNS_GATES,
        COLUMNS_CANDIDATE,
        5,
        1,
        local_pad,
    )
    inputs_grad_columns = jnp.concatenate(
        [
            inputs_grad_columns[..., :flow_start],
            inputs_grad_columns[..., flow_start:] + flow_grad,
        ],
        -1,
    )
    state_back, inputs_back = (
        lax.all_to_all(
            state_grad_columns.astype(jnp.bfloat16),
            SPACE,
            split_axis=1,
            concat_axis=2,
            tiled=True,
        ),
        lax.all_to_all(
            inputs_grad_columns.astype(jnp.bfloat16),
            SPACE,
            split_axis=1,
            concat_axis=2,
            tiled=True,
        ),
    )
    net_grad, inputs_grad = gru_backward(
        state_back.astype(jnp.float32),
        rows_kept,
        weights,
        grads,
        ROWS_GATES,
        ROWS_CANDIDATE,
        1,
        5,
        local_pad,
    )
    inputs_total = inputs_grad + inputs_back.astype(jnp.float32)
    motion_grad = (inputs_total[..., CTX:flow_start] * slope(motion_pre)).astype(jnp.bfloat16)
    record(grads, MOTION_MIX, joint_stack, motion_grad)
    joint_grad = apply(
        patches(row_pad(motion_grad, 3), 3, 3), flipped(weights[MOTION_MIX], 3, 3)
    )
    branch_grad = jnp.concatenate(
        [
            joint_grad[..., :C2] * slope(corr_mix_pre),
            joint_grad[..., C2:] * slope(flow_mix_pre),
        ],
        -1,
    ).astype(jnp.bfloat16)
    record(grads, CORR_MIX, corr_stack, branch_grad[..., :C2])
    record(grads, FLOW_MIX, flow_mix_stack, branch_grad[..., C2:])
    branch_pad = row_pad(branch_grad, 3)
    corr_one_grad = apply(
        patches(branch_pad[..., :C2], 3, 3), flipped(weights[CORR_MIX], 3, 3)
    )
    flow_one_grad = apply(
        patches(branch_pad[..., C2:], 3, 3), flipped(weights[FLOW_MIX], 3, 3)
    )
    corr_pre_grad = (corr_one_grad * slope(corr_pre)).astype(jnp.bfloat16)
    flow_pre_grad = (flow_one_grad * slope(flow_pre)).astype(jnp.bfloat16)
    record(grads, CORR_IN, corr, corr_pre_grad)
    record(grads, FLOW_IN, flow_stack, flow_pre_grad)
    corr_grads = apply_back(corr_pre_grad, weights[CORR_IN])
    flow_total = inputs_total[..., flow_start:] + apply(
        patches(row_pad(flow_pre_grad, 7), 7, 7), flipped(weights[FLOW_IN], 7, 7)
    )
    flow_grads = jnp.transpose(flow_total, (0, 3, 1, 2))
    net_grads = net_grad
    context_grads = inputs_total[..., :CTX]
    count = params.shape[0]
    local = pack(grads, 3 * count // (LANES * 16) * 16 + BLOCK)
    collected = reduce_grads(local, lax.axis_size(SPACE), count)
    losses = lax.psum(partials, SPACE) / divisor
    return (
        nets_out,
        flows_out,
        masks_out,
        losses,
        collected,
        net_grads,
        context_grads,
        corr_grads,
        flow_grads,
    )


BATCH = 2
ROWS = 5
WIDE = 128
TALL = 40
COLS = 16
AREA = 640
PITCH = 20
SPREAD = TALL * PITCH
SPAN = 896
EDGE = 64


def mm(a, b):
    return jnp.dot(a, b, preferred_element_type=jnp.float32)


def nt(a, b):
    return lax.dot_general(a, b, (((1,), (1,)), ((), ())), preferred_element_type=jnp.float32)


def tn(a, b):
    return lax.dot_general(a, b, (((0,), (0,)), ((), ())), preferred_element_type=jnp.float32)


def half_of(value):
    return value.astype(jnp.bfloat16)


def full_of(value):
    return value.astype(jnp.float32)


def join(parts, axis=1):
    return jnp.concatenate(list(parts), axis=axis)


def quarter_of(value):
    return half_of(0.25 * full_of(value))


def lane_index(shape):
    return lax.broadcasted_iota(jnp.int32, shape, 1)


def row_index(shape):
    return lax.broadcasted_iota(jnp.int32, shape, 0)


def act_slope(pre):
    sigma = jax.nn.sigmoid(pre)
    act = pre * sigma
    return act, sigma + act * (1.0 - sigma)


def flat_rows():
    table = shapes()
    offset = 0
    starts = {}
    for name, height, width in table:
        starts[name] = offset // LANES
        offset += height * width
    bias_row = offset // LANES
    spots = {}
    inner = 0
    for name, height, width in table:
        spots[name] = inner
        inner += width
    return starts, bias_row, spots, inner


def cast_rows(dst, to, src, start, count, kind):
    big = 256
    whole = count // big

    if whole > 1:

        def body(step, carry):
            at = pl.multiple_of(step * big, big)
            dst[pl.ds(to + at, big), :] = src[pl.ds(start + at, big), :].astype(kind)
            return carry

        lax.fori_loop(0, whole, body, 0)
    elif whole == 1:
        dst[to : to + big, :] = src[start : start + big, :].astype(kind)
    rest = count - whole * big
    if rest:
        low = whole * big
        dst[to + low : to + count, :] = src[start + low : start + count, :].astype(kind)


MARGIN = 16


def stage_plan(count, start, rows):
    stop = start + rows
    pieces, fill = [], 0
    for rank in range(4):
        first = rank * count // LANES
        last = -(-(rank + 1) * count // LANES)
        low, high = max(start, first), min(stop, last)
        if low >= high:
            continue
        place = low - first + rank * BLOCK
        base = place // 16 * 16
        length = -(-(place - base + high - low) // 16) * 16
        to = MARGIN + low - start - (place - base)
        seam = MARGIN + low - start if start < first else None
        pieces.append((base, length, fill, to, seam))
        fill += length
    return pieces


class Stages:
    def __init__(self, v, count, segments):
        self.v, self.at = v, 0
        self.plans = [stage_plan(count, start, rows) for start, rows in segments]
        self.fetch(0)

    def copies(self, index):
        v, slot = self.v, index % 2
        return [
            pltpu.make_async_copy(
                v.out_all.at[base : base + length], v.stage.at[slot, fill : fill + length], v.ssem.at[slot, number]
            )
            for number, (base, length, fill, to, seam) in enumerate(self.plans[index])
        ]

    def fetch(self, index):
        if index < len(self.plans):
            for copy in self.copies(index):
                copy.start()

    def take(self):
        v, index = self.v, self.at
        self.at += 1
        for copy in self.copies(index):
            copy.wait()
        self.fetch(index + 1)
        for base, length, fill, to, seam in self.plans[index]:
            saved = None if seam is None else v.flat[seam : seam + 1, :]
            cast_rows(v.flat, to, v.stage.at[index % 2], fill, length, jnp.float32)
            if seam is not None:
                v.flat[seam : seam + 1, :] = v.flat[seam : seam + 1, :] + saved


def strided(ref, start, count, stride):
    if stride == 1:
        return ref[pl.ds(start, count), :]
    return ref[pl.ds(start, count, stride=stride), :]


def unpack_pairs(flat, row, count, dst, to, lane):
    dst[to : to + count, lane : lane + LANES] = half_of(strided(flat, MARGIN + 2 * row, count, 2))
    dst[to : to + count, lane + LANES : lane + 2 * LANES] = half_of(strided(flat, MARGIN + 2 * row + 1, count, 2))


def pack_pairs(flat, row, count, low, high):
    flat[pl.ds(MARGIN + 2 * row, count, stride=2), :] = low
    flat[pl.ds(MARGIN + 2 * row + 1, count, stride=2), :] = high


def split_pick(which, quarter):
    source = lax.broadcasted_iota(jnp.int32, (LANES, HEAD), 0)
    target = lax.broadcasted_iota(jnp.int32, (LANES, HEAD), 1)
    return jnp.where(source == 2 * (target - 64 * quarter) + which, 1.0, 0.0).astype(jnp.bfloat16)


UNPACK = (
    (CORR_IN, 648), (CORR_MIX, 3456), (FLOW_IN, 98), (FLOW_MIX, 576), (MOTION_MIX, 2268),
    (ROWS_GATES, 3840), (ROWS_CANDIDATE, 1920), (None, 21), (COLUMNS_GATES, 3840), (COLUMNS_CANDIDATE, 1920),
    (FLOW_HIDDEN, 2304), (MASK_HIDDEN, 2304), (FLOW_OUT, 36), (MASK_OUT, 1152),
)


def stage_of(v, name, rows):
    assert UNPACK[v.stages.at] == (name, rows)
    v.stages.take()


def unpack_gru(v, gates_name, cand_name, w_i, w_s):
    flat = v.flat
    stage_of(v, gates_name, 3840)
    for tap in range(5):
        unpack_pairs(flat, tap * 384, 128, w_s, tap * 128, 0)
        unpack_pairs(flat, tap * 384 + 128, 256, w_i, tap * 256, 0)
    stage_of(v, cand_name, 1920)
    for tap in range(5):
        w_s[tap * 128 : (tap + 1) * 128, 256:384] = half_of(strided(flat, MARGIN + tap * 384, 128, 1))
        w_i[tap * 256 : (tap + 1) * 256, 256:384] = half_of(strided(flat, MARGIN + tap * 384 + 128, 256, 1))


def unpack_encoder(v, count):
    starts, bias_row, spots, inner = flat_rows()
    flat = v.flat
    v.stages = Stages(v, count, [(bias_row if name is None else starts[name], rows) for name, rows in UNPACK])

    def stage(name, rows):
        stage_of(v, name, rows)

    stage(CORR_IN, 648)
    unpack_pairs(flat, 0, 324, v.w_ci, 0, 0)

    stage(CORR_MIX, 3456)
    lane = lane_index((128, LANES))
    low_half = lane < 64

    def mix_step(step, carry):
        at = MARGIN + 384 * step
        r0, r1, r2 = (strided(flat, at + i, 128, 3) for i in range(3))
        r1s, r2s = pltpu.roll(r1, 64, 1), pltpu.roll(r2, 64, 1)
        v.pair_a[pl.ds(0, 128, stride=2), :] = r0
        v.pair_a[pl.ds(1, 128, stride=2), :] = jnp.where(low_half, r1s, r2s)
        v.pair_b[pl.ds(0, 128, stride=2), :] = jnp.where(low_half, r1, 0.0)
        v.pair_b[pl.ds(1, 128, stride=2), :] = jnp.where(low_half, r2s, 0.0)
        to = pl.ds(pl.multiple_of(step * 256, 256), 256)
        v.w_cm[to, 0:128] = half_of(v.pair_a[...])
        v.w_cm[to, 128:256] = half_of(v.pair_b[...])
        return carry

    lax.fori_loop(0, 9, mix_step, 0)

    stage(FLOW_IN, 98)
    v.flow_tmp[...] = jnp.zeros_like(v.flow_tmp)
    for across in range(7):
        for comp in range(2):
            v.flow_tmp[pl.ds(across * 16 + comp, 7, stride=2), :] = strided(
                flat, MARGIN + across * 2 + comp, 7, 14
            )
    v.w_fi[...] = half_of(v.flow_tmp[...])

    stage(FLOW_MIX, 576)
    for step in range(9):
        r0 = strided(flat, MARGIN + 64 * step, 64, 1)
        high_half = lane_index((64, LANES)) >= 64
        v.pair_a[pl.ds(0, 64, stride=2), :] = jnp.where(high_half, pltpu.roll(r0, 64, 1), 0.0)
        v.pair_a[pl.ds(1, 64, stride=2), :] = jnp.where(high_half, r0, 0.0)
        v.w_fm[step * 128 : (step + 1) * 128, :] = half_of(v.pair_a[0:128, :])

    stage(MOTION_MIX, 2268)
    lane36 = lane_index((36, LANES))
    for i in range(64):
        if i == 0:
            value = strided(flat, MARGIN, 36, 63)
        elif i == 63:
            value = pltpu.roll(strided(flat, MARGIN + 62, 36, 63), 126, 1)
        else:
            low = pltpu.roll(strided(flat, MARGIN + i - 1, 36, 63), 2 * i, 1)
            high = pltpu.roll(strided(flat, MARGIN + i, 36, 63), 2 * i, 1)
            value = jnp.where(lane36 < 2 * i, low, high)
        v.mm_tmp[pl.ds(i, 36, stride=64), :] = jnp.where(lane36 < 126, value, 0.0)
    for step in range(9):
        v.w_mm[step * 256 : (step + 1) * 256, :] = half_of(v.mm_tmp[step * 256 : (step + 1) * 256, :])

    unpack_gru(v, ROWS_GATES, ROWS_CANDIDATE, v.w_ri, v.w_rs)

    stage(None, 21)
    place = 0
    lane1 = lane_index((1, LANES))
    for name, height, width in shapes():
        spot = spots[name]
        for block in range(-(-width // LANES)):
            at = spot + block * LANES
            row, shift = at // LANES, at % LANES
            value = flat[MARGIN + row : MARGIN + row + 1, :]
            if shift:
                after = flat[MARGIN + row + 1 : MARGIN + row + 2, :]
                value = jnp.where(
                    lane1 < LANES - shift, pltpu.roll(value, LANES - shift, 1), pltpu.roll(after, LANES - shift, 1)
                )
            left = width - block * LANES
            if left < LANES:
                value = jnp.where(lane1 < left, value, 0.0)
            if name == FLOW_MIX:
                value = pltpu.roll(value, 64, 1)
            v.bias[place : place + 1, :] = value
            place += 1


def unpack_heads(v):
    flat = v.flat
    low_half = lane_index((128, LANES)) < 64

    def stage(name, rows):
        stage_of(v, name, rows)

    unpack_gru(v, COLUMNS_GATES, COLUMNS_CANDIDATE, v.w_li, v.w_ls)

    for name, lane0 in ((FLOW_HIDDEN, 0), (MASK_HIDDEN, 256)):
        stage(name, 2304)
        for tap in range(9):
            unpack_pairs(flat, tap * 128, 128, v.w_h, tap * 128, lane0)

    stage(FLOW_OUT, 36)
    v.fo_tmp[...] = jnp.zeros_like(v.fo_tmp)
    for which in range(2):
        total = jnp.zeros((9, HEAD), jnp.float32)
        for quarter in range(4):
            total = total + mm(half_of(strided(flat, MARGIN + quarter, 9, 4)), split_pick(which, quarter))
        v.fo_tmp[pl.ds(which, 9, stride=2), 0:128] = total[:, :128]
        v.fo_tmp2[pl.ds(which, 9, stride=2), 0:128] = total[:, 128:]
    v.fo_tmp2[18:32, :] = jnp.zeros((14, LANES), jnp.float32)
    v.w_fo[:, 0:128] = half_of(v.fo_tmp[...])
    v.w_fo[:, 128:256] = half_of(v.fo_tmp2[...])

    stage(MASK_OUT, 1152)
    r = [strided(flat, MARGIN + i, 128, 9) for i in range(9)]
    rs = [pltpu.roll(r[i], 64, 1) for i in range(4, 9)]
    for block in range(5):
        even = r[block] if block < 4 else jnp.where(low_half, r[4], 0.0)
        odd = jnp.where(low_half, rs[block], rs[block + 1]) if block < 4 else jnp.where(low_half, rs[4], 0.0)
        v.pair_a[pl.ds(0, 128, stride=2), :] = even
        v.pair_a[pl.ds(1, 128, stride=2), :] = odd
        v.w_mo[:, block * 128 : (block + 1) * 128] = half_of(v.pair_a[...])


BIAS_AT = {}
_place = 0
for _name, _height, _width in shapes():
    BIAS_AT[_name] = _place
    _place += -(-_width // 128)
BIAS_ROWS = 32


def bias_of(v, name, blocks):
    at = BIAS_AT[name]
    return jnp.concatenate([v.bias[at + i : at + i + 1, :] for i in range(blocks)], axis=1)


class Halo:
    def __init__(self, v, sem, up_src, down_src, from_down, from_up):
        up = {SPACE: jnp.maximum(v.spot - 1, 0)}
        down = {SPACE: jnp.minimum(v.spot + 1, v.space - 1)}
        self.v = v
        self.up = remote(up_src, from_down, v.hsend.at[sem, 0], v.hrecv.at[sem, 0], up)
        self.down = remote(down_src, from_up, v.hsend.at[sem, 1], v.hrecv.at[sem, 1], down)

    def start(self):
        pl.when(self.v.spot > 0)(self.up.start)
        pl.when(self.v.spot < self.v.space - 1)(self.down.start)

    def receive(self):
        pl.when(self.v.spot < self.v.space - 1)(self.up.wait_recv)
        pl.when(self.v.spot > 0)(self.down.wait_recv)

    def sent(self):
        pl.when(self.v.spot > 0)(self.up.wait_send)
        pl.when(self.v.spot < self.v.space - 1)(self.down.wait_send)


def drain_bytes(ref, sem):
    pltpu.make_async_copy(ref, ref, sem).wait()


class Swap:
    def __init__(self, v, sem, src, dst, broadcast=False):
        self.v, self.sem, self.src, self.dst, self.broadcast = v, sem, src, dst, broadcast

    def start(self, b=None):
        v = self.v

        def body(step, carry):
            to = v.spot + step
            to = jnp.where(to >= v.space, to - v.space, to)
            src = self.src if self.broadcast else self.src.at[to]
            dst = self.dst.at[v.spot]
            if b is not None:
                src, dst = src.at[b], dst.at[b]
            remote(src, dst, v.asend.at[self.sem], v.arecv.at[self.sem], {SPACE: to}).start()
            return carry

        lax.fori_loop(1, v.space, body, 0)

    def receive(self):
        drain_bytes(self.dst.at[0 : self.v.space - 1], self.v.arecv.at[self.sem])

    def sent(self):
        drain_bytes(self.dst.at[0 : self.v.space - 1], self.v.asend.at[self.sem])


def spread_rows(v, b, acts, rows, dst, row0, width, backward=False):
    x = lax.rem(row_index((rows, LANES)), WIDE)
    for block, act in enumerate(acts):
        v.tmp[8 : 8 + rows, :] = act
        for tap in range(3):
            d = (1 - tap) if backward else (tap - 1)
            value = act if d == 0 else v.tmp[8 + d : 8 + d + rows, :]
            if d == -1:
                value = jnp.where(x > 0, value, 0.0)
            if d == 1:
                value = jnp.where(x < WIDE - 1, value, 0.0)
            lane = tap * width + block * LANES
            if backward:
                dst[row0 : row0 + rows, b + lane : b + lane + LANES] = half_of(value)
            else:
                dst[b, row0 : row0 + rows, lane : lane + LANES] = half_of(value)


def spread_five(v, value, dst, lane_of, backward=False):
    x = lax.rem(row_index((AREA, LANES)), WIDE)
    v.tmp[8 : 8 + AREA, :] = value
    for tap in range(5):
        d = (2 - tap) if backward else (tap - 2)
        moved = value if d == 0 else v.tmp[8 + d : 8 + d + AREA, :]
        if d:
            moved = jnp.where((x + d >= 0) & (x + d < WIDE), moved, 0.0)
        if backward:
            taps_part(v, tap, lane_of, lane_of + LANES)[...] = half_of(moved)
        else:
            lane = lane_of(tap)
            dst[:, lane : lane + LANES] = half_of(moved)


def lines_of(ref, b, lines):
    return jnp.concatenate([ref[b, y] for y in range(lines)], axis=1)


def edge_rows(v, value, rows):
    low = jnp.where(v.spot > 0, value[0:rows], 0.0)
    high = jnp.where(v.spot < v.space - 1, value[-rows:], 0.0)
    return jnp.concatenate([low, value[rows:-rows], high], axis=0)


def early_taps(v):
    def flow(b, carry):
        up = jnp.where(v.spot > 0, v.flow_up[b], 0.0)
        down = jnp.where(v.spot < v.space - 1, v.flow_down[b], 0.0)
        lane = lane_index((16, LANES))
        v.fs[...] = jnp.zeros_like(v.fs)
        for across in range(7):
            d = across - 3
            for part, value in enumerate((up, v.flow[b], down)):
                moved = value
                if d:
                    moved = pltpu.roll(value, (-d) % LANES, 1)
                    moved = jnp.where((lane + d >= 0) & (lane + d < WIDE), moved, 0.0)
                v.fs[across, part * 10 : part * 10 + 10, :] = moved[0:10, :]
        for y in range(9):
            for across in range(7):
                v.flow_tmp[across * 16 : across * 16 + 16, :] = v.fs[across, 2 * y : 2 * y + 16, :]
            v.xt[b, :, y * 128 : (y + 1) * 128] = half_of(v.flow_tmp[...])
        return carry

    lax.fori_loop(0, BATCH, flow, 0)

    def image(b, carry):
        at = pl.ds(pl.multiple_of(b * AREA, AREA), AREA)
        spread_five(v, full_of(v.context[b]), v.xi.at[at], lambda t: t * 256)
        spread_five(v, full_of(v.net[b]), v.xs.at[at], lambda t: t * 128)
        return carry

    lax.fori_loop(0, BATCH, image, 0)


def gather_start(v, count):
    pieces = 8
    rows = BLOCK // 2 // pieces
    half = lax.rem(v.spot, 2)
    shift = lax.rem(v.rank * count, LANES)
    chunk = 512
    keep = lane_index((chunk, LANES)) >= shift
    v.tmp[7:8, :] = jnp.zeros((1, LANES), jnp.float32)

    def rotate(step, carry):
        at = pl.ds(pl.multiple_of(step * chunk, chunk), chunk)
        moved = pltpu.roll(full_of(v.gath[at, :]), shift, 1)
        v.tmp[8 : 8 + chunk, :] = moved
        v.gath[at, :] = half_of(jnp.where(keep, moved, v.tmp[7 : 7 + chunk, :]))
        v.tmp[7:8, :] = v.tmp[7 + chunk : 8 + chunk, :]
        return carry

    lax.fori_loop(0, BLOCK // chunk, rotate, 0)

    def piece(rank, which, index):
        return pl.ds(pl.multiple_of(rank * BLOCK + which * (BLOCK // 2) + index * rows, 16), rows)

    mine = pl.ds(pl.multiple_of(v.rank * BLOCK, 16), BLOCK)
    own = v.gath.at[0:BLOCK]
    v.g_x = [
        remote(
            v.gath.at[piece(0, half, k)], v.out_all.at[piece(v.rank, half, k)], v.gsend.at[0, k], v.grecv.at[0, k],
            {DP: v.other},
        )
        for k in range(pieces)
    ]
    v.g_own = remote(own, v.out_all.at[mine], v.gsend.at[4, 0], v.grecv.at[4, 0], {DP: v.mate})
    v.g_here = pltpu.make_async_copy(own, v.out_all.at[mine], v.gsend.at[4, 1])

    def forward(number, which, k, device):
        block = v.out_all.at[piece(v.other, which, k)]
        return remote(block, block, v.gsend.at[number, k], v.grecv.at[number, k], device)

    v.g_twin = [forward(1, half, k, {SPACE: v.twin}) for k in range(pieces)]
    v.g_mate = [forward(2, half, k, {DP: v.mate}) for k in range(pieces)]
    v.g_last = [forward(3, 1 - half, k, {DP: v.mate}) for k in range(pieces)]
    for copy in v.g_x:
        copy.start()
    v.g_own.start()
    v.g_here.start()


def gather_pass(v, first, last):
    for k in range(first, last):
        v.g_x[k].wait_recv()
        v.g_twin[k].start()
        v.g_mate[k].start()


def gather_end(v):
    for k in range(len(v.g_x)):
        v.g_twin[k].wait_recv()
        v.g_last[k].start()
    for k in range(len(v.g_x)):
        v.g_x[k].wait_send()
        v.g_twin[k].wait_send()
        v.g_mate[k].wait()
        v.g_last[k].wait()
    v.g_own.wait()
    v.g_here.wait()


def forward_rows(v):
    spot, last = v.spot, v.space - 1
    def image(b, carry):
        pieces = (
            (v.corr_up, 0, 256, 2, spot > 0),
            (v.corr, 256, 640, 5, None),
            (v.corr_down, 896, 256, 2, spot < last),
        )
        bias = bias_of(v, CORR_IN, 2)
        for ref, row0, rows, lines, seen in pieces:
            act, slope = act_slope(tn(lines_of(ref, b, lines), v.w_ci[...]) + bias)
            if seen is None:
                v.slope_ci[b] = half_of(slope)
            else:
                act = jnp.where(seen, act, 0.0)
            spread_rows(v, b, (act[:, :128], act[:, 128:]), rows, v.hx_c, row0, 256)

        act, slope = act_slope(tn(v.xt[b], v.w_fi[...]) + bias_of(v, FLOW_IN, 1))
        v.slope_fi[b] = half_of(slope[256:896])
        spread_rows(v, b, (edge_rows(v, act, 2 * WIDE),), 9 * WIDE, v.hx_f, 0, 128)

        pre = mm(join(v.hx_c[b, a * 128 : a * 128 + 896, :] for a in range(3)), v.w_cm[...]) + bias_of(v, CORR_MIX, 2)
        flow_pre = mm(join(v.hx_f[b, a * 128 : a * 128 + 896, :] for a in range(3)), v.w_fm[...])
        flow_pre = flow_pre + bias_of(v, FLOW_MIX, 1)
        low, low_slope = act_slope(pre[:, :128])
        high, high_slope = act_slope(pre[:, 128:] + flow_pre)
        v.slope_j[b, :, 0:128] = half_of(low_slope)
        v.slope_j[b, :, 128:256] = half_of(high_slope)
        spread_rows(v, b, (edge_rows(v, low, WIDE), edge_rows(v, high, WIDE)), 896, v.hx_j, 0, 256)

        pre = mm(join(v.hx_j[b, a * 128 : a * 128 + 640, :] for a in range(3)), v.w_mm[...])
        pre = pre + bias_of(v, MOTION_MIX, 1)
        act, slope = act_slope(pre)
        v.slope_m[b] = half_of(jnp.where(lane_index((AREA, LANES)) < 126, slope, 0.0))
        pick = jnp.where(lane_index((16, LANES)) == row_index((16, LANES)) + 126, 1.0, 0.0)
        own_flow = v.flow[b]
        for y in range(ROWS):
            v.tmp2[0:2, :] = own_flow[2 * y : 2 * y + 2, :]
            v.tmp2[2:16, :] = jnp.zeros((14, LANES), jnp.float32)
            v.motion[b, y * 128 : (y + 1) * 128, :] = act[y * 128 : (y + 1) * 128, :] + tn(
                half_of(v.tmp2[0:16, :]), half_of(pick)
            )
        v.motion[b] = full_of(half_of(v.motion[b]))
        pack_rows(v, v.motion, b, v.a_motion)
        v.swap_motion.start(b)
        return carry

    lax.fori_loop(0, BATCH, image, 0)

    def gru(b, carry):
        at = pl.ds(pl.multiple_of(b * AREA, AREA), AREA)
        s = full_of(v.net[b])
        spread_five(v, v.motion[b], v.xi.at[at], lambda t: t * 256 + 128)
        both = mm(v.xi[at, :], v.w_ri[...])
        gates = jax.nn.sigmoid(both[:, :256] + mm(v.xs[at, :], v.w_rs[:, :256]) + bias_of(v, ROWS_GATES, 2))
        update, reset = gates[:, :128], gates[:, 128:]
        v.ru[b] = update
        v.rr[b] = reset
        spread_five(v, full_of(half_of(reset * s)), v.xr.at[at], lambda t: t * 128)
        cand = jnp.tanh(both[:, 256:] + mm(v.xr[at, :], v.w_rs[:, 256:]) + bias_of(v, ROWS_CANDIDATE, 1))
        v.rc[b] = cand
        v.state[b] = s + update * (cand - s)
        pack_rows(v, v.state, b, v.a_state)
        v.swap_state.start(b)
        return carry

    lax.fori_loop(0, BATCH, gru, 0)


def pack_rows(v, src, b, dst):
    def peer(t, carry):
        for y in range(ROWS):
            at = pl.multiple_of(y * WIDE + t * COLS, COLS)
            dst[t, b, y * COLS : (y + 1) * COLS, :] = half_of(src[b, pl.ds(at, COLS), :])
        return carry

    lax.fori_loop(0, v.space, peer, 0)


def take_own(v, src, dst):
    dst[v.spot] = src[v.spot]


def columns_zero(v):
    def zero(b, carry):
        for ref, wide in ((v.xc, 384), (v.xcr, 128), (v.gc, 384)):
            for low in (0, 32 + AREA):
                ref[b, low : low + 32, :] = jnp.zeros((32, wide), jnp.bfloat16)
        return carry

    lax.fori_loop(0, BATCH, zero, 0)


def columns_in(v):
    def peer(t, carry):
        at = pl.ds(pl.multiple_of(32 + t * ROWS * COLS, 16), ROWS * COLS)
        for b in range(BATCH):
            v.xc[b, at, 0:128] = v.b_state[t, b]
            v.xc[b, at, 128:256] = v.b_context[t, b]
            v.xc[b, at, 256:384] = v.b_motion[t, b]
        return carry

    lax.fori_loop(0, v.space, peer, 0)


FX_ROWS = 16 + (TALL + 2) * PITCH


def fx_base(b):
    return pl.multiple_of(b * FX_ROWS, 8)


def columns_forward(v):
    def gru(b, carry):
        s = full_of(v.xc[b, 32 : 32 + AREA, 0:128])
        bias = join((bias_of(v, COLUMNS_GATES, 2), bias_of(v, COLUMNS_CANDIDATE, 1)))
        rows = [slice(t * COLS, t * COLS + AREA) for t in range(5)]
        both = mm(join(v.xc[b, rows[t], 128:384] for t in range(5)), v.w_li[...]) + bias
        gates = mm(join(v.xc[b, rows[t], 0:128] for t in range(5)), v.w_ls[:, 0:256])
        gates = jax.nn.sigmoid(gates + both[:, :256])
        update, reset = gates[:, :128], gates[:, 128:]
        v.lu[b] = update
        v.lr[b] = reset
        v.xcr[b, 32 : 32 + AREA, :] = half_of(reset * s)
        cand = jnp.tanh(both[:, 256:] + mm(join(v.xcr[b, rows[t], :] for t in range(5)), v.w_ls[:, 256:384]))
        v.lc[b] = cand
        final = s + update * (cand - s)
        v.out_net[b] = half_of(final)
        v.final[...] = full_of(half_of(final))
        fx = fx_base(b)
        v.mm_tmp[pl.ds(fx, FX_ROWS), :] = jnp.zeros((FX_ROWS, LANES), jnp.float32)
        for x in range(COLS):
            v.mm_tmp[pl.ds(fx + 8 + PITCH + 2 + x, TALL, stride=PITCH), :] = v.final[pl.ds(x, TALL, stride=COLS), :]
        for j in range(2):
            v.e_left[b, j, 0:TALL, :] = half_of(v.final[pl.ds(j, TALL, stride=COLS), :])
            v.e_right[b, j, 0:TALL, :] = half_of(v.final[pl.ds(COLS - 2 + j, TALL, stride=COLS), :])
        return carry

    lax.fori_loop(0, BATCH, gru, 0)
    v.halo_final.start()


def ring_masks(v, shape):
    x = lax.rem(row_index(shape), PITCH)
    place = v.spot * COLS + x - 2
    seen = (place >= 0) & (place < WIDE) & (x >= 1) & (x < PITCH - 1)
    own = (x >= 2) & (x < PITCH - 2)
    return seen, own


def mask_gradient(v):
    def image(b, carry):
        value = nt(quarter_of(v.grad_mask[b]), v.w_mo[:, 0:MASK])
        for block in range(2):
            v.final[...] = value[:, block * 128 : (block + 1) * 128]
            v.tmp[0:SPREAD, :] = jnp.zeros((SPREAD, LANES), jnp.float32)
            for x in range(COLS):
                v.tmp[pl.ds(2 + x, TALL, stride=PITCH), :] = v.final[pl.ds(x, TALL, stride=COLS), :]
            v.hgo[b, :, 256 + block * 128 : 384 + block * 128] = half_of(v.tmp[0:SPREAD, :])
            v.m_left[b, block, 0:TALL, :] = half_of(v.final[pl.ds(0, TALL, stride=COLS), :])
            v.m_right[b, block, 0:TALL, :] = half_of(v.final[pl.ds(COLS - 1, TALL, stride=COLS), :])
        return carry

    lax.fori_loop(0, BATCH, image, 0)
    v.halo_mask.start()


def heads_part(v, b, tap):
    ref = v.hx_c if tap < 6 else v.hx_f
    lane = tap % 6 * 128
    return ref.at[b, 0:SPREAD, lane : lane + 128]


def taps_part(v, t, low, high):
    ref = v.hx_f if t % 3 == 2 else v.hx_c
    lane = (t % 3) % 2 * 384
    return ref.at[t // 3, 0:AREA, lane + low : lane + high]


def split_three(value):
    first = half_of(value)
    second = half_of(value - full_of(first))
    third = half_of(value - full_of(first) - full_of(second))
    return first, second, third


def column_grid():
    lane = lane_index((COLS, SPAN))
    columns = jnp.where((lax.rem(lane, PITCH) == row_index((COLS, SPAN)) + 2) & (lane < SPREAD), 1.0, 0.0)
    lane = lane_index((TALL, SPAN))
    rows = jnp.where(lax.div(lane, PITCH) == row_index((TALL, SPAN)), 1.0, 0.0)
    return columns, half_of(rows)


def widen(value, columns, rows, parts):
    spread = 0.0
    for piece in split_three(value)[:parts]:
        spread = spread + mm(piece, rows)
    return jnp.sum(spread * columns, axis=0, keepdims=True)


def widen_all(v):
    columns, rows = column_grid()
    first = row_index((8, SPAN)) == 0
    second = row_index((8, SPAN)) == 1
    for b in range(BATCH):
        low, high = (widen(v.target[b, c], columns, rows, 3) for c in range(2))
        v.target_wide[b] = jnp.where(first, low, jnp.where(second, high, 0.0))
        v.valid_wide[b] = jnp.broadcast_to(widen(v.valid[b].astype(jnp.float32), columns, rows, 1), (8, SPAN))


def narrow(v, b, wide, columns, rows):
    for c in range(2):
        total = 0.0
        for piece in split_three(wide[c : c + 1, :] * columns):
            total = total + nt(piece, rows)
        v.out_flow[b, c] = total


def heads(v):
    spot, last = v.spot, v.space - 1
    v.halo_final.receive()
    v.swap_count.receive()
    v.counts[v.spot] = v.count_out[...]
    counts = jnp.sum(v.counts[...], axis=0)
    seen, own = ring_masks(v, (SPREAD, LANES))
    steps = [(a - 1) * PITCH + (c - 1) for a in range(3) for c in range(3)]
    plane = jnp.float32(TALL * WIDE)
    columns, rows = column_grid()

    def image(b, carry):
        fx = fx_base(b)
        for j in range(2):
            left = jnp.where(spot > 0, full_of(v.f_left[b, j, 0:TALL, :]), 0.0)
            right = jnp.where(spot < last, full_of(v.f_right[b, j, 0:TALL, :]), 0.0)
            v.mm_tmp[pl.ds(fx + 8 + PITCH + j, TALL, stride=PITCH), :] = left
            v.mm_tmp[pl.ds(fx + 8 + PITCH + PITCH - 2 + j, TALL, stride=PITCH), :] = right
        for tap in range(9):
            at = 8 + PITCH + steps[tap]
            heads_part(v, b, tap)[...] = half_of(v.mm_tmp[pl.ds(fx + at, SPREAD), :])
        for part in range(2):
            name = (FLOW_HIDDEN, MASK_HIDDEN)[part]
            lanes = slice(part * 256, (part + 1) * 256)
            act, slope = act_slope(mm(join((v.hx_c[b, 0:SPREAD, :], v.hx_f[b, 0:SPREAD, :])), v.w_h[:, lanes]) + bias_of(v, name, 2))
            v.slope_h[b, :, lanes] = half_of(slope)
            if part == 0:
                for block in range(2):
                    value = jnp.where(seen, act[:, block * 128 : (block + 1) * 128], 0.0)
                    v.feat[b, 0:SPREAD, block * 128 : (block + 1) * 128] = half_of(value)
                v.feat[b, SPREAD:SPAN, :] = jnp.zeros((SPAN - SPREAD, HEAD), jnp.bfloat16)
            else:
                for block in range(2):
                    v.tmp[0:SPREAD, :] = act[:, block * 128 : (block + 1) * 128]
                    for x in range(COLS):
                        v.final[pl.ds(x, TALL, stride=COLS), :] = v.tmp[pl.ds(2 + x, TALL, stride=PITCH), :]
                    v.mf[b, :, block * 128 : (block + 1) * 128] = half_of(v.final[...])
        moved = nt(v.w_fo[...], v.feat[b])
        v.dt[...] = moved
        delta = jnp.zeros((8, SPAN), jnp.float32)
        for tap in range(9):
            pair = jnp.concatenate([v.dt[2 * tap : 2 * tap + 2, :], jnp.zeros((6, SPAN), jnp.float32)], axis=0)
            delta = delta + pltpu.roll(pair, (-steps[tap]) % SPAN, 1)
        v.tmp[0:SPAN, :] = jnp.zeros((SPAN, LANES), jnp.float32)
        v.final[...] = full_of(v.xc[b, 32 : 32 + AREA, 256:384])
        for x in range(COLS):
            v.tmp[pl.ds(2 + x, TALL, stride=PITCH), :] = v.final[pl.ds(x, TALL, stride=COLS), :]
        pick = jnp.where(lane_index((16, LANES)) == row_index((16, LANES)) + 126, 1.0, 0.0)
        base = nt(half_of(pick), half_of(v.tmp[0:SPAN, :]))[0:8, :]
        bias = v.bias[BIAS_AT[FLOW_OUT] : BIAS_AT[FLOW_OUT] + 1, :]
        first = row_index((8, SPAN)) == 0
        second = row_index((8, SPAN)) == 1
        shift = jnp.where(first, bias[0:1, 0:1], jnp.where(second, bias[0:1, 1:2], 0.0))
        new = base + delta + shift
        narrow(v, b, new, columns, rows)
        error = new - v.target_wide[b]
        root = jnp.sqrt(error * error + 1.0)
        valid = jnp.where(first | second, v.valid_wide[b], 0.0)
        piece = jnp.sum(valid * root)
        divisor = jnp.maximum(v.pick_count(counts, b), 1.0)
        gradient = plane / divisor * valid * error / root
        v.dg[b] = gradient
        v.losses[...] = jnp.where(row_index((8, LANES)) == b, piece, v.losses[...])
        return carry

    v.losses[...] = jnp.zeros((8, LANES), jnp.float32)
    lax.fori_loop(0, BATCH, image, 0)
    v.halo_dg.start()
    v.swap_loss.start()


def mask_output(v):
    def image(b, carry):
        store = pltpu.make_async_copy(v.mask_low, v.out_mask.at[b], v.osem.at[3])
        pl.when(b > 0)(store.wait)
        for block in range(5):
            wide = min(128, MASK - block * 128)
            lanes = slice(block * 128, block * 128 + wide)
            at = BIAS_AT[MASK_OUT] + block
            value = mm(v.mf[b], v.w_mo[:, lanes]) + v.bias[at : at + 1, 0:wide]
            v.mask_low[:, lanes] = half_of(0.25 * value)
        store.start()
        return carry

    lax.fori_loop(0, BATCH, image, 0)


def heads_back(v):
    spot, last = v.spot, v.space - 1
    seen, own = ring_masks(v, (SPREAD, LANES))
    steps = [(a - 1) * PITCH + (c - 1) for a in range(3) for c in range(3)]
    v.halo_dg.receive()
    v.halo_mask.receive()

    def zb(c, low, rows):
        at = c * (2 * EDGE + SPREAD) + low
        return v.mm_tmp.at[at : at + rows]

    def image(b, carry):
        x = lax.rem(lane_index((8, SPAN)), PITCH)
        own_dg = v.dg[b]
        left = jnp.where((x < 2) & (spot > 0), pltpu.roll(v.dg_left[b], SPAN - COLS, 1), 0.0)
        right = jnp.where((x >= PITCH - 2) & (spot < last), pltpu.roll(v.dg_right[b], COLS, 1), 0.0)
        inside = lane_index((8, SPAN)) < SPREAD
        wide_dg = full_of(half_of(jnp.where(inside, own_dg + left + right, 0.0)))
        own_low = full_of(half_of(own_dg))
        v.dt[...] = jnp.zeros_like(v.dt)
        v.dto[...] = jnp.zeros_like(v.dto)
        for tap in range(9):
            v.dt[2 * tap : 2 * tap + 2, :] = pltpu.roll(wide_dg, steps[tap] % SPAN, 1)[0:2, :]
            v.dto[2 * tap : 2 * tap + 2, :] = pltpu.roll(own_low, steps[tap] % SPAN, 1)[0:2, :]
        v.dtb[b] = half_of(v.dto[...])
        from_flow = tn(half_of(v.dt[...]), v.w_fo[...])
        for block in range(2):
            left = jnp.where(spot > 0, full_of(v.n_left[b, block, 0:TALL, :]), 0.0)
            right = jnp.where(spot < last, full_of(v.n_right[b, block, 0:TALL, :]), 0.0)
            v.tmp[0:SPREAD, :] = full_of(v.hgo[b, :, 256 + block * 128 : 384 + block * 128])
            v.tmp[pl.ds(1, TALL, stride=PITCH), :] = left
            v.tmp[pl.ds(PITCH - 2, TALL, stride=PITCH), :] = right
            v.hgo[b, :, 256 + block * 128 : 384 + block * 128] = half_of(v.tmp[0:SPREAD, :])
        for block in range(4):
            lanes = slice(block * 128, (block + 1) * 128)
            value = from_flow[0:SPREAD, lanes] if block < 2 else full_of(v.hgo[b, :, lanes])
            value = value * full_of(v.slope_h[b, :, lanes])
            v.hgo[b, :, lanes] = half_of(jnp.where(seen, value, 0.0))
        total = jnp.zeros((SPREAD, LANES), jnp.float32)
        for a in range(3):
            value = nt(v.hgo[b], v.w_h[a * 384 : (a + 1) * 384, :])
            for c in range(3):
                zb(c, EDGE, SPREAD)[...] = value[:, c * 128 : (c + 1) * 128]
            for c in range(3):
                at = EDGE - steps[a * 3 + c]
                total = total + zb(c, at, SPREAD)[...]
        for block in range(4):
            lanes = slice(block * 128, (block + 1) * 128)
            v.hgo[b, :, lanes] = half_of(jnp.where(own, full_of(v.hgo[b, :, lanes]), 0.0))
        v.tmp[0:SPREAD, :] = total
        for x in range(COLS):
            v.final[pl.ds(x, TALL, stride=COLS), :] = v.tmp[pl.ds(2 + x, TALL, stride=PITCH), :]
        r = v.final[...] + full_of(v.grad_net[b])

        s = full_of(v.xc[b, 32 : 32 + AREA, 0:128])
        update, reset, cand = v.lu[b], v.lr[b], v.lc[b]
        cg = half_of(r * update * (1.0 - cand * cand))
        v.gc[b, 32 : 32 + AREA, 256:384] = cg
        rows = [slice((4 - t) * COLS, (4 - t) * COLS + AREA) for t in range(5)]
        reset_grad = nt(
            join(v.gc[b, rows[t], 256:384] for t in range(5)),
            join(v.w_ls[t * 128 : (t + 1) * 128, 256:384] for t in range(5)),
        )
        v.gc[b, 32 : 32 + AREA, 0:128] = half_of(r * (cand - s) * update * (1.0 - update))
        v.gc[b, 32 : 32 + AREA, 128:256] = half_of(reset_grad * s * reset * (1.0 - reset))
        state_grad = r * (1.0 - update) + reset_grad * reset
        state_grad = state_grad + nt(
            join(v.gc[b, rows[t], 0:256] for t in range(5)),
            join(v.w_ls[t * 128 : (t + 1) * 128, 0:256] for t in range(5)),
        )
        inputs_grad = nt(
            join(v.gc[b, rows[t], :] for t in range(5)), join(v.w_li[t * 256 : (t + 1) * 256, :] for t in range(5))
        )
        high = half_of(own_dg)
        low = half_of(own_dg - full_of(high))
        pick = half_of(jnp.where(lane_index((8, LANES)) == row_index((8, LANES)) + 126, 1.0, 0.0))
        v.tmp[0:SPAN, :] = tn(high, pick) + tn(low, pick)
        for x in range(COLS):
            v.final[pl.ds(x, TALL, stride=COLS), :] = v.tmp[pl.ds(2 + x, TALL, stride=PITCH), :]
        v.lu[b] = state_grad
        v.lr[b] = inputs_grad[:, 0:128]
        v.lc[b] = inputs_grad[:, 128:256] + v.final[...]

        def peer(t, carry):
            at = pl.ds(pl.multiple_of(t * ROWS * COLS, 16), ROWS * COLS)
            v.a_state[t, b] = half_of(v.lu[b, at, :])
            v.a_context[t, b] = half_of(v.lr[b, at, :])
            v.a_motion[t, b] = half_of(v.lc[b, at, :])
            return carry

        lax.fori_loop(0, v.space, peer, 0)
        v.back_state.start(b)
        return carry

    v.swap_loss.receive()
    for c in range(3):
        zb(c, 0, EDGE)[...] = jnp.zeros((EDGE, LANES), jnp.float32)
        zb(c, EDGE + SPREAD, EDGE)[...] = jnp.zeros((EDGE, LANES), jnp.float32)
    lax.fori_loop(0, BATCH, image, 0)


def unpack_back(v, src, dst):
    def peer(t, carry):
        for b in range(BATCH):
            value = full_of(src[t, b])
            for y in range(ROWS):
                at = pl.multiple_of(y * WIDE + t * COLS, COLS)
                dst[b, pl.ds(at, COLS), :] = value[y * COLS : (y + 1) * COLS, :]
        return carry

    lax.fori_loop(0, v.space, peer, 0)


def seams():
    starts, bias_row, _, _ = flat_rows()
    edges = sorted(starts.values()) + [bias_row]
    tiles = sorted({row // 16 for row in edges if row % 16})
    parts = {}
    for low, high in zip(edges, edges[1:]):
        for tile in tiles:
            if low < (tile + 1) * 16 and high > tile * 16:
                parts[tile] = parts.get(tile, 0) + 1
    return {tile: (index, parts[tile]) for index, tile in enumerate(tiles)}


class Flush:
    def __init__(self, v):
        self.v, self.at, self.busy, self.small = v, 0, {}, []
        self.tiles = seams()
        self.left = {tile: parts for tile, (_, parts) in self.tiles.items()}
        v.seam[...] = jnp.zeros_like(v.seam)
        top = (max(self.tiles) + 1) * 16
        rest = v.out_flat.shape[0] - top
        v.seam_low[16 * 16 : 16 * 16 + rest, :] = jnp.zeros((rest, LANES), jnp.bfloat16)
        self.write(16, rest, top)

    def write(self, index, rows, base):
        v = self.v
        copy = pltpu.make_async_copy(
            v.seam_low.at[index * 16 : index * 16 + rows], v.out_flat.at[base : base + rows], v.fsem.at[index]
        )
        copy.start()
        self.small.append(copy)

    def send(self, low, length, base):
        v, slot = self.v, self.at % 2
        self.at += 1
        if slot in self.busy:
            self.busy[slot].wait()
        cast_rows(v.stage.at[slot], 0, v.flat, low, length, jnp.bfloat16)
        copy = pltpu.make_async_copy(
            v.stage.at[slot, 0:length], v.out_flat.at[base : base + length], v.ssem.at[slot, 0]
        )
        copy.start()
        self.busy[slot] = copy

    def layer(self, start, rows):
        v, stop = self.v, start + rows
        for tile in self.tiles:
            low, high = max(start, tile * 16), min(stop, tile * 16 + 16)
            if low >= high:
                continue
            index = self.tiles[tile][0]
            v.seam[index, low - tile * 16 : high - tile * 16, :] = v.flat[MARGIN + low - start : MARGIN + high - start, :]
            self.left[tile] -= 1
            if not self.left[tile]:
                v.seam_low[index * 16 : index * 16 + 16, :] = half_of(v.seam[index])
                self.write(index, 16, tile * 16)
        low, high = -(-start // 16) * 16, stop // 16 * 16
        if high > low:
            self.send(MARGIN + low - start, high - low, low)

    def settle(self):
        for copy in list(self.busy.values()) + self.small:
            copy.wait()
        self.busy, self.small = {}, []


SHARE = 3072


class Reduce:
    ORDER = (
        (3, 3072, 3072), (3, 0, 3072), (2, 3072, 3072), (2, 0, 3072), (1, 3072, 3072), (1, 0, 3072),
        (0, 1024, 3072), (0, 4096, 2048), (0, 0, 1024),
    )

    def __init__(self, v, count):
        self.v, self.count = v, count
        self.flying, self.queue, self.late = [], [], []
        self.copies = {}
        rank = v.rank
        self.lower, self.upper = lax.rem(rank, 2), lax.div(rank, 2)
        self.side, self.depth = lax.rem(v.spot, 2), lax.div(v.spot, 2)
        self.group = v.space // 2

    def part(self, k):
        return self.ORDER[k][2] // 4 // self.v.space

    def slice_at(self, k, spot):
        return lax.rem(spot, 2) * (self.ORDER[k][2] // 8) + lax.div(spot, 2) * self.part(k)

    def offer(self, *numbers, now=False):
        if now:
            self.queue += list(numbers)
        else:
            self.late += list(numbers)

    LONG = 6

    def stages(self, k):
        if k < self.LONG:
            return (self.core, self.across, self.side_sum, self.deep_sum, self.deep_out, self.owner, self.beside)
        if k < len(self.ORDER) - 1:
            return (self.core, self.across, self.stripes, self.along, self.beside)
        return (self.ranks, self.stripes, self.along, self.beside)

    def tick(self):
        for entry in self.flying:
            self.stages(entry[0])[entry[1]](entry[0])
            entry[1] += 1
        self.flying = [entry for entry in self.flying if entry[1] < len(self.stages(entry[0]))]
        if self.queue:
            number = self.queue.pop(0)
            self.v.flush.settle()
            self.begin(number)
            self.flying.append([number, 0])
        self.queue, self.late = self.queue + self.late, []

    def begin(self, k):
        v, slot = self.v, k % 2
        quarter, low, size = self.ORDER[k]
        start = quarter * self.count // (LANES * 16) * 16 + low
        half = size // 2
        if k == len(self.ORDER) - 1:
            self.begin_ranks(start, size // 4)
            return

        def rows(which):
            return v.out_flat.at[pl.ds(pl.multiple_of(start + which * half, 16), half)]

        copy = remote(
            rows(1 - self.lower), v.rcore.at[slot, 0:half], v.rsend.at[0, slot], v.rrecv.at[0, slot], {DP: v.mate}
        )
        own = pltpu.make_async_copy(rows(self.lower), v.own.at[slot, 0:half], v.rlocal.at[slot])
        copy.start()
        own.start()
        self.copies[k] = (copy, own)

    def begin_ranks(self, start, rows):
        v = self.v

        def block(rank):
            at = start + lax.rem(rank, 2) * (2 * rows) + lax.div(rank, 2) * rows
            return v.out_flat.at[pl.ds(pl.multiple_of(at, 16), rows)]

        for turn in range(1, 4):
            to = lax.rem(v.rank + turn, 4)
            remote(block(to), v.dall.at[v.rank], v.dsend, v.drecv, {DP: to}).start()
        self.mine = pltpu.make_async_copy(block(v.rank), v.dall.at[v.rank], v.rlocal.at[0])
        self.mine.start()

    def ranks(self, k):
        v, slot, part = self.v, k % 2, self.part(k)
        self.mine.wait()
        drain_bytes(v.dall.at[0:3], v.dsend)
        drain_bytes(v.dall.at[0:3], v.drecv)
        self.finish_f(k)
        value = full_of(v.dall[0]) + full_of(v.dall[1]) + full_of(v.dall[2]) + full_of(v.dall[3])
        rows = self.ORDER[k][2] // 4
        v.ks[slot, 0:rows, :] = value
        v.ts[slot, 0:rows, :] = half_of(value)
        v.acc[slot, 0:part, :] = v.ks[slot, pl.ds(pl.multiple_of(self.slice_at(k, v.spot), 16), part), :]
        self.each(lambda step: self.s_copy(k, step).start(), 1, v.space)

    def finish_f(self, k):
        drain_bytes(self.s_all(k - 2), self.v.s2send.at[k % 2])
        self.f_sent(k - 2)

    def core(self, k):
        v, slot = self.v, k % 2
        copy, own = self.copies[k]
        copy.wait()
        own.wait()
        if k >= 2:
            self.x_copy(k - 2).wait_send()
        quarter = self.ORDER[k][2] // 4

        def add(step, carry):
            at = pl.multiple_of(step * 128, 128)
            near = pl.ds(pl.multiple_of(self.upper * quarter + at, 128), 128)
            far = pl.ds(pl.multiple_of((1 - self.upper) * quarter + at, 128), 128)
            to = pl.ds(at, 128)
            v.tx[slot, to, :] = half_of(full_of(v.own[slot, far, :]) + full_of(v.rcore[slot, far, :]))
            v.ks[slot, to, :] = full_of(v.own[slot, near, :]) + full_of(v.rcore[slot, near, :])
            return carry

        lax.fori_loop(0, quarter // 128, add, 0)
        self.x_copy(k).start()

    def x_copy(self, k):
        v, slot = self.v, k % 2
        rows = slice(0, self.ORDER[k][2] // 4)
        return remote(
            v.tx.at[slot, rows], v.rx.at[slot, rows], v.rsend.at[1, slot], v.rrecv.at[1, slot], {DP: v.other}
        )

    def s_copy(self, k, step):
        v, slot, part = self.v, k % 2, self.part(k)
        to = lax.rem(v.spot + step, v.space)
        src = v.ts.at[slot, pl.ds(pl.multiple_of(self.slice_at(k, to), 16), part)]
        dst = v.rs.at[slot, v.spot, 0:part]
        return remote(src, dst, v.s2send.at[slot], v.s2recv.at[slot], {SPACE: to})

    def s_all(self, k):
        return self.v.rs.at[k % 2, 0 : self.v.space - 1, 0 : self.part(k)]

    def each(self, what, start, stop):
        def body(step, carry):
            what(step)
            return carry

        lax.fori_loop(start, stop, body, 0)

    def across(self, k):
        v, slot = self.v, k % 2
        self.x_copy(k).wait_recv()
        if k < self.LONG:
            self.across_long(k)
            return

        def add(step, carry):
            to = pl.ds(pl.multiple_of(step * 128, 128), 128)
            value = v.ks[slot, to, :] + full_of(v.rx[slot, to, :])
            v.ks[slot, to, :] = value
            v.ts[slot, to, :] = half_of(value)
            return carry

        lax.fori_loop(0, self.ORDER[k][2] // 4 // 128, add, 0)
        part = self.part(k)
        v.acc[slot, 0:part, :] = v.ks[slot, pl.ds(pl.multiple_of(self.slice_at(k, v.spot), 16), part), :]
        self.each(lambda step: self.s_copy(k, step).start(), 1, v.space)

    def across_long(self, k):
        v, slot = self.v, k % 2
        if k >= 2:
            self.side_copy(k - 2).wait_send()
        rows = self.ORDER[k][2] // 8

        def add(step, carry):
            at = pl.multiple_of(step * 128, 128)
            near = pl.ds(pl.multiple_of(self.side * rows + at, 128), 128)
            far = pl.ds(pl.multiple_of((1 - self.side) * rows + at, 128), 128)
            to = pl.ds(at, 128)
            v.ty[slot, to, :] = half_of(v.ks[slot, far, :] + full_of(v.rx[slot, far, :]))
            v.ky[slot, to, :] = v.ks[slot, near, :] + full_of(v.rx[slot, near, :])
            return carry

        lax.fori_loop(0, rows // 128, add, 0)
        self.side_copy(k).start()

    def side_copy(self, k):
        v, slot = self.v, k % 2
        return remote(v.ty.at[slot], v.ry.at[slot], v.rsend.at[2, slot], v.rrecv.at[2, slot], {SPACE: v.twin})

    def deep_at(self, k, depth):
        return pl.ds(pl.multiple_of(depth * self.part(k), 16), self.part(k))

    def deep_copy(self, k, step):
        v, slot = self.v, k % 2
        to = lax.rem(self.depth + step, self.group)
        return remote(
            v.tz.at[slot, self.deep_at(k, to)], v.rz.at[slot, self.depth], v.z1send.at[slot],
            v.z1recv.at[slot], {SPACE: to * 2 + self.side},
        )

    def deep_all(self, k):
        return self.v.rz.at[k % 2, 0 : self.group - 1]

    def side_sum(self, k):
        v, slot = self.v, k % 2
        self.side_copy(k).wait_recv()
        if k >= 2:
            drain_bytes(self.deep_all(k - 2), v.z1send.at[slot])
        value = v.ky[slot] + full_of(v.ry[slot])
        v.tz[slot] = half_of(value)
        v.ky[slot] = value
        v.kz[slot] = v.ky[slot, self.deep_at(k, self.depth), :]
        self.each(lambda step: self.deep_copy(k, step).start(), 1, self.group)

    def out_copy(self, k, step):
        v, slot = self.v, k % 3
        to = lax.rem(self.depth + step, self.group)
        block = v.az.at[slot, self.deep_at(k, self.depth)]
        return remote(
            block, block, v.z2send.at[slot], v.z2recv.at[slot], {SPACE: to * 2 + self.side}
        )

    def deep_sum(self, k):
        v, slot = self.v, k % 2
        drain_bytes(self.deep_all(k), v.z1recv.at[slot])

        def add(step, value):
            return value + full_of(v.rz[slot, lax.rem(self.depth + step, self.group)])

        value = lax.fori_loop(1, self.group, add, v.kz[slot])
        if k >= 2:
            self.own_wait(k - 2)
        v.az[k % 3, self.deep_at(k, self.depth), :] = half_of(value)
        self.each(lambda step: self.out_copy(k, step).start(), 1, self.group)

    def own_rows(self, k, lower, upper):
        quarter, low, size = self.ORDER[k]
        at = low + lower * (size // 2) + upper * (size // 4) + self.side * (size // 8)
        return pl.ds(pl.multiple_of(at, 16), size // 8)

    def own_copy(self, k):
        v = self.v
        rows = self.own_rows(k, self.lower, self.upper)
        return remote(v.az.at[k % 3], v.gath.at[rows], v.osend.at[k % 3], v.orecv.at[k], {DP: self.ORDER[k][0]})

    def own_wait(self, k):
        pl.when(self.v.rank != self.ORDER[k][0])(self.own_copy(k).wait_send)

    def deep_out(self, k):
        v = self.v
        several = v.az.at[k % 3, 0 : (self.group - 1) * self.part(k)]
        drain_bytes(several, v.z2send.at[k % 3])
        drain_bytes(several, v.z2recv.at[k % 3])
        pl.when(v.rank != self.ORDER[k][0])(self.own_copy(k).start)

        @pl.when(v.rank == self.ORDER[k][0])
        def _():
            v.gath[self.own_rows(k, self.lower, self.upper), :] = v.az[k % 3]

    def owner(self, k):
        v = self.v

        @pl.when(v.rank == self.ORDER[k][0])
        def _():
            drain_bytes(v.gath.at[0 : 3 * (self.ORDER[k][2] // 8)], v.orecv.at[k])
            for copy in self.y_copies(k):
                copy.start()

    def place(self, k, lower, upper, spot):
        quarter, low, size = self.ORDER[k]
        at = low + lower * (size // 2) + upper * (size // 4) + self.slice_at(k, spot)
        return pl.ds(pl.multiple_of(at, 16), self.part(k))

    def f_copy(self, k, step):
        v, slot = self.v, k % 2
        quarter = self.ORDER[k][0]
        to = lax.rem(self.depth + step, self.group) * 2 + self.side
        return remote(
            v.fin.at[slot, 0 : self.part(k)], v.gath.at[self.place(k, self.lower, self.upper, v.spot)],
            v.fsend.at[slot], v.frecv.at[k], {DP: quarter, SPACE: to},
        )

    def f_all(self, k, what):
        v = self.v
        pl.when(v.rank != self.ORDER[k][0])(lambda: what(self.f_copy(k, 0)))
        self.each(lambda step: what(self.f_copy(k, step)), 1, self.group)

    def f_sent(self, k):
        v = self.v
        quarter = self.ORDER[k][0]
        pl.when(v.rank != quarter)(lambda: self.f_copy(k, 0).wait_send())
        drain_bytes(v.gath.at[0 : (self.group - 1) * self.part(k)], v.fsend.at[k % 2])

    def stripes(self, k):
        v, slot, part = self.v, k % 2, self.part(k)
        quarter = self.ORDER[k][0]
        drain_bytes(self.s_all(k), v.s2recv.at[slot])

        def add(step, value):
            return value + full_of(v.rs[slot, lax.rem(v.spot + step, v.space), 0:part])

        value = half_of(lax.fori_loop(1, v.space, add, v.acc[slot, 0:part, :]))
        v.fin[slot, 0:part, :] = value

        @pl.when(v.rank == quarter)
        def _():
            v.gath[self.place(k, self.lower, self.upper, v.spot), :] = v.fin[slot, 0:part, :]

        self.f_all(k, lambda copy: copy.start())

    def y_copies(self, k):
        v = self.v
        quarter, low, size = self.ORDER[k]
        out = []
        for i in range(4):
            at = pl.multiple_of(low + i * (size // 4) + self.side * (size // 8), 16)
            block = v.gath.at[pl.ds(at, size // 8)]
            out.append(remote(block, block, v.ysend.at[k], v.yrecv.at[k], {SPACE: v.twin}))
        return out

    def along(self, k):
        v = self.v
        quarter = self.ORDER[k][0]

        @pl.when(v.rank == quarter)
        def _():
            drain_bytes(v.gath.at[0 : (4 * self.group - 1) * self.part(k)], v.frecv.at[k])
            for copy in self.y_copies(k):
                copy.start()

    def beside(self, k):
        v = self.v

        @pl.when(v.rank == self.ORDER[k][0])
        def _():
            several = v.gath.at[0 : self.ORDER[k][2] // 2]
            drain_bytes(several, v.ysend.at[k])
            drain_bytes(several, v.yrecv.at[k])

    def settle(self):
        v = self.v
        for k in range(self.LONG - 2, self.LONG):
            self.side_copy(k).wait_send()
            drain_bytes(self.deep_all(k), v.z1send.at[k % 2])
            self.own_wait(k)
        for k in range(len(self.ORDER) - 3, len(self.ORDER) - 1):
            self.x_copy(k).wait_send()
        for k in range(len(self.ORDER) - 2, len(self.ORDER)):
            drain_bytes(self.s_all(k), v.s2send.at[k % 2])
            self.f_sent(k)

    def ready(self):
        v, count = self.v, self.count
        v.gath[2 * SHARE :, :] = jnp.zeros((32, LANES), jnp.bfloat16)

        @pl.when(v.rank == 3)
        def _():
            at = self.bias_base() - 3 * count // (LANES * 16) * 16
            v.gath[at : at + 32, :] = half_of(full_of(v.gath[at : at + 32, :]) + v.bsum[...])

    def lay(self, first, last):
        v, count = self.v, self.count
        offset = v.rank * count - quarter_base(v.rank, count) * LANES
        skip = lax.div(offset, LANES)
        shift = lax.rem(offset, LANES)
        near = lane_index((256, LANES)) < LANES - shift

        def staged(slot):
            return v.mm_tmp.at[pl.ds(pl.multiple_of(slot * 256, 256), 256)]

        def out(step):
            at = pl.multiple_of(step * 256, 256)
            slot = lax.rem(step, 2)
            return pltpu.make_async_copy(staged(slot), v.out_grads.at[pl.ds(at, 256)], v.osem.at[4 + slot])

        def place(step, carry):
            at = pl.multiple_of(step * 256, 256)
            v.tmp[0:288, :] = pltpu.roll(full_of(v.gath[pl.ds(at, 288), :]), lax.rem(LANES - shift, LANES), 1)
            pl.when(step > first + 1)(out(step - 2).wait)
            staged(lax.rem(step, 2))[...] = jnp.where(near, v.tmp[pl.ds(skip, 256), :], v.tmp[pl.ds(skip + 1, 256), :])
            out(step).start()
            return carry

        lax.fori_loop(first, last, place, 0)
        for step in (last - 2, last - 1):
            out(step).wait()

    def bias_base(self):
        return flat_rows()[1] // 16 * 16

    def bias_core(self):
        v = self.v
        self.b1 = remote(v.bown, v.bcore, v.bsend.at[0], v.brecv.at[0], {DP: v.mate})
        self.b1.start()

    def bias_across(self):
        v = self.v
        self.b1.wait()
        v.btwo[...] = v.bown[...] + v.bcore[...]
        self.b2 = remote(v.btwo, v.bacross, v.bsend.at[1], v.brecv.at[1], {DP: v.other})
        self.b2.start()

    def bias_stripes(self):
        v = self.v
        self.b2.wait()
        v.bfour[...] = v.btwo[...] + v.bacross[...]
        self.b3 = Swap(v, 8, v.bfour, v.ball, True)
        self.b3.start()

    def bias_end(self):
        v = self.v
        self.b3.receive()
        self.b3.sent()
        v.ball[v.spot] = v.bfour[...]
        v.bsum[...] = jnp.sum(v.ball[...], axis=0)


def ones_sum(g):
    return mm(jnp.ones((8, g.shape[0]), jnp.bfloat16), g)[0:1, :]


def keep_bias(v, name, value):
    for block in range(-(-value.shape[1] // 128)):
        at = BIAS_AT[name] + block
        v.gbias[at : at + 1, :] = value[:, block * 128 : (block + 1) * 128]


def gradients_gru(v, gates_name, cand_name, parts, g_of):
    starts, _, _, _ = flat_rows()
    total = 0.0
    for b in range(BATCH):
        total = total + ones_sum(g_of(b))
    keep_bias(v, gates_name, total[:, 0:256])
    keep_bias(v, cand_name, total[:, 256:384])

    def taps(number, first, last):
        return lambda b: join(parts(t)[number](b) for t in range(first, last))

    state = tn_all(taps(0, 0, 5), g_of, 0, 256)
    for t in range(5):
        pack_pairs(v.flat, t * 384, 128, state[t * 128 : (t + 1) * 128, 0:128], state[t * 128 : (t + 1) * 128, 128:256])
    state = tn_all(taps(2, 0, 5), g_of, 256, 384)
    for t in range(5):
        v.mm_tmp[pl.ds(MARGIN + t * 384, 128), :] = state[t * 128 : (t + 1) * 128, :]
    for first, last in ((0, 2), (2, 4), (4, 5)):
        inputs = tn_all(taps(1, first, last), g_of, 0, 384)
        for t in range(first, last):
            rows = slice((t - first) * 256, (t - first + 1) * 256)
            pack_pairs(v.flat, t * 384 + 128, 256, inputs[rows, 0:128], inputs[rows, 128:256])
            v.mm_tmp[pl.ds(MARGIN + t * 384 + 128, 256), :] = inputs[rows, 256:384]
    v.flush.layer(starts[gates_name], 3840)
    cast_rows(v.flat, MARGIN, v.mm_tmp, MARGIN, 1920, jnp.float32)
    v.flush.layer(starts[cand_name], 1920)


def tn_all(part, g_of, low, high):
    return tn(join((part(b) for b in range(BATCH)), 0), join((g_of(b, low, high) for b in range(BATCH)), 0))


def gradients_heads(v):
    starts, _, _, _ = flat_rows()
    total = 0.0
    for b in range(BATCH):
        total = total + ones_sum(v.hgo[b])
    keep_bias(v, FLOW_HIDDEN, total[:, 0:256])
    keep_bias(v, MASK_HIDDEN, total[:, 256:512])
    for name, lane in ((FLOW_HIDDEN, 0), (MASK_HIDDEN, 256)):
        grads = join((v.hgo[b, :, lane : lane + 256] for b in range(BATCH)), 0)
        for group in range(3):
            taps = [join(heads_part(v, b, group * 3 + c)[...] for c in range(3)) for b in range(BATCH)]
            value = tn(join(taps, 0), grads)
            for c in range(3):
                rows = slice(c * 128, (c + 1) * 128)
                pack_pairs(v.flat, (group * 3 + c) * 128, 128, value[rows, 0:128], value[rows, 128:256])
        v.flush.layer(starts[name], 2304)

    total = 0.0
    sums = 0.0
    for b in range(BATCH):
        total = total + mm(v.dtb[b], v.feat[b])
        sums = sums + jnp.sum(full_of(half_of(v.dg[b])), axis=1, keepdims=True)
    lane1 = lane_index((1, LANES))
    at = BIAS_AT[FLOW_OUT]
    v.gbias[at : at + 1, :] = jnp.where(lane1 == 0, sums[0:1, :], jnp.where(lane1 == 1, sums[1:2, :], 0.0))
    v.fo_tmp[...] = total[:, 0:128]
    v.fo_tmp2[...] = total[:, 128:256]
    for quarter in range(4):
        value = 0.0
        for which in range(2):
            rows = jnp.concatenate(
                [v.fo_tmp[pl.ds(which, 9, stride=2), :], v.fo_tmp2[pl.ds(which, 9, stride=2), :]], axis=1
            )
            value = value + nt(half_of(rows), split_pick(which, quarter))
        v.flat[pl.ds(MARGIN + quarter, 9, stride=4), :] = value
    v.flush.layer(starts[FLOW_OUT], 36)

    lane = lane_index((128, LANES))
    low_half = lane < 64
    even, odd = [], []
    total = 0.0
    for b in range(BATCH):
        total = total + ones_sum(quarter_of(v.grad_mask[b]))
    for block in range(5):
        wide = min(128, MASK - block * 128)
        at = BIAS_AT[MASK_OUT] + block
        v.gbias[at : at + 1, 0:wide] = total[:, block * 128 : block * 128 + wide]
        value = 0.0
        for b in range(BATCH):
            value = value + tn(v.mf[b], quarter_of(v.grad_mask[b, :, block * 128 : block * 128 + wide]))
        v.pair_a[:, 0:wide] = value
        even.append(v.pair_a[pl.ds(0, 128, stride=2), :])
        odd.append(pltpu.roll(v.pair_a[pl.ds(1, 128, stride=2), :], 64, 1))
    for i in range(4):
        v.flat[pl.ds(MARGIN + i, 128, stride=9), :] = even[i]
    v.flat[pl.ds(MARGIN + 4, 128, stride=9), :] = jnp.where(low_half, even[4], odd[0])
    for i in range(4):
        v.flat[pl.ds(MARGIN + 5 + i, 128, stride=9), :] = jnp.where(low_half, odd[i], odd[i + 1])
    v.flush.layer(starts[MASK_OUT], 1152)


def rows_back(v):
    v.back_state.receive()
    take_own(v, v.a_state, v.b_state)
    unpack_back(v, v.b_state, v.state)
    v.reduce.tick()

    def image(b, carry):
        r = v.state[b]
        s = full_of(v.net[b])
        update, reset, cand = v.ru[b], v.rr[b], v.rc[b]
        cg = full_of(half_of(r * update * (1.0 - cand * cand)))
        spread_five(v, cg, None, 256, True)
        reset_grad = nt(
            join(taps_part(v, t, 256, 384)[...] for t in range(5)),
            join(v.w_rs[t * 128 : (t + 1) * 128, 256:384] for t in range(5)),
        )
        low = full_of(half_of(r * (cand - s) * update * (1.0 - update)))
        high = full_of(half_of(reset_grad * s * reset * (1.0 - reset)))
        spread_five(v, low, None, 0, True)
        spread_five(v, high, None, 128, True)
        v.gr[b] = taps_part(v, 2, 0, 384)[...]
        state_grad = r * (1.0 - update) + reset_grad * reset
        state_grad = state_grad + nt(
            join(taps_part(v, t, 0, 256)[...] for t in range(5)),
            join(v.w_rs[t * 128 : (t + 1) * 128, 0:256] for t in range(5)),
        )
        v.ru[b] = state_grad
        inputs_grad = nt(
            join(taps_part(v, t, 0, 384)[...] for t in range(5)),
            join(v.w_ri[t * 256 : (t + 1) * 256, :] for t in range(5)),
        )
        v.rr[b] = inputs_grad[:, 0:128]
        v.rc[b] = inputs_grad[:, 128:256]
        return carry

    lax.fori_loop(0, BATCH, image, 0)
    v.store_gnet.start()
    v.back_context.receive()
    v.back_motion.receive()
    take_own(v, v.a_context, v.b_context)
    take_own(v, v.a_motion, v.b_motion)
    unpack_back(v, v.b_context, v.lr)
    unpack_back(v, v.b_motion, v.lu)

    def total(b, carry):
        v.rr[b] = v.rr[b] + v.lr[b]
        motion = v.rc[b] + v.lu[b]
        v.mge[b, 256:896, :] = half_of(motion * full_of(v.slope_m[b]))
        high = half_of(motion)
        low = half_of(motion - full_of(high))
        pick = half_of(jnp.where(lane_index((16, LANES)) == row_index((16, LANES)) + 126, 1.0, 0.0))
        v.gf_base[b] = (nt(pick, high) + nt(pick, low))[0:8, :]
        return carry

    lax.fori_loop(0, BATCH, total, 0)
    v.halo_mg.start()
    v.store_gctx.start()


def gcorr_stores(v, b):
    return [
        pltpu.make_async_copy(v.mm_tmp.at[y * 328 : y * 328 + CORR], v.out_gcorr.at[b, y], v.gsem.at[y])
        for y in range(ROWS)
    ]


def branch_back(v):
    v.halo_mg.receive()

    def image(b, carry):
        up = jnp.where(v.spot > 0, full_of(v.mge[b, 0:256, :]), 0.0)
        own = full_of(v.mge[b, 256:896, :])
        down = jnp.where(v.spot < v.space - 1, full_of(v.mge[b, 896:1152, :]), 0.0)
        spread_rows(v, 0, (jnp.concatenate([up, own, down], axis=0),), 1152, v.xi, 0, 128, True)
        joint = nt(
            join(v.xi[(2 - a) * 128 : (2 - a) * 128 + 896, 0:384] for a in range(3)),
            join(v.w_mm[k * 256 : (k + 1) * 256, :] for k in range(9)),
        )
        branch = joint * full_of(v.slope_j[b])
        low = full_of(half_of(edge_rows(v, branch[:, 0:128], WIDE)))
        high = full_of(half_of(edge_rows(v, branch[:, 128:256], WIDE)))
        spread_rows(v, 0, (low, high), 896, v.hx_j.at[b], 0, 256, True)
        return carry

    lax.fori_loop(0, BATCH, image, 0)


def branch_own(v, b, low=0, high=256):
    return v.hx_j[b, 128:768, 256 + low : 256 + high]


def flow_back(v):
    def image(b, carry):
        rows = [slice((2 - a) * 128, (2 - a) * 128 + 640) for a in range(3)]
        flow_grad = nt(
            join(v.hx_j[b, rows[a], c * 256 + 128 : (c + 1) * 256] for a in range(3) for c in range(3)),
            join(v.w_fm[k * 128 : (k + 1) * 128, :] for k in range(9)),
        )
        v.fpg[b] = half_of(flow_grad * full_of(v.slope_fi[b]))
        z = nt(v.w_fi[...], v.fpg[b])
        total = jnp.zeros((32, LANES), jnp.float32)
        lane = lane_index((32, LANES))
        for across in range(7):
            v.fs[across] = jnp.zeros((32, LANES), jnp.float32)
            for y in range(ROWS):
                v.fs[across, 2 * y : 2 * y + 16, :] += z[across * 16 : across * 16 + 16, y * 128 : (y + 1) * 128]
            d = across - 3
            value = v.fs[across]
            if d:
                value = pltpu.roll(value, d % LANES, 1)
                value = jnp.where((lane - d >= 0) & (lane - d < WIDE), value, 0.0)
            total = total + value
        v.gf[b] = total
        return carry

    lax.fori_loop(0, BATCH, image, 0)
    v.halo_gf.start()


def corr_back(v):
    def image(b, carry):
        corr_grad = nt(
            join(v.hx_j[b, (2 - a) * 128 : (2 - a) * 128 + 640, :] for a in range(3)),
            join(v.w_cm[k * 256 : (k + 1) * 256, :] for k in range(9)),
        )
        v.cpg[b] = half_of(corr_grad * full_of(v.slope_ci[b]))
        stores = gcorr_stores(v, b)
        for store in stores:
            pl.when(b > 0)(store.wait)
        gcorr = nt(v.w_ci[...], v.cpg[b])
        for y in range(ROWS):
            v.mm_tmp[y * 328 : y * 328 + CORR, :] = gcorr[:, y * WIDE : (y + 1) * WIDE]
        for store in stores:
            store.start()
        return carry

    lax.fori_loop(0, BATCH, image, 0)


def summed(v, ref, name):
    total = 0.0
    for b in range(BATCH):
        total = total + ones_sum(ref(b))
    keep_bias(v, name, total)


def gradients_motion(v):
    starts = flat_rows()[0]
    summed(v, lambda b: v.mge[b, 256:896, :], MOTION_MIX)
    grads = join((v.mge[b, 256:896, :] for b in range(BATCH)), 0)
    for a in range(3):
        taps = join((v.hx_j[b, a * 128 : a * 128 + 640, :] for b in range(BATCH)), 0)
        v.mm_tmp[a * 768 : (a + 1) * 768, :] = tn(taps, grads)
    lane36 = lane_index((36, LANES))
    for r in range(63):
        first = v.mm_tmp[pl.ds(r, 36, stride=64), :]
        second = v.mm_tmp[pl.ds(r + 1, 36, stride=64), :]
        if r:
            first = pltpu.roll(first, LANES - 2 * r, 1)
        second = pltpu.roll(second, 126 - 2 * r, 1)
        v.flat[pl.ds(MARGIN + r, 36, stride=63), :] = jnp.where(lane36 < 126 - 2 * r, first, second)
    v.flush.layer(starts[MOTION_MIX], 2268)


def gradients_branches(v):
    starts = flat_rows()[0]
    summed(v, lambda b: branch_own(v, b), CORR_MIX)
    summed(v, lambda b: branch_own(v, b, 128, 256), FLOW_MIX)
    grads = join((branch_own(v, b, 128, 256) for b in range(BATCH)), 0)
    for k in range(9):
        a, c = k // 3, k % 3
        if c == 0:
            taps = join((v.hx_f[b, (a + 1) * 128 : (a + 1) * 128 + 640, :] for b in range(BATCH)), 0)
            group = tn(taps, grads)
        v.pair_a[0:128, :] = group[c * 128 : (c + 1) * 128]
        even, odd = (v.pair_a[pl.ds(i, 64, stride=2), :] for i in range(2))
        v.flat[MARGIN + 64 * k : MARGIN + 64 * (k + 1), :] = jnp.where(
            lane_index((64, LANES)) < 64, pltpu.roll(even, 64, 1), odd
        )
    v.flush.layer(starts[FLOW_MIX], 576)

    low_half = lane_index((128, LANES)) < 64
    grads = join((branch_own(v, b) for b in range(BATCH)), 0)
    for k in range(9):
        a, c = k // 3, k % 3
        if c == 0:
            taps = join((v.hx_c[b, (a + 1) * 128 : (a + 1) * 128 + 640, :] for b in range(BATCH)), 0)
            group = tn(taps, grads)
        v.pair_a[...] = group[c * 256 : (c + 1) * 256, 0:128]
        v.pair_b[...] = group[c * 256 : (c + 1) * 256, 128:256]
        even, odd = (v.pair_a[pl.ds(i, 128, stride=2), :] for i in range(2))
        even_high, odd_high = (v.pair_b[pl.ds(i, 128, stride=2), :] for i in range(2))
        odd, odd_high = pltpu.roll(odd, 64, 1), pltpu.roll(odd_high, 64, 1)
        at = MARGIN + 384 * k
        v.flat[pl.ds(at, 128, stride=3), :] = even
        v.flat[pl.ds(at + 1, 128, stride=3), :] = jnp.where(low_half, even_high, odd)
        v.flat[pl.ds(at + 2, 128, stride=3), :] = jnp.where(low_half, odd, odd_high)
        if k == 4:
            v.reduce.tick()
    v.flush.layer(starts[CORR_MIX], 3456)


def gradients_flow_in(v):
    starts = flat_rows()[0]
    summed(v, lambda b: v.fpg[b], FLOW_IN)
    value = 0.0
    for b in range(BATCH):
        value = value + mm(v.xt[b, :, 256:896], v.fpg[b])
    v.flow_tmp[...] = value
    for across in range(7):
        for comp in range(2):
            v.flat[pl.ds(MARGIN + across * 2 + comp, 7, stride=14), :] = v.flow_tmp[
                pl.ds(across * 16 + comp, 7, stride=2), :
            ]
    v.flush.layer(starts[FLOW_IN], 98)


def gradients_corr_in(v):
    starts = flat_rows()[0]
    summed(v, lambda b: v.cpg[b], CORR_IN)
    value = 0.0
    for b in range(BATCH):
        value = value + mm(lines_of(v.corr, b, ROWS), v.cpg[b])
    pack_pairs(v.flat, 0, 324, value[:, 0:128], value[:, 128:256])
    v.flush.layer(starts[CORR_IN], 648)


def bias_tile(v):
    starts, bias_row, spots, inner = flat_rows()
    lead = bias_row % 16
    lane1 = lane_index((1, LANES))
    v.bown[...] = jnp.zeros_like(v.bown)
    for name, height, width in shapes():
        for block in range(-(-width // LANES)):
            value = v.gbias[BIAS_AT[name] + block : BIAS_AT[name] + block + 1, :]
            if name == FLOW_MIX:
                value = pltpu.roll(value, 64, 1)
            left = width - block * LANES
            if left < LANES:
                value = jnp.where(lane1 < left, value, 0.0)
            at = spots[name] + block * LANES
            row, shift = lead + at // LANES, at % LANES
            moved = pltpu.roll(value, shift, 1) if shift else value
            v.bown[row : row + 1, :] = v.bown[row : row + 1, :] + jnp.where(lane1 >= shift, moved, 0.0)
            if shift:
                v.bown[row + 1 : row + 2, :] = v.bown[row + 1 : row + 2, :] + jnp.where(lane1 < shift, moved, 0.0)


def finish(v):
    spot, last = v.spot, v.space - 1
    v.halo_gf.receive()
    for b in range(BATCH):
        v.tmp2[...] = v.gf[b]
        up = jnp.where(spot > 0, v.gf_up[b], 0.0)
        down = jnp.where(spot < last, v.gf_down[b], 0.0)
        v.tmp2[6:12, :] += up[16:22, :]
        v.tmp2[10:16, :] += down[0:6, :]
        for y in range(ROWS):
            v.out_gflow[b, 2 * y : 2 * y + 2, :] = (
                v.tmp2[6 + 2 * y : 8 + 2 * y, :] + v.gf_base[b, 0:2, y * 128 : (y + 1) * 128]
            )
    v.loss_in[v.spot] = v.losses[...]
    total = jnp.sum(v.loss_in[...], axis=0)
    counts = jnp.sum(v.counts[...], axis=0)
    value = total / jnp.maximum(counts, 1.0)
    for b in range(BATCH):
        v.out_loss[b] = v.pick_count(value, b)


class View:
    pass


def main_kernel(names, space, count, *refs):
    v = View()
    for name, ref in zip(names, refs):
        setattr(v, name, ref)
    v.space = space
    v.lu, v.lc = v.motion, v.state
    v.spot = lax.axis_index(SPACE)
    v.rank = lax.axis_index(DP)
    v.mate, v.other, v.twin = mate_of(v.rank), lax.rem(v.rank + 2, 4), mate_of(v.spot)
    spot = v.spot
    barrier = pltpu.get_barrier_semaphore()

    def hello(step, carry):
        pl.semaphore_signal(barrier, inc=1, device_id={SPACE: lax.rem(spot + step, space)}, device_id_type=MESH)
        return carry

    lax.fori_loop(1, space, hello, 0)
    for turn in range(1, 4):

        def greet_rank(step, carry):
            place = lax.rem(spot + 2 * step, space)
            device = {DP: lax.rem(v.rank + turn, 4), SPACE: place}
            pl.semaphore_signal(barrier, inc=1, device_id=device, device_id_type=MESH)
            return carry

        lax.fori_loop(0, space // 2, greet_rank, 0)
    pl.semaphore_wait(barrier, space - 1 + 3 * (space // 2))

    v.store_gnet = pltpu.make_async_copy(v.ru, v.out_gnet, v.osem.at[0])
    v.store_gctx = pltpu.make_async_copy(v.rr, v.out_gctx, v.osem.at[1])
    rows = row_index((8, LANES))
    counted = jnp.zeros((8, LANES), jnp.float32)
    for b in range(BATCH):
        counted = jnp.where(rows == b, jnp.sum(v.valid[b].astype(jnp.float32)), counted)
    v.count_out[...] = counted
    v.pick_count = lambda counts, b: jnp.sum(jnp.where((rows == b) & (lane_index((8, LANES)) == 0), counts, 0.0))
    v.swap_count = Swap(v, 0, v.count_out, v.counts, True)
    v.swap_context = Swap(v, 1, v.a_context, v.b_context)
    v.swap_motion = Swap(v, 2, v.a_motion, v.b_motion)
    v.swap_state = Swap(v, 3, v.a_state, v.b_state)
    v.back_context = Swap(v, 4, v.a_context, v.b_context)
    v.back_motion = Swap(v, 5, v.a_motion, v.b_motion)
    v.back_state = Swap(v, 6, v.a_state, v.b_state)
    v.swap_loss = Swap(v, 7, v.losses, v.loss_in, True)
    v.halo_corr = Halo(v, 0, v.corr.at[:, 0:2], v.corr.at[:, 3:5], v.corr_down, v.corr_up)
    v.halo_flow = Halo(v, 1, v.flow, v.flow, v.flow_down, v.flow_up)
    v.halo_final = Halo(v, 2, v.e_left, v.e_right, v.f_right, v.f_left)
    v.halo_mask = Halo(v, 3, v.m_left, v.m_right, v.n_right, v.n_left)
    v.halo_dg = Halo(v, 4, v.dg, v.dg, v.dg_right, v.dg_left)
    v.halo_mg = Halo(v, 5, v.mge.at[:, 256:512], v.mge.at[:, 640:896], v.mge.at[:, 896:1152], v.mge.at[:, 0:256])
    v.halo_gf = Halo(v, 6, v.gf, v.gf, v.gf_down, v.gf_up)

    load = pltpu.make_async_copy(v.local, v.gath.at[0:BLOCK], v.gsend.at[4, 2])
    load.start()
    for b in range(BATCH):
        for y in range(ROWS):
            v.flow[b, 2 * y : 2 * y + 2, :] = full_of(v.flow_in[b, y])
        v.flow[b, 2 * ROWS : 16, :] = jnp.zeros((16 - 2 * ROWS, LANES), jnp.float32)
    v.halo_flow.start()
    v.halo_corr.start()
    v.swap_count.start()
    load.wait()
    gather_start(v, count)

    def first(b, carry):
        v.state[b] = full_of(v.context[b])
        pack_rows(v, v.state, b, v.a_context)
        return carry

    lax.fori_loop(0, BATCH, first, 0)
    v.swap_context.start()
    v.halo_flow.receive()
    widen_all(v)
    gather_pass(v, 0, 3)
    early_taps(v)
    gather_pass(v, 3, 6)
    columns_zero(v)
    gather_pass(v, 6, 8)
    gather_end(v)
    unpack_encoder(v, count)
    v.halo_corr.receive()
    forward_rows(v)
    keep = [pltpu.make_async_copy(v.hx_c, v.out_keep_c, v.ksem.at[0]), pltpu.make_async_copy(v.hx_f, v.out_keep_f, v.ksem.at[1])]
    for copy in keep:
        copy.start()
    unpack_heads(v)
    v.swap_context.receive()
    v.swap_motion.receive()
    v.swap_state.receive()
    take_own(v, v.a_context, v.b_context)
    take_own(v, v.a_motion, v.b_motion)
    take_own(v, v.a_state, v.b_state)
    columns_in(v)
    columns_forward(v)
    mask_gradient(v)
    for copy in keep:
        copy.wait()
    heads(v)
    mask_output(v)
    v.swap_context.sent()
    v.swap_motion.sent()
    v.swap_state.sent()
    heads_back(v)
    v.flush = Flush(v)
    red = v.reduce = Reduce(v, count)
    gradients_heads(v)
    v.back_context.start()
    v.back_motion.start()
    red.offer(0)
    red.tick()
    gradients_gru(
        v,
        COLUMNS_GATES,
        COLUMNS_CANDIDATE,
        lambda t: (
            lambda b: v.xc[b, t * COLS : t * COLS + AREA, 0:128],
            lambda b: v.xc[b, t * COLS : t * COLS + AREA, 128:384],
            lambda b: v.xcr[b, t * COLS : t * COLS + AREA, :],
        ),
        lambda b, low=0, high=384: v.gc[b, 32 : 32 + AREA, low:high],
    )
    red.offer(1, 2)
    red.tick()
    rows_back(v)
    red.tick()
    keep = [
        pltpu.make_async_copy(v.out_keep_c, v.hx_c, v.ksem.at[0]),
        pltpu.make_async_copy(v.out_keep_f, v.hx_f, v.ksem.at[1]),
    ]
    for copy in keep:
        copy.start()
    gradients_gru(
        v,
        ROWS_GATES,
        ROWS_CANDIDATE,
        lambda t: (
            lambda b: v.xs[b * AREA : (b + 1) * AREA, t * 128 : (t + 1) * 128],
            lambda b: v.xi[b * AREA : (b + 1) * AREA, t * 256 : (t + 1) * 256],
            lambda b: v.xr[b * AREA : (b + 1) * AREA, t * 128 : (t + 1) * 128],
        ),
        lambda b, low=0, high=384: v.gr[b, :, low:high],
    )
    red.offer(3, 4)
    red.tick()
    gradients_motion(v)
    red.offer(5)
    red.tick()
    branch_back(v)
    red.tick()
    for copy in keep:
        copy.wait()
    gradients_branches(v)
    red.offer(6, now=True)
    red.tick()
    flow_back(v)
    red.tick()
    gradients_flow_in(v)
    red.offer(7, now=True)
    red.tick()
    corr_back(v)
    red.tick()
    gradients_corr_in(v)
    bias_tile(v)
    red.bias_core()
    red.offer(8, now=True)
    red.tick()
    for store in gcorr_stores(v, 0):
        store.wait()
    finish(v)
    red.bias_across()
    red.tick()
    red.bias_stripes()
    pl.when(v.rank == 0)(lambda: red.lay(4, 15))
    red.tick()
    red.bias_end()
    red.ready()
    pl.when(v.rank > 0)(lambda: red.lay(0, 24))
    red.tick()
    pl.when(v.rank == 0)(lambda: red.lay(15, 24))
    red.tick()
    assert not red.flying and not red.queue
    pl.when(v.rank == 0)(lambda: red.lay(0, 4))
    red.settle()
    for swap in (v.swap_count, v.back_context, v.back_motion, v.back_state, v.swap_loss):
        swap.sent()
    for halo in (v.halo_corr, v.halo_flow, v.halo_final, v.halo_mask, v.halo_dg, v.halo_mg, v.halo_gf):
        halo.sent()
    v.store_gnet.wait()
    v.store_gctx.wait()
    pltpu.make_async_copy(v.mask_low, v.out_mask.at[0], v.osem.at[3]).wait()


def main_call(space, count, local, net, context, corr, flow, target, valid, grad_net, grad_mask):
    total = 3 * count // (LANES * 16) * 16 + BLOCK
    low, wide = jnp.bfloat16, jnp.float32
    peers = (space, BATCH, ROWS * COLS, LANES)
    ins = dict(
        local=local, net=net, context=context, corr=corr, flow_in=flow, target=target, valid=valid,
        grad_net=grad_net, grad_mask=grad_mask,
    )
    outs = dict(
        out_net=((BATCH, AREA, 128), low),
        out_flow=((BATCH, 2, COLS, TALL), wide),
        out_mask=((BATCH, AREA, MASK), low),
        out_loss=((BATCH,), wide),
        out_flat=((total, 128), low),
        out_gnet=((BATCH, AREA, 128), wide),
        out_gctx=((BATCH, AREA, 128), wide),
        out_gcorr=((BATCH, ROWS, CORR, 128), wide),
        out_gflow=((BATCH, 16, 128), wide),
        out_keep_c=((BATCH, 1152, 768), low),
        out_keep_f=((BATCH, 1152, 384), low),
        out_all=((4 * BLOCK, 128), low),
        out_grads=((BLOCK, 128), wide),
    )
    scratch = dict(
        stage=((2, 3904, 128), low),
        seam=((16, 16, 128), wide),
        mask_low=((AREA, MASK), low),
        seam_low=((16 * 20, 128), low),
        own=((2, SHARE // 2, 128), low),
        rcore=((2, SHARE // 2, 128), low),
        tx=((2, SHARE // 4, 128), low),
        rx=((2, SHARE // 4, 128), low),
        ks=((2, SHARE // 4, 128), wide),
        ts=((2, SHARE // 4, 128), low),
        acc=((2, SHARE // 4 // space, 128), wide),
        rs=((2, space, SHARE // 4 // space, 128), low),
        fin=((2, SHARE // 4 // space, 128), low),
        dall=((4, 256, 128), low),
        ty=((2, SHARE // 8, 128), low),
        ry=((2, SHARE // 8, 128), low),
        ky=((2, SHARE // 8, 128), wide),
        tz=((2, SHARE // 8, 128), low),
        rz=((2, space // 2, SHARE // 4 // space, 128), low),
        kz=((2, SHARE // 4 // space, 128), wide),
        az=((3, SHARE // 8, 128), low),
        gath=((2 * SHARE + 32, 128), low),
        bown=((32, 128), wide), bcore=((32, 128), wide), btwo=((32, 128), wide), bacross=((32, 128), wide),
        bfour=((32, 128), wide), ball=((space, 32, 128), wide), bsum=((32, 128), wide),
        flat=((3904, 128), wide),
        pair_a=((256, 128), wide),
        pair_b=((256, 128), wide),
        flow_tmp=((112, 128), wide),
        mm_tmp=((3 * (2 * EDGE + SPREAD), 128), wide),
        fo_tmp=((32, 128), wide),
        fo_tmp2=((32, 128), wide),
        w_ci=((CORR, 256), low),
        w_cm=((2304, 256), low),
        w_fi=((112, 128), low),
        w_fm=((1152, 128), low),
        w_mm=((2304, 128), low),
        w_ri=((1280, 384), low),
        w_rs=((640, 384), low),
        w_li=((1280, 384), low),
        w_ls=((640, 384), low),
        w_h=((1152, 512), low),
        w_fo=((32, 256), low),
        w_mo=((256, 640), low),
        bias=((BIAS_ROWS, 128), wide),
        gbias=((BIAS_ROWS, 128), wide),
        corr_up=((BATCH, 2, CORR, 128), low),
        corr_down=((BATCH, 2, CORR, 128), low),
        flow_up=((BATCH, 16, 128), wide),
        flow_down=((BATCH, 16, 128), wide),
        fs=((7, 32, 128), wide),
        xt=((BATCH, 112, 1152), low),
        tmp=((1168, 128), wide),
        tmp2=((32, 128), wide),
        hx_c=((BATCH, 1152, 768), low),
        hx_f=((BATCH, 1152, 384), low),
        hx_j=((BATCH, 896, 768), low),
        slope_ci=((BATCH, AREA, 256), low),
        slope_fi=((BATCH, AREA, 128), low),
        slope_j=((BATCH, 896, 256), low),
        slope_m=((BATCH, AREA, 128), low),
        motion=((BATCH, AREA, 128), wide),
        state=((BATCH, AREA, 128), wide),
        xi=((BATCH * AREA, 1280), low),
        xs=((BATCH * AREA, 640), low),
        xr=((BATCH * AREA, 640), low),
        ru=((BATCH, AREA, 128), wide),
        rr=((BATCH, AREA, 128), wide),
        rc=((BATCH, AREA, 128), wide),
        lr=((BATCH, AREA, 128), wide),
        a_state=(peers, low), a_context=(peers, low), a_motion=(peers, low),
        b_state=(peers, low), b_context=(peers, low), b_motion=(peers, low),
        xc=((BATCH, AREA + 64, 384), low),
        xcr=((BATCH, AREA + 64, 128), low),
        gc=((BATCH, AREA + 64, 384), low),
        final=((AREA, 128), wide),
        e_left=((BATCH, 2, 48, 128), low), e_right=((BATCH, 2, 48, 128), low),
        f_left=((BATCH, 2, 48, 128), low), f_right=((BATCH, 2, 48, 128), low),
        m_left=((BATCH, 2, 48, 128), low), m_right=((BATCH, 2, 48, 128), low),
        n_left=((BATCH, 2, 48, 128), low), n_right=((BATCH, 2, 48, 128), low),
        slope_h=((BATCH, SPREAD, 512), low),
        feat=((BATCH, SPAN, 256), low),
        mf=((BATCH, AREA, 256), low),
        dg=((BATCH, 8, SPAN), wide),
        target_wide=((BATCH, 8, SPAN), wide),
        valid_wide=((BATCH, 8, SPAN), wide),
        flow=((BATCH, 16, 128), wide),
        dg_left=((BATCH, 8, SPAN), wide), dg_right=((BATCH, 8, SPAN), wide),
        dt=((32, SPAN), wide),
        dto=((32, SPAN), wide),
        dtb=((BATCH, 32, SPAN), low),
        hgo=((BATCH, SPREAD, 512), low),
        gr=((BATCH, AREA, 384), low),
        mge=((BATCH, 1152, 128), low),
        cpg=((BATCH, AREA, 256), low),
        fpg=((BATCH, AREA, 128), low),
        gf_base=((BATCH, 8, AREA), wide),
        gf=((BATCH, 32, 128), wide), gf_up=((BATCH, 32, 128), wide), gf_down=((BATCH, 32, 128), wide),
        count_out=((8, 128), wide), counts=((space, 8, 128), wide),
        losses=((8, 128), wide), loss_in=((space, 8, 128), wide),
    )
    sems = dict(
        hsend=pltpu.SemaphoreType.DMA((7, 2)), hrecv=pltpu.SemaphoreType.DMA((7, 2)),
        asend=pltpu.SemaphoreType.DMA((9,)), arecv=pltpu.SemaphoreType.DMA((9,)),
        ssem=pltpu.SemaphoreType.DMA((2, 2)),
        fsem=pltpu.SemaphoreType.DMA((17,)),
        rsend=pltpu.SemaphoreType.DMA((3, 2)), rrecv=pltpu.SemaphoreType.DMA((3, 2)),
        z1send=pltpu.SemaphoreType.DMA((2,)), z1recv=pltpu.SemaphoreType.DMA((2,)),
        z2send=pltpu.SemaphoreType.DMA((3,)), z2recv=pltpu.SemaphoreType.DMA((3,)),
        osend=pltpu.SemaphoreType.DMA((3,)), orecv=pltpu.SemaphoreType.DMA((9,)),
        rlocal=pltpu.SemaphoreType.DMA((2,)),
        s2send=pltpu.SemaphoreType.DMA((2,)), s2recv=pltpu.SemaphoreType.DMA((2,)),
        fsend=pltpu.SemaphoreType.DMA((2,)), frecv=pltpu.SemaphoreType.DMA((9,)),
        ysend=pltpu.SemaphoreType.DMA((9,)), yrecv=pltpu.SemaphoreType.DMA((9,)),
        dsend=pltpu.SemaphoreType.DMA, drecv=pltpu.SemaphoreType.DMA,
        bsend=pltpu.SemaphoreType.DMA((2,)), brecv=pltpu.SemaphoreType.DMA((2,)),
        ksem=pltpu.SemaphoreType.DMA((2,)),
        gsend=pltpu.SemaphoreType.DMA((5, 8)), grecv=pltpu.SemaphoreType.DMA((5, 8)),
        gsem=pltpu.SemaphoreType.DMA((ROWS,)),
        osem=pltpu.SemaphoreType.DMA((6,)),
    )
    vmem = pl.BlockSpec(memory_space=pltpu.VMEM)
    hbm = pl.BlockSpec(memory_space=pl.ANY)
    names = list(ins) + list(outs) + list(scratch) + list(sems)
    return pl.pallas_call(
        functools.partial(main_kernel, names, space, count),
        out_shape=[jax.ShapeDtypeStruct(*entry) for entry in outs.values()],
        in_specs=[hbm if name == "local" else vmem for name in ins],
        out_specs=[pl.BlockSpec(memory_space=pltpu.SMEM) if name == "out_loss" else hbm if name in ("out_flat", "out_gnet", "out_gctx", "out_gcorr", "out_keep_c", "out_keep_f", "out_mask", "out_grads", "out_all") else vmem for name in outs],
        scratch_shapes=[pltpu.VMEM(*entry) for entry in scratch.values()] + list(sems.values()),
        compiler_params=pltpu.CompilerParams(
            collective_id=2, has_side_effects=True, vmem_limit_bytes=VMEM_LIMIT
        ),
    )(*ins.values())


VMEM_LIMIT = 64 * 2**20 - 2**16


def shards_wide(net, context, corr, flow, target, valid, grad_net, grad_mask, params):
    space = lax.axis_size(SPACE)
    count = params.shape[0]
    local = jnp.pad(params, (0, BLOCK * LANES - count)).reshape(BLOCK, LANES)
    outs = main_call(
        space, count, local, net.reshape(BATCH, AREA, HID), context.reshape(BATCH, AREA, CTX),
        jnp.transpose(corr, (0, 1, 3, 2)), jnp.transpose(flow, (0, 2, 1, 3)), jnp.transpose(target, (0, 1, 3, 2)),
        jnp.transpose(valid, (0, 2, 1)),
        grad_net.reshape(BATCH, AREA, HID), grad_mask.reshape(BATCH, AREA, MASK),
    )
    new_net, new_flow, mask, loss, _, gnet, gctx, gcorr, gflow = outs[:9]
    new_flow = jnp.transpose(new_flow, (0, 1, 3, 2))
    grads = outs[-1].reshape(-1)[:count]
    return (
        new_net.reshape(BATCH, TALL, COLS, HID),
        new_flow,
        mask.reshape(BATCH, TALL, COLS, MASK),
        loss,
        grads,
        gnet.reshape(BATCH, ROWS, WIDE, HID),
        gctx.reshape(BATCH, ROWS, WIDE, CTX),
        jnp.transpose(gcorr, (0, 1, 3, 2)),
        jnp.transpose(gflow[:, 0 : 2 * ROWS].reshape(BATCH, ROWS, 2, WIDE), (0, 2, 1, 3)),
    )


def solution(mesh):
    def plan(*arrays):
        net, valid = arrays[0], arrays[5]
        if (net.shape[1:3], valid.shape[1:]) == ((ROWS, WIDE), (TALL, COLS)):
            return shards_wide(*arrays)
        return shards(*arrays)

    return jax.shard_map(
        plan,
        mesh=mesh,
        in_specs=(
            P(DP, SPACE, None, None),
            P(DP, SPACE, None, None),
            P(DP, SPACE, None, None),
            P(DP, None, SPACE, None),
            P(DP, None, None, SPACE),
            P(DP, None, SPACE),
            P(DP, None, SPACE, None),
            P(DP, None, SPACE, None),
            P(DP),
        ),
        out_specs=(
            P(DP, None, SPACE, None),
            P(DP, None, None, SPACE),
            P(DP, None, SPACE, None),
            P(DP),
            P(DP),
            P(DP, SPACE, None, None),
            P(DP, SPACE, None, None),
            P(DP, SPACE, None, None),
            P(DP, None, SPACE, None),
        ),
        check_vma=False,
    )
```

```python
import functools

import jax
import jax.numpy as jnp
from jax import lax
from jax.experimental import pallas as pl
from jax.experimental.pallas import tpu as pltpu
from jax.sharding import PartitionSpec as P

HID = 128
CTX = 128
MOT = 128
CORR = 324
SPACE = "space"
DP = "dp"
(
    CORR_IN,
    CORR_MIX,
    FLOW_IN,
    FLOW_MIX,
    MOTION_MIX,
    ROWS_GATES,
    ROWS_CANDIDATE,
    COLUMNS_GATES,
    COLUMNS_CANDIDATE,
    FLOW_HIDDEN,
    FLOW_OUT,
    MASK_HIDDEN,
    MASK_OUT,
) = range(13)
C1 = 256
C2 = 192
F1 = 128
F2 = 64
HEAD = 256
MASK = 576


def with_halo(block, sides, width):
    for axis, dim in sides:
        count = lax.axis_size(axis)
        forward = [(i, i + 1) for i in range(count - 1)]
        backward = [(target, source) for source, target in forward]
        low = lax.ppermute(
            lax.slice_in_dim(block, block.shape[dim] - width, None, axis=dim), axis, forward
        )
        high = lax.ppermute(lax.slice_in_dim(block, 0, width, axis=dim), axis, backward)
        block = jnp.concatenate([low, block, high], axis=dim)
    return block


def shapes():
    inputs_width = HID + CTX + MOT
    return [
        (CORR_IN, CORR, C1),
        (CORR_MIX, 9 * C1, C2),
        (FLOW_IN, 98, F1),
        (FLOW_MIX, 9 * F1, F2),
        (MOTION_MIX, 9 * (C2 + F2), MOT - 2),
        (ROWS_GATES, 5 * inputs_width, 2 * HID),
        (ROWS_CANDIDATE, 5 * inputs_width, HID),
        (COLUMNS_GATES, 5 * inputs_width, 2 * HID),
        (COLUMNS_CANDIDATE, 5 * inputs_width, HID),
        (FLOW_HIDDEN, 9 * HID, HEAD),
        (FLOW_OUT, 9 * HEAD, 2),
        (MASK_HIDDEN, 9 * HID, HEAD),
        (MASK_OUT, HEAD, MASK),
    ]


def unpack(flat):
    weights = {}
    biases = {}
    offset = 0
    table = shapes()
    for name, height, width in table:
        weights[name] = flat[offset // LANES : (offset + height * width) // LANES].reshape(height, width)
        offset = offset + height * width
    rest = flat[offset // LANES :].reshape(-1)
    offset = 0
    for name, height, width in table:
        biases[name] = rest[offset : offset + width].astype(jnp.float32)
        offset = offset + width
    return (weights, biases)


def pack(grads, total):
    table = shapes()
    rows = [grads[entry[0]][0].astype(jnp.bfloat16).reshape(-1, LANES) for entry in table]
    biases = jnp.concatenate([grads[entry[0]][1] for entry in table]).astype(jnp.bfloat16)
    left = total * LANES - sum(entry[1] * entry[2] for entry in table) - biases.shape[0]
    return jnp.concatenate(rows + [jnp.pad(biases, (0, left)).reshape(-1, LANES)])


def patches(padded, tall, wide):
    out_rows = padded.shape[1] - tall + 1
    out_columns = padded.shape[2] - wide + 1
    return jnp.concatenate(
        [
            padded[:, down : down + out_rows, across : across + out_columns]
            for down in range(tall)
            for across in range(wide)
        ],
        axis=-1,
    )


def apply(stacked, weight):
    return jnp.einsum("bhwk,ko->bhwo", stacked, weight, preferred_element_type=jnp.float32)


def apply_back(grad, weight):
    return jnp.einsum("bhwo,ko->bhwk", grad, weight, preferred_element_type=jnp.float32)


def weight_grad(stacked, pre_grad):
    return jnp.einsum("bhwk,bhwo->ko", stacked, pre_grad, preferred_element_type=jnp.float32)


def record(grads, name, stacked, pre_grad):
    grads[name] = (
        weight_grad(stacked, pre_grad),
        jnp.sum(pre_grad, axis=(0, 1, 2), dtype=jnp.float32),
    )


def flipped(weight, tall, wide):
    inner = weight.shape[0] // (tall * wide)
    shaped = weight.reshape(tall, wide, inner, weight.shape[1])[::-1, ::-1]
    return jnp.transpose(shaped, (0, 1, 3, 2)).reshape(-1, inner)


def slope(pre):
    sigma = jax.nn.sigmoid(pre)
    return sigma * (1.0 + pre * (1.0 - sigma))


def local_pad(field, tall, wide):
    return jnp.pad(field, ((0, 0), (tall // 2, tall // 2), (wide // 2, wide // 2), (0, 0)))


def row_pad(field, tall):
    field = with_halo(field, ((SPACE, 1),), tall // 2)
    return jnp.pad(field, ((0, 0), (0, 0), (tall // 2, tall // 2), (0, 0)))


def column_pad(field, tall, wide):
    field = with_halo(field, ((SPACE, 2),), wide // 2)
    return jnp.pad(field, ((0, 0), (tall // 2, tall // 2), (0, 0), (0, 0)))


MESH = pl.DeviceIdType.MESH
LANES = 128
BLOCK = 6144


def quarter_start(rank, count):
    return lax.div(rank * count, LANES)


def quarter_base(rank, count):
    return lax.div(rank * count, LANES * 16) * 16


def mate_of(rank):
    return rank + 1 - 2 * lax.rem(rank, 2)


def remote(src, dst, send, recv, device):
    return pltpu.make_async_remote_copy(
        src_ref=src, dst_ref=dst, send_sem=send, recv_sem=recv, device_id=device, device_id_type=MESH
    )


def greet(devices):
    barrier = pltpu.get_barrier_semaphore()
    for device in devices:
        pl.semaphore_signal(barrier, inc=1, device_id=device, device_id_type=MESH)
    pl.semaphore_wait(barrier, len(devices))


def lane_matrix(shift, forward):
    source = lax.broadcasted_iota(jnp.int32, (LANES, 2 * LANES), 0)
    target = lax.broadcasted_iota(jnp.int32, (LANES, 2 * LANES), 1)
    if forward:
        return jnp.where(target == source + shift, 1.0, 0.0).astype(jnp.bfloat16)
    return jnp.where(lax.rem(target + LANES, 2 * LANES) == source - shift + LANES, 1.0, 0.0).astype(jnp.bfloat16)


def gather_kernel(count, local_ref, out_ref, own_ref, send, recv):
    rank, spot = lax.axis_index(DP), lax.axis_index(SPACE)
    mate, across, twin = mate_of(rank), lax.rem(rank + 2, 4), mate_of(spot)
    pieces = 4
    rows = BLOCK // 2 // pieces
    peers = ({DP: mate}, {DP: across}, {SPACE: twin})
    greet(peers)
    matrix = lane_matrix(lax.rem(rank * count, LANES), True)
    first = lax.broadcasted_iota(jnp.int32, (256, LANES), 0) == 0

    def rotate(step, carry):
        at = pl.ds(pl.multiple_of(step * 256, 256), 256)
        both = jnp.dot(local_ref[at, :], matrix, preferred_element_type=jnp.float32)
        spill = pltpu.roll(both[:, LANES:], 1, 0)
        own_ref[at, :] = (both[:, :LANES] + jnp.where(first, carry, spill)).astype(jnp.bfloat16)
        return spill[0:1]

    lax.fori_loop(0, BLOCK // 256, rotate, jnp.zeros((1, LANES), jnp.float32))

    half, other_half = lax.rem(spot, 2), lax.rem(spot + 1, 2)

    def piece(which, index):
        return pl.ds(pl.multiple_of(which * (BLOCK // 2) + index * rows, 16), rows)

    own_x = [
        remote(own_ref.at[piece(half, k)], out_ref.at[rank, piece(half, k)], send.at[0, k], recv.at[0, k], peers[1])
        for k in range(pieces)
    ]
    own_c = remote(own_ref, out_ref.at[rank], send.at[4, 0], recv.at[4, 0], peers[0])
    for copy in own_x:
        copy.start()
    own_c.start()
    later = []
    for k in range(pieces):
        own_x[k].wait_recv()
        block = out_ref.at[across, piece(half, k)]
        to_twin = remote(block, block, send.at[1, k], recv.at[1, k], peers[2])
        to_mate = remote(block, block, send.at[2, k], recv.at[2, k], peers[0])
        to_twin.start()
        to_mate.start()
        later.append((to_twin, to_mate))
    for at in range(BLOCK // 256):
        out_ref[rank, at * 256 : (at + 1) * 256, :] = own_ref[at * 256 : (at + 1) * 256, :]
    for k in range(pieces):
        later[k][0].wait_recv()
        block = out_ref.at[across, piece(other_half, k)]
        to_mate = remote(block, block, send.at[3, k], recv.at[3, k], peers[0])
        to_mate.start()
        later.append((to_mate,))
    for k in range(pieces):
        own_x[k].wait_send()
        later[k][0].wait_send()
        later[k][1].wait()
        later[pieces + k][0].wait()
    own_c.wait()


def gather_blocks(params):
    count = params.shape[0]
    local = jnp.pad(params, (0, BLOCK * LANES - count)).reshape(BLOCK, LANES)
    return pl.pallas_call(
        functools.partial(gather_kernel, count),
        out_shape=jax.ShapeDtypeStruct((4, BLOCK, LANES), jnp.bfloat16),
        in_specs=[pl.BlockSpec(memory_space=pltpu.VMEM)],
        out_specs=pl.BlockSpec(memory_space=pltpu.VMEM),
        scratch_shapes=[
            pltpu.VMEM((BLOCK, LANES), jnp.bfloat16),
            pltpu.SemaphoreType.DMA((5, 4)),
            pltpu.SemaphoreType.DMA((5, 4)),
        ],
        compiler_params=pltpu.CompilerParams(
            collective_id=0, has_side_effects=True, vmem_limit_bytes=32 * 2**20
        ),
    )(local)


def gather_params(params):
    count = params.shape[0]
    blocks = gather_blocks(params)
    pieces = []
    reach = 0
    for rank in range(4):
        start = rank * count // LANES
        stop = -(-(rank + 1) * count // LANES)
        head = blocks[rank, :1] if rank == 0 else blocks[rank, :1] + pieces.pop()
        pieces += [head, blocks[rank, 1 : stop - start - 1], blocks[rank, stop - start - 1 : stop - start]]
    return jnp.concatenate(pieces)


def reduce_kernel(count, space, pieces, grads_ref, out_ref, rc, tx, rx, acc, ty, ry, tz, rz, gath, send, recv, zsend, zrecv):
    rank, spot = lax.axis_index(DP), lax.axis_index(SPACE)
    mate, across, twin = mate_of(rank), lax.rem(rank + 2, 4), mate_of(spot)
    group = space // 2
    side, depth = lax.rem(spot, 2), lax.div(spot, 2)
    rows = BLOCK // pieces
    half = rows // 2
    part = half // group

    def partner(step):
        return lax.rem(depth + step, group)

    peers = [{DP: mate}, {DP: across}, {SPACE: twin}]
    barrier = pltpu.get_barrier_semaphore()
    for device in peers:
        pl.semaphore_signal(barrier, inc=1, device_id=device, device_id_type=MESH)

    def hello(step, carry):
        pl.semaphore_signal(barrier, inc=1, device_id={SPACE: partner(step) * 2 + side}, device_id_type=MESH)
        return carry

    lax.fori_loop(1, group, hello, 0)
    pl.semaphore_wait(barrier, 3 + group - 1)

    gath[BLOCK:, :] = jnp.zeros((32, LANES), jnp.bfloat16)
    lower = lax.rem(rank, 2)
    upper = lax.div(rank, 2)

    def base(who):
        return pl.multiple_of(quarter_base(who, count), 16)

    def rows_of(start, index, length):
        return pl.ds(pl.multiple_of(start + index, 16), length)

    core = []
    for p in range(pieces):
        for high in range(2):
            copy = remote(
                grads_ref.at[rows_of(base(2 * high + 1 - lower), p * rows, rows)],
                rc.at[p, high],
                send.at[high, p],
                recv.at[high, p],
                peers[0],
            )
            copy.start()
            core.append(copy)
    step_rows = 192 if half % 192 == 0 else 16
    xs, ys, gs = [], [], []

    def z_copy(p, step):
        to = partner(step)
        return remote(
            tz.at[p, pl.ds(pl.multiple_of(to * part, 16), part)],
            rz.at[p, pl.ds(pl.multiple_of(depth * part, 16), part)],
            zsend.at[0, p, step],
            zrecv.at[0, p, step],
            {SPACE: to * 2 + side},
        )

    def home(p, which, slot):
        return pl.ds(pl.multiple_of(p * rows + which * half + slot * part, 16), part)

    def g_copy(p, step):
        block = gath.at[home(p, side, depth)]
        return remote(block, block, zsend.at[1, p, step], zrecv.at[1, p, step], {SPACE: partner(step) * 2 + side})

    def each(body):
        def run(step, carry):
            body(step)
            return carry

        lax.fori_loop(1, group, run, 0)

    def stage_core(p):
        core[2 * p].wait_recv()
        core[2 * p + 1].wait_recv()
        far = 1 - upper

        def add(step, carry):
            at = pl.multiple_of(step * step_rows, 16)
            mine = grads_ref[rows_of(base(2 * far + lower), p * rows + at, step_rows), :].astype(jnp.float32)
            tx[p, pl.ds(at, step_rows), :] = (
                mine + rc[p, far, pl.ds(at, step_rows), :].astype(jnp.float32)
            ).astype(jnp.bfloat16)
            return carry

        lax.fori_loop(0, rows // step_rows, add, 0)
        copy = remote(tx.at[p], rx.at[p], send.at[2, p], recv.at[2, p], peers[1])
        copy.start()
        xs.append(copy)

    def stage_x(p):
        xs[p].wait_recv()

        def total(at):
            return (
                grads_ref[rows_of(base(rank), p * rows + at, step_rows), :].astype(jnp.float32)
                + rc[p, upper, pl.ds(at, step_rows), :].astype(jnp.float32)
                + rx[p, pl.ds(at, step_rows), :].astype(jnp.float32)
            )

        def add(step, carry):
            at = pl.multiple_of(step * step_rows, 16)
            far = pl.multiple_of((1 - side) * half + at, 16)
            near = pl.multiple_of(side * half + at, 16)
            ty[p, pl.ds(at, step_rows), :] = total(far).astype(jnp.bfloat16)
            acc[p, pl.ds(at, step_rows), :] = total(near)
            return carry

        lax.fori_loop(0, half // step_rows, add, 0)
        copy = remote(ty.at[p], ry.at[p], send.at[3, p], recv.at[3, p], peers[2])
        copy.start()
        ys.append(copy)

    def stage_y(p):
        ys[p].wait_recv()

        def add(step, carry):
            at = pl.ds(pl.multiple_of(step * step_rows, 16), step_rows)
            value = acc[p, at, :] + ry[p, at, :].astype(jnp.float32)
            acc[p, at, :] = value
            tz[p, at, :] = value.astype(jnp.bfloat16)
            return carry

        lax.fori_loop(0, half // step_rows, add, 0)
        each(lambda step: z_copy(p, step).start())

    def stage_z(p):
        each(lambda step: z_copy(p, step).wait_recv())
        value = acc[p, pl.ds(pl.multiple_of(depth * part, 16), part), :]

        def add(step, value):
            other = lax.rem(depth + group - step, group)
            return value + rz[p, pl.ds(pl.multiple_of(other * part, 16), part), :].astype(jnp.float32)

        value = lax.fori_loop(1, group, add, value)
        gath[home(p, side, depth), :] = value.astype(jnp.bfloat16)
        each(lambda step: g_copy(p, step).start())

    def stage_zg(p):
        each(lambda step: g_copy(p, step).wait_recv())
        block = gath.at[pl.ds(pl.multiple_of(p * rows + side * half, 16), half)]
        copy = remote(block, block, send.at[4, p], recv.at[4, p], peers[2])
        copy.start()
        gs.append(copy)

    def stage_yg(p):
        gs[p].wait_recv()

    stages = [stage_core, stage_x, stage_y, stage_z, stage_zg, stage_yg]
    for tick in range(pieces + len(stages) - 1):
        for number in reversed(range(len(stages))):
            if 0 <= tick - number < pieces:
                stages[number](tick - number)

    for copy in core + xs + ys + gs:
        copy.wait_send()
    for p in range(pieces):

        def done(step):
            z_copy(p, step).wait_send()
            g_copy(p, step).wait_send()

        each(done)

    offset = rank * count - quarter_base(rank, count) * LANES
    skip = lax.div(offset, LANES)
    matrix = lane_matrix(lax.rem(offset, LANES), False)
    wide = jnp.where(
        lax.broadcasted_iota(jnp.int32, (256, 288), 1)
        == lax.broadcasted_iota(jnp.int32, (256, 288), 0) + skip,
        1.0,
        0.0,
    ).astype(jnp.bfloat16)
    wide_next = jnp.where(
        lax.broadcasted_iota(jnp.int32, (256, 288), 1)
        == lax.broadcasted_iota(jnp.int32, (256, 288), 0) + skip + 1,
        1.0,
        0.0,
    ).astype(jnp.bfloat16)

    def place(step, carry):
        at = pl.multiple_of(step * 256, 256)
        block = gath[pl.ds(at, 288), :]
        both = jnp.dot(block, matrix, preferred_element_type=jnp.float32).astype(jnp.bfloat16)
        out_ref[pl.ds(at, 256), :] = jnp.dot(wide, both[:, :LANES], preferred_element_type=jnp.float32) + jnp.dot(
            wide_next, both[:, LANES:], preferred_element_type=jnp.float32
        )
        return carry

    lax.fori_loop(0, BLOCK // 256, place, 0)


def reduce_grads(flat, space, count):
    pieces = next(k for k in (4, 2, 1) if BLOCK // (k * space) % 16 == 0)
    rows = BLOCK // pieces
    half = rows // 2
    out = pl.pallas_call(
        functools.partial(reduce_kernel, count, space, pieces),
        out_shape=jax.ShapeDtypeStruct((BLOCK, LANES), jnp.float32),
        in_specs=[pl.BlockSpec(memory_space=pltpu.VMEM)],
        out_specs=pl.BlockSpec(memory_space=pltpu.VMEM),
        scratch_shapes=[
            pltpu.VMEM((pieces, 2, rows, LANES), jnp.bfloat16),
            pltpu.VMEM((pieces, rows, LANES), jnp.bfloat16),
            pltpu.VMEM((pieces, rows, LANES), jnp.bfloat16),
            pltpu.VMEM((pieces, half, LANES), jnp.float32),
            pltpu.VMEM((pieces, half, LANES), jnp.bfloat16),
            pltpu.VMEM((pieces, half, LANES), jnp.bfloat16),
            pltpu.VMEM((pieces, half, LANES), jnp.bfloat16),
            pltpu.VMEM((pieces, half, LANES), jnp.bfloat16),
            pltpu.VMEM((BLOCK + 32, LANES), jnp.bfloat16),
            pltpu.SemaphoreType.DMA((5, pieces)),
            pltpu.SemaphoreType.DMA((5, pieces)),
            pltpu.SemaphoreType.DMA((2, pieces, space // 2)),
            pltpu.SemaphoreType.DMA((2, pieces, space // 2)),
        ],
        compiler_params=pltpu.CompilerParams(
            collective_id=1, has_side_effects=True, vmem_limit_bytes=48 * 2**20
        ),
    )(flat)
    return out.reshape(-1)[:count]


def gru_forward(state, inputs, weights, biases, gate_name, candidate_name, tall, wide, padder):
    joined_stack = patches(padder(jnp.concatenate([state, inputs], -1), tall, wide), tall, wide)
    gates = jax.nn.sigmoid(apply(joined_stack, weights[gate_name]) + biases[gate_name])
    hidden = state.shape[-1]
    update = gates[..., :hidden]
    reset = gates[..., hidden:]
    state_wide = state.astype(jnp.float32)
    mixed = jnp.concatenate([(reset * state_wide).astype(jnp.bfloat16), inputs], -1)
    mixed_stack = patches(padder(mixed, tall, wide), tall, wide)
    candidate = jnp.tanh(apply(mixed_stack, weights[candidate_name]) + biases[candidate_name])
    result = state_wide + update * (candidate - state_wide)
    return (result, (joined_stack, mixed_stack, update, reset, candidate, state_wide))


def gru_backward(result_grad, kept, weights, grads, gate_name, candidate_name, tall, wide, padder):
    joined_stack, mixed_stack, update, reset, candidate, state_wide = kept
    hidden = update.shape[-1]
    candidate_grad = (result_grad * update * (1.0 - candidate * candidate)).astype(jnp.bfloat16)
    record(grads, candidate_name, mixed_stack, candidate_grad)
    mixed_grad = apply(
        patches(padder(candidate_grad, tall, wide), tall, wide),
        flipped(weights[candidate_name], tall, wide),
    )
    reset_grad = mixed_grad[..., :hidden]
    gate_grad = jnp.concatenate(
        [
            result_grad * (candidate - state_wide) * update * (1.0 - update),
            reset_grad * state_wide * reset * (1.0 - reset),
        ],
        -1,
    ).astype(jnp.bfloat16)
    record(grads, gate_name, joined_stack, gate_grad)
    joined_grad = apply(
        patches(padder(gate_grad, tall, wide), tall, wide), flipped(weights[gate_name], tall, wide)
    )
    state_grad = result_grad * (1.0 - update) + reset_grad * reset + joined_grad[..., :hidden]
    inputs_grad = joined_grad[..., hidden:] + mixed_grad[..., hidden:]
    return (state_grad, inputs_grad)


def shards(net, context, corr, flow, target, valid, grad_net, grad_mask, params):
    flow_start = CTX + MOT - 2
    plane = jnp.float32(target.shape[2] * net.shape[2])
    counts = lax.psum(jnp.sum(valid, axis=(1, 2)).astype(jnp.float32), SPACE)
    divisor = jnp.maximum(counts, 1.0)
    weights, biases = unpack(gather_params(params))
    grads = {}
    flow_rows = jnp.transpose(flow, (0, 2, 3, 1))
    corr_pre = apply(corr, weights[CORR_IN]) + biases[CORR_IN]
    corr_one = jax.nn.silu(corr_pre).astype(jnp.bfloat16)
    corr_stack = patches(row_pad(corr_one, 3), 3, 3)
    corr_mix_pre = apply(corr_stack, weights[CORR_MIX]) + biases[CORR_MIX]
    corr_two = jax.nn.silu(corr_mix_pre).astype(jnp.bfloat16)
    flow_stack = patches(row_pad(flow_rows, 7), 7, 7)
    flow_pre = apply(flow_stack, weights[FLOW_IN]) + biases[FLOW_IN]
    flow_one = jax.nn.silu(flow_pre).astype(jnp.bfloat16)
    flow_mix_stack = patches(row_pad(flow_one, 3), 3, 3)
    flow_mix_pre = apply(flow_mix_stack, weights[FLOW_MIX]) + biases[FLOW_MIX]
    flow_two = jax.nn.silu(flow_mix_pre).astype(jnp.bfloat16)
    joint_stack = patches(row_pad(jnp.concatenate([corr_two, flow_two], -1), 3), 3, 3)
    motion_pre = apply(joint_stack, weights[MOTION_MIX]) + biases[MOTION_MIX]
    motion = jax.nn.silu(motion_pre).astype(jnp.bfloat16)
    inputs = jnp.concatenate([context, motion, flow_rows], -1)
    state, rows_kept = gru_forward(
        net, inputs, weights, biases, ROWS_GATES, ROWS_CANDIDATE, 1, 5, local_pad
    )
    state_columns, inputs_columns = (
        lax.all_to_all(
            state.astype(jnp.bfloat16), SPACE, split_axis=2, concat_axis=1, tiled=True
        ),
        lax.all_to_all(inputs, SPACE, split_axis=2, concat_axis=1, tiled=True),
    )
    target_here = jnp.transpose(target, (0, 2, 3, 1))
    valid_here = valid.astype(jnp.float32)
    net_cotangent = grad_net
    mask_cotangent = grad_mask
    final, columns_kept = gru_forward(
        state_columns,
        inputs_columns,
        weights,
        biases,
        COLUMNS_GATES,
        COLUMNS_CANDIDATE,
        5,
        1,
        local_pad,
    )
    final_low = final.astype(jnp.bfloat16)
    heads_weight = jnp.concatenate([weights[FLOW_HIDDEN], weights[MASK_HIDDEN]], 1)
    heads_bias = jnp.concatenate([biases[FLOW_HIDDEN], biases[MASK_HIDDEN]])
    net_stack = patches(column_pad(final_low, 3, 3), 3, 3)
    heads_pre = apply(net_stack, heads_weight) + heads_bias
    heads_act = jax.nn.silu(heads_pre).astype(jnp.bfloat16)
    flow_features = heads_act[..., :HEAD]
    mask_features = heads_act[..., HEAD:]
    hidden_stack = patches(column_pad(flow_features, 3, 3), 3, 3)
    delta = apply(hidden_stack, weights[FLOW_OUT]) + biases[FLOW_OUT]
    mask_full = 0.25 * (apply(mask_features, weights[MASK_OUT]) + biases[MASK_OUT])
    new_flow = inputs_columns[..., flow_start:].astype(jnp.float32) + delta
    error = new_flow - target_here
    root = jnp.sqrt(error * error + 1.0)
    partials = jnp.sum(valid_here * jnp.sum(root, axis=-1), axis=(1, 2))
    flow_grad = plane / divisor[:, None, None, None] * valid_here[..., None] * error / root
    mask_low = mask_full.astype(jnp.bfloat16)
    nets_out = final_low
    flows_out = jnp.transpose(new_flow, (0, 3, 1, 2))
    masks_out = mask_low
    delta_grad = flow_grad.astype(jnp.bfloat16)
    mask_grad = (0.25 * mask_cotangent.astype(jnp.float32)).astype(jnp.bfloat16)
    record(grads, MASK_OUT, mask_features, mask_grad)
    record(grads, FLOW_OUT, hidden_stack, delta_grad)
    from_flow = apply(
        patches(column_pad(delta_grad, 3, 3), 3, 3), flipped(weights[FLOW_OUT], 3, 3)
    )
    from_mask = apply_back(mask_grad, weights[MASK_OUT])
    heads_grad = (jnp.concatenate([from_flow, from_mask], -1) * slope(heads_pre)).astype(
        jnp.bfloat16
    )
    heads_wgrad = weight_grad(net_stack, heads_grad)
    heads_bgrad = jnp.sum(heads_grad, axis=(0, 1, 2), dtype=jnp.float32)
    grads[FLOW_HIDDEN] = (heads_wgrad[:, :HEAD], heads_bgrad[:HEAD])
    grads[MASK_HIDDEN] = (heads_wgrad[:, HEAD:], heads_bgrad[HEAD:])
    final_grad = net_cotangent.astype(jnp.float32) + apply(
        patches(column_pad(heads_grad, 3, 3), 3, 3), flipped(heads_weight, 3, 3)
    )
    state_grad_columns, inputs_grad_columns = gru_backward(
        final_grad,
        columns_kept,
        weights,
        grads,
        COLUMNS_GATES,
        COLUMNS_CANDIDATE,
        5,
        1,
        local_pad,
    )
    inputs_grad_columns = jnp.concatenate(
        [
            inputs_grad_columns[..., :flow_start],
            inputs_grad_columns[..., flow_start:] + flow_grad,
        ],
        -1,
    )
    state_back, inputs_back = (
        lax.all_to_all(
            state_grad_columns.astype(jnp.bfloat16),
            SPACE,
            split_axis=1,
            concat_axis=2,
            tiled=True,
        ),
        lax.all_to_all(
            inputs_grad_columns.astype(jnp.bfloat16),
            SPACE,
            split_axis=1,
            concat_axis=2,
            tiled=True,
        ),
    )
    net_grad, inputs_grad = gru_backward(
        state_back.astype(jnp.float32),
        rows_kept,
        weights,
        grads,
        ROWS_GATES,
        ROWS_CANDIDATE,
        1,
        5,
        local_pad,
    )
    inputs_total = inputs_grad + inputs_back.astype(jnp.float32)
    motion_grad = (inputs_total[..., CTX:flow_start] * slope(motion_pre)).astype(jnp.bfloat16)
    record(grads, MOTION_MIX, joint_stack, motion_grad)
    joint_grad = apply(
        patches(row_pad(motion_grad, 3), 3, 3), flipped(weights[MOTION_MIX], 3, 3)
    )
    branch_grad = jnp.concatenate(
        [
            joint_grad[..., :C2] * slope(corr_mix_pre),
            joint_grad[..., C2:] * slope(flow_mix_pre),
        ],
        -1,
    ).astype(jnp.bfloat16)
    record(grads, CORR_MIX, corr_stack, branch_grad[..., :C2])
    record(grads, FLOW_MIX, flow_mix_stack, branch_grad[..., C2:])
    branch_pad = row_pad(branch_grad, 3)
    corr_one_grad = apply(
        patches(branch_pad[..., :C2], 3, 3), flipped(weights[CORR_MIX], 3, 3)
    )
    flow_one_grad = apply(
        patches(branch_pad[..., C2:], 3, 3), flipped(weights[FLOW_MIX], 3, 3)
    )
    corr_pre_grad = (corr_one_grad * slope(corr_pre)).astype(jnp.bfloat16)
    flow_pre_grad = (flow_one_grad * slope(flow_pre)).astype(jnp.bfloat16)
    record(grads, CORR_IN, corr, corr_pre_grad)
    record(grads, FLOW_IN, flow_stack, flow_pre_grad)
    corr_grads = apply_back(corr_pre_grad, weights[CORR_IN])
    flow_total = inputs_total[..., flow_start:] + apply(
        patches(row_pad(flow_pre_grad, 7), 7, 7), flipped(weights[FLOW_IN], 7, 7)
    )
    flow_grads = jnp.transpose(flow_total, (0, 3, 1, 2))
    net_grads = net_grad
    context_grads = inputs_total[..., :CTX]
    count = params.shape[0]
    local = pack(grads, 3 * count // (LANES * 16) * 16 + BLOCK)
    collected = reduce_grads(local, lax.axis_size(SPACE), count)
    losses = lax.psum(partials, SPACE) / divisor
    return (
        nets_out,
        flows_out,
        masks_out,
        losses,
        collected,
        net_grads,
        context_grads,
        corr_grads,
        flow_grads,
    )


BATCH = 2
ROWS = 5
WIDE = 128
TALL = 40
COLS = 16
AREA = 640
PITCH = 20
SPREAD = TALL * PITCH
SPAN = 896
EDGE = 64


def mm(a, b):
    return jnp.dot(a, b, preferred_element_type=jnp.float32)


def nt(a, b):
    return lax.dot_general(a, b, (((1,), (1,)), ((), ())), preferred_element_type=jnp.float32)


def tn(a, b):
    return lax.dot_general(a, b, (((0,), (0,)), ((), ())), preferred_element_type=jnp.float32)


def half_of(value):
    return value.astype(jnp.bfloat16)


def full_of(value):
    return value.astype(jnp.float32)


def join(parts, axis=1):
    return jnp.concatenate(list(parts), axis=axis)


def quarter_of(value):
    return half_of(0.25 * full_of(value))


def lane_index(shape):
    return lax.broadcasted_iota(jnp.int32, shape, 1)


def row_index(shape):
    return lax.broadcasted_iota(jnp.int32, shape, 0)


def act_slope(pre):
    sigma = jax.nn.sigmoid(pre)
    act = pre * sigma
    return act, sigma + act * (1.0 - sigma)


def flat_rows():
    table = shapes()
    offset = 0
    starts = {}
    for name, height, width in table:
        starts[name] = offset // LANES
        offset += height * width
    bias_row = offset // LANES
    spots = {}
    inner = 0
    for name, height, width in table:
        spots[name] = inner
        inner += width
    return starts, bias_row, spots, inner


def cast_rows(dst, to, src, start, count, kind):
    big = 256
    whole = count // big

    if whole > 1:

        def body(step, carry):
            at = pl.multiple_of(step * big, big)
            dst[pl.ds(to + at, big), :] = src[pl.ds(start + at, big), :].astype(kind)
            return carry

        lax.fori_loop(0, whole, body, 0)
    elif whole == 1:
        dst[to : to + big, :] = src[start : start + big, :].astype(kind)
    rest = count - whole * big
    if rest:
        low = whole * big
        dst[to + low : to + count, :] = src[start + low : start + count, :].astype(kind)


MARGIN = 16


def stage_plan(count, start, rows):
    stop = start + rows
    pieces, fill = [], 0
    for rank in range(4):
        first = rank * count // LANES
        last = -(-(rank + 1) * count // LANES)
        low, high = max(start, first), min(stop, last)
        if low >= high:
            continue
        place = low - first + rank * BLOCK
        base = place // 16 * 16
        length = -(-(place - base + high - low) // 16) * 16
        to = MARGIN + low - start - (place - base)
        seam = MARGIN + low - start if start < first else None
        pieces.append((base, length, fill, to, seam))
        fill += length
    return pieces


class Stages:
    def __init__(self, v, count, segments):
        self.v, self.at, self.hold = v, 0, (4,)
        self.plans = [stage_plan(count, start, rows) for start, rows in segments]
        self.fetch(0)

    def copies(self, index):
        v, slot = self.v, index % 2
        return [
            pltpu.make_async_copy(
                v.out_all.at[base : base + length], v.stage.at[slot, fill : fill + length], v.ssem.at[slot, number]
            )
            for number, (base, length, fill, to, seam) in enumerate(self.plans[index])
        ]

    def fetch(self, index):
        if index < len(self.plans):
            for copy in self.copies(index):
                copy.start()

    def take(self):
        v, index = self.v, self.at
        self.at += 1
        for copy in self.copies(index):
            copy.wait()
        if index + 1 not in self.hold:
            self.fetch(index + 1)
        for base, length, fill, to, seam in self.plans[index]:
            saved = None if seam is None else v.flat[seam : seam + 1, :]
            cast_rows(v.flat, to, v.stage.at[index % 2], fill, length, jnp.float32)
            if seam is not None:
                v.flat[seam : seam + 1, :] = v.flat[seam : seam + 1, :] + saved


def strided(ref, start, count, stride):
    if stride == 1:
        return ref[pl.ds(start, count), :]
    return ref[pl.ds(start, count, stride=stride), :]


def unpack_pairs(flat, row, count, dst, to, lane):
    dst[to : to + count, lane : lane + LANES] = half_of(strided(flat, MARGIN + 2 * row, count, 2))
    dst[to : to + count, lane + LANES : lane + 2 * LANES] = half_of(strided(flat, MARGIN + 2 * row + 1, count, 2))


def pack_pairs(flat, row, count, low, high):
    flat[pl.ds(MARGIN + 2 * row, count, stride=2), :] = low
    flat[pl.ds(MARGIN + 2 * row + 1, count, stride=2), :] = high


def split_pick(which, quarter):
    source = lax.broadcasted_iota(jnp.int32, (LANES, HEAD), 0)
    target = lax.broadcasted_iota(jnp.int32, (LANES, HEAD), 1)
    return jnp.where(source == 2 * (target - 64 * quarter) + which, 1.0, 0.0).astype(jnp.bfloat16)


UNPACK = (
    (CORR_IN, 648), (CORR_MIX, 3456), (FLOW_IN, 98), (FLOW_MIX, 576), (MOTION_MIX, 2268),
    (ROWS_GATES, 3840), (ROWS_CANDIDATE, 1920), (COLUMNS_GATES, 3840), (COLUMNS_CANDIDATE, 1920),
    (FLOW_HIDDEN, 2304), (MASK_HIDDEN, 2304), (FLOW_OUT, 36), (MASK_OUT, 1152),
)


def stage_of(v, name, rows):
    assert UNPACK[v.stages.at] == (name, rows)
    v.stages.take()


def unpack_gru(v, gates_name, cand_name, w_i, w_s):
    flat = v.flat
    stage_of(v, gates_name, 3840)
    for tap in range(5):
        unpack_pairs(flat, tap * 384, 128, w_s, tap * 128, 0)
        unpack_pairs(flat, tap * 384 + 128, 256, w_i, tap * 256, 0)
    stage_of(v, cand_name, 1920)
    for tap in range(5):
        w_s[tap * 128 : (tap + 1) * 128, 256:384] = half_of(strided(flat, MARGIN + tap * 384, 128, 1))
        w_i[tap * 256 : (tap + 1) * 256, 256:384] = half_of(strided(flat, MARGIN + tap * 384 + 128, 256, 1))


def unpack_encoder(v, count):
    starts, bias_row, spots, inner = flat_rows()
    flat = v.flat
    v.stages = Stages(v, count, [(starts[name], rows) for name, rows in UNPACK])

    def stage(name, rows):
        stage_of(v, name, rows)

    @pl.when(v.rank != 3)
    def _():
        drain_bytes(v.bz, v.grecv.at[0, 4])

    flat[0:64, :] = full_of(v.bz[...])
    start = bias_row - 3 * count // LANES - BIAS_LOW
    place = 0
    lane1 = lane_index((1, LANES))
    for name, height, width in shapes():
        spot = spots[name]
        for block in range(-(-width // LANES)):
            at = spot + block * LANES
            row, shift = at // LANES, at % LANES
            value = flat[start + row : start + row + 1, :]
            if shift:
                after = flat[start + row + 1 : start + row + 2, :]
                value = jnp.where(
                    lane1 < LANES - shift, pltpu.roll(value, LANES - shift, 1), pltpu.roll(after, LANES - shift, 1)
                )
            left = width - block * LANES
            if left < LANES:
                value = jnp.where(lane1 < left, value, 0.0)
            if name == FLOW_MIX:
                value = pltpu.roll(value, 64, 1)
            v.bias[place : place + 1, :] = value
            place += 1

    stage(CORR_IN, 648)
    unpack_pairs(flat, 0, 324, v.w_ci, 0, 0)

    stage(CORR_MIX, 3456)
    lane = lane_index((128, LANES))
    low_half = lane < 64

    def mix_step(step, carry):
        at = MARGIN + 384 * step
        r0, r1, r2 = (strided(flat, at + i, 128, 3) for i in range(3))
        r1s, r2s = pltpu.roll(r1, 64, 1), pltpu.roll(r2, 64, 1)
        v.pair_a[pl.ds(0, 128, stride=2), :] = r0
        v.pair_a[pl.ds(1, 128, stride=2), :] = jnp.where(low_half, r1s, r2s)
        v.pair_b[pl.ds(0, 128, stride=2), :] = jnp.where(low_half, r1, 0.0)
        v.pair_b[pl.ds(1, 128, stride=2), :] = jnp.where(low_half, r2s, 0.0)
        to = pl.ds(pl.multiple_of(step * 256, 256), 256)
        v.w_cm[to, 0:128] = half_of(v.pair_a[...])
        v.w_cm[to, 128:256] = half_of(v.pair_b[...])
        return carry

    lax.fori_loop(0, 9, mix_step, 0)

    stage(FLOW_IN, 98)
    v.flow_tmp[...] = jnp.zeros_like(v.flow_tmp)
    for across in range(7):
        for comp in range(2):
            v.flow_tmp[pl.ds(across * 16 + comp, 7, stride=2), :] = strided(
                flat, MARGIN + across * 2 + comp, 7, 14
            )
    v.w_fi[...] = half_of(v.flow_tmp[...])

    stage(FLOW_MIX, 576)
    for step in range(9):
        r0 = strided(flat, MARGIN + 64 * step, 64, 1)
        high_half = lane_index((64, LANES)) >= 64
        v.pair_a[pl.ds(0, 64, stride=2), :] = jnp.where(high_half, pltpu.roll(r0, 64, 1), 0.0)
        v.pair_a[pl.ds(1, 64, stride=2), :] = jnp.where(high_half, r0, 0.0)
        v.w_fm[step * 128 : (step + 1) * 128, :] = half_of(v.pair_a[0:128, :])


def unpack_rows(v):
    flat = v.flat
    v.stages.fetch(4)

    def stage(name, rows):
        stage_of(v, name, rows)

    stage(MOTION_MIX, 2268)
    lane36 = lane_index((36, LANES))
    for i in range(64):
        if i == 0:
            value = strided(flat, MARGIN, 36, 63)
        elif i == 63:
            value = pltpu.roll(strided(flat, MARGIN + 62, 36, 63), 126, 1)
        else:
            low = pltpu.roll(strided(flat, MARGIN + i - 1, 36, 63), 2 * i, 1)
            high = pltpu.roll(strided(flat, MARGIN + i, 36, 63), 2 * i, 1)
            value = jnp.where(lane36 < 2 * i, low, high)
        v.mm_tmp[pl.ds(i, 36, stride=64), :] = jnp.where(lane36 < 126, value, 0.0)
    for step in range(9):
        v.w_mm[step * 256 : (step + 1) * 256, :] = half_of(v.mm_tmp[step * 256 : (step + 1) * 256, :])

    unpack_gru(v, ROWS_GATES, ROWS_CANDIDATE, v.w_ri, v.w_rs)


def unpack_heads(v):
    flat = v.flat
    low_half = lane_index((128, LANES)) < 64

    def stage(name, rows):
        stage_of(v, name, rows)

    unpack_gru(v, COLUMNS_GATES, COLUMNS_CANDIDATE, v.w_li, v.w_ls)

    for name, lane0 in ((FLOW_HIDDEN, 0), (MASK_HIDDEN, 256)):
        stage(name, 2304)
        for tap in range(9):
            unpack_pairs(flat, tap * 128, 128, v.w_h, tap * 128, lane0)

    stage(FLOW_OUT, 36)
    v.fo_tmp[...] = jnp.zeros_like(v.fo_tmp)
    for which in range(2):
        total = jnp.zeros((9, HEAD), jnp.float32)
        for quarter in range(4):
            total = total + mm(half_of(strided(flat, MARGIN + quarter, 9, 4)), split_pick(which, quarter))
        v.fo_tmp[pl.ds(which, 9, stride=2), 0:128] = total[:, :128]
        v.fo_tmp2[pl.ds(which, 9, stride=2), 0:128] = total[:, 128:]
    v.fo_tmp2[18:32, :] = jnp.zeros((14, LANES), jnp.float32)
    v.w_fo[:, 0:128] = half_of(v.fo_tmp[...])
    v.w_fo[:, 128:256] = half_of(v.fo_tmp2[...])

    stage(MASK_OUT, 1152)
    r = [strided(flat, MARGIN + i, 128, 9) for i in range(9)]
    rs = [pltpu.roll(r[i], 64, 1) for i in range(4, 9)]
    for block in range(5):
        even = r[block] if block < 4 else jnp.where(low_half, r[4], 0.0)
        odd = jnp.where(low_half, rs[block], rs[block + 1]) if block < 4 else jnp.where(low_half, rs[4], 0.0)
        v.pair_a[pl.ds(0, 128, stride=2), :] = even
        v.pair_a[pl.ds(1, 128, stride=2), :] = odd
        v.w_mo[:, block * 128 : (block + 1) * 128] = half_of(v.pair_a[...])


BIAS_AT = {}
_place = 0
for _name, _height, _width in shapes():
    BIAS_AT[_name] = _place
    _place += -(-_width // 128)
BIAS_ROWS = 32


def bias_of(v, name, blocks):
    at = BIAS_AT[name]
    return jnp.concatenate([v.bias[at + i : at + i + 1, :] for i in range(blocks)], axis=1)


class Halo:
    def __init__(self, v, sem, up_src, down_src, from_down, from_up):
        up = {SPACE: jnp.maximum(v.spot - 1, 0)}
        down = {SPACE: jnp.minimum(v.spot + 1, v.space - 1)}
        self.v = v
        self.up = remote(up_src, from_down, v.hsend.at[sem, 0], v.hrecv.at[sem, 0], up)
        self.down = remote(down_src, from_up, v.hsend.at[sem, 1], v.hrecv.at[sem, 1], down)

    def start(self):
        pl.when(self.v.spot > 0)(self.up.start)
        pl.when(self.v.spot < self.v.space - 1)(self.down.start)

    def receive(self):
        pl.when(self.v.spot < self.v.space - 1)(self.up.wait_recv)
        pl.when(self.v.spot > 0)(self.down.wait_recv)

    def sent(self):
        pl.when(self.v.spot > 0)(self.up.wait_send)
        pl.when(self.v.spot < self.v.space - 1)(self.down.wait_send)


def drain_bytes(ref, sem):
    pltpu.make_async_copy(ref, ref, sem).wait()


class Swap:
    def __init__(self, v, sem, src, dst, broadcast=False):
        self.v, self.sem, self.src, self.dst, self.broadcast = v, sem, src, dst, broadcast

    def start(self, b=None):
        v = self.v

        def body(step, carry):
            to = v.spot + step
            to = jnp.where(to >= v.space, to - v.space, to)
            src = self.src if self.broadcast else self.src.at[to]
            dst = self.dst.at[v.spot]
            if b is not None:
                src, dst = src.at[b], dst.at[b]
            remote(src, dst, v.asend.at[self.sem], v.arecv.at[self.sem], {SPACE: to}).start()
            return carry

        lax.fori_loop(1, v.space, body, 0)

    def receive(self):
        drain_bytes(self.dst.at[0 : self.v.space - 1], self.v.arecv.at[self.sem])

    def sent(self):
        drain_bytes(self.dst.at[0 : self.v.space - 1], self.v.asend.at[self.sem])


def spread_rows(v, b, acts, rows, dst, row0, width, backward=False):
    x = lax.rem(row_index((rows, LANES)), WIDE)
    for block, act in enumerate(acts):
        v.tmp[8 : 8 + rows, :] = act
        for tap in range(3):
            d = (1 - tap) if backward else (tap - 1)
            value = act if d == 0 else v.tmp[8 + d : 8 + d + rows, :]
            if d == -1:
                value = jnp.where(x > 0, value, 0.0)
            if d == 1:
                value = jnp.where(x < WIDE - 1, value, 0.0)
            lane = tap * width + block * LANES
            if backward:
                dst[row0 : row0 + rows, b + lane : b + lane + LANES] = half_of(value)
            else:
                dst[b, row0 : row0 + rows, lane : lane + LANES] = half_of(value)


def spread_five(v, value, dst, lane_of, backward=False):
    x = lax.rem(row_index((AREA, LANES)), WIDE)
    v.tmp[8 : 8 + AREA, :] = value
    for tap in range(5):
        d = (2 - tap) if backward else (tap - 2)
        moved = value if d == 0 else v.tmp[8 + d : 8 + d + AREA, :]
        if d:
            moved = jnp.where((x + d >= 0) & (x + d < WIDE), moved, 0.0)
        if backward:
            taps_part(v, tap, lane_of, lane_of + LANES)[...] = half_of(moved)
        else:
            lane = lane_of(tap)
            dst[:, lane : lane + LANES] = half_of(moved)


def lines_of(ref, b, lines):
    return jnp.concatenate([ref[b, y] for y in range(lines)], axis=1)


def edge_rows(v, value, rows):
    low = jnp.where(v.spot > 0, value[0:rows], 0.0)
    high = jnp.where(v.spot < v.space - 1, value[-rows:], 0.0)
    return jnp.concatenate([low, value[rows:-rows], high], axis=0)


def early_taps(v):
    def flow(b, carry):
        up = jnp.where(v.spot > 0, v.flow_up[b], 0.0)
        down = jnp.where(v.spot < v.space - 1, v.flow_down[b], 0.0)
        lane = lane_index((16, LANES))
        v.fs[...] = jnp.zeros_like(v.fs)
        for across in range(7):
            d = across - 3
            for part, value in enumerate((up, v.flow[b], down)):
                moved = value
                if d:
                    moved = pltpu.roll(value, (-d) % LANES, 1)
                    moved = jnp.where((lane + d >= 0) & (lane + d < WIDE), moved, 0.0)
                v.fs[across, part * 10 : part * 10 + 10, :] = moved[0:10, :]
        for y in range(9):
            for across in range(7):
                v.flow_tmp[across * 16 : across * 16 + 16, :] = v.fs[across, 2 * y : 2 * y + 16, :]
            v.xt[b, :, y * 128 : (y + 1) * 128] = half_of(v.flow_tmp[...])
        return carry

    lax.fori_loop(0, BATCH, flow, 0)

    def image(b, carry):
        at = pl.ds(pl.multiple_of(b * AREA, AREA), AREA)
        spread_five(v, full_of(v.context[b]), v.xi.at[at], lambda t: t * 256)
        spread_five(v, full_of(v.net[b]), v.xs.at[at], lambda t: t * 128)
        return carry

    lax.fori_loop(0, BATCH, image, 0)


def gather_start(v, count):
    shift = lax.rem(v.rank * count, LANES)
    chunk = 512
    keep = lane_index((chunk, LANES)) >= shift
    v.tmp[7:8, :] = jnp.zeros((1, LANES), jnp.float32)

    def rotate(step, carry):
        at = pl.ds(pl.multiple_of(step * chunk, chunk), chunk)
        moved = pltpu.roll(full_of(v.gath[at, :]), shift, 1)
        v.tmp[8 : 8 + chunk, :] = moved
        v.gath[at, :] = half_of(jnp.where(keep, moved, v.tmp[7 : 7 + chunk, :]))
        v.tmp[7:8, :] = v.tmp[7 + chunk : 8 + chunk, :]
        return carry

    lax.fori_loop(0, BLOCK // chunk, rotate, 0)

    quad = BLOCK // 4
    pieces = 4
    rows = quad // pieces
    half, core = lax.rem(v.spot, 2), lax.rem(v.rank, 2)
    near, far = v.rank - core, lax.rem(v.rank - core + 2, 4)

    def piece(rank, which, core, index):
        return pl.ds(pl.multiple_of(rank * BLOCK + (which * 2 + core) * quad + index * rows, 16), rows)

    def whole(rank, which, core):
        return pl.ds(pl.multiple_of(rank * BLOCK + (which * 2 + core) * quad, 16), quad)

    mine = pl.ds(pl.multiple_of(v.rank * BLOCK, 16), BLOCK)
    v.g_here = pltpu.make_async_copy(v.gath.at[0:BLOCK], v.out_all.at[mine], v.lsem)
    v.g_own = []
    for number, (which, side) in enumerate(((half, 1 - core), (half, core), (1 - half, 0), (1 - half, 1))):
        v.g_own.append(
            remote(
                v.gath.at[whole(0, which, side)], v.out_all.at[whole(v.rank, which, side)],
                v.gsend.at[0, number], v.grecv.at[0, number], {DP: v.mate},
            )
        )

    def block_copy(number, k, rank, which, side, device):
        block = v.out_all.at[piece(rank, which, side, k)]
        return remote(block, block, v.gsend.at[number, k], v.grecv.at[number, k], device)

    v.g_x, v.g_twin, v.g_mate, v.g_last = [], [], [], []
    for turn in range(2):
        base = 1 + 4 * turn
        v.g_x.append([block_copy(base, k, near + turn, half, core, {DP: v.other}) for k in range(pieces)])
        v.g_twin.append([block_copy(base + 1, k, far + turn, half, core, {SPACE: v.twin}) for k in range(pieces)])
        v.g_mate.append([block_copy(base + 2, k, far + turn, half, core, {DP: v.mate}) for k in range(pieces)])
        v.g_last.append([block_copy(base + 3, k, far + turn, 1 - half, core, {DP: v.mate}) for k in range(pieces)])
    v.g_here.start()
    for copy in v.g_own:
        copy.start()

    @pl.when(v.rank == 3)
    def _():
        for rank in range(3):
            remote(
                v.gath.at[BIAS_LOW : BIAS_LOW + 64], v.bz, v.gsend.at[0, 4 + rank], v.grecv.at[0, 4], {DP: rank}
            ).start()
        v.bz[...] = v.gath[BIAS_LOW : BIAS_LOW + 64, :]

    v.g_here.wait()
    v.g_own[0].wait_recv()
    for copy in v.g_x[0]:
        copy.start()


BIAS_LOW = 6048


def gather_pass(v, turn, first, last):
    for k in range(first, last):
        v.g_x[turn][k].wait_recv()
        v.g_twin[turn][k].start()
        v.g_mate[turn][k].start()


def gather_turn(v, turn):
    for k in range(len(v.g_x[turn])):
        v.g_twin[turn][k].wait_recv()
        v.g_last[turn][k].start()
    for k in range(len(v.g_x[turn])):
        v.g_mate[turn][k].wait_recv()
        v.g_last[turn][k].wait_recv()


def gather_end(v):
    for turn in range(2):
        for group in (v.g_x, v.g_twin, v.g_mate, v.g_last):
            for copy in group[turn]:
                copy.wait_send()
    for copy in v.g_own:
        copy.wait_send()

    @pl.when(v.rank == 3)
    def _():
        for rank in range(3):
            remote(
                v.gath.at[BIAS_LOW : BIAS_LOW + 64], v.bz, v.gsend.at[0, 4 + rank], v.grecv.at[0, 4], {DP: rank}
            ).wait_send()


def forward_rows(v):
    spot, last = v.spot, v.space - 1
    def image(b, carry):
        pieces = (
            (v.corr_up, 0, 256, 2, spot > 0),
            (v.corr, 256, 640, 5, None),
            (v.corr_down, 896, 256, 2, spot < last),
        )
        bias = bias_of(v, CORR_IN, 2)
        for ref, row0, rows, lines, seen in pieces:
            act, slope = act_slope(tn(lines_of(ref, b, lines), v.w_ci[...]) + bias)
            if seen is None:
                v.slope_ci[b] = half_of(slope)
            else:
                act = jnp.where(seen, act, 0.0)
            spread_rows(v, b, (act[:, :128], act[:, 128:]), rows, v.hx_c, row0, 256)

        act, slope = act_slope(tn(v.xt[b], v.w_fi[...]) + bias_of(v, FLOW_IN, 1))
        v.slope_fi[b] = half_of(slope[256:896])
        spread_rows(v, b, (edge_rows(v, act, 2 * WIDE),), 9 * WIDE, v.hx_f, 0, 128)

        pre = mm(join(v.hx_c[b, a * 128 : a * 128 + 896, :] for a in range(3)), v.w_cm[...]) + bias_of(v, CORR_MIX, 2)
        flow_pre = mm(join(v.hx_f[b, a * 128 : a * 128 + 896, :] for a in range(3)), v.w_fm[...])
        flow_pre = flow_pre + bias_of(v, FLOW_MIX, 1)
        low, low_slope = act_slope(pre[:, :128])
        high, high_slope = act_slope(pre[:, 128:] + flow_pre)
        v.slope_j[b, :, 0:128] = half_of(low_slope)
        v.slope_j[b, :, 128:256] = half_of(high_slope)
        spread_rows(v, b, (edge_rows(v, low, WIDE), edge_rows(v, high, WIDE)), 896, v.hx_j, 0, 256)

        pl.when(b == 0)(lambda: gather_pass(v, 1, 0, 2))
        pl.when(b == 1)(lambda: gather_pass(v, 1, 2, 4))
        return carry

    lax.fori_loop(0, BATCH, image, 0)
    gather_turn(v, 1)
    gather_end(v)
    unpack_rows(v)

    def moving(b, carry):
        pre = mm(join(v.hx_j[b, a * 128 : a * 128 + 640, :] for a in range(3)), v.w_mm[...])
        pre = pre + bias_of(v, MOTION_MIX, 1)
        act, slope = act_slope(pre)
        v.slope_m[b] = half_of(jnp.where(lane_index((AREA, LANES)) < 126, slope, 0.0))
        pick = jnp.where(lane_index((16, LANES)) == row_index((16, LANES)) + 126, 1.0, 0.0)
        own_flow = v.flow[b]
        for y in range(ROWS):
            v.tmp2[0:2, :] = own_flow[2 * y : 2 * y + 2, :]
            v.tmp2[2:16, :] = jnp.zeros((14, LANES), jnp.float32)
            v.motion[b, y * 128 : (y + 1) * 128, :] = act[y * 128 : (y + 1) * 128, :] + tn(
                half_of(v.tmp2[0:16, :]), half_of(pick)
            )
        v.motion[b] = full_of(half_of(v.motion[b]))
        pack_rows(v, v.motion, b, v.a_motion)
        v.swap_motion.start(b)
        return carry

    lax.fori_loop(0, BATCH, moving, 0)

    def gru(b, carry):
        at = pl.ds(pl.multiple_of(b * AREA, AREA), AREA)
        s = full_of(v.net[b])
        spread_five(v, v.motion[b], v.xi.at[at], lambda t: t * 256 + 128)
        both = mm(v.xi[at, :], v.w_ri[...])
        gates = jax.nn.sigmoid(both[:, :256] + mm(v.xs[at, :], v.w_rs[:, :256]) + bias_of(v, ROWS_GATES, 2))
        update, reset = gates[:, :128], gates[:, 128:]
        v.ru[b] = update
        v.rr[b] = reset
        spread_five(v, full_of(half_of(reset * s)), v.xr.at[at], lambda t: t * 128)
        cand = jnp.tanh(both[:, 256:] + mm(v.xr[at, :], v.w_rs[:, 256:]) + bias_of(v, ROWS_CANDIDATE, 1))
        v.rc[b] = cand
        v.state[b] = s + update * (cand - s)
        pack_rows(v, v.state, b, v.a_state)
        v.swap_state.start(b)
        return carry

    lax.fori_loop(0, BATCH, gru, 0)


def pack_rows(v, src, b, dst):
    def peer(t, carry):
        for y in range(ROWS):
            at = pl.multiple_of(y * WIDE + t * COLS, COLS)
            dst[t, b, y * COLS : (y + 1) * COLS, :] = half_of(src[b, pl.ds(at, COLS), :])
        return carry

    lax.fori_loop(0, v.space, peer, 0)


def take_own(v, src, dst):
    dst[v.spot] = src[v.spot]


def columns_zero(v):
    def zero(b, carry):
        for ref, wide in ((v.xc, 384), (v.xcr, 128), (v.gc, 384)):
            for low in (0, 32 + AREA):
                ref[b, low : low + 32, :] = jnp.zeros((32, wide), jnp.bfloat16)
        return carry

    lax.fori_loop(0, BATCH, zero, 0)


def columns_in(v):
    def peer(t, carry):
        at = pl.ds(pl.multiple_of(32 + t * ROWS * COLS, 16), ROWS * COLS)
        for b in range(BATCH):
            v.xc[b, at, 0:128] = v.b_state[t, b]
            v.xc[b, at, 128:256] = v.b_context[t, b]
            v.xc[b, at, 256:384] = v.b_motion[t, b]
        return carry

    lax.fori_loop(0, v.space, peer, 0)


FX_ROWS = 16 + (TALL + 2) * PITCH


def fx_base(b):
    return pl.multiple_of(b * FX_ROWS, 8)


def columns_forward(v):
    def gru(b, carry):
        s = full_of(v.xc[b, 32 : 32 + AREA, 0:128])
        bias = join((bias_of(v, COLUMNS_GATES, 2), bias_of(v, COLUMNS_CANDIDATE, 1)))
        rows = [slice(t * COLS, t * COLS + AREA) for t in range(5)]
        both = mm(join(v.xc[b, rows[t], 128:384] for t in range(5)), v.w_li[...]) + bias
        gates = mm(join(v.xc[b, rows[t], 0:128] for t in range(5)), v.w_ls[:, 0:256])
        gates = jax.nn.sigmoid(gates + both[:, :256])
        update, reset = gates[:, :128], gates[:, 128:]
        v.lu[b] = update
        v.lr[b] = reset
        v.xcr[b, 32 : 32 + AREA, :] = half_of(reset * s)
        cand = jnp.tanh(both[:, 256:] + mm(join(v.xcr[b, rows[t], :] for t in range(5)), v.w_ls[:, 256:384]))
        v.lc[b] = cand
        final = s + update * (cand - s)
        v.out_net[b] = half_of(final)
        v.final[...] = full_of(half_of(final))
        fx = fx_base(b)
        v.mm_tmp[pl.ds(fx, FX_ROWS), :] = jnp.zeros((FX_ROWS, LANES), jnp.float32)
        for x in range(COLS):
            v.mm_tmp[pl.ds(fx + 8 + PITCH + 2 + x, TALL, stride=PITCH), :] = v.final[pl.ds(x, TALL, stride=COLS), :]
        for j in range(2):
            v.e_left[b, j, 0:TALL, :] = half_of(v.final[pl.ds(j, TALL, stride=COLS), :])
            v.e_right[b, j, 0:TALL, :] = half_of(v.final[pl.ds(COLS - 2 + j, TALL, stride=COLS), :])
        return carry

    lax.fori_loop(0, BATCH, gru, 0)
    v.halo_final.start()


def ring_masks(v, shape):
    x = lax.rem(row_index(shape), PITCH)
    place = v.spot * COLS + x - 2
    seen = (place >= 0) & (place < WIDE) & (x >= 1) & (x < PITCH - 1)
    own = (x >= 2) & (x < PITCH - 2)
    return seen, own


def mask_gradient(v):
    def image(b, carry):
        value = nt(quarter_of(v.grad_mask[b]), v.w_mo[:, 0:MASK])
        for block in range(2):
            v.final[...] = value[:, block * 128 : (block + 1) * 128]
            v.tmp[0:SPREAD, :] = jnp.zeros((SPREAD, LANES), jnp.float32)
            for x in range(COLS):
                v.tmp[pl.ds(2 + x, TALL, stride=PITCH), :] = v.final[pl.ds(x, TALL, stride=COLS), :]
            v.hgo[b, :, 256 + block * 128 : 384 + block * 128] = half_of(v.tmp[0:SPREAD, :])
            v.m_left[b, block, 0:TALL, :] = half_of(v.final[pl.ds(0, TALL, stride=COLS), :])
            v.m_right[b, block, 0:TALL, :] = half_of(v.final[pl.ds(COLS - 1, TALL, stride=COLS), :])
        return carry

    lax.fori_loop(0, BATCH, image, 0)
    v.halo_mask.start()


def heads_part(v, b, tap):
    ref = v.hx_c if tap < 6 else v.hx_f
    lane = tap % 6 * 128
    return ref.at[b, 0:SPREAD, lane : lane + 128]


def taps_part(v, t, low, high):
    ref = v.hx_f if t % 3 == 2 else v.hx_c
    lane = (t % 3) % 2 * 384
    return ref.at[t // 3, 0:AREA, lane + low : lane + high]


def split_three(value):
    first = half_of(value)
    second = half_of(value - full_of(first))
    third = half_of(value - full_of(first) - full_of(second))
    return first, second, third


def column_grid():
    lane = lane_index((COLS, SPAN))
    columns = jnp.where((lax.rem(lane, PITCH) == row_index((COLS, SPAN)) + 2) & (lane < SPREAD), 1.0, 0.0)
    lane = lane_index((TALL, SPAN))
    rows = jnp.where(lax.div(lane, PITCH) == row_index((TALL, SPAN)), 1.0, 0.0)
    return columns, half_of(rows)


def widen(value, columns, rows, parts):
    spread = 0.0
    for piece in split_three(value)[:parts]:
        spread = spread + mm(piece, rows)
    return jnp.sum(spread * columns, axis=0, keepdims=True)


def widen_all(v):
    columns, rows = column_grid()
    first = row_index((8, SPAN)) == 0
    second = row_index((8, SPAN)) == 1
    for b in range(BATCH):
        low, high = (widen(v.target[b, c], columns, rows, 3) for c in range(2))
        v.target_wide[b] = jnp.where(first, low, jnp.where(second, high, 0.0))
        v.valid_wide[b] = jnp.broadcast_to(widen(v.valid[b].astype(jnp.float32), columns, rows, 1), (8, SPAN))


def narrow(v, b, wide, columns, rows):
    for c in range(2):
        total = 0.0
        for piece in split_three(wide[c : c + 1, :] * columns):
            total = total + nt(piece, rows)
        v.out_flow[b, c] = total


def heads(v):
    spot, last = v.spot, v.space - 1
    v.halo_final.receive()
    v.swap_count.receive()
    v.counts[v.spot] = v.count_out[...]
    counts = jnp.sum(v.counts[...], axis=0)
    seen, own = ring_masks(v, (SPREAD, LANES))
    steps = [(a - 1) * PITCH + (c - 1) for a in range(3) for c in range(3)]
    plane = jnp.float32(TALL * WIDE)
    columns, rows = column_grid()

    def image(b, carry):
        fx = fx_base(b)
        for j in range(2):
            left = jnp.where(spot > 0, full_of(v.f_left[b, j, 0:TALL, :]), 0.0)
            right = jnp.where(spot < last, full_of(v.f_right[b, j, 0:TALL, :]), 0.0)
            v.mm_tmp[pl.ds(fx + 8 + PITCH + j, TALL, stride=PITCH), :] = left
            v.mm_tmp[pl.ds(fx + 8 + PITCH + PITCH - 2 + j, TALL, stride=PITCH), :] = right
        for tap in range(9):
            at = 8 + PITCH + steps[tap]
            heads_part(v, b, tap)[...] = half_of(v.mm_tmp[pl.ds(fx + at, SPREAD), :])
        for part in range(2):
            name = (FLOW_HIDDEN, MASK_HIDDEN)[part]
            lanes = slice(part * 256, (part + 1) * 256)
            act, slope = act_slope(mm(join((v.hx_c[b, 0:SPREAD, :], v.hx_f[b, 0:SPREAD, :])), v.w_h[:, lanes]) + bias_of(v, name, 2))
            v.slope_h[b, :, lanes] = half_of(slope)
            if part == 0:
                for block in range(2):
                    value = jnp.where(seen, act[:, block * 128 : (block + 1) * 128], 0.0)
                    v.feat[b, 0:SPREAD, block * 128 : (block + 1) * 128] = half_of(value)
                v.feat[b, SPREAD:SPAN, :] = jnp.zeros((SPAN - SPREAD, HEAD), jnp.bfloat16)
            else:
                for block in range(2):
                    v.tmp[0:SPREAD, :] = act[:, block * 128 : (block + 1) * 128]
                    for x in range(COLS):
                        v.final[pl.ds(x, TALL, stride=COLS), :] = v.tmp[pl.ds(2 + x, TALL, stride=PITCH), :]
                    v.mf[b, :, block * 128 : (block + 1) * 128] = half_of(v.final[...])
        moved = nt(v.w_fo[...], v.feat[b])
        v.dt[...] = moved
        delta = jnp.zeros((8, SPAN), jnp.float32)
        for tap in range(9):
            pair = jnp.concatenate([v.dt[2 * tap : 2 * tap + 2, :], jnp.zeros((6, SPAN), jnp.float32)], axis=0)
            delta = delta + pltpu.roll(pair, (-steps[tap]) % SPAN, 1)
        v.tmp[0:SPAN, :] = jnp.zeros((SPAN, LANES), jnp.float32)
        v.final[...] = full_of(v.xc[b, 32 : 32 + AREA, 256:384])
        for x in range(COLS):
            v.tmp[pl.ds(2 + x, TALL, stride=PITCH), :] = v.final[pl.ds(x, TALL, stride=COLS), :]
        pick = jnp.where(lane_index((16, LANES)) == row_index((16, LANES)) + 126, 1.0, 0.0)
        base = nt(half_of(pick), half_of(v.tmp[0:SPAN, :]))[0:8, :]
        bias = v.bias[BIAS_AT[FLOW_OUT] : BIAS_AT[FLOW_OUT] + 1, :]
        first = row_index((8, SPAN)) == 0
        second = row_index((8, SPAN)) == 1
        shift = jnp.where(first, bias[0:1, 0:1], jnp.where(second, bias[0:1, 1:2], 0.0))
        new = base + delta + shift
        narrow(v, b, new, columns, rows)
        error = new - v.target_wide[b]
        root = jnp.sqrt(error * error + 1.0)
        valid = jnp.where(first | second, v.valid_wide[b], 0.0)
        piece = jnp.sum(valid * root)
        divisor = jnp.maximum(v.pick_count(counts, b), 1.0)
        gradient = plane / divisor * valid * error / root
        v.dg[b] = gradient
        v.losses[...] = jnp.where(row_index((8, LANES)) == b, piece, v.losses[...])
        return carry

    v.losses[...] = jnp.zeros((8, LANES), jnp.float32)
    lax.fori_loop(0, BATCH, image, 0)
    v.halo_dg.start()
    v.swap_loss.start()


def mask_output(v):
    def image(b, carry):
        store = pltpu.make_async_copy(v.mask_low, v.out_mask.at[b], v.osem.at[3])
        pl.when(b > 0)(store.wait)
        for block in range(5):
            wide = min(128, MASK - block * 128)
            lanes = slice(block * 128, block * 128 + wide)
            at = BIAS_AT[MASK_OUT] + block
            value = mm(v.mf[b], v.w_mo[:, lanes]) + v.bias[at : at + 1, 0:wide]
            v.mask_low[:, lanes] = half_of(0.25 * value)
        store.start()
        return carry

    lax.fori_loop(0, BATCH, image, 0)


def heads_back(v):
    spot, last = v.spot, v.space - 1
    seen, own = ring_masks(v, (SPREAD, LANES))
    steps = [(a - 1) * PITCH + (c - 1) for a in range(3) for c in range(3)]
    v.halo_dg.receive()
    v.halo_mask.receive()

    def zb(c, low, rows):
        at = c * (2 * EDGE + SPREAD) + low
        return v.mm_tmp.at[at : at + rows]

    def image(b, carry):
        x = lax.rem(lane_index((8, SPAN)), PITCH)
        own_dg = v.dg[b]
        left = jnp.where((x < 2) & (spot > 0), pltpu.roll(v.dg_left[b], SPAN - COLS, 1), 0.0)
        right = jnp.where((x >= PITCH - 2) & (spot < last), pltpu.roll(v.dg_right[b], COLS, 1), 0.0)
        inside = lane_index((8, SPAN)) < SPREAD
        wide_dg = full_of(half_of(jnp.where(inside, own_dg + left + right, 0.0)))
        own_low = full_of(half_of(own_dg))
        v.dt[...] = jnp.zeros_like(v.dt)
        v.dto[...] = jnp.zeros_like(v.dto)
        for tap in range(9):
            v.dt[2 * tap : 2 * tap + 2, :] = pltpu.roll(wide_dg, steps[tap] % SPAN, 1)[0:2, :]
            v.dto[2 * tap : 2 * tap + 2, :] = pltpu.roll(own_low, steps[tap] % SPAN, 1)[0:2, :]
        v.dtb[b] = half_of(v.dto[...])
        from_flow = tn(half_of(v.dt[...]), v.w_fo[...])
        for block in range(2):
            left = jnp.where(spot > 0, full_of(v.n_left[b, block, 0:TALL, :]), 0.0)
            right = jnp.where(spot < last, full_of(v.n_right[b, block, 0:TALL, :]), 0.0)
            v.tmp[0:SPREAD, :] = full_of(v.hgo[b, :, 256 + block * 128 : 384 + block * 128])
            v.tmp[pl.ds(1, TALL, stride=PITCH), :] = left
            v.tmp[pl.ds(PITCH - 2, TALL, stride=PITCH), :] = right
            v.hgo[b, :, 256 + block * 128 : 384 + block * 128] = half_of(v.tmp[0:SPREAD, :])
        for block in range(4):
            lanes = slice(block * 128, (block + 1) * 128)
            value = from_flow[0:SPREAD, lanes] if block < 2 else full_of(v.hgo[b, :, lanes])
            value = value * full_of(v.slope_h[b, :, lanes])
            v.hgo[b, :, lanes] = half_of(jnp.where(seen, value, 0.0))
        total = jnp.zeros((SPREAD, LANES), jnp.float32)
        for a in range(3):
            value = nt(v.hgo[b], v.w_h[a * 384 : (a + 1) * 384, :])
            for c in range(3):
                zb(c, EDGE, SPREAD)[...] = value[:, c * 128 : (c + 1) * 128]
            for c in range(3):
                at = EDGE - steps[a * 3 + c]
                total = total + zb(c, at, SPREAD)[...]
        for block in range(4):
            lanes = slice(block * 128, (block + 1) * 128)
            v.hgo[b, :, lanes] = half_of(jnp.where(own, full_of(v.hgo[b, :, lanes]), 0.0))
        v.tmp[0:SPREAD, :] = total
        for x in range(COLS):
            v.final[pl.ds(x, TALL, stride=COLS), :] = v.tmp[pl.ds(2 + x, TALL, stride=PITCH), :]
        r = v.final[...] + full_of(v.grad_net[b])

        s = full_of(v.xc[b, 32 : 32 + AREA, 0:128])
        update, reset, cand = v.lu[b], v.lr[b], v.lc[b]
        cg = half_of(r * update * (1.0 - cand * cand))
        v.gc[b, 32 : 32 + AREA, 256:384] = cg
        rows = [slice((4 - t) * COLS, (4 - t) * COLS + AREA) for t in range(5)]
        reset_grad = nt(
            join(v.gc[b, rows[t], 256:384] for t in range(5)),
            join(v.w_ls[t * 128 : (t + 1) * 128, 256:384] for t in range(5)),
        )
        v.gc[b, 32 : 32 + AREA, 0:128] = half_of(r * (cand - s) * update * (1.0 - update))
        v.gc[b, 32 : 32 + AREA, 128:256] = half_of(reset_grad * s * reset * (1.0 - reset))
        state_grad = r * (1.0 - update) + reset_grad * reset
        state_grad = state_grad + nt(
            join(v.gc[b, rows[t], 0:256] for t in range(5)),
            join(v.w_ls[t * 128 : (t + 1) * 128, 0:256] for t in range(5)),
        )
        inputs_grad = nt(
            join(v.gc[b, rows[t], :] for t in range(5)), join(v.w_li[t * 256 : (t + 1) * 256, :] for t in range(5))
        )
        high = half_of(own_dg)
        low = half_of(own_dg - full_of(high))
        pick = half_of(jnp.where(lane_index((8, LANES)) == row_index((8, LANES)) + 126, 1.0, 0.0))
        v.tmp[0:SPAN, :] = tn(high, pick) + tn(low, pick)
        for x in range(COLS):
            v.final[pl.ds(x, TALL, stride=COLS), :] = v.tmp[pl.ds(2 + x, TALL, stride=PITCH), :]
        v.lu[b] = state_grad
        v.lr[b] = inputs_grad[:, 0:128]
        v.lc[b] = inputs_grad[:, 128:256] + v.final[...]

        def peer(t, carry):
            at = pl.ds(pl.multiple_of(t * ROWS * COLS, 16), ROWS * COLS)
            v.a_state[t, b] = half_of(v.lu[b, at, :])
            v.a_context[t, b] = half_of(v.lr[b, at, :])
            v.a_motion[t, b] = half_of(v.lc[b, at, :])
            return carry

        lax.fori_loop(0, v.space, peer, 0)
        v.back_state.start(b)
        return carry

    v.swap_loss.receive()
    for c in range(3):
        zb(c, 0, EDGE)[...] = jnp.zeros((EDGE, LANES), jnp.float32)
        zb(c, EDGE + SPREAD, EDGE)[...] = jnp.zeros((EDGE, LANES), jnp.float32)
    lax.fori_loop(0, BATCH, image, 0)


def unpack_back(v, src, dst):
    def peer(t, carry):
        for b in range(BATCH):
            value = full_of(src[t, b])
            for y in range(ROWS):
                at = pl.multiple_of(y * WIDE + t * COLS, COLS)
                dst[b, pl.ds(at, COLS), :] = value[y * COLS : (y + 1) * COLS, :]
        return carry

    lax.fori_loop(0, v.space, peer, 0)


def seams():
    starts, bias_row, _, _ = flat_rows()
    edges = sorted(starts.values()) + [bias_row]
    tiles = sorted({row // 16 for row in edges if row % 16})
    parts = {}
    for low, high in zip(edges, edges[1:]):
        for tile in tiles:
            if low < (tile + 1) * 16 and high > tile * 16:
                parts[tile] = parts.get(tile, 0) + 1
    return {tile: (index, parts[tile]) for index, tile in enumerate(tiles)}


class Flush:
    def __init__(self, v):
        self.v, self.at, self.busy, self.small = v, 0, {}, []
        self.tiles = seams()
        self.left = {tile: parts for tile, (_, parts) in self.tiles.items()}
        v.seam[...] = jnp.zeros_like(v.seam)
        top = (max(self.tiles) + 1) * 16
        rest = v.out_flat.shape[0] - top
        v.seam_low[16 * 16 : 16 * 16 + rest, :] = jnp.zeros((rest, LANES), jnp.bfloat16)
        self.write(16, rest, top)

    def write(self, index, rows, base):
        v = self.v
        copy = pltpu.make_async_copy(
            v.seam_low.at[index * 16 : index * 16 + rows], v.out_flat.at[base : base + rows], v.fsem.at[index]
        )
        copy.start()
        self.small.append(copy)

    def send(self, low, length, base):
        v, slot = self.v, self.at % 2
        self.at += 1
        if slot in self.busy:
            self.busy[slot].wait()
        cast_rows(v.stage.at[slot], 0, v.flat, low, length, jnp.bfloat16)
        copy = pltpu.make_async_copy(
            v.stage.at[slot, 0:length], v.out_flat.at[base : base + length], v.ssem.at[slot, 0]
        )
        copy.start()
        self.busy[slot] = copy

    def layer(self, start, rows):
        v, stop = self.v, start + rows
        for tile in self.tiles:
            low, high = max(start, tile * 16), min(stop, tile * 16 + 16)
            if low >= high:
                continue
            index = self.tiles[tile][0]
            v.seam[index, low - tile * 16 : high - tile * 16, :] = v.flat[MARGIN + low - start : MARGIN + high - start, :]
            self.left[tile] -= 1
            if not self.left[tile]:
                v.seam_low[index * 16 : index * 16 + 16, :] = half_of(v.seam[index])
                self.write(index, 16, tile * 16)
        low, high = -(-start // 16) * 16, stop // 16 * 16
        if high > low:
            self.send(MARGIN + low - start, high - low, low)

    def settle(self):
        for copy in list(self.busy.values()) + self.small:
            copy.wait()
        self.busy, self.small = {}, []


SHARE = 3072


class Reduce:
    ORDER = (
        (3, 3072, 3072), (3, 0, 3072), (2, 3072, 3072), (2, 0, 3072), (1, 3072, 3072), (1, 0, 3072),
        (0, 1024, 3072), (0, 4096, 2048), (0, 0, 1024),
    )

    def __init__(self, v, count):
        self.v, self.count = v, count
        self.flying, self.queue, self.late = [], [], []
        self.copies = {}
        rank = v.rank
        self.lower, self.upper = lax.rem(rank, 2), lax.div(rank, 2)
        self.side, self.depth = lax.rem(v.spot, 2), lax.div(v.spot, 2)
        self.group = v.space // 2

    def part(self, k):
        return self.ORDER[k][2] // 4 // self.v.space

    def slice_at(self, k, spot):
        return lax.rem(spot, 2) * (self.ORDER[k][2] // 8) + lax.div(spot, 2) * self.part(k)

    def offer(self, *numbers, now=True):
        if now:
            self.queue += list(numbers)
        else:
            self.late += list(numbers)

    LONG = 6

    def stages(self, k):
        if k < self.LONG:
            return (self.core, self.across, self.side_sum, self.deep_sum, self.deep_out, self.owner, self.beside)
        if k < len(self.ORDER) - 1:
            return (self.core, self.across, self.stripes, self.along, self.beside)
        return (self.ranks, self.stripes, self.along, self.beside)

    def tick(self):
        for entry in self.flying:
            self.stages(entry[0])[entry[1]](entry[0])
            entry[1] += 1
        self.flying = [entry for entry in self.flying if entry[1] < len(self.stages(entry[0]))]
        if self.queue:
            number = self.queue.pop(0)
            self.v.flush.settle()
            self.begin(number)
            self.flying.append([number, 0])
        self.queue, self.late = self.queue + self.late, []

    def begin(self, k):
        v, slot = self.v, k % 2
        quarter, low, size = self.ORDER[k]
        start = quarter * self.count // (LANES * 16) * 16 + low
        half = size // 2
        if k == len(self.ORDER) - 1:
            self.begin_ranks(start, size // 4)
            return

        def rows(which):
            return v.out_flat.at[pl.ds(pl.multiple_of(start + which * half, 16), half)]

        copy = remote(
            rows(1 - self.lower), v.rcore.at[slot, 0:half], v.rsend.at[0, slot], v.rrecv.at[0, slot], {DP: v.mate}
        )
        own = pltpu.make_async_copy(rows(self.lower), v.own.at[slot, 0:half], v.rlocal.at[slot])
        copy.start()
        own.start()
        self.copies[k] = (copy, own)

    def begin_ranks(self, start, rows):
        v = self.v

        def block(rank):
            at = start + lax.rem(rank, 2) * (2 * rows) + lax.div(rank, 2) * rows
            return v.out_flat.at[pl.ds(pl.multiple_of(at, 16), rows)]

        for turn in range(1, 4):
            to = lax.rem(v.rank + turn, 4)
            remote(block(to), v.dall.at[v.rank], v.dsend, v.drecv, {DP: to}).start()
        self.mine = pltpu.make_async_copy(block(v.rank), v.dall.at[v.rank], v.rlocal.at[0])
        self.mine.start()

    def ranks(self, k):
        v, slot, part = self.v, k % 2, self.part(k)
        self.mine.wait()
        drain_bytes(v.dall.at[0:3], v.dsend)
        drain_bytes(v.dall.at[0:3], v.drecv)
        self.finish_f(k)
        value = full_of(v.dall[0]) + full_of(v.dall[1]) + full_of(v.dall[2]) + full_of(v.dall[3])
        rows = self.ORDER[k][2] // 4
        v.ks[slot, 0:rows, :] = value
        v.ts[slot, 0:rows, :] = half_of(value)
        v.acc[slot, 0:part, :] = v.ks[slot, pl.ds(pl.multiple_of(self.slice_at(k, v.spot), 16), part), :]
        self.each(lambda step: self.s_copy(k, step).start(), 1, v.space)

    def finish_f(self, k):
        drain_bytes(self.s_all(k - 2), self.v.s2send.at[k % 2])
        self.f_sent(k - 2)

    def core(self, k):
        v, slot = self.v, k % 2
        copy, own = self.copies[k]
        copy.wait()
        own.wait()
        if k >= 2:
            self.x_copy(k - 2).wait_send()
        quarter = self.ORDER[k][2] // 4

        def add(step, carry):
            at = pl.multiple_of(step * 128, 128)
            near = pl.ds(pl.multiple_of(self.upper * quarter + at, 128), 128)
            far = pl.ds(pl.multiple_of((1 - self.upper) * quarter + at, 128), 128)
            to = pl.ds(at, 128)
            v.tx[slot, to, :] = half_of(full_of(v.own[slot, far, :]) + full_of(v.rcore[slot, far, :]))
            v.ks[slot, to, :] = full_of(v.own[slot, near, :]) + full_of(v.rcore[slot, near, :])
            return carry

        lax.fori_loop(0, quarter // 128, add, 0)
        self.x_copy(k).start()

    def x_copy(self, k):
        v, slot = self.v, k % 2
        rows = slice(0, self.ORDER[k][2] // 4)
        return remote(
            v.tx.at[slot, rows], v.rx.at[slot, rows], v.rsend.at[1, slot], v.rrecv.at[1, slot], {DP: v.other}
        )

    def s_copy(self, k, step):
        v, slot, part = self.v, k % 2, self.part(k)
        to = lax.rem(v.spot + step, v.space)
        src = v.ts.at[slot, pl.ds(pl.multiple_of(self.slice_at(k, to), 16), part)]
        dst = v.rs.at[slot, v.spot, 0:part]
        return remote(src, dst, v.s2send.at[slot], v.s2recv.at[slot], {SPACE: to})

    def s_all(self, k):
        return self.v.rs.at[k % 2, 0 : self.v.space - 1, 0 : self.part(k)]

    def each(self, what, start, stop):
        def body(step, carry):
            what(step)
            return carry

        lax.fori_loop(start, stop, body, 0)

    def across(self, k):
        v, slot = self.v, k % 2
        self.x_copy(k).wait_recv()
        if k < self.LONG:
            self.across_long(k)
            return

        def add(step, carry):
            to = pl.ds(pl.multiple_of(step * 128, 128), 128)
            value = v.ks[slot, to, :] + full_of(v.rx[slot, to, :])
            v.ks[slot, to, :] = value
            v.ts[slot, to, :] = half_of(value)
            return carry

        lax.fori_loop(0, self.ORDER[k][2] // 4 // 128, add, 0)
        part = self.part(k)
        v.acc[slot, 0:part, :] = v.ks[slot, pl.ds(pl.multiple_of(self.slice_at(k, v.spot), 16), part), :]
        self.each(lambda step: self.s_copy(k, step).start(), 1, v.space)

    def across_long(self, k):
        v, slot = self.v, k % 2
        if k >= 2:
            self.side_copy(k - 2).wait_send()
        rows = self.ORDER[k][2] // 8

        def add(step, carry):
            at = pl.multiple_of(step * 128, 128)
            near = pl.ds(pl.multiple_of(self.side * rows + at, 128), 128)
            far = pl.ds(pl.multiple_of((1 - self.side) * rows + at, 128), 128)
            to = pl.ds(at, 128)
            v.ty[slot, to, :] = half_of(v.ks[slot, far, :] + full_of(v.rx[slot, far, :]))
            v.ky[slot, to, :] = v.ks[slot, near, :] + full_of(v.rx[slot, near, :])
            return carry

        lax.fori_loop(0, rows // 128, add, 0)
        self.side_copy(k).start()

    def side_copy(self, k):
        v, slot = self.v, k % 2
        return remote(v.ty.at[slot], v.ry.at[slot], v.rsend.at[2, slot], v.rrecv.at[2, slot], {SPACE: v.twin})

    def deep_at(self, k, depth):
        return pl.ds(pl.multiple_of(depth * self.part(k), 16), self.part(k))

    def deep_copy(self, k, step):
        v, slot = self.v, k % 2
        to = lax.rem(self.depth + step, self.group)
        return remote(
            v.tz.at[slot, self.deep_at(k, to)], v.rz.at[slot, self.depth], v.z1send.at[slot],
            v.z1recv.at[slot], {SPACE: to * 2 + self.side},
        )

    def deep_all(self, k):
        return self.v.rz.at[k % 2, 0 : self.group - 1]

    def side_sum(self, k):
        v, slot = self.v, k % 2
        self.side_copy(k).wait_recv()
        if k >= 2:
            drain_bytes(self.deep_all(k - 2), v.z1send.at[slot])
        value = v.ky[slot] + full_of(v.ry[slot])
        v.tz[slot] = half_of(value)
        v.ky[slot] = value
        v.kz[slot] = v.ky[slot, self.deep_at(k, self.depth), :]
        self.each(lambda step: self.deep_copy(k, step).start(), 1, self.group)

    def out_copy(self, k, step):
        v, slot = self.v, k % 3
        to = lax.rem(self.depth + step, self.group)
        block = v.az.at[slot, self.deep_at(k, self.depth)]
        return remote(
            block, block, v.z2send.at[slot], v.z2recv.at[slot], {SPACE: to * 2 + self.side}
        )

    def deep_sum(self, k):
        v, slot = self.v, k % 2
        drain_bytes(self.deep_all(k), v.z1recv.at[slot])

        def add(step, value):
            return value + full_of(v.rz[slot, lax.rem(self.depth + step, self.group)])

        value = lax.fori_loop(1, self.group, add, v.kz[slot])
        if k >= 2:
            self.own_wait(k - 2)
        v.az[k % 3, self.deep_at(k, self.depth), :] = half_of(value)
        self.each(lambda step: self.out_copy(k, step).start(), 1, self.group)

    def own_rows(self, k, lower, upper):
        quarter, low, size = self.ORDER[k]
        at = low + lower * (size // 2) + upper * (size // 4) + self.side * (size // 8)
        return pl.ds(pl.multiple_of(at, 16), size // 8)

    def own_copy(self, k):
        v = self.v
        rows = self.own_rows(k, self.lower, self.upper)
        return remote(v.az.at[k % 3], v.gath.at[rows], v.osend.at[k % 3], v.orecv.at[k], {DP: self.ORDER[k][0]})

    def own_wait(self, k):
        pl.when(self.v.rank != self.ORDER[k][0])(self.own_copy(k).wait_send)

    def deep_out(self, k):
        v = self.v
        several = v.az.at[k % 3, 0 : (self.group - 1) * self.part(k)]
        drain_bytes(several, v.z2send.at[k % 3])
        drain_bytes(several, v.z2recv.at[k % 3])
        pl.when(v.rank != self.ORDER[k][0])(self.own_copy(k).start)

        @pl.when(v.rank == self.ORDER[k][0])
        def _():
            v.gath[self.own_rows(k, self.lower, self.upper), :] = v.az[k % 3]

    def owner(self, k):
        v = self.v

        @pl.when(v.rank == self.ORDER[k][0])
        def _():
            drain_bytes(v.gath.at[0 : 3 * (self.ORDER[k][2] // 8)], v.orecv.at[k])
            for copy in self.y_copies(k):
                copy.start()

    def place(self, k, lower, upper, spot):
        quarter, low, size = self.ORDER[k]
        at = low + lower * (size // 2) + upper * (size // 4) + self.slice_at(k, spot)
        return pl.ds(pl.multiple_of(at, 16), self.part(k))

    def f_copy(self, k, step):
        v, slot = self.v, k % 2
        quarter = self.ORDER[k][0]
        to = lax.rem(self.depth + step, self.group) * 2 + self.side
        return remote(
            v.fin.at[slot, 0 : self.part(k)], v.gath.at[self.place(k, self.lower, self.upper, v.spot)],
            v.fsend.at[slot], v.frecv.at[k], {DP: quarter, SPACE: to},
        )

    def f_all(self, k, what):
        v = self.v
        pl.when(v.rank != self.ORDER[k][0])(lambda: what(self.f_copy(k, 0)))
        self.each(lambda step: what(self.f_copy(k, step)), 1, self.group)

    def f_sent(self, k):
        v = self.v
        quarter = self.ORDER[k][0]
        pl.when(v.rank != quarter)(lambda: self.f_copy(k, 0).wait_send())
        drain_bytes(v.gath.at[0 : (self.group - 1) * self.part(k)], v.fsend.at[k % 2])

    def stripes(self, k):
        v, slot, part = self.v, k % 2, self.part(k)
        quarter = self.ORDER[k][0]
        drain_bytes(self.s_all(k), v.s2recv.at[slot])

        def add(step, value):
            return value + full_of(v.rs[slot, lax.rem(v.spot + step, v.space), 0:part])

        value = half_of(lax.fori_loop(1, v.space, add, v.acc[slot, 0:part, :]))
        v.fin[slot, 0:part, :] = value

        @pl.when(v.rank == quarter)
        def _():
            v.gath[self.place(k, self.lower, self.upper, v.spot), :] = v.fin[slot, 0:part, :]

        self.f_all(k, lambda copy: copy.start())

    def y_copies(self, k):
        v = self.v
        quarter, low, size = self.ORDER[k]
        out = []
        for i in range(4):
            at = pl.multiple_of(low + i * (size // 4) + self.side * (size // 8), 16)
            block = v.gath.at[pl.ds(at, size // 8)]
            out.append(remote(block, block, v.ysend.at[k], v.yrecv.at[k], {SPACE: v.twin}))
        return out

    def along(self, k):
        v = self.v
        quarter = self.ORDER[k][0]

        @pl.when(v.rank == quarter)
        def _():
            drain_bytes(v.gath.at[0 : (4 * self.group - 1) * self.part(k)], v.frecv.at[k])
            for copy in self.y_copies(k):
                copy.start()

    def beside(self, k):
        v = self.v

        @pl.when(v.rank == self.ORDER[k][0])
        def _():
            several = v.gath.at[0 : self.ORDER[k][2] // 2]
            drain_bytes(several, v.ysend.at[k])
            drain_bytes(several, v.yrecv.at[k])

    def settle(self):
        v = self.v
        for k in range(self.LONG - 2, self.LONG):
            self.side_copy(k).wait_send()
            drain_bytes(self.deep_all(k), v.z1send.at[k % 2])
            self.own_wait(k)
        for k in range(len(self.ORDER) - 3, len(self.ORDER) - 1):
            self.x_copy(k).wait_send()
        for k in range(len(self.ORDER) - 2, len(self.ORDER)):
            drain_bytes(self.s_all(k), v.s2send.at[k % 2])
            self.f_sent(k)

    def ready(self):
        v, count = self.v, self.count
        v.gath[2 * SHARE :, :] = jnp.zeros((32, LANES), jnp.bfloat16)

        @pl.when(v.rank == 3)
        def _():
            at = self.bias_base() - 3 * count // (LANES * 16) * 16
            v.gath[at : at + 32, :] = half_of(full_of(v.gath[at : at + 32, :]) + v.bsum[...])

    def lay(self, first, last):
        v, count = self.v, self.count
        offset = v.rank * count - quarter_base(v.rank, count) * LANES
        skip = lax.div(offset, LANES)
        shift = lax.rem(offset, LANES)
        near = lane_index((256, LANES)) < LANES - shift

        def staged(slot):
            return v.mm_tmp.at[pl.ds(pl.multiple_of(slot * 256, 256), 256)]

        def out(step):
            at = pl.multiple_of(step * 256, 256)
            slot = lax.rem(step, 2)
            return pltpu.make_async_copy(staged(slot), v.out_grads.at[pl.ds(at, 256)], v.osem.at[4 + slot])

        def place(step, carry):
            at = pl.multiple_of(step * 256, 256)
            v.tmp[0:288, :] = pltpu.roll(full_of(v.gath[pl.ds(at, 288), :]), lax.rem(LANES - shift, LANES), 1)
            pl.when(step > first + 1)(out(step - 2).wait)
            staged(lax.rem(step, 2))[...] = jnp.where(near, v.tmp[pl.ds(skip, 256), :], v.tmp[pl.ds(skip + 1, 256), :])
            out(step).start()
            return carry

        lax.fori_loop(first, last, place, 0)
        for step in (last - 2, last - 1):
            out(step).wait()

    def bias_base(self):
        return flat_rows()[1] // 16 * 16

    def bias_core(self):
        v = self.v
        self.b1 = remote(v.bown, v.bcore, v.bsend.at[0], v.brecv.at[0], {DP: v.mate})
        self.b1.start()

    def bias_across(self):
        v = self.v
        self.b1.wait()
        v.btwo[...] = v.bown[...] + v.bcore[...]
        self.b2 = remote(v.btwo, v.bacross, v.bsend.at[1], v.brecv.at[1], {DP: v.other})
        self.b2.start()

    def bias_stripes(self):
        v = self.v
        self.b2.wait()
        v.bfour[...] = v.btwo[...] + v.bacross[...]
        self.b3 = Swap(v, 8, v.bfour, v.ball, True)
        self.b3.start()

    def bias_end(self):
        v = self.v
        self.b3.receive()
        self.b3.sent()
        v.ball[v.spot] = v.bfour[...]
        v.bsum[...] = jnp.sum(v.ball[...], axis=0)


def ones_sum(g):
    return mm(jnp.ones((8, g.shape[0]), jnp.bfloat16), g)[0:1, :]


def keep_bias(v, name, value):
    for block in range(-(-value.shape[1] // 128)):
        at = BIAS_AT[name] + block
        v.gbias[at : at + 1, :] = value[:, block * 128 : (block + 1) * 128]


def gradients_gru(v, gates_name, cand_name, parts, g_of):
    starts, _, _, _ = flat_rows()
    total = 0.0
    for b in range(BATCH):
        total = total + ones_sum(g_of(b))
    keep_bias(v, gates_name, total[:, 0:256])
    keep_bias(v, cand_name, total[:, 256:384])

    def taps(number, first, last):
        return lambda b: join(parts(t)[number](b) for t in range(first, last))

    state = tn_all(taps(0, 0, 5), g_of, 0, 256)
    for t in range(5):
        pack_pairs(v.flat, t * 384, 128, state[t * 128 : (t + 1) * 128, 0:128], state[t * 128 : (t + 1) * 128, 128:256])
    state = tn_all(taps(2, 0, 5), g_of, 256, 384)
    for t in range(5):
        v.mm_tmp[pl.ds(MARGIN + t * 384, 128), :] = state[t * 128 : (t + 1) * 128, :]
    for first, last in ((0, 2), (2, 4), (4, 5)):
        inputs = tn_all(taps(1, first, last), g_of, 0, 384)
        for t in range(first, last):
            rows = slice((t - first) * 256, (t - first + 1) * 256)
            pack_pairs(v.flat, t * 384 + 128, 256, inputs[rows, 0:128], inputs[rows, 128:256])
            v.mm_tmp[pl.ds(MARGIN + t * 384 + 128, 256), :] = inputs[rows, 256:384]
    v.flush.layer(starts[gates_name], 3840)
    cast_rows(v.flat, MARGIN, v.mm_tmp, MARGIN, 1920, jnp.float32)
    v.flush.layer(starts[cand_name], 1920)


def tn_all(part, g_of, low, high):
    return tn(join((part(b) for b in range(BATCH)), 0), join((g_of(b, low, high) for b in range(BATCH)), 0))


def gradients_heads(v):
    starts, _, _, _ = flat_rows()
    total = 0.0
    for b in range(BATCH):
        total = total + ones_sum(v.hgo[b])
    keep_bias(v, FLOW_HIDDEN, total[:, 0:256])
    keep_bias(v, MASK_HIDDEN, total[:, 256:512])
    for name, lane in ((FLOW_HIDDEN, 0), (MASK_HIDDEN, 256)):
        grads = join((v.hgo[b, :, lane : lane + 256] for b in range(BATCH)), 0)
        for group in range(3):
            taps = [join(heads_part(v, b, group * 3 + c)[...] for c in range(3)) for b in range(BATCH)]
            value = tn(join(taps, 0), grads)
            for c in range(3):
                rows = slice(c * 128, (c + 1) * 128)
                pack_pairs(v.flat, (group * 3 + c) * 128, 128, value[rows, 0:128], value[rows, 128:256])
        v.flush.layer(starts[name], 2304)

    total = 0.0
    sums = 0.0
    for b in range(BATCH):
        total = total + mm(v.dtb[b], v.feat[b])
        sums = sums + jnp.sum(full_of(half_of(v.dg[b])), axis=1, keepdims=True)
    lane1 = lane_index((1, LANES))
    at = BIAS_AT[FLOW_OUT]
    v.gbias[at : at + 1, :] = jnp.where(lane1 == 0, sums[0:1, :], jnp.where(lane1 == 1, sums[1:2, :], 0.0))
    v.fo_tmp[...] = total[:, 0:128]
    v.fo_tmp2[...] = total[:, 128:256]
    for quarter in range(4):
        value = 0.0
        for which in range(2):
            rows = jnp.concatenate(
                [v.fo_tmp[pl.ds(which, 9, stride=2), :], v.fo_tmp2[pl.ds(which, 9, stride=2), :]], axis=1
            )
            value = value + nt(half_of(rows), split_pick(which, quarter))
        v.flat[pl.ds(MARGIN + quarter, 9, stride=4), :] = value
    v.flush.layer(starts[FLOW_OUT], 36)

    lane = lane_index((128, LANES))
    low_half = lane < 64
    even, odd = [], []
    total = 0.0
    for b in range(BATCH):
        total = total + ones_sum(quarter_of(v.grad_mask[b]))
    for block in range(5):
        wide = min(128, MASK - block * 128)
        at = BIAS_AT[MASK_OUT] + block
        v.gbias[at : at + 1, 0:wide] = total[:, block * 128 : block * 128 + wide]
        value = 0.0
        for b in range(BATCH):
            value = value + tn(v.mf[b], quarter_of(v.grad_mask[b, :, block * 128 : block * 128 + wide]))
        v.pair_a[:, 0:wide] = value
        even.append(v.pair_a[pl.ds(0, 128, stride=2), :])
        odd.append(pltpu.roll(v.pair_a[pl.ds(1, 128, stride=2), :], 64, 1))
    for i in range(4):
        v.flat[pl.ds(MARGIN + i, 128, stride=9), :] = even[i]
    v.flat[pl.ds(MARGIN + 4, 128, stride=9), :] = jnp.where(low_half, even[4], odd[0])
    for i in range(4):
        v.flat[pl.ds(MARGIN + 5 + i, 128, stride=9), :] = jnp.where(low_half, odd[i], odd[i + 1])
    v.flush.layer(starts[MASK_OUT], 1152)


def rows_back(v):
    v.back_state.receive()
    take_own(v, v.a_state, v.b_state)
    unpack_back(v, v.b_state, v.state)
    v.reduce.tick()

    def image(b, carry):
        r = v.state[b]
        s = full_of(v.net[b])
        update, reset, cand = v.ru[b], v.rr[b], v.rc[b]
        cg = full_of(half_of(r * update * (1.0 - cand * cand)))
        spread_five(v, cg, None, 256, True)
        reset_grad = nt(
            join(taps_part(v, t, 256, 384)[...] for t in range(5)),
            join(v.w_rs[t * 128 : (t + 1) * 128, 256:384] for t in range(5)),
        )
        low = full_of(half_of(r * (cand - s) * update * (1.0 - update)))
        high = full_of(half_of(reset_grad * s * reset * (1.0 - reset)))
        spread_five(v, low, None, 0, True)
        spread_five(v, high, None, 128, True)
        v.gr[b] = taps_part(v, 2, 0, 384)[...]
        state_grad = r * (1.0 - update) + reset_grad * reset
        state_grad = state_grad + nt(
            join(taps_part(v, t, 0, 256)[...] for t in range(5)),
            join(v.w_rs[t * 128 : (t + 1) * 128, 0:256] for t in range(5)),
        )
        v.ru[b] = state_grad
        inputs_grad = nt(
            join(taps_part(v, t, 0, 384)[...] for t in range(5)),
            join(v.w_ri[t * 256 : (t + 1) * 256, :] for t in range(5)),
        )
        v.rr[b] = inputs_grad[:, 0:128]
        v.rc[b] = inputs_grad[:, 128:256]
        return carry

    lax.fori_loop(0, BATCH, image, 0)
    v.store_gnet.start()
    v.back_context.receive()
    v.back_motion.receive()
    take_own(v, v.a_context, v.b_context)
    take_own(v, v.a_motion, v.b_motion)
    unpack_back(v, v.b_context, v.lr)
    unpack_back(v, v.b_motion, v.lu)

    def total(b, carry):
        v.rr[b] = v.rr[b] + v.lr[b]
        motion = v.rc[b] + v.lu[b]
        v.mge[b, 256:896, :] = half_of(motion * full_of(v.slope_m[b]))
        high = half_of(motion)
        low = half_of(motion - full_of(high))
        pick = half_of(jnp.where(lane_index((16, LANES)) == row_index((16, LANES)) + 126, 1.0, 0.0))
        v.gf_base[b] = (nt(pick, high) + nt(pick, low))[0:8, :]
        return carry

    lax.fori_loop(0, BATCH, total, 0)
    v.halo_mg.start()
    v.store_gctx.start()


def gcorr_stores(v, b):
    return [
        pltpu.make_async_copy(v.mm_tmp.at[y * 328 : y * 328 + CORR], v.out_gcorr.at[b, y], v.gsem.at[y])
        for y in range(ROWS)
    ]


def branch_back(v):
    v.halo_mg.receive()

    def image(b, carry):
        up = jnp.where(v.spot > 0, full_of(v.mge[b, 0:256, :]), 0.0)
        own = full_of(v.mge[b, 256:896, :])
        down = jnp.where(v.spot < v.space - 1, full_of(v.mge[b, 896:1152, :]), 0.0)
        spread_rows(v, 0, (jnp.concatenate([up, own, down], axis=0),), 1152, v.xi, 0, 128, True)
        joint = nt(
            join(v.xi[(2 - a) * 128 : (2 - a) * 128 + 896, 0:384] for a in range(3)),
            join(v.w_mm[k * 256 : (k + 1) * 256, :] for k in range(9)),
        )
        branch = joint * full_of(v.slope_j[b])
        low = full_of(half_of(edge_rows(v, branch[:, 0:128], WIDE)))
        high = full_of(half_of(edge_rows(v, branch[:, 128:256], WIDE)))
        spread_rows(v, 0, (low, high), 896, v.hx_j.at[b], 0, 256, True)
        return carry

    lax.fori_loop(0, BATCH, image, 0)


def branch_own(v, b, low=0, high=256):
    return v.hx_j[b, 128:768, 256 + low : 256 + high]


def flow_back(v):
    def image(b, carry):
        rows = [slice((2 - a) * 128, (2 - a) * 128 + 640) for a in range(3)]
        flow_grad = nt(
            join(v.hx_j[b, rows[a], c * 256 + 128 : (c + 1) * 256] for a in range(3) for c in range(3)),
            join(v.w_fm[k * 128 : (k + 1) * 128, :] for k in range(9)),
        )
        v.fpg[b] = half_of(flow_grad * full_of(v.slope_fi[b]))
        z = nt(v.w_fi[...], v.fpg[b])
        total = jnp.zeros((32, LANES), jnp.float32)
        lane = lane_index((32, LANES))
        for across in range(7):
            v.fs[across] = jnp.zeros((32, LANES), jnp.float32)
            for y in range(ROWS):
                v.fs[across, 2 * y : 2 * y + 16, :] += z[across * 16 : across * 16 + 16, y * 128 : (y + 1) * 128]
            d = across - 3
            value = v.fs[across]
            if d:
                value = pltpu.roll(value, d % LANES, 1)
                value = jnp.where((lane - d >= 0) & (lane - d < WIDE), value, 0.0)
            total = total + value
        v.gf[b] = total
        return carry

    lax.fori_loop(0, BATCH, image, 0)
    v.halo_gf.start()


def corr_back(v):
    def image(b, carry):
        corr_grad = nt(
            join(v.hx_j[b, (2 - a) * 128 : (2 - a) * 128 + 640, :] for a in range(3)),
            join(v.w_cm[k * 256 : (k + 1) * 256, :] for k in range(9)),
        )
        v.cpg[b] = half_of(corr_grad * full_of(v.slope_ci[b]))
        stores = gcorr_stores(v, b)
        for store in stores:
            pl.when(b > 0)(store.wait)
        gcorr = nt(v.w_ci[...], v.cpg[b])
        for y in range(ROWS):
            v.mm_tmp[y * 328 : y * 328 + CORR, :] = gcorr[:, y * WIDE : (y + 1) * WIDE]
        for store in stores:
            store.start()
        return carry

    lax.fori_loop(0, BATCH, image, 0)


def summed(v, ref, name):
    total = 0.0
    for b in range(BATCH):
        total = total + ones_sum(ref(b))
    keep_bias(v, name, total)


def gradients_motion(v):
    starts = flat_rows()[0]
    summed(v, lambda b: v.mge[b, 256:896, :], MOTION_MIX)
    grads = join((v.mge[b, 256:896, :] for b in range(BATCH)), 0)
    for a in range(3):
        taps = join((v.hx_j[b, a * 128 : a * 128 + 640, :] for b in range(BATCH)), 0)
        v.mm_tmp[a * 768 : (a + 1) * 768, :] = tn(taps, grads)
    lane36 = lane_index((36, LANES))
    for r in range(63):
        first = v.mm_tmp[pl.ds(r, 36, stride=64), :]
        second = v.mm_tmp[pl.ds(r + 1, 36, stride=64), :]
        if r:
            first = pltpu.roll(first, LANES - 2 * r, 1)
        second = pltpu.roll(second, 126 - 2 * r, 1)
        v.flat[pl.ds(MARGIN + r, 36, stride=63), :] = jnp.where(lane36 < 126 - 2 * r, first, second)
    v.flush.layer(starts[MOTION_MIX], 2268)


def gradients_branches(v):
    starts = flat_rows()[0]
    summed(v, lambda b: branch_own(v, b), CORR_MIX)
    summed(v, lambda b: branch_own(v, b, 128, 256), FLOW_MIX)
    grads = join((branch_own(v, b, 128, 256) for b in range(BATCH)), 0)
    for k in range(9):
        a, c = k // 3, k % 3
        if c == 0:
            taps = join((v.hx_f[b, (a + 1) * 128 : (a + 1) * 128 + 640, :] for b in range(BATCH)), 0)
            group = tn(taps, grads)
        v.pair_a[0:128, :] = group[c * 128 : (c + 1) * 128]
        even, odd = (v.pair_a[pl.ds(i, 64, stride=2), :] for i in range(2))
        v.flat[MARGIN + 64 * k : MARGIN + 64 * (k + 1), :] = jnp.where(
            lane_index((64, LANES)) < 64, pltpu.roll(even, 64, 1), odd
        )
    v.flush.layer(starts[FLOW_MIX], 576)

    low_half = lane_index((128, LANES)) < 64
    grads = join((branch_own(v, b) for b in range(BATCH)), 0)
    for k in range(9):
        a, c = k // 3, k % 3
        if c == 0:
            taps = join((v.hx_c[b, (a + 1) * 128 : (a + 1) * 128 + 640, :] for b in range(BATCH)), 0)
            group = tn(taps, grads)
        v.pair_a[...] = group[c * 256 : (c + 1) * 256, 0:128]
        v.pair_b[...] = group[c * 256 : (c + 1) * 256, 128:256]
        even, odd = (v.pair_a[pl.ds(i, 128, stride=2), :] for i in range(2))
        even_high, odd_high = (v.pair_b[pl.ds(i, 128, stride=2), :] for i in range(2))
        odd, odd_high = pltpu.roll(odd, 64, 1), pltpu.roll(odd_high, 64, 1)
        at = MARGIN + 384 * k
        v.flat[pl.ds(at, 128, stride=3), :] = even
        v.flat[pl.ds(at + 1, 128, stride=3), :] = jnp.where(low_half, even_high, odd)
        v.flat[pl.ds(at + 2, 128, stride=3), :] = jnp.where(low_half, odd, odd_high)
        if k == 4:
            v.reduce.tick()
    v.flush.layer(starts[CORR_MIX], 3456)


def gradients_flow_in(v):
    starts = flat_rows()[0]
    summed(v, lambda b: v.fpg[b], FLOW_IN)
    value = 0.0
    for b in range(BATCH):
        value = value + mm(v.xt[b, :, 256:896], v.fpg[b])
    v.flow_tmp[...] = value
    for across in range(7):
        for comp in range(2):
            v.flat[pl.ds(MARGIN + across * 2 + comp, 7, stride=14), :] = v.flow_tmp[
                pl.ds(across * 16 + comp, 7, stride=2), :
            ]
    v.flush.layer(starts[FLOW_IN], 98)


def gradients_corr_in(v):
    starts = flat_rows()[0]
    summed(v, lambda b: v.cpg[b], CORR_IN)
    value = 0.0
    for b in range(BATCH):
        value = value + mm(lines_of(v.corr, b, ROWS), v.cpg[b])
    pack_pairs(v.flat, 0, 324, value[:, 0:128], value[:, 128:256])
    v.flush.layer(starts[CORR_IN], 648)


def bias_tile(v):
    starts, bias_row, spots, inner = flat_rows()
    lead = bias_row % 16
    lane1 = lane_index((1, LANES))
    v.bown[...] = jnp.zeros_like(v.bown)
    for name, height, width in shapes():
        for block in range(-(-width // LANES)):
            value = v.gbias[BIAS_AT[name] + block : BIAS_AT[name] + block + 1, :]
            if name == FLOW_MIX:
                value = pltpu.roll(value, 64, 1)
            left = width - block * LANES
            if left < LANES:
                value = jnp.where(lane1 < left, value, 0.0)
            at = spots[name] + block * LANES
            row, shift = lead + at // LANES, at % LANES
            moved = pltpu.roll(value, shift, 1) if shift else value
            v.bown[row : row + 1, :] = v.bown[row : row + 1, :] + jnp.where(lane1 >= shift, moved, 0.0)
            if shift:
                v.bown[row + 1 : row + 2, :] = v.bown[row + 1 : row + 2, :] + jnp.where(lane1 < shift, moved, 0.0)


def finish(v):
    spot, last = v.spot, v.space - 1
    v.halo_gf.receive()
    for b in range(BATCH):
        v.tmp2[...] = v.gf[b]
        up = jnp.where(spot > 0, v.gf_up[b], 0.0)
        down = jnp.where(spot < last, v.gf_down[b], 0.0)
        v.tmp2[6:12, :] += up[16:22, :]
        v.tmp2[10:16, :] += down[0:6, :]
        for y in range(ROWS):
            v.out_gflow[b, 2 * y : 2 * y + 2, :] = (
                v.tmp2[6 + 2 * y : 8 + 2 * y, :] + v.gf_base[b, 0:2, y * 128 : (y + 1) * 128]
            )
    v.loss_in[v.spot] = v.losses[...]
    total = jnp.sum(v.loss_in[...], axis=0)
    counts = jnp.sum(v.counts[...], axis=0)
    value = total / jnp.maximum(counts, 1.0)
    for b in range(BATCH):
        v.out_loss[b] = v.pick_count(value, b)


class View:
    pass


def main_kernel(names, space, count, *refs):
    v = View()
    for name, ref in zip(names, refs):
        setattr(v, name, ref)
    v.space = space
    v.lu, v.lc = v.motion, v.state
    v.spot = lax.axis_index(SPACE)
    v.rank = lax.axis_index(DP)
    v.mate, v.other, v.twin = mate_of(v.rank), lax.rem(v.rank + 2, 4), mate_of(v.spot)
    spot = v.spot
    barrier = pltpu.get_barrier_semaphore()

    def hello(step, carry):
        pl.semaphore_signal(barrier, inc=1, device_id={SPACE: lax.rem(spot + step, space)}, device_id_type=MESH)
        return carry

    lax.fori_loop(1, space, hello, 0)
    for turn in range(1, 4):

        def greet_rank(step, carry):
            place = lax.rem(spot + 2 * step, space)
            device = {DP: lax.rem(v.rank + turn, 4), SPACE: place}
            pl.semaphore_signal(barrier, inc=1, device_id=device, device_id_type=MESH)
            return carry

        lax.fori_loop(0, space // 2, greet_rank, 0)
    pl.semaphore_wait(barrier, space - 1 + 3 * (space // 2))

    v.store_gnet = pltpu.make_async_copy(v.ru, v.out_gnet, v.osem.at[0])
    v.store_gctx = pltpu.make_async_copy(v.rr, v.out_gctx, v.osem.at[1])
    rows = row_index((8, LANES))
    counted = jnp.zeros((8, LANES), jnp.float32)
    for b in range(BATCH):
        counted = jnp.where(rows == b, jnp.sum(v.valid[b].astype(jnp.float32)), counted)
    v.count_out[...] = counted
    v.pick_count = lambda counts, b: jnp.sum(jnp.where((rows == b) & (lane_index((8, LANES)) == 0), counts, 0.0))
    v.swap_count = Swap(v, 0, v.count_out, v.counts, True)
    v.swap_context = Swap(v, 1, v.a_context, v.b_context)
    v.swap_motion = Swap(v, 2, v.a_motion, v.b_motion)
    v.swap_state = Swap(v, 3, v.a_state, v.b_state)
    v.back_context = Swap(v, 4, v.a_context, v.b_context)
    v.back_motion = Swap(v, 5, v.a_motion, v.b_motion)
    v.back_state = Swap(v, 6, v.a_state, v.b_state)
    v.swap_loss = Swap(v, 7, v.losses, v.loss_in, True)
    v.halo_corr = Halo(v, 0, v.corr.at[:, 0:2], v.corr.at[:, 3:5], v.corr_down, v.corr_up)
    v.halo_flow = Halo(v, 1, v.flow, v.flow, v.flow_down, v.flow_up)
    v.halo_final = Halo(v, 2, v.e_left, v.e_right, v.f_right, v.f_left)
    v.halo_mask = Halo(v, 3, v.m_left, v.m_right, v.n_right, v.n_left)
    v.halo_dg = Halo(v, 4, v.dg, v.dg, v.dg_right, v.dg_left)
    v.halo_mg = Halo(v, 5, v.mge.at[:, 256:512], v.mge.at[:, 640:896], v.mge.at[:, 896:1152], v.mge.at[:, 0:256])
    v.halo_gf = Halo(v, 6, v.gf, v.gf, v.gf_down, v.gf_up)

    load = pltpu.make_async_copy(v.local, v.gath.at[0:BLOCK], v.lsem)
    load.start()
    for b in range(BATCH):
        for y in range(ROWS):
            v.flow[b, 2 * y : 2 * y + 2, :] = full_of(v.flow_in[b, y])
        v.flow[b, 2 * ROWS : 16, :] = jnp.zeros((16 - 2 * ROWS, LANES), jnp.float32)
    v.halo_flow.start()
    v.halo_corr.start()
    v.swap_count.start()
    load.wait()
    gather_start(v, count)

    def first(b, carry):
        v.state[b] = full_of(v.context[b])
        pack_rows(v, v.state, b, v.a_context)
        return carry

    lax.fori_loop(0, BATCH, first, 0)
    v.swap_context.start()
    v.halo_flow.receive()
    widen_all(v)
    gather_pass(v, 0, 0, 2)
    early_taps(v)
    gather_pass(v, 0, 2, 4)
    for copy in v.g_own[1:]:
        copy.wait_recv()
    for copy in v.g_x[1]:
        copy.start()
    columns_zero(v)
    gather_turn(v, 0)
    unpack_encoder(v, count)
    v.halo_corr.receive()
    forward_rows(v)
    keep = [pltpu.make_async_copy(v.hx_c, v.out_keep_c, v.ksem.at[0]), pltpu.make_async_copy(v.hx_f, v.out_keep_f, v.ksem.at[1])]
    for copy in keep:
        copy.start()
    unpack_heads(v)
    v.swap_context.receive()
    v.swap_motion.receive()
    v.swap_state.receive()
    take_own(v, v.a_context, v.b_context)
    take_own(v, v.a_motion, v.b_motion)
    take_own(v, v.a_state, v.b_state)
    columns_in(v)
    columns_forward(v)
    mask_gradient(v)
    for copy in keep:
        copy.wait()
    heads(v)
    mask_output(v)
    v.swap_context.sent()
    v.swap_motion.sent()
    v.swap_state.sent()
    heads_back(v)
    v.flush = Flush(v)
    red = v.reduce = Reduce(v, count)
    gradients_heads(v)
    v.back_context.start()
    v.back_motion.start()
    red.offer(0)
    red.tick()
    gradients_gru(
        v,
        COLUMNS_GATES,
        COLUMNS_CANDIDATE,
        lambda t: (
            lambda b: v.xc[b, t * COLS : t * COLS + AREA, 0:128],
            lambda b: v.xc[b, t * COLS : t * COLS + AREA, 128:384],
            lambda b: v.xcr[b, t * COLS : t * COLS + AREA, :],
        ),
        lambda b, low=0, high=384: v.gc[b, 32 : 32 + AREA, low:high],
    )
    red.offer(1, 2)
    red.tick()
    rows_back(v)
    red.tick()
    keep = [
        pltpu.make_async_copy(v.out_keep_c, v.hx_c, v.ksem.at[0]),
        pltpu.make_async_copy(v.out_keep_f, v.hx_f, v.ksem.at[1]),
    ]
    for copy in keep:
        copy.start()
    gradients_gru(
        v,
        ROWS_GATES,
        ROWS_CANDIDATE,
        lambda t: (
            lambda b: v.xs[b * AREA : (b + 1) * AREA, t * 128 : (t + 1) * 128],
            lambda b: v.xi[b * AREA : (b + 1) * AREA, t * 256 : (t + 1) * 256],
            lambda b: v.xr[b * AREA : (b + 1) * AREA, t * 128 : (t + 1) * 128],
        ),
        lambda b, low=0, high=384: v.gr[b, :, low:high],
    )
    red.offer(3, 4)
    red.tick()
    gradients_motion(v)
    red.offer(5)
    red.tick()
    branch_back(v)
    red.tick()
    for copy in keep:
        copy.wait()
    gradients_branches(v)
    red.offer(6, now=True)
    red.tick()
    flow_back(v)
    red.tick()
    gradients_flow_in(v)
    red.offer(7, now=True)
    red.tick()
    corr_back(v)
    red.tick()
    gradients_corr_in(v)
    bias_tile(v)
    red.bias_core()
    red.offer(8, now=True)
    red.tick()
    for store in gcorr_stores(v, 0):
        store.wait()
    finish(v)
    red.bias_across()
    red.tick()
    red.bias_stripes()
    pl.when(v.rank == 0)(lambda: red.lay(4, 15))
    red.tick()
    red.bias_end()
    red.ready()
    pl.when(v.rank > 0)(lambda: red.lay(0, 24))
    red.tick()
    pl.when(v.rank == 0)(lambda: red.lay(15, 24))
    red.tick()
    assert not red.flying and not red.queue
    pl.when(v.rank == 0)(lambda: red.lay(0, 4))
    red.settle()
    for swap in (v.swap_count, v.back_context, v.back_motion, v.back_state, v.swap_loss):
        swap.sent()
    for halo in (v.halo_corr, v.halo_flow, v.halo_final, v.halo_mask, v.halo_dg, v.halo_mg, v.halo_gf):
        halo.sent()
    v.store_gnet.wait()
    v.store_gctx.wait()
    pltpu.make_async_copy(v.mask_low, v.out_mask.at[0], v.osem.at[3]).wait()


def main_call(space, count, local, net, context, corr, flow, target, valid, grad_net, grad_mask):
    total = 3 * count // (LANES * 16) * 16 + BLOCK
    low, wide = jnp.bfloat16, jnp.float32
    peers = (space, BATCH, ROWS * COLS, LANES)
    ins = dict(
        local=local, net=net, context=context, corr=corr, flow_in=flow, target=target, valid=valid,
        grad_net=grad_net, grad_mask=grad_mask,
    )
    outs = dict(
        out_net=((BATCH, AREA, 128), low),
        out_flow=((BATCH, 2, COLS, TALL), wide),
        out_mask=((BATCH, AREA, MASK), low),
        out_loss=((BATCH,), wide),
        out_flat=((total, 128), low),
        out_gnet=((BATCH, AREA, 128), wide),
        out_gctx=((BATCH, AREA, 128), wide),
        out_gcorr=((BATCH, ROWS, CORR, 128), wide),
        out_gflow=((BATCH, 16, 128), wide),
        out_keep_c=((BATCH, 1152, 768), low),
        out_keep_f=((BATCH, 1152, 384), low),
        out_all=((4 * BLOCK, 128), low),
        out_grads=((BLOCK, 128), wide),
    )
    scratch = dict(
        stage=((2, 3904, 128), low),
        seam=((16, 16, 128), wide),
        mask_low=((AREA, MASK), low),
        seam_low=((16 * 20, 128), low),
        own=((2, SHARE // 2, 128), low),
        rcore=((2, SHARE // 2, 128), low),
        tx=((2, SHARE // 4, 128), low),
        rx=((2, SHARE // 4, 128), low),
        ks=((2, SHARE // 4, 128), wide),
        ts=((2, SHARE // 4, 128), low),
        acc=((2, SHARE // 4 // space, 128), wide),
        rs=((2, space, SHARE // 4 // space, 128), low),
        fin=((2, SHARE // 4 // space, 128), low),
        dall=((4, 256, 128), low),
        bz=((64, 128), low),
        ty=((2, SHARE // 8, 128), low),
        ry=((2, SHARE // 8, 128), low),
        ky=((2, SHARE // 8, 128), wide),
        tz=((2, SHARE // 8, 128), low),
        rz=((2, space // 2, SHARE // 4 // space, 128), low),
        kz=((2, SHARE // 4 // space, 128), wide),
        az=((3, SHARE // 8, 128), low),
        gath=((2 * SHARE + 32, 128), low),
        bown=((32, 128), wide), bcore=((32, 128), wide), btwo=((32, 128), wide), bacross=((32, 128), wide),
        bfour=((32, 128), wide), ball=((space, 32, 128), wide), bsum=((32, 128), wide),
        flat=((3904, 128), wide),
        pair_a=((256, 128), wide),
        pair_b=((256, 128), wide),
        flow_tmp=((112, 128), wide),
        mm_tmp=((3 * (2 * EDGE + SPREAD), 128), wide),
        fo_tmp=((32, 128), wide),
        fo_tmp2=((32, 128), wide),
        w_ci=((CORR, 256), low),
        w_cm=((2304, 256), low),
        w_fi=((112, 128), low),
        w_fm=((1152, 128), low),
        w_mm=((2304, 128), low),
        w_ri=((1280, 384), low),
        w_rs=((640, 384), low),
        w_li=((1280, 384), low),
        w_ls=((640, 384), low),
        w_h=((1152, 512), low),
        w_fo=((32, 256), low),
        w_mo=((256, 640), low),
        bias=((BIAS_ROWS, 128), wide),
        gbias=((BIAS_ROWS, 128), wide),
        corr_up=((BATCH, 2, CORR, 128), low),
        corr_down=((BATCH, 2, CORR, 128), low),
        flow_up=((BATCH, 16, 128), wide),
        flow_down=((BATCH, 16, 128), wide),
        fs=((7, 32, 128), wide),
        xt=((BATCH, 112, 1152), low),
        tmp=((1168, 128), wide),
        tmp2=((32, 128), wide),
        hx_c=((BATCH, 1152, 768), low),
        hx_f=((BATCH, 1152, 384), low),
        hx_j=((BATCH, 896, 768), low),
        slope_ci=((BATCH, AREA, 256), low),
        slope_fi=((BATCH, AREA, 128), low),
        slope_j=((BATCH, 896, 256), low),
        slope_m=((BATCH, AREA, 128), low),
        motion=((BATCH, AREA, 128), wide),
        state=((BATCH, AREA, 128), wide),
        xi=((BATCH * AREA, 1280), low),
        xs=((BATCH * AREA, 640), low),
        xr=((BATCH * AREA, 640), low),
        ru=((BATCH, AREA, 128), wide),
        rr=((BATCH, AREA, 128), wide),
        rc=((BATCH, AREA, 128), wide),
        lr=((BATCH, AREA, 128), wide),
        a_state=(peers, low), a_context=(peers, low), a_motion=(peers, low),
        b_state=(peers, low), b_context=(peers, low), b_motion=(peers, low),
        xc=((BATCH, AREA + 64, 384), low),
        xcr=((BATCH, AREA + 64, 128), low),
        gc=((BATCH, AREA + 64, 384), low),
        final=((AREA, 128), wide),
        e_left=((BATCH, 2, 48, 128), low), e_right=((BATCH, 2, 48, 128), low),
        f_left=((BATCH, 2, 48, 128), low), f_right=((BATCH, 2, 48, 128), low),
        m_left=((BATCH, 2, 48, 128), low), m_right=((BATCH, 2, 48, 128), low),
        n_left=((BATCH, 2, 48, 128), low), n_right=((BATCH, 2, 48, 128), low),
        slope_h=((BATCH, SPREAD, 512), low),
        feat=((BATCH, SPAN, 256), low),
        mf=((BATCH, AREA, 256), low),
        dg=((BATCH, 8, SPAN), wide),
        target_wide=((BATCH, 8, SPAN), wide),
        valid_wide=((BATCH, 8, SPAN), wide),
        flow=((BATCH, 16, 128), wide),
        dg_left=((BATCH, 8, SPAN), wide), dg_right=((BATCH, 8, SPAN), wide),
        dt=((32, SPAN), wide),
        dto=((32, SPAN), wide),
        dtb=((BATCH, 32, SPAN), low),
        hgo=((BATCH, SPREAD, 512), low),
        gr=((BATCH, AREA, 384), low),
        mge=((BATCH, 1152, 128), low),
        cpg=((BATCH, AREA, 256), low),
        fpg=((BATCH, AREA, 128), low),
        gf_base=((BATCH, 8, AREA), wide),
        gf=((BATCH, 32, 128), wide), gf_up=((BATCH, 32, 128), wide), gf_down=((BATCH, 32, 128), wide),
        count_out=((8, 128), wide), counts=((space, 8, 128), wide),
        losses=((8, 128), wide), loss_in=((space, 8, 128), wide),
    )
    sems = dict(
        hsend=pltpu.SemaphoreType.DMA((7, 2)), hrecv=pltpu.SemaphoreType.DMA((7, 2)),
        asend=pltpu.SemaphoreType.DMA((9,)), arecv=pltpu.SemaphoreType.DMA((9,)),
        ssem=pltpu.SemaphoreType.DMA((2, 2)),
        fsem=pltpu.SemaphoreType.DMA((17,)),
        rsend=pltpu.SemaphoreType.DMA((3, 2)), rrecv=pltpu.SemaphoreType.DMA((3, 2)),
        z1send=pltpu.SemaphoreType.DMA((2,)), z1recv=pltpu.SemaphoreType.DMA((2,)),
        z2send=pltpu.SemaphoreType.DMA((3,)), z2recv=pltpu.SemaphoreType.DMA((3,)),
        osend=pltpu.SemaphoreType.DMA((3,)), orecv=pltpu.SemaphoreType.DMA((9,)),
        rlocal=pltpu.SemaphoreType.DMA((2,)),
        s2send=pltpu.SemaphoreType.DMA((2,)), s2recv=pltpu.SemaphoreType.DMA((2,)),
        fsend=pltpu.SemaphoreType.DMA((2,)), frecv=pltpu.SemaphoreType.DMA((9,)),
        ysend=pltpu.SemaphoreType.DMA((9,)), yrecv=pltpu.SemaphoreType.DMA((9,)),
        dsend=pltpu.SemaphoreType.DMA, drecv=pltpu.SemaphoreType.DMA,
        bsend=pltpu.SemaphoreType.DMA((2,)), brecv=pltpu.SemaphoreType.DMA((2,)),
        ksem=pltpu.SemaphoreType.DMA((2,)),
        gsend=pltpu.SemaphoreType.DMA((9, 8)), grecv=pltpu.SemaphoreType.DMA((9, 8)), lsem=pltpu.SemaphoreType.DMA,
        gsem=pltpu.SemaphoreType.DMA((ROWS,)),
        osem=pltpu.SemaphoreType.DMA((6,)),
    )
    vmem = pl.BlockSpec(memory_space=pltpu.VMEM)
    hbm = pl.BlockSpec(memory_space=pl.ANY)
    names = list(ins) + list(outs) + list(scratch) + list(sems)
    return pl.pallas_call(
        functools.partial(main_kernel, names, space, count),
        out_shape=[jax.ShapeDtypeStruct(*entry) for entry in outs.values()],
        in_specs=[hbm if name == "local" else vmem for name in ins],
        out_specs=[pl.BlockSpec(memory_space=pltpu.SMEM) if name == "out_loss" else hbm if name in ("out_flat", "out_gnet", "out_gctx", "out_gcorr", "out_keep_c", "out_keep_f", "out_mask", "out_grads", "out_all") else vmem for name in outs],
        scratch_shapes=[pltpu.VMEM(*entry) for entry in scratch.values()] + list(sems.values()),
        compiler_params=pltpu.CompilerParams(
            collective_id=2, has_side_effects=True, vmem_limit_bytes=VMEM_LIMIT
        ),
    )(*ins.values())


VMEM_LIMIT = 64 * 2**20 - 2**16


def shards_wide(net, context, corr, flow, target, valid, grad_net, grad_mask, params):
    space = lax.axis_size(SPACE)
    count = params.shape[0]
    local = jnp.pad(params, (0, BLOCK * LANES - count)).reshape(BLOCK, LANES)
    outs = main_call(
        space, count, local, net.reshape(BATCH, AREA, HID), context.reshape(BATCH, AREA, CTX),
        jnp.transpose(corr, (0, 1, 3, 2)), jnp.transpose(flow, (0, 2, 1, 3)), jnp.transpose(target, (0, 1, 3, 2)),
        jnp.transpose(valid, (0, 2, 1)),
        grad_net.reshape(BATCH, AREA, HID), grad_mask.reshape(BATCH, AREA, MASK),
    )
    new_net, new_flow, mask, loss, _, gnet, gctx, gcorr, gflow = outs[:9]
    new_flow = jnp.transpose(new_flow, (0, 1, 3, 2))
    grads = outs[-1].reshape(-1)[:count]
    return (
        new_net.reshape(BATCH, TALL, COLS, HID),
        new_flow,
        mask.reshape(BATCH, TALL, COLS, MASK),
        loss,
        grads,
        gnet.reshape(BATCH, ROWS, WIDE, HID),
        gctx.reshape(BATCH, ROWS, WIDE, CTX),
        jnp.transpose(gcorr, (0, 1, 3, 2)),
        jnp.transpose(gflow[:, 0 : 2 * ROWS].reshape(BATCH, ROWS, 2, WIDE), (0, 2, 1, 3)),
    )


def solution(mesh):
    def plan(*arrays):
        net, valid = arrays[0], arrays[5]
        if (net.shape[1:3], valid.shape[1:]) == ((ROWS, WIDE), (TALL, COLS)):
            return shards_wide(*arrays)
        return shards(*arrays)

    return jax.shard_map(
        plan,
        mesh=mesh,
        in_specs=(
            P(DP, SPACE, None, None),
            P(DP, SPACE, None, None),
            P(DP, SPACE, None, None),
            P(DP, None, SPACE, None),
            P(DP, None, None, SPACE),
            P(DP, None, SPACE),
            P(DP, None, SPACE, None),
            P(DP, None, SPACE, None),
            P(DP),
        ),
        out_specs=(
            P(DP, None, SPACE, None),
            P(DP, None, None, SPACE),
            P(DP, None, SPACE, None),
            P(DP),
            P(DP),
            P(DP, SPACE, None, None),
            P(DP, SPACE, None, None),
            P(DP, SPACE, None, None),
            P(DP, None, SPACE, None),
        ),
        check_vma=False,
    )
```

```python
import functools

import jax
import jax.numpy as jnp
from jax import lax
from jax.experimental import pallas as pl
from jax.experimental.pallas import tpu as pltpu
from jax.sharding import PartitionSpec as P

HID = 128
CTX = 128
MOT = 128
CORR = 324
SPACE = "space"
DP = "dp"
(
    CORR_IN,
    CORR_MIX,
    FLOW_IN,
    FLOW_MIX,
    MOTION_MIX,
    ROWS_GATES,
    ROWS_CANDIDATE,
    COLUMNS_GATES,
    COLUMNS_CANDIDATE,
    FLOW_HIDDEN,
    FLOW_OUT,
    MASK_HIDDEN,
    MASK_OUT,
) = range(13)
C1 = 256
C2 = 192
F1 = 128
F2 = 64
HEAD = 256
MASK = 576


def with_halo(block, sides, width):
    for axis, dim in sides:
        count = lax.axis_size(axis)
        forward = [(i, i + 1) for i in range(count - 1)]
        backward = [(target, source) for source, target in forward]
        low = lax.ppermute(
            lax.slice_in_dim(block, block.shape[dim] - width, None, axis=dim), axis, forward
        )
        high = lax.ppermute(lax.slice_in_dim(block, 0, width, axis=dim), axis, backward)
        block = jnp.concatenate([low, block, high], axis=dim)
    return block


def shapes():
    inputs_width = HID + CTX + MOT
    return [
        (CORR_IN, CORR, C1),
        (CORR_MIX, 9 * C1, C2),
        (FLOW_IN, 98, F1),
        (FLOW_MIX, 9 * F1, F2),
        (MOTION_MIX, 9 * (C2 + F2), MOT - 2),
        (ROWS_GATES, 5 * inputs_width, 2 * HID),
        (ROWS_CANDIDATE, 5 * inputs_width, HID),
        (COLUMNS_GATES, 5 * inputs_width, 2 * HID),
        (COLUMNS_CANDIDATE, 5 * inputs_width, HID),
        (FLOW_HIDDEN, 9 * HID, HEAD),
        (FLOW_OUT, 9 * HEAD, 2),
        (MASK_HIDDEN, 9 * HID, HEAD),
        (MASK_OUT, HEAD, MASK),
    ]


def unpack(flat):
    weights = {}
    biases = {}
    offset = 0
    table = shapes()
    for name, height, width in table:
        weights[name] = flat[offset // LANES : (offset + height * width) // LANES].reshape(height, width)
        offset = offset + height * width
    rest = flat[offset // LANES :].reshape(-1)
    offset = 0
    for name, height, width in table:
        biases[name] = rest[offset : offset + width].astype(jnp.float32)
        offset = offset + width
    return (weights, biases)


def pack(grads, total):
    table = shapes()
    rows = [grads[entry[0]][0].astype(jnp.bfloat16).reshape(-1, LANES) for entry in table]
    biases = jnp.concatenate([grads[entry[0]][1] for entry in table]).astype(jnp.bfloat16)
    left = total * LANES - sum(entry[1] * entry[2] for entry in table) - biases.shape[0]
    return jnp.concatenate(rows + [jnp.pad(biases, (0, left)).reshape(-1, LANES)])


def patches(padded, tall, wide):
    out_rows = padded.shape[1] - tall + 1
    out_columns = padded.shape[2] - wide + 1
    return jnp.concatenate(
        [
            padded[:, down : down + out_rows, across : across + out_columns]
            for down in range(tall)
            for across in range(wide)
        ],
        axis=-1,
    )


def apply(stacked, weight):
    return jnp.einsum("bhwk,ko->bhwo", stacked, weight, preferred_element_type=jnp.float32)


def apply_back(grad, weight):
    return jnp.einsum("bhwo,ko->bhwk", grad, weight, preferred_element_type=jnp.float32)


def weight_grad(stacked, pre_grad):
    return jnp.einsum("bhwk,bhwo->ko", stacked, pre_grad, preferred_element_type=jnp.float32)


def record(grads, name, stacked, pre_grad):
    grads[name] = (
        weight_grad(stacked, pre_grad),
        jnp.sum(pre_grad, axis=(0, 1, 2), dtype=jnp.float32),
    )


def flipped(weight, tall, wide):
    inner = weight.shape[0] // (tall * wide)
    shaped = weight.reshape(tall, wide, inner, weight.shape[1])[::-1, ::-1]
    return jnp.transpose(shaped, (0, 1, 3, 2)).reshape(-1, inner)


def slope(pre):
    sigma = jax.nn.sigmoid(pre)
    return sigma * (1.0 + pre * (1.0 - sigma))


def local_pad(field, tall, wide):
    return jnp.pad(field, ((0, 0), (tall // 2, tall // 2), (wide // 2, wide // 2), (0, 0)))


def row_pad(field, tall):
    field = with_halo(field, ((SPACE, 1),), tall // 2)
    return jnp.pad(field, ((0, 0), (0, 0), (tall // 2, tall // 2), (0, 0)))


def column_pad(field, tall, wide):
    field = with_halo(field, ((SPACE, 2),), wide // 2)
    return jnp.pad(field, ((0, 0), (tall // 2, tall // 2), (0, 0), (0, 0)))


MESH = pl.DeviceIdType.MESH
LANES = 128
BLOCK = 6144


def quarter_start(rank, count):
    return lax.div(rank * count, LANES)


def quarter_base(rank, count):
    return lax.div(rank * count, LANES * 16) * 16


def mate_of(rank):
    return rank + 1 - 2 * lax.rem(rank, 2)


def remote(src, dst, send, recv, device):
    return pltpu.make_async_remote_copy(
        src_ref=src, dst_ref=dst, send_sem=send, recv_sem=recv, device_id=device, device_id_type=MESH
    )


def greet(devices):
    barrier = pltpu.get_barrier_semaphore()
    for device in devices:
        pl.semaphore_signal(barrier, inc=1, device_id=device, device_id_type=MESH)
    pl.semaphore_wait(barrier, len(devices))


def lane_matrix(shift, forward):
    source = lax.broadcasted_iota(jnp.int32, (LANES, 2 * LANES), 0)
    target = lax.broadcasted_iota(jnp.int32, (LANES, 2 * LANES), 1)
    if forward:
        return jnp.where(target == source + shift, 1.0, 0.0).astype(jnp.bfloat16)
    return jnp.where(lax.rem(target + LANES, 2 * LANES) == source - shift + LANES, 1.0, 0.0).astype(jnp.bfloat16)


def gather_kernel(count, local_ref, out_ref, own_ref, send, recv):
    rank, spot = lax.axis_index(DP), lax.axis_index(SPACE)
    mate, across, twin = mate_of(rank), lax.rem(rank + 2, 4), mate_of(spot)
    pieces = 4
    rows = BLOCK // 2 // pieces
    peers = ({DP: mate}, {DP: across}, {SPACE: twin})
    greet(peers)
    matrix = lane_matrix(lax.rem(rank * count, LANES), True)
    first = lax.broadcasted_iota(jnp.int32, (256, LANES), 0) == 0

    def rotate(step, carry):
        at = pl.ds(pl.multiple_of(step * 256, 256), 256)
        both = jnp.dot(local_ref[at, :], matrix, preferred_element_type=jnp.float32)
        spill = pltpu.roll(both[:, LANES:], 1, 0)
        own_ref[at, :] = (both[:, :LANES] + jnp.where(first, carry, spill)).astype(jnp.bfloat16)
        return spill[0:1]

    lax.fori_loop(0, BLOCK // 256, rotate, jnp.zeros((1, LANES), jnp.float32))

    half, other_half = lax.rem(spot, 2), lax.rem(spot + 1, 2)

    def piece(which, index):
        return pl.ds(pl.multiple_of(which * (BLOCK // 2) + index * rows, 16), rows)

    own_x = [
        remote(own_ref.at[piece(half, k)], out_ref.at[rank, piece(half, k)], send.at[0, k], recv.at[0, k], peers[1])
        for k in range(pieces)
    ]
    own_c = remote(own_ref, out_ref.at[rank], send.at[4, 0], recv.at[4, 0], peers[0])
    for copy in own_x:
        copy.start()
    own_c.start()
    later = []
    for k in range(pieces):
        own_x[k].wait_recv()
        block = out_ref.at[across, piece(half, k)]
        to_twin = remote(block, block, send.at[1, k], recv.at[1, k], peers[2])
        to_mate = remote(block, block, send.at[2, k], recv.at[2, k], peers[0])
        to_twin.start()
        to_mate.start()
        later.append((to_twin, to_mate))
    for at in range(BLOCK // 256):
        out_ref[rank, at * 256 : (at + 1) * 256, :] = own_ref[at * 256 : (at + 1) * 256, :]
    for k in range(pieces):
        later[k][0].wait_recv()
        block = out_ref.at[across, piece(other_half, k)]
        to_mate = remote(block, block, send.at[3, k], recv.at[3, k], peers[0])
        to_mate.start()
        later.append((to_mate,))
    for k in range(pieces):
        own_x[k].wait_send()
        later[k][0].wait_send()
        later[k][1].wait()
        later[pieces + k][0].wait()
    own_c.wait()


def gather_blocks(params):
    count = params.shape[0]
    local = jnp.pad(params, (0, BLOCK * LANES - count)).reshape(BLOCK, LANES)
    return pl.pallas_call(
        functools.partial(gather_kernel, count),
        out_shape=jax.ShapeDtypeStruct((4, BLOCK, LANES), jnp.bfloat16),
        in_specs=[pl.BlockSpec(memory_space=pltpu.VMEM)],
        out_specs=pl.BlockSpec(memory_space=pltpu.VMEM),
        scratch_shapes=[
            pltpu.VMEM((BLOCK, LANES), jnp.bfloat16),
            pltpu.SemaphoreType.DMA((5, 4)),
            pltpu.SemaphoreType.DMA((5, 4)),
        ],
        compiler_params=pltpu.CompilerParams(
            collective_id=0, has_side_effects=True, vmem_limit_bytes=32 * 2**20
        ),
    )(local)


def gather_params(params):
    count = params.shape[0]
    blocks = gather_blocks(params)
    pieces = []
    reach = 0
    for rank in range(4):
        start = rank * count // LANES
        stop = -(-(rank + 1) * count // LANES)
        head = blocks[rank, :1] if rank == 0 else blocks[rank, :1] + pieces.pop()
        pieces += [head, blocks[rank, 1 : stop - start - 1], blocks[rank, stop - start - 1 : stop - start]]
    return jnp.concatenate(pieces)


def reduce_kernel(count, space, pieces, grads_ref, out_ref, rc, tx, rx, acc, ty, ry, tz, rz, gath, send, recv, zsend, zrecv):
    rank, spot = lax.axis_index(DP), lax.axis_index(SPACE)
    mate, across, twin = mate_of(rank), lax.rem(rank + 2, 4), mate_of(spot)
    group = space // 2
    side, depth = lax.rem(spot, 2), lax.div(spot, 2)
    rows = BLOCK // pieces
    half = rows // 2
    part = half // group

    def partner(step):
        return lax.rem(depth + step, group)

    peers = [{DP: mate}, {DP: across}, {SPACE: twin}]
    barrier = pltpu.get_barrier_semaphore()
    for device in peers:
        pl.semaphore_signal(barrier, inc=1, device_id=device, device_id_type=MESH)

    def hello(step, carry):
        pl.semaphore_signal(barrier, inc=1, device_id={SPACE: partner(step) * 2 + side}, device_id_type=MESH)
        return carry

    lax.fori_loop(1, group, hello, 0)
    pl.semaphore_wait(barrier, 3 + group - 1)

    gath[BLOCK:, :] = jnp.zeros((32, LANES), jnp.bfloat16)
    lower = lax.rem(rank, 2)
    upper = lax.div(rank, 2)

    def base(who):
        return pl.multiple_of(quarter_base(who, count), 16)

    def rows_of(start, index, length):
        return pl.ds(pl.multiple_of(start + index, 16), length)

    core = []
    for p in range(pieces):
        for high in range(2):
            copy = remote(
                grads_ref.at[rows_of(base(2 * high + 1 - lower), p * rows, rows)],
                rc.at[p, high],
                send.at[high, p],
                recv.at[high, p],
                peers[0],
            )
            copy.start()
            core.append(copy)
    step_rows = 192 if half % 192 == 0 else 16
    xs, ys, gs = [], [], []

    def z_copy(p, step):
        to = partner(step)
        return remote(
            tz.at[p, pl.ds(pl.multiple_of(to * part, 16), part)],
            rz.at[p, pl.ds(pl.multiple_of(depth * part, 16), part)],
            zsend.at[0, p, step],
            zrecv.at[0, p, step],
            {SPACE: to * 2 + side},
        )

    def home(p, which, slot):
        return pl.ds(pl.multiple_of(p * rows + which * half + slot * part, 16), part)

    def g_copy(p, step):
        block = gath.at[home(p, side, depth)]
        return remote(block, block, zsend.at[1, p, step], zrecv.at[1, p, step], {SPACE: partner(step) * 2 + side})

    def each(body):
        def run(step, carry):
            body(step)
            return carry

        lax.fori_loop(1, group, run, 0)

    def stage_core(p):
        core[2 * p].wait_recv()
        core[2 * p + 1].wait_recv()
        far = 1 - upper

        def add(step, carry):
            at = pl.multiple_of(step * step_rows, 16)
            mine = grads_ref[rows_of(base(2 * far + lower), p * rows + at, step_rows), :].astype(jnp.float32)
            tx[p, pl.ds(at, step_rows), :] = (
                mine + rc[p, far, pl.ds(at, step_rows), :].astype(jnp.float32)
            ).astype(jnp.bfloat16)
            return carry

        lax.fori_loop(0, rows // step_rows, add, 0)
        copy = remote(tx.at[p], rx.at[p], send.at[2, p], recv.at[2, p], peers[1])
        copy.start()
        xs.append(copy)

    def stage_x(p):
        xs[p].wait_recv()

        def total(at):
            return (
                grads_ref[rows_of(base(rank), p * rows + at, step_rows), :].astype(jnp.float32)
                + rc[p, upper, pl.ds(at, step_rows), :].astype(jnp.float32)
                + rx[p, pl.ds(at, step_rows), :].astype(jnp.float32)
            )

        def add(step, carry):
            at = pl.multiple_of(step * step_rows, 16)
            far = pl.multiple_of((1 - side) * half + at, 16)
            near = pl.multiple_of(side * half + at, 16)
            ty[p, pl.ds(at, step_rows), :] = total(far).astype(jnp.bfloat16)
            acc[p, pl.ds(at, step_rows), :] = total(near)
            return carry

        lax.fori_loop(0, half // step_rows, add, 0)
        copy = remote(ty.at[p], ry.at[p], send.at[3, p], recv.at[3, p], peers[2])
        copy.start()
        ys.append(copy)

    def stage_y(p):
        ys[p].wait_recv()

        def add(step, carry):
            at = pl.ds(pl.multiple_of(step * step_rows, 16), step_rows)
            value = acc[p, at, :] + ry[p, at, :].astype(jnp.float32)
            acc[p, at, :] = value
            tz[p, at, :] = value.astype(jnp.bfloat16)
            return carry

        lax.fori_loop(0, half // step_rows, add, 0)
        each(lambda step: z_copy(p, step).start())

    def stage_z(p):
        each(lambda step: z_copy(p, step).wait_recv())
        value = acc[p, pl.ds(pl.multiple_of(depth * part, 16), part), :]

        def add(step, value):
            other = lax.rem(depth + group - step, group)
            return value + rz[p, pl.ds(pl.multiple_of(other * part, 16), part), :].astype(jnp.float32)

        value = lax.fori_loop(1, group, add, value)
        gath[home(p, side, depth), :] = value.astype(jnp.bfloat16)
        each(lambda step: g_copy(p, step).start())

    def stage_zg(p):
        each(lambda step: g_copy(p, step).wait_recv())
        block = gath.at[pl.ds(pl.multiple_of(p * rows + side * half, 16), half)]
        copy = remote(block, block, send.at[4, p], recv.at[4, p], peers[2])
        copy.start()
        gs.append(copy)

    def stage_yg(p):
        gs[p].wait_recv()

    stages = [stage_core, stage_x, stage_y, stage_z, stage_zg, stage_yg]
    for tick in range(pieces + len(stages) - 1):
        for number in reversed(range(len(stages))):
            if 0 <= tick - number < pieces:
                stages[number](tick - number)

    for copy in core + xs + ys + gs:
        copy.wait_send()
    for p in range(pieces):

        def done(step):
            z_copy(p, step).wait_send()
            g_copy(p, step).wait_send()

        each(done)

    offset = rank * count - quarter_base(rank, count) * LANES
    skip = lax.div(offset, LANES)
    matrix = lane_matrix(lax.rem(offset, LANES), False)
    wide = jnp.where(
        lax.broadcasted_iota(jnp.int32, (256, 288), 1)
        == lax.broadcasted_iota(jnp.int32, (256, 288), 0) + skip,
        1.0,
        0.0,
    ).astype(jnp.bfloat16)
    wide_next = jnp.where(
        lax.broadcasted_iota(jnp.int32, (256, 288), 1)
        == lax.broadcasted_iota(jnp.int32, (256, 288), 0) + skip + 1,
        1.0,
        0.0,
    ).astype(jnp.bfloat16)

    def place(step, carry):
        at = pl.multiple_of(step * 256, 256)
        block = gath[pl.ds(at, 288), :]
        both = jnp.dot(block, matrix, preferred_element_type=jnp.float32).astype(jnp.bfloat16)
        out_ref[pl.ds(at, 256), :] = jnp.dot(wide, both[:, :LANES], preferred_element_type=jnp.float32) + jnp.dot(
            wide_next, both[:, LANES:], preferred_element_type=jnp.float32
        )
        return carry

    lax.fori_loop(0, BLOCK // 256, place, 0)


def reduce_grads(flat, space, count):
    pieces = next(k for k in (4, 2, 1) if BLOCK // (k * space) % 16 == 0)
    rows = BLOCK // pieces
    half = rows // 2
    out = pl.pallas_call(
        functools.partial(reduce_kernel, count, space, pieces),
        out_shape=jax.ShapeDtypeStruct((BLOCK, LANES), jnp.float32),
        in_specs=[pl.BlockSpec(memory_space=pltpu.VMEM)],
        out_specs=pl.BlockSpec(memory_space=pltpu.VMEM),
        scratch_shapes=[
            pltpu.VMEM((pieces, 2, rows, LANES), jnp.bfloat16),
            pltpu.VMEM((pieces, rows, LANES), jnp.bfloat16),
            pltpu.VMEM((pieces, rows, LANES), jnp.bfloat16),
            pltpu.VMEM((pieces, half, LANES), jnp.float32),
            pltpu.VMEM((pieces, half, LANES), jnp.bfloat16),
            pltpu.VMEM((pieces, half, LANES), jnp.bfloat16),
            pltpu.VMEM((pieces, half, LANES), jnp.bfloat16),
            pltpu.VMEM((pieces, half, LANES), jnp.bfloat16),
            pltpu.VMEM((BLOCK + 32, LANES), jnp.bfloat16),
            pltpu.SemaphoreType.DMA((5, pieces)),
            pltpu.SemaphoreType.DMA((5, pieces)),
            pltpu.SemaphoreType.DMA((2, pieces, space // 2)),
            pltpu.SemaphoreType.DMA((2, pieces, space // 2)),
        ],
        compiler_params=pltpu.CompilerParams(
            collective_id=1, has_side_effects=True, vmem_limit_bytes=48 * 2**20
        ),
    )(flat)
    return out.reshape(-1)[:count]


def gru_forward(state, inputs, weights, biases, gate_name, candidate_name, tall, wide, padder):
    joined_stack = patches(padder(jnp.concatenate([state, inputs], -1), tall, wide), tall, wide)
    gates = jax.nn.sigmoid(apply(joined_stack, weights[gate_name]) + biases[gate_name])
    hidden = state.shape[-1]
    update = gates[..., :hidden]
    reset = gates[..., hidden:]
    state_wide = state.astype(jnp.float32)
    mixed = jnp.concatenate([(reset * state_wide).astype(jnp.bfloat16), inputs], -1)
    mixed_stack = patches(padder(mixed, tall, wide), tall, wide)
    candidate = jnp.tanh(apply(mixed_stack, weights[candidate_name]) + biases[candidate_name])
    result = state_wide + update * (candidate - state_wide)
    return (result, (joined_stack, mixed_stack, update, reset, candidate, state_wide))


def gru_backward(result_grad, kept, weights, grads, gate_name, candidate_name, tall, wide, padder):
    joined_stack, mixed_stack, update, reset, candidate, state_wide = kept
    hidden = update.shape[-1]
    candidate_grad = (result_grad * update * (1.0 - candidate * candidate)).astype(jnp.bfloat16)
    record(grads, candidate_name, mixed_stack, candidate_grad)
    mixed_grad = apply(
        patches(padder(candidate_grad, tall, wide), tall, wide),
        flipped(weights[candidate_name], tall, wide),
    )
    reset_grad = mixed_grad[..., :hidden]
    gate_grad = jnp.concatenate(
        [
            result_grad * (candidate - state_wide) * update * (1.0 - update),
            reset_grad * state_wide * reset * (1.0 - reset),
        ],
        -1,
    ).astype(jnp.bfloat16)
    record(grads, gate_name, joined_stack, gate_grad)
    joined_grad = apply(
        patches(padder(gate_grad, tall, wide), tall, wide), flipped(weights[gate_name], tall, wide)
    )
    state_grad = result_grad * (1.0 - update) + reset_grad * reset + joined_grad[..., :hidden]
    inputs_grad = joined_grad[..., hidden:] + mixed_grad[..., hidden:]
    return (state_grad, inputs_grad)


def shards(net, context, corr, flow, target, valid, grad_net, grad_mask, params):
    flow_start = CTX + MOT - 2
    plane = jnp.float32(target.shape[2] * net.shape[2])
    counts = lax.psum(jnp.sum(valid, axis=(1, 2)).astype(jnp.float32), SPACE)
    divisor = jnp.maximum(counts, 1.0)
    weights, biases = unpack(gather_params(params))
    grads = {}
    flow_rows = jnp.transpose(flow, (0, 2, 3, 1))
    corr_pre = apply(corr, weights[CORR_IN]) + biases[CORR_IN]
    corr_one = jax.nn.silu(corr_pre).astype(jnp.bfloat16)
    corr_stack = patches(row_pad(corr_one, 3), 3, 3)
    corr_mix_pre = apply(corr_stack, weights[CORR_MIX]) + biases[CORR_MIX]
    corr_two = jax.nn.silu(corr_mix_pre).astype(jnp.bfloat16)
    flow_stack = patches(row_pad(flow_rows, 7), 7, 7)
    flow_pre = apply(flow_stack, weights[FLOW_IN]) + biases[FLOW_IN]
    flow_one = jax.nn.silu(flow_pre).astype(jnp.bfloat16)
    flow_mix_stack = patches(row_pad(flow_one, 3), 3, 3)
    flow_mix_pre = apply(flow_mix_stack, weights[FLOW_MIX]) + biases[FLOW_MIX]
    flow_two = jax.nn.silu(flow_mix_pre).astype(jnp.bfloat16)
    joint_stack = patches(row_pad(jnp.concatenate([corr_two, flow_two], -1), 3), 3, 3)
    motion_pre = apply(joint_stack, weights[MOTION_MIX]) + biases[MOTION_MIX]
    motion = jax.nn.silu(motion_pre).astype(jnp.bfloat16)
    inputs = jnp.concatenate([context, motion, flow_rows], -1)
    state, rows_kept = gru_forward(
        net, inputs, weights, biases, ROWS_GATES, ROWS_CANDIDATE, 1, 5, local_pad
    )
    state_columns, inputs_columns = (
        lax.all_to_all(
            state.astype(jnp.bfloat16), SPACE, split_axis=2, concat_axis=1, tiled=True
        ),
        lax.all_to_all(inputs, SPACE, split_axis=2, concat_axis=1, tiled=True),
    )
    target_here = jnp.transpose(target, (0, 2, 3, 1))
    valid_here = valid.astype(jnp.float32)
    net_cotangent = grad_net
    mask_cotangent = grad_mask
    final, columns_kept = gru_forward(
        state_columns,
        inputs_columns,
        weights,
        biases,
        COLUMNS_GATES,
        COLUMNS_CANDIDATE,
        5,
        1,
        local_pad,
    )
    final_low = final.astype(jnp.bfloat16)
    heads_weight = jnp.concatenate([weights[FLOW_HIDDEN], weights[MASK_HIDDEN]], 1)
    heads_bias = jnp.concatenate([biases[FLOW_HIDDEN], biases[MASK_HIDDEN]])
    net_stack = patches(column_pad(final_low, 3, 3), 3, 3)
    heads_pre = apply(net_stack, heads_weight) + heads_bias
    heads_act = jax.nn.silu(heads_pre).astype(jnp.bfloat16)
    flow_features = heads_act[..., :HEAD]
    mask_features = heads_act[..., HEAD:]
    hidden_stack = patches(column_pad(flow_features, 3, 3), 3, 3)
    delta = apply(hidden_stack, weights[FLOW_OUT]) + biases[FLOW_OUT]
    mask_full = 0.25 * (apply(mask_features, weights[MASK_OUT]) + biases[MASK_OUT])
    new_flow = inputs_columns[..., flow_start:].astype(jnp.float32) + delta
    error = new_flow - target_here
    root = jnp.sqrt(error * error + 1.0)
    partials = jnp.sum(valid_here * jnp.sum(root, axis=-1), axis=(1, 2))
    flow_grad = plane / divisor[:, None, None, None] * valid_here[..., None] * error / root
    mask_low = mask_full.astype(jnp.bfloat16)
    nets_out = final_low
    flows_out = jnp.transpose(new_flow, (0, 3, 1, 2))
    masks_out = mask_low
    delta_grad = flow_grad.astype(jnp.bfloat16)
    mask_grad = (0.25 * mask_cotangent.astype(jnp.float32)).astype(jnp.bfloat16)
    record(grads, MASK_OUT, mask_features, mask_grad)
    record(grads, FLOW_OUT, hidden_stack, delta_grad)
    from_flow = apply(
        patches(column_pad(delta_grad, 3, 3), 3, 3), flipped(weights[FLOW_OUT], 3, 3)
    )
    from_mask = apply_back(mask_grad, weights[MASK_OUT])
    heads_grad = (jnp.concatenate([from_flow, from_mask], -1) * slope(heads_pre)).astype(
        jnp.bfloat16
    )
    heads_wgrad = weight_grad(net_stack, heads_grad)
    heads_bgrad = jnp.sum(heads_grad, axis=(0, 1, 2), dtype=jnp.float32)
    grads[FLOW_HIDDEN] = (heads_wgrad[:, :HEAD], heads_bgrad[:HEAD])
    grads[MASK_HIDDEN] = (heads_wgrad[:, HEAD:], heads_bgrad[HEAD:])
    final_grad = net_cotangent.astype(jnp.float32) + apply(
        patches(column_pad(heads_grad, 3, 3), 3, 3), flipped(heads_weight, 3, 3)
    )
    state_grad_columns, inputs_grad_columns = gru_backward(
        final_grad,
        columns_kept,
        weights,
        grads,
        COLUMNS_GATES,
        COLUMNS_CANDIDATE,
        5,
        1,
        local_pad,
    )
    inputs_grad_columns = jnp.concatenate(
        [
            inputs_grad_columns[..., :flow_start],
            inputs_grad_columns[..., flow_start:] + flow_grad,
        ],
        -1,
    )
    state_back, inputs_back = (
        lax.all_to_all(
            state_grad_columns.astype(jnp.bfloat16),
            SPACE,
            split_axis=1,
            concat_axis=2,
            tiled=True,
        ),
        lax.all_to_all(
            inputs_grad_columns.astype(jnp.bfloat16),
            SPACE,
            split_axis=1,
            concat_axis=2,
            tiled=True,
        ),
    )
    net_grad, inputs_grad = gru_backward(
        state_back.astype(jnp.float32),
        rows_kept,
        weights,
        grads,
        ROWS_GATES,
        ROWS_CANDIDATE,
        1,
        5,
        local_pad,
    )
    inputs_total = inputs_grad + inputs_back.astype(jnp.float32)
    motion_grad = (inputs_total[..., CTX:flow_start] * slope(motion_pre)).astype(jnp.bfloat16)
    record(grads, MOTION_MIX, joint_stack, motion_grad)
    joint_grad = apply(
        patches(row_pad(motion_grad, 3), 3, 3), flipped(weights[MOTION_MIX], 3, 3)
    )
    branch_grad = jnp.concatenate(
        [
            joint_grad[..., :C2] * slope(corr_mix_pre),
            joint_grad[..., C2:] * slope(flow_mix_pre),
        ],
        -1,
    ).astype(jnp.bfloat16)
    record(grads, CORR_MIX, corr_stack, branch_grad[..., :C2])
    record(grads, FLOW_MIX, flow_mix_stack, branch_grad[..., C2:])
    branch_pad = row_pad(branch_grad, 3)
    corr_one_grad = apply(
        patches(branch_pad[..., :C2], 3, 3), flipped(weights[CORR_MIX], 3, 3)
    )
    flow_one_grad = apply(
        patches(branch_pad[..., C2:], 3, 3), flipped(weights[FLOW_MIX], 3, 3)
    )
    corr_pre_grad = (corr_one_grad * slope(corr_pre)).astype(jnp.bfloat16)
    flow_pre_grad = (flow_one_grad * slope(flow_pre)).astype(jnp.bfloat16)
    record(grads, CORR_IN, corr, corr_pre_grad)
    record(grads, FLOW_IN, flow_stack, flow_pre_grad)
    corr_grads = apply_back(corr_pre_grad, weights[CORR_IN])
    flow_total = inputs_total[..., flow_start:] + apply(
        patches(row_pad(flow_pre_grad, 7), 7, 7), flipped(weights[FLOW_IN], 7, 7)
    )
    flow_grads = jnp.transpose(flow_total, (0, 3, 1, 2))
    net_grads = net_grad
    context_grads = inputs_total[..., :CTX]
    count = params.shape[0]
    local = pack(grads, 3 * count // (LANES * 16) * 16 + BLOCK)
    collected = reduce_grads(local, lax.axis_size(SPACE), count)
    losses = lax.psum(partials, SPACE) / divisor
    return (
        nets_out,
        flows_out,
        masks_out,
        losses,
        collected,
        net_grads,
        context_grads,
        corr_grads,
        flow_grads,
    )


BATCH = 2
ROWS = 5
WIDE = 128
TALL = 40
COLS = 16
AREA = 640
PITCH = 20
SPREAD = TALL * PITCH
SPAN = 896
EDGE = 64


def mm(a, b):
    return jnp.dot(a, b, preferred_element_type=jnp.float32)


def nt(a, b):
    return lax.dot_general(a, b, (((1,), (1,)), ((), ())), preferred_element_type=jnp.float32)


def tn(a, b):
    return lax.dot_general(a, b, (((0,), (0,)), ((), ())), preferred_element_type=jnp.float32)


def half_of(value):
    return value.astype(jnp.bfloat16)


def full_of(value):
    return value.astype(jnp.float32)


def join(parts, axis=1):
    return jnp.concatenate(list(parts), axis=axis)


def quarter_of(value):
    return half_of(0.25 * full_of(value))


def lane_index(shape):
    return lax.broadcasted_iota(jnp.int32, shape, 1)


def row_index(shape):
    return lax.broadcasted_iota(jnp.int32, shape, 0)


def act_slope(pre):
    sigma = jax.nn.sigmoid(pre)
    act = pre * sigma
    return act, sigma + act * (1.0 - sigma)


def flat_rows():
    table = shapes()
    offset = 0
    starts = {}
    for name, height, width in table:
        starts[name] = offset // LANES
        offset += height * width
    bias_row = offset // LANES
    spots = {}
    inner = 0
    for name, height, width in table:
        spots[name] = inner
        inner += width
    return starts, bias_row, spots, inner


def cast_rows(dst, to, src, start, count, kind):
    big = 256
    whole = count // big

    if whole > 1:

        def body(step, carry):
            at = pl.multiple_of(step * big, big)
            dst[pl.ds(to + at, big), :] = src[pl.ds(start + at, big), :].astype(kind)
            return carry

        lax.fori_loop(0, whole, body, 0)
    elif whole == 1:
        dst[to : to + big, :] = src[start : start + big, :].astype(kind)
    rest = count - whole * big
    if rest:
        low = whole * big
        dst[to + low : to + count, :] = src[start + low : start + count, :].astype(kind)


MARGIN = 16


def stage_plan(count, start, rows):
    stop = start + rows
    pieces, fill = [], 0
    for rank in range(4):
        first = rank * count // LANES
        last = -(-(rank + 1) * count // LANES)
        low, high = max(start, first), min(stop, last)
        if low >= high:
            continue
        place = low - first + rank * BLOCK
        base = place // 16 * 16
        length = -(-(place - base + high - low) // 16) * 16
        to = MARGIN + low - start - (place - base)
        seam = MARGIN + low - start if start < first else None
        pieces.append((base, length, fill, to, seam))
        fill += length
    return pieces


class Stages:
    def __init__(self, v, count, segments):
        self.v, self.at, self.hold = v, 0, (4,)
        self.plans = [stage_plan(count, start, rows) for start, rows in segments]
        self.fetch(0)

    def copies(self, index):
        v, slot = self.v, index % 2
        return [
            pltpu.make_async_copy(
                v.out_all.at[base : base + length], v.stage.at[slot, fill : fill + length], v.ssem.at[slot, number]
            )
            for number, (base, length, fill, to, seam) in enumerate(self.plans[index])
        ]

    def fetch(self, index):
        if index < len(self.plans):
            for copy in self.copies(index):
                copy.start()

    def take(self):
        v, index = self.v, self.at
        self.at += 1
        for copy in self.copies(index):
            copy.wait()
        if index + 1 not in self.hold:
            self.fetch(index + 1)
        for base, length, fill, to, seam in self.plans[index]:
            saved = None if seam is None else v.flat[seam : seam + 1, :]
            cast_rows(v.flat, to, v.stage.at[index % 2], fill, length, jnp.float32)
            if seam is not None:
                v.flat[seam : seam + 1, :] = v.flat[seam : seam + 1, :] + saved


def strided(ref, start, count, stride):
    if stride == 1:
        return ref[pl.ds(start, count), :]
    return ref[pl.ds(start, count, stride=stride), :]


def unpack_pairs(flat, row, count, dst, to, lane):
    dst[to : to + count, lane : lane + LANES] = half_of(strided(flat, MARGIN + 2 * row, count, 2))
    dst[to : to + count, lane + LANES : lane + 2 * LANES] = half_of(strided(flat, MARGIN + 2 * row + 1, count, 2))


def pack_pairs(flat, row, count, low, high):
    flat[pl.ds(MARGIN + 2 * row, count, stride=2), :] = low
    flat[pl.ds(MARGIN + 2 * row + 1, count, stride=2), :] = high


def split_pick(which, quarter):
    source = lax.broadcasted_iota(jnp.int32, (LANES, HEAD), 0)
    target = lax.broadcasted_iota(jnp.int32, (LANES, HEAD), 1)
    return jnp.where(source == 2 * (target - 64 * quarter) + which, 1.0, 0.0).astype(jnp.bfloat16)


UNPACK = (
    (CORR_IN, 648), (CORR_MIX, 3456), (FLOW_IN, 98), (FLOW_MIX, 576), (MOTION_MIX, 2268),
    (ROWS_GATES, 3840), (ROWS_CANDIDATE, 1920), (COLUMNS_GATES, 3840), (COLUMNS_CANDIDATE, 1920),
    (FLOW_HIDDEN, 2304), (MASK_HIDDEN, 2304), (FLOW_OUT, 36), (MASK_OUT, 1152),
)


def stage_of(v, name, rows):
    assert UNPACK[v.stages.at] == (name, rows)
    v.stages.take()


def unpack_gru(v, gates_name, cand_name, w_i, w_s):
    flat = v.flat
    stage_of(v, gates_name, 3840)
    for tap in range(5):
        unpack_pairs(flat, tap * 384, 128, w_s, tap * 128, 0)
        unpack_pairs(flat, tap * 384 + 128, 256, w_i, tap * 256, 0)
    stage_of(v, cand_name, 1920)
    for tap in range(5):
        w_s[tap * 128 : (tap + 1) * 128, 256:384] = half_of(strided(flat, MARGIN + tap * 384, 128, 1))
        w_i[tap * 256 : (tap + 1) * 256, 256:384] = half_of(strided(flat, MARGIN + tap * 384 + 128, 256, 1))


def unpack_encoder(v, count):
    starts, bias_row, spots, inner = flat_rows()
    flat = v.flat
    v.stages = Stages(v, count, [(starts[name], rows) for name, rows in UNPACK])

    def stage(name, rows):
        stage_of(v, name, rows)

    @pl.when(v.rank != 3)
    def _():
        drain_bytes(v.bz, v.grecv.at[0, 4])

    flat[0:64, :] = full_of(v.bz[...])
    start = bias_row - 3 * count // LANES - BIAS_LOW
    place = 0
    lane1 = lane_index((1, LANES))
    for name, height, width in shapes():
        spot = spots[name]
        for block in range(-(-width // LANES)):
            at = spot + block * LANES
            row, shift = at // LANES, at % LANES
            value = flat[start + row : start + row + 1, :]
            if shift:
                after = flat[start + row + 1 : start + row + 2, :]
                value = jnp.where(
                    lane1 < LANES - shift, pltpu.roll(value, LANES - shift, 1), pltpu.roll(after, LANES - shift, 1)
                )
            left = width - block * LANES
            if left < LANES:
                value = jnp.where(lane1 < left, value, 0.0)
            if name == FLOW_MIX:
                value = pltpu.roll(value, 64, 1)
            v.bias[place : place + 1, :] = value
            place += 1

    stage(CORR_IN, 648)
    unpack_pairs(flat, 0, 324, v.w_ci, 0, 0)

    stage(CORR_MIX, 3456)
    lane = lane_index((128, LANES))
    low_half = lane < 64

    def mix_step(step, carry):
        at = MARGIN + 384 * step
        r0, r1, r2 = (strided(flat, at + i, 128, 3) for i in range(3))
        r1s, r2s = pltpu.roll(r1, 64, 1), pltpu.roll(r2, 64, 1)
        v.pair_a[pl.ds(0, 128, stride=2), :] = r0
        v.pair_a[pl.ds(1, 128, stride=2), :] = jnp.where(low_half, r1s, r2s)
        v.pair_b[pl.ds(0, 128, stride=2), :] = jnp.where(low_half, r1, 0.0)
        v.pair_b[pl.ds(1, 128, stride=2), :] = jnp.where(low_half, r2s, 0.0)
        to = pl.ds(pl.multiple_of(step * 256, 256), 256)
        v.w_cm[to, 0:128] = half_of(v.pair_a[...])
        v.w_cm[to, 128:256] = half_of(v.pair_b[...])
        return carry

    lax.fori_loop(0, 9, mix_step, 0)

    stage(FLOW_IN, 98)
    v.flow_tmp[...] = jnp.zeros_like(v.flow_tmp)
    for across in range(7):
        for comp in range(2):
            v.flow_tmp[pl.ds(across * 16 + comp, 7, stride=2), :] = strided(
                flat, MARGIN + across * 2 + comp, 7, 14
            )
    v.w_fi[...] = half_of(v.flow_tmp[...])

    stage(FLOW_MIX, 576)
    for step in range(9):
        r0 = strided(flat, MARGIN + 64 * step, 64, 1)
        high_half = lane_index((64, LANES)) >= 64
        v.pair_a[pl.ds(0, 64, stride=2), :] = jnp.where(high_half, pltpu.roll(r0, 64, 1), 0.0)
        v.pair_a[pl.ds(1, 64, stride=2), :] = jnp.where(high_half, r0, 0.0)
        v.w_fm[step * 128 : (step + 1) * 128, :] = half_of(v.pair_a[0:128, :])


def unpack_rows(v):
    flat = v.flat
    v.stages.fetch(4)

    def stage(name, rows):
        stage_of(v, name, rows)

    stage(MOTION_MIX, 2268)
    lane36 = lane_index((36, LANES))
    for i in range(64):
        if i == 0:
            value = strided(flat, MARGIN, 36, 63)
        elif i == 63:
            value = pltpu.roll(strided(flat, MARGIN + 62, 36, 63), 126, 1)
        else:
            low = pltpu.roll(strided(flat, MARGIN + i - 1, 36, 63), 2 * i, 1)
            high = pltpu.roll(strided(flat, MARGIN + i, 36, 63), 2 * i, 1)
            value = jnp.where(lane36 < 2 * i, low, high)
        v.mm_tmp[pl.ds(i, 36, stride=64), :] = jnp.where(lane36 < 126, value, 0.0)
    for step in range(9):
        v.w_mm[step * 256 : (step + 1) * 256, :] = half_of(v.mm_tmp[step * 256 : (step + 1) * 256, :])

    unpack_gru(v, ROWS_GATES, ROWS_CANDIDATE, v.w_ri, v.w_rs)


def unpack_heads(v):
    flat = v.flat
    low_half = lane_index((128, LANES)) < 64

    def stage(name, rows):
        stage_of(v, name, rows)

    unpack_gru(v, COLUMNS_GATES, COLUMNS_CANDIDATE, v.w_li, v.w_ls)

    for name, lane0 in ((FLOW_HIDDEN, 0), (MASK_HIDDEN, 256)):
        stage(name, 2304)
        for tap in range(9):
            unpack_pairs(flat, tap * 128, 128, v.w_h, tap * 128, lane0)

    stage(FLOW_OUT, 36)
    v.fo_tmp[...] = jnp.zeros_like(v.fo_tmp)
    for which in range(2):
        total = jnp.zeros((9, HEAD), jnp.float32)
        for quarter in range(4):
            total = total + mm(half_of(strided(flat, MARGIN + quarter, 9, 4)), split_pick(which, quarter))
        v.fo_tmp[pl.ds(which, 9, stride=2), 0:128] = total[:, :128]
        v.fo_tmp2[pl.ds(which, 9, stride=2), 0:128] = total[:, 128:]
    v.fo_tmp2[18:32, :] = jnp.zeros((14, LANES), jnp.float32)
    v.w_fo[:, 0:128] = half_of(v.fo_tmp[...])
    v.w_fo[:, 128:256] = half_of(v.fo_tmp2[...])

    stage(MASK_OUT, 1152)
    r = [strided(flat, MARGIN + i, 128, 9) for i in range(9)]
    rs = [pltpu.roll(r[i], 64, 1) for i in range(4, 9)]
    for block in range(5):
        even = r[block] if block < 4 else jnp.where(low_half, r[4], 0.0)
        odd = jnp.where(low_half, rs[block], rs[block + 1]) if block < 4 else jnp.where(low_half, rs[4], 0.0)
        v.pair_a[pl.ds(0, 128, stride=2), :] = even
        v.pair_a[pl.ds(1, 128, stride=2), :] = odd
        v.w_mo[:, block * 128 : (block + 1) * 128] = half_of(v.pair_a[...])


BIAS_AT = {}
_place = 0
for _name, _height, _width in shapes():
    BIAS_AT[_name] = _place
    _place += -(-_width // 128)
BIAS_ROWS = 32


def bias_of(v, name, blocks):
    at = BIAS_AT[name]
    return jnp.concatenate([v.bias[at + i : at + i + 1, :] for i in range(blocks)], axis=1)


class Halo:
    def __init__(self, v, sem, up_src, down_src, from_down, from_up):
        up = {SPACE: jnp.maximum(v.spot - 1, 0)}
        down = {SPACE: jnp.minimum(v.spot + 1, v.space - 1)}
        self.v = v
        self.up = remote(up_src, from_down, v.hsend.at[sem, 0], v.hrecv.at[sem, 0], up)
        self.down = remote(down_src, from_up, v.hsend.at[sem, 1], v.hrecv.at[sem, 1], down)

    def start(self):
        pl.when(self.v.spot > 0)(self.up.start)
        pl.when(self.v.spot < self.v.space - 1)(self.down.start)

    def receive(self):
        pl.when(self.v.spot < self.v.space - 1)(self.up.wait_recv)
        pl.when(self.v.spot > 0)(self.down.wait_recv)

    def sent(self):
        pl.when(self.v.spot > 0)(self.up.wait_send)
        pl.when(self.v.spot < self.v.space - 1)(self.down.wait_send)


def drain_bytes(ref, sem):
    pltpu.make_async_copy(ref, ref, sem).wait()


class Swap:
    def __init__(self, v, sem, src, dst, broadcast=False):
        self.v, self.sem, self.src, self.dst, self.broadcast = v, sem, src, dst, broadcast

    def start(self, b=None):
        v = self.v

        def body(step, carry):
            to = v.spot + step
            to = jnp.where(to >= v.space, to - v.space, to)
            src = self.src if self.broadcast else self.src.at[to]
            dst = self.dst.at[v.spot]
            if b is not None:
                src, dst = src.at[b], dst.at[b]
            remote(src, dst, v.asend.at[self.sem], v.arecv.at[self.sem], {SPACE: to}).start()
            return carry

        lax.fori_loop(1, v.space, body, 0)

    def receive(self):
        drain_bytes(self.dst.at[0 : self.v.space - 1], self.v.arecv.at[self.sem])

    def sent(self):
        drain_bytes(self.dst.at[0 : self.v.space - 1], self.v.asend.at[self.sem])


def spread_rows(v, b, acts, rows, dst, row0, width, backward=False):
    x = lax.rem(row_index((rows, LANES)), WIDE)
    for block, act in enumerate(acts):
        v.tmp[8 : 8 + rows, :] = act
        for tap in range(3):
            d = (1 - tap) if backward else (tap - 1)
            value = act if d == 0 else v.tmp[8 + d : 8 + d + rows, :]
            if d == -1:
                value = jnp.where(x > 0, value, 0.0)
            if d == 1:
                value = jnp.where(x < WIDE - 1, value, 0.0)
            lane = tap * width + block * LANES
            if backward:
                dst[row0 : row0 + rows, b + lane : b + lane + LANES] = half_of(value)
            else:
                dst[b, row0 : row0 + rows, lane : lane + LANES] = half_of(value)


def spread_five(v, value, dst, lane_of, backward=False):
    x = lax.rem(row_index((AREA, LANES)), WIDE)
    v.tmp[8 : 8 + AREA, :] = value
    for tap in range(5):
        d = (2 - tap) if backward else (tap - 2)
        moved = value if d == 0 else v.tmp[8 + d : 8 + d + AREA, :]
        if d:
            moved = jnp.where((x + d >= 0) & (x + d < WIDE), moved, 0.0)
        if backward:
            taps_part(v, tap, lane_of, lane_of + LANES)[...] = half_of(moved)
        else:
            lane = lane_of(tap)
            dst[:, lane : lane + LANES] = half_of(moved)


def lines_of(ref, b, lines):
    return jnp.concatenate([ref[b, y] for y in range(lines)], axis=1)


def edge_rows(v, value, rows):
    low = jnp.where(v.spot > 0, value[0:rows], 0.0)
    high = jnp.where(v.spot < v.space - 1, value[-rows:], 0.0)
    return jnp.concatenate([low, value[rows:-rows], high], axis=0)


def early_taps(v):
    def flow(b, carry):
        up = jnp.where(v.spot > 0, v.flow_up[b], 0.0)
        down = jnp.where(v.spot < v.space - 1, v.flow_down[b], 0.0)
        lane = lane_index((16, LANES))
        v.fs[...] = jnp.zeros_like(v.fs)
        for across in range(7):
            d = across - 3
            for part, value in enumerate((up, v.flow[b], down)):
                moved = value
                if d:
                    moved = pltpu.roll(value, (-d) % LANES, 1)
                    moved = jnp.where((lane + d >= 0) & (lane + d < WIDE), moved, 0.0)
                v.fs[across, part * 10 : part * 10 + 10, :] = moved[0:10, :]
        for y in range(9):
            for across in range(7):
                v.flow_tmp[across * 16 : across * 16 + 16, :] = v.fs[across, 2 * y : 2 * y + 16, :]
            v.xt[b, :, y * 128 : (y + 1) * 128] = half_of(v.flow_tmp[...])
        return carry

    lax.fori_loop(0, BATCH, flow, 0)

    def image(b, carry):
        at = pl.ds(pl.multiple_of(b * AREA, AREA), AREA)
        spread_five(v, full_of(v.context[b]), v.xi.at[at], lambda t: t * 256)
        spread_five(v, full_of(v.net[b]), v.xs.at[at], lambda t: t * 128)
        return carry

    lax.fori_loop(0, BATCH, image, 0)


def gather_start(v, count):
    shift = lax.rem(v.rank * count, LANES)
    chunk = 512
    keep = lane_index((chunk, LANES)) >= shift
    v.tmp[7:8, :] = jnp.zeros((1, LANES), jnp.float32)

    def rotate(step, carry):
        at = pl.ds(pl.multiple_of(step * chunk, chunk), chunk)
        moved = pltpu.roll(full_of(v.gath[at, :]), shift, 1)
        v.tmp[8 : 8 + chunk, :] = moved
        v.gath[at, :] = half_of(jnp.where(keep, moved, v.tmp[7 : 7 + chunk, :]))
        v.tmp[7:8, :] = v.tmp[7 + chunk : 8 + chunk, :]
        return carry

    lax.fori_loop(0, BLOCK // chunk, rotate, 0)

    quad = BLOCK // 4
    pieces = 4
    rows = quad // pieces
    half, core = lax.rem(v.spot, 2), lax.rem(v.rank, 2)
    near, far = v.rank - core, lax.rem(v.rank - core + 2, 4)

    def piece(rank, which, core, index):
        return pl.ds(pl.multiple_of(rank * BLOCK + (which * 2 + core) * quad + index * rows, 16), rows)

    def whole(rank, which, core):
        return pl.ds(pl.multiple_of(rank * BLOCK + (which * 2 + core) * quad, 16), quad)

    mine = pl.ds(pl.multiple_of(v.rank * BLOCK, 16), BLOCK)
    v.g_here = pltpu.make_async_copy(v.gath.at[0:BLOCK], v.out_all.at[mine], v.lsem)
    v.g_own = []
    for number, (which, side) in enumerate(((half, 1 - core), (half, core), (1 - half, 0), (1 - half, 1))):
        v.g_own.append(
            remote(
                v.gath.at[whole(0, which, side)], v.out_all.at[whole(v.rank, which, side)],
                v.gsend.at[0, number], v.grecv.at[0, number], {DP: v.mate},
            )
        )

    def block_copy(number, k, rank, which, side, device):
        block = v.out_all.at[piece(rank, which, side, k)]
        return remote(block, block, v.gsend.at[number, k], v.grecv.at[number, k], device)

    v.g_x, v.g_twin, v.g_mate, v.g_last = [], [], [], []
    for turn in range(2):
        base = 1 + 4 * turn
        v.g_x.append([block_copy(base, k, near + turn, half, core, {DP: v.other}) for k in range(pieces)])
        v.g_twin.append([block_copy(base + 1, k, far + turn, half, core, {SPACE: v.twin}) for k in range(pieces)])
        v.g_mate.append([block_copy(base + 2, k, far + turn, half, core, {DP: v.mate}) for k in range(pieces)])
        v.g_last.append([block_copy(base + 3, k, far + turn, 1 - half, core, {DP: v.mate}) for k in range(pieces)])
    v.g_here.start()
    for copy in v.g_own:
        copy.start()

    @pl.when(v.rank == 3)
    def _():
        for rank in range(3):
            remote(
                v.gath.at[BIAS_LOW : BIAS_LOW + 64], v.bz, v.gsend.at[0, 4 + rank], v.grecv.at[0, 4], {DP: rank}
            ).start()
        v.bz[...] = v.gath[BIAS_LOW : BIAS_LOW + 64, :]

    v.g_here.wait()
    def send_first():
        for copy in v.g_x[0]:
            copy.start()

    pl.when(core == 0)(send_first)
    v.g_own[0].wait_recv()
    pl.when(core == 1)(send_first)


BIAS_LOW = 6048


def gather_pass(v, turn, first, last):
    for k in range(first, last):
        v.g_x[turn][k].wait_recv()
        v.g_twin[turn][k].start()
        v.g_mate[turn][k].start()


def gather_turn(v, turn):
    for k in range(len(v.g_x[turn])):
        v.g_twin[turn][k].wait_recv()
        v.g_last[turn][k].start()
    for k in range(len(v.g_x[turn])):
        v.g_mate[turn][k].wait_recv()
        v.g_last[turn][k].wait_recv()


def gather_end(v):
    for turn in range(2):
        for group in (v.g_x, v.g_twin, v.g_mate, v.g_last):
            for copy in group[turn]:
                copy.wait_send()
    for copy in v.g_own:
        copy.wait_send()

    @pl.when(v.rank == 3)
    def _():
        for rank in range(3):
            remote(
                v.gath.at[BIAS_LOW : BIAS_LOW + 64], v.bz, v.gsend.at[0, 4 + rank], v.grecv.at[0, 4], {DP: rank}
            ).wait_send()


def forward_rows(v):
    spot, last = v.spot, v.space - 1
    def image(b, carry):
        pieces = (
            (v.corr_up, 0, 256, 2, spot > 0),
            (v.corr, 256, 640, 5, None),
            (v.corr_down, 896, 256, 2, spot < last),
        )
        bias = bias_of(v, CORR_IN, 2)
        for ref, row0, rows, lines, seen in pieces:
            act, slope = act_slope(tn(lines_of(ref, b, lines), v.w_ci[...]) + bias)
            if seen is None:
                v.slope_ci[b] = half_of(slope)
            else:
                act = jnp.where(seen, act, 0.0)
            spread_rows(v, b, (act[:, :128], act[:, 128:]), rows, v.hx_c, row0, 256)

        act, slope = act_slope(tn(v.xt[b], v.w_fi[...]) + bias_of(v, FLOW_IN, 1))
        v.slope_fi[b] = half_of(slope[256:896])
        spread_rows(v, b, (edge_rows(v, act, 2 * WIDE),), 9 * WIDE, v.hx_f, 0, 128)

        pre = mm(join(v.hx_c[b, a * 128 : a * 128 + 896, :] for a in range(3)), v.w_cm[...]) + bias_of(v, CORR_MIX, 2)
        flow_pre = mm(join(v.hx_f[b, a * 128 : a * 128 + 896, :] for a in range(3)), v.w_fm[...])
        flow_pre = flow_pre + bias_of(v, FLOW_MIX, 1)
        low, low_slope = act_slope(pre[:, :128])
        high, high_slope = act_slope(pre[:, 128:] + flow_pre)
        v.slope_j[b, :, 0:128] = half_of(low_slope)
        v.slope_j[b, :, 128:256] = half_of(high_slope)
        spread_rows(v, b, (edge_rows(v, low, WIDE), edge_rows(v, high, WIDE)), 896, v.hx_j, 0, 256)

        pl.when(b == 0)(lambda: gather_pass(v, 1, 0, 2))
        pl.when(b == 1)(lambda: gather_pass(v, 1, 2, 4))
        return carry

    lax.fori_loop(0, BATCH, image, 0)
    gather_turn(v, 1)
    gather_end(v)
    unpack_rows(v)

    def moving(b, carry):
        pre = mm(join(v.hx_j[b, a * 128 : a * 128 + 640, :] for a in range(3)), v.w_mm[...])
        pre = pre + bias_of(v, MOTION_MIX, 1)
        act, slope = act_slope(pre)
        v.slope_m[b] = half_of(jnp.where(lane_index((AREA, LANES)) < 126, slope, 0.0))
        pick = jnp.where(lane_index((16, LANES)) == row_index((16, LANES)) + 126, 1.0, 0.0)
        own_flow = v.flow[b]
        for y in range(ROWS):
            v.tmp2[0:2, :] = own_flow[2 * y : 2 * y + 2, :]
            v.tmp2[2:16, :] = jnp.zeros((14, LANES), jnp.float32)
            v.motion[b, y * 128 : (y + 1) * 128, :] = act[y * 128 : (y + 1) * 128, :] + tn(
                half_of(v.tmp2[0:16, :]), half_of(pick)
            )
        v.motion[b] = full_of(half_of(v.motion[b]))
        pack_rows(v, v.motion, b, v.a_motion)
        v.swap_motion.start(b)
        return carry

    lax.fori_loop(0, BATCH, moving, 0)

    def gru(b, carry):
        at = pl.ds(pl.multiple_of(b * AREA, AREA), AREA)
        s = full_of(v.net[b])
        spread_five(v, v.motion[b], v.xi.at[at], lambda t: t * 256 + 128)
        both = mm(v.xi[at, :], v.w_ri[...])
        gates = jax.nn.sigmoid(both[:, :256] + mm(v.xs[at, :], v.w_rs[:, :256]) + bias_of(v, ROWS_GATES, 2))
        update, reset = gates[:, :128], gates[:, 128:]
        v.ru[b] = update
        v.rr[b] = reset
        spread_five(v, full_of(half_of(reset * s)), v.xr.at[at], lambda t: t * 128)
        cand = jnp.tanh(both[:, 256:] + mm(v.xr[at, :], v.w_rs[:, 256:]) + bias_of(v, ROWS_CANDIDATE, 1))
        v.rc[b] = cand
        v.state[b] = s + update * (cand - s)
        pack_rows(v, v.state, b, v.a_state)
        v.swap_state.start(b)
        return carry

    lax.fori_loop(0, BATCH, gru, 0)


def pack_rows(v, src, b, dst):
    def peer(t, carry):
        for y in range(ROWS):
            at = pl.multiple_of(y * WIDE + t * COLS, COLS)
            dst[t, b, y * COLS : (y + 1) * COLS, :] = half_of(src[b, pl.ds(at, COLS), :])
        return carry

    lax.fori_loop(0, v.space, peer, 0)


def take_own(v, src, dst):
    dst[v.spot] = src[v.spot]


def columns_zero(v):
    def zero(b, carry):
        for ref, wide in ((v.xc, 384), (v.xcr, 128), (v.gc, 384)):
            for low in (0, 32 + AREA):
                ref[b, low : low + 32, :] = jnp.zeros((32, wide), jnp.bfloat16)
        return carry

    lax.fori_loop(0, BATCH, zero, 0)


def columns_in(v):
    def peer(t, carry):
        at = pl.ds(pl.multiple_of(32 + t * ROWS * COLS, 16), ROWS * COLS)
        for b in range(BATCH):
            v.xc[b, at, 0:128] = v.b_state[t, b]
            v.xc[b, at, 128:256] = v.b_context[t, b]
            v.xc[b, at, 256:384] = v.b_motion[t, b]
        return carry

    lax.fori_loop(0, v.space, peer, 0)


FX_ROWS = 16 + (TALL + 2) * PITCH


def fx_base(b):
    return pl.multiple_of(b * FX_ROWS, 8)


def columns_forward(v):
    def gru(b, carry):
        s = full_of(v.xc[b, 32 : 32 + AREA, 0:128])
        bias = join((bias_of(v, COLUMNS_GATES, 2), bias_of(v, COLUMNS_CANDIDATE, 1)))
        rows = [slice(t * COLS, t * COLS + AREA) for t in range(5)]
        both = mm(join(v.xc[b, rows[t], 128:384] for t in range(5)), v.w_li[...]) + bias
        gates = mm(join(v.xc[b, rows[t], 0:128] for t in range(5)), v.w_ls[:, 0:256])
        gates = jax.nn.sigmoid(gates + both[:, :256])
        update, reset = gates[:, :128], gates[:, 128:]
        v.lu[b] = update
        v.lr[b] = reset
        v.xcr[b, 32 : 32 + AREA, :] = half_of(reset * s)
        cand = jnp.tanh(both[:, 256:] + mm(join(v.xcr[b, rows[t], :] for t in range(5)), v.w_ls[:, 256:384]))
        v.lc[b] = cand
        final = s + update * (cand - s)
        v.out_net[b] = half_of(final)
        v.final[...] = full_of(half_of(final))
        fx = fx_base(b)
        v.mm_tmp[pl.ds(fx, FX_ROWS), :] = jnp.zeros((FX_ROWS, LANES), jnp.float32)
        for x in range(COLS):
            v.mm_tmp[pl.ds(fx + 8 + PITCH + 2 + x, TALL, stride=PITCH), :] = v.final[pl.ds(x, TALL, stride=COLS), :]
        for j in range(2):
            v.e_left[b, j, 0:TALL, :] = half_of(v.final[pl.ds(j, TALL, stride=COLS), :])
            v.e_right[b, j, 0:TALL, :] = half_of(v.final[pl.ds(COLS - 2 + j, TALL, stride=COLS), :])
        return carry

    lax.fori_loop(0, BATCH, gru, 0)
    v.halo_final.start()


def ring_masks(v, shape):
    x = lax.rem(row_index(shape), PITCH)
    place = v.spot * COLS + x - 2
    seen = (place >= 0) & (place < WIDE) & (x >= 1) & (x < PITCH - 1)
    own = (x >= 2) & (x < PITCH - 2)
    return seen, own


def mask_gradient(v):
    def image(b, carry):
        value = nt(quarter_of(v.grad_mask[b]), v.w_mo[:, 0:MASK])
        for block in range(2):
            v.final[...] = value[:, block * 128 : (block + 1) * 128]
            v.tmp[0:SPREAD, :] = jnp.zeros((SPREAD, LANES), jnp.float32)
            for x in range(COLS):
                v.tmp[pl.ds(2 + x, TALL, stride=PITCH), :] = v.final[pl.ds(x, TALL, stride=COLS), :]
            v.hgo[b, :, 256 + block * 128 : 384 + block * 128] = half_of(v.tmp[0:SPREAD, :])
            v.m_left[b, block, 0:TALL, :] = half_of(v.final[pl.ds(0, TALL, stride=COLS), :])
            v.m_right[b, block, 0:TALL, :] = half_of(v.final[pl.ds(COLS - 1, TALL, stride=COLS), :])
        return carry

    lax.fori_loop(0, BATCH, image, 0)
    v.halo_mask.start()


def heads_part(v, b, tap):
    ref = v.hx_c if tap < 6 else v.hx_f
    lane = tap % 6 * 128
    return ref.at[b, 0:SPREAD, lane : lane + 128]


def taps_part(v, t, low, high):
    ref = v.hx_f if t % 3 == 2 else v.hx_c
    lane = (t % 3) % 2 * 384
    return ref.at[t // 3, 0:AREA, lane + low : lane + high]


def split_three(value):
    first = half_of(value)
    second = half_of(value - full_of(first))
    third = half_of(value - full_of(first) - full_of(second))
    return first, second, third


def column_grid():
    lane = lane_index((COLS, SPAN))
    columns = jnp.where((lax.rem(lane, PITCH) == row_index((COLS, SPAN)) + 2) & (lane < SPREAD), 1.0, 0.0)
    lane = lane_index((TALL, SPAN))
    rows = jnp.where(lax.div(lane, PITCH) == row_index((TALL, SPAN)), 1.0, 0.0)
    return columns, half_of(rows)


def widen(value, columns, rows, parts):
    spread = 0.0
    for piece in split_three(value)[:parts]:
        spread = spread + mm(piece, rows)
    return jnp.sum(spread * columns, axis=0, keepdims=True)


def widen_all(v):
    columns, rows = column_grid()
    first = row_index((8, SPAN)) == 0
    second = row_index((8, SPAN)) == 1
    for b in range(BATCH):
        low, high = (widen(v.target[b, c], columns, rows, 3) for c in range(2))
        v.target_wide[b] = jnp.where(first, low, jnp.where(second, high, 0.0))
        v.valid_wide[b] = jnp.broadcast_to(widen(v.valid[b].astype(jnp.float32), columns, rows, 1), (8, SPAN))


def narrow(v, b, wide, columns, rows):
    for c in range(2):
        total = 0.0
        for piece in split_three(wide[c : c + 1, :] * columns):
            total = total + nt(piece, rows)
        v.out_flow[b, c] = total


def heads(v):
    spot, last = v.spot, v.space - 1
    v.halo_final.receive()
    v.swap_count.receive()
    v.counts[v.spot] = v.count_out[...]
    counts = jnp.sum(v.counts[...], axis=0)
    seen, own = ring_masks(v, (SPREAD, LANES))
    steps = [(a - 1) * PITCH + (c - 1) for a in range(3) for c in range(3)]
    plane = jnp.float32(TALL * WIDE)
    columns, rows = column_grid()

    def image(b, carry):
        fx = fx_base(b)
        for j in range(2):
            left = jnp.where(spot > 0, full_of(v.f_left[b, j, 0:TALL, :]), 0.0)
            right = jnp.where(spot < last, full_of(v.f_right[b, j, 0:TALL, :]), 0.0)
            v.mm_tmp[pl.ds(fx + 8 + PITCH + j, TALL, stride=PITCH), :] = left
            v.mm_tmp[pl.ds(fx + 8 + PITCH + PITCH - 2 + j, TALL, stride=PITCH), :] = right
        for tap in range(9):
            at = 8 + PITCH + steps[tap]
            heads_part(v, b, tap)[...] = half_of(v.mm_tmp[pl.ds(fx + at, SPREAD), :])
        for part in range(2):
            name = (FLOW_HIDDEN, MASK_HIDDEN)[part]
            lanes = slice(part * 256, (part + 1) * 256)
            act, slope = act_slope(mm(join((v.hx_c[b, 0:SPREAD, :], v.hx_f[b, 0:SPREAD, :])), v.w_h[:, lanes]) + bias_of(v, name, 2))
            v.slope_h[b, :, lanes] = half_of(slope)
            if part == 0:
                for block in range(2):
                    value = jnp.where(seen, act[:, block * 128 : (block + 1) * 128], 0.0)
                    v.feat[b, 0:SPREAD, block * 128 : (block + 1) * 128] = half_of(value)
                v.feat[b, SPREAD:SPAN, :] = jnp.zeros((SPAN - SPREAD, HEAD), jnp.bfloat16)
            else:
                for block in range(2):
                    v.tmp[0:SPREAD, :] = act[:, block * 128 : (block + 1) * 128]
                    for x in range(COLS):
                        v.final[pl.ds(x, TALL, stride=COLS), :] = v.tmp[pl.ds(2 + x, TALL, stride=PITCH), :]
                    v.mf[b, :, block * 128 : (block + 1) * 128] = half_of(v.final[...])
        moved = nt(v.w_fo[...], v.feat[b])
        v.dt[...] = moved
        delta = jnp.zeros((8, SPAN), jnp.float32)
        for tap in range(9):
            pair = jnp.concatenate([v.dt[2 * tap : 2 * tap + 2, :], jnp.zeros((6, SPAN), jnp.float32)], axis=0)
            delta = delta + pltpu.roll(pair, (-steps[tap]) % SPAN, 1)
        v.tmp[0:SPAN, :] = jnp.zeros((SPAN, LANES), jnp.float32)
        v.final[...] = full_of(v.xc[b, 32 : 32 + AREA, 256:384])
        for x in range(COLS):
            v.tmp[pl.ds(2 + x, TALL, stride=PITCH), :] = v.final[pl.ds(x, TALL, stride=COLS), :]
        pick = jnp.where(lane_index((16, LANES)) == row_index((16, LANES)) + 126, 1.0, 0.0)
        base = nt(half_of(pick), half_of(v.tmp[0:SPAN, :]))[0:8, :]
        bias = v.bias[BIAS_AT[FLOW_OUT] : BIAS_AT[FLOW_OUT] + 1, :]
        first = row_index((8, SPAN)) == 0
        second = row_index((8, SPAN)) == 1
        shift = jnp.where(first, bias[0:1, 0:1], jnp.where(second, bias[0:1, 1:2], 0.0))
        new = base + delta + shift
        narrow(v, b, new, columns, rows)
        error = new - v.target_wide[b]
        root = jnp.sqrt(error * error + 1.0)
        valid = jnp.where(first | second, v.valid_wide[b], 0.0)
        piece = jnp.sum(valid * root)
        divisor = jnp.maximum(v.pick_count(counts, b), 1.0)
        gradient = plane / divisor * valid * error / root
        v.dg[b] = gradient
        v.losses[...] = jnp.where(row_index((8, LANES)) == b, piece, v.losses[...])
        return carry

    v.losses[...] = jnp.zeros((8, LANES), jnp.float32)
    lax.fori_loop(0, BATCH, image, 0)
    v.halo_dg.start()
    v.swap_loss.start()


def mask_output(v):
    def image(b, carry):
        store = pltpu.make_async_copy(v.mask_low, v.out_mask.at[b], v.osem.at[3])
        pl.when(b > 0)(store.wait)
        for block in range(5):
            wide = min(128, MASK - block * 128)
            lanes = slice(block * 128, block * 128 + wide)
            at = BIAS_AT[MASK_OUT] + block
            value = mm(v.mf[b], v.w_mo[:, lanes]) + v.bias[at : at + 1, 0:wide]
            v.mask_low[:, lanes] = half_of(0.25 * value)
        store.start()
        return carry

    lax.fori_loop(0, BATCH, image, 0)


def heads_back(v):
    spot, last = v.spot, v.space - 1
    seen, own = ring_masks(v, (SPREAD, LANES))
    steps = [(a - 1) * PITCH + (c - 1) for a in range(3) for c in range(3)]
    v.halo_dg.receive()
    v.halo_mask.receive()

    def zb(c, low, rows):
        at = c * (2 * EDGE + SPREAD) + low
        return v.mm_tmp.at[at : at + rows]

    def image(b, carry):
        x = lax.rem(lane_index((8, SPAN)), PITCH)
        own_dg = v.dg[b]
        left = jnp.where((x < 2) & (spot > 0), pltpu.roll(v.dg_left[b], SPAN - COLS, 1), 0.0)
        right = jnp.where((x >= PITCH - 2) & (spot < last), pltpu.roll(v.dg_right[b], COLS, 1), 0.0)
        inside = lane_index((8, SPAN)) < SPREAD
        wide_dg = full_of(half_of(jnp.where(inside, own_dg + left + right, 0.0)))
        own_low = full_of(half_of(own_dg))
        v.dt[...] = jnp.zeros_like(v.dt)
        v.dto[...] = jnp.zeros_like(v.dto)
        for tap in range(9):
            v.dt[2 * tap : 2 * tap + 2, :] = pltpu.roll(wide_dg, steps[tap] % SPAN, 1)[0:2, :]
            v.dto[2 * tap : 2 * tap + 2, :] = pltpu.roll(own_low, steps[tap] % SPAN, 1)[0:2, :]
        v.dtb[b] = half_of(v.dto[...])
        from_flow = tn(half_of(v.dt[...]), v.w_fo[...])
        for block in range(2):
            left = jnp.where(spot > 0, full_of(v.n_left[b, block, 0:TALL, :]), 0.0)
            right = jnp.where(spot < last, full_of(v.n_right[b, block, 0:TALL, :]), 0.0)
            v.tmp[0:SPREAD, :] = full_of(v.hgo[b, :, 256 + block * 128 : 384 + block * 128])
            v.tmp[pl.ds(1, TALL, stride=PITCH), :] = left
            v.tmp[pl.ds(PITCH - 2, TALL, stride=PITCH), :] = right
            v.hgo[b, :, 256 + block * 128 : 384 + block * 128] = half_of(v.tmp[0:SPREAD, :])
        for block in range(4):
            lanes = slice(block * 128, (block + 1) * 128)
            value = from_flow[0:SPREAD, lanes] if block < 2 else full_of(v.hgo[b, :, lanes])
            value = value * full_of(v.slope_h[b, :, lanes])
            v.hgo[b, :, lanes] = half_of(jnp.where(seen, value, 0.0))
        total = jnp.zeros((SPREAD, LANES), jnp.float32)
        for a in range(3):
            value = nt(v.hgo[b], v.w_h[a * 384 : (a + 1) * 384, :])
            for c in range(3):
                zb(c, EDGE, SPREAD)[...] = value[:, c * 128 : (c + 1) * 128]
            for c in range(3):
                at = EDGE - steps[a * 3 + c]
                total = total + zb(c, at, SPREAD)[...]
        for block in range(4):
            lanes = slice(block * 128, (block + 1) * 128)
            v.hgo[b, :, lanes] = half_of(jnp.where(own, full_of(v.hgo[b, :, lanes]), 0.0))
        v.tmp[0:SPREAD, :] = total
        for x in range(COLS):
            v.final[pl.ds(x, TALL, stride=COLS), :] = v.tmp[pl.ds(2 + x, TALL, stride=PITCH), :]
        r = v.final[...] + full_of(v.grad_net[b])

        s = full_of(v.xc[b, 32 : 32 + AREA, 0:128])
        update, reset, cand = v.lu[b], v.lr[b], v.lc[b]
        cg = half_of(r * update * (1.0 - cand * cand))
        v.gc[b, 32 : 32 + AREA, 256:384] = cg
        rows = [slice((4 - t) * COLS, (4 - t) * COLS + AREA) for t in range(5)]
        reset_grad = nt(
            join(v.gc[b, rows[t], 256:384] for t in range(5)),
            join(v.w_ls[t * 128 : (t + 1) * 128, 256:384] for t in range(5)),
        )
        v.gc[b, 32 : 32 + AREA, 0:128] = half_of(r * (cand - s) * update * (1.0 - update))
        v.gc[b, 32 : 32 + AREA, 128:256] = half_of(reset_grad * s * reset * (1.0 - reset))
        state_grad = r * (1.0 - update) + reset_grad * reset
        state_grad = state_grad + nt(
            join(v.gc[b, rows[t], 0:256] for t in range(5)),
            join(v.w_ls[t * 128 : (t + 1) * 128, 0:256] for t in range(5)),
        )
        inputs_grad = nt(
            join(v.gc[b, rows[t], :] for t in range(5)), join(v.w_li[t * 256 : (t + 1) * 256, :] for t in range(5))
        )
        high = half_of(own_dg)
        low = half_of(own_dg - full_of(high))
        pick = half_of(jnp.where(lane_index((8, LANES)) == row_index((8, LANES)) + 126, 1.0, 0.0))
        v.tmp[0:SPAN, :] = tn(high, pick) + tn(low, pick)
        for x in range(COLS):
            v.final[pl.ds(x, TALL, stride=COLS), :] = v.tmp[pl.ds(2 + x, TALL, stride=PITCH), :]
        v.lu[b] = state_grad
        v.lr[b] = inputs_grad[:, 0:128]
        v.lc[b] = inputs_grad[:, 128:256] + v.final[...]

        def peer(t, carry):
            at = pl.ds(pl.multiple_of(t * ROWS * COLS, 16), ROWS * COLS)
            v.a_state[t, b] = half_of(v.lu[b, at, :])
            v.a_context[t, b] = half_of(v.lr[b, at, :])
            v.a_motion[t, b] = half_of(v.lc[b, at, :])
            return carry

        lax.fori_loop(0, v.space, peer, 0)
        v.back_state.start(b)
        return carry

    v.swap_loss.receive()
    for c in range(3):
        zb(c, 0, EDGE)[...] = jnp.zeros((EDGE, LANES), jnp.float32)
        zb(c, EDGE + SPREAD, EDGE)[...] = jnp.zeros((EDGE, LANES), jnp.float32)
    lax.fori_loop(0, BATCH, image, 0)


def unpack_back(v, src, dst):
    def peer(t, carry):
        for b in range(BATCH):
            value = full_of(src[t, b])
            for y in range(ROWS):
                at = pl.multiple_of(y * WIDE + t * COLS, COLS)
                dst[b, pl.ds(at, COLS), :] = value[y * COLS : (y + 1) * COLS, :]
        return carry

    lax.fori_loop(0, v.space, peer, 0)


def seams():
    starts, bias_row, _, _ = flat_rows()
    edges = sorted(starts.values()) + [bias_row]
    tiles = sorted({row // 16 for row in edges if row % 16})
    parts = {}
    for low, high in zip(edges, edges[1:]):
        for tile in tiles:
            if low < (tile + 1) * 16 and high > tile * 16:
                parts[tile] = parts.get(tile, 0) + 1
    return {tile: (index, parts[tile]) for index, tile in enumerate(tiles)}


class Flush:
    def __init__(self, v):
        self.v, self.at, self.busy, self.small = v, 0, {}, []
        self.tiles = seams()
        self.left = {tile: parts for tile, (_, parts) in self.tiles.items()}
        v.seam[...] = jnp.zeros_like(v.seam)
        top = (max(self.tiles) + 1) * 16
        rest = v.out_flat.shape[0] - top
        v.seam_low[16 * 16 : 16 * 16 + rest, :] = jnp.zeros((rest, LANES), jnp.bfloat16)
        self.write(16, rest, top)

    def write(self, index, rows, base):
        v = self.v
        copy = pltpu.make_async_copy(
            v.seam_low.at[index * 16 : index * 16 + rows], v.out_flat.at[base : base + rows], v.fsem.at[index]
        )
        copy.start()
        self.small.append(copy)

    def send(self, low, length, base):
        v, slot = self.v, self.at % 2
        self.at += 1
        if slot in self.busy:
            self.busy[slot].wait()
        cast_rows(v.stage.at[slot], 0, v.flat, low, length, jnp.bfloat16)
        copy = pltpu.make_async_copy(
            v.stage.at[slot, 0:length], v.out_flat.at[base : base + length], v.ssem.at[slot, 0]
        )
        copy.start()
        self.busy[slot] = copy

    def layer(self, start, rows):
        v, stop = self.v, start + rows
        for tile in self.tiles:
            low, high = max(start, tile * 16), min(stop, tile * 16 + 16)
            if low >= high:
                continue
            index = self.tiles[tile][0]
            v.seam[index, low - tile * 16 : high - tile * 16, :] = v.flat[MARGIN + low - start : MARGIN + high - start, :]
            self.left[tile] -= 1
            if not self.left[tile]:
                v.seam_low[index * 16 : index * 16 + 16, :] = half_of(v.seam[index])
                self.write(index, 16, tile * 16)
        low, high = -(-start // 16) * 16, stop // 16 * 16
        if high > low:
            self.send(MARGIN + low - start, high - low, low)

    def settle(self):
        for copy in list(self.busy.values()) + self.small:
            copy.wait()
        self.busy, self.small = {}, []


SHARE = 3072


class Reduce:
    ORDER = (
        (3, 3072, 3072), (3, 0, 3072), (2, 3072, 3072), (2, 0, 3072), (1, 3072, 3072), (1, 0, 3072),
        (0, 1024, 3072), (0, 4096, 2048), (0, 0, 1024),
    )

    def __init__(self, v, count):
        self.v, self.count = v, count
        self.flying, self.queue, self.late = [], [], []
        self.copies = {}
        rank = v.rank
        self.lower, self.upper = lax.rem(rank, 2), lax.div(rank, 2)
        self.side, self.depth = lax.rem(v.spot, 2), lax.div(v.spot, 2)
        self.group = v.space // 2

    def part(self, k):
        return self.ORDER[k][2] // 4 // self.v.space

    def slice_at(self, k, spot):
        return lax.rem(spot, 2) * (self.ORDER[k][2] // 8) + lax.div(spot, 2) * self.part(k)

    def offer(self, *numbers, now=True):
        if now:
            self.queue += list(numbers)
        else:
            self.late += list(numbers)

    LONG = 5

    def stages(self, k):
        if k < self.LONG:
            return (self.core, self.across, self.side_sum, self.deep_sum, self.deep_out, self.owner, self.beside)
        if k < len(self.ORDER) - 1:
            return (self.core, self.across, self.stripes, self.along, self.beside)
        return (self.ranks, self.stripes, self.along)

    def tick(self):
        for entry in self.flying:
            self.stages(entry[0])[entry[1]](entry[0])
            entry[1] += 1
        self.flying = [entry for entry in self.flying if entry[1] < len(self.stages(entry[0]))]
        if self.queue:
            number = self.queue.pop(0)
            self.v.flush.settle()
            self.begin(number)
            self.flying.append([number, 0])
        self.queue, self.late = self.queue + self.late, []

    def begin(self, k):
        v, slot = self.v, k % 2
        quarter, low, size = self.ORDER[k]
        start = quarter * self.count // (LANES * 16) * 16 + low
        half = size // 2
        if k == len(self.ORDER) - 1:
            self.begin_ranks(start, size // 4)
            return

        def rows(which):
            return v.out_flat.at[pl.ds(pl.multiple_of(start + which * half, 16), half)]

        copy = remote(
            rows(1 - self.lower), v.rcore.at[slot, 0:half], v.rsend.at[0, slot], v.rrecv.at[0, slot], {DP: v.mate}
        )
        own = pltpu.make_async_copy(rows(self.lower), v.own.at[slot, 0:half], v.rlocal.at[slot])
        copy.start()
        own.start()
        self.copies[k] = (copy, own)

    def begin_ranks(self, start, rows):
        v = self.v

        def block(rank):
            at = start + lax.rem(rank, 2) * (2 * rows) + lax.div(rank, 2) * rows
            return v.out_flat.at[pl.ds(pl.multiple_of(at, 16), rows)]

        for turn in range(1, 4):
            to = lax.rem(v.rank + turn, 4)
            remote(block(to), v.dall.at[v.rank], v.dsend, v.drecv, {DP: to}).start()
        self.mine = pltpu.make_async_copy(block(v.rank), v.dall.at[v.rank], v.rlocal.at[0])
        self.mine.start()

    def ranks(self, k):
        v, slot, part = self.v, k % 2, self.part(k)
        self.mine.wait()
        drain_bytes(v.dall.at[0:3], v.dsend)
        drain_bytes(v.dall.at[0:3], v.drecv)
        self.finish_f(k)
        value = full_of(v.dall[0]) + full_of(v.dall[1]) + full_of(v.dall[2]) + full_of(v.dall[3])
        rows = self.ORDER[k][2] // 4
        v.ks[slot, 0:rows, :] = value
        v.ts[slot, 0:rows, :] = half_of(value)
        v.acc[slot, 0:part, :] = v.ks[slot, pl.ds(pl.multiple_of(self.slice_at(k, v.spot), 16), part), :]
        self.each(lambda step: self.s_copy(k, step).start(), 1, v.space)

    def finish_f(self, k):
        drain_bytes(self.s_all(k - 2), self.v.s2send.at[k % 2])
        self.f_sent(k - 2)

    def core(self, k):
        v, slot = self.v, k % 2
        copy, own = self.copies[k]
        copy.wait()
        own.wait()
        if k >= 2:
            self.x_copy(k - 2).wait_send()
        quarter = self.ORDER[k][2] // 4

        def add(step, carry):
            at = pl.multiple_of(step * 128, 128)
            near = pl.ds(pl.multiple_of(self.upper * quarter + at, 128), 128)
            far = pl.ds(pl.multiple_of((1 - self.upper) * quarter + at, 128), 128)
            to = pl.ds(at, 128)
            v.tx[slot, to, :] = half_of(full_of(v.own[slot, far, :]) + full_of(v.rcore[slot, far, :]))
            v.ks[slot, to, :] = full_of(v.own[slot, near, :]) + full_of(v.rcore[slot, near, :])
            return carry

        lax.fori_loop(0, quarter // 128, add, 0)
        self.x_copy(k).start()

    def x_copy(self, k):
        v, slot = self.v, k % 2
        rows = slice(0, self.ORDER[k][2] // 4)
        return remote(
            v.tx.at[slot, rows], v.rx.at[slot, rows], v.rsend.at[1, slot], v.rrecv.at[1, slot], {DP: v.other}
        )

    def s_copy(self, k, step):
        v, slot, part = self.v, k % 2, self.part(k)
        to = lax.rem(v.spot + step, v.space)
        src = v.ts.at[slot, pl.ds(pl.multiple_of(self.slice_at(k, to), 16), part)]
        dst = v.rs.at[slot, v.spot, 0:part]
        return remote(src, dst, v.s2send.at[slot], v.s2recv.at[slot], {SPACE: to})

    def s_all(self, k):
        return self.v.rs.at[k % 2, 0 : self.v.space - 1, 0 : self.part(k)]

    def each(self, what, start, stop):
        def body(step, carry):
            what(step)
            return carry

        lax.fori_loop(start, stop, body, 0)

    def across(self, k):
        v, slot = self.v, k % 2
        self.x_copy(k).wait_recv()
        if k < self.LONG:
            self.across_long(k)
            return
        if k - 2 >= self.LONG:
            drain_bytes(self.s_all(k - 2), v.s2send.at[slot])

        def add(step, carry):
            to = pl.ds(pl.multiple_of(step * 128, 128), 128)
            value = v.ks[slot, to, :] + full_of(v.rx[slot, to, :])
            v.ks[slot, to, :] = value
            v.ts[slot, to, :] = half_of(value)
            return carry

        lax.fori_loop(0, self.ORDER[k][2] // 4 // 128, add, 0)
        part = self.part(k)
        v.acc[slot, 0:part, :] = v.ks[slot, pl.ds(pl.multiple_of(self.slice_at(k, v.spot), 16), part), :]
        self.each(lambda step: self.s_copy(k, step).start(), 1, v.space)

    def across_long(self, k):
        v, slot = self.v, k % 2
        if k >= 2:
            self.side_copy(k - 2).wait_send()
        rows = self.ORDER[k][2] // 8

        def add(step, carry):
            at = pl.multiple_of(step * 128, 128)
            near = pl.ds(pl.multiple_of(self.side * rows + at, 128), 128)
            far = pl.ds(pl.multiple_of((1 - self.side) * rows + at, 128), 128)
            to = pl.ds(at, 128)
            v.ty[slot, to, :] = half_of(v.ks[slot, far, :] + full_of(v.rx[slot, far, :]))
            v.ky[slot, to, :] = v.ks[slot, near, :] + full_of(v.rx[slot, near, :])
            return carry

        lax.fori_loop(0, rows // 128, add, 0)
        self.side_copy(k).start()

    def side_copy(self, k):
        v, slot = self.v, k % 2
        return remote(v.ty.at[slot], v.ry.at[slot], v.rsend.at[2, slot], v.rrecv.at[2, slot], {SPACE: v.twin})

    def deep_at(self, k, depth):
        return pl.ds(pl.multiple_of(depth * self.part(k), 16), self.part(k))

    def deep_copy(self, k, step):
        v, slot = self.v, k % 2
        to = lax.rem(self.depth + step, self.group)
        return remote(
            v.tz.at[slot, self.deep_at(k, to)], v.rz.at[slot, self.depth], v.z1send.at[slot],
            v.z1recv.at[slot], {SPACE: to * 2 + self.side},
        )

    def deep_all(self, k):
        return self.v.rz.at[k % 2, 0 : self.group - 1]

    def side_sum(self, k):
        v, slot = self.v, k % 2
        self.side_copy(k).wait_recv()
        if k >= 2:
            drain_bytes(self.deep_all(k - 2), v.z1send.at[slot])
        value = v.ky[slot] + full_of(v.ry[slot])
        v.tz[slot] = half_of(value)
        v.ky[slot] = value
        v.kz[slot] = v.ky[slot, self.deep_at(k, self.depth), :]
        self.each(lambda step: self.deep_copy(k, step).start(), 1, self.group)

    def out_copy(self, k, step):
        v, slot = self.v, k % 3
        to = lax.rem(self.depth + step, self.group)
        block = v.az.at[slot, self.deep_at(k, self.depth)]
        return remote(
            block, block, v.z2send.at[slot], v.z2recv.at[slot], {SPACE: to * 2 + self.side}
        )

    def deep_sum(self, k):
        v, slot = self.v, k % 2
        drain_bytes(self.deep_all(k), v.z1recv.at[slot])

        def add(step, value):
            return value + full_of(v.rz[slot, lax.rem(self.depth + step, self.group)])

        value = lax.fori_loop(1, self.group, add, v.kz[slot])
        if k >= 2:
            self.own_wait(k - 2)
        v.az[k % 3, self.deep_at(k, self.depth), :] = half_of(value)
        self.each(lambda step: self.out_copy(k, step).start(), 1, self.group)

    def own_rows(self, k, lower, upper):
        quarter, low, size = self.ORDER[k]
        at = low + lower * (size // 2) + upper * (size // 4) + self.side * (size // 8)
        return pl.ds(pl.multiple_of(at, 16), size // 8)

    def own_copy(self, k):
        v = self.v
        rows = self.own_rows(k, self.lower, self.upper)
        return remote(v.az.at[k % 3], v.gath.at[rows], v.osend.at[k % 3], v.orecv.at[k], {DP: self.ORDER[k][0]})

    def own_wait(self, k):
        pl.when(self.v.rank != self.ORDER[k][0])(self.own_copy(k).wait_send)

    def deep_out(self, k):
        v = self.v
        several = v.az.at[k % 3, 0 : (self.group - 1) * self.part(k)]
        drain_bytes(several, v.z2send.at[k % 3])
        drain_bytes(several, v.z2recv.at[k % 3])
        pl.when(v.rank != self.ORDER[k][0])(self.own_copy(k).start)

        @pl.when(v.rank == self.ORDER[k][0])
        def _():
            v.gath[self.own_rows(k, self.lower, self.upper), :] = v.az[k % 3]

    def owner(self, k):
        v = self.v

        @pl.when(v.rank == self.ORDER[k][0])
        def _():
            drain_bytes(v.gath.at[0 : 3 * (self.ORDER[k][2] // 8)], v.orecv.at[k])
            for copy in self.y_copies(k):
                copy.start()

    def place(self, k, lower, upper, spot):
        quarter, low, size = self.ORDER[k]
        at = low + lower * (size // 2) + upper * (size // 4) + self.slice_at(k, spot)
        return pl.ds(pl.multiple_of(at, 16), self.part(k))

    def f_copy(self, k, step):
        v, slot = self.v, k % 2
        quarter = self.ORDER[k][0]
        if k == len(self.ORDER) - 1:
            to = lax.rem(v.spot + step, v.space)
        else:
            to = lax.rem(self.depth + step, self.group) * 2 + self.side
        return remote(
            v.fin.at[slot, 0 : self.part(k)], v.gath.at[self.place(k, self.lower, self.upper, v.spot)],
            v.fsend.at[slot], v.frecv.at[k], {DP: quarter, SPACE: to},
        )

    def fan(self, k):
        return self.v.space if k == len(self.ORDER) - 1 else self.group

    def f_all(self, k, what):
        v = self.v
        pl.when(v.rank != self.ORDER[k][0])(lambda: what(self.f_copy(k, 0)))
        self.each(lambda step: what(self.f_copy(k, step)), 1, self.fan(k))

    def f_sent(self, k):
        v = self.v
        quarter = self.ORDER[k][0]
        pl.when(v.rank != quarter)(lambda: self.f_copy(k, 0).wait_send())
        drain_bytes(v.gath.at[0 : (self.fan(k) - 1) * self.part(k)], v.fsend.at[k % 2])

    def stripes(self, k):
        v, slot, part = self.v, k % 2, self.part(k)
        quarter = self.ORDER[k][0]
        drain_bytes(self.s_all(k), v.s2recv.at[slot])

        def add(step, value):
            return value + full_of(v.rs[slot, lax.rem(v.spot + step, v.space), 0:part])

        value = half_of(lax.fori_loop(1, v.space, add, v.acc[slot, 0:part, :]))
        if k - 2 >= self.LONG and k < len(self.ORDER) - 1:
            self.f_sent(k - 2)
        v.fin[slot, 0:part, :] = value

        @pl.when(v.rank == quarter)
        def _():
            v.gath[self.place(k, self.lower, self.upper, v.spot), :] = v.fin[slot, 0:part, :]

        self.f_all(k, lambda copy: copy.start())

    def y_copies(self, k):
        v = self.v
        quarter, low, size = self.ORDER[k]
        out = []
        for i in range(4):
            at = pl.multiple_of(low + i * (size // 4) + self.side * (size // 8), 16)
            block = v.gath.at[pl.ds(at, size // 8)]
            out.append(remote(block, block, v.ysend.at[k], v.yrecv.at[k], {SPACE: v.twin}))
        return out

    def along(self, k):
        v = self.v
        quarter = self.ORDER[k][0]

        @pl.when(v.rank == quarter)
        def _():
            drain_bytes(v.gath.at[0 : (4 * self.fan(k) - 1) * self.part(k)], v.frecv.at[k])
            if k < len(self.ORDER) - 1:
                for copy in self.y_copies(k):
                    copy.start()

    def beside(self, k):
        v = self.v

        @pl.when(v.rank == self.ORDER[k][0])
        def _():
            several = v.gath.at[0 : self.ORDER[k][2] // 2]
            drain_bytes(several, v.ysend.at[k])
            drain_bytes(several, v.yrecv.at[k])

    def settle(self):
        v = self.v
        for k in range(self.LONG - 2, self.LONG):
            self.side_copy(k).wait_send()
            drain_bytes(self.deep_all(k), v.z1send.at[k % 2])
            self.own_wait(k)
        for k in range(len(self.ORDER) - 3, len(self.ORDER) - 1):
            self.x_copy(k).wait_send()
        for k in range(len(self.ORDER) - 2, len(self.ORDER)):
            drain_bytes(self.s_all(k), v.s2send.at[k % 2])
            self.f_sent(k)

    def ready(self):
        v, count = self.v, self.count
        v.gath[2 * SHARE :, :] = jnp.zeros((32, LANES), jnp.bfloat16)

        @pl.when(v.rank == 3)
        def _():
            at = self.bias_base() - 3 * count // (LANES * 16) * 16
            v.gath[at : at + 32, :] = half_of(full_of(v.gath[at : at + 32, :]) + v.bsum[...])

    def lay(self, first, last):
        v, count = self.v, self.count
        offset = v.rank * count - quarter_base(v.rank, count) * LANES
        skip = lax.div(offset, LANES)
        shift = lax.rem(offset, LANES)
        near = lane_index((256, LANES)) < LANES - shift

        def staged(slot):
            return v.mm_tmp.at[pl.ds(pl.multiple_of(slot * 256, 256), 256)]

        def out(step):
            at = pl.multiple_of(step * 256, 256)
            slot = lax.rem(step, 2)
            return pltpu.make_async_copy(staged(slot), v.out_grads.at[pl.ds(at, 256)], v.osem.at[4 + slot])

        def place(step, carry):
            at = pl.multiple_of(step * 256, 256)
            v.tmp[0:288, :] = pltpu.roll(full_of(v.gath[pl.ds(at, 288), :]), lax.rem(LANES - shift, LANES), 1)
            pl.when(step > first + 1)(out(step - 2).wait)
            staged(lax.rem(step, 2))[...] = jnp.where(near, v.tmp[pl.ds(skip, 256), :], v.tmp[pl.ds(skip + 1, 256), :])
            out(step).start()
            return carry

        lax.fori_loop(first, last, place, 0)
        for step in (last - 2, last - 1):
            out(step).wait()

    def bias_base(self):
        return flat_rows()[1] // 16 * 16

    def bias_core(self):
        v = self.v
        self.b1 = remote(v.bown, v.bcore, v.bsend.at[0], v.brecv.at[0], {DP: v.mate})
        self.b1.start()

    def bias_across(self):
        v = self.v
        self.b1.wait()
        v.btwo[...] = v.bown[...] + v.bcore[...]
        self.b2 = remote(v.btwo, v.bacross, v.bsend.at[1], v.brecv.at[1], {DP: v.other})
        self.b2.start()

    def bias_stripes(self):
        v = self.v
        self.b2.wait()
        v.bfour[...] = v.btwo[...] + v.bacross[...]
        self.b3 = Swap(v, 8, v.bfour, v.ball, True)
        self.b3.start()

    def bias_end(self):
        v = self.v
        self.b3.receive()
        self.b3.sent()
        v.ball[v.spot] = v.bfour[...]
        v.bsum[...] = jnp.sum(v.ball[...], axis=0)


def ones_sum(g):
    return mm(jnp.ones((8, g.shape[0]), jnp.bfloat16), g)[0:1, :]


def keep_bias(v, name, value):
    for block in range(-(-value.shape[1] // 128)):
        at = BIAS_AT[name] + block
        v.gbias[at : at + 1, :] = value[:, block * 128 : (block + 1) * 128]


def gradients_gru(v, gates_name, cand_name, parts, g_of):
    starts, _, _, _ = flat_rows()
    total = 0.0
    for b in range(BATCH):
        total = total + ones_sum(g_of(b))
    keep_bias(v, gates_name, total[:, 0:256])
    keep_bias(v, cand_name, total[:, 256:384])

    def taps(number, first, last):
        return lambda b: join(parts(t)[number](b) for t in range(first, last))

    state = tn_all(taps(0, 0, 5), g_of, 0, 256)
    for t in range(5):
        pack_pairs(v.flat, t * 384, 128, state[t * 128 : (t + 1) * 128, 0:128], state[t * 128 : (t + 1) * 128, 128:256])
    state = tn_all(taps(2, 0, 5), g_of, 256, 384)
    for t in range(5):
        v.mm_tmp[pl.ds(MARGIN + t * 384, 128), :] = state[t * 128 : (t + 1) * 128, :]
    for first, last in ((0, 2), (2, 4), (4, 5)):
        inputs = tn_all(taps(1, first, last), g_of, 0, 384)
        for t in range(first, last):
            rows = slice((t - first) * 256, (t - first + 1) * 256)
            pack_pairs(v.flat, t * 384 + 128, 256, inputs[rows, 0:128], inputs[rows, 128:256])
            v.mm_tmp[pl.ds(MARGIN + t * 384 + 128, 256), :] = inputs[rows, 256:384]
    v.flush.layer(starts[gates_name], 3840)
    cast_rows(v.flat, MARGIN, v.mm_tmp, MARGIN, 1920, jnp.float32)
    v.flush.layer(starts[cand_name], 1920)


def tn_all(part, g_of, low, high):
    return tn(join((part(b) for b in range(BATCH)), 0), join((g_of(b, low, high) for b in range(BATCH)), 0))


def gradients_heads(v):
    starts, _, _, _ = flat_rows()
    total = 0.0
    for b in range(BATCH):
        total = total + ones_sum(v.hgo[b])
    keep_bias(v, FLOW_HIDDEN, total[:, 0:256])
    keep_bias(v, MASK_HIDDEN, total[:, 256:512])
    for name, lane in ((FLOW_HIDDEN, 0), (MASK_HIDDEN, 256)):
        grads = join((v.hgo[b, :, lane : lane + 256] for b in range(BATCH)), 0)
        for group in range(3):
            taps = [join(heads_part(v, b, group * 3 + c)[...] for c in range(3)) for b in range(BATCH)]
            value = tn(join(taps, 0), grads)
            for c in range(3):
                rows = slice(c * 128, (c + 1) * 128)
                pack_pairs(v.flat, (group * 3 + c) * 128, 128, value[rows, 0:128], value[rows, 128:256])
        v.flush.layer(starts[name], 2304)

    total = 0.0
    sums = 0.0
    for b in range(BATCH):
        total = total + mm(v.dtb[b], v.feat[b])
        sums = sums + jnp.sum(full_of(half_of(v.dg[b])), axis=1, keepdims=True)
    lane1 = lane_index((1, LANES))
    at = BIAS_AT[FLOW_OUT]
    v.gbias[at : at + 1, :] = jnp.where(lane1 == 0, sums[0:1, :], jnp.where(lane1 == 1, sums[1:2, :], 0.0))
    v.fo_tmp[...] = total[:, 0:128]
    v.fo_tmp2[...] = total[:, 128:256]
    for quarter in range(4):
        value = 0.0
        for which in range(2):
            rows = jnp.concatenate(
                [v.fo_tmp[pl.ds(which, 9, stride=2), :], v.fo_tmp2[pl.ds(which, 9, stride=2), :]], axis=1
            )
            value = value + nt(half_of(rows), split_pick(which, quarter))
        v.flat[pl.ds(MARGIN + quarter, 9, stride=4), :] = value
    v.flush.layer(starts[FLOW_OUT], 36)

    lane = lane_index((128, LANES))
    low_half = lane < 64
    even, odd = [], []
    total = 0.0
    for b in range(BATCH):
        total = total + ones_sum(quarter_of(v.grad_mask[b]))
    for block in range(5):
        wide = min(128, MASK - block * 128)
        at = BIAS_AT[MASK_OUT] + block
        v.gbias[at : at + 1, 0:wide] = total[:, block * 128 : block * 128 + wide]
        value = 0.0
        for b in range(BATCH):
            value = value + tn(v.mf[b], quarter_of(v.grad_mask[b, :, block * 128 : block * 128 + wide]))
        v.pair_a[:, 0:wide] = value
        even.append(v.pair_a[pl.ds(0, 128, stride=2), :])
        odd.append(pltpu.roll(v.pair_a[pl.ds(1, 128, stride=2), :], 64, 1))
    for i in range(4):
        v.flat[pl.ds(MARGIN + i, 128, stride=9), :] = even[i]
    v.flat[pl.ds(MARGIN + 4, 128, stride=9), :] = jnp.where(low_half, even[4], odd[0])
    for i in range(4):
        v.flat[pl.ds(MARGIN + 5 + i, 128, stride=9), :] = jnp.where(low_half, odd[i], odd[i + 1])
    v.flush.layer(starts[MASK_OUT], 1152)


def rows_back(v):
    v.back_state.receive()
    take_own(v, v.a_state, v.b_state)
    unpack_back(v, v.b_state, v.state)

    def image(b, carry):
        r = v.state[b]
        s = full_of(v.net[b])
        update, reset, cand = v.ru[b], v.rr[b], v.rc[b]
        cg = full_of(half_of(r * update * (1.0 - cand * cand)))
        spread_five(v, cg, None, 256, True)
        reset_grad = nt(
            join(taps_part(v, t, 256, 384)[...] for t in range(5)),
            join(v.w_rs[t * 128 : (t + 1) * 128, 256:384] for t in range(5)),
        )
        low = full_of(half_of(r * (cand - s) * update * (1.0 - update)))
        high = full_of(half_of(reset_grad * s * reset * (1.0 - reset)))
        spread_five(v, low, None, 0, True)
        spread_five(v, high, None, 128, True)
        v.gr[b] = taps_part(v, 2, 0, 384)[...]
        state_grad = r * (1.0 - update) + reset_grad * reset
        state_grad = state_grad + nt(
            join(taps_part(v, t, 0, 256)[...] for t in range(5)),
            join(v.w_rs[t * 128 : (t + 1) * 128, 0:256] for t in range(5)),
        )
        v.ru[b] = state_grad
        inputs_grad = nt(
            join(taps_part(v, t, 0, 384)[...] for t in range(5)),
            join(v.w_ri[t * 256 : (t + 1) * 256, :] for t in range(5)),
        )
        v.rr[b] = inputs_grad[:, 0:128]
        v.rc[b] = inputs_grad[:, 128:256]
        return carry

    lax.fori_loop(0, BATCH, image, 0)
    v.store_gnet.start()
    v.back_context.receive()
    v.back_motion.receive()
    take_own(v, v.a_context, v.b_context)
    take_own(v, v.a_motion, v.b_motion)
    unpack_back(v, v.b_context, v.lr)
    unpack_back(v, v.b_motion, v.lu)

    def total(b, carry):
        v.rr[b] = v.rr[b] + v.lr[b]
        motion = v.rc[b] + v.lu[b]
        v.mge[b, 256:896, :] = half_of(motion * full_of(v.slope_m[b]))
        high = half_of(motion)
        low = half_of(motion - full_of(high))
        pick = half_of(jnp.where(lane_index((16, LANES)) == row_index((16, LANES)) + 126, 1.0, 0.0))
        v.gf_base[b] = (nt(pick, high) + nt(pick, low))[0:8, :]
        return carry

    lax.fori_loop(0, BATCH, total, 0)
    v.halo_mg.start()
    v.store_gctx.start()


def branch_back(v):
    v.halo_mg.receive()

    def image(b, carry):
        up = jnp.where(v.spot > 0, full_of(v.mge[b, 0:256, :]), 0.0)
        own = full_of(v.mge[b, 256:896, :])
        down = jnp.where(v.spot < v.space - 1, full_of(v.mge[b, 896:1152, :]), 0.0)
        spread_rows(v, 0, (jnp.concatenate([up, own, down], axis=0),), 1152, v.xi, 0, 128, True)
        joint = nt(
            join(v.xi[(2 - a) * 128 : (2 - a) * 128 + 896, 0:384] for a in range(3)),
            join(v.w_mm[k * 256 : (k + 1) * 256, :] for k in range(9)),
        )
        branch = joint * full_of(v.slope_j[b])
        low = full_of(half_of(edge_rows(v, branch[:, 0:128], WIDE)))
        high = full_of(half_of(edge_rows(v, branch[:, 128:256], WIDE)))
        spread_rows(v, 0, (low, high), 896, v.hx_j.at[b], 0, 256, True)
        return carry

    lax.fori_loop(0, BATCH, image, 0)


def branch_own(v, b, low=0, high=256):
    return v.hx_j[b, 128:768, 256 + low : 256 + high]


def flow_back(v):
    def image(b, carry):
        rows = [slice((2 - a) * 128, (2 - a) * 128 + 640) for a in range(3)]
        flow_grad = nt(
            join(v.hx_j[b, rows[a], c * 256 + 128 : (c + 1) * 256] for a in range(3) for c in range(3)),
            join(v.w_fm[k * 128 : (k + 1) * 128, :] for k in range(9)),
        )
        v.fpg[b] = half_of(flow_grad * full_of(v.slope_fi[b]))
        z = nt(v.w_fi[...], v.fpg[b])
        total = jnp.zeros((32, LANES), jnp.float32)
        lane = lane_index((32, LANES))
        for across in range(7):
            v.fs[across] = jnp.zeros((32, LANES), jnp.float32)
            for y in range(ROWS):
                v.fs[across, 2 * y : 2 * y + 16, :] += z[across * 16 : across * 16 + 16, y * 128 : (y + 1) * 128]
            d = across - 3
            value = v.fs[across]
            if d:
                value = pltpu.roll(value, d % LANES, 1)
                value = jnp.where((lane - d >= 0) & (lane - d < WIDE), value, 0.0)
            total = total + value
        v.gf[b] = total
        return carry

    lax.fori_loop(0, BATCH, image, 0)
    v.halo_gf.start()


def gcorr_store(v):
    return pltpu.make_async_copy(v.flat.at[0 : ROWS * CORR * BATCH], v.out_gcorr, v.gsem)


def corr_back(v):
    def image(b, carry):
        corr_grad = nt(
            join(v.hx_j[b, (2 - a) * 128 : (2 - a) * 128 + 640, :] for a in range(3)),
            join(v.w_cm[k * 256 : (k + 1) * 256, :] for k in range(9)),
        )
        v.cpg[b] = half_of(corr_grad * full_of(v.slope_ci[b]))
        gcorr = nt(v.w_ci[...], v.cpg[b])
        for y in range(ROWS):
            v.flat[pl.ds(y * BATCH * CORR + b, CORR, stride=BATCH), :] = gcorr[:, y * WIDE : (y + 1) * WIDE]
        return carry

    lax.fori_loop(0, BATCH, image, 0)
    gcorr_store(v).start()


def summed(v, ref, name):
    total = 0.0
    for b in range(BATCH):
        total = total + ones_sum(ref(b))
    keep_bias(v, name, total)


def gradients_motion(v):
    starts = flat_rows()[0]
    summed(v, lambda b: v.mge[b, 256:896, :], MOTION_MIX)
    grads = join((v.mge[b, 256:896, :] for b in range(BATCH)), 0)
    for a in range(3):
        taps = join((v.hx_j[b, a * 128 : a * 128 + 640, :] for b in range(BATCH)), 0)
        v.mm_tmp[a * 768 : (a + 1) * 768, :] = tn(taps, grads)
    lane36 = lane_index((36, LANES))
    for r in range(63):
        first = v.mm_tmp[pl.ds(r, 36, stride=64), :]
        second = v.mm_tmp[pl.ds(r + 1, 36, stride=64), :]
        if r:
            first = pltpu.roll(first, LANES - 2 * r, 1)
        second = pltpu.roll(second, 126 - 2 * r, 1)
        v.flat[pl.ds(MARGIN + r, 36, stride=63), :] = jnp.where(lane36 < 126 - 2 * r, first, second)
    v.flush.layer(starts[MOTION_MIX], 2268)


def gradients_branches(v):
    starts = flat_rows()[0]
    summed(v, lambda b: branch_own(v, b), CORR_MIX)
    summed(v, lambda b: branch_own(v, b, 128, 256), FLOW_MIX)
    grads = join((branch_own(v, b, 128, 256) for b in range(BATCH)), 0)
    for k in range(9):
        a, c = k // 3, k % 3
        if c == 0:
            taps = join((v.hx_f[b, (a + 1) * 128 : (a + 1) * 128 + 640, :] for b in range(BATCH)), 0)
            group = tn(taps, grads)
        v.pair_a[0:128, :] = group[c * 128 : (c + 1) * 128]
        even, odd = (v.pair_a[pl.ds(i, 64, stride=2), :] for i in range(2))
        v.flat[MARGIN + 64 * k : MARGIN + 64 * (k + 1), :] = jnp.where(
            lane_index((64, LANES)) < 64, pltpu.roll(even, 64, 1), odd
        )
    v.flush.layer(starts[FLOW_MIX], 576)

    low_half = lane_index((128, LANES)) < 64
    grads = join((branch_own(v, b) for b in range(BATCH)), 0)
    for k in range(9):
        a, c = k // 3, k % 3
        if c == 0:
            taps = join((v.hx_c[b, (a + 1) * 128 : (a + 1) * 128 + 640, :] for b in range(BATCH)), 0)
            group = tn(taps, grads)
        v.pair_a[...] = group[c * 256 : (c + 1) * 256, 0:128]
        v.pair_b[...] = group[c * 256 : (c + 1) * 256, 128:256]
        even, odd = (v.pair_a[pl.ds(i, 128, stride=2), :] for i in range(2))
        even_high, odd_high = (v.pair_b[pl.ds(i, 128, stride=2), :] for i in range(2))
        odd, odd_high = pltpu.roll(odd, 64, 1), pltpu.roll(odd_high, 64, 1)
        at = MARGIN + 384 * k
        v.flat[pl.ds(at, 128, stride=3), :] = even
        v.flat[pl.ds(at + 1, 128, stride=3), :] = jnp.where(low_half, even_high, odd)
        v.flat[pl.ds(at + 2, 128, stride=3), :] = jnp.where(low_half, odd, odd_high)
    v.flush.layer(starts[CORR_MIX], 3456)


def gradients_flow_in(v):
    starts = flat_rows()[0]
    summed(v, lambda b: v.fpg[b], FLOW_IN)
    value = 0.0
    for b in range(BATCH):
        value = value + mm(v.xt[b, :, 256:896], v.fpg[b])
    v.flow_tmp[...] = value
    for across in range(7):
        for comp in range(2):
            v.flat[pl.ds(MARGIN + across * 2 + comp, 7, stride=14), :] = v.flow_tmp[
                pl.ds(across * 16 + comp, 7, stride=2), :
            ]
    v.flush.layer(starts[FLOW_IN], 98)


def gradients_corr_in(v):
    starts = flat_rows()[0]
    summed(v, lambda b: v.cpg[b], CORR_IN)
    value = 0.0
    for b in range(BATCH):
        value = value + mm(lines_of(v.corr, b, ROWS), v.cpg[b])
    gcorr_store(v).wait()
    pack_pairs(v.flat, 0, 324, value[:, 0:128], value[:, 128:256])
    v.flush.layer(starts[CORR_IN], 648)


def bias_tile(v):
    starts, bias_row, spots, inner = flat_rows()
    lead = bias_row % 16
    lane1 = lane_index((1, LANES))
    v.bown[...] = jnp.zeros_like(v.bown)
    for name, height, width in shapes():
        for block in range(-(-width // LANES)):
            value = v.gbias[BIAS_AT[name] + block : BIAS_AT[name] + block + 1, :]
            if name == FLOW_MIX:
                value = pltpu.roll(value, 64, 1)
            left = width - block * LANES
            if left < LANES:
                value = jnp.where(lane1 < left, value, 0.0)
            at = spots[name] + block * LANES
            row, shift = lead + at // LANES, at % LANES
            moved = pltpu.roll(value, shift, 1) if shift else value
            v.bown[row : row + 1, :] = v.bown[row : row + 1, :] + jnp.where(lane1 >= shift, moved, 0.0)
            if shift:
                v.bown[row + 1 : row + 2, :] = v.bown[row + 1 : row + 2, :] + jnp.where(lane1 < shift, moved, 0.0)


def finish(v):
    spot, last = v.spot, v.space - 1
    v.halo_gf.receive()
    for b in range(BATCH):
        v.tmp2[...] = v.gf[b]
        up = jnp.where(spot > 0, v.gf_up[b], 0.0)
        down = jnp.where(spot < last, v.gf_down[b], 0.0)
        v.tmp2[6:12, :] += up[16:22, :]
        v.tmp2[10:16, :] += down[0:6, :]
        for y in range(ROWS):
            v.out_gflow[b, y] = (
                v.tmp2[6 + 2 * y : 8 + 2 * y, :] + v.gf_base[b, 0:2, y * 128 : (y + 1) * 128]
            )
    v.loss_in[v.spot] = v.losses[...]
    total = jnp.sum(v.loss_in[...], axis=0)
    counts = jnp.sum(v.counts[...], axis=0)
    value = total / jnp.maximum(counts, 1.0)
    for b in range(BATCH):
        v.out_loss[b] = v.pick_count(value, b)


class View:
    pass


def main_kernel(names, space, count, *refs):
    v = View()
    for name, ref in zip(names, refs):
        setattr(v, name, ref)
    v.space = space
    v.lu, v.lc = v.motion, v.state
    v.spot = lax.axis_index(SPACE)
    v.rank = lax.axis_index(DP)
    v.mate, v.other, v.twin = mate_of(v.rank), lax.rem(v.rank + 2, 4), mate_of(v.spot)
    spot = v.spot
    barrier = pltpu.get_barrier_semaphore()

    def hello(step, carry):
        pl.semaphore_signal(barrier, inc=1, device_id={SPACE: lax.rem(spot + step, space)}, device_id_type=MESH)
        return carry

    lax.fori_loop(1, space, hello, 0)
    for turn in range(1, 4):

        def greet_rank(step, carry):
            place = lax.rem(spot + step, space)
            device = {DP: lax.rem(v.rank + turn, 4), SPACE: place}
            pl.semaphore_signal(barrier, inc=1, device_id=device, device_id_type=MESH)
            return carry

        lax.fori_loop(0, space, greet_rank, 0)
    pl.semaphore_wait(barrier, 4 * space - 1)

    v.store_gnet = pltpu.make_async_copy(v.ru, v.out_gnet, v.osem.at[0])
    v.store_gctx = pltpu.make_async_copy(v.rr, v.out_gctx, v.osem.at[1])
    rows = row_index((8, LANES))
    counted = jnp.zeros((8, LANES), jnp.float32)
    for b in range(BATCH):
        counted = jnp.where(rows == b, jnp.sum(v.valid[b].astype(jnp.float32)), counted)
    v.count_out[...] = counted
    v.pick_count = lambda counts, b: jnp.sum(jnp.where((rows == b) & (lane_index((8, LANES)) == 0), counts, 0.0))
    v.swap_count = Swap(v, 0, v.count_out, v.counts, True)
    v.swap_context = Swap(v, 1, v.a_context, v.b_context)
    v.swap_motion = Swap(v, 2, v.a_motion, v.b_motion)
    v.swap_state = Swap(v, 3, v.a_state, v.b_state)
    v.back_context = Swap(v, 4, v.a_context, v.b_context)
    v.back_motion = Swap(v, 5, v.a_motion, v.b_motion)
    v.back_state = Swap(v, 6, v.a_state, v.b_state)
    v.swap_loss = Swap(v, 7, v.losses, v.loss_in, True)
    v.halo_corr = Halo(v, 0, v.corr.at[:, 0:2], v.corr.at[:, 3:5], v.corr_down, v.corr_up)
    v.halo_flow = Halo(v, 1, v.flow, v.flow, v.flow_down, v.flow_up)
    v.halo_final = Halo(v, 2, v.e_left, v.e_right, v.f_right, v.f_left)
    v.halo_mask = Halo(v, 3, v.m_left, v.m_right, v.n_right, v.n_left)
    v.halo_dg = Halo(v, 4, v.dg, v.dg, v.dg_right, v.dg_left)
    v.halo_mg = Halo(v, 5, v.mge.at[:, 256:512], v.mge.at[:, 640:896], v.mge.at[:, 896:1152], v.mge.at[:, 0:256])
    v.halo_gf = Halo(v, 6, v.gf, v.gf, v.gf_down, v.gf_up)

    load = pltpu.make_async_copy(v.local, v.gath.at[0:BLOCK], v.lsem)
    load.start()
    for b in range(BATCH):
        for y in range(ROWS):
            v.flow[b, 2 * y : 2 * y + 2, :] = full_of(v.flow_in[b, y])
        v.flow[b, 2 * ROWS : 16, :] = jnp.zeros((16 - 2 * ROWS, LANES), jnp.float32)
    v.halo_flow.start()
    v.halo_corr.start()
    v.swap_count.start()
    load.wait()
    gather_start(v, count)

    def first(b, carry):
        v.state[b] = full_of(v.context[b])
        pack_rows(v, v.state, b, v.a_context)
        return carry

    lax.fori_loop(0, BATCH, first, 0)
    v.swap_context.start()
    v.halo_flow.receive()
    widen_all(v)
    gather_pass(v, 0, 0, 2)
    early_taps(v)
    gather_pass(v, 0, 2, 4)
    for copy in v.g_own[1:]:
        copy.wait_recv()
    for copy in v.g_x[1]:
        copy.start()
    columns_zero(v)
    gather_turn(v, 0)
    unpack_encoder(v, count)
    v.halo_corr.receive()
    forward_rows(v)
    keep = [pltpu.make_async_copy(v.hx_c, v.out_keep_c, v.ksem.at[0]), pltpu.make_async_copy(v.hx_f, v.out_keep_f, v.ksem.at[1])]
    for copy in keep:
        copy.start()
    unpack_heads(v)
    v.swap_context.receive()
    v.swap_motion.receive()
    v.swap_state.receive()
    take_own(v, v.a_context, v.b_context)
    take_own(v, v.a_motion, v.b_motion)
    take_own(v, v.a_state, v.b_state)
    columns_in(v)
    columns_forward(v)
    mask_gradient(v)
    for copy in keep:
        copy.wait()
    heads(v)
    mask_output(v)
    v.swap_context.sent()
    v.swap_motion.sent()
    v.swap_state.sent()
    heads_back(v)
    v.flush = Flush(v)
    red = v.reduce = Reduce(v, count)
    gradients_heads(v)
    v.back_context.start()
    v.back_motion.start()
    red.offer(0)
    red.tick()
    gradients_gru(
        v,
        COLUMNS_GATES,
        COLUMNS_CANDIDATE,
        lambda t: (
            lambda b: v.xc[b, t * COLS : t * COLS + AREA, 0:128],
            lambda b: v.xc[b, t * COLS : t * COLS + AREA, 128:384],
            lambda b: v.xcr[b, t * COLS : t * COLS + AREA, :],
        ),
        lambda b, low=0, high=384: v.gc[b, 32 : 32 + AREA, low:high],
    )
    red.offer(1, 2)
    red.tick()
    rows_back(v)
    red.tick()
    keep = [
        pltpu.make_async_copy(v.out_keep_c, v.hx_c, v.ksem.at[0]),
        pltpu.make_async_copy(v.out_keep_f, v.hx_f, v.ksem.at[1]),
    ]
    for copy in keep:
        copy.start()
    gradients_gru(
        v,
        ROWS_GATES,
        ROWS_CANDIDATE,
        lambda t: (
            lambda b: v.xs[b * AREA : (b + 1) * AREA, t * 128 : (t + 1) * 128],
            lambda b: v.xi[b * AREA : (b + 1) * AREA, t * 256 : (t + 1) * 256],
            lambda b: v.xr[b * AREA : (b + 1) * AREA, t * 128 : (t + 1) * 128],
        ),
        lambda b, low=0, high=384: v.gr[b, :, low:high],
    )
    red.offer(3, 4)
    red.tick()
    gradients_motion(v)
    red.offer(5)
    red.tick()
    branch_back(v)
    red.tick()
    for copy in keep:
        copy.wait()
    gradients_branches(v)
    red.offer(6, now=True)
    red.tick()
    flow_back(v)
    gradients_flow_in(v)
    red.offer(7, now=True)
    red.tick()
    corr_back(v)
    red.tick()
    gradients_corr_in(v)
    bias_tile(v)
    red.bias_core()
    red.offer(8, now=True)
    red.tick()
    finish(v)
    red.bias_across()
    red.tick()
    red.bias_stripes()
    red.tick()
    red.bias_end()
    red.ready()
    pl.when(v.rank > 0)(lambda: red.lay(0, 24))
    pl.when(v.rank == 0)(lambda: red.lay(4, 15))
    red.tick()
    pl.when(v.rank == 0)(lambda: red.lay(15, 24))
    pl.when(v.rank == 0)(lambda: red.lay(0, 4))
    assert not red.flying and not red.queue
    red.settle()
    for swap in (v.swap_count, v.back_context, v.back_motion, v.back_state, v.swap_loss):
        swap.sent()
    for halo in (v.halo_corr, v.halo_flow, v.halo_final, v.halo_mask, v.halo_dg, v.halo_mg, v.halo_gf):
        halo.sent()
    v.store_gnet.wait()
    v.store_gctx.wait()
    pltpu.make_async_copy(v.mask_low, v.out_mask.at[0], v.osem.at[3]).wait()


def main_call(space, count, local, net, context, corr, flow, target, valid, grad_net, grad_mask):
    total = 3 * count // (LANES * 16) * 16 + BLOCK
    low, wide = jnp.bfloat16, jnp.float32
    peers = (space, BATCH, ROWS * COLS, LANES)
    ins = dict(
        local=local, net=net, context=context, corr=corr, flow_in=flow, target=target, valid=valid,
        grad_net=grad_net, grad_mask=grad_mask,
    )
    outs = dict(
        out_net=((BATCH, AREA, 128), low),
        out_flow=((BATCH, 2, COLS, TALL), wide),
        out_mask=((BATCH, AREA, MASK), low),
        out_loss=((BATCH,), wide),
        out_flat=((total, 128), low),
        out_gnet=((BATCH, AREA, 128), wide),
        out_gctx=((BATCH, AREA, 128), wide),
        out_gcorr=((ROWS * CORR * BATCH, 128), wide),
        out_gflow=((BATCH, ROWS, 2, 128), wide),
        out_keep_c=((BATCH, 1152, 768), low),
        out_keep_f=((BATCH, 1152, 384), low),
        out_all=((4 * BLOCK, 128), low),
        out_grads=((BLOCK, 128), wide),
    )
    scratch = dict(
        stage=((2, 3904, 128), low),
        seam=((16, 16, 128), wide),
        mask_low=((AREA, MASK), low),
        seam_low=((16 * 20, 128), low),
        own=((2, SHARE // 2, 128), low),
        rcore=((2, SHARE // 2, 128), low),
        tx=((2, SHARE // 4, 128), low),
        rx=((2, SHARE // 4, 128), low),
        ks=((2, SHARE // 4, 128), wide),
        ts=((2, SHARE // 4, 128), low),
        acc=((2, SHARE // 4 // space, 128), wide),
        rs=((2, space, SHARE // 4 // space, 128), low),
        fin=((2, SHARE // 4 // space, 128), low),
        dall=((4, 256, 128), low),
        bz=((64, 128), low),
        ty=((2, SHARE // 8, 128), low),
        ry=((2, SHARE // 8, 128), low),
        ky=((2, SHARE // 8, 128), wide),
        tz=((2, SHARE // 8, 128), low),
        rz=((2, space // 2, SHARE // 4 // space, 128), low),
        kz=((2, SHARE // 4 // space, 128), wide),
        az=((3, SHARE // 8, 128), low),
        gath=((2 * SHARE + 32, 128), low),
        bown=((32, 128), wide), bcore=((32, 128), wide), btwo=((32, 128), wide), bacross=((32, 128), wide),
        bfour=((32, 128), wide), ball=((space, 32, 128), wide), bsum=((32, 128), wide),
        flat=((3904, 128), wide),
        pair_a=((256, 128), wide),
        pair_b=((256, 128), wide),
        flow_tmp=((112, 128), wide),
        mm_tmp=((3 * (2 * EDGE + SPREAD), 128), wide),
        fo_tmp=((32, 128), wide),
        fo_tmp2=((32, 128), wide),
        w_ci=((CORR, 256), low),
        w_cm=((2304, 256), low),
        w_fi=((112, 128), low),
        w_fm=((1152, 128), low),
        w_mm=((2304, 128), low),
        w_ri=((1280, 384), low),
        w_rs=((640, 384), low),
        w_li=((1280, 384), low),
        w_ls=((640, 384), low),
        w_h=((1152, 512), low),
        w_fo=((32, 256), low),
        w_mo=((256, 640), low),
        bias=((BIAS_ROWS, 128), wide),
        gbias=((BIAS_ROWS, 128), wide),
        corr_up=((BATCH, 2, CORR, 128), low),
        corr_down=((BATCH, 2, CORR, 128), low),
        flow_up=((BATCH, 16, 128), wide),
        flow_down=((BATCH, 16, 128), wide),
        fs=((7, 32, 128), wide),
        xt=((BATCH, 112, 1152), low),
        tmp=((1168, 128), wide),
        tmp2=((32, 128), wide),
        hx_c=((BATCH, 1152, 768), low),
        hx_f=((BATCH, 1152, 384), low),
        hx_j=((BATCH, 896, 768), low),
        slope_ci=((BATCH, AREA, 256), low),
        slope_fi=((BATCH, AREA, 128), low),
        slope_j=((BATCH, 896, 256), low),
        slope_m=((BATCH, AREA, 128), low),
        motion=((BATCH, AREA, 128), wide),
        state=((BATCH, AREA, 128), wide),
        xi=((BATCH * AREA, 1280), low),
        xs=((BATCH * AREA, 640), low),
        xr=((BATCH * AREA, 640), low),
        ru=((BATCH, AREA, 128), wide),
        rr=((BATCH, AREA, 128), wide),
        rc=((BATCH, AREA, 128), wide),
        lr=((BATCH, AREA, 128), wide),
        a_state=(peers, low), a_context=(peers, low), a_motion=(peers, low),
        b_state=(peers, low), b_context=(peers, low), b_motion=(peers, low),
        xc=((BATCH, AREA + 64, 384), low),
        xcr=((BATCH, AREA + 64, 128), low),
        gc=((BATCH, AREA + 64, 384), low),
        final=((AREA, 128), wide),
        e_left=((BATCH, 2, 48, 128), low), e_right=((BATCH, 2, 48, 128), low),
        f_left=((BATCH, 2, 48, 128), low), f_right=((BATCH, 2, 48, 128), low),
        m_left=((BATCH, 2, 48, 128), low), m_right=((BATCH, 2, 48, 128), low),
        n_left=((BATCH, 2, 48, 128), low), n_right=((BATCH, 2, 48, 128), low),
        slope_h=((BATCH, SPREAD, 512), low),
        feat=((BATCH, SPAN, 256), low),
        mf=((BATCH, AREA, 256), low),
        dg=((BATCH, 8, SPAN), wide),
        target_wide=((BATCH, 8, SPAN), wide),
        valid_wide=((BATCH, 8, SPAN), wide),
        flow=((BATCH, 16, 128), wide),
        dg_left=((BATCH, 8, SPAN), wide), dg_right=((BATCH, 8, SPAN), wide),
        dt=((32, SPAN), wide),
        dto=((32, SPAN), wide),
        dtb=((BATCH, 32, SPAN), low),
        hgo=((BATCH, SPREAD, 512), low),
        gr=((BATCH, AREA, 384), low),
        mge=((BATCH, 1152, 128), low),
        cpg=((BATCH, AREA, 256), low),
        fpg=((BATCH, AREA, 128), low),
        gf_base=((BATCH, 8, AREA), wide),
        gf=((BATCH, 32, 128), wide), gf_up=((BATCH, 32, 128), wide), gf_down=((BATCH, 32, 128), wide),
        count_out=((8, 128), wide), counts=((space, 8, 128), wide),
        losses=((8, 128), wide), loss_in=((space, 8, 128), wide),
    )
    sems = dict(
        hsend=pltpu.SemaphoreType.DMA((7, 2)), hrecv=pltpu.SemaphoreType.DMA((7, 2)),
        asend=pltpu.SemaphoreType.DMA((9,)), arecv=pltpu.SemaphoreType.DMA((9,)),
        ssem=pltpu.SemaphoreType.DMA((2, 2)),
        fsem=pltpu.SemaphoreType.DMA((17,)),
        rsend=pltpu.SemaphoreType.DMA((3, 2)), rrecv=pltpu.SemaphoreType.DMA((3, 2)),
        z1send=pltpu.SemaphoreType.DMA((2,)), z1recv=pltpu.SemaphoreType.DMA((2,)),
        z2send=pltpu.SemaphoreType.DMA((3,)), z2recv=pltpu.SemaphoreType.DMA((3,)),
        osend=pltpu.SemaphoreType.DMA((3,)), orecv=pltpu.SemaphoreType.DMA((9,)),
        rlocal=pltpu.SemaphoreType.DMA((2,)),
        s2send=pltpu.SemaphoreType.DMA((2,)), s2recv=pltpu.SemaphoreType.DMA((2,)),
        fsend=pltpu.SemaphoreType.DMA((2,)), frecv=pltpu.SemaphoreType.DMA((9,)),
        ysend=pltpu.SemaphoreType.DMA((9,)), yrecv=pltpu.SemaphoreType.DMA((9,)),
        dsend=pltpu.SemaphoreType.DMA, drecv=pltpu.SemaphoreType.DMA,
        bsend=pltpu.SemaphoreType.DMA((2,)), brecv=pltpu.SemaphoreType.DMA((2,)),
        ksem=pltpu.SemaphoreType.DMA((2,)),
        gsend=pltpu.SemaphoreType.DMA((9, 8)), grecv=pltpu.SemaphoreType.DMA((9, 8)), lsem=pltpu.SemaphoreType.DMA,
        gsem=pltpu.SemaphoreType.DMA,
        osem=pltpu.SemaphoreType.DMA((6,)),
    )
    vmem = pl.BlockSpec(memory_space=pltpu.VMEM)
    hbm = pl.BlockSpec(memory_space=pl.ANY)
    names = list(ins) + list(outs) + list(scratch) + list(sems)
    return pl.pallas_call(
        functools.partial(main_kernel, names, space, count),
        out_shape=[jax.ShapeDtypeStruct(*entry) for entry in outs.values()],
        in_specs=[hbm if name == "local" else vmem for name in ins],
        out_specs=[pl.BlockSpec(memory_space=pltpu.SMEM) if name == "out_loss" else hbm if name in ("out_flat", "out_gnet", "out_gctx", "out_gcorr", "out_keep_c", "out_keep_f", "out_mask", "out_grads", "out_all") else vmem for name in outs],
        scratch_shapes=[pltpu.VMEM(*entry) for entry in scratch.values()] + list(sems.values()),
        compiler_params=pltpu.CompilerParams(
            collective_id=2, has_side_effects=True, vmem_limit_bytes=VMEM_LIMIT
        ),
    )(*ins.values())


VMEM_LIMIT = 64 * 2**20 - 2**16


def shards_wide(net, context, corr, flow, target, valid, grad_net, grad_mask, params):
    space = lax.axis_size(SPACE)
    count = params.shape[0]
    local = jnp.pad(params, (0, BLOCK * LANES - count)).reshape(BLOCK, LANES)
    outs = main_call(
        space, count, local, net.reshape(BATCH, AREA, HID), context.reshape(BATCH, AREA, CTX),
        jnp.transpose(corr, (0, 1, 3, 2)), jnp.transpose(flow, (0, 2, 1, 3)), jnp.transpose(target, (0, 1, 3, 2)),
        jnp.transpose(valid, (0, 2, 1)),
        grad_net.reshape(BATCH, AREA, HID), grad_mask.reshape(BATCH, AREA, MASK),
    )
    new_net, new_flow, mask, loss, _, gnet, gctx, gcorr, gflow = outs[:9]
    new_flow = jnp.transpose(new_flow, (0, 1, 3, 2))
    grads = outs[-1].reshape(-1)[:count]
    return (
        new_net.reshape(BATCH, TALL, COLS, HID),
        new_flow,
        mask.reshape(BATCH, TALL, COLS, MASK),
        loss,
        grads,
        gnet.reshape(BATCH, ROWS, WIDE, HID),
        gctx.reshape(BATCH, ROWS, WIDE, CTX),
        jnp.transpose(gcorr.reshape(ROWS, CORR, BATCH, WIDE), (2, 0, 3, 1)),
        jnp.transpose(gflow, (0, 2, 1, 3)),
    )


def solution(mesh):
    def plan(*arrays):
        net, valid = arrays[0], arrays[5]
        if (net.shape[1:3], valid.shape[1:]) == ((ROWS, WIDE), (TALL, COLS)):
            return shards_wide(*arrays)
        return shards(*arrays)

    return jax.shard_map(
        plan,
        mesh=mesh,
        in_specs=(
            P(DP, SPACE, None, None),
            P(DP, SPACE, None, None),
            P(DP, SPACE, None, None),
            P(DP, None, SPACE, None),
            P(DP, None, None, SPACE),
            P(DP, None, SPACE),
            P(DP, None, SPACE, None),
            P(DP, None, SPACE, None),
            P(DP),
        ),
        out_specs=(
            P(DP, None, SPACE, None),
            P(DP, None, None, SPACE),
            P(DP, None, SPACE, None),
            P(DP),
            P(DP),
            P(DP, SPACE, None, None),
            P(DP, SPACE, None, None),
            P(DP, SPACE, None, None),
            P(DP, None, SPACE, None),
        ),
        check_vma=False,
    )
```

```python
import functools

import jax
import jax.numpy as jnp
from jax import lax
from jax.experimental import pallas as pl
from jax.experimental.pallas import tpu as pltpu
from jax.sharding import PartitionSpec as P

HID = 128
CTX = 128
MOT = 128
CORR = 324
SPACE = "space"
DP = "dp"
(
    CORR_IN,
    CORR_MIX,
    FLOW_IN,
    FLOW_MIX,
    MOTION_MIX,
    ROWS_GATES,
    ROWS_CANDIDATE,
    COLUMNS_GATES,
    COLUMNS_CANDIDATE,
    FLOW_HIDDEN,
    FLOW_OUT,
    MASK_HIDDEN,
    MASK_OUT,
) = range(13)
C1 = 256
C2 = 192
F1 = 128
F2 = 64
HEAD = 256
MASK = 576


def with_halo(block, sides, width):
    for axis, dim in sides:
        count = lax.axis_size(axis)
        forward = [(i, i + 1) for i in range(count - 1)]
        backward = [(target, source) for source, target in forward]
        low = lax.ppermute(
            lax.slice_in_dim(block, block.shape[dim] - width, None, axis=dim), axis, forward
        )
        high = lax.ppermute(lax.slice_in_dim(block, 0, width, axis=dim), axis, backward)
        block = jnp.concatenate([low, block, high], axis=dim)
    return block


def shapes():
    inputs_width = HID + CTX + MOT
    return [
        (CORR_IN, CORR, C1),
        (CORR_MIX, 9 * C1, C2),
        (FLOW_IN, 98, F1),
        (FLOW_MIX, 9 * F1, F2),
        (MOTION_MIX, 9 * (C2 + F2), MOT - 2),
        (ROWS_GATES, 5 * inputs_width, 2 * HID),
        (ROWS_CANDIDATE, 5 * inputs_width, HID),
        (COLUMNS_GATES, 5 * inputs_width, 2 * HID),
        (COLUMNS_CANDIDATE, 5 * inputs_width, HID),
        (FLOW_HIDDEN, 9 * HID, HEAD),
        (FLOW_OUT, 9 * HEAD, 2),
        (MASK_HIDDEN, 9 * HID, HEAD),
        (MASK_OUT, HEAD, MASK),
    ]


def unpack(flat):
    weights = {}
    biases = {}
    offset = 0
    table = shapes()
    for name, height, width in table:
        weights[name] = flat[offset // LANES : (offset + height * width) // LANES].reshape(height, width)
        offset = offset + height * width
    rest = flat[offset // LANES :].reshape(-1)
    offset = 0
    for name, height, width in table:
        biases[name] = rest[offset : offset + width].astype(jnp.float32)
        offset = offset + width
    return (weights, biases)


def pack(grads, total):
    table = shapes()
    rows = [grads[entry[0]][0].astype(jnp.bfloat16).reshape(-1, LANES) for entry in table]
    biases = jnp.concatenate([grads[entry[0]][1] for entry in table]).astype(jnp.bfloat16)
    left = total * LANES - sum(entry[1] * entry[2] for entry in table) - biases.shape[0]
    return jnp.concatenate(rows + [jnp.pad(biases, (0, left)).reshape(-1, LANES)])


def patches(padded, tall, wide):
    out_rows = padded.shape[1] - tall + 1
    out_columns = padded.shape[2] - wide + 1
    return jnp.concatenate(
        [
            padded[:, down : down + out_rows, across : across + out_columns]
            for down in range(tall)
            for across in range(wide)
        ],
        axis=-1,
    )


def apply(stacked, weight):
    return jnp.einsum("bhwk,ko->bhwo", stacked, weight, preferred_element_type=jnp.float32)


def apply_back(grad, weight):
    return jnp.einsum("bhwo,ko->bhwk", grad, weight, preferred_element_type=jnp.float32)


def weight_grad(stacked, pre_grad):
    return jnp.einsum("bhwk,bhwo->ko", stacked, pre_grad, preferred_element_type=jnp.float32)


def record(grads, name, stacked, pre_grad):
    grads[name] = (
        weight_grad(stacked, pre_grad),
        jnp.sum(pre_grad, axis=(0, 1, 2), dtype=jnp.float32),
    )


def flipped(weight, tall, wide):
    inner = weight.shape[0] // (tall * wide)
    shaped = weight.reshape(tall, wide, inner, weight.shape[1])[::-1, ::-1]
    return jnp.transpose(shaped, (0, 1, 3, 2)).reshape(-1, inner)


def slope(pre):
    sigma = jax.nn.sigmoid(pre)
    return sigma * (1.0 + pre * (1.0 - sigma))


def local_pad(field, tall, wide):
    return jnp.pad(field, ((0, 0), (tall // 2, tall // 2), (wide // 2, wide // 2), (0, 0)))


def row_pad(field, tall):
    field = with_halo(field, ((SPACE, 1),), tall // 2)
    return jnp.pad(field, ((0, 0), (0, 0), (tall // 2, tall // 2), (0, 0)))


def column_pad(field, tall, wide):
    field = with_halo(field, ((SPACE, 2),), wide // 2)
    return jnp.pad(field, ((0, 0), (tall // 2, tall // 2), (0, 0), (0, 0)))


MESH = pl.DeviceIdType.MESH
LANES = 128
BLOCK = 6144


def quarter_start(rank, count):
    return lax.div(rank * count, LANES)


def quarter_base(rank, count):
    return lax.div(rank * count, LANES * 16) * 16


def mate_of(rank):
    return rank + 1 - 2 * lax.rem(rank, 2)


def remote(src, dst, send, recv, device):
    return pltpu.make_async_remote_copy(
        src_ref=src, dst_ref=dst, send_sem=send, recv_sem=recv, device_id=device, device_id_type=MESH
    )


def greet(devices):
    barrier = pltpu.get_barrier_semaphore()
    for device in devices:
        pl.semaphore_signal(barrier, inc=1, device_id=device, device_id_type=MESH)
    pl.semaphore_wait(barrier, len(devices))


def lane_matrix(shift, forward):
    source = lax.broadcasted_iota(jnp.int32, (LANES, 2 * LANES), 0)
    target = lax.broadcasted_iota(jnp.int32, (LANES, 2 * LANES), 1)
    if forward:
        return jnp.where(target == source + shift, 1.0, 0.0).astype(jnp.bfloat16)
    return jnp.where(lax.rem(target + LANES, 2 * LANES) == source - shift + LANES, 1.0, 0.0).astype(jnp.bfloat16)


def gather_kernel(count, local_ref, out_ref, own_ref, send, recv):
    rank, spot = lax.axis_index(DP), lax.axis_index(SPACE)
    mate, across, twin = mate_of(rank), lax.rem(rank + 2, 4), mate_of(spot)
    pieces = 4
    rows = BLOCK // 2 // pieces
    peers = ({DP: mate}, {DP: across}, {SPACE: twin})
    greet(peers)
    matrix = lane_matrix(lax.rem(rank * count, LANES), True)
    first = lax.broadcasted_iota(jnp.int32, (256, LANES), 0) == 0

    def rotate(step, carry):
        at = pl.ds(pl.multiple_of(step * 256, 256), 256)
        both = jnp.dot(local_ref[at, :], matrix, preferred_element_type=jnp.float32)
        spill = pltpu.roll(both[:, LANES:], 1, 0)
        own_ref[at, :] = (both[:, :LANES] + jnp.where(first, carry, spill)).astype(jnp.bfloat16)
        return spill[0:1]

    lax.fori_loop(0, BLOCK // 256, rotate, jnp.zeros((1, LANES), jnp.float32))

    half, other_half = lax.rem(spot, 2), lax.rem(spot + 1, 2)

    def piece(which, index):
        return pl.ds(pl.multiple_of(which * (BLOCK // 2) + index * rows, 16), rows)

    own_x = [
        remote(own_ref.at[piece(half, k)], out_ref.at[rank, piece(half, k)], send.at[0, k], recv.at[0, k], peers[1])
        for k in range(pieces)
    ]
    own_c = remote(own_ref, out_ref.at[rank], send.at[4, 0], recv.at[4, 0], peers[0])
    for copy in own_x:
        copy.start()
    own_c.start()
    later = []
    for k in range(pieces):
        own_x[k].wait_recv()
        block = out_ref.at[across, piece(half, k)]
        to_twin = remote(block, block, send.at[1, k], recv.at[1, k], peers[2])
        to_mate = remote(block, block, send.at[2, k], recv.at[2, k], peers[0])
        to_twin.start()
        to_mate.start()
        later.append((to_twin, to_mate))
    for at in range(BLOCK // 256):
        out_ref[rank, at * 256 : (at + 1) * 256, :] = own_ref[at * 256 : (at + 1) * 256, :]
    for k in range(pieces):
        later[k][0].wait_recv()
        block = out_ref.at[across, piece(other_half, k)]
        to_mate = remote(block, block, send.at[3, k], recv.at[3, k], peers[0])
        to_mate.start()
        later.append((to_mate,))
    for k in range(pieces):
        own_x[k].wait_send()
        later[k][0].wait_send()
        later[k][1].wait()
        later[pieces + k][0].wait()
    own_c.wait()


def gather_blocks(params):
    count = params.shape[0]
    local = jnp.pad(params, (0, BLOCK * LANES - count)).reshape(BLOCK, LANES)
    return pl.pallas_call(
        functools.partial(gather_kernel, count),
        out_shape=jax.ShapeDtypeStruct((4, BLOCK, LANES), jnp.bfloat16),
        in_specs=[pl.BlockSpec(memory_space=pltpu.VMEM)],
        out_specs=pl.BlockSpec(memory_space=pltpu.VMEM),
        scratch_shapes=[
            pltpu.VMEM((BLOCK, LANES), jnp.bfloat16),
            pltpu.SemaphoreType.DMA((5, 4)),
            pltpu.SemaphoreType.DMA((5, 4)),
        ],
        compiler_params=pltpu.CompilerParams(
            collective_id=0, has_side_effects=True, vmem_limit_bytes=32 * 2**20
        ),
    )(local)


def gather_params(params):
    count = params.shape[0]
    blocks = gather_blocks(params)
    pieces = []
    reach = 0
    for rank in range(4):
        start = rank * count // LANES
        stop = -(-(rank + 1) * count // LANES)
        head = blocks[rank, :1] if rank == 0 else blocks[rank, :1] + pieces.pop()
        pieces += [head, blocks[rank, 1 : stop - start - 1], blocks[rank, stop - start - 1 : stop - start]]
    return jnp.concatenate(pieces)


def reduce_kernel(count, space, pieces, grads_ref, out_ref, rc, tx, rx, acc, ty, ry, tz, rz, gath, send, recv, zsend, zrecv):
    rank, spot = lax.axis_index(DP), lax.axis_index(SPACE)
    mate, across, twin = mate_of(rank), lax.rem(rank + 2, 4), mate_of(spot)
    group = space // 2
    side, depth = lax.rem(spot, 2), lax.div(spot, 2)
    rows = BLOCK // pieces
    half = rows // 2
    part = half // group

    def partner(step):
        return lax.rem(depth + step, group)

    peers = [{DP: mate}, {DP: across}, {SPACE: twin}]
    barrier = pltpu.get_barrier_semaphore()
    for device in peers:
        pl.semaphore_signal(barrier, inc=1, device_id=device, device_id_type=MESH)

    def hello(step, carry):
        pl.semaphore_signal(barrier, inc=1, device_id={SPACE: partner(step) * 2 + side}, device_id_type=MESH)
        return carry

    lax.fori_loop(1, group, hello, 0)
    pl.semaphore_wait(barrier, 3 + group - 1)

    gath[BLOCK:, :] = jnp.zeros((32, LANES), jnp.bfloat16)
    lower = lax.rem(rank, 2)
    upper = lax.div(rank, 2)

    def base(who):
        return pl.multiple_of(quarter_base(who, count), 16)

    def rows_of(start, index, length):
        return pl.ds(pl.multiple_of(start + index, 16), length)

    core = []
    for p in range(pieces):
        for high in range(2):
            copy = remote(
                grads_ref.at[rows_of(base(2 * high + 1 - lower), p * rows, rows)],
                rc.at[p, high],
                send.at[high, p],
                recv.at[high, p],
                peers[0],
            )
            copy.start()
            core.append(copy)
    step_rows = 192 if half % 192 == 0 else 16
    xs, ys, gs = [], [], []

    def z_copy(p, step):
        to = partner(step)
        return remote(
            tz.at[p, pl.ds(pl.multiple_of(to * part, 16), part)],
            rz.at[p, pl.ds(pl.multiple_of(depth * part, 16), part)],
            zsend.at[0, p, step],
            zrecv.at[0, p, step],
            {SPACE: to * 2 + side},
        )

    def home(p, which, slot):
        return pl.ds(pl.multiple_of(p * rows + which * half + slot * part, 16), part)

    def g_copy(p, step):
        block = gath.at[home(p, side, depth)]
        return remote(block, block, zsend.at[1, p, step], zrecv.at[1, p, step], {SPACE: partner(step) * 2 + side})

    def each(body):
        def run(step, carry):
            body(step)
            return carry

        lax.fori_loop(1, group, run, 0)

    def stage_core(p):
        core[2 * p].wait_recv()
        core[2 * p + 1].wait_recv()
        far = 1 - upper

        def add(step, carry):
            at = pl.multiple_of(step * step_rows, 16)
            mine = grads_ref[rows_of(base(2 * far + lower), p * rows + at, step_rows), :].astype(jnp.float32)
            tx[p, pl.ds(at, step_rows), :] = (
                mine + rc[p, far, pl.ds(at, step_rows), :].astype(jnp.float32)
            ).astype(jnp.bfloat16)
            return carry

        lax.fori_loop(0, rows // step_rows, add, 0)
        copy = remote(tx.at[p], rx.at[p], send.at[2, p], recv.at[2, p], peers[1])
        copy.start()
        xs.append(copy)

    def stage_x(p):
        xs[p].wait_recv()

        def total(at):
            return (
                grads_ref[rows_of(base(rank), p * rows + at, step_rows), :].astype(jnp.float32)
                + rc[p, upper, pl.ds(at, step_rows), :].astype(jnp.float32)
                + rx[p, pl.ds(at, step_rows), :].astype(jnp.float32)
            )

        def add(step, carry):
            at = pl.multiple_of(step * step_rows, 16)
            far = pl.multiple_of((1 - side) * half + at, 16)
            near = pl.multiple_of(side * half + at, 16)
            ty[p, pl.ds(at, step_rows), :] = total(far).astype(jnp.bfloat16)
            acc[p, pl.ds(at, step_rows), :] = total(near)
            return carry

        lax.fori_loop(0, half // step_rows, add, 0)
        copy = remote(ty.at[p], ry.at[p], send.at[3, p], recv.at[3, p], peers[2])
        copy.start()
        ys.append(copy)

    def stage_y(p):
        ys[p].wait_recv()

        def add(step, carry):
            at = pl.ds(pl.multiple_of(step * step_rows, 16), step_rows)
            value = acc[p, at, :] + ry[p, at, :].astype(jnp.float32)
            acc[p, at, :] = value
            tz[p, at, :] = value.astype(jnp.bfloat16)
            return carry

        lax.fori_loop(0, half // step_rows, add, 0)
        each(lambda step: z_copy(p, step).start())

    def stage_z(p):
        each(lambda step: z_copy(p, step).wait_recv())
        value = acc[p, pl.ds(pl.multiple_of(depth * part, 16), part), :]

        def add(step, value):
            other = lax.rem(depth + group - step, group)
            return value + rz[p, pl.ds(pl.multiple_of(other * part, 16), part), :].astype(jnp.float32)

        value = lax.fori_loop(1, group, add, value)
        gath[home(p, side, depth), :] = value.astype(jnp.bfloat16)
        each(lambda step: g_copy(p, step).start())

    def stage_zg(p):
        each(lambda step: g_copy(p, step).wait_recv())
        block = gath.at[pl.ds(pl.multiple_of(p * rows + side * half, 16), half)]
        copy = remote(block, block, send.at[4, p], recv.at[4, p], peers[2])
        copy.start()
        gs.append(copy)

    def stage_yg(p):
        gs[p].wait_recv()

    stages = [stage_core, stage_x, stage_y, stage_z, stage_zg, stage_yg]
    for tick in range(pieces + len(stages) - 1):
        for number in reversed(range(len(stages))):
            if 0 <= tick - number < pieces:
                stages[number](tick - number)

    for copy in core + xs + ys + gs:
        copy.wait_send()
    for p in range(pieces):

        def done(step):
            z_copy(p, step).wait_send()
            g_copy(p, step).wait_send()

        each(done)

    offset = rank * count - quarter_base(rank, count) * LANES
    skip = lax.div(offset, LANES)
    matrix = lane_matrix(lax.rem(offset, LANES), False)
    wide = jnp.where(
        lax.broadcasted_iota(jnp.int32, (256, 288), 1)
        == lax.broadcasted_iota(jnp.int32, (256, 288), 0) + skip,
        1.0,
        0.0,
    ).astype(jnp.bfloat16)
    wide_next = jnp.where(
        lax.broadcasted_iota(jnp.int32, (256, 288), 1)
        == lax.broadcasted_iota(jnp.int32, (256, 288), 0) + skip + 1,
        1.0,
        0.0,
    ).astype(jnp.bfloat16)

    def place(step, carry):
        at = pl.multiple_of(step * 256, 256)
        block = gath[pl.ds(at, 288), :]
        both = jnp.dot(block, matrix, preferred_element_type=jnp.float32).astype(jnp.bfloat16)
        out_ref[pl.ds(at, 256), :] = jnp.dot(wide, both[:, :LANES], preferred_element_type=jnp.float32) + jnp.dot(
            wide_next, both[:, LANES:], preferred_element_type=jnp.float32
        )
        return carry

    lax.fori_loop(0, BLOCK // 256, place, 0)


def reduce_grads(flat, space, count):
    pieces = next(k for k in (4, 2, 1) if BLOCK // (k * space) % 16 == 0)
    rows = BLOCK // pieces
    half = rows // 2
    out = pl.pallas_call(
        functools.partial(reduce_kernel, count, space, pieces),
        out_shape=jax.ShapeDtypeStruct((BLOCK, LANES), jnp.float32),
        in_specs=[pl.BlockSpec(memory_space=pltpu.VMEM)],
        out_specs=pl.BlockSpec(memory_space=pltpu.VMEM),
        scratch_shapes=[
            pltpu.VMEM((pieces, 2, rows, LANES), jnp.bfloat16),
            pltpu.VMEM((pieces, rows, LANES), jnp.bfloat16),
            pltpu.VMEM((pieces, rows, LANES), jnp.bfloat16),
            pltpu.VMEM((pieces, half, LANES), jnp.float32),
            pltpu.VMEM((pieces, half, LANES), jnp.bfloat16),
            pltpu.VMEM((pieces, half, LANES), jnp.bfloat16),
            pltpu.VMEM((pieces, half, LANES), jnp.bfloat16),
            pltpu.VMEM((pieces, half, LANES), jnp.bfloat16),
            pltpu.VMEM((BLOCK + 32, LANES), jnp.bfloat16),
            pltpu.SemaphoreType.DMA((5, pieces)),
            pltpu.SemaphoreType.DMA((5, pieces)),
            pltpu.SemaphoreType.DMA((2, pieces, space // 2)),
            pltpu.SemaphoreType.DMA((2, pieces, space // 2)),
        ],
        compiler_params=pltpu.CompilerParams(
            collective_id=1, has_side_effects=True, vmem_limit_bytes=48 * 2**20
        ),
    )(flat)
    return out.reshape(-1)[:count]


def gru_forward(state, inputs, weights, biases, gate_name, candidate_name, tall, wide, padder):
    joined_stack = patches(padder(jnp.concatenate([state, inputs], -1), tall, wide), tall, wide)
    gates = jax.nn.sigmoid(apply(joined_stack, weights[gate_name]) + biases[gate_name])
    hidden = state.shape[-1]
    update = gates[..., :hidden]
    reset = gates[..., hidden:]
    state_wide = state.astype(jnp.float32)
    mixed = jnp.concatenate([(reset * state_wide).astype(jnp.bfloat16), inputs], -1)
    mixed_stack = patches(padder(mixed, tall, wide), tall, wide)
    candidate = jnp.tanh(apply(mixed_stack, weights[candidate_name]) + biases[candidate_name])
    result = state_wide + update * (candidate - state_wide)
    return (result, (joined_stack, mixed_stack, update, reset, candidate, state_wide))


def gru_backward(result_grad, kept, weights, grads, gate_name, candidate_name, tall, wide, padder):
    joined_stack, mixed_stack, update, reset, candidate, state_wide = kept
    hidden = update.shape[-1]
    candidate_grad = (result_grad * update * (1.0 - candidate * candidate)).astype(jnp.bfloat16)
    record(grads, candidate_name, mixed_stack, candidate_grad)
    mixed_grad = apply(
        patches(padder(candidate_grad, tall, wide), tall, wide),
        flipped(weights[candidate_name], tall, wide),
    )
    reset_grad = mixed_grad[..., :hidden]
    gate_grad = jnp.concatenate(
        [
            result_grad * (candidate - state_wide) * update * (1.0 - update),
            reset_grad * state_wide * reset * (1.0 - reset),
        ],
        -1,
    ).astype(jnp.bfloat16)
    record(grads, gate_name, joined_stack, gate_grad)
    joined_grad = apply(
        patches(padder(gate_grad, tall, wide), tall, wide), flipped(weights[gate_name], tall, wide)
    )
    state_grad = result_grad * (1.0 - update) + reset_grad * reset + joined_grad[..., :hidden]
    inputs_grad = joined_grad[..., hidden:] + mixed_grad[..., hidden:]
    return (state_grad, inputs_grad)


def shards(net, context, corr, flow, target, valid, grad_net, grad_mask, params):
    flow_start = CTX + MOT - 2
    plane = jnp.float32(target.shape[2] * net.shape[2])
    counts = lax.psum(jnp.sum(valid, axis=(1, 2)).astype(jnp.float32), SPACE)
    divisor = jnp.maximum(counts, 1.0)
    weights, biases = unpack(gather_params(params))
    grads = {}
    flow_rows = jnp.transpose(flow, (0, 2, 3, 1))
    corr_pre = apply(corr, weights[CORR_IN]) + biases[CORR_IN]
    corr_one = jax.nn.silu(corr_pre).astype(jnp.bfloat16)
    corr_stack = patches(row_pad(corr_one, 3), 3, 3)
    corr_mix_pre = apply(corr_stack, weights[CORR_MIX]) + biases[CORR_MIX]
    corr_two = jax.nn.silu(corr_mix_pre).astype(jnp.bfloat16)
    flow_stack = patches(row_pad(flow_rows, 7), 7, 7)
    flow_pre = apply(flow_stack, weights[FLOW_IN]) + biases[FLOW_IN]
    flow_one = jax.nn.silu(flow_pre).astype(jnp.bfloat16)
    flow_mix_stack = patches(row_pad(flow_one, 3), 3, 3)
    flow_mix_pre = apply(flow_mix_stack, weights[FLOW_MIX]) + biases[FLOW_MIX]
    flow_two = jax.nn.silu(flow_mix_pre).astype(jnp.bfloat16)
    joint_stack = patches(row_pad(jnp.concatenate([corr_two, flow_two], -1), 3), 3, 3)
    motion_pre = apply(joint_stack, weights[MOTION_MIX]) + biases[MOTION_MIX]
    motion = jax.nn.silu(motion_pre).astype(jnp.bfloat16)
    inputs = jnp.concatenate([context, motion, flow_rows], -1)
    state, rows_kept = gru_forward(
        net, inputs, weights, biases, ROWS_GATES, ROWS_CANDIDATE, 1, 5, local_pad
    )
    state_columns, inputs_columns = (
        lax.all_to_all(
            state.astype(jnp.bfloat16), SPACE, split_axis=2, concat_axis=1, tiled=True
        ),
        lax.all_to_all(inputs, SPACE, split_axis=2, concat_axis=1, tiled=True),
    )
    target_here = jnp.transpose(target, (0, 2, 3, 1))
    valid_here = valid.astype(jnp.float32)
    net_cotangent = grad_net
    mask_cotangent = grad_mask
    final, columns_kept = gru_forward(
        state_columns,
        inputs_columns,
        weights,
        biases,
        COLUMNS_GATES,
        COLUMNS_CANDIDATE,
        5,
        1,
        local_pad,
    )
    final_low = final.astype(jnp.bfloat16)
    heads_weight = jnp.concatenate([weights[FLOW_HIDDEN], weights[MASK_HIDDEN]], 1)
    heads_bias = jnp.concatenate([biases[FLOW_HIDDEN], biases[MASK_HIDDEN]])
    net_stack = patches(column_pad(final_low, 3, 3), 3, 3)
    heads_pre = apply(net_stack, heads_weight) + heads_bias
    heads_act = jax.nn.silu(heads_pre).astype(jnp.bfloat16)
    flow_features = heads_act[..., :HEAD]
    mask_features = heads_act[..., HEAD:]
    hidden_stack = patches(column_pad(flow_features, 3, 3), 3, 3)
    delta = apply(hidden_stack, weights[FLOW_OUT]) + biases[FLOW_OUT]
    mask_full = 0.25 * (apply(mask_features, weights[MASK_OUT]) + biases[MASK_OUT])
    new_flow = inputs_columns[..., flow_start:].astype(jnp.float32) + delta
    error = new_flow - target_here
    root = jnp.sqrt(error * error + 1.0)
    partials = jnp.sum(valid_here * jnp.sum(root, axis=-1), axis=(1, 2))
    flow_grad = plane / divisor[:, None, None, None] * valid_here[..., None] * error / root
    mask_low = mask_full.astype(jnp.bfloat16)
    nets_out = final_low
    flows_out = jnp.transpose(new_flow, (0, 3, 1, 2))
    masks_out = mask_low
    delta_grad = flow_grad.astype(jnp.bfloat16)
    mask_grad = (0.25 * mask_cotangent.astype(jnp.float32)).astype(jnp.bfloat16)
    record(grads, MASK_OUT, mask_features, mask_grad)
    record(grads, FLOW_OUT, hidden_stack, delta_grad)
    from_flow = apply(
        patches(column_pad(delta_grad, 3, 3), 3, 3), flipped(weights[FLOW_OUT], 3, 3)
    )
    from_mask = apply_back(mask_grad, weights[MASK_OUT])
    heads_grad = (jnp.concatenate([from_flow, from_mask], -1) * slope(heads_pre)).astype(
        jnp.bfloat16
    )
    heads_wgrad = weight_grad(net_stack, heads_grad)
    heads_bgrad = jnp.sum(heads_grad, axis=(0, 1, 2), dtype=jnp.float32)
    grads[FLOW_HIDDEN] = (heads_wgrad[:, :HEAD], heads_bgrad[:HEAD])
    grads[MASK_HIDDEN] = (heads_wgrad[:, HEAD:], heads_bgrad[HEAD:])
    final_grad = net_cotangent.astype(jnp.float32) + apply(
        patches(column_pad(heads_grad, 3, 3), 3, 3), flipped(heads_weight, 3, 3)
    )
    state_grad_columns, inputs_grad_columns = gru_backward(
        final_grad,
        columns_kept,
        weights,
        grads,
        COLUMNS_GATES,
        COLUMNS_CANDIDATE,
        5,
        1,
        local_pad,
    )
    inputs_grad_columns = jnp.concatenate(
        [
            inputs_grad_columns[..., :flow_start],
            inputs_grad_columns[..., flow_start:] + flow_grad,
        ],
        -1,
    )
    state_back, inputs_back = (
        lax.all_to_all(
            state_grad_columns.astype(jnp.bfloat16),
            SPACE,
            split_axis=1,
            concat_axis=2,
            tiled=True,
        ),
        lax.all_to_all(
            inputs_grad_columns.astype(jnp.bfloat16),
            SPACE,
            split_axis=1,
            concat_axis=2,
            tiled=True,
        ),
    )
    net_grad, inputs_grad = gru_backward(
        state_back.astype(jnp.float32),
        rows_kept,
        weights,
        grads,
        ROWS_GATES,
        ROWS_CANDIDATE,
        1,
        5,
        local_pad,
    )
    inputs_total = inputs_grad + inputs_back.astype(jnp.float32)
    motion_grad = (inputs_total[..., CTX:flow_start] * slope(motion_pre)).astype(jnp.bfloat16)
    record(grads, MOTION_MIX, joint_stack, motion_grad)
    joint_grad = apply(
        patches(row_pad(motion_grad, 3), 3, 3), flipped(weights[MOTION_MIX], 3, 3)
    )
    branch_grad = jnp.concatenate(
        [
            joint_grad[..., :C2] * slope(corr_mix_pre),
            joint_grad[..., C2:] * slope(flow_mix_pre),
        ],
        -1,
    ).astype(jnp.bfloat16)
    record(grads, CORR_MIX, corr_stack, branch_grad[..., :C2])
    record(grads, FLOW_MIX, flow_mix_stack, branch_grad[..., C2:])
    branch_pad = row_pad(branch_grad, 3)
    corr_one_grad = apply(
        patches(branch_pad[..., :C2], 3, 3), flipped(weights[CORR_MIX], 3, 3)
    )
    flow_one_grad = apply(
        patches(branch_pad[..., C2:], 3, 3), flipped(weights[FLOW_MIX], 3, 3)
    )
    corr_pre_grad = (corr_one_grad * slope(corr_pre)).astype(jnp.bfloat16)
    flow_pre_grad = (flow_one_grad * slope(flow_pre)).astype(jnp.bfloat16)
    record(grads, CORR_IN, corr, corr_pre_grad)
    record(grads, FLOW_IN, flow_stack, flow_pre_grad)
    corr_grads = apply_back(corr_pre_grad, weights[CORR_IN])
    flow_total = inputs_total[..., flow_start:] + apply(
        patches(row_pad(flow_pre_grad, 7), 7, 7), flipped(weights[FLOW_IN], 7, 7)
    )
    flow_grads = jnp.transpose(flow_total, (0, 3, 1, 2))
    net_grads = net_grad
    context_grads = inputs_total[..., :CTX]
    count = params.shape[0]
    local = pack(grads, 3 * count // (LANES * 16) * 16 + BLOCK)
    collected = reduce_grads(local, lax.axis_size(SPACE), count)
    losses = lax.psum(partials, SPACE) / divisor
    return (
        nets_out,
        flows_out,
        masks_out,
        losses,
        collected,
        net_grads,
        context_grads,
        corr_grads,
        flow_grads,
    )


BATCH = 2
ROWS = 5
WIDE = 128
TALL = 40
COLS = 16
AREA = 640
PITCH = 20
SPREAD = TALL * PITCH
SPAN = 896
EDGE = 64


def mm(a, b):
    return jnp.dot(a, b, preferred_element_type=jnp.float32)


def nt(a, b):
    return lax.dot_general(a, b, (((1,), (1,)), ((), ())), preferred_element_type=jnp.float32)


def tn(a, b):
    return lax.dot_general(a, b, (((0,), (0,)), ((), ())), preferred_element_type=jnp.float32)


def half_of(value):
    return value.astype(jnp.bfloat16)


def full_of(value):
    return value.astype(jnp.float32)


def join(parts, axis=1):
    return jnp.concatenate(list(parts), axis=axis)


def quarter_of(value):
    return half_of(0.25 * full_of(value))


def lane_index(shape):
    return lax.broadcasted_iota(jnp.int32, shape, 1)


def row_index(shape):
    return lax.broadcasted_iota(jnp.int32, shape, 0)


def act_slope(pre):
    sigma = jax.nn.sigmoid(pre)
    act = pre * sigma
    return act, sigma + act * (1.0 - sigma)


def flat_rows():
    table = shapes()
    offset = 0
    starts = {}
    for name, height, width in table:
        starts[name] = offset // LANES
        offset += height * width
    bias_row = offset // LANES
    spots = {}
    inner = 0
    for name, height, width in table:
        spots[name] = inner
        inner += width
    return starts, bias_row, spots, inner


def cast_rows(dst, to, src, start, count, kind):
    big = 256
    whole = count // big

    if whole > 1:

        def body(step, carry):
            at = pl.multiple_of(step * big, big)
            dst[pl.ds(to + at, big), :] = src[pl.ds(start + at, big), :].astype(kind)
            return carry

        lax.fori_loop(0, whole, body, 0)
    elif whole == 1:
        dst[to : to + big, :] = src[start : start + big, :].astype(kind)
    rest = count - whole * big
    if rest:
        low = whole * big
        dst[to + low : to + count, :] = src[start + low : start + count, :].astype(kind)


MARGIN = 16


def stage_plan(count, start, rows):
    stop = start + rows
    pieces, fill = [], 0
    for rank in range(4):
        first = rank * count // LANES
        last = -(-(rank + 1) * count // LANES)
        low, high = max(start, first), min(stop, last)
        if low >= high:
            continue
        place = low - first + rank * BLOCK
        base = place // 16 * 16
        length = -(-(place - base + high - low) // 16) * 16
        to = MARGIN + low - start - (place - base)
        seam = MARGIN + low - start if start < first else None
        pieces.append((base, length, fill, to, seam))
        fill += length
    return pieces


class Stages:
    def __init__(self, v, count, segments):
        self.v, self.at, self.hold = v, 0, (4,)
        self.plans = [stage_plan(count, start, rows) for start, rows in segments]
        self.fetch(0)

    def copies(self, index):
        v, slot = self.v, index % 2
        return [
            pltpu.make_async_copy(
                v.out_all.at[base : base + length], v.stage.at[slot, fill : fill + length], v.ssem.at[slot, number]
            )
            for number, (base, length, fill, to, seam) in enumerate(self.plans[index])
        ]

    def fetch(self, index):
        if index < len(self.plans):
            for copy in self.copies(index):
                copy.start()

    def take(self):
        v, index = self.v, self.at
        self.at += 1
        for copy in self.copies(index):
            copy.wait()
        if index + 1 not in self.hold:
            self.fetch(index + 1)
        for base, length, fill, to, seam in self.plans[index]:
            saved = None if seam is None else v.flat[seam : seam + 1, :]
            cast_rows(v.flat, to, v.stage.at[index % 2], fill, length, jnp.float32)
            if seam is not None:
                v.flat[seam : seam + 1, :] = v.flat[seam : seam + 1, :] + saved


def strided(ref, start, count, stride):
    if stride == 1:
        return ref[pl.ds(start, count), :]
    return ref[pl.ds(start, count, stride=stride), :]


def unpack_pairs(flat, row, count, dst, to, lane):
    dst[to : to + count, lane : lane + LANES] = half_of(strided(flat, MARGIN + 2 * row, count, 2))
    dst[to : to + count, lane + LANES : lane + 2 * LANES] = half_of(strided(flat, MARGIN + 2 * row + 1, count, 2))


def pack_pairs(flat, row, count, low, high):
    flat[pl.ds(MARGIN + 2 * row, count, stride=2), :] = low
    flat[pl.ds(MARGIN + 2 * row + 1, count, stride=2), :] = high


def split_pick(which, quarter):
    source = lax.broadcasted_iota(jnp.int32, (LANES, HEAD), 0)
    target = lax.broadcasted_iota(jnp.int32, (LANES, HEAD), 1)
    return jnp.where(source == 2 * (target - 64 * quarter) + which, 1.0, 0.0).astype(jnp.bfloat16)


UNPACK = (
    (CORR_IN, 648), (CORR_MIX, 3456), (FLOW_IN, 98), (FLOW_MIX, 576), (MOTION_MIX, 2268),
    (ROWS_GATES, 3840), (ROWS_CANDIDATE, 1920), (COLUMNS_GATES, 3840), (COLUMNS_CANDIDATE, 1920),
    (FLOW_HIDDEN, 2304), (MASK_HIDDEN, 2304), (FLOW_OUT, 36), (MASK_OUT, 1152),
)


def stage_of(v, name, rows):
    assert UNPACK[v.stages.at] == (name, rows)
    v.stages.take()


def unpack_gru(v, gates_name, cand_name, w_i, w_s):
    flat = v.flat
    stage_of(v, gates_name, 3840)
    for tap in range(5):
        unpack_pairs(flat, tap * 384, 128, w_s, tap * 128, 0)
        unpack_pairs(flat, tap * 384 + 128, 256, w_i, tap * 256, 0)
    stage_of(v, cand_name, 1920)
    for tap in range(5):
        w_s[tap * 128 : (tap + 1) * 128, 256:384] = half_of(strided(flat, MARGIN + tap * 384, 128, 1))
        w_i[tap * 256 : (tap + 1) * 256, 256:384] = half_of(strided(flat, MARGIN + tap * 384 + 128, 256, 1))


def unpack_encoder(v, count):
    starts, bias_row, spots, inner = flat_rows()
    flat = v.flat
    v.stages = Stages(v, count, [(starts[name], rows) for name, rows in UNPACK])

    def stage(name, rows):
        stage_of(v, name, rows)

    @pl.when(v.rank != 3)
    def _():
        drain_bytes(v.bz, v.grecv.at[0, 4])

    flat[0:64, :] = full_of(v.bz[...])
    start = bias_row - 3 * count // LANES - BIAS_LOW
    place = 0
    lane1 = lane_index((1, LANES))
    for name, height, width in shapes():
        spot = spots[name]
        for block in range(-(-width // LANES)):
            at = spot + block * LANES
            row, shift = at // LANES, at % LANES
            value = flat[start + row : start + row + 1, :]
            if shift:
                after = flat[start + row + 1 : start + row + 2, :]
                value = jnp.where(
                    lane1 < LANES - shift, pltpu.roll(value, LANES - shift, 1), pltpu.roll(after, LANES - shift, 1)
                )
            left = width - block * LANES
            if left < LANES:
                value = jnp.where(lane1 < left, value, 0.0)
            if name == FLOW_MIX:
                value = pltpu.roll(value, 64, 1)
            v.bias[place : place + 1, :] = value
            place += 1

    stage(CORR_IN, 648)
    unpack_pairs(flat, 0, 324, v.w_ci, 0, 0)

    stage(CORR_MIX, 3456)
    lane = lane_index((128, LANES))
    low_half = lane < 64

    def mix_step(step, carry):
        at = MARGIN + 384 * step
        r0, r1, r2 = (strided(flat, at + i, 128, 3) for i in range(3))
        r1s, r2s = pltpu.roll(r1, 64, 1), pltpu.roll(r2, 64, 1)
        v.pair_a[pl.ds(0, 128, stride=2), :] = r0
        v.pair_a[pl.ds(1, 128, stride=2), :] = jnp.where(low_half, r1s, r2s)
        v.pair_b[pl.ds(0, 128, stride=2), :] = jnp.where(low_half, r1, 0.0)
        v.pair_b[pl.ds(1, 128, stride=2), :] = jnp.where(low_half, r2s, 0.0)
        to = pl.ds(pl.multiple_of(step * 256, 256), 256)
        v.w_cm[to, 0:128] = half_of(v.pair_a[...])
        v.w_cm[to, 128:256] = half_of(v.pair_b[...])
        return carry

    lax.fori_loop(0, 9, mix_step, 0)

    stage(FLOW_IN, 98)
    v.flow_tmp[...] = jnp.zeros_like(v.flow_tmp)
    for across in range(7):
        for comp in range(2):
            v.flow_tmp[pl.ds(across * 16 + comp, 7, stride=2), :] = strided(
                flat, MARGIN + across * 2 + comp, 7, 14
            )
    v.w_fi[...] = half_of(v.flow_tmp[...])

    stage(FLOW_MIX, 576)
    for step in range(9):
        r0 = strided(flat, MARGIN + 64 * step, 64, 1)
        high_half = lane_index((64, LANES)) >= 64
        v.pair_a[pl.ds(0, 64, stride=2), :] = jnp.where(high_half, pltpu.roll(r0, 64, 1), 0.0)
        v.pair_a[pl.ds(1, 64, stride=2), :] = jnp.where(high_half, r0, 0.0)
        v.w_fm[step * 128 : (step + 1) * 128, :] = half_of(v.pair_a[0:128, :])


def unpack_rows(v):
    flat = v.flat
    v.stages.fetch(4)

    def stage(name, rows):
        stage_of(v, name, rows)

    stage(MOTION_MIX, 2268)
    lane36 = lane_index((36, LANES))
    for i in range(64):
        if i == 0:
            value = strided(flat, MARGIN, 36, 63)
        elif i == 63:
            value = pltpu.roll(strided(flat, MARGIN + 62, 36, 63), 126, 1)
        else:
            low = pltpu.roll(strided(flat, MARGIN + i - 1, 36, 63), 2 * i, 1)
            high = pltpu.roll(strided(flat, MARGIN + i, 36, 63), 2 * i, 1)
            value = jnp.where(lane36 < 2 * i, low, high)
        v.mm_tmp[pl.ds(i, 36, stride=64), :] = jnp.where(lane36 < 126, value, 0.0)
    for step in range(9):
        v.w_mm[step * 256 : (step + 1) * 256, :] = half_of(v.mm_tmp[step * 256 : (step + 1) * 256, :])

    unpack_gru(v, ROWS_GATES, ROWS_CANDIDATE, v.w_ri, v.w_rs)


def unpack_heads(v):
    flat = v.flat
    low_half = lane_index((128, LANES)) < 64

    def stage(name, rows):
        stage_of(v, name, rows)

    unpack_gru(v, COLUMNS_GATES, COLUMNS_CANDIDATE, v.w_li, v.w_ls)

    for name, lane0 in ((FLOW_HIDDEN, 0), (MASK_HIDDEN, 256)):
        stage(name, 2304)
        for tap in range(9):
            unpack_pairs(flat, tap * 128, 128, v.w_h, tap * 128, lane0)

    stage(FLOW_OUT, 36)
    v.fo_tmp[...] = jnp.zeros_like(v.fo_tmp)
    for which in range(2):
        total = jnp.zeros((9, HEAD), jnp.float32)
        for quarter in range(4):
            total = total + mm(half_of(strided(flat, MARGIN + quarter, 9, 4)), split_pick(which, quarter))
        v.fo_tmp[pl.ds(which, 9, stride=2), 0:128] = total[:, :128]
        v.fo_tmp2[pl.ds(which, 9, stride=2), 0:128] = total[:, 128:]
    v.fo_tmp2[18:32, :] = jnp.zeros((14, LANES), jnp.float32)
    v.w_fo[:, 0:128] = half_of(v.fo_tmp[...])
    v.w_fo[:, 128:256] = half_of(v.fo_tmp2[...])

    stage(MASK_OUT, 1152)
    r = [strided(flat, MARGIN + i, 128, 9) for i in range(9)]
    rs = [pltpu.roll(r[i], 64, 1) for i in range(4, 9)]
    for block in range(5):
        even = r[block] if block < 4 else jnp.where(low_half, r[4], 0.0)
        odd = jnp.where(low_half, rs[block], rs[block + 1]) if block < 4 else jnp.where(low_half, rs[4], 0.0)
        v.pair_a[pl.ds(0, 128, stride=2), :] = even
        v.pair_a[pl.ds(1, 128, stride=2), :] = odd
        v.w_mo[:, block * 128 : (block + 1) * 128] = half_of(v.pair_a[...])


BIAS_AT = {}
_place = 0
for _name, _height, _width in shapes():
    BIAS_AT[_name] = _place
    _place += -(-_width // 128)
BIAS_ROWS = 32


def bias_of(v, name, blocks):
    at = BIAS_AT[name]
    return jnp.concatenate([v.bias[at + i : at + i + 1, :] for i in range(blocks)], axis=1)


class Halo:
    def __init__(self, v, sem, up_src, down_src, from_down, from_up):
        up = {SPACE: jnp.maximum(v.spot - 1, 0)}
        down = {SPACE: jnp.minimum(v.spot + 1, v.space - 1)}
        self.v = v
        self.up = remote(up_src, from_down, v.hsend.at[sem, 0], v.hrecv.at[sem, 0], up)
        self.down = remote(down_src, from_up, v.hsend.at[sem, 1], v.hrecv.at[sem, 1], down)

    def start(self):
        pl.when(self.v.spot > 0)(self.up.start)
        pl.when(self.v.spot < self.v.space - 1)(self.down.start)

    def receive(self):
        pl.when(self.v.spot < self.v.space - 1)(self.up.wait_recv)
        pl.when(self.v.spot > 0)(self.down.wait_recv)

    def sent(self):
        pl.when(self.v.spot > 0)(self.up.wait_send)
        pl.when(self.v.spot < self.v.space - 1)(self.down.wait_send)


def drain_bytes(ref, sem):
    pltpu.make_async_copy(ref, ref, sem).wait()


class Swap:
    def __init__(self, v, sem, src, dst, broadcast=False):
        self.v, self.sem, self.src, self.dst, self.broadcast = v, sem, src, dst, broadcast

    def start(self, b=None):
        v = self.v

        def body(step, carry):
            to = v.spot + step
            to = jnp.where(to >= v.space, to - v.space, to)
            src = self.src if self.broadcast else self.src.at[to]
            dst = self.dst.at[v.spot]
            if b is not None:
                src, dst = src.at[b], dst.at[b]
            remote(src, dst, v.asend.at[self.sem], v.arecv.at[self.sem], {SPACE: to}).start()
            return carry

        lax.fori_loop(1, v.space, body, 0)

    def receive(self):
        drain_bytes(self.dst.at[0 : self.v.space - 1], self.v.arecv.at[self.sem])

    def sent(self):
        drain_bytes(self.dst.at[0 : self.v.space - 1], self.v.asend.at[self.sem])


def spread_rows(v, b, acts, rows, dst, row0, width, backward=False):
    x = lax.rem(row_index((rows, LANES)), WIDE)
    for block, act in enumerate(acts):
        v.tmp[8 : 8 + rows, :] = act
        for tap in range(3):
            d = (1 - tap) if backward else (tap - 1)
            value = act if d == 0 else v.tmp[8 + d : 8 + d + rows, :]
            if d == -1:
                value = jnp.where(x > 0, value, 0.0)
            if d == 1:
                value = jnp.where(x < WIDE - 1, value, 0.0)
            lane = tap * width + block * LANES
            if backward:
                dst[row0 : row0 + rows, b + lane : b + lane + LANES] = half_of(value)
            else:
                dst[b, row0 : row0 + rows, lane : lane + LANES] = half_of(value)


def spread_five(v, value, dst, lane_of, backward=False):
    x = lax.rem(row_index((AREA, LANES)), WIDE)
    v.tmp[8 : 8 + AREA, :] = value
    for tap in range(5):
        d = (2 - tap) if backward else (tap - 2)
        moved = value if d == 0 else v.tmp[8 + d : 8 + d + AREA, :]
        if d:
            moved = jnp.where((x + d >= 0) & (x + d < WIDE), moved, 0.0)
        if backward:
            taps_part(v, tap, lane_of, lane_of + LANES)[...] = half_of(moved)
        else:
            lane = lane_of(tap)
            dst[:, lane : lane + LANES] = half_of(moved)


def lines_of(ref, b, lines):
    return jnp.concatenate([ref[b, y] for y in range(lines)], axis=1)


def edge_rows(v, value, rows):
    low = jnp.where(v.spot > 0, value[0:rows], 0.0)
    high = jnp.where(v.spot < v.space - 1, value[-rows:], 0.0)
    return jnp.concatenate([low, value[rows:-rows], high], axis=0)


def early_taps(v):
    def flow(b, carry):
        up = jnp.where(v.spot > 0, v.flow_up[b], 0.0)
        down = jnp.where(v.spot < v.space - 1, v.flow_down[b], 0.0)
        lane = lane_index((16, LANES))
        v.fs[...] = jnp.zeros_like(v.fs)
        for across in range(7):
            d = across - 3
            for part, value in enumerate((up, v.flow[b], down)):
                moved = value
                if d:
                    moved = pltpu.roll(value, (-d) % LANES, 1)
                    moved = jnp.where((lane + d >= 0) & (lane + d < WIDE), moved, 0.0)
                v.fs[across, part * 10 : part * 10 + 10, :] = moved[0:10, :]
        for y in range(9):
            for across in range(7):
                v.flow_tmp[across * 16 : across * 16 + 16, :] = v.fs[across, 2 * y : 2 * y + 16, :]
            v.xt[b, :, y * 128 : (y + 1) * 128] = half_of(v.flow_tmp[...])
        return carry

    lax.fori_loop(0, BATCH, flow, 0)

    def image(b, carry):
        at = pl.ds(pl.multiple_of(b * AREA, AREA), AREA)
        spread_five(v, full_of(v.context[b]), v.xi.at[at], lambda t: t * 256)
        spread_five(v, full_of(v.net[b]), v.xs.at[at], lambda t: t * 128)
        return carry

    lax.fori_loop(0, BATCH, image, 0)


def gather_start(v, count):
    shift = lax.rem(v.rank * count, LANES)
    chunk = 512
    keep = lane_index((chunk, LANES)) >= shift
    v.tmp[7:8, :] = jnp.zeros((1, LANES), jnp.float32)

    def rotate(step, carry):
        at = pl.ds(pl.multiple_of(step * chunk, chunk), chunk)
        moved = pltpu.roll(full_of(v.gath[at, :]), shift, 1)
        v.tmp[8 : 8 + chunk, :] = moved
        v.gath[at, :] = half_of(jnp.where(keep, moved, v.tmp[7 : 7 + chunk, :]))
        v.tmp[7:8, :] = v.tmp[7 + chunk : 8 + chunk, :]
        return carry

    lax.fori_loop(0, BLOCK // chunk, rotate, 0)

    quad = BLOCK // 4
    pieces = 4
    rows = quad // pieces
    half, core = lax.rem(v.spot, 2), lax.rem(v.rank, 2)
    near, far = v.rank - core, lax.rem(v.rank - core + 2, 4)

    def piece(rank, which, core, index):
        return pl.ds(pl.multiple_of(rank * BLOCK + (which * 2 + core) * quad + index * rows, 16), rows)

    def whole(rank, which, core):
        return pl.ds(pl.multiple_of(rank * BLOCK + (which * 2 + core) * quad, 16), quad)

    mine = pl.ds(pl.multiple_of(v.rank * BLOCK, 16), BLOCK)
    v.g_here = pltpu.make_async_copy(v.gath.at[0:BLOCK], v.out_all.at[mine], v.lsem)
    v.g_own = []
    for number, (which, side) in enumerate(((half, 1 - core), (half, core), (1 - half, 0), (1 - half, 1))):
        v.g_own.append(
            remote(
                v.gath.at[whole(0, which, side)], v.out_all.at[whole(v.rank, which, side)],
                v.gsend.at[0, number], v.grecv.at[0, number], {DP: v.mate},
            )
        )

    def block_copy(number, k, rank, which, side, device):
        block = v.out_all.at[piece(rank, which, side, k)]
        return remote(block, block, v.gsend.at[number, k], v.grecv.at[number, k], device)

    v.g_x, v.g_twin, v.g_mate, v.g_last = [], [], [], []
    for turn in range(2):
        base = 1 + 4 * turn
        v.g_x.append([block_copy(base, k, near + turn, half, core, {DP: v.other}) for k in range(pieces)])
        v.g_twin.append([block_copy(base + 1, k, far + turn, half, core, {SPACE: v.twin}) for k in range(pieces)])
        v.g_mate.append([block_copy(base + 2, k, far + turn, half, core, {DP: v.mate}) for k in range(pieces)])
        v.g_last.append([block_copy(base + 3, k, far + turn, 1 - half, core, {DP: v.mate}) for k in range(pieces)])
    v.g_here.start()
    for copy in v.g_own:
        copy.start()

    @pl.when(v.rank == 3)
    def _():
        for rank in range(3):
            remote(
                v.gath.at[BIAS_LOW : BIAS_LOW + 64], v.bz, v.gsend.at[0, 4 + rank], v.grecv.at[0, 4], {DP: rank}
            ).start()
        v.bz[...] = v.gath[BIAS_LOW : BIAS_LOW + 64, :]

    v.g_here.wait()
    def send_first():
        for copy in v.g_x[0]:
            copy.start()

    pl.when(core == 0)(send_first)
    v.g_own[0].wait_recv()
    pl.when(core == 1)(send_first)


BIAS_LOW = 6048


def gather_pass(v, turn, first, last):
    for k in range(first, last):
        v.g_x[turn][k].wait_recv()
        v.g_twin[turn][k].start()
        v.g_mate[turn][k].start()


def gather_last(v, turn):
    for k in range(len(v.g_x[turn])):
        v.g_twin[turn][k].wait_recv()
        v.g_last[turn][k].start()


def gather_turn(v, turn):
    gather_last(v, turn)
    gather_rest(v, turn)


def gather_rest(v, turn):
    for k in range(len(v.g_x[turn])):
        v.g_mate[turn][k].wait_recv()
        v.g_last[turn][k].wait_recv()


def gather_end(v):
    for turn in range(2):
        for group in (v.g_x, v.g_twin, v.g_mate, v.g_last):
            for copy in group[turn]:
                copy.wait_send()
    for copy in v.g_own:
        copy.wait_send()

    @pl.when(v.rank == 3)
    def _():
        for rank in range(3):
            remote(
                v.gath.at[BIAS_LOW : BIAS_LOW + 64], v.bz, v.gsend.at[0, 4 + rank], v.grecv.at[0, 4], {DP: rank}
            ).wait_send()


def forward_rows(v):
    spot, last = v.spot, v.space - 1
    def image(b, carry):
        pieces = (
            (v.corr_up, 0, 256, 2, spot > 0),
            (v.corr, 256, 640, 5, None),
            (v.corr_down, 896, 256, 2, spot < last),
        )
        bias = bias_of(v, CORR_IN, 2)
        for ref, row0, rows, lines, seen in pieces:
            act, slope = act_slope(tn(lines_of(ref, b, lines), v.w_ci[...]) + bias)
            if seen is None:
                v.slope_ci[b] = half_of(slope)
            else:
                act = jnp.where(seen, act, 0.0)
            spread_rows(v, b, (act[:, :128], act[:, 128:]), rows, v.hx_c, row0, 256)

        act, slope = act_slope(tn(v.xt[b], v.w_fi[...]) + bias_of(v, FLOW_IN, 1))
        v.slope_fi[b] = half_of(slope[256:896])
        spread_rows(v, b, (edge_rows(v, act, 2 * WIDE),), 9 * WIDE, v.hx_f, 0, 128)

        pl.when(b == 0)(lambda: gather_pass(v, 1, 0, 3))
        pl.when(b == 1)(lambda: gather_last(v, 1))
        pre = mm(join(v.hx_c[b, a * 128 : a * 128 + 896, :] for a in range(3)), v.w_cm[...]) + bias_of(v, CORR_MIX, 2)
        flow_pre = mm(join(v.hx_f[b, a * 128 : a * 128 + 896, :] for a in range(3)), v.w_fm[...])
        flow_pre = flow_pre + bias_of(v, FLOW_MIX, 1)
        low, low_slope = act_slope(pre[:, :128])
        high, high_slope = act_slope(pre[:, 128:] + flow_pre)
        v.slope_j[b, :, 0:128] = half_of(low_slope)
        v.slope_j[b, :, 128:256] = half_of(high_slope)
        spread_rows(v, b, (edge_rows(v, low, WIDE), edge_rows(v, high, WIDE)), 896, v.hx_j, 0, 256)

        pl.when(b == 0)(lambda: gather_pass(v, 1, 3, 4))
        return carry

    lax.fori_loop(0, BATCH, image, 0)
    gather_rest(v, 1)
    gather_end(v)
    unpack_rows(v)

    def moving(b, carry):
        pre = mm(join(v.hx_j[b, a * 128 : a * 128 + 640, :] for a in range(3)), v.w_mm[...])
        pre = pre + bias_of(v, MOTION_MIX, 1)
        act, slope = act_slope(pre)
        v.slope_m[b] = half_of(jnp.where(lane_index((AREA, LANES)) < 126, slope, 0.0))
        pick = jnp.where(lane_index((16, LANES)) == row_index((16, LANES)) + 126, 1.0, 0.0)
        own_flow = v.flow[b]
        for y in range(ROWS):
            v.tmp2[0:2, :] = own_flow[2 * y : 2 * y + 2, :]
            v.tmp2[2:16, :] = jnp.zeros((14, LANES), jnp.float32)
            v.motion[b, y * 128 : (y + 1) * 128, :] = act[y * 128 : (y + 1) * 128, :] + tn(
                half_of(v.tmp2[0:16, :]), half_of(pick)
            )
        v.motion[b] = full_of(half_of(v.motion[b]))
        pack_rows(v, v.motion, b, v.a_motion)
        v.swap_motion.start(b)
        return carry

    lax.fori_loop(0, BATCH, moving, 0)

    def gru(b, carry):
        at = pl.ds(pl.multiple_of(b * AREA, AREA), AREA)
        s = full_of(v.net[b])
        spread_five(v, v.motion[b], v.xi.at[at], lambda t: t * 256 + 128)
        both = mm(v.xi[at, :], v.w_ri[...])
        gates = jax.nn.sigmoid(both[:, :256] + mm(v.xs[at, :], v.w_rs[:, :256]) + bias_of(v, ROWS_GATES, 2))
        update, reset = gates[:, :128], gates[:, 128:]
        v.ru[b] = update
        v.rr[b] = reset
        spread_five(v, full_of(half_of(reset * s)), v.xr.at[at], lambda t: t * 128)
        cand = jnp.tanh(both[:, 256:] + mm(v.xr[at, :], v.w_rs[:, 256:]) + bias_of(v, ROWS_CANDIDATE, 1))
        v.rc[b] = cand
        v.state[b] = s + update * (cand - s)
        pack_rows(v, v.state, b, v.a_state)
        v.swap_state.start(b)
        return carry

    lax.fori_loop(0, BATCH, gru, 0)


def pack_rows(v, src, b, dst):
    def peer(t, carry):
        for y in range(ROWS):
            at = pl.multiple_of(y * WIDE + t * COLS, COLS)
            dst[t, b, y * COLS : (y + 1) * COLS, :] = half_of(src[b, pl.ds(at, COLS), :])
        return carry

    lax.fori_loop(0, v.space, peer, 0)


def take_own(v, src, dst):
    dst[v.spot] = src[v.spot]


def columns_zero(v):
    def zero(b, carry):
        for ref, wide in ((v.xc, 384), (v.xcr, 128), (v.gc, 384)):
            for low in (0, 32 + AREA):
                ref[b, low : low + 32, :] = jnp.zeros((32, wide), jnp.bfloat16)
        return carry

    lax.fori_loop(0, BATCH, zero, 0)


def columns_in(v):
    def peer(t, carry):
        at = pl.ds(pl.multiple_of(32 + t * ROWS * COLS, 16), ROWS * COLS)
        for b in range(BATCH):
            v.xc[b, at, 0:128] = v.b_state[t, b]
            v.xc[b, at, 128:256] = v.b_context[t, b]
            v.xc[b, at, 256:384] = v.b_motion[t, b]
        return carry

    lax.fori_loop(0, v.space, peer, 0)


FX_ROWS = 16 + (TALL + 2) * PITCH


def fx_base(b):
    return pl.multiple_of(b * FX_ROWS, 8)


def columns_forward(v):
    def gru(b, carry):
        s = full_of(v.xc[b, 32 : 32 + AREA, 0:128])
        bias = join((bias_of(v, COLUMNS_GATES, 2), bias_of(v, COLUMNS_CANDIDATE, 1)))
        rows = [slice(t * COLS, t * COLS + AREA) for t in range(5)]
        both = mm(join(v.xc[b, rows[t], 128:384] for t in range(5)), v.w_li[...]) + bias
        gates = mm(join(v.xc[b, rows[t], 0:128] for t in range(5)), v.w_ls[:, 0:256])
        gates = jax.nn.sigmoid(gates + both[:, :256])
        update, reset = gates[:, :128], gates[:, 128:]
        v.lu[b] = update
        v.lr[b] = reset
        v.xcr[b, 32 : 32 + AREA, :] = half_of(reset * s)
        cand = jnp.tanh(both[:, 256:] + mm(join(v.xcr[b, rows[t], :] for t in range(5)), v.w_ls[:, 256:384]))
        v.lc[b] = cand
        final = s + update * (cand - s)
        v.out_net[b] = half_of(final)
        v.final[...] = full_of(half_of(final))
        fx = fx_base(b)
        v.mm_tmp[pl.ds(fx, FX_ROWS), :] = jnp.zeros((FX_ROWS, LANES), jnp.float32)
        for x in range(COLS):
            v.mm_tmp[pl.ds(fx + 8 + PITCH + 2 + x, TALL, stride=PITCH), :] = v.final[pl.ds(x, TALL, stride=COLS), :]
        for j in range(2):
            v.e_left[b, j, 0:TALL, :] = half_of(v.final[pl.ds(j, TALL, stride=COLS), :])
            v.e_right[b, j, 0:TALL, :] = half_of(v.final[pl.ds(COLS - 2 + j, TALL, stride=COLS), :])
        return carry

    lax.fori_loop(0, BATCH, gru, 0)
    v.halo_final.start()


def ring_masks(v, shape):
    x = lax.rem(row_index(shape), PITCH)
    place = v.spot * COLS + x - 2
    seen = (place >= 0) & (place < WIDE) & (x >= 1) & (x < PITCH - 1)
    own = (x >= 2) & (x < PITCH - 2)
    return seen, own


def mask_gradient(v):
    def image(b, carry):
        value = nt(quarter_of(v.grad_mask[b]), v.w_mo[:, 0:MASK])
        for block in range(2):
            v.final[...] = value[:, block * 128 : (block + 1) * 128]
            v.tmp[0:SPREAD, :] = jnp.zeros((SPREAD, LANES), jnp.float32)
            for x in range(COLS):
                v.tmp[pl.ds(2 + x, TALL, stride=PITCH), :] = v.final[pl.ds(x, TALL, stride=COLS), :]
            v.hgo[b, :, 256 + block * 128 : 384 + block * 128] = half_of(v.tmp[0:SPREAD, :])
            v.m_left[b, block, 0:TALL, :] = half_of(v.final[pl.ds(0, TALL, stride=COLS), :])
            v.m_right[b, block, 0:TALL, :] = half_of(v.final[pl.ds(COLS - 1, TALL, stride=COLS), :])
        return carry

    lax.fori_loop(0, BATCH, image, 0)
    v.halo_mask.start()


def heads_part(v, b, tap):
    ref = v.hx_c if tap < 6 else v.hx_f
    lane = tap % 6 * 128
    return ref.at[b, 0:SPREAD, lane : lane + 128]


def taps_part(v, t, low, high):
    ref = v.hx_f if t % 3 == 2 else v.hx_c
    lane = (t % 3) % 2 * 384
    return ref.at[t // 3, 0:AREA, lane + low : lane + high]


def split_three(value):
    first = half_of(value)
    second = half_of(value - full_of(first))
    third = half_of(value - full_of(first) - full_of(second))
    return first, second, third


def column_grid():
    lane = lane_index((COLS, SPAN))
    columns = jnp.where((lax.rem(lane, PITCH) == row_index((COLS, SPAN)) + 2) & (lane < SPREAD), 1.0, 0.0)
    lane = lane_index((TALL, SPAN))
    rows = jnp.where(lax.div(lane, PITCH) == row_index((TALL, SPAN)), 1.0, 0.0)
    return columns, half_of(rows)


def widen(value, columns, rows, parts):
    spread = 0.0
    for piece in split_three(value)[:parts]:
        spread = spread + mm(piece, rows)
    return jnp.sum(spread * columns, axis=0, keepdims=True)


def widen_all(v):
    columns, rows = column_grid()
    first = row_index((8, SPAN)) == 0
    second = row_index((8, SPAN)) == 1
    for b in range(BATCH):
        low, high = (widen(v.target[b, c], columns, rows, 3) for c in range(2))
        v.target_wide[b] = jnp.where(first, low, jnp.where(second, high, 0.0))
        v.valid_wide[b] = jnp.broadcast_to(widen(v.valid[b].astype(jnp.float32), columns, rows, 1), (8, SPAN))


def narrow(v, b, wide, columns, rows):
    for c in range(2):
        total = 0.0
        for piece in split_three(wide[c : c + 1, :] * columns):
            total = total + nt(piece, rows)
        v.out_flow[b, c] = total


def heads(v):
    spot, last = v.spot, v.space - 1
    v.halo_final.receive()
    v.swap_count.receive()
    v.counts[v.spot] = v.count_out[...]
    counts = jnp.sum(v.counts[...], axis=0)
    seen, own = ring_masks(v, (SPREAD, LANES))
    steps = [(a - 1) * PITCH + (c - 1) for a in range(3) for c in range(3)]
    plane = jnp.float32(TALL * WIDE)
    columns, rows = column_grid()

    def image(b, carry):
        fx = fx_base(b)
        for j in range(2):
            left = jnp.where(spot > 0, full_of(v.f_left[b, j, 0:TALL, :]), 0.0)
            right = jnp.where(spot < last, full_of(v.f_right[b, j, 0:TALL, :]), 0.0)
            v.mm_tmp[pl.ds(fx + 8 + PITCH + j, TALL, stride=PITCH), :] = left
            v.mm_tmp[pl.ds(fx + 8 + PITCH + PITCH - 2 + j, TALL, stride=PITCH), :] = right
        for tap in range(9):
            at = 8 + PITCH + steps[tap]
            heads_part(v, b, tap)[...] = half_of(v.mm_tmp[pl.ds(fx + at, SPREAD), :])
        for part in range(2):
            name = (FLOW_HIDDEN, MASK_HIDDEN)[part]
            lanes = slice(part * 256, (part + 1) * 256)
            act, slope = act_slope(mm(join((v.hx_c[b, 0:SPREAD, :], v.hx_f[b, 0:SPREAD, :])), v.w_h[:, lanes]) + bias_of(v, name, 2))
            v.slope_h[b, :, lanes] = half_of(slope)
            if part == 0:
                for block in range(2):
                    value = jnp.where(seen, act[:, block * 128 : (block + 1) * 128], 0.0)
                    v.feat[b, 0:SPREAD, block * 128 : (block + 1) * 128] = half_of(value)
                v.feat[b, SPREAD:SPAN, :] = jnp.zeros((SPAN - SPREAD, HEAD), jnp.bfloat16)
            else:
                for block in range(2):
                    v.tmp[0:SPREAD, :] = act[:, block * 128 : (block + 1) * 128]
                    for x in range(COLS):
                        v.final[pl.ds(x, TALL, stride=COLS), :] = v.tmp[pl.ds(2 + x, TALL, stride=PITCH), :]
                    v.mf[b, :, block * 128 : (block + 1) * 128] = half_of(v.final[...])
        moved = nt(v.w_fo[...], v.feat[b])
        v.dt[...] = moved
        delta = jnp.zeros((8, SPAN), jnp.float32)
        for tap in range(9):
            pair = jnp.concatenate([v.dt[2 * tap : 2 * tap + 2, :], jnp.zeros((6, SPAN), jnp.float32)], axis=0)
            delta = delta + pltpu.roll(pair, (-steps[tap]) % SPAN, 1)
        v.tmp[0:SPAN, :] = jnp.zeros((SPAN, LANES), jnp.float32)
        v.final[...] = full_of(v.xc[b, 32 : 32 + AREA, 256:384])
        for x in range(COLS):
            v.tmp[pl.ds(2 + x, TALL, stride=PITCH), :] = v.final[pl.ds(x, TALL, stride=COLS), :]
        pick = jnp.where(lane_index((16, LANES)) == row_index((16, LANES)) + 126, 1.0, 0.0)
        base = nt(half_of(pick), half_of(v.tmp[0:SPAN, :]))[0:8, :]
        bias = v.bias[BIAS_AT[FLOW_OUT] : BIAS_AT[FLOW_OUT] + 1, :]
        first = row_index((8, SPAN)) == 0
        second = row_index((8, SPAN)) == 1
        shift = jnp.where(first, bias[0:1, 0:1], jnp.where(second, bias[0:1, 1:2], 0.0))
        new = base + delta + shift
        narrow(v, b, new, columns, rows)
        error = new - v.target_wide[b]
        root = jnp.sqrt(error * error + 1.0)
        valid = jnp.where(first | second, v.valid_wide[b], 0.0)
        piece = jnp.sum(valid * root)
        divisor = jnp.maximum(v.pick_count(counts, b), 1.0)
        gradient = plane / divisor * valid * error / root
        v.dg[b] = gradient
        v.losses[...] = jnp.where(row_index((8, LANES)) == b, piece, v.losses[...])
        return carry

    v.losses[...] = jnp.zeros((8, LANES), jnp.float32)
    lax.fori_loop(0, BATCH, image, 0)
    v.halo_dg.start()
    v.swap_loss.start()


def mask_output(v):
    def image(b, carry):
        store = pltpu.make_async_copy(v.mask_low, v.out_mask.at[b], v.osem.at[3])
        pl.when(b > 0)(store.wait)
        for block in range(5):
            wide = min(128, MASK - block * 128)
            lanes = slice(block * 128, block * 128 + wide)
            at = BIAS_AT[MASK_OUT] + block
            value = mm(v.mf[b], v.w_mo[:, lanes]) + v.bias[at : at + 1, 0:wide]
            v.mask_low[:, lanes] = half_of(0.25 * value)
        store.start()
        return carry

    lax.fori_loop(0, BATCH, image, 0)


def heads_back(v):
    spot, last = v.spot, v.space - 1
    seen, own = ring_masks(v, (SPREAD, LANES))
    steps = [(a - 1) * PITCH + (c - 1) for a in range(3) for c in range(3)]
    v.halo_dg.receive()
    v.halo_mask.receive()

    def zb(c, low, rows):
        at = c * (2 * EDGE + SPREAD) + low
        return v.mm_tmp.at[at : at + rows]

    def image(b, carry):
        x = lax.rem(lane_index((8, SPAN)), PITCH)
        own_dg = v.dg[b]
        left = jnp.where((x < 2) & (spot > 0), pltpu.roll(v.dg_left[b], SPAN - COLS, 1), 0.0)
        right = jnp.where((x >= PITCH - 2) & (spot < last), pltpu.roll(v.dg_right[b], COLS, 1), 0.0)
        inside = lane_index((8, SPAN)) < SPREAD
        wide_dg = full_of(half_of(jnp.where(inside, own_dg + left + right, 0.0)))
        own_low = full_of(half_of(own_dg))
        v.dt[...] = jnp.zeros_like(v.dt)
        v.dto[...] = jnp.zeros_like(v.dto)
        for tap in range(9):
            v.dt[2 * tap : 2 * tap + 2, :] = pltpu.roll(wide_dg, steps[tap] % SPAN, 1)[0:2, :]
            v.dto[2 * tap : 2 * tap + 2, :] = pltpu.roll(own_low, steps[tap] % SPAN, 1)[0:2, :]
        v.dtb[b] = half_of(v.dto[...])
        from_flow = tn(half_of(v.dt[...]), v.w_fo[...])
        for block in range(2):
            left = jnp.where(spot > 0, full_of(v.n_left[b, block, 0:TALL, :]), 0.0)
            right = jnp.where(spot < last, full_of(v.n_right[b, block, 0:TALL, :]), 0.0)
            v.tmp[0:SPREAD, :] = full_of(v.hgo[b, :, 256 + block * 128 : 384 + block * 128])
            v.tmp[pl.ds(1, TALL, stride=PITCH), :] = left
            v.tmp[pl.ds(PITCH - 2, TALL, stride=PITCH), :] = right
            v.hgo[b, :, 256 + block * 128 : 384 + block * 128] = half_of(v.tmp[0:SPREAD, :])
        for block in range(4):
            lanes = slice(block * 128, (block + 1) * 128)
            value = from_flow[0:SPREAD, lanes] if block < 2 else full_of(v.hgo[b, :, lanes])
            value = value * full_of(v.slope_h[b, :, lanes])
            v.hgo[b, :, lanes] = half_of(jnp.where(seen, value, 0.0))
        total = jnp.zeros((SPREAD, LANES), jnp.float32)
        for a in range(3):
            value = nt(v.hgo[b], v.w_h[a * 384 : (a + 1) * 384, :])
            for c in range(3):
                zb(c, EDGE, SPREAD)[...] = value[:, c * 128 : (c + 1) * 128]
            for c in range(3):
                at = EDGE - steps[a * 3 + c]
                total = total + zb(c, at, SPREAD)[...]
        for block in range(4):
            lanes = slice(block * 128, (block + 1) * 128)
            v.hgo[b, :, lanes] = half_of(jnp.where(own, full_of(v.hgo[b, :, lanes]), 0.0))
        v.tmp[0:SPREAD, :] = total
        for x in range(COLS):
            v.final[pl.ds(x, TALL, stride=COLS), :] = v.tmp[pl.ds(2 + x, TALL, stride=PITCH), :]
        r = v.final[...] + full_of(v.grad_net[b])

        s = full_of(v.xc[b, 32 : 32 + AREA, 0:128])
        update, reset, cand = v.lu[b], v.lr[b], v.lc[b]
        cg = half_of(r * update * (1.0 - cand * cand))
        v.gc[b, 32 : 32 + AREA, 256:384] = cg
        rows = [slice((4 - t) * COLS, (4 - t) * COLS + AREA) for t in range(5)]
        reset_grad = nt(
            join(v.gc[b, rows[t], 256:384] for t in range(5)),
            join(v.w_ls[t * 128 : (t + 1) * 128, 256:384] for t in range(5)),
        )
        v.gc[b, 32 : 32 + AREA, 0:128] = half_of(r * (cand - s) * update * (1.0 - update))
        v.gc[b, 32 : 32 + AREA, 128:256] = half_of(reset_grad * s * reset * (1.0 - reset))
        state_grad = r * (1.0 - update) + reset_grad * reset
        state_grad = state_grad + nt(
            join(v.gc[b, rows[t], 0:256] for t in range(5)),
            join(v.w_ls[t * 128 : (t + 1) * 128, 0:256] for t in range(5)),
        )
        inputs_grad = nt(
            join(v.gc[b, rows[t], :] for t in range(5)), join(v.w_li[t * 256 : (t + 1) * 256, :] for t in range(5))
        )
        high = half_of(own_dg)
        low = half_of(own_dg - full_of(high))
        pick = half_of(jnp.where(lane_index((8, LANES)) == row_index((8, LANES)) + 126, 1.0, 0.0))
        v.tmp[0:SPAN, :] = tn(high, pick) + tn(low, pick)
        for x in range(COLS):
            v.final[pl.ds(x, TALL, stride=COLS), :] = v.tmp[pl.ds(2 + x, TALL, stride=PITCH), :]
        v.lu[b] = state_grad
        v.lr[b] = inputs_grad[:, 0:128]
        v.lc[b] = inputs_grad[:, 128:256] + v.final[...]

        def peer(t, carry):
            at = pl.ds(pl.multiple_of(t * ROWS * COLS, 16), ROWS * COLS)
            v.a_state[t, b] = half_of(v.lu[b, at, :])
            v.a_context[t, b] = half_of(v.lr[b, at, :])
            v.a_motion[t, b] = half_of(v.lc[b, at, :])
            return carry

        lax.fori_loop(0, v.space, peer, 0)
        v.back_state.start(b)
        return carry

    v.swap_loss.receive()
    for c in range(3):
        zb(c, 0, EDGE)[...] = jnp.zeros((EDGE, LANES), jnp.float32)
        zb(c, EDGE + SPREAD, EDGE)[...] = jnp.zeros((EDGE, LANES), jnp.float32)
    lax.fori_loop(0, BATCH, image, 0)


def unpack_back(v, src, dst):
    def peer(t, carry):
        for b in range(BATCH):
            value = full_of(src[t, b])
            for y in range(ROWS):
                at = pl.multiple_of(y * WIDE + t * COLS, COLS)
                dst[b, pl.ds(at, COLS), :] = value[y * COLS : (y + 1) * COLS, :]
        return carry

    lax.fori_loop(0, v.space, peer, 0)


def seams():
    starts, bias_row, _, _ = flat_rows()
    edges = sorted(starts.values()) + [bias_row]
    tiles = sorted({row // 16 for row in edges if row % 16})
    parts = {}
    for low, high in zip(edges, edges[1:]):
        for tile in tiles:
            if low < (tile + 1) * 16 and high > tile * 16:
                parts[tile] = parts.get(tile, 0) + 1
    return {tile: (index, parts[tile]) for index, tile in enumerate(tiles)}


class Flush:
    def __init__(self, v):
        self.v, self.at, self.busy, self.small = v, 0, {}, []
        self.tiles = seams()
        self.left = {tile: parts for tile, (_, parts) in self.tiles.items()}
        v.seam[...] = jnp.zeros_like(v.seam)
        top = (max(self.tiles) + 1) * 16
        rest = v.out_flat.shape[0] - top
        v.seam_low[16 * 16 : 16 * 16 + rest, :] = jnp.zeros((rest, LANES), jnp.bfloat16)
        self.write(16, rest, top)

    def write(self, index, rows, base):
        v = self.v
        copy = pltpu.make_async_copy(
            v.seam_low.at[index * 16 : index * 16 + rows], v.out_flat.at[base : base + rows], v.fsem.at[index]
        )
        copy.start()
        self.small.append(copy)

    def send(self, low, length, base):
        v, slot = self.v, self.at % 2
        self.at += 1
        if slot in self.busy:
            self.busy[slot].wait()
        cast_rows(v.stage.at[slot], 0, v.flat, low, length, jnp.bfloat16)
        copy = pltpu.make_async_copy(
            v.stage.at[slot, 0:length], v.out_flat.at[base : base + length], v.ssem.at[slot, 0]
        )
        copy.start()
        self.busy[slot] = copy

    def layer(self, start, rows):
        v, stop = self.v, start + rows
        for tile in self.tiles:
            low, high = max(start, tile * 16), min(stop, tile * 16 + 16)
            if low >= high:
                continue
            index = self.tiles[tile][0]
            v.seam[index, low - tile * 16 : high - tile * 16, :] = v.flat[MARGIN + low - start : MARGIN + high - start, :]
            self.left[tile] -= 1
            if not self.left[tile]:
                v.seam_low[index * 16 : index * 16 + 16, :] = half_of(v.seam[index])
                self.write(index, 16, tile * 16)
        low, high = -(-start // 16) * 16, stop // 16 * 16
        if high > low:
            self.send(MARGIN + low - start, high - low, low)

    def settle(self):
        for copy in list(self.busy.values()) + self.small:
            copy.wait()
        self.busy, self.small = {}, []


SHARE = 3072


class Reduce:
    ORDER = (
        (3, 3072, 3072), (3, 0, 3072), (2, 3072, 3072), (2, 0, 3072), (1, 3072, 3072), (1, 0, 3072),
        (0, 1024, 3072), (0, 4096, 2048), (0, 0, 1024),
    )

    def __init__(self, v, count):
        self.v, self.count = v, count
        self.flying, self.queue, self.late = [], [], []
        self.copies = {}
        rank = v.rank
        self.lower, self.upper = lax.rem(rank, 2), lax.div(rank, 2)
        self.side, self.depth = lax.rem(v.spot, 2), lax.div(v.spot, 2)
        self.group = v.space // 2

    def part(self, k):
        return self.ORDER[k][2] // 4 // self.v.space

    def slice_at(self, k, spot):
        return lax.rem(spot, 2) * (self.ORDER[k][2] // 8) + lax.div(spot, 2) * self.part(k)

    def offer(self, *numbers, now=True):
        if now:
            self.queue += list(numbers)
        else:
            self.late += list(numbers)

    LONG = 5

    def stages(self, k):
        if k < self.LONG:
            return (self.core, self.across, self.side_sum, self.deep_sum, self.deep_out, self.owner, self.beside)
        if k < len(self.ORDER) - 1:
            return (self.core, self.across, self.stripes, self.along, self.beside)
        return (self.ranks, self.stripes, self.along)

    def tick(self):
        for entry in self.flying:
            self.stages(entry[0])[entry[1]](entry[0])
            entry[1] += 1
        self.flying = [entry for entry in self.flying if entry[1] < len(self.stages(entry[0]))]
        if self.queue:
            number = self.queue.pop(0)
            self.v.flush.settle()
            self.begin(number)
            self.flying.append([number, 0])
        self.queue, self.late = self.queue + self.late, []

    def begin(self, k):
        v, slot = self.v, k % 2
        quarter, low, size = self.ORDER[k]
        start = quarter * self.count // (LANES * 16) * 16 + low
        half = size // 2
        if k == len(self.ORDER) - 1:
            self.begin_ranks(start, size // 4)
            return

        def rows(which):
            return v.out_flat.at[pl.ds(pl.multiple_of(start + which * half, 16), half)]

        copy = remote(
            rows(1 - self.lower), v.rcore.at[slot, 0:half], v.rsend.at[0, slot], v.rrecv.at[0, slot], {DP: v.mate}
        )
        own = pltpu.make_async_copy(rows(self.lower), v.own.at[slot, 0:half], v.rlocal.at[slot])
        copy.start()
        own.start()
        self.copies[k] = (copy, own)

    def begin_ranks(self, start, rows):
        v = self.v

        def block(rank):
            at = start + lax.rem(rank, 2) * (2 * rows) + lax.div(rank, 2) * rows
            return v.out_flat.at[pl.ds(pl.multiple_of(at, 16), rows)]

        for turn in range(1, 4):
            to = lax.rem(v.rank + turn, 4)
            remote(block(to), v.dall.at[v.rank], v.dsend, v.drecv, {DP: to}).start()
        self.mine = pltpu.make_async_copy(block(v.rank), v.dall.at[v.rank], v.rlocal.at[0])
        self.mine.start()

    def ranks(self, k):
        v, slot, part = self.v, k % 2, self.part(k)
        self.mine.wait()
        drain_bytes(v.dall.at[0:3], v.dsend)
        drain_bytes(v.dall.at[0:3], v.drecv)
        self.finish_f(k)
        value = full_of(v.dall[0]) + full_of(v.dall[1]) + full_of(v.dall[2]) + full_of(v.dall[3])
        rows = self.ORDER[k][2] // 4
        v.ks[slot, 0:rows, :] = value
        v.ts[slot, 0:rows, :] = half_of(value)
        v.acc[slot, 0:part, :] = v.ks[slot, pl.ds(pl.multiple_of(self.slice_at(k, v.spot), 16), part), :]
        self.each(lambda step: self.s_copy(k, step).start(), 1, v.space)

    def finish_f(self, k):
        drain_bytes(self.s_all(k - 2), self.v.s2send.at[k % 2])
        self.f_sent(k - 2)

    def core(self, k):
        v, slot = self.v, k % 2
        copy, own = self.copies[k]
        copy.wait()
        own.wait()
        if k >= 2:
            self.x_copy(k - 2).wait_send()
        quarter = self.ORDER[k][2] // 4

        def add(step, carry):
            at = pl.multiple_of(step * 128, 128)
            near = pl.ds(pl.multiple_of(self.upper * quarter + at, 128), 128)
            far = pl.ds(pl.multiple_of((1 - self.upper) * quarter + at, 128), 128)
            to = pl.ds(at, 128)
            v.tx[slot, to, :] = half_of(full_of(v.own[slot, far, :]) + full_of(v.rcore[slot, far, :]))
            v.ks[slot, to, :] = full_of(v.own[slot, near, :]) + full_of(v.rcore[slot, near, :])
            return carry

        lax.fori_loop(0, quarter // 128, add, 0)
        self.x_copy(k).start()

    def x_copy(self, k):
        v, slot = self.v, k % 2
        rows = slice(0, self.ORDER[k][2] // 4)
        return remote(
            v.tx.at[slot, rows], v.rx.at[slot, rows], v.rsend.at[1, slot], v.rrecv.at[1, slot], {DP: v.other}
        )

    def s_copy(self, k, step):
        v, slot, part = self.v, k % 2, self.part(k)
        to = lax.rem(v.spot + step, v.space)
        src = v.ts.at[slot, pl.ds(pl.multiple_of(self.slice_at(k, to), 16), part)]
        dst = v.rs.at[slot, v.spot, 0:part]
        return remote(src, dst, v.s2send.at[slot], v.s2recv.at[slot], {SPACE: to})

    def s_all(self, k):
        return self.v.rs.at[k % 2, 0 : self.v.space - 1, 0 : self.part(k)]

    def each(self, what, start, stop):
        def body(step, carry):
            what(step)
            return carry

        lax.fori_loop(start, stop, body, 0)

    def across(self, k):
        v, slot = self.v, k % 2
        self.x_copy(k).wait_recv()
        if k < self.LONG:
            self.across_long(k)
            return
        if k - 2 >= self.LONG:
            drain_bytes(self.s_all(k - 2), v.s2send.at[slot])

        def add(step, carry):
            to = pl.ds(pl.multiple_of(step * 128, 128), 128)
            value = v.ks[slot, to, :] + full_of(v.rx[slot, to, :])
            v.ks[slot, to, :] = value
            v.ts[slot, to, :] = half_of(value)
            return carry

        lax.fori_loop(0, self.ORDER[k][2] // 4 // 128, add, 0)
        part = self.part(k)
        v.acc[slot, 0:part, :] = v.ks[slot, pl.ds(pl.multiple_of(self.slice_at(k, v.spot), 16), part), :]
        self.each(lambda step: self.s_copy(k, step).start(), 1, v.space)

    def across_long(self, k):
        v, slot = self.v, k % 2
        if k >= 2:
            self.side_copy(k - 2).wait_send()
        rows = self.ORDER[k][2] // 8

        def add(step, carry):
            at = pl.multiple_of(step * 128, 128)
            near = pl.ds(pl.multiple_of(self.side * rows + at, 128), 128)
            far = pl.ds(pl.multiple_of((1 - self.side) * rows + at, 128), 128)
            to = pl.ds(at, 128)
            v.ty[slot, to, :] = half_of(v.ks[slot, far, :] + full_of(v.rx[slot, far, :]))
            v.ky[slot, to, :] = v.ks[slot, near, :] + full_of(v.rx[slot, near, :])
            return carry

        lax.fori_loop(0, rows // 128, add, 0)
        self.side_copy(k).start()

    def side_copy(self, k):
        v, slot = self.v, k % 2
        return remote(v.ty.at[slot], v.ry.at[slot], v.rsend.at[2, slot], v.rrecv.at[2, slot], {SPACE: v.twin})

    def deep_at(self, k, depth):
        return pl.ds(pl.multiple_of(depth * self.part(k), 16), self.part(k))

    def deep_copy(self, k, step):
        v, slot = self.v, k % 2
        to = lax.rem(self.depth + step, self.group)
        return remote(
            v.tz.at[slot, self.deep_at(k, to)], v.rz.at[slot, self.depth], v.z1send.at[slot],
            v.z1recv.at[slot], {SPACE: to * 2 + self.side},
        )

    def deep_all(self, k):
        return self.v.rz.at[k % 2, 0 : self.group - 1]

    def side_sum(self, k):
        v, slot = self.v, k % 2
        self.side_copy(k).wait_recv()
        if k >= 2:
            drain_bytes(self.deep_all(k - 2), v.z1send.at[slot])
        value = v.ky[slot] + full_of(v.ry[slot])
        v.tz[slot] = half_of(value)
        v.ky[slot] = value
        v.kz[slot] = v.ky[slot, self.deep_at(k, self.depth), :]
        self.each(lambda step: self.deep_copy(k, step).start(), 1, self.group)

    def out_copy(self, k, step):
        v, slot = self.v, k % 3
        to = lax.rem(self.depth + step, self.group)
        block = v.az.at[slot, self.deep_at(k, self.depth)]
        return remote(
            block, block, v.z2send.at[slot], v.z2recv.at[slot], {SPACE: to * 2 + self.side}
        )

    def deep_sum(self, k):
        v, slot = self.v, k % 2
        drain_bytes(self.deep_all(k), v.z1recv.at[slot])

        def add(step, value):
            return value + full_of(v.rz[slot, lax.rem(self.depth + step, self.group)])

        value = lax.fori_loop(1, self.group, add, v.kz[slot])
        if k >= 2:
            self.own_wait(k - 2)
        v.az[k % 3, self.deep_at(k, self.depth), :] = half_of(value)
        self.each(lambda step: self.out_copy(k, step).start(), 1, self.group)

    def own_rows(self, k, lower, upper):
        quarter, low, size = self.ORDER[k]
        at = low + lower * (size // 2) + upper * (size // 4) + self.side * (size // 8)
        return pl.ds(pl.multiple_of(at, 16), size // 8)

    def own_copy(self, k):
        v = self.v
        rows = self.own_rows(k, self.lower, self.upper)
        return remote(v.az.at[k % 3], v.gath.at[rows], v.osend.at[k % 3], v.orecv.at[k], {DP: self.ORDER[k][0]})

    def own_wait(self, k):
        pl.when(self.v.rank != self.ORDER[k][0])(self.own_copy(k).wait_send)

    def deep_out(self, k):
        v = self.v
        several = v.az.at[k % 3, 0 : (self.group - 1) * self.part(k)]
        drain_bytes(several, v.z2send.at[k % 3])
        drain_bytes(several, v.z2recv.at[k % 3])
        pl.when(v.rank != self.ORDER[k][0])(self.own_copy(k).start)

        @pl.when(v.rank == self.ORDER[k][0])
        def _():
            v.gath[self.own_rows(k, self.lower, self.upper), :] = v.az[k % 3]

    def owner(self, k):
        v = self.v

        @pl.when(v.rank == self.ORDER[k][0])
        def _():
            drain_bytes(v.gath.at[0 : 3 * (self.ORDER[k][2] // 8)], v.orecv.at[k])
            for copy in self.y_copies(k):
                copy.start()

    def place(self, k, lower, upper, spot):
        quarter, low, size = self.ORDER[k]
        at = low + lower * (size // 2) + upper * (size // 4) + self.slice_at(k, spot)
        return pl.ds(pl.multiple_of(at, 16), self.part(k))

    def f_copy(self, k, step):
        v, slot = self.v, k % 2
        quarter = self.ORDER[k][0]
        if k == len(self.ORDER) - 1:
            to = lax.rem(v.spot + step, v.space)
        else:
            to = lax.rem(self.depth + step, self.group) * 2 + self.side
        return remote(
            v.fin.at[slot, 0 : self.part(k)], v.gath.at[self.place(k, self.lower, self.upper, v.spot)],
            v.fsend.at[slot], v.frecv.at[k], {DP: quarter, SPACE: to},
        )

    def fan(self, k):
        return self.v.space if k == len(self.ORDER) - 1 else self.group

    def f_all(self, k, what):
        v = self.v
        pl.when(v.rank != self.ORDER[k][0])(lambda: what(self.f_copy(k, 0)))
        self.each(lambda step: what(self.f_copy(k, step)), 1, self.fan(k))

    def f_sent(self, k):
        v = self.v
        quarter = self.ORDER[k][0]
        pl.when(v.rank != quarter)(lambda: self.f_copy(k, 0).wait_send())
        drain_bytes(v.gath.at[0 : (self.fan(k) - 1) * self.part(k)], v.fsend.at[k % 2])

    def stripes(self, k):
        v, slot, part = self.v, k % 2, self.part(k)
        quarter = self.ORDER[k][0]
        drain_bytes(self.s_all(k), v.s2recv.at[slot])

        def add(step, value):
            return value + full_of(v.rs[slot, lax.rem(v.spot + step, v.space), 0:part])

        value = half_of(lax.fori_loop(1, v.space, add, v.acc[slot, 0:part, :]))
        if k - 2 >= self.LONG and k < len(self.ORDER) - 1:
            self.f_sent(k - 2)
        v.fin[slot, 0:part, :] = value

        @pl.when(v.rank == quarter)
        def _():
            v.gath[self.place(k, self.lower, self.upper, v.spot), :] = v.fin[slot, 0:part, :]

        self.f_all(k, lambda copy: copy.start())

    def y_copies(self, k):
        v = self.v
        quarter, low, size = self.ORDER[k]
        out = []
        for i in range(4):
            at = pl.multiple_of(low + i * (size // 4) + self.side * (size // 8), 16)
            block = v.gath.at[pl.ds(at, size // 8)]
            out.append(remote(block, block, v.ysend.at[k], v.yrecv.at[k], {SPACE: v.twin}))
        return out

    def along(self, k):
        v = self.v
        quarter = self.ORDER[k][0]

        @pl.when(v.rank == quarter)
        def _():
            drain_bytes(v.gath.at[0 : (4 * self.fan(k) - 1) * self.part(k)], v.frecv.at[k])
            if k < len(self.ORDER) - 1:
                for copy in self.y_copies(k):
                    copy.start()

    def beside(self, k):
        v = self.v

        @pl.when(v.rank == self.ORDER[k][0])
        def _():
            several = v.gath.at[0 : self.ORDER[k][2] // 2]
            drain_bytes(several, v.ysend.at[k])
            drain_bytes(several, v.yrecv.at[k])

    def settle(self):
        v = self.v
        for k in range(self.LONG - 2, self.LONG):
            self.side_copy(k).wait_send()
            drain_bytes(self.deep_all(k), v.z1send.at[k % 2])
            self.own_wait(k)
        for k in range(len(self.ORDER) - 3, len(self.ORDER) - 1):
            self.x_copy(k).wait_send()
        for k in range(len(self.ORDER) - 2, len(self.ORDER)):
            drain_bytes(self.s_all(k), v.s2send.at[k % 2])
            self.f_sent(k)

    def ready(self):
        v, count = self.v, self.count
        v.gath[2 * SHARE :, :] = jnp.zeros((32, LANES), jnp.bfloat16)

        @pl.when(v.rank == 3)
        def _():
            at = self.bias_base() - 3 * count // (LANES * 16) * 16
            v.gath[at : at + 32, :] = half_of(full_of(v.gath[at : at + 32, :]) + v.bsum[...])

    def lay(self, first, last):
        v, count = self.v, self.count
        offset = v.rank * count - quarter_base(v.rank, count) * LANES
        skip = lax.div(offset, LANES)
        shift = lax.rem(offset, LANES)
        near = lane_index((256, LANES)) < LANES - shift

        def staged(slot):
            return v.mm_tmp.at[pl.ds(pl.multiple_of(slot * 512, 512), 512)]

        def out(step):
            at = pl.multiple_of(step * 512, 512)
            slot = lax.rem(step, 2)
            return pltpu.make_async_copy(staged(slot), v.out_grads.at[pl.ds(at, 512)], v.osem.at[4 + slot])

        def place(step, carry):
            turn = lax.rem(LANES - shift, LANES)
            for part in range(2):
                at = pl.multiple_of(step * 512 + part * 256, 256)
                v.tmp[part * 288 : part * 288 + 288, :] = pltpu.roll(full_of(v.gath[pl.ds(at, 288), :]), turn, 1)
            pl.when(step > first + 1)(out(step - 2).wait)
            for part in range(2):
                low = v.tmp[pl.ds(part * 288 + skip, 256), :]
                high = v.tmp[pl.ds(part * 288 + skip + 1, 256), :]
                to = pl.multiple_of(lax.rem(step, 2) * 512 + part * 256, 256)
                v.mm_tmp[pl.ds(to, 256), :] = jnp.where(near, low, high)
            out(step).start()
            return carry

        lax.fori_loop(first, last, place, 0)
        for step in (last - 2, last - 1):
            out(step).wait()

    def bias_base(self):
        return flat_rows()[1] // 16 * 16

    def bias_core(self):
        v = self.v
        self.b1 = remote(v.bown, v.bcore, v.bsend.at[0], v.brecv.at[0], {DP: v.mate})
        self.b1.start()

    def bias_across(self):
        v = self.v
        self.b1.wait()
        v.btwo[...] = v.bown[...] + v.bcore[...]
        self.b2 = remote(v.btwo, v.bacross, v.bsend.at[1], v.brecv.at[1], {DP: v.other})
        self.b2.start()

    def bias_stripes(self):
        v = self.v
        self.b2.wait()
        v.bfour[...] = v.btwo[...] + v.bacross[...]
        self.b3 = Swap(v, 8, v.bfour, v.ball, True)
        self.b3.start()

    def bias_end(self):
        v = self.v
        self.b3.receive()
        self.b3.sent()
        v.ball[v.spot] = v.bfour[...]
        v.bsum[...] = jnp.sum(v.ball[...], axis=0)


def ones_sum(g):
    return mm(jnp.ones((8, g.shape[0]), jnp.bfloat16), g)[0:1, :]


def keep_bias(v, name, value):
    for block in range(-(-value.shape[1] // 128)):
        at = BIAS_AT[name] + block
        v.gbias[at : at + 1, :] = value[:, block * 128 : (block + 1) * 128]


def gradients_gru(v, gates_name, cand_name, parts, g_of):
    starts, _, _, _ = flat_rows()
    total = 0.0
    for b in range(BATCH):
        total = total + ones_sum(g_of(b))
    keep_bias(v, gates_name, total[:, 0:256])
    keep_bias(v, cand_name, total[:, 256:384])

    def taps(number, first, last):
        return lambda b: join(parts(t)[number](b) for t in range(first, last))

    state = tn_all(taps(0, 0, 5), g_of, 0, 256)
    for t in range(5):
        pack_pairs(v.flat, t * 384, 128, state[t * 128 : (t + 1) * 128, 0:128], state[t * 128 : (t + 1) * 128, 128:256])
    state = tn_all(taps(2, 0, 5), g_of, 256, 384)
    for t in range(5):
        v.mm_tmp[pl.ds(MARGIN + t * 384, 128), :] = state[t * 128 : (t + 1) * 128, :]
    for first, last in ((0, 2), (2, 4), (4, 5)):
        inputs = tn_all(taps(1, first, last), g_of, 0, 384)
        for t in range(first, last):
            rows = slice((t - first) * 256, (t - first + 1) * 256)
            pack_pairs(v.flat, t * 384 + 128, 256, inputs[rows, 0:128], inputs[rows, 128:256])
            v.mm_tmp[pl.ds(MARGIN + t * 384 + 128, 256), :] = inputs[rows, 256:384]
    v.flush.layer(starts[gates_name], 3840)
    cast_rows(v.flat, MARGIN, v.mm_tmp, MARGIN, 1920, jnp.float32)
    v.flush.layer(starts[cand_name], 1920)


def tn_all(part, g_of, low, high):
    return tn(join((part(b) for b in range(BATCH)), 0), join((g_of(b, low, high) for b in range(BATCH)), 0))


def gradients_heads(v):
    starts, _, _, _ = flat_rows()
    total = 0.0
    for b in range(BATCH):
        total = total + ones_sum(v.hgo[b])
    keep_bias(v, FLOW_HIDDEN, total[:, 0:256])
    keep_bias(v, MASK_HIDDEN, total[:, 256:512])
    for name, lane in ((FLOW_HIDDEN, 0), (MASK_HIDDEN, 256)):
        grads = join((v.hgo[b, :, lane : lane + 256] for b in range(BATCH)), 0)
        for group in range(3):
            taps = [join(heads_part(v, b, group * 3 + c)[...] for c in range(3)) for b in range(BATCH)]
            value = tn(join(taps, 0), grads)
            for c in range(3):
                rows = slice(c * 128, (c + 1) * 128)
                pack_pairs(v.flat, (group * 3 + c) * 128, 128, value[rows, 0:128], value[rows, 128:256])
        v.flush.layer(starts[name], 2304)

    total = 0.0
    sums = 0.0
    for b in range(BATCH):
        total = total + mm(v.dtb[b], v.feat[b])
        sums = sums + jnp.sum(full_of(half_of(v.dg[b])), axis=1, keepdims=True)
    lane1 = lane_index((1, LANES))
    at = BIAS_AT[FLOW_OUT]
    v.gbias[at : at + 1, :] = jnp.where(lane1 == 0, sums[0:1, :], jnp.where(lane1 == 1, sums[1:2, :], 0.0))
    v.fo_tmp[...] = total[:, 0:128]
    v.fo_tmp2[...] = total[:, 128:256]
    for quarter in range(4):
        value = 0.0
        for which in range(2):
            rows = jnp.concatenate(
                [v.fo_tmp[pl.ds(which, 9, stride=2), :], v.fo_tmp2[pl.ds(which, 9, stride=2), :]], axis=1
            )
            value = value + nt(half_of(rows), split_pick(which, quarter))
        v.flat[pl.ds(MARGIN + quarter, 9, stride=4), :] = value
    v.flush.layer(starts[FLOW_OUT], 36)

    lane = lane_index((128, LANES))
    low_half = lane < 64
    even, odd = [], []
    total = 0.0
    for b in range(BATCH):
        total = total + ones_sum(quarter_of(v.grad_mask[b]))
    for block in range(5):
        wide = min(128, MASK - block * 128)
        at = BIAS_AT[MASK_OUT] + block
        v.gbias[at : at + 1, 0:wide] = total[:, block * 128 : block * 128 + wide]
        value = 0.0
        for b in range(BATCH):
            value = value + tn(v.mf[b], quarter_of(v.grad_mask[b, :, block * 128 : block * 128 + wide]))
        v.pair_a[:, 0:wide] = value
        even.append(v.pair_a[pl.ds(0, 128, stride=2), :])
        odd.append(pltpu.roll(v.pair_a[pl.ds(1, 128, stride=2), :], 64, 1))
    for i in range(4):
        v.flat[pl.ds(MARGIN + i, 128, stride=9), :] = even[i]
    v.flat[pl.ds(MARGIN + 4, 128, stride=9), :] = jnp.where(low_half, even[4], odd[0])
    for i in range(4):
        v.flat[pl.ds(MARGIN + 5 + i, 128, stride=9), :] = jnp.where(low_half, odd[i], odd[i + 1])
    v.flush.layer(starts[MASK_OUT], 1152)


def rows_back(v):
    v.back_state.receive()
    take_own(v, v.a_state, v.b_state)
    unpack_back(v, v.b_state, v.state)

    def image(b, carry):
        r = v.state[b]
        s = full_of(v.net[b])
        update, reset, cand = v.ru[b], v.rr[b], v.rc[b]
        cg = full_of(half_of(r * update * (1.0 - cand * cand)))
        spread_five(v, cg, None, 256, True)
        reset_grad = nt(
            join(taps_part(v, t, 256, 384)[...] for t in range(5)),
            join(v.w_rs[t * 128 : (t + 1) * 128, 256:384] for t in range(5)),
        )
        low = full_of(half_of(r * (cand - s) * update * (1.0 - update)))
        high = full_of(half_of(reset_grad * s * reset * (1.0 - reset)))
        spread_five(v, low, None, 0, True)
        spread_five(v, high, None, 128, True)
        v.gr[b] = taps_part(v, 2, 0, 384)[...]
        state_grad = r * (1.0 - update) + reset_grad * reset
        state_grad = state_grad + nt(
            join(taps_part(v, t, 0, 256)[...] for t in range(5)),
            join(v.w_rs[t * 128 : (t + 1) * 128, 0:256] for t in range(5)),
        )
        v.ru[b] = state_grad
        inputs_grad = nt(
            join(taps_part(v, t, 0, 384)[...] for t in range(5)),
            join(v.w_ri[t * 256 : (t + 1) * 256, :] for t in range(5)),
        )
        v.rr[b] = inputs_grad[:, 0:128]
        v.rc[b] = inputs_grad[:, 128:256]
        return carry

    lax.fori_loop(0, BATCH, image, 0)
    v.store_gnet.start()
    v.back_context.receive()
    v.back_motion.receive()
    take_own(v, v.a_context, v.b_context)
    take_own(v, v.a_motion, v.b_motion)
    unpack_back(v, v.b_context, v.lr)
    unpack_back(v, v.b_motion, v.lu)

    def total(b, carry):
        v.rr[b] = v.rr[b] + v.lr[b]
        motion = v.rc[b] + v.lu[b]
        v.mge[b, 256:896, :] = half_of(motion * full_of(v.slope_m[b]))
        high = half_of(motion)
        low = half_of(motion - full_of(high))
        pick = half_of(jnp.where(lane_index((16, LANES)) == row_index((16, LANES)) + 126, 1.0, 0.0))
        v.gf_base[b] = (nt(pick, high) + nt(pick, low))[0:8, :]
        return carry

    lax.fori_loop(0, BATCH, total, 0)
    v.halo_mg.start()
    v.store_gctx.start()


def branch_back(v):
    v.halo_mg.receive()

    def image(b, carry):
        up = jnp.where(v.spot > 0, full_of(v.mge[b, 0:256, :]), 0.0)
        own = full_of(v.mge[b, 256:896, :])
        down = jnp.where(v.spot < v.space - 1, full_of(v.mge[b, 896:1152, :]), 0.0)
        spread_rows(v, 0, (jnp.concatenate([up, own, down], axis=0),), 1152, v.xi, 0, 128, True)
        joint = nt(
            join(v.xi[(2 - a) * 128 : (2 - a) * 128 + 896, 0:384] for a in range(3)),
            join(v.w_mm[k * 256 : (k + 1) * 256, :] for k in range(9)),
        )
        branch = joint * full_of(v.slope_j[b])
        low = full_of(half_of(edge_rows(v, branch[:, 0:128], WIDE)))
        high = full_of(half_of(edge_rows(v, branch[:, 128:256], WIDE)))
        spread_rows(v, 0, (low, high), 896, v.hx_j.at[b], 0, 256, True)
        return carry

    lax.fori_loop(0, BATCH, image, 0)


def branch_own(v, b, low=0, high=256):
    return v.hx_j[b, 128:768, 256 + low : 256 + high]


def flow_back(v):
    def image(b, carry):
        rows = [slice((2 - a) * 128, (2 - a) * 128 + 640) for a in range(3)]
        flow_grad = nt(
            join(v.hx_j[b, rows[a], c * 256 + 128 : (c + 1) * 256] for a in range(3) for c in range(3)),
            join(v.w_fm[k * 128 : (k + 1) * 128, :] for k in range(9)),
        )
        v.fpg[b] = half_of(flow_grad * full_of(v.slope_fi[b]))
        z = nt(v.w_fi[...], v.fpg[b])
        total = jnp.zeros((32, LANES), jnp.float32)
        lane = lane_index((32, LANES))
        for across in range(7):
            v.fs[across] = jnp.zeros((32, LANES), jnp.float32)
            for y in range(ROWS):
                v.fs[across, 2 * y : 2 * y + 16, :] += z[across * 16 : across * 16 + 16, y * 128 : (y + 1) * 128]
            d = across - 3
            value = v.fs[across]
            if d:
                value = pltpu.roll(value, d % LANES, 1)
                value = jnp.where((lane - d >= 0) & (lane - d < WIDE), value, 0.0)
            total = total + value
        v.gf[b] = total
        return carry

    lax.fori_loop(0, BATCH, image, 0)
    v.halo_gf.start()


def gcorr_store(v):
    return pltpu.make_async_copy(v.flat.at[0 : ROWS * CORR * BATCH], v.out_gcorr, v.gsem)


def corr_back(v):
    def image(b, carry):
        corr_grad = nt(
            join(v.hx_j[b, (2 - a) * 128 : (2 - a) * 128 + 640, :] for a in range(3)),
            join(v.w_cm[k * 256 : (k + 1) * 256, :] for k in range(9)),
        )
        v.cpg[b] = half_of(corr_grad * full_of(v.slope_ci[b]))
        gcorr = nt(v.w_ci[...], v.cpg[b])
        for y in range(ROWS):
            v.flat[pl.ds(y * BATCH * CORR + b, CORR, stride=BATCH), :] = gcorr[:, y * WIDE : (y + 1) * WIDE]
        return carry

    lax.fori_loop(0, BATCH, image, 0)
    gcorr_store(v).start()


def summed(v, ref, name):
    total = 0.0
    for b in range(BATCH):
        total = total + ones_sum(ref(b))
    keep_bias(v, name, total)


def gradients_motion(v):
    starts = flat_rows()[0]
    summed(v, lambda b: v.mge[b, 256:896, :], MOTION_MIX)
    grads = join((v.mge[b, 256:896, :] for b in range(BATCH)), 0)
    for a in range(3):
        taps = join((v.hx_j[b, a * 128 : a * 128 + 640, :] for b in range(BATCH)), 0)
        v.mm_tmp[a * 768 : (a + 1) * 768, :] = tn(taps, grads)
    lane36 = lane_index((36, LANES))
    for r in range(63):
        first = v.mm_tmp[pl.ds(r, 36, stride=64), :]
        second = v.mm_tmp[pl.ds(r + 1, 36, stride=64), :]
        if r:
            first = pltpu.roll(first, LANES - 2 * r, 1)
        second = pltpu.roll(second, 126 - 2 * r, 1)
        v.flat[pl.ds(MARGIN + r, 36, stride=63), :] = jnp.where(lane36 < 126 - 2 * r, first, second)
    v.flush.layer(starts[MOTION_MIX], 2268)


def gradients_branches(v):
    starts = flat_rows()[0]
    summed(v, lambda b: branch_own(v, b), CORR_MIX)
    summed(v, lambda b: branch_own(v, b, 128, 256), FLOW_MIX)
    grads = join((branch_own(v, b, 128, 256) for b in range(BATCH)), 0)
    for k in range(9):
        a, c = k // 3, k % 3
        if c == 0:
            taps = join((v.hx_f[b, (a + 1) * 128 : (a + 1) * 128 + 640, :] for b in range(BATCH)), 0)
            group = tn(taps, grads)
        v.pair_a[0:128, :] = group[c * 128 : (c + 1) * 128]
        even, odd = (v.pair_a[pl.ds(i, 64, stride=2), :] for i in range(2))
        v.flat[MARGIN + 64 * k : MARGIN + 64 * (k + 1), :] = jnp.where(
            lane_index((64, LANES)) < 64, pltpu.roll(even, 64, 1), odd
        )
    v.flush.layer(starts[FLOW_MIX], 576)

    low_half = lane_index((128, LANES)) < 64
    grads = join((branch_own(v, b) for b in range(BATCH)), 0)
    for k in range(9):
        a, c = k // 3, k % 3
        if c == 0:
            taps = join((v.hx_c[b, (a + 1) * 128 : (a + 1) * 128 + 640, :] for b in range(BATCH)), 0)
            group = tn(taps, grads)
        v.pair_a[...] = group[c * 256 : (c + 1) * 256, 0:128]
        v.pair_b[...] = group[c * 256 : (c + 1) * 256, 128:256]
        even, odd = (v.pair_a[pl.ds(i, 128, stride=2), :] for i in range(2))
        even_high, odd_high = (v.pair_b[pl.ds(i, 128, stride=2), :] for i in range(2))
        odd, odd_high = pltpu.roll(odd, 64, 1), pltpu.roll(odd_high, 64, 1)
        at = MARGIN + 384 * k
        v.flat[pl.ds(at, 128, stride=3), :] = even
        v.flat[pl.ds(at + 1, 128, stride=3), :] = jnp.where(low_half, even_high, odd)
        v.flat[pl.ds(at + 2, 128, stride=3), :] = jnp.where(low_half, odd, odd_high)
    v.flush.layer(starts[CORR_MIX], 3456)


def gradients_flow_in(v):
    starts = flat_rows()[0]
    summed(v, lambda b: v.fpg[b], FLOW_IN)
    value = 0.0
    for b in range(BATCH):
        value = value + mm(v.xt[b, :, 256:896], v.fpg[b])
    v.flow_tmp[...] = value
    for across in range(7):
        for comp in range(2):
            v.flat[pl.ds(MARGIN + across * 2 + comp, 7, stride=14), :] = v.flow_tmp[
                pl.ds(across * 16 + comp, 7, stride=2), :
            ]
    v.flush.layer(starts[FLOW_IN], 98)


def gradients_corr_in(v):
    starts = flat_rows()[0]
    summed(v, lambda b: v.cpg[b], CORR_IN)
    value = 0.0
    for b in range(BATCH):
        value = value + mm(lines_of(v.corr, b, ROWS), v.cpg[b])
    gcorr_store(v).wait()
    pack_pairs(v.flat, 0, 324, value[:, 0:128], value[:, 128:256])
    v.flush.layer(starts[CORR_IN], 648)


def bias_tile(v):
    starts, bias_row, spots, inner = flat_rows()
    lead = bias_row % 16
    lane1 = lane_index((1, LANES))
    v.bown[...] = jnp.zeros_like(v.bown)
    for name, height, width in shapes():
        for block in range(-(-width // LANES)):
            value = v.gbias[BIAS_AT[name] + block : BIAS_AT[name] + block + 1, :]
            if name == FLOW_MIX:
                value = pltpu.roll(value, 64, 1)
            left = width - block * LANES
            if left < LANES:
                value = jnp.where(lane1 < left, value, 0.0)
            at = spots[name] + block * LANES
            row, shift = lead + at // LANES, at % LANES
            moved = pltpu.roll(value, shift, 1) if shift else value
            v.bown[row : row + 1, :] = v.bown[row : row + 1, :] + jnp.where(lane1 >= shift, moved, 0.0)
            if shift:
                v.bown[row + 1 : row + 2, :] = v.bown[row + 1 : row + 2, :] + jnp.where(lane1 < shift, moved, 0.0)


def finish(v):
    spot, last = v.spot, v.space - 1
    v.halo_gf.receive()
    for b in range(BATCH):
        v.tmp2[...] = v.gf[b]
        up = jnp.where(spot > 0, v.gf_up[b], 0.0)
        down = jnp.where(spot < last, v.gf_down[b], 0.0)
        v.tmp2[6:12, :] += up[16:22, :]
        v.tmp2[10:16, :] += down[0:6, :]
        for y in range(ROWS):
            v.out_gflow[b, y] = (
                v.tmp2[6 + 2 * y : 8 + 2 * y, :] + v.gf_base[b, 0:2, y * 128 : (y + 1) * 128]
            )
    v.loss_in[v.spot] = v.losses[...]
    total = jnp.sum(v.loss_in[...], axis=0)
    counts = jnp.sum(v.counts[...], axis=0)
    value = total / jnp.maximum(counts, 1.0)
    for b in range(BATCH):
        v.out_loss[b] = v.pick_count(value, b)


class View:
    pass


def main_kernel(names, space, count, *refs):
    v = View()
    for name, ref in zip(names, refs):
        setattr(v, name, ref)
    v.space = space
    v.lu, v.lc = v.motion, v.state
    v.spot = lax.axis_index(SPACE)
    v.rank = lax.axis_index(DP)
    v.mate, v.other, v.twin = mate_of(v.rank), lax.rem(v.rank + 2, 4), mate_of(v.spot)
    spot = v.spot
    barrier = pltpu.get_barrier_semaphore()

    def hello(step, carry):
        pl.semaphore_signal(barrier, inc=1, device_id={SPACE: lax.rem(spot + step, space)}, device_id_type=MESH)
        return carry

    lax.fori_loop(1, space, hello, 0)
    for turn in range(1, 4):

        def greet_rank(step, carry):
            place = lax.rem(spot + step, space)
            device = {DP: lax.rem(v.rank + turn, 4), SPACE: place}
            pl.semaphore_signal(barrier, inc=1, device_id=device, device_id_type=MESH)
            return carry

        lax.fori_loop(0, space, greet_rank, 0)
    pl.semaphore_wait(barrier, 4 * space - 1)

    v.store_gnet = pltpu.make_async_copy(v.ru, v.out_gnet, v.osem.at[0])
    v.store_gctx = pltpu.make_async_copy(v.rr, v.out_gctx, v.osem.at[1])
    rows = row_index((8, LANES))
    counted = jnp.zeros((8, LANES), jnp.float32)
    for b in range(BATCH):
        counted = jnp.where(rows == b, jnp.sum(v.valid[b].astype(jnp.float32)), counted)
    v.count_out[...] = counted
    v.pick_count = lambda counts, b: jnp.sum(jnp.where((rows == b) & (lane_index((8, LANES)) == 0), counts, 0.0))
    v.swap_count = Swap(v, 0, v.count_out, v.counts, True)
    v.swap_context = Swap(v, 1, v.a_context, v.b_context)
    v.swap_motion = Swap(v, 2, v.a_motion, v.b_motion)
    v.swap_state = Swap(v, 3, v.a_state, v.b_state)
    v.back_context = Swap(v, 4, v.a_context, v.b_context)
    v.back_motion = Swap(v, 5, v.a_motion, v.b_motion)
    v.back_state = Swap(v, 6, v.a_state, v.b_state)
    v.swap_loss = Swap(v, 7, v.losses, v.loss_in, True)
    v.halo_corr = Halo(v, 0, v.corr.at[:, 0:2], v.corr.at[:, 3:5], v.corr_down, v.corr_up)
    v.halo_flow = Halo(v, 1, v.flow, v.flow, v.flow_down, v.flow_up)
    v.halo_final = Halo(v, 2, v.e_left, v.e_right, v.f_right, v.f_left)
    v.halo_mask = Halo(v, 3, v.m_left, v.m_right, v.n_right, v.n_left)
    v.halo_dg = Halo(v, 4, v.dg, v.dg, v.dg_right, v.dg_left)
    v.halo_mg = Halo(v, 5, v.mge.at[:, 256:512], v.mge.at[:, 640:896], v.mge.at[:, 896:1152], v.mge.at[:, 0:256])
    v.halo_gf = Halo(v, 6, v.gf, v.gf, v.gf_down, v.gf_up)

    load = pltpu.make_async_copy(v.local, v.gath.at[0:BLOCK], v.lsem)
    load.start()
    for b in range(BATCH):
        for y in range(ROWS):
            v.flow[b, 2 * y : 2 * y + 2, :] = full_of(v.flow_in[b, y])
        v.flow[b, 2 * ROWS : 16, :] = jnp.zeros((16 - 2 * ROWS, LANES), jnp.float32)
    v.halo_flow.start()
    v.halo_corr.start()
    v.swap_count.start()
    load.wait()
    gather_start(v, count)

    def first(b, carry):
        v.state[b] = full_of(v.context[b])
        pack_rows(v, v.state, b, v.a_context)
        return carry

    lax.fori_loop(0, BATCH, first, 0)
    v.swap_context.start()
    v.halo_flow.receive()
    widen_all(v)
    gather_pass(v, 0, 0, 2)
    early_taps(v)
    gather_pass(v, 0, 2, 4)
    for copy in v.g_own[1:]:
        copy.wait_recv()
    for copy in v.g_x[1]:
        copy.start()
    columns_zero(v)
    gather_turn(v, 0)
    unpack_encoder(v, count)
    v.halo_corr.receive()
    forward_rows(v)
    keep = [pltpu.make_async_copy(v.hx_c, v.out_keep_c, v.ksem.at[0]), pltpu.make_async_copy(v.hx_f, v.out_keep_f, v.ksem.at[1])]
    for copy in keep:
        copy.start()
    unpack_heads(v)
    v.swap_context.receive()
    v.swap_motion.receive()
    v.swap_state.receive()
    take_own(v, v.a_context, v.b_context)
    take_own(v, v.a_motion, v.b_motion)
    take_own(v, v.a_state, v.b_state)
    columns_in(v)
    columns_forward(v)
    mask_gradient(v)
    for copy in keep:
        copy.wait()
    heads(v)
    mask_output(v)
    v.swap_context.sent()
    v.swap_motion.sent()
    v.swap_state.sent()
    heads_back(v)
    v.flush = Flush(v)
    red = v.reduce = Reduce(v, count)
    gradients_heads(v)
    v.back_context.start()
    v.back_motion.start()
    red.offer(0)
    red.tick()
    gradients_gru(
        v,
        COLUMNS_GATES,
        COLUMNS_CANDIDATE,
        lambda t: (
            lambda b: v.xc[b, t * COLS : t * COLS + AREA, 0:128],
            lambda b: v.xc[b, t * COLS : t * COLS + AREA, 128:384],
            lambda b: v.xcr[b, t * COLS : t * COLS + AREA, :],
        ),
        lambda b, low=0, high=384: v.gc[b, 32 : 32 + AREA, low:high],
    )
    red.offer(1, 2)
    red.tick()
    rows_back(v)
    red.tick()
    keep = [
        pltpu.make_async_copy(v.out_keep_c, v.hx_c, v.ksem.at[0]),
        pltpu.make_async_copy(v.out_keep_f, v.hx_f, v.ksem.at[1]),
    ]
    for copy in keep:
        copy.start()
    gradients_gru(
        v,
        ROWS_GATES,
        ROWS_CANDIDATE,
        lambda t: (
            lambda b: v.xs[b * AREA : (b + 1) * AREA, t * 128 : (t + 1) * 128],
            lambda b: v.xi[b * AREA : (b + 1) * AREA, t * 256 : (t + 1) * 256],
            lambda b: v.xr[b * AREA : (b + 1) * AREA, t * 128 : (t + 1) * 128],
        ),
        lambda b, low=0, high=384: v.gr[b, :, low:high],
    )
    red.offer(3, 4)
    red.tick()
    gradients_motion(v)
    red.offer(5)
    red.tick()
    branch_back(v)
    red.tick()
    for copy in keep:
        copy.wait()
    gradients_branches(v)
    red.offer(6, now=True)
    red.tick()
    flow_back(v)
    gradients_flow_in(v)
    red.offer(7, now=True)
    red.tick()
    corr_back(v)
    red.tick()
    gradients_corr_in(v)
    bias_tile(v)
    red.bias_core()
    red.offer(8, now=True)
    red.tick()
    finish(v)
    red.bias_across()
    red.tick()
    red.bias_stripes()
    red.tick()
    red.bias_end()
    red.ready()
    pl.when(v.rank > 0)(lambda: red.lay(0, 12))
    pl.when(v.rank == 0)(lambda: red.lay(2, 7))
    red.tick()
    pl.when(v.rank == 0)(lambda: red.lay(7, 12))
    pl.when(v.rank == 0)(lambda: red.lay(0, 2))
    assert not red.flying and not red.queue
    red.settle()
    for swap in (v.swap_count, v.back_context, v.back_motion, v.back_state, v.swap_loss):
        swap.sent()
    for halo in (v.halo_corr, v.halo_flow, v.halo_final, v.halo_mask, v.halo_dg, v.halo_mg, v.halo_gf):
        halo.sent()
    v.store_gnet.wait()
    v.store_gctx.wait()
    pltpu.make_async_copy(v.mask_low, v.out_mask.at[0], v.osem.at[3]).wait()


def main_call(space, count, local, net, context, corr, flow, target, valid, grad_net, grad_mask):
    total = 3 * count // (LANES * 16) * 16 + BLOCK
    low, wide = jnp.bfloat16, jnp.float32
    peers = (space, BATCH, ROWS * COLS, LANES)
    ins = dict(
        local=local, net=net, context=context, corr=corr, flow_in=flow, target=target, valid=valid,
        grad_net=grad_net, grad_mask=grad_mask,
    )
    outs = dict(
        out_net=((BATCH, AREA, 128), low),
        out_flow=((BATCH, 2, COLS, TALL), wide),
        out_mask=((BATCH, AREA, MASK), low),
        out_loss=((BATCH,), wide),
        out_flat=((total, 128), low),
        out_gnet=((BATCH, AREA, 128), wide),
        out_gctx=((BATCH, AREA, 128), wide),
        out_gcorr=((ROWS * CORR * BATCH, 128), wide),
        out_gflow=((BATCH, ROWS, 2, 128), wide),
        out_keep_c=((BATCH, 1152, 768), low),
        out_keep_f=((BATCH, 1152, 384), low),
        out_all=((4 * BLOCK, 128), low),
        out_grads=((BLOCK, 128), wide),
    )
    scratch = dict(
        stage=((2, 3904, 128), low),
        seam=((16, 16, 128), wide),
        mask_low=((AREA, MASK), low),
        seam_low=((16 * 20, 128), low),
        own=((2, SHARE // 2, 128), low),
        rcore=((2, SHARE // 2, 128), low),
        tx=((2, SHARE // 4, 128), low),
        rx=((2, SHARE // 4, 128), low),
        ks=((2, SHARE // 4, 128), wide),
        ts=((2, SHARE // 4, 128), low),
        acc=((2, SHARE // 4 // space, 128), wide),
        rs=((2, space, SHARE // 4 // space, 128), low),
        fin=((2, SHARE // 4 // space, 128), low),
        dall=((4, 256, 128), low),
        bz=((64, 128), low),
        ty=((2, SHARE // 8, 128), low),
        ry=((2, SHARE // 8, 128), low),
        ky=((2, SHARE // 8, 128), wide),
        tz=((2, SHARE // 8, 128), low),
        rz=((2, space // 2, SHARE // 4 // space, 128), low),
        kz=((2, SHARE // 4 // space, 128), wide),
        az=((3, SHARE // 8, 128), low),
        gath=((2 * SHARE + 32, 128), low),
        bown=((32, 128), wide), bcore=((32, 128), wide), btwo=((32, 128), wide), bacross=((32, 128), wide),
        bfour=((32, 128), wide), ball=((space, 32, 128), wide), bsum=((32, 128), wide),
        flat=((3904, 128), wide),
        pair_a=((256, 128), wide),
        pair_b=((256, 128), wide),
        flow_tmp=((112, 128), wide),
        mm_tmp=((3 * (2 * EDGE + SPREAD), 128), wide),
        fo_tmp=((32, 128), wide),
        fo_tmp2=((32, 128), wide),
        w_ci=((CORR, 256), low),
        w_cm=((2304, 256), low),
        w_fi=((112, 128), low),
        w_fm=((1152, 128), low),
        w_mm=((2304, 128), low),
        w_ri=((1280, 384), low),
        w_rs=((640, 384), low),
        w_li=((1280, 384), low),
        w_ls=((640, 384), low),
        w_h=((1152, 512), low),
        w_fo=((32, 256), low),
        w_mo=((256, 640), low),
        bias=((BIAS_ROWS, 128), wide),
        gbias=((BIAS_ROWS, 128), wide),
        corr_up=((BATCH, 2, CORR, 128), low),
        corr_down=((BATCH, 2, CORR, 128), low),
        flow_up=((BATCH, 16, 128), wide),
        flow_down=((BATCH, 16, 128), wide),
        fs=((7, 32, 128), wide),
        xt=((BATCH, 112, 1152), low),
        tmp=((1168, 128), wide),
        tmp2=((32, 128), wide),
        hx_c=((BATCH, 1152, 768), low),
        hx_f=((BATCH, 1152, 384), low),
        hx_j=((BATCH, 896, 768), low),
        slope_ci=((BATCH, AREA, 256), low),
        slope_fi=((BATCH, AREA, 128), low),
        slope_j=((BATCH, 896, 256), low),
        slope_m=((BATCH, AREA, 128), low),
        motion=((BATCH, AREA, 128), wide),
        state=((BATCH, AREA, 128), wide),
        xi=((BATCH * AREA, 1280), low),
        xs=((BATCH * AREA, 640), low),
        xr=((BATCH * AREA, 640), low),
        ru=((BATCH, AREA, 128), wide),
        rr=((BATCH, AREA, 128), wide),
        rc=((BATCH, AREA, 128), wide),
        lr=((BATCH, AREA, 128), wide),
        a_state=(peers, low), a_context=(peers, low), a_motion=(peers, low),
        b_state=(peers, low), b_context=(peers, low), b_motion=(peers, low),
        xc=((BATCH, AREA + 64, 384), low),
        xcr=((BATCH, AREA + 64, 128), low),
        gc=((BATCH, AREA + 64, 384), low),
        final=((AREA, 128), wide),
        e_left=((BATCH, 2, 48, 128), low), e_right=((BATCH, 2, 48, 128), low),
        f_left=((BATCH, 2, 48, 128), low), f_right=((BATCH, 2, 48, 128), low),
        m_left=((BATCH, 2, 48, 128), low), m_right=((BATCH, 2, 48, 128), low),
        n_left=((BATCH, 2, 48, 128), low), n_right=((BATCH, 2, 48, 128), low),
        slope_h=((BATCH, SPREAD, 512), low),
        feat=((BATCH, SPAN, 256), low),
        mf=((BATCH, AREA, 256), low),
        dg=((BATCH, 8, SPAN), wide),
        target_wide=((BATCH, 8, SPAN), wide),
        valid_wide=((BATCH, 8, SPAN), wide),
        flow=((BATCH, 16, 128), wide),
        dg_left=((BATCH, 8, SPAN), wide), dg_right=((BATCH, 8, SPAN), wide),
        dt=((32, SPAN), wide),
        dto=((32, SPAN), wide),
        dtb=((BATCH, 32, SPAN), low),
        hgo=((BATCH, SPREAD, 512), low),
        gr=((BATCH, AREA, 384), low),
        mge=((BATCH, 1152, 128), low),
        cpg=((BATCH, AREA, 256), low),
        fpg=((BATCH, AREA, 128), low),
        gf_base=((BATCH, 8, AREA), wide),
        gf=((BATCH, 32, 128), wide), gf_up=((BATCH, 32, 128), wide), gf_down=((BATCH, 32, 128), wide),
        count_out=((8, 128), wide), counts=((space, 8, 128), wide),
        losses=((8, 128), wide), loss_in=((space, 8, 128), wide),
    )
    sems = dict(
        hsend=pltpu.SemaphoreType.DMA((7, 2)), hrecv=pltpu.SemaphoreType.DMA((7, 2)),
        asend=pltpu.SemaphoreType.DMA((9,)), arecv=pltpu.SemaphoreType.DMA((9,)),
        ssem=pltpu.SemaphoreType.DMA((2, 2)),
        fsem=pltpu.SemaphoreType.DMA((17,)),
        rsend=pltpu.SemaphoreType.DMA((3, 2)), rrecv=pltpu.SemaphoreType.DMA((3, 2)),
        z1send=pltpu.SemaphoreType.DMA((2,)), z1recv=pltpu.SemaphoreType.DMA((2,)),
        z2send=pltpu.SemaphoreType.DMA((3,)), z2recv=pltpu.SemaphoreType.DMA((3,)),
        osend=pltpu.SemaphoreType.DMA((3,)), orecv=pltpu.SemaphoreType.DMA((9,)),
        rlocal=pltpu.SemaphoreType.DMA((2,)),
        s2send=pltpu.SemaphoreType.DMA((2,)), s2recv=pltpu.SemaphoreType.DMA((2,)),
        fsend=pltpu.SemaphoreType.DMA((2,)), frecv=pltpu.SemaphoreType.DMA((9,)),
        ysend=pltpu.SemaphoreType.DMA((9,)), yrecv=pltpu.SemaphoreType.DMA((9,)),
        dsend=pltpu.SemaphoreType.DMA, drecv=pltpu.SemaphoreType.DMA,
        bsend=pltpu.SemaphoreType.DMA((2,)), brecv=pltpu.SemaphoreType.DMA((2,)),
        ksem=pltpu.SemaphoreType.DMA((2,)),
        gsend=pltpu.SemaphoreType.DMA((9, 8)), grecv=pltpu.SemaphoreType.DMA((9, 8)), lsem=pltpu.SemaphoreType.DMA,
        gsem=pltpu.SemaphoreType.DMA,
        osem=pltpu.SemaphoreType.DMA((6,)),
    )
    vmem = pl.BlockSpec(memory_space=pltpu.VMEM)
    hbm = pl.BlockSpec(memory_space=pl.ANY)
    names = list(ins) + list(outs) + list(scratch) + list(sems)
    return pl.pallas_call(
        functools.partial(main_kernel, names, space, count),
        out_shape=[jax.ShapeDtypeStruct(*entry) for entry in outs.values()],
        in_specs=[hbm if name == "local" else vmem for name in ins],
        out_specs=[pl.BlockSpec(memory_space=pltpu.SMEM) if name == "out_loss" else hbm if name in ("out_flat", "out_gnet", "out_gctx", "out_gcorr", "out_keep_c", "out_keep_f", "out_mask", "out_grads", "out_all") else vmem for name in outs],
        scratch_shapes=[pltpu.VMEM(*entry) for entry in scratch.values()] + list(sems.values()),
        compiler_params=pltpu.CompilerParams(
            collective_id=2, has_side_effects=True, vmem_limit_bytes=VMEM_LIMIT
        ),
    )(*ins.values())


VMEM_LIMIT = 64 * 2**20 - 2**16


def shards_wide(net, context, corr, flow, target, valid, grad_net, grad_mask, params):
    space = lax.axis_size(SPACE)
    count = params.shape[0]
    local = jnp.pad(params, (0, BLOCK * LANES - count)).reshape(BLOCK, LANES)
    outs = main_call(
        space, count, local, net.reshape(BATCH, AREA, HID), context.reshape(BATCH, AREA, CTX),
        jnp.transpose(corr, (0, 1, 3, 2)), jnp.transpose(flow, (0, 2, 1, 3)), jnp.transpose(target, (0, 1, 3, 2)),
        jnp.transpose(valid, (0, 2, 1)),
        grad_net.reshape(BATCH, AREA, HID), grad_mask.reshape(BATCH, AREA, MASK),
    )
    new_net, new_flow, mask, loss, _, gnet, gctx, gcorr, gflow = outs[:9]
    new_flow = jnp.transpose(new_flow, (0, 1, 3, 2))
    grads = outs[-1].reshape(-1)[:count]
    return (
        new_net.reshape(BATCH, TALL, COLS, HID),
        new_flow,
        mask.reshape(BATCH, TALL, COLS, MASK),
        loss,
        grads,
        gnet.reshape(BATCH, ROWS, WIDE, HID),
        gctx.reshape(BATCH, ROWS, WIDE, CTX),
        jnp.transpose(gcorr.reshape(ROWS, CORR, BATCH, WIDE), (2, 0, 3, 1)),
        jnp.transpose(gflow, (0, 2, 1, 3)),
    )


def solution(mesh):
    def plan(*arrays):
        net, valid = arrays[0], arrays[5]
        if (net.shape[1:3], valid.shape[1:]) == ((ROWS, WIDE), (TALL, COLS)):
            return shards_wide(*arrays)
        return shards(*arrays)

    return jax.shard_map(
        plan,
        mesh=mesh,
        in_specs=(
            P(DP, SPACE, None, None),
            P(DP, SPACE, None, None),
            P(DP, SPACE, None, None),
            P(DP, None, SPACE, None),
            P(DP, None, None, SPACE),
            P(DP, None, SPACE),
            P(DP, None, SPACE, None),
            P(DP, None, SPACE, None),
            P(DP),
        ),
        out_specs=(
            P(DP, None, SPACE, None),
            P(DP, None, None, SPACE),
            P(DP, None, SPACE, None),
            P(DP),
            P(DP),
            P(DP, SPACE, None, None),
            P(DP, SPACE, None, None),
            P(DP, SPACE, None, None),
            P(DP, None, SPACE, None),
        ),
        check_vma=False,
    )
```
